32 devices in a mesh: replica: 4 (over y, x), fsdp: 8 (over z, core).
Axes of the slice: x: 2, y: 2, z: 4, core: 2. Of those that a mesh axis runs over, the one named last changes fastest.
Arguments:
- tokens: bfloat16 [4096, 2048], P(('replica', 'fsdp')), may hold values from -6 to 6
- attn_gain: bfloat16 [2048], P('fsdp'), may hold values from 0.5 to 1.5
- w_query: bfloat16 [2048, 2048], P('fsdp'), may hold values from -0.125 to 0.125
- w_key: bfloat16 [2048, 2048], P('fsdp'), may hold values from -0.125 to 0.125
- w_value: bfloat16 [2048, 2048], P('fsdp'), may hold values from -0.125 to 0.125
- w_out: bfloat16 [2048, 2048], P('fsdp'), may hold values from -0.75 to 0.75
- ffn_gain: bfloat16 [2048], P('fsdp'), may hold values from 0.5 to 1.5
- w_gate: bfloat16 [2048, 8192], P('fsdp'), may hold values from -0.125 to 0.125
- w_up: bfloat16 [2048, 8192], P('fsdp'), may hold values from -0.125 to 0.125
- w_down: bfloat16 [8192, 2048], P('fsdp'), may hold values from -0.0625 to 0.0625
- cotangent: bfloat16 [4096, 2048], P(('replica', 'fsdp')), may hold values from -6 to 6
Outputs:
- outputs: bfloat16 [4096, 2048], P(('replica', 'fsdp'))
- grad_tokens: float32 [4096, 2048], P(('replica', 'fsdp'))
- grad_attn_gain: float32 [2048], P('fsdp')
- grad_w_query: float32 [2048, 2048], P('fsdp')
- grad_w_key: float32 [2048, 2048], P('fsdp')
- grad_w_value: float32 [2048, 2048], P('fsdp')
- grad_w_out: float32 [2048, 2048], P('fsdp')
- grad_ffn_gain: float32 [2048], P('fsdp')
- grad_w_gate: float32 [2048, 8192], P('fsdp')
- grad_w_up: float32 [2048, 8192], P('fsdp')
- grad_w_down: float32 [8192, 2048], P('fsdp')
The draws below stay inside these ranges and needn't reach their ends.
All inputs are finite; a program needn't handle non-finite values.
Results may differ from the reference program's by a relative error of at most 0.023.
Values may be sent and summed in bfloat16 or wider, within the bound.
A program may use at most 576 MiB of HBM per device.

```python
import jax
import jax.numpy as jnp
from jax import lax

D = 2048
FF = 8192
HEAD_DIM = 64
TOK_DEV = 128
BLOCK = 512
TOKENS = 4096
N_REPLICA = 4
N_FSDP = 8


def level_of(key, shape, split, least, largest):
    gain = 1.0
    for axis_at, blocks in split:
        heights = jax.random.uniform(jax.random.fold_in(jax.random.fold_in(key, 6), axis_at), (blocks,), jnp.float32, least / len(split), largest / len(split))
        gain = gain * jnp.repeat(jnp.exp(heights), shape[axis_at] // blocks).reshape((-1,) + (1,) * (len(shape) - 1 - axis_at))
    return gain


def bell_draw(rng, dims, deviation, most, split=(), kind=jnp.bfloat16):
    drawn = jax.random.normal(rng, dims, jnp.float32) * deviation
    if len(split) > 0:
        drawn = level_of(rng, dims, split, -0.22, 0.18) * drawn
    return jnp.clip(drawn, min=-most, max=most).astype(kind)


def setup_inputs(seed: int = 0) -> dict:
    key_list = jax.random.split(jax.random.key(seed), 12)
    tokens = bell_draw(key_list[0], (TOKENS, D), 1.0, 6.0, ((0, 32),))
    attn_gain = jnp.clip(1.0 + 0.1 * jax.random.normal(key_list[1], (D,), jnp.float32), 0.5, 1.5).astype(jnp.bfloat16)
    w_query = bell_draw(key_list[2], (D, D), D ** -0.5, 0.125, ((0, 8),))
    w_key = bell_draw(key_list[3], (D, D), D ** -0.5, 0.125, ((0, 8),))
    w_value = bell_draw(key_list[4], (D, D), D ** -0.5, 0.125, ((0, 8),))
    w_out = bell_draw(key_list[5], (D, D), (max(D // 32, 2)) ** -0.5, 0.75, ((0, 8),))
    ffn_gain = jnp.clip(1.0 + 0.1 * jax.random.normal(key_list[6], (D,), jnp.float32), 0.5, 1.5).astype(jnp.bfloat16)
    w_gate = bell_draw(key_list[7], (D, FF), D ** -0.5, 0.125, ((0, 8),))
    w_up = bell_draw(key_list[8], (D, FF), D ** -0.5, 0.125, ((0, 8),))
    w_down = bell_draw(key_list[9], (FF, D), FF ** -0.5, 0.0625, ((0, 8),))
    cotangent = bell_draw(key_list[10], (TOKENS, D), 1.0, 6.0, ((0, 32),))
    return dict(tokens=tokens, attn_gain=attn_gain, w_query=w_query, w_key=w_key, w_value=w_value, w_out=w_out, ffn_gain=ffn_gain, w_gate=w_gate, w_up=w_up, w_down=w_down, cotangent=cotangent)


@jax.custom_vjp
def low(v):
    return lax.optimization_barrier(v.astype(jnp.bfloat16)).astype(jnp.float32)

@jax.custom_vjp
def low_back(v):
    return v

def low_keep(v):
    return (low(v), None)

def low_pass(kept, grad):
    return (grad,)

def back_keep(v):
    return (v, None)

def back_low(kept, grad):
    return (low(grad),)
low.defvjp(low_keep, low_pass)
low_back.defvjp(back_keep, back_low)
eps_norm = 1e-05
rope_base = 130000.0
masked_score = -1e+30
exact_mode = lax.Precision.HIGHEST

def rms_factor(values):
    return lax.rsqrt(lax.optimization_barrier(jnp.mean(values * values, axis=-1, keepdims=True)) + eps_norm)

def rope_tables(positions, head_width):
    halfway = head_width // 2
    spacing = jnp.arange(halfway, dtype=jnp.float32) * 2.0 / head_width
    frequency = rope_base ** (-spacing)
    angles = positions.astype(jnp.float32)[:, None] * frequency[None, :]
    return (jnp.cos(angles), jnp.sin(angles))

def rotate(values, cosine, sine_table, head_width):
    row_count = values.shape[0]
    halfway = head_width // 2
    split_heads = values.reshape(row_count, -1, head_width)
    former = split_heads[..., :halfway]
    latter = split_heads[..., halfway:]
    cos_rows = cosine[:, None, :]
    sin_rows = sine_table[:, None, :]
    turned = jnp.concatenate([former * cos_rows - latter * sin_rows, latter * cos_rows + former * sin_rows], axis=-1)
    return turned.reshape(values.shape)

def matmul(left, right):
    return jnp.dot(left, right, precision=exact_mode, preferred_element_type=jnp.float32)

def attention(queries, keys_all, values_all):
    seq_rows = queries.shape[0]
    keys_heads = keys_all.reshape(seq_rows, -1, HEAD_DIM)
    values_heads = values_all.reshape(seq_rows, -1, HEAD_DIM)
    key_positions = jnp.arange(seq_rows, dtype=jnp.int32)

    def one_block(block_pair):
        block_queries, first_row = block_pair
        query_heads = block_queries.reshape(BLOCK, -1, HEAD_DIM)
        scores = jnp.einsum('qhd,khd->hqk', query_heads, keys_heads, precision=exact_mode) * HEAD_DIM ** (-0.5)
        query_positions = first_row + jnp.arange(BLOCK, dtype=jnp.int32)
        causal = key_positions[None, :] <= query_positions[:, None]
        scores = low_back(jnp.where(causal[None], scores, masked_score))
        weights_low = low(jax.nn.softmax(scores, axis=-1))
        mixed_rows = jnp.einsum('hqk,khd->qhd', weights_low, values_heads, precision=exact_mode)
        return mixed_rows.reshape(BLOCK, -1)
    blocks = queries.reshape(seq_rows // BLOCK, BLOCK, -1)
    starts = jnp.arange(seq_rows // BLOCK, dtype=jnp.int32) * BLOCK
    mixed_rows = lax.map(jax.checkpoint(one_block), (blocks, starts))
    return mixed_rows.reshape(seq_rows, -1)

def layer(inputs, attn_gain, w_query, w_key, w_value, w_out, ffn_gain, w_gate, w_up, w_down):
    seq_rows = inputs.shape[0]
    cosine, sine_table = rope_tables(jnp.arange(seq_rows, dtype=jnp.int32), HEAD_DIM)
    normed_one = inputs * rms_factor(inputs)
    lowered_one = low(normed_one * attn_gain)
    queries = low(rotate(low_back(matmul(lowered_one, w_query)), cosine, sine_table, HEAD_DIM))
    keys_all = low(rotate(low_back(matmul(lowered_one, w_key)), cosine, sine_table, HEAD_DIM))
    values_all = low(low_back(matmul(lowered_one, w_value)))
    attended = low(low_back(attention(queries, keys_all, values_all)))
    after_attn = inputs + low_back(matmul(attended, w_out))
    normed_two = after_attn * rms_factor(after_attn)
    lowered_two = low(normed_two * ffn_gain)
    gate_values = low_back(matmul(lowered_two, w_gate))
    up_values = low_back(matmul(lowered_two, w_up))
    hidden = low(jax.nn.silu(gate_values) * up_values)
    return after_attn + matmul(hidden, w_down)

def reference(tokens, attn_gain, w_query, w_key, w_value, w_out, ffn_gain, w_gate, w_up, w_down, cotangent):
    seq_rows = TOK_DEV * N_FSDP
    inputs = tokens.astype(jnp.float32).reshape(N_REPLICA, seq_rows, D)
    params = tuple((weight_arg.astype(jnp.float32) for weight_arg in (attn_gain, w_query, w_key, w_value, w_out, ffn_gain, w_gate, w_up, w_down)))

    def forward(inputs_all, weight_set):

        def one_seq(seq_in):
            return layer(seq_in, *weight_set)
        return lax.map(jax.checkpoint(one_seq), inputs_all)
    outputs, pullback = jax.vjp(forward, inputs, params)
    grad_in, grad_weights = pullback(cotangent.astype(jnp.float32).reshape(N_REPLICA, seq_rows, D))
    return (outputs.reshape(-1, D).astype(jnp.bfloat16), grad_in.reshape(-1, D), grad_weights[0], grad_weights[1], grad_weights[2], grad_weights[3], grad_weights[4], grad_weights[5], grad_weights[6], grad_weights[7], grad_weights[8])
```

```python
import functools

import jax
import jax.numpy as jnp
from jax import lax
from jax.experimental import pallas as pl
from jax.experimental.pallas import tpu as pltpu
from jax.sharding import PartitionSpec as P

HEAD_DIM = 64

eps_norm = 1e-05
rope_base = 130000.0
masked_score = -1e30


def rms_factor(values):
    return lax.rsqrt(jnp.mean(values * values, axis=-1, keepdims=True) + eps_norm)


def rope_tables(row_count, width):
    lane = jnp.arange(width, dtype=jnp.int32) % HEAD_DIM
    halfway = HEAD_DIM // 2
    spacing = (lane % halfway).astype(jnp.float32) * 2.0 / HEAD_DIM
    frequency = rope_base ** (-spacing)
    positions = jnp.arange(row_count, dtype=jnp.int32).astype(jnp.float32)
    angles = positions[:, None] * frequency[None, :]
    sign = jnp.where(lane < halfway, -1.0, 1.0)
    return jnp.cos(angles), jnp.sin(angles) * sign[None, :]


def partner(values):
    halfway = HEAD_DIM // 2
    lane = lax.broadcasted_iota(jnp.int32, (1, values.shape[1]), 1) % HEAD_DIM
    return jnp.where(
        lane < halfway, jnp.roll(values, -halfway, axis=1), jnp.roll(values, halfway, axis=1)
    )


def dot(left, right):
    return jnp.dot(left, right, preferred_element_type=jnp.float32)


def contract_last(left, right):
    return lax.dot_general(
        left, right, (((1,), (1,)), ((), ())), preferred_element_type=jnp.float32
    )


def contract_first(left, right):
    return lax.dot_general(
        left, right, (((0,), (0,)), ((), ())), preferred_element_type=jnp.float32
    )


def scores_of(queries, keys, first_row):
    rows, columns = queries.shape[0], keys.shape[0]
    scores = contract_last(queries, keys) * HEAD_DIM**-0.5
    at_row = lax.broadcasted_iota(jnp.int32, (rows, columns), 0) + first_row
    at_column = lax.broadcasted_iota(jnp.int32, (rows, columns), 1)
    return jnp.where(at_column <= at_row, scores, masked_score)


def attend_kernel(block, q_ref, k_ref, v_ref, out_ref, log_ref):
    rows = q_ref.shape[0]
    for first in range(0, rows, block):
        here = pl.ds(first, block)
        seen = pl.ds(0, first + block)
        mixed = []
        for at in range(0, q_ref.shape[1], HEAD_DIM):
            head = pl.ds(at, HEAD_DIM)
            scores = scores_of(q_ref[here, head], k_ref[seen, head], first)
            most = jnp.max(scores, axis=-1, keepdims=True)
            weights = jnp.exp(scores - most)
            total = jnp.sum(weights, axis=-1, keepdims=True)
            low = (weights / total).astype(jnp.bfloat16)
            mixed.append(dot(low, v_ref[seen, head]))
            log_ref[here, head] = jnp.broadcast_to(most + jnp.log(total), (block, HEAD_DIM))
        out_ref[here, :] = jnp.concatenate(mixed, axis=1).astype(out_ref.dtype)


def attend(queries, keys, values, block=256):
    rows, width = queries.shape
    pair = 2 * HEAD_DIM
    spec = pl.BlockSpec((rows, pair), lambda i: (0, i))
    return pl.pallas_call(
        functools.partial(attend_kernel, block),
        grid=(width // pair,),
        in_specs=[spec] * 3,
        out_specs=[spec] * 2,
        out_shape=[
            jax.ShapeDtypeStruct((rows, width), jnp.bfloat16),
            jax.ShapeDtypeStruct((rows, width), jnp.float32),
        ],
        compiler_params=pltpu.CompilerParams(vmem_limit_bytes=48 * 2**20),
        cost_estimate=pl.CostEstimate(
            flops=2 * 2 * rows * rows * width, bytes_accessed=12 * rows * width, transcendentals=rows * rows * 4
        ),
        name="attend",
    )(queries, keys, values)


def attend_back_kernel(block, q_ref, k_ref, v_ref, g_ref, log_ref, gq_ref, gk_ref, gv_ref):
    rows = q_ref.shape[0]
    scale = HEAD_DIM**-0.5
    gk_ref[...] = jnp.zeros_like(gk_ref)
    gv_ref[...] = jnp.zeros_like(gv_ref)
    for first in range(0, rows, block):
        here = pl.ds(first, block)
        seen = pl.ds(0, first + block)
        for_queries, for_keys, for_values = [], [], []
        for at in range(0, q_ref.shape[1], HEAD_DIM):
            head = pl.ds(at, HEAD_DIM)
            queries, grads = q_ref[here, head], g_ref[here, head]
            keys = k_ref[seen, head]
            scores = scores_of(queries, keys, first)
            weights = jnp.exp(scores - log_ref[here, at : at + 1])
            grad_weights = contract_last(grads, v_ref[seen, head])
            delta = jnp.sum(weights * grad_weights, axis=-1, keepdims=True)
            grad_scores = (weights * (grad_weights - delta)).astype(jnp.bfloat16)
            for_queries.append(dot(grad_scores, keys))
            for_keys.append(contract_first(grad_scores, queries))
            for_values.append(contract_first(weights.astype(jnp.bfloat16), grads))
        gq_ref[here, :] = jnp.concatenate(for_queries, axis=1) * scale
        gk_ref[seen, :] += jnp.concatenate(for_keys, axis=1) * scale
        gv_ref[seen, :] += jnp.concatenate(for_values, axis=1)


def attend_back(queries, keys, values, grads, logs, block=256):
    rows, width = queries.shape
    pair = 2 * HEAD_DIM
    spec = pl.BlockSpec((rows, pair), lambda i: (0, i))
    return pl.pallas_call(
        functools.partial(attend_back_kernel, block),
        grid=(width // pair,),
        in_specs=[spec] * 5,
        out_specs=[spec] * 3,
        out_shape=[jax.ShapeDtypeStruct((rows, width), jnp.float32)] * 3,
        compiler_params=pltpu.CompilerParams(vmem_limit_bytes=48 * 2**20),
        cost_estimate=pl.CostEstimate(
            flops=5 * 2 * rows * rows * width, bytes_accessed=24 * rows * width, transcendentals=rows * rows * 4
        ),
        name="attend_back",
    )(queries, keys, values, grads, logs)


def gather(values):
    return lax.all_gather(values, "fsdp", axis=0, tiled=True)


def scatter(partial):
    return lax.psum_scatter(
        partial.astype(jnp.bfloat16), "fsdp", scatter_dimension=0, tiled=True
    ).astype(jnp.float32)


def columns_of(shard):
    return lax.all_to_all(shard, "fsdp", split_axis=1, concat_axis=0, tiled=True)


def rows_of(slab):
    fsdp, replica = lax.axis_size("fsdp"), lax.axis_size("replica")
    height, width = slab.shape
    pieces = slab.astype(jnp.bfloat16).reshape(fsdp, replica, -1, width).transpose(1, 0, 2, 3)
    mine = lax.psum_scatter(pieces.reshape(height, width), "replica", scatter_dimension=0, tiled=True)
    mine = mine.reshape(fsdp, -1, width)
    swapped = lax.all_to_all(mine, "fsdp", split_axis=0, concat_axis=0, tiled=True)
    return lax.all_gather(swapped, "replica", axis=0, tiled=False)


def laid_out(pieces):
    replica, fsdp, rows, width = pieces.shape
    return pieces.transpose(0, 2, 1, 3).reshape(replica * rows, fsdp * width).astype(jnp.float32)


def local(
    tokens, attn_gain, w_query, w_key, w_value, w_out, ffn_gain, w_gate, w_up, w_down, cotangent
):
    fsdp_count = lax.axis_size("fsdp")
    gains = lax.all_gather(jnp.stack([attn_gain, ffn_gain]), "fsdp", axis=1, tiled=True)
    gain_one = gains[0].astype(jnp.float32)
    gain_two = gains[1].astype(jnp.float32)
    inputs = tokens.astype(jnp.float32)
    factor_one = rms_factor(inputs)
    normed_one = inputs * factor_one
    lowered_one = gather((normed_one * gain_one).astype(jnp.bfloat16))
    slab_query, slab_key, slab_value = columns_of(w_query), columns_of(w_key), columns_of(w_value)
    slab_gate, slab_up = columns_of(w_gate), columns_of(w_up)
    cosine, sine = rope_tables(lowered_one.shape[0], slab_query.shape[1])

    def rotate(values):
        return (values * cosine + partner(values) * sine).astype(jnp.bfloat16)

    def rotate_back(values):
        return (values * cosine - partner(values) * sine).astype(jnp.bfloat16)

    queries = rotate(dot(lowered_one, slab_query))
    keys = rotate(dot(lowered_one, slab_key))
    values = dot(lowered_one, slab_value).astype(jnp.bfloat16)
    attended, logs = attend(queries, keys, values)
    after_attn = inputs + scatter(dot(attended, w_out))
    factor_two = rms_factor(after_attn)
    normed_two = after_attn * factor_two
    lowered_two = gather((normed_two * gain_two).astype(jnp.bfloat16))
    cotangents = gather(cotangent)
    gate = dot(lowered_two, slab_gate)
    up = dot(lowered_two, slab_up)
    sigmoid = jax.nn.sigmoid(gate)
    silu = gate * sigmoid
    hidden = (silu * up).astype(jnp.bfloat16)
    grad_hidden = contract_last(cotangents, w_down)
    grad_gate = (grad_hidden * up * sigmoid * (1.0 + gate * (1.0 - sigmoid))).astype(jnp.bfloat16)
    grad_up = (grad_hidden * silu).astype(jnp.bfloat16)
    grad_normed_two = scatter(contract_last(grad_gate, slab_gate) + contract_last(grad_up, slab_up))
    outputs = (after_attn + scatter(dot(hidden, w_down))).astype(jnp.bfloat16)
    gain_two_term = jnp.sum(grad_normed_two * normed_two, axis=0)
    scaled_two = grad_normed_two * gain_two
    grad_after = cotangent.astype(jnp.float32) + factor_two * (
        scaled_two - normed_two * jnp.mean(scaled_two * normed_two, axis=-1, keepdims=True)
    )
    grad_branch = gather(grad_after.astype(jnp.bfloat16))
    grad_attended = contract_last(grad_branch, w_out).astype(jnp.bfloat16)
    grad_query, grad_key, grad_value = attend_back(queries, keys, values, grad_attended, logs)
    grad_query, grad_key = rotate_back(grad_query), rotate_back(grad_key)
    grad_value = grad_value.astype(jnp.bfloat16)
    grad_normed_one = scatter(
        contract_last(grad_query, slab_query)
        + contract_last(grad_key, slab_key)
        + contract_last(grad_value, slab_value)
    )
    gain_one_term = jnp.sum(grad_normed_one * normed_one, axis=0)
    scaled_one = grad_normed_one * gain_one
    grad_tokens = grad_after + factor_one * (
        scaled_one - normed_one * jnp.mean(scaled_one * normed_one, axis=-1, keepdims=True)
    )
    gain_terms = lax.psum(jnp.stack([gain_one_term, gain_two_term]), ("replica", "fsdp"))
    width = attn_gain.shape[0]
    gain_grads = lax.dynamic_slice_in_dim(gain_terms, lax.axis_index("fsdp") * width, width, 1)

    def over_replicas(left, right):
        return lax.psum(contract_first(left, right).astype(jnp.bfloat16), "replica").astype(jnp.float32)

    grad_w_down = over_replicas(hidden, cotangents)
    grad_w_out = over_replicas(attended, grad_branch)
    ffn_pieces = rows_of(contract_first(lowered_two, jnp.concatenate([grad_gate, grad_up], axis=1)))
    half = ffn_pieces.shape[-1] // 2
    grad_w_gate, grad_w_up = laid_out(ffn_pieces[..., :half]), laid_out(ffn_pieces[..., half:])
    attn_pieces = rows_of(
        contract_first(lowered_one, jnp.concatenate([grad_query, grad_key, grad_value], axis=1))
    )
    third = attn_pieces.shape[-1] // 3
    grad_w_query, grad_w_key, grad_w_value = [
        laid_out(attn_pieces[..., i * third : (i + 1) * third]) for i in range(3)
    ]
    return (
        outputs,
        grad_tokens,
        gain_grads[0],
        grad_w_query,
        grad_w_key,
        grad_w_value,
        grad_w_out,
        gain_grads[1],
        grad_w_gate,
        grad_w_up,
        grad_w_down,
    )


def solution(mesh):
    rows = P("fsdp", None)
    tokens = P(("replica", "fsdp"), None)
    gain = P("fsdp")
    return jax.shard_map(
        local,
        mesh=mesh,
        in_specs=(tokens, gain, rows, rows, rows, rows, gain, rows, rows, rows, tokens),
        out_specs=(tokens, tokens, gain, rows, rows, rows, rows, gain, rows, rows, rows),
        check_vma=False,
    )
```

```python
import functools

import jax
import jax.numpy as jnp
import numpy as np
from jax import lax
from jax.experimental import pallas as pl
from jax.experimental.pallas import tpu as pltpu
from jax.sharding import PartitionSpec as P

HEAD_DIM = 64

eps_norm = 1e-05
rope_base = 130000.0
masked_score = -1e30


def rms_factor(values):
    return lax.rsqrt(jnp.mean(values * values, axis=-1, keepdims=True) + eps_norm)


def rope_tables(row_count):
    lane = np.arange(2 * HEAD_DIM) % HEAD_DIM
    halfway = HEAD_DIM // 2
    spacing = ((lane % halfway) * np.float32(2.0) / HEAD_DIM).astype(np.float32)
    frequency = np.power(np.float32(rope_base), -spacing)
    angles = np.arange(row_count, dtype=np.float32)[:, None] * frequency[None, :]
    sign = np.where(lane < halfway, -1.0, 1.0).astype(np.float32)
    return np.cos(angles).astype(np.float32), (np.sin(angles) * sign[None, :]).astype(np.float32)


def dot(left, right):
    return jnp.dot(left, right, preferred_element_type=jnp.float32)


def contract_last(left, right):
    return lax.dot_general(
        left, right, (((1,), (1,)), ((), ())), preferred_element_type=jnp.float32
    )


def contract_first(left, right):
    return lax.dot_general(
        left, right, (((0,), (0,)), ((), ())), preferred_element_type=jnp.float32
    )


def scores_of(queries, keys, first_row):
    rows, columns = queries.shape[0], keys.shape[0]
    scores = contract_last(queries, keys) * HEAD_DIM**-0.5
    at_row = lax.broadcasted_iota(jnp.int32, (rows, columns), 0) + first_row
    at_column = lax.broadcasted_iota(jnp.int32, (rows, columns), 1)
    return jnp.where(at_column <= at_row, scores, masked_score)


MESH = pl.DeviceIdType.MESH
VMEM_LIMIT = 60 * 2**20


def remote(src, dst, send, recv, **where):
    return pltpu.make_async_remote_copy(
        src_ref=src, dst_ref=dst, send_sem=send, recv_sem=recv, device_id=where, device_id_type=MESH
    )


def await_bytes(ref, sem):
    pltpu.make_async_copy(ref, ref, sem).wait()


def rows_at(ref, index, size):
    return ref.at[pl.ds(pl.multiple_of(index * size, size), size)]


class Place:
    def __init__(self):
        self.fsdp, self.replicas = lax.axis_size("fsdp"), lax.axis_size("replica")
        self.me, self.replica = lax.axis_index("fsdp"), lax.axis_index("replica")
        self.chips = self.fsdp // 2
        self.chip, self.core = self.me // 2, self.me % 2
        self.sibling = self.me + 1 - 2 * self.core
        self.above = self.chip + 1 < self.chips
        self.below = self.chip >= 1

    def enter(self):
        barrier = pltpu.get_barrier_semaphore()

        def greet(k, _):
            to = lax.rem(self.me + k, self.fsdp)
            pl.semaphore_signal(barrier, inc=1, device_id={"fsdp": to}, device_id_type=MESH)
            return 0

        def greet_replica(k, _):
            to = lax.rem(self.replica + k, self.replicas)
            pl.semaphore_signal(barrier, inc=1, device_id={"replica": to}, device_id_type=MESH)
            return 0

        lax.fori_loop(1, self.fsdp, greet, 0)
        lax.fori_loop(1, self.replicas, greet_replica, 0)
        pl.semaphore_wait(barrier, self.fsdp - 1 + self.replicas - 1)


def line_sems(chips):
    dma = pltpu.SemaphoreType.DMA
    return [dma((chips,)), dma((chips,)), dma((chips,)), dma((chips,)), dma((chips,)), dma(())]


class Gather:
    def __init__(self, place, buf, block, sems):
        self.p, self.buf, self.block = place, buf, block
        self.up_out, self.up_in, self.down_out, self.down_in, self.side_out, self.side_in = sems

    def held(self, chip):
        return rows_at(self.buf, 2 * chip + self.p.core, self.block)

    def up(self, step):
        ref = self.held(self.p.chip - step + 1)
        return remote(ref, ref, self.up_out.at[step], self.up_in.at[step], fsdp=self.p.me + 2)

    def down(self, step):
        ref = self.held(self.p.chip + step - 1)
        return remote(ref, ref, self.down_out.at[step], self.down_in.at[step], fsdp=self.p.me - 2)

    def side(self, chip):
        ref = self.held(chip)
        return remote(ref, ref, self.side_out.at[chip], self.side_in, fsdp=self.p.sibling)

    def start(self):
        p = self.p
        pl.when(p.above)(lambda: self.up(1).start())
        pl.when(p.below)(lambda: self.down(1).start())
        self.side(p.chip).start()

    def step(self, step):
        p = self.p
        from_below, from_above = p.chip - step, p.chip + step

        @pl.when(from_below >= 0)
        def _():
            await_bytes(self.held(from_below), self.up_in.at[step])
            if step + 1 < p.chips:
                pl.when(p.above)(lambda: self.up(step + 1).start())
            self.side(from_below).start()

        @pl.when(from_above < p.chips)
        def _():
            await_bytes(self.held(from_above), self.down_in.at[step])
            if step + 1 < p.chips:
                pl.when(p.below)(lambda: self.down(step + 1).start())
            self.side(from_above).start()

    def finish(self):
        p = self.p
        await_bytes(self.buf.at[pl.ds(0, p.chips * self.block)], self.side_in)
        for step in range(1, p.chips):
            pl.when(jnp.logical_and(p.above, p.chip - step + 1 >= 0))(
                lambda step=step: self.up(step).wait_send()
            )
            pl.when(jnp.logical_and(p.below, p.chip + step - 1 < p.chips))(
                lambda step=step: self.down(step).wait_send()
            )
        for chip in range(p.chips):
            self.side(chip).wait_send()

    def run(self):
        self.start()
        for step in range(1, self.p.chips):
            self.step(step)
        self.finish()


class Scatter:
    def __init__(self, place, terms, across, from_below, from_above, block, sems):
        self.p, self.terms, self.across, self.block = place, terms, across, block
        self.from_below, self.from_above = from_below, from_above
        self.up_out, self.up_in, self.down_out, self.down_in, self.side_out, self.side_in = sems

    def side(self, chip):
        p = self.p
        return remote(
            rows_at(self.terms, 2 * chip + 1 - p.core, self.block),
            rows_at(self.across, chip, self.block),
            self.side_out.at[chip],
            self.side_in.at[chip],
            fsdp=p.sibling,
        )

    def term(self, chip):
        return rows_at(self.terms, 2 * chip + self.p.core, self.block)

    def up(self, step):
        return remote(
            self.term(self.p.chips - step + self.p.chip),
            self.from_below.at[step - 1],
            self.up_out.at[step],
            self.up_in.at[step],
            fsdp=self.p.me + 2,
        )

    def down(self, step):
        return remote(
            self.term(self.p.chip - self.p.chips + step),
            self.from_above.at[step - 1],
            self.down_out.at[step],
            self.down_in.at[step],
            fsdp=self.p.me - 2,
        )

    def add(self, chip, arrived):
        term = self.term(chip)
        term[...] = (term[...].astype(jnp.float32) + arrived[...].astype(jnp.float32)).astype(term.dtype)

    def cross(self, chip):
        arrived = rows_at(self.across, chip, self.block)
        await_bytes(arrived, self.side_in.at[chip])
        self.add(chip, arrived)

    def step(self, step):
        p = self.p
        rising, falling = p.chips - step + p.chip, p.chip - p.chips + step

        @pl.when(jnp.logical_and(p.above, rising < p.chips))
        def _():
            if step > 1:

                @pl.when(p.below)
                def _():
                    arrived = self.from_below.at[step - 2]
                    await_bytes(arrived, self.up_in.at[step - 1])
                    self.add(rising, arrived)

            self.up(step).start()

        @pl.when(jnp.logical_and(p.below, falling >= 0))
        def _():
            if step > 1:

                @pl.when(p.above)
                def _():
                    arrived = self.from_above.at[step - 2]
                    await_bytes(arrived, self.down_in.at[step - 1])
                    self.add(falling, arrived)

            self.down(step).start()

    def finish(self, total):
        p, last = self.p, self.p.chips - 1
        total[...] = self.term(p.chip)[...].astype(jnp.float32)

        @pl.when(p.below)
        def _():
            await_bytes(self.from_below.at[last - 1], self.up_in.at[last])
            total[...] += self.from_below[last - 1].astype(jnp.float32)

        @pl.when(p.above)
        def _():
            await_bytes(self.from_above.at[last - 1], self.down_in.at[last])
            total[...] += self.from_above[last - 1].astype(jnp.float32)

    def drain(self):
        p = self.p
        for step in range(1, p.chips):
            pl.when(jnp.logical_and(p.above, p.chips - step + p.chip < p.chips))(
                lambda step=step: self.up(step).wait_send()
            )
            pl.when(jnp.logical_and(p.below, p.chip - p.chips + step >= 0))(
                lambda step=step: self.down(step).wait_send()
            )
        for chip in range(p.chips):
            self.side(chip).wait_send()


def scatter_sems(chips):
    dma = pltpu.SemaphoreType.DMA
    return [dma((chips,))] * 6


class Turn:
    def __init__(self, place, weight, slab, first, sems):
        self.p, self.weight, self.slab, self.first = place, weight, slab, first
        self.far_out, self.far_in, self.near_out, self.near_in, self.pass_out, self.pass_in, self.own = sems
        self.height, self.width = weight.shape[0], slab.shape[1]
        self.share = self.height // place.replicas

    def far_rows(self):
        return (self.p.fsdp - 2) * self.share

    def piece(self, block, share):
        at = self.first + block * self.height + share * self.share
        return self.slab.at[pl.ds(pl.multiple_of(at, self.share), self.share)]

    def whole(self, block):
        at = self.first + block * self.height
        return self.slab.at[pl.ds(pl.multiple_of(at, self.height), self.height)]

    def columns(self, to):
        return pl.ds(pl.multiple_of(to * self.width, self.width), self.width)

    def start(self):
        p = self.p

        def send(k, _):
            to = lax.rem(2 * p.chip + 2 + k, p.fsdp)
            share = pl.ds(pl.multiple_of(p.replica * self.share, self.share), self.share)
            remote(
                self.weight.at[share, self.columns(to)],
                self.piece(p.me, p.replica),
                self.far_out,
                self.far_in,
                fsdp=to,
            ).start()
            return 0

        lax.fori_loop(0, p.fsdp - 2, send, 0)
        self.near().start()
        self.mine().start()

    def near(self):
        p = self.p
        return remote(
            self.weight.at[:, self.columns(p.sibling)], self.whole(p.me), self.near_out, self.near_in, fsdp=p.sibling
        )

    def mine(self):
        return pltpu.make_async_copy(self.weight.at[:, self.columns(self.p.me)], self.whole(self.p.me), self.own)

    def await_far(self):
        await_bytes(self.slab.at[pl.ds(0, self.far_rows())], self.far_in)

    def pass_on(self):
        p = self.p

        def one(k, _):
            ref = self.piece(lax.rem(2 * p.chip + 2 + k, p.fsdp), p.replica)

            def send(j, _):
                remote(
                    ref, ref, self.pass_out, self.pass_in, replica=lax.rem(p.replica + j, p.replicas)
                ).start()
                return 0

            return lax.fori_loop(1, p.replicas, send, 0)

        lax.fori_loop(0, p.fsdp - 2, one, 0)

    def finish(self):
        p = self.p
        passed = self.slab.at[pl.ds(0, (p.replicas - 1) * self.far_rows())]
        await_bytes(passed, self.pass_in)
        await_bytes(self.whole(p.sibling), self.near_in)
        self.mine().wait()

    def drain(self):
        p = self.p
        await_bytes(self.slab.at[pl.ds(0, self.far_rows())], self.far_out)
        self.near().wait_send()
        await_bytes(self.slab.at[pl.ds(0, (p.replicas - 1) * self.far_rows())], self.pass_out)


def turn_sems():
    return [pltpu.SemaphoreType.DMA(())] * 7


def partner(values):
    halfway = HEAD_DIM // 2
    width = values.shape[1]
    lane = lax.broadcasted_iota(jnp.int32, values.shape, 1) % HEAD_DIM
    return jnp.where(
        lane < halfway,
        pltpu.roll(values, width - halfway, axis=1),
        pltpu.roll(values, halfway, axis=1),
    )


def front_kernel(
    tokens,
    gain_one,
    gain_two,
    w_query,
    w_key,
    w_value,
    w_out,
    w_gate,
    w_up,
    cosine,
    sine,
    lowered_one_out,
    lowered_two_out,
    slab_qkv_out,
    slab_gate,
    slab_up,
    queries,
    keys,
    values,
    attended,
    logs,
    after_attn,
    gains,
    lowered_one,
    lowered_two,
    slab_qkv,
    terms,
    across,
    from_below,
    from_above,
    gain_rows,
    gain_out,
    gain_in,
    copy_sems,
    *sems,
):
    place = Place()
    chips, block = place.chips, tokens.shape[0]
    model, width = tokens.shape[1], queries.shape[1]
    share = gain_one.shape[1]
    rows = chips * 2 * block
    one_sems, two_sems, scatter_at = sems[:6], sems[6:12], sems[12:18]
    turn_at = [sems[18 + 7 * i : 25 + 7 * i] for i in range(5)]
    turns = [
        Turn(place, weight, slab_qkv, i * model, turn_at[i])
        for i, weight in enumerate((w_query, w_key, w_value))
    ]
    late = [Turn(place, w_gate, slab_gate, 0, turn_at[3]), Turn(place, w_up, slab_up, 0, turn_at[4])]

    gain_rows[...] = jnp.zeros_like(gain_rows)
    gain_rows[0:1, :] = gain_one[...].astype(jnp.float32)
    gain_rows[1:2, :] = gain_two[...].astype(jnp.float32)
    place.enter()

    def send_gains(k, _):
        to = lax.rem(place.me + k, place.fsdp)
        remote(gain_rows, gains.at[place.me], gain_out, gain_in, fsdp=to).start()
        return 0

    lax.fori_loop(1, place.fsdp, send_gains, 0)
    for turn in turns:
        turn.start()
    gains[place.me] = gain_rows[...]
    inputs = tokens[...].astype(jnp.float32)
    factor = lax.rsqrt(jnp.mean(inputs * inputs, axis=-1, keepdims=True) + eps_norm)
    await_bytes(gains.at[pl.ds(0, place.fsdp - 1)], gain_in)
    here = pl.ds(pl.multiple_of(place.me * block, block), block)
    for j in range(model // share):
        at = pl.ds(j * share, share)
        normed = tokens[:, at].astype(jnp.float32) * factor
        lowered_one[here, at] = (normed * gains[j, 0:1, :]).astype(jnp.bfloat16)
    first = Gather(place, lowered_one, block, one_sems)
    first.start()
    for turn in turns:
        turn.await_far()
        turn.pass_on()
    late[0].start()
    late[1].start()
    for step in range(1, chips):
        first.step(step)
    first.finish()
    keep_one = pltpu.make_async_copy(lowered_one, lowered_one_out, copy_sems.at[0])
    keep_one.start()
    for turn in turns:
        turn.finish()
    keep_slab = pltpu.make_async_copy(slab_qkv, slab_qkv_out, copy_sems.at[1])
    keep_slab.start()

    tile = 2 * block

    def project(t, _):
        at = pl.ds(pl.multiple_of(t * tile, tile), tile)
        left = lowered_one[at, :]
        for i, ref in enumerate((queries, keys, values)):
            out = dot(left, slab_qkv[i * model : (i + 1) * model, :])
            if i < 2:
                for j in range(0, width, 2 * HEAD_DIM):
                    pair = out[:, j : j + 2 * HEAD_DIM]
                    pair = pair * cosine[at, :] + partner(pair) * sine[at, :]
                    ref[at, j : j + 2 * HEAD_DIM] = pair.astype(jnp.bfloat16)
            else:
                ref[at, :] = out.astype(jnp.bfloat16)
        return 0

    lax.fori_loop(0, chips, project, 0)
    late[0].await_far()
    late[0].pass_on()
    scatter = Scatter(place, terms, across, from_below, from_above, block, scatter_at)
    pair = 2 * HEAD_DIM
    for t in range(chips):
        here_t, seen = pl.ds(t * tile, tile), pl.ds(0, (t + 1) * tile)

        def heads(h, _, t=t, here_t=here_t, seen=seen):
            lanes = pl.ds(pl.multiple_of(h * pair, pair), pair)
            q2, k2, v2 = queries[here_t, lanes], keys[seen, lanes], values[seen, lanes]
            mixed, stats = [], []
            for at in (0, HEAD_DIM):
                head = slice(at, at + HEAD_DIM)
                scores = scores_of(q2[:, head], k2[:, head], t * tile)
                most = jnp.max(scores, axis=-1, keepdims=True)
                weights = jnp.exp(scores - most)
                total = jnp.sum(weights, axis=-1, keepdims=True)
                mixed.append(dot((weights / total).astype(jnp.bfloat16), v2[:, head]))
                stats.append(jnp.broadcast_to(most + jnp.log(total), (tile, HEAD_DIM)))
            attended[here_t, lanes] = jnp.concatenate(mixed, axis=1).astype(jnp.bfloat16)
            logs[here_t, lanes] = jnp.concatenate(stats, axis=1)
            return 0

        lax.fori_loop(0, width // pair, heads, 0)
        terms[here_t, :] = dot(attended[here_t, :], w_out[...]).astype(jnp.bfloat16)
        scatter.side(t).start()
    late[1].await_far()
    late[1].pass_on()
    for t in range(chips):
        scatter.cross(t)
    for step in range(1, chips):
        scatter.step(step)
    scatter.finish(after_attn)
    after_attn[...] += tokens[...].astype(jnp.float32)
    after = after_attn[...]
    factor = lax.rsqrt(jnp.mean(after * after, axis=-1, keepdims=True) + eps_norm)
    for j in range(model // share):
        at = pl.ds(j * share, share)
        normed = after_attn[:, at] * factor
        lowered_two[here, at] = (normed * gains[j, 1:2, :]).astype(jnp.bfloat16)
    second = Gather(place, lowered_two, block, two_sems)
    second.run()
    keep_two = pltpu.make_async_copy(lowered_two, lowered_two_out, copy_sems.at[2])
    keep_two.start()
    for turn in late:
        turn.finish()
    scatter.drain()
    for turn in turns + late:
        turn.drain()
    await_bytes(gains.at[pl.ds(0, place.fsdp - 1)], gain_out)
    keep_one.wait()
    keep_slab.wait()
    keep_two.wait()


def front(tokens, gain_one, gain_two, w_query, w_key, w_value, w_out, w_gate, w_up, cosine, sine):
    fsdp = lax.axis_size("fsdp")
    chips = fsdp // 2
    block, model = tokens.shape
    rows, width, wide = fsdp * block, w_query.shape[1] // fsdp, w_gate.shape[1] // fsdp
    share = gain_one.shape[0]
    low, full = jnp.bfloat16, jnp.float32
    hbm, vmem = pl.BlockSpec(memory_space=pl.ANY), pl.BlockSpec(memory_space=pltpu.VMEM)
    shape = jax.ShapeDtypeStruct
    return pl.pallas_call(
        front_kernel,
        in_specs=[vmem] * 3 + [hbm] * 3 + [vmem] + [hbm] * 2 + [vmem] * 2,
        out_specs=[hbm] * 5 + [vmem] * 7,
        out_shape=[
            shape((rows, model), low),
            shape((rows, model), low),
            shape((3 * model, width), low),
            shape((model, wide), low),
            shape((model, wide), low),
            shape((rows, width), low),
            shape((rows, width), low),
            shape((rows, width), low),
            shape((rows, width), low),
            shape((rows, width), full),
            shape((block, model), full),
            shape((fsdp, 8, share), full),
        ],
        scratch_shapes=[
            pltpu.VMEM((rows, model), low),
            pltpu.VMEM((rows, model), low),
            pltpu.VMEM((3 * model, width), low),
            pltpu.VMEM((rows, model), low),
            pltpu.VMEM((chips * block, model), low),
            pltpu.VMEM((chips - 1, block, model), low),
            pltpu.VMEM((chips - 1, block, model), low),
            pltpu.VMEM((8, share), full),
            pltpu.SemaphoreType.DMA(()),
            pltpu.SemaphoreType.DMA(()),
            pltpu.SemaphoreType.DMA((3,)),
        ]
        + line_sems(chips)
        + line_sems(chips)
        + scatter_sems(chips)
        + turn_sems() * 5,
        compiler_params=pltpu.CompilerParams(
            collective_id=0, has_side_effects=True, vmem_limit_bytes=VMEM_LIMIT
        ),
        name="front",
    )(
        tokens,
        gain_one.reshape(1, -1),
        gain_two.reshape(1, -1),
        w_query,
        w_key,
        w_value,
        w_out,
        w_gate,
        w_up,
        cosine,
        sine,
    )


def middle_kernel(low_ref, cot_ref, gate_ref, up_ref, down_ref, hidden_ref, grad_gate_ref, grad_up_ref):
    tile = 256

    def rows(t, _):
        at = pl.ds(pl.multiple_of(t * tile, tile), tile)
        gate = dot(low_ref[at, :], gate_ref[...])
        up = dot(low_ref[at, :], up_ref[...])
        grad_hidden = contract_last(cot_ref[at, :], down_ref[...])
        sigmoid = jax.nn.sigmoid(gate)
        silu = gate * sigmoid
        hidden_ref[at, :] = (silu * up).astype(jnp.bfloat16)
        grad_gate_ref[at, :] = (
            grad_hidden * up * sigmoid * (1.0 + gate * (1.0 - sigmoid))
        ).astype(jnp.bfloat16)
        grad_up_ref[at, :] = (grad_hidden * silu).astype(jnp.bfloat16)
        return 0

    lax.fori_loop(0, low_ref.shape[0] // tile, rows, 0)


def middle(lowered_two, cotangents, slab_gate, slab_up, w_down):
    rows, model = lowered_two.shape
    wide = slab_gate.shape[1]
    block = 256
    whole = pl.BlockSpec((rows, model), lambda i: (0, 0), pipeline_mode=pl.Buffered(1))
    columns = pl.BlockSpec((model, block), lambda i: (0, i))
    out = pl.BlockSpec((rows, block), lambda i: (0, i))
    return pl.pallas_call(
        middle_kernel,
        grid=(wide // block,),
        in_specs=[whole, whole, columns, columns, pl.BlockSpec((block, model), lambda i: (i, 0))],
        out_specs=[out] * 3,
        out_shape=[jax.ShapeDtypeStruct((rows, wide), jnp.bfloat16)] * 3,
        compiler_params=pltpu.CompilerParams(vmem_limit_bytes=VMEM_LIMIT),
        cost_estimate=pl.CostEstimate(
            flops=6 * rows * model * wide, bytes_accessed=4 * rows * model + 6 * model * wide, transcendentals=rows * wide
        ),
        name="middle",
    )(lowered_two, cotangents, slab_gate, slab_up, w_down)


def attend_back_kernel(block, q_ref, k_ref, v_ref, g_ref, log_ref, gq_ref, gk_ref, gv_ref):
    rows = q_ref.shape[0]
    scale = HEAD_DIM**-0.5
    gk_ref[...] = jnp.zeros_like(gk_ref)
    gv_ref[...] = jnp.zeros_like(gv_ref)
    for first in range(0, rows, block):
        here = pl.ds(first, block)
        seen = pl.ds(0, first + block)
        for_queries, for_keys, for_values = [], [], []
        for at in range(0, q_ref.shape[1], HEAD_DIM):
            head = pl.ds(at, HEAD_DIM)
            queries, grads = q_ref[here, head], g_ref[here, head]
            keys = k_ref[seen, head]
            scores = scores_of(queries, keys, first)
            weights = jnp.exp(scores - log_ref[here, at : at + 1])
            grad_weights = contract_last(grads, v_ref[seen, head])
            delta = jnp.sum(weights * grad_weights, axis=-1, keepdims=True)
            grad_scores = (weights * (grad_weights - delta)).astype(jnp.bfloat16)
            for_queries.append(dot(grad_scores, keys))
            for_keys.append(contract_first(grad_scores, queries))
            for_values.append(contract_first(weights.astype(jnp.bfloat16), grads))
        gq_ref[here, :] = jnp.concatenate(for_queries, axis=1) * scale
        gk_ref[seen, :] += jnp.concatenate(for_keys, axis=1) * scale
        gv_ref[seen, :] += jnp.concatenate(for_values, axis=1)


def attend_back(queries, keys, values, grads, logs, block=256):
    rows, width = queries.shape
    pair = 2 * HEAD_DIM
    spec = pl.BlockSpec((rows, pair), lambda i: (0, i))
    return pl.pallas_call(
        functools.partial(attend_back_kernel, block),
        grid=(width // pair,),
        in_specs=[spec] * 5,
        out_specs=[spec] * 3,
        out_shape=[jax.ShapeDtypeStruct((rows, width), jnp.float32)] * 3,
        compiler_params=pltpu.CompilerParams(vmem_limit_bytes=48 * 2**20),
        cost_estimate=pl.CostEstimate(
            flops=5 * 2 * rows * rows * width, bytes_accessed=24 * rows * width, transcendentals=rows * rows * 4
        ),
        name="attend_back",
    )(queries, keys, values, grads, logs)


def rotate_back(values, cosine, sine):
    halfway = HEAD_DIM // 2
    turns = values.shape[1] // cosine.shape[1]
    lane = lax.broadcasted_iota(jnp.int32, (1, values.shape[1]), 1) % HEAD_DIM
    other = jnp.where(
        lane < halfway, jnp.roll(values, -halfway, axis=1), jnp.roll(values, halfway, axis=1)
    )
    cosine, sine = jnp.tile(cosine, (1, turns)), jnp.tile(sine, (1, turns))
    return (values * cosine - other * sine).astype(jnp.bfloat16)


def gather(values):
    return lax.all_gather(values, "fsdp", axis=0, tiled=True)


def scatter(partial):
    return lax.psum_scatter(
        partial.astype(jnp.bfloat16), "fsdp", scatter_dimension=0, tiled=True
    ).astype(jnp.float32)


def rows_of(slab):
    fsdp, replica = lax.axis_size("fsdp"), lax.axis_size("replica")
    height, width = slab.shape
    pieces = slab.astype(jnp.bfloat16).reshape(fsdp, replica, -1, width).transpose(1, 0, 2, 3)
    mine = lax.psum_scatter(pieces.reshape(height, width), "replica", scatter_dimension=0, tiled=True)
    mine = mine.reshape(fsdp, -1, width)
    swapped = lax.all_to_all(mine, "fsdp", split_axis=0, concat_axis=0, tiled=True)
    return lax.all_gather(swapped, "replica", axis=0, tiled=False)


def laid_out(pieces):
    replica, fsdp, rows, width = pieces.shape
    return pieces.transpose(0, 2, 1, 3).reshape(replica * rows, fsdp * width).astype(jnp.float32)


def local(
    tokens, attn_gain, w_query, w_key, w_value, w_out, ffn_gain, w_gate, w_up, w_down, cotangent
):
    inputs = tokens.astype(jnp.float32)
    factor_one = rms_factor(inputs)
    normed_one = inputs * factor_one
    cosine, sine = rope_tables(tokens.shape[0] * lax.axis_size("fsdp"))
    (
        lowered_one,
        lowered_two,
        slab_qkv,
        slab_gate,
        slab_up,
        queries,
        keys,
        values,
        attended,
        logs,
        after_attn,
        gains,
    ) = front(tokens, attn_gain, ffn_gain, w_query, w_key, w_value, w_out, w_gate, w_up, cosine, sine)
    slab_query, slab_key, slab_value = jnp.split(slab_qkv, 3)
    gain_one, gain_two = gains[:, 0, :].reshape(-1), gains[:, 1, :].reshape(-1)
    factor_two = rms_factor(after_attn)
    normed_two = after_attn * factor_two
    cotangents = gather(cotangent)
    hidden, grad_gate, grad_up = middle(lowered_two, cotangents, slab_gate, slab_up, w_down)
    grad_normed_two = scatter(contract_last(grad_gate, slab_gate) + contract_last(grad_up, slab_up))
    outputs = (after_attn + scatter(dot(hidden, w_down))).astype(jnp.bfloat16)
    gain_two_term = jnp.sum(grad_normed_two * normed_two, axis=0)
    scaled_two = grad_normed_two * gain_two
    grad_after = cotangent.astype(jnp.float32) + factor_two * (
        scaled_two - normed_two * jnp.mean(scaled_two * normed_two, axis=-1, keepdims=True)
    )
    grad_branch = gather(grad_after.astype(jnp.bfloat16))
    grad_attended = contract_last(grad_branch, w_out).astype(jnp.bfloat16)
    grad_query, grad_key, grad_value = attend_back(queries, keys, values, grad_attended, logs)
    grad_query, grad_key = rotate_back(grad_query, cosine, sine), rotate_back(grad_key, cosine, sine)
    grad_value = grad_value.astype(jnp.bfloat16)
    grad_normed_one = scatter(
        contract_last(grad_query, slab_query)
        + contract_last(grad_key, slab_key)
        + contract_last(grad_value, slab_value)
    )
    gain_one_term = jnp.sum(grad_normed_one * normed_one, axis=0)
    scaled_one = grad_normed_one * gain_one
    grad_tokens = grad_after + factor_one * (
        scaled_one - normed_one * jnp.mean(scaled_one * normed_one, axis=-1, keepdims=True)
    )
    gain_terms = lax.psum(jnp.stack([gain_one_term, gain_two_term]), ("replica", "fsdp"))
    width = attn_gain.shape[0]
    gain_grads = lax.dynamic_slice_in_dim(gain_terms, lax.axis_index("fsdp") * width, width, 1)

    def over_replicas(left, right):
        return lax.psum(contract_first(left, right).astype(jnp.bfloat16), "replica").astype(jnp.float32)

    grad_w_down = over_replicas(hidden, cotangents)
    grad_w_out = over_replicas(attended, grad_branch)
    ffn_pieces = rows_of(contract_first(lowered_two, jnp.concatenate([grad_gate, grad_up], axis=1)))
    half = ffn_pieces.shape[-1] // 2
    grad_w_gate, grad_w_up = laid_out(ffn_pieces[..., :half]), laid_out(ffn_pieces[..., half:])
    attn_pieces = rows_of(
        contract_first(lowered_one, jnp.concatenate([grad_query, grad_key, grad_value], axis=1))
    )
    third = attn_pieces.shape[-1] // 3
    grad_w_query, grad_w_key, grad_w_value = [
        laid_out(attn_pieces[..., i * third : (i + 1) * third]) for i in range(3)
    ]
    return (
        outputs,
        grad_tokens,
        gain_grads[0],
        grad_w_query,
        grad_w_key,
        grad_w_value,
        grad_w_out,
        gain_grads[1],
        grad_w_gate,
        grad_w_up,
        grad_w_down,
    )


def solution(mesh):
    rows = P("fsdp", None)
    tokens = P(("replica", "fsdp"), None)
    gain = P("fsdp")
    return jax.shard_map(
        local,
        mesh=mesh,
        in_specs=(tokens, gain, rows, rows, rows, rows, gain, rows, rows, rows, tokens),
        out_specs=(tokens, tokens, gain, rows, rows, rows, rows, gain, rows, rows, rows),
        check_vma=False,
    )
```

```python
import functools

import jax
import jax.numpy as jnp
import numpy as np
from jax import lax
from jax.experimental import pallas as pl
from jax.experimental.pallas import tpu as pltpu
from jax.sharding import PartitionSpec as P

HEAD_DIM = 64

eps_norm = 1e-05
rope_base = 130000.0
masked_score = -1e30


def rope_tables(row_count):
    lane = np.arange(2 * HEAD_DIM) % HEAD_DIM
    halfway = HEAD_DIM // 2
    spacing = ((lane % halfway) * np.float32(2.0) / HEAD_DIM).astype(np.float32)
    frequency = np.power(np.float32(rope_base), -spacing)
    angles = np.arange(row_count, dtype=np.float32)[:, None] * frequency[None, :]
    sign = np.where(lane < halfway, -1.0, 1.0).astype(np.float32)
    return np.cos(angles).astype(np.float32), (np.sin(angles) * sign[None, :]).astype(np.float32)


def dot(left, right):
    return jnp.dot(left, right, preferred_element_type=jnp.float32)


def contract_last(left, right):
    return lax.dot_general(
        left, right, (((1,), (1,)), ((), ())), preferred_element_type=jnp.float32
    )


def contract_first(left, right):
    return lax.dot_general(
        left, right, (((0,), (0,)), ((), ())), preferred_element_type=jnp.float32
    )


def scores_of(queries, keys, first_row):
    rows, columns = queries.shape[0], keys.shape[0]
    scores = contract_last(queries, keys) * HEAD_DIM**-0.5
    at_row = lax.broadcasted_iota(jnp.int32, (rows, columns), 0) + first_row
    at_column = lax.broadcasted_iota(jnp.int32, (rows, columns), 1)
    return jnp.where(at_column <= at_row, scores, masked_score)


MESH = pl.DeviceIdType.MESH
VMEM_LIMIT = 60 * 2**20


def remote(src, dst, send, recv, **where):
    return pltpu.make_async_remote_copy(
        src_ref=src, dst_ref=dst, send_sem=send, recv_sem=recv, device_id=where, device_id_type=MESH
    )


def await_bytes(ref, sem):
    pltpu.make_async_copy(ref, ref, sem).wait()


def rows_at(ref, index, size):
    return ref.at[pl.ds(pl.multiple_of(index * size, size), size)]


class Place:
    def __init__(self):
        self.fsdp, self.replicas = lax.axis_size("fsdp"), lax.axis_size("replica")
        self.me, self.replica = lax.axis_index("fsdp"), lax.axis_index("replica")
        self.chips = self.fsdp // 2
        self.chip, self.core = self.me // 2, self.me % 2
        self.sibling = self.me + 1 - 2 * self.core
        self.high, self.wide = 2, self.replicas // 2
        self.a, self.b = self.replica // self.wide, self.replica % self.wide
        self.above = self.chip + 1 < self.chips
        self.below = self.chip >= 1

    def enter(self):
        barrier = pltpu.get_barrier_semaphore()

        def greet(k, _):
            to = lax.rem(self.me + k, self.fsdp)
            pl.semaphore_signal(barrier, inc=1, device_id={"fsdp": to}, device_id_type=MESH)
            return 0

        def greet_replica(k, _):
            to = lax.rem(self.replica + k, self.replicas)
            pl.semaphore_signal(barrier, inc=1, device_id={"replica": to}, device_id_type=MESH)
            return 0

        lax.fori_loop(1, self.fsdp, greet, 0)
        lax.fori_loop(1, self.replicas, greet_replica, 0)
        pl.semaphore_wait(barrier, self.fsdp - 1 + self.replicas - 1)


def line_sems(chips):
    dma = pltpu.SemaphoreType.DMA
    return [dma((chips,)), dma((chips,)), dma((chips,)), dma((chips,)), dma((chips,)), dma(())]


class Gather:
    def __init__(self, place, buf, block, sems):
        self.p, self.buf, self.block = place, buf, block
        self.up_out, self.up_in, self.down_out, self.down_in, self.side_out, self.side_in = sems

    def held(self, chip):
        return rows_at(self.buf, 2 * chip + self.p.core, self.block)

    def up(self, step):
        ref = self.held(self.p.chip - step + 1)
        return remote(ref, ref, self.up_out.at[step], self.up_in.at[step], fsdp=self.p.me + 2)

    def down(self, step):
        ref = self.held(self.p.chip + step - 1)
        return remote(ref, ref, self.down_out.at[step], self.down_in.at[step], fsdp=self.p.me - 2)

    def side(self, chip):
        ref = self.held(chip)
        return remote(ref, ref, self.side_out.at[chip], self.side_in, fsdp=self.p.sibling)

    def start(self):
        p = self.p
        pl.when(p.above)(lambda: self.up(1).start())
        pl.when(p.below)(lambda: self.down(1).start())
        self.side(p.chip).start()

    def step(self, step):
        p = self.p
        from_below, from_above = p.chip - step, p.chip + step

        @pl.when(from_below >= 0)
        def _():
            await_bytes(self.held(from_below), self.up_in.at[step])
            if step + 1 < p.chips:
                pl.when(p.above)(lambda: self.up(step + 1).start())
            self.side(from_below).start()

        @pl.when(from_above < p.chips)
        def _():
            await_bytes(self.held(from_above), self.down_in.at[step])
            if step + 1 < p.chips:
                pl.when(p.below)(lambda: self.down(step + 1).start())
            self.side(from_above).start()

    def finish(self):
        p = self.p
        await_bytes(self.buf.at[pl.ds(0, p.chips * self.block)], self.side_in)
        for step in range(1, p.chips):
            pl.when(jnp.logical_and(p.above, p.chip - step + 1 >= 0))(
                lambda step=step: self.up(step).wait_send()
            )
            pl.when(jnp.logical_and(p.below, p.chip + step - 1 < p.chips))(
                lambda step=step: self.down(step).wait_send()
            )
        for chip in range(p.chips):
            self.side(chip).wait_send()

    def run(self):
        self.start()
        for step in range(1, self.p.chips):
            self.step(step)
        self.finish()


class Scatter:
    def __init__(self, place, terms, across, slots, block, sems):
        self.p, self.terms, self.across, self.slots, self.block = place, terms, across, slots, block
        self.up_out, self.up_in, self.down_out, self.down_in, self.side_out, self.side_in = sems

    def side(self, chip):
        p = self.p
        return remote(
            rows_at(self.terms, 2 * chip + 1 - p.core, self.block),
            rows_at(self.across, chip, self.block),
            self.side_out.at[chip],
            self.side_in.at[chip],
            fsdp=p.sibling,
        )

    def term(self, chip):
        return rows_at(self.terms, 2 * chip + self.p.core, self.block)

    def up(self, step):
        return remote(
            self.term(self.p.chips - step + self.p.chip),
            self.slots.at[step - self.p.chip - 1],
            self.up_out.at[step],
            self.up_in.at[step],
            fsdp=self.p.me + 2,
        )

    def down(self, step):
        return remote(
            self.term(self.p.chip - self.p.chips + step),
            self.slots.at[step + 1],
            self.down_out.at[step],
            self.down_in.at[step],
            fsdp=self.p.me - 2,
        )

    def add(self, chip, arrived):
        term = self.term(chip)
        term[...] = (term[...].astype(jnp.float32) + arrived[...].astype(jnp.float32)).astype(term.dtype)

    def cross(self, chip):
        arrived = rows_at(self.across, chip, self.block)
        await_bytes(arrived, self.side_in.at[chip])
        self.add(chip, arrived)

    def step(self, step):
        p = self.p
        rising, falling = p.chips - step + p.chip, p.chip - p.chips + step

        @pl.when(jnp.logical_and(p.above, rising < p.chips))
        def _():
            if step > 1:

                @pl.when(p.below)
                def _():
                    arrived = self.slots.at[step - 1 - p.chip]
                    await_bytes(arrived, self.up_in.at[step - 1])
                    self.add(rising, arrived)

            self.up(step).start()

        @pl.when(jnp.logical_and(p.below, falling >= 0))
        def _():
            if step > 1:

                @pl.when(p.above)
                def _():
                    arrived = self.slots.at[step]
                    await_bytes(arrived, self.down_in.at[step - 1])
                    self.add(falling, arrived)

            self.down(step).start()

    def finish(self, total):
        p, last = self.p, self.p.chips - 1
        total[...] = self.term(p.chip)[...].astype(jnp.float32)

        @pl.when(p.below)
        def _():
            await_bytes(self.slots.at[last - p.chip], self.up_in.at[last])
            total[...] += self.slots[last - p.chip].astype(jnp.float32)

        @pl.when(p.above)
        def _():
            await_bytes(self.slots.at[last + 1], self.down_in.at[last])
            total[...] += self.slots[last + 1].astype(jnp.float32)

    def drain(self):
        p = self.p
        for step in range(1, p.chips):
            pl.when(jnp.logical_and(p.above, p.chips - step + p.chip < p.chips))(
                lambda step=step: self.up(step).wait_send()
            )
            pl.when(jnp.logical_and(p.below, p.chip - p.chips + step >= 0))(
                lambda step=step: self.down(step).wait_send()
            )
        for chip in range(p.chips):
            self.side(chip).wait_send()


def scatter_sems(chips):
    dma = pltpu.SemaphoreType.DMA
    return [dma((chips,))] * 6


class Turn:
    def __init__(self, place, weight, slab, first, sems):
        self.p, self.weight, self.slab, self.first = place, weight, slab, first
        self.far_out, self.far_in, self.near_out, self.near_in, self.pass_out, self.pass_in, self.own = sems
        self.height, self.width = weight.shape[0], slab.shape[1]
        self.share = self.height // place.replicas

    def far_rows(self):
        return (self.p.fsdp - 2) * self.share

    def piece(self, block, share):
        at = self.first + block * self.height + share * self.share
        return self.slab.at[pl.ds(pl.multiple_of(at, self.share), self.share)]

    def whole(self, block):
        at = self.first + block * self.height
        return self.slab.at[pl.ds(pl.multiple_of(at, self.height), self.height)]

    def columns(self, to):
        return pl.ds(pl.multiple_of(to * self.width, self.width), self.width)

    def start(self):
        p = self.p

        def send(k, _):
            to = lax.rem(2 * p.chip + 2 + k, p.fsdp)
            share = pl.ds(pl.multiple_of(p.replica * self.share, self.share), self.share)
            remote(
                self.weight.at[share, self.columns(to)],
                self.piece(p.me, p.replica),
                self.far_out,
                self.far_in,
                fsdp=to,
            ).start()
            return 0

        lax.fori_loop(0, p.fsdp - 2, send, 0)
        self.near().start()
        self.mine().start()

    def near(self):
        p = self.p
        return remote(
            self.weight.at[:, self.columns(p.sibling)], self.whole(p.me), self.near_out, self.near_in, fsdp=p.sibling
        )

    def mine(self):
        return pltpu.make_async_copy(self.weight.at[:, self.columns(self.p.me)], self.whole(self.p.me), self.own)

    def await_far(self):
        await_bytes(self.slab.at[pl.ds(0, self.far_rows())], self.far_in)

    def pass_on(self):
        p = self.p

        def one(k, _):
            ref = self.piece(lax.rem(2 * p.chip + 2 + k, p.fsdp), p.replica)

            def send(j, _):
                remote(
                    ref, ref, self.pass_out, self.pass_in, replica=lax.rem(p.replica + j, p.replicas)
                ).start()
                return 0

            return lax.fori_loop(1, p.replicas, send, 0)

        lax.fori_loop(0, p.fsdp - 2, one, 0)

    def finish(self):
        p = self.p
        passed = self.slab.at[pl.ds(0, (p.replicas - 1) * self.far_rows())]
        await_bytes(passed, self.pass_in)
        await_bytes(self.whole(p.sibling), self.near_in)
        self.mine().wait()

    def drain(self):
        p = self.p
        await_bytes(self.slab.at[pl.ds(0, self.far_rows())], self.far_out)
        self.near().wait_send()
        await_bytes(self.slab.at[pl.ds(0, (p.replicas - 1) * self.far_rows())], self.pass_out)


def turn_sems():
    return [pltpu.SemaphoreType.DMA(())] * 7


def partner(values):
    halfway = HEAD_DIM // 2
    width = values.shape[1]
    lane = lax.broadcasted_iota(jnp.int32, values.shape, 1) % HEAD_DIM
    return jnp.where(
        lane < halfway,
        pltpu.roll(values, width - halfway, axis=1),
        pltpu.roll(values, halfway, axis=1),
    )


def front_kernel(
    tokens,
    gain_one,
    gain_two,
    w_query,
    w_key,
    w_value,
    w_out,
    w_gate,
    w_up,
    cosine,
    sine,
    lowered_one_out,
    lowered_two_out,
    slab_qkv_out,
    slab_gate,
    slab_up,
    queries,
    keys,
    values,
    attended,
    logs,
    after_attn,
    gains,
    lowered_one,
    lowered_two,
    slab_qkv,
    terms,
    across,
    slots,
    gain_rows,
    gain_out,
    gain_in,
    copy_sems,
    *sems,
):
    place = Place()
    chips, block = place.chips, tokens.shape[0]
    model, width = tokens.shape[1], queries.shape[1]
    share = gain_one.shape[1]
    rows = chips * 2 * block
    one_sems, two_sems, scatter_at = sems[:6], sems[6:12], sems[12:18]
    turn_at = [sems[18 + 7 * i : 25 + 7 * i] for i in range(5)]
    turns = [
        Turn(place, weight, slab_qkv, i * model, turn_at[i])
        for i, weight in enumerate((w_query, w_key, w_value))
    ]
    late = [Turn(place, w_gate, slab_gate, 0, turn_at[3]), Turn(place, w_up, slab_up, 0, turn_at[4])]

    gain_rows[...] = jnp.zeros_like(gain_rows)
    gain_rows[0:1, :] = gain_one[...].astype(jnp.float32)
    gain_rows[1:2, :] = gain_two[...].astype(jnp.float32)
    place.enter()

    def send_gains(k, _):
        to = lax.rem(place.me + k, place.fsdp)
        remote(gain_rows, gains.at[place.me], gain_out, gain_in, fsdp=to).start()
        return 0

    lax.fori_loop(1, place.fsdp, send_gains, 0)
    for turn in turns:
        turn.start()
    gains[place.me] = gain_rows[...]
    inputs = tokens[...].astype(jnp.float32)
    factor = lax.rsqrt(jnp.mean(inputs * inputs, axis=-1, keepdims=True) + eps_norm)
    await_bytes(gains.at[pl.ds(0, place.fsdp - 1)], gain_in)
    here = pl.ds(pl.multiple_of(place.me * block, block), block)
    for j in range(model // share):
        at = pl.ds(j * share, share)
        normed = tokens[:, at].astype(jnp.float32) * factor
        lowered_one[here, at] = (normed * gains[j, 0:1, :]).astype(jnp.bfloat16)
    first = Gather(place, lowered_one, block, one_sems)
    first.start()
    for turn in turns:
        turn.await_far()
        turn.pass_on()
    late[0].start()
    late[1].start()
    for step in range(1, chips):
        first.step(step)
    first.finish()
    keep_one = pltpu.make_async_copy(lowered_one, lowered_one_out, copy_sems.at[0])
    keep_one.start()
    for turn in turns:
        turn.finish()
    keep_slab = pltpu.make_async_copy(slab_qkv, slab_qkv_out, copy_sems.at[1])
    keep_slab.start()

    tile = 2 * block

    def project(t, _):
        at = pl.ds(pl.multiple_of(t * tile, tile), tile)
        left = lowered_one[at, :]
        for i, ref in enumerate((queries, keys, values)):
            out = dot(left, slab_qkv[i * model : (i + 1) * model, :])
            if i < 2:
                for j in range(0, width, 2 * HEAD_DIM):
                    pair = out[:, j : j + 2 * HEAD_DIM]
                    pair = pair * cosine[at, :] + partner(pair) * sine[at, :]
                    ref[at, j : j + 2 * HEAD_DIM] = pair.astype(jnp.bfloat16)
            else:
                ref[at, :] = out.astype(jnp.bfloat16)
        return 0

    lax.fori_loop(0, chips, project, 0)
    late[0].await_far()
    late[0].pass_on()
    scatter = Scatter(place, terms, across, slots, block, scatter_at)
    pair = 2 * HEAD_DIM
    for t in range(chips):
        here_t, seen = pl.ds(t * tile, tile), pl.ds(0, (t + 1) * tile)

        def heads(h, _, t=t, here_t=here_t, seen=seen):
            lanes = pl.ds(pl.multiple_of(h * pair, pair), pair)
            q2, k2, v2 = queries[here_t, lanes], keys[seen, lanes], values[seen, lanes]
            mixed, stats = [], []
            for at in (0, HEAD_DIM):
                head = slice(at, at + HEAD_DIM)
                scores = scores_of(q2[:, head], k2[:, head], t * tile)
                most = jnp.max(scores, axis=-1, keepdims=True)
                weights = jnp.exp(scores - most)
                total = jnp.sum(weights, axis=-1, keepdims=True)
                mixed.append(dot((weights / total).astype(jnp.bfloat16), v2[:, head]))
                stats.append(jnp.broadcast_to(most + jnp.log(total), (tile, HEAD_DIM)))
            attended[here_t, lanes] = jnp.concatenate(mixed, axis=1).astype(jnp.bfloat16)
            logs[here_t, lanes] = jnp.concatenate(stats, axis=1)
            return 0

        lax.fori_loop(0, width // pair, heads, 0)
        terms[here_t, :] = dot(attended[here_t, :], w_out[...]).astype(jnp.bfloat16)
        scatter.side(t).start()
    late[1].await_far()
    late[1].pass_on()
    for t in range(chips):
        scatter.cross(t)
    for step in range(1, chips):
        scatter.step(step)
    scatter.finish(after_attn)
    after_attn[...] += tokens[...].astype(jnp.float32)
    after = after_attn[...]
    factor = lax.rsqrt(jnp.mean(after * after, axis=-1, keepdims=True) + eps_norm)
    for j in range(model // share):
        at = pl.ds(j * share, share)
        normed = after_attn[:, at] * factor
        lowered_two[here, at] = (normed * gains[j, 1:2, :]).astype(jnp.bfloat16)
    second = Gather(place, lowered_two, block, two_sems)
    second.run()
    keep_two = pltpu.make_async_copy(lowered_two, lowered_two_out, copy_sems.at[2])
    keep_two.start()
    for turn in late:
        turn.finish()
    scatter.drain()
    for turn in turns + late:
        turn.drain()
    await_bytes(gains.at[pl.ds(0, place.fsdp - 1)], gain_out)
    keep_one.wait()
    keep_slab.wait()
    keep_two.wait()


def front(tokens, gain_one, gain_two, w_query, w_key, w_value, w_out, w_gate, w_up, cosine, sine):
    fsdp = lax.axis_size("fsdp")
    chips = fsdp // 2
    block, model = tokens.shape
    rows, width, wide = fsdp * block, w_query.shape[1] // fsdp, w_gate.shape[1] // fsdp
    share = gain_one.shape[0]
    low, full = jnp.bfloat16, jnp.float32
    hbm, vmem = pl.BlockSpec(memory_space=pl.ANY), pl.BlockSpec(memory_space=pltpu.VMEM)
    shape = jax.ShapeDtypeStruct
    return pl.pallas_call(
        front_kernel,
        in_specs=[vmem] * 3 + [hbm] * 3 + [vmem] + [hbm] * 2 + [vmem] * 2,
        out_specs=[hbm] * 5 + [vmem] * 7,
        out_shape=[
            shape((rows, model), low),
            shape((rows, model), low),
            shape((3 * model, width), low),
            shape((model, wide), low),
            shape((model, wide), low),
            shape((rows, width), low),
            shape((rows, width), low),
            shape((rows, width), low),
            shape((rows, width), low),
            shape((rows, width), full),
            shape((block, model), full),
            shape((fsdp, 8, share), full),
        ],
        scratch_shapes=[
            pltpu.VMEM((rows, model), low),
            pltpu.VMEM((rows, model), low),
            pltpu.VMEM((3 * model, width), low),
            pltpu.VMEM((rows, model), low),
            pltpu.VMEM((chips * block, model), low),
            pltpu.VMEM((chips + 1, block, model), low),
            pltpu.VMEM((8, share), full),
            pltpu.SemaphoreType.DMA(()),
            pltpu.SemaphoreType.DMA(()),
            pltpu.SemaphoreType.DMA((3,)),
        ]
        + line_sems(chips)
        + line_sems(chips)
        + scatter_sems(chips)
        + turn_sems() * 5,
        compiler_params=pltpu.CompilerParams(
            collective_id=0, has_side_effects=True, vmem_limit_bytes=VMEM_LIMIT
        ),
        name="front",
    )(
        tokens,
        gain_one.reshape(1, -1),
        gain_two.reshape(1, -1),
        w_query,
        w_key,
        w_value,
        w_out,
        w_gate,
        w_up,
        cosine,
        sine,
    )


class Reduce:
    def __init__(self, place, part, out, buffers, sems, turned):
        self.p, self.part, self.out, self.sems, self.turned = place, part, out, sems, turned
        self.own, self.first, self.second = buffers[:2], buffers[2:4], buffers[4:6]
        self.half = part.shape[0] // 2
        self.width = part.shape[-1]
        p = place
        self.counts = ((p.wide, p.high), (p.high, p.wide))

    def peer(self, half, stage, k):
        p = self.p
        if half == stage:
            to = lax.rem(p.b + k, p.wide)
            return to, p.a * p.wide + to
        to = lax.rem(p.a + k, p.high)
        return to, to * p.wide + p.b

    def rows(self, half):
        return pl.ds(half * self.half, self.half)

    def sent(self, half, to):
        if half == 0:
            return self.part.at[self.rows(0), :, to]
        return self.part.at[self.rows(1), to]

    def start(self):
        for half in range(2):
            for k in range(1, self.counts[half][0]):
                to, replica = self.peer(half, 0, k)
                remote(
                    self.sent(half, to),
                    self.first[half].at[k - 1],
                    self.sems.at[half, 1],
                    self.sems.at[half, 2],
                    replica=replica,
                ).start()
        for half in range(2):
            mine = self.p.b if half == 0 else self.p.a
            pltpu.make_async_copy(self.sent(half, mine), self.own[half], self.sems.at[half, 0]).start()

    def exchange(self):
        for half in range(2):
            own, arrived = self.own[half], self.first[half]
            await_bytes(arrived, self.sems.at[half, 2])
            await_bytes(own, self.sems.at[half, 0])

            def add(n, _, own=own, arrived=arrived):
                for m in range(own.shape[1]):
                    total = own[n, m].astype(jnp.float32)
                    for k in range(arrived.shape[0]):
                        total += arrived[k, n, m].astype(jnp.float32)
                    own[n, m] = total.astype(own.dtype)
                return 0

            lax.fori_loop(0, self.half, add, 0)
            for k in range(1, self.counts[half][1]):
                to, replica = self.peer(half, 1, k)
                remote(
                    own.at[:, to],
                    self.second[half].at[k - 1],
                    self.sems.at[half, 3],
                    self.sems.at[half, 4],
                    replica=replica,
                ).start()

    def placed(self, half, rows):
        a, b = rows
        if self.turned:
            width = self.out.shape[-1] // 2
            return self.out.at[a, b, :, pl.ds(half * width, width)]
        return self.out.at[half, a, b]

    def total(self):
        p = self.p
        for half in range(2):
            own, arrived = self.own[half], self.second[half]
            mine = p.a if half == 0 else p.b
            await_bytes(arrived, self.sems.at[half, 4])

            def add(n, _, own=own, arrived=arrived, mine=mine):
                total = own[n, mine].astype(jnp.float32)
                for k in range(arrived.shape[0]):
                    total += arrived[k, n].astype(jnp.float32)
                own[n, mine] = total.astype(own.dtype)
                return 0

            lax.fori_loop(0, self.half, add, 0)
        if self.turned:
            columns = pl.ds(pl.multiple_of(p.me * self.width, self.width), self.width)
            target = self.out.at[p.a, p.b, :, columns]

            def each(to, do):
                pl.when(to < self.half)(lambda: do(self.own[0].at[to, p.a]))
                pl.when(to >= self.half)(lambda: do(self.own[1].at[to - self.half, p.b]))

            def send(k, _):
                to = lax.rem(p.me + k, p.fsdp)
                each(
                    to,
                    lambda ref: remote(
                        ref, target, self.sems.at[0, 5], self.sems.at[0, 6], fsdp=to
                    ).start(),
                )
                return 0

            lax.fori_loop(1, p.fsdp, send, 0)
            each(p.me, lambda ref: pltpu.make_async_copy(ref, target, self.sems.at[0, 6]).start())
        else:
            for half in range(2):
                mine = p.a if half == 0 else p.b
                pltpu.make_async_copy(
                    self.own[half].at[0, mine], self.out.at[half, p.a, p.b], self.sems.at[half, 6]
                ).start()

    def spread(self):
        p = self.p
        if self.turned:
            await_bytes(self.out.at[p.a, p.b], self.sems.at[0, 6])
        for half in range(2):
            ref = self.placed(half, (p.a, p.b))
            if not self.turned:
                await_bytes(ref, self.sems.at[half, 6])
            for k in range(1, self.counts[half][1]):
                _, replica = self.peer(half, 1, k)
                remote(ref, ref, self.sems.at[half, 7], self.sems.at[half, 8], replica=replica).start()

    def spread_bytes(self, half):
        some = pl.ds(0, self.counts[half][1] - 1)
        return self.placed(half, (some, 0) if half == 0 else (0, some))

    def held(self, half):
        every = pl.ds(0, self.counts[half][1])
        return self.placed(half, (every, self.p.b) if half == 0 else (self.p.a, every))

    def widen(self):
        for half in range(2):
            await_bytes(self.spread_bytes(half), self.sems.at[half, 8])
            ref = self.held(half)
            for k in range(1, self.counts[half][0]):
                _, replica = self.peer(half, 0, k)
                remote(ref, ref, self.sems.at[half, 9], self.sems.at[half, 10], replica=replica).start()

    def widen_bytes(self, half):
        every, some = pl.ds(0, self.counts[half][1]), pl.ds(0, self.counts[half][0] - 1)
        return self.placed(half, (every, some) if half == 0 else (some, every))

    def finish(self):
        p = self.p
        for half in range(2):
            await_bytes(self.widen_bytes(half), self.sems.at[half, 10])
            await_bytes(self.first[half], self.sems.at[half, 1])
            await_bytes(self.second[half], self.sems.at[half, 3])
            await_bytes(self.spread_bytes(half), self.sems.at[half, 7])
            await_bytes(self.widen_bytes(half), self.sems.at[half, 9])
        if self.turned:
            await_bytes(
                self.out.at[p.a, p.b, :, pl.ds(0, (p.fsdp - 1) * self.width)], self.sems.at[0, 5]
            )


def reduce_scratch(n, high, wide, rows, columns):
    low = functools.partial(pltpu.VMEM, dtype=jnp.bfloat16)
    half = n // 2
    return [
        low((half, high, rows, columns)),
        low((half, wide, rows, columns)),
        low((wide - 1, half, high, rows, columns)),
        low((high - 1, half, wide, rows, columns)),
        low((high - 1, half, rows, columns)),
        low((wide - 1, half, rows, columns)),
        pltpu.SemaphoreType.DMA((2, 11)),
    ]


def back_kernel(
    tokens,
    cotangent,
    after_attn,
    gains,
    terms_in,
    part_down,
    part_gate,
    part_up,
    lowered_one,
    slab_qkv,
    w_out,
    queries,
    keys,
    values,
    attended,
    logs,
    cosine,
    sine,
    grad_tokens,
    gain_out,
    out_down,
    out_gate,
    out_up,
    out_qkv,
    out_out,
    terms,
    across,
    slots,
    branch,
    grad_after,
    summed,
    grad_low,
    grad_key,
    grad_value,
    grads,
    part_qkv,
    part_out,
    gain_terms,
    gain_slots,
    gain_sums,
    gain_sems,
    load_sems,
    *rest,
):
    place = Place()
    chips, block = place.chips, tokens.shape[0]
    model, width = tokens.shape[1], queries.shape[1]
    share = gains.shape[2]
    tile = 2 * block
    scatter_at, gather_at, rest = rest[:6], rest[6:12], rest[12:]

    def reducer(i, part, out, turned):
        at = rest[7 * i : 7 * i + 7]
        return Reduce(place, part, out, at[:6], at[6], turned)

    down = reducer(0, part_down, out_down, False)
    gate = reducer(1, part_gate, out_gate, True)
    up = reducer(2, part_up, out_up, True)
    qkv = reducer(3, part_qkv, out_qkv, True)
    out = reducer(4, part_out, out_out, False)

    def load(t):
        at = pl.ds(t * tile, tile)
        return pltpu.make_async_copy(terms_in.at[at], terms.at[at], load_sems.at[t])

    for t in range(chips):
        load(t).start()
    place.enter()
    scatter = Scatter(place, terms, across, slots, block, scatter_at)
    for t in range(chips):
        load(t).wait()
        scatter.side(t).start()
    down.start()
    gate.start()
    up.start()
    for t in range(chips):
        scatter.cross(t)
    for step in range(1, chips):
        scatter.step(step)
    scatter.finish(summed)

    def norm_back(values, gain_row, grad, result, carried):
        held = values[...].astype(jnp.float32)
        factor = lax.rsqrt(jnp.mean(held * held, axis=-1, keepdims=True) + eps_norm)
        dots = jnp.zeros((block, 1), jnp.float32)
        for j in range(model // share):
            at = pl.ds(j * share, share)
            normed = values[:, at].astype(jnp.float32) * factor
            product = grad[:, at] * normed
            gain_terms[j, gain_row : gain_row + 1, :] = jnp.sum(product, axis=0, keepdims=True)
            dots += jnp.sum(product * gains[j, gain_row : gain_row + 1, :], axis=-1, keepdims=True)
        dots = dots / model
        for j in range(model // share):
            at = pl.ds(j * share, share)
            normed = values[:, at].astype(jnp.float32) * factor
            scaled = grad[:, at] * gains[j, gain_row : gain_row + 1, :]
            result[:, at] = carried[:, at].astype(jnp.float32) + factor * (scaled - normed * dots)

    gain_terms[...] = jnp.zeros_like(gain_terms)
    norm_back(after_attn, 1, summed, grad_after, cotangent)
    here = pl.ds(pl.multiple_of(place.me * block, block), block)
    branch[here, :] = grad_after[...].astype(jnp.bfloat16)
    gather = Gather(place, branch, block, gather_at)
    gather.start()
    scatter.drain()
    down.exchange()
    for step in range(1, chips):
        gather.step(step)
    gather.finish()
    gate.exchange()
    down.total()

    def attend_rows(t, _):
        at = pl.ds(pl.multiple_of(t * tile, tile), tile)
        grad_low[at, :] = contract_last(branch[at, :], w_out[...]).astype(jnp.bfloat16)
        return 0

    lax.fori_loop(0, chips, attend_rows, 0)
    high, wide, piece = place.high, place.wide, part_out.shape[3]
    columns = part_out.shape[-1]
    for half in range(2):
        for at in range(0, columns, 512):
            got = contract_first(
                attended[...], branch[:, half * columns + at : half * columns + at + 512]
            ).astype(jnp.bfloat16)
            part_out[half, :, :, :, at : at + 512] = got.reshape(high, wide, piece, 512)
    out.start()
    reload = pltpu.make_async_copy(lowered_one, branch, load_sems.at[0])
    reload.start()
    down.spread()

    scale = HEAD_DIM**-0.5
    grad_key[...] = jnp.zeros_like(grad_key)
    grad_value[...] = jnp.zeros_like(grad_value)
    pair = 2 * HEAD_DIM
    height = tile * 1024 // max(queries.shape[0], 1024)
    for first in range(0, queries.shape[0], height):
        rows, seen = pl.ds(first, height), pl.ds(0, first + height)

        def heads(h, _, first=first, rows=rows, seen=seen):
            lanes = pl.ds(pl.multiple_of(h * pair, pair), pair)
            q2, g2, log2 = queries[rows, lanes], grad_low[rows, lanes], logs[rows, lanes]
            k2, v2 = keys[seen, lanes], values[seen, lanes]
            for_queries, for_keys, for_values = [], [], []
            for at in (0, HEAD_DIM):
                head = slice(at, at + HEAD_DIM)
                q, g, k = q2[:, head], g2[:, head], k2[:, head]
                weights = jnp.exp(scores_of(q, k, first) - log2[:, at : at + 1])
                grad_weights = contract_last(g, v2[:, head])
                delta = jnp.sum(weights * grad_weights, axis=-1, keepdims=True)
                grad_scores = (weights * (grad_weights - delta)).astype(jnp.bfloat16)
                for_queries.append(dot(grad_scores, k))
                for_keys.append(contract_first(grad_scores, q))
                for_values.append(contract_first(weights.astype(jnp.bfloat16), g))
            got = jnp.concatenate(for_queries, axis=1) * scale
            got = got * cosine[rows, :] - partner(got) * sine[rows, :]
            grads[rows, lanes] = got.astype(jnp.bfloat16)
            grad_key[seen, lanes] += jnp.concatenate(for_keys, axis=1) * scale
            grad_value[seen, lanes] += jnp.concatenate(for_values, axis=1)
            return 0

        lax.fori_loop(0, width // pair, heads, 0)
    up.exchange()
    gate.total()

    def turn_back(t, _):
        at = pl.ds(pl.multiple_of(t * tile, tile), tile)
        for j in range(0, width, pair):
            got = grad_key[at, j : j + pair]
            got = got * cosine[at, :] - partner(got) * sine[at, :]
            grads[at, width + j : width + j + pair] = got.astype(jnp.bfloat16)
        grads[at, 2 * width :] = grad_value[at, :].astype(jnp.bfloat16)
        got = contract_last(grads[at, :width], slab_qkv[:model, :])
        got += contract_last(grads[at, width : 2 * width], slab_qkv[model : 2 * model, :])
        got += contract_last(grads[at, 2 * width :], slab_qkv[2 * model :, :])
        terms[at, :] = got.astype(jnp.bfloat16)
        return 0

    lax.fori_loop(0, chips, turn_back, 0)
    for t in range(chips):
        scatter.side(t).start()
    reload.wait()

    def weigh(j, _):
        rows = part_qkv.shape[3]
        left = branch[:, pl.ds(pl.multiple_of(j * share, share), share)]
        got = contract_first(left, grads[...]).astype(jnp.bfloat16)
        part_qkv[j] = got.reshape(high, wide, rows, 3 * width)
        return 0

    lax.fori_loop(0, place.fsdp, weigh, 0)
    qkv.start()
    for t in range(chips):
        scatter.cross(t)
    for step in range(1, chips):
        scatter.step(step)
    up.total()
    gate.spread()
    out.exchange()
    scatter.finish(summed)
    norm_back(tokens, 0, summed, grad_tokens, grad_after)

    def send_gain(k, _):
        to = lax.rem(place.me + k, place.fsdp)
        remote(
            gain_terms.at[to], gain_slots.at[place.me], gain_sems.at[0], gain_sems.at[1], fsdp=to
        ).start()
        return 0

    lax.fori_loop(1, place.fsdp, send_gain, 0)
    gain_slots[place.me] = gain_terms[place.me]
    down.widen()
    up.spread()
    gate.widen()
    qkv.exchange()
    out.total()
    await_bytes(gain_slots.at[pl.ds(0, place.fsdp - 1)], gain_sems.at[1])
    gain_sums[place.replica] = jnp.sum(gain_slots[...], axis=0)

    def send_sum(k, _):
        ref = gain_sums.at[place.replica]
        to = lax.rem(place.replica + k, place.replicas)
        remote(ref, ref, gain_sems.at[2], gain_sems.at[3], replica=to).start()
        return 0

    lax.fori_loop(1, place.replicas, send_sum, 0)
    qkv.total()
    out.spread()
    up.widen()
    qkv.spread()
    out.widen()
    qkv.widen()
    await_bytes(gain_sums.at[pl.ds(0, place.replicas - 1)], gain_sems.at[3])
    gain_out[...] = jnp.sum(gain_sums[...], axis=0)
    await_bytes(gain_slots.at[pl.ds(0, place.fsdp - 1)], gain_sems.at[0])
    await_bytes(gain_sums.at[pl.ds(0, place.replicas - 1)], gain_sems.at[2])
    scatter.drain()
    for reduce in (down, gate, up, out, qkv):
        reduce.finish()


def back(
    tokens,
    cotangent,
    after_attn,
    gains,
    terms,
    part_down,
    part_gate,
    part_up,
    lowered_one,
    slab_qkv,
    w_out,
    queries,
    keys,
    values,
    attended,
    logs,
    cosine,
    sine,
):
    fsdp, replicas = lax.axis_size("fsdp"), lax.axis_size("replica")
    chips, high, wide = fsdp // 2, 2, replicas // 2
    block, model = tokens.shape
    rows, width = queries.shape
    share = gains.shape[2]
    low, full = jnp.bfloat16, jnp.float32
    hbm, vmem = pl.BlockSpec(memory_space=pl.ANY), pl.BlockSpec(memory_space=pltpu.VMEM)
    shape = jax.ShapeDtypeStruct
    thin = share // replicas
    hidden = part_down.shape[0]
    columns = part_gate.shape[1]
    down_piece = (2, high, wide, hidden // (2 * replicas), model)
    wide_piece = (fsdp, high, wide, thin, columns)
    qkv_piece = (fsdp, high, wide, thin, 3 * width)
    out_piece = (2, high, wide, width // replicas, model // 2)
    dma = pltpu.SemaphoreType.DMA
    return pl.pallas_call(
        back_kernel,
        in_specs=[vmem] * 4 + [hbm] * 5 + [vmem] * 9,
        out_specs=[vmem] * 2 + [hbm] * 5,
        out_shape=[
            shape((block, model), full),
            shape((8, share), full),
            shape(down_piece, low),
            shape((high, wide, thin, fsdp * columns), low),
            shape((high, wide, thin, fsdp * columns), low),
            shape((high, wide, thin, fsdp * 3 * width), low),
            shape(out_piece, low),
        ],
        scratch_shapes=[
            pltpu.VMEM((rows, model), low),
            pltpu.VMEM((chips * block, model), low),
            pltpu.VMEM((chips + 1, block, model), low),
            pltpu.VMEM((rows, model), low),
            pltpu.VMEM((block, model), full),
            pltpu.VMEM((block, model), full),
            pltpu.VMEM((rows, width), low),
            pltpu.VMEM((rows, width), full),
            pltpu.VMEM((rows, width), full),
            pltpu.VMEM((rows, 3 * width), low),
            pltpu.VMEM(qkv_piece, low),
            pltpu.VMEM(out_piece, low),
            pltpu.VMEM((fsdp, 8, share), full),
            pltpu.VMEM((fsdp, 8, share), full),
            pltpu.VMEM((replicas, 8, share), full),
            dma((4,)),
            dma((chips,)),
        ]
        + scatter_sems(chips)
        + line_sems(chips)
        + reduce_scratch(*down_piece)
        + reduce_scratch(*wide_piece)
        + reduce_scratch(*wide_piece)
        + reduce_scratch(*qkv_piece)
        + reduce_scratch(*out_piece),
        compiler_params=pltpu.CompilerParams(
            collective_id=1, has_side_effects=True, vmem_limit_bytes=VMEM_LIMIT
        ),
        name="back",
    )(
        tokens,
        cotangent,
        after_attn,
        gains,
        terms,
        part_down.reshape(down_piece),
        part_gate.reshape(wide_piece),
        part_up.reshape(wide_piece),
        lowered_one,
        slab_qkv,
        w_out,
        queries,
        keys,
        values,
        attended,
        logs,
        cosine,
        sine,
    )


def middle_kernel(
    low_ref, cot_ref, gate_ref, up_ref, down_ref, hidden_ref, grad_gate_ref, grad_up_ref, terms_ref, sums_ref
):
    gate = dot(low_ref[...], gate_ref[...])
    up = dot(low_ref[...], up_ref[...])
    grad_hidden = contract_last(cot_ref[...], down_ref[...])
    sigmoid = jax.nn.sigmoid(gate)
    silu = gate * sigmoid
    hidden = (silu * up).astype(jnp.bfloat16)
    grad_gate = (grad_hidden * up * sigmoid * (1.0 + gate * (1.0 - sigmoid))).astype(jnp.bfloat16)
    grad_up = (grad_hidden * silu).astype(jnp.bfloat16)
    hidden_ref[...] = hidden
    grad_gate_ref[...] = grad_gate
    grad_up_ref[...] = grad_up
    terms_ref[...] = (
        contract_last(grad_gate, gate_ref[...]) + contract_last(grad_up, up_ref[...])
    ).astype(jnp.bfloat16)
    sums_ref[...] = dot(hidden, down_ref[...]).astype(jnp.bfloat16)


def middle(lowered_two, cotangents, slab_gate, slab_up, w_down):
    rows, model = lowered_two.shape
    wide = slab_gate.shape[1]
    tile = 256
    low = jnp.bfloat16
    by_rows = pl.BlockSpec((tile, model), lambda i: (i, 0))
    by_tile = pl.BlockSpec((tile, wide), lambda i: (i, 0))

    def whole(shape):
        return pl.BlockSpec(shape, lambda i: (0, 0), pipeline_mode=pl.Buffered(1))

    return pl.pallas_call(
        middle_kernel,
        grid=(rows // tile,),
        in_specs=[by_rows, by_rows, whole((model, wide)), whole((model, wide)), whole((wide, model))],
        out_specs=[by_tile] * 3 + [by_rows] * 2,
        out_shape=[jax.ShapeDtypeStruct((rows, wide), low)] * 3
        + [jax.ShapeDtypeStruct((rows, model), low)] * 2,
        compiler_params=pltpu.CompilerParams(vmem_limit_bytes=VMEM_LIMIT),
        cost_estimate=pl.CostEstimate(
            flops=12 * rows * model * wide, bytes_accessed=8 * rows * model + 6 * model * wide, transcendentals=rows * wide
        ),
        name="middle",
    )(lowered_two, cotangents, slab_gate, slab_up, w_down)


def weigh_kernel(low_ref, gate_ref, up_ref, hidden_ref, cot_ref, out_down, out_gate, out_up):
    out_down[...] = contract_first(hidden_ref[...], cot_ref[...]).astype(jnp.bfloat16)
    out_gate[...] = contract_first(low_ref[...], gate_ref[...]).astype(jnp.bfloat16)
    out_up[...] = contract_first(low_ref[...], up_ref[...]).astype(jnp.bfloat16)


def weigh(lowered_two, grad_gate, grad_up, hidden, cotangents):
    rows, model = lowered_two.shape
    wide = hidden.shape[1]
    steps = 4
    low = jnp.bfloat16

    def whole(shape):
        return pl.BlockSpec(shape, lambda i: (0, 0), pipeline_mode=pl.Buffered(1))

    return pl.pallas_call(
        weigh_kernel,
        grid=(steps,),
        in_specs=[
            pl.BlockSpec((rows, model // steps), lambda i: (0, i)),
            whole((rows, wide)),
            whole((rows, wide)),
            pl.BlockSpec((rows, wide // steps), lambda i: (0, i)),
            whole((rows, model)),
        ],
        out_specs=[
            pl.BlockSpec((wide // steps, model), lambda i: (i, 0)),
            pl.BlockSpec((model // steps, wide), lambda i: (i, 0)),
            pl.BlockSpec((model // steps, wide), lambda i: (i, 0)),
        ],
        out_shape=[
            jax.ShapeDtypeStruct((wide, model), low),
            jax.ShapeDtypeStruct((model, wide), low),
            jax.ShapeDtypeStruct((model, wide), low),
        ],
        compiler_params=pltpu.CompilerParams(vmem_limit_bytes=VMEM_LIMIT),
        cost_estimate=pl.CostEstimate(
            flops=6 * rows * model * wide, bytes_accessed=4 * rows * model + 6 * rows * wide + 6 * model * wide, transcendentals=0
        ),
        name="weigh",
    )(lowered_two, grad_gate, grad_up, hidden, cotangents)


def gather(values):
    return lax.all_gather(values, "fsdp", axis=0, tiled=True)


def scatter(partial):
    return lax.psum_scatter(partial, "fsdp", scatter_dimension=0, tiled=True).astype(jnp.float32)


def local(
    tokens, attn_gain, w_query, w_key, w_value, w_out, ffn_gain, w_gate, w_up, w_down, cotangent
):
    cosine, sine = rope_tables(tokens.shape[0] * lax.axis_size("fsdp"))
    (
        lowered_one,
        lowered_two,
        slab_qkv,
        slab_gate,
        slab_up,
        queries,
        keys,
        values,
        attended,
        logs,
        after_attn,
        gains,
    ) = front(tokens, attn_gain, ffn_gain, w_query, w_key, w_value, w_out, w_gate, w_up, cosine, sine)
    cotangents = gather(cotangent)
    hidden, grad_gate, grad_up, terms, sums = middle(
        lowered_two, cotangents, slab_gate, slab_up, w_down
    )
    outputs = (after_attn + scatter(sums)).astype(jnp.bfloat16)
    part_down, part_gate, part_up = weigh(lowered_two, grad_gate, grad_up, hidden, cotangents)
    grad_tokens, gain_grads, low_down, low_gate, low_up, low_qkv, low_out = back(
        tokens,
        cotangent,
        after_attn,
        gains,
        terms,
        part_down,
        part_gate,
        part_up,
        lowered_one,
        slab_qkv,
        w_out,
        queries,
        keys,
        values,
        attended,
        logs,
        cosine,
        sine,
    )

    def wider(low, like):
        return low.reshape(like.shape).astype(jnp.float32)

    count, width = lax.axis_size("fsdp"), queries.shape[1]
    low_qkv = low_qkv.reshape(-1, count, 3, width)
    low_out = low_out.reshape(2, w_out.shape[0], -1).transpose(1, 0, 2)
    return (
        outputs,
        grad_tokens,
        gain_grads[0],
        wider(low_qkv[:, :, 0], w_query),
        wider(low_qkv[:, :, 1], w_key),
        wider(low_qkv[:, :, 2], w_value),
        wider(low_out, w_out),
        gain_grads[1],
        wider(low_gate, w_gate),
        wider(low_up, w_up),
        wider(low_down, w_down),
    )


def solution(mesh):
    rows = P("fsdp", None)
    tokens = P(("replica", "fsdp"), None)
    gain = P("fsdp")
    return jax.shard_map(
        local,
        mesh=mesh,
        in_specs=(tokens, gain, rows, rows, rows, rows, gain, rows, rows, rows, tokens),
        out_specs=(tokens, tokens, gain, rows, rows, rows, rows, gain, rows, rows, rows),
        check_vma=False,
    )
```

```python
import functools

import jax
import jax.numpy as jnp
import numpy as np
from jax import lax
from jax.experimental import pallas as pl
from jax.experimental.pallas import tpu as pltpu
from jax.sharding import PartitionSpec as P

HEAD_DIM = 64

eps_norm = 1e-05
rope_base = 130000.0
masked_score = -1e30


def rope_tables(row_count):
    lane = np.arange(2 * HEAD_DIM) % HEAD_DIM
    halfway = HEAD_DIM // 2
    spacing = ((lane % halfway) * np.float32(2.0) / HEAD_DIM).astype(np.float32)
    frequency = np.power(np.float32(rope_base), -spacing)
    angles = np.arange(row_count, dtype=np.float32)[:, None] * frequency[None, :]
    sign = np.where(lane < halfway, -1.0, 1.0).astype(np.float32)
    return np.cos(angles).astype(np.float32), (np.sin(angles) * sign[None, :]).astype(np.float32)


def dot(left, right):
    return jnp.dot(left, right, preferred_element_type=jnp.float32)


def contract_last(left, right):
    return lax.dot_general(
        left, right, (((1,), (1,)), ((), ())), preferred_element_type=jnp.float32
    )


def contract_first(left, right):
    return lax.dot_general(
        left, right, (((0,), (0,)), ((), ())), preferred_element_type=jnp.float32
    )


def scores_of(queries, keys, first_row):
    rows, columns = queries.shape[0], keys.shape[0]
    scores = contract_last(queries, keys) * HEAD_DIM**-0.5
    at_row = lax.broadcasted_iota(jnp.int32, (rows, columns), 0) + first_row
    at_column = lax.broadcasted_iota(jnp.int32, (rows, columns), 1)
    return jnp.where(at_column <= at_row, scores, masked_score)


MESH = pl.DeviceIdType.MESH
VMEM_LIMIT = 60 * 2**20


def remote(src, dst, send, recv, **where):
    return pltpu.make_async_remote_copy(
        src_ref=src, dst_ref=dst, send_sem=send, recv_sem=recv, device_id=where, device_id_type=MESH
    )


def await_bytes(ref, sem):
    pltpu.make_async_copy(ref, ref, sem).wait()


def rows_at(ref, index, size):
    return ref.at[pl.ds(pl.multiple_of(index * size, size), size)]


class Place:
    def __init__(self):
        self.fsdp, self.replicas = lax.axis_size("fsdp"), lax.axis_size("replica")
        self.me, self.replica = lax.axis_index("fsdp"), lax.axis_index("replica")
        self.chips = self.fsdp // 2
        self.chip, self.core = self.me // 2, self.me % 2
        self.sibling = self.me + 1 - 2 * self.core
        self.high, self.wide = 2, self.replicas // 2
        self.a, self.b = self.replica // self.wide, self.replica % self.wide
        self.above = self.chip + 1 < self.chips
        self.below = self.chip >= 1

    def nearest(self, k):
        found = jnp.int32(0)
        for chip in range(self.chips):
            order = sorted(range(self.chips), key=lambda other, chip=chip: (abs(other - chip), other))
            found = found + jnp.where(self.chip == chip, order[k], 0)
        return found

    def enter(self):
        barrier = pltpu.get_barrier_semaphore()

        def greet(k, _):
            to = lax.rem(self.me + k, self.fsdp)
            pl.semaphore_signal(barrier, inc=1, device_id={"fsdp": to}, device_id_type=MESH)
            return 0

        def greet_replica(k, _):
            to = lax.rem(self.replica + k, self.replicas)
            pl.semaphore_signal(barrier, inc=1, device_id={"replica": to}, device_id_type=MESH)
            return 0

        lax.fori_loop(1, self.fsdp, greet, 0)
        lax.fori_loop(1, self.replicas, greet_replica, 0)
        pl.semaphore_wait(barrier, self.fsdp - 1 + self.replicas - 1)


def line_sems(chips):
    return [pltpu.SemaphoreType.DMA((chips,))] * 6


class Gather:
    def __init__(self, place, buf, block, sems, own=None):
        self.p, self.buf, self.block, self.own = place, buf, block, own
        self.up_out, self.up_in, self.down_out, self.down_in, self.side_out, self.side_in = sems

    def held(self, chip):
        return rows_at(self.buf, 2 * chip + self.p.core, self.block)

    def up(self, step):
        ref = self.held(self.p.chip - step + 1)
        src = self.own if step == 1 and self.own is not None else ref
        return remote(src, ref, self.up_out.at[step], self.up_in.at[step], fsdp=self.p.me + 2)

    def down(self, step):
        ref = self.held(self.p.chip + step - 1)
        src = self.own if step == 1 and self.own is not None else ref
        return remote(src, ref, self.down_out.at[step], self.down_in.at[step], fsdp=self.p.me - 2)

    def side(self, chip, src=None):
        ref = self.held(chip)
        src = ref if src is None else src
        return remote(src, ref, self.side_out.at[chip], self.side_in.at[chip], fsdp=self.p.sibling)

    def start(self):
        p = self.p
        pl.when(p.above)(lambda: self.up(1).start())
        pl.when(p.below)(lambda: self.down(1).start())
        self.side(p.chip, self.own).start()

    def step(self, step):
        p = self.p
        from_below, from_above = p.chip - step, p.chip + step

        @pl.when(from_below >= 0)
        def _():
            await_bytes(self.held(from_below), self.up_in.at[step])
            if step + 1 < p.chips:
                pl.when(p.above)(lambda: self.up(step + 1).start())
            self.side(from_below).start()

        @pl.when(from_above < p.chips)
        def _():
            await_bytes(self.held(from_above), self.down_in.at[step])
            if step + 1 < p.chips:
                pl.when(p.below)(lambda: self.down(step + 1).start())
            self.side(from_above).start()

    def across(self, chip):
        await_bytes(rows_at(self.buf, 2 * chip + 1 - self.p.core, self.block), self.side_in.at[chip])

    def drain(self):
        p = self.p
        for step in range(1, p.chips):
            pl.when(jnp.logical_and(p.above, p.chip - step + 1 >= 0))(
                lambda step=step: self.up(step).wait_send()
            )
            pl.when(jnp.logical_and(p.below, p.chip + step - 1 < p.chips))(
                lambda step=step: self.down(step).wait_send()
            )
        for chip in range(p.chips):
            self.side(chip).wait_send()

    def finish(self):
        for chip in range(self.p.chips):
            self.across(chip)
        self.drain()


class Scatter:
    def __init__(self, place, terms, across, slots, block, sems):
        self.p, self.terms, self.across, self.slots, self.block = place, terms, across, slots, block
        self.up_out, self.up_in, self.down_out, self.down_in, self.side_out, self.side_in = sems

    def side(self, chip):
        p = self.p
        return remote(
            rows_at(self.terms, 2 * chip + 1 - p.core, self.block),
            rows_at(self.across, chip, self.block),
            self.side_out.at[chip],
            self.side_in.at[chip],
            fsdp=p.sibling,
        )

    def term(self, chip):
        return rows_at(self.terms, 2 * chip + self.p.core, self.block)

    def up(self, step):
        return remote(
            self.term(self.p.chips - step + self.p.chip),
            self.slots.at[step - self.p.chip - 1],
            self.up_out.at[step],
            self.up_in.at[step],
            fsdp=self.p.me + 2,
        )

    def down(self, step):
        return remote(
            self.term(self.p.chip - self.p.chips + step),
            self.slots.at[step + 1],
            self.down_out.at[step],
            self.down_in.at[step],
            fsdp=self.p.me - 2,
        )

    def add(self, chip, arrived):
        term = self.term(chip)
        term[...] = (term[...].astype(jnp.float32) + arrived[...].astype(jnp.float32)).astype(term.dtype)

    def cross(self, chip):
        arrived = rows_at(self.across, chip, self.block)
        await_bytes(arrived, self.side_in.at[chip])
        self.add(chip, arrived)

    def step(self, step):
        p = self.p
        rising, falling = p.chips - step + p.chip, p.chip - p.chips + step

        @pl.when(jnp.logical_and(p.above, rising < p.chips))
        def _():
            if step > 1:

                @pl.when(p.below)
                def _():
                    arrived = self.slots.at[step - 1 - p.chip]
                    await_bytes(arrived, self.up_in.at[step - 1])
                    self.add(rising, arrived)

            self.up(step).start()

        @pl.when(jnp.logical_and(p.below, falling >= 0))
        def _():
            if step > 1:

                @pl.when(p.above)
                def _():
                    arrived = self.slots.at[step]
                    await_bytes(arrived, self.down_in.at[step - 1])
                    self.add(falling, arrived)

            self.down(step).start()

    def finish(self, total):
        p, last = self.p, self.p.chips - 1
        total[...] = self.term(p.chip)[...].astype(jnp.float32)

        @pl.when(p.below)
        def _():
            await_bytes(self.slots.at[last - p.chip], self.up_in.at[last])
            total[...] += self.slots[last - p.chip].astype(jnp.float32)

        @pl.when(p.above)
        def _():
            await_bytes(self.slots.at[last + 1], self.down_in.at[last])
            total[...] += self.slots[last + 1].astype(jnp.float32)

    def drain(self):
        p = self.p
        for step in range(1, p.chips):
            pl.when(jnp.logical_and(p.above, p.chips - step + p.chip < p.chips))(
                lambda step=step: self.up(step).wait_send()
            )
            pl.when(jnp.logical_and(p.below, p.chip - p.chips + step >= 0))(
                lambda step=step: self.down(step).wait_send()
            )
        for chip in range(p.chips):
            self.side(chip).wait_send()


def scatter_sems(chips):
    dma = pltpu.SemaphoreType.DMA
    return [dma((chips,))] * 6


class Turn:
    def __init__(self, place, weight, slab, first, sems):
        self.p, self.weight, self.slab, self.first = place, weight, slab, first
        self.far_out, self.far_in, self.near_out, self.near_in, self.pass_out, self.pass_in, self.own = sems
        self.height, self.width = weight.shape[0], slab.shape[1]
        self.share = self.height // place.replicas

    def far_rows(self):
        return (self.p.fsdp - 2) * self.share

    def piece(self, block, share):
        at = self.first + block * self.height + share * self.share
        return self.slab.at[pl.ds(pl.multiple_of(at, self.share), self.share)]

    def whole(self, block):
        at = self.first + block * self.height
        return self.slab.at[pl.ds(pl.multiple_of(at, self.height), self.height)]

    def columns(self, to):
        return pl.ds(pl.multiple_of(to * self.width, self.width), self.width)

    def start(self):
        p = self.p

        def send(k, _):
            to = lax.rem(2 * p.chip + 2 + k, p.fsdp)
            share = pl.ds(pl.multiple_of(p.replica * self.share, self.share), self.share)
            remote(
                self.weight.at[share, self.columns(to)],
                self.piece(p.me, p.replica),
                self.far_out,
                self.far_in,
                fsdp=to,
            ).start()
            return 0

        lax.fori_loop(0, p.fsdp - 2, send, 0)
        self.near().start()
        self.mine().start()

    def near(self):
        p = self.p
        return remote(
            self.weight.at[:, self.columns(p.sibling)], self.whole(p.me), self.near_out, self.near_in, fsdp=p.sibling
        )

    def mine(self):
        return pltpu.make_async_copy(self.weight.at[:, self.columns(self.p.me)], self.whole(self.p.me), self.own)

    def await_far(self):
        await_bytes(self.slab.at[pl.ds(0, self.far_rows())], self.far_in)

    def pass_on(self):
        p = self.p

        def one(k, _):
            ref = self.piece(lax.rem(2 * p.chip + 2 + k, p.fsdp), p.replica)

            def send(j, _):
                remote(
                    ref, ref, self.pass_out, self.pass_in, replica=lax.rem(p.replica + j, p.replicas)
                ).start()
                return 0

            return lax.fori_loop(1, p.replicas, send, 0)

        lax.fori_loop(0, p.fsdp - 2, one, 0)

    def finish(self):
        p = self.p
        passed = self.slab.at[pl.ds(0, (p.replicas - 1) * self.far_rows())]
        await_bytes(passed, self.pass_in)
        await_bytes(self.whole(p.sibling), self.near_in)
        self.mine().wait()

    def drain(self):
        p = self.p
        await_bytes(self.slab.at[pl.ds(0, self.far_rows())], self.far_out)
        self.near().wait_send()
        await_bytes(self.slab.at[pl.ds(0, (p.replicas - 1) * self.far_rows())], self.pass_out)


def turn_sems():
    return [pltpu.SemaphoreType.DMA(())] * 7


def partner(values):
    halfway = HEAD_DIM // 2
    width = values.shape[1]
    lane = lax.broadcasted_iota(jnp.int32, values.shape, 1) % HEAD_DIM
    return jnp.where(
        lane < halfway,
        pltpu.roll(values, width - halfway, axis=1),
        pltpu.roll(values, halfway, axis=1),
    )


def front_kernel(
    tokens,
    cotangent,
    gain_one,
    gain_two,
    w_query,
    w_key,
    w_value,
    w_out,
    w_gate,
    w_up,
    w_down,
    cosine,
    sine,
    lowered_one,
    lowered_two_out,
    cotangents,
    slab_qkv_out,
    hidden_out,
    grad_gate_out,
    grad_up_out,
    terms_out,
    sums_out,
    queries,
    keys,
    values,
    attended,
    logs,
    after_attn,
    gains,
    low,
    tiles,
    lowered_two,
    slab_qkv,
    slab_gate,
    slab_up,
    held_down,
    terms,
    across,
    slots,
    tile_hidden,
    tile_gate,
    tile_up,
    tile_terms,
    tile_sums,
    gain_rows,
    gain_out,
    gain_in,
    copy_sems,
    load_sems,
    store_sems,
    *sems,
):
    place = Place()
    chips, block = place.chips, tokens.shape[0]
    model, width = tokens.shape[1], queries.shape[1]
    share = gain_one.shape[1]
    tile = 2 * block
    one_at, cot_at, two_at, scatter_at = sems[:6], sems[6:12], sems[12:18], sems[18:24]
    turn_at = [sems[24 + 7 * i : 31 + 7 * i] for i in range(5)]
    turns = [
        Turn(place, weight, slab_qkv, i * model, turn_at[i])
        for i, weight in enumerate((w_query, w_key, w_value))
    ]
    turn_gate = Turn(place, w_gate, slab_gate, 0, turn_at[3])
    turn_up = Turn(place, w_up, slab_up, 0, turn_at[4])
    here = pl.ds(pl.multiple_of(place.me * block, block), block)

    gain_rows[...] = jnp.zeros_like(gain_rows)
    gain_rows[0:1, :] = gain_one[...].astype(jnp.float32)
    gain_rows[1:2, :] = gain_two[...].astype(jnp.float32)
    load_down = pltpu.make_async_copy(w_down, held_down, copy_sems.at[0])
    load_down.start()
    keep_cot = pltpu.make_async_copy(cotangent, cotangents.at[here], copy_sems.at[1])
    keep_cot.start()
    place.enter()

    def send_gains(k, _):
        to = lax.rem(place.me + k, place.fsdp)
        remote(gain_rows, gains.at[place.me], gain_out, gain_in, fsdp=to).start()
        return 0

    lax.fori_loop(1, place.fsdp, send_gains, 0)
    for turn in turns:
        turn.start()
    gains[place.me] = gain_rows[...]
    inputs = tokens[...].astype(jnp.float32)
    factor = lax.rsqrt(jnp.mean(inputs * inputs, axis=-1, keepdims=True) + eps_norm)
    await_bytes(gains.at[pl.ds(0, place.fsdp - 1)], gain_in)
    for j in range(model // share):
        at = pl.ds(j * share, share)
        normed = tokens[:, at].astype(jnp.float32) * factor
        low[:, at] = (normed * gains[j, 0:1, :]).astype(jnp.bfloat16)
    first = Gather(place, lowered_one, block, one_at, low)
    first.start()
    keep_low = pltpu.make_async_copy(low, lowered_one.at[here], copy_sems.at[2])
    keep_low.start()
    for turn in turns:
        turn.await_far()
        turn.pass_on()
    for step in range(1, chips):
        if step == chips - 1:
            turn_gate.start()
        first.step(step)
    turn_up.start()
    third = Gather(place, cotangents, block, cot_at, cotangent)
    third.start()
    keep_low.wait()
    first.finish()

    def load(source, t, slot):
        return pltpu.make_async_copy(rows_at(source, t, tile), tiles.at[slot], load_sems.at[slot])

    load(lowered_one, 0, 0).start()
    for turn in turns:
        turn.finish()
    keep_slab = pltpu.make_async_copy(slab_qkv, slab_qkv_out, copy_sems.at[3])
    keep_slab.start()
    for t in range(chips):
        if t + 1 < chips:
            load(lowered_one, t + 1, (t + 1) % 2).start()
        load(lowered_one, t, t % 2).wait()
        at = pl.ds(t * tile, tile)
        for i, ref in enumerate((queries, keys, values)):
            out = dot(tiles[t % 2], slab_qkv[i * model : (i + 1) * model, :])
            if i < 2:
                for j in range(0, width, 2 * HEAD_DIM):
                    pair = out[:, j : j + 2 * HEAD_DIM]
                    pair = pair * cosine[at, :] + partner(pair) * sine[at, :]
                    ref[at, j : j + 2 * HEAD_DIM] = pair.astype(jnp.bfloat16)
            else:
                ref[at, :] = out.astype(jnp.bfloat16)
    scatter = Scatter(place, terms, across, slots, block, scatter_at)
    pair = 2 * HEAD_DIM
    for t in range(chips):
        here_t, seen = pl.ds(t * tile, tile), pl.ds(0, (t + 1) * tile)

        def heads(h, _, t=t, here_t=here_t, seen=seen):
            lanes = pl.ds(pl.multiple_of(h * pair, pair), pair)
            q2, k2, v2 = queries[here_t, lanes], keys[seen, lanes], values[seen, lanes]
            mixed, stats = [], []
            for at in (0, HEAD_DIM):
                head = slice(at, at + HEAD_DIM)
                scores = scores_of(q2[:, head], k2[:, head], t * tile)
                most = jnp.max(scores, axis=-1, keepdims=True)
                weights = jnp.exp(scores - most)
                total = jnp.sum(weights, axis=-1, keepdims=True)
                mixed.append(dot((weights / total).astype(jnp.bfloat16), v2[:, head]))
                stats.append(jnp.broadcast_to(most + jnp.log(total), (tile, HEAD_DIM)))
            attended[here_t, lanes] = jnp.concatenate(mixed, axis=1).astype(jnp.bfloat16)
            logs[here_t, lanes] = jnp.concatenate(stats, axis=1)
            return 0

        lax.fori_loop(0, width // pair, heads, 0)
        terms[here_t, :] = dot(attended[here_t, :], w_out[...]).astype(jnp.bfloat16)
        scatter.side(t).start()
    turn_gate.await_far()
    turn_gate.pass_on()
    for t in range(chips):
        scatter.cross(t)
    for step in range(1, chips):
        scatter.step(step)
        if step == 1:
            turn_up.await_far()
            turn_up.pass_on()
        if step < chips - 1:
            third.step(step)
    scatter.finish(after_attn)
    after_attn[...] += tokens[...].astype(jnp.float32)
    after = after_attn[...]
    factor = lax.rsqrt(jnp.mean(after * after, axis=-1, keepdims=True) + eps_norm)
    for j in range(model // share):
        at = pl.ds(j * share, share)
        normed = after_attn[:, at] * factor
        lowered_two[here, at] = (normed * gains[j, 1:2, :]).astype(jnp.bfloat16)
    second = Gather(place, lowered_two, block, two_at)
    second.start()
    third.step(chips - 1)
    keep_cot.wait()
    third.finish()
    load(cotangents, place.nearest(0), 0).start()
    turn_gate.finish()
    turn_up.finish()
    load_down.wait()

    def stores(k, t):
        slot = k % 2
        pairs = (
            (tile_hidden, hidden_out),
            (tile_gate, grad_gate_out),
            (tile_up, grad_up_out),
            (tile_terms, terms_out),
            (tile_sums, sums_out),
        )
        return [
            pltpu.make_async_copy(held.at[slot], rows_at(out, t, tile), store_sems.at[i, slot])
            for i, (held, out) in enumerate(pairs)
        ]

    for k in range(chips):
        t, slot = place.nearest(k), k % 2
        if k > 0:
            second.step(k)
        second.across(t)
        if k + 1 < chips:
            load(cotangents, place.nearest(k + 1), (k + 1) % 2).start()
        load(cotangents, t, slot).wait()
        if k > 1:
            for store in stores(k - 2, place.nearest(k - 2)):
                store.wait()
        rows = lowered_two[pl.ds(pl.multiple_of(t * tile, tile), tile), :]
        gate = dot(rows, slab_gate[...])
        up = dot(rows, slab_up[...])
        grad_hidden = contract_last(tiles[slot], held_down[...])
        sigmoid = jax.nn.sigmoid(gate)
        silu = gate * sigmoid
        hidden = (silu * up).astype(jnp.bfloat16)
        grad_gate = (grad_hidden * up * sigmoid * (1.0 + gate * (1.0 - sigmoid))).astype(jnp.bfloat16)
        grad_up = (grad_hidden * silu).astype(jnp.bfloat16)
        tile_hidden[slot] = hidden
        tile_gate[slot] = grad_gate
        tile_up[slot] = grad_up
        got = contract_last(grad_gate, slab_gate[...]) + contract_last(grad_up, slab_up[...])
        tile_terms[slot] = got.astype(jnp.bfloat16)
        tile_sums[slot] = dot(hidden, held_down[...]).astype(jnp.bfloat16)
        for store in stores(k, t):
            store.start()
    keep_two = pltpu.make_async_copy(lowered_two, lowered_two_out, copy_sems.at[4])
    keep_two.start()
    second.drain()
    scatter.drain()
    for turn in turns + [turn_gate, turn_up]:
        turn.drain()
    await_bytes(gains.at[pl.ds(0, place.fsdp - 1)], gain_out)
    keep_slab.wait()
    for k in range(max(chips - 2, 0), chips):
        for store in stores(k, place.nearest(k)):
            store.wait()
    keep_two.wait()


def front(
    tokens, cotangent, gain_one, gain_two, w_query, w_key, w_value, w_out, w_gate, w_up, w_down, cosine, sine
):
    fsdp = lax.axis_size("fsdp")
    chips = fsdp // 2
    block, model = tokens.shape
    rows, width, wide = fsdp * block, w_query.shape[1] // fsdp, w_gate.shape[1] // fsdp
    tile = 2 * block
    share = gain_one.shape[0]
    low, full = jnp.bfloat16, jnp.float32
    hbm, vmem = pl.BlockSpec(memory_space=pl.ANY), pl.BlockSpec(memory_space=pltpu.VMEM)
    shape = jax.ShapeDtypeStruct
    dma = pltpu.SemaphoreType.DMA
    return pl.pallas_call(
        front_kernel,
        in_specs=[vmem] * 4 + [hbm] * 3 + [vmem] + [hbm] * 3 + [vmem] * 2,
        out_specs=[hbm] * 9 + [vmem] * 7,
        out_shape=[
            shape((rows, model), low),
            shape((rows, model), low),
            shape((rows, model), low),
            shape((3 * model, width), low),
            shape((rows, wide), low),
            shape((rows, wide), low),
            shape((rows, wide), low),
            shape((rows, model), low),
            shape((rows, model), low),
            shape((rows, width), low),
            shape((rows, width), low),
            shape((rows, width), low),
            shape((rows, width), low),
            shape((rows, width), full),
            shape((block, model), full),
            shape((fsdp, 8, share), full),
        ],
        scratch_shapes=[
            pltpu.VMEM((block, model), low),
            pltpu.VMEM((2, tile, model), low),
            pltpu.VMEM((rows, model), low),
            pltpu.VMEM((3 * model, width), low),
            pltpu.VMEM((model, wide), low),
            pltpu.VMEM((model, wide), low),
            pltpu.VMEM((wide, model), low),
            pltpu.VMEM((rows, model), low),
            pltpu.VMEM((chips * block, model), low),
            pltpu.VMEM((chips + 1, block, model), low),
            pltpu.VMEM((2, tile, wide), low),
            pltpu.VMEM((2, tile, wide), low),
            pltpu.VMEM((2, tile, wide), low),
            pltpu.VMEM((2, tile, model), low),
            pltpu.VMEM((2, tile, model), low),
            pltpu.VMEM((8, share), full),
            dma(()),
            dma(()),
            dma((5,)),
            dma((2,)),
            dma((5, 2)),
        ]
        + line_sems(chips) * 3
        + scatter_sems(chips)
        + turn_sems() * 5,
        compiler_params=pltpu.CompilerParams(
            collective_id=0, has_side_effects=True, vmem_limit_bytes=VMEM_LIMIT
        ),
        name="front",
    )(
        tokens,
        cotangent,
        gain_one.reshape(1, -1),
        gain_two.reshape(1, -1),
        w_query,
        w_key,
        w_value,
        w_out,
        w_gate,
        w_up,
        w_down,
        cosine,
        sine,
    )


class Reduce:
    def __init__(self, place, part, out, buffers, sems, turned):
        self.p, self.part, self.out, self.sems, self.turned = place, part, out, sems, turned
        self.own, self.first, self.second = buffers[:2], buffers[2:4], buffers[4:6]
        self.half = part.shape[0] // 2
        self.count = out.shape[0] if turned else 1
        self.width = part.shape[-1] // self.count
        p = place
        self.counts = ((p.wide, p.high), (p.high, p.wide))

    def peer(self, half, stage, k):
        p = self.p
        if half == stage:
            to = lax.rem(p.b + k, p.wide)
            return to, p.a * p.wide + to
        to = lax.rem(p.a + k, p.high)
        return to, to * p.wide + p.b

    def rows(self, half):
        return pl.ds(half * self.half, self.half)

    def sent(self, half, to):
        if half == 0:
            return self.part.at[self.rows(0), :, to]
        return self.part.at[self.rows(1), to]

    def start(self):
        for half in range(2):
            for k in range(1, self.counts[half][0]):
                to, replica = self.peer(half, 0, k)
                remote(
                    self.sent(half, to),
                    self.first[half].at[k - 1],
                    self.sems.at[half, 1],
                    self.sems.at[half, 2],
                    replica=replica,
                ).start()
        for half in range(2):
            mine = self.p.b if half == 0 else self.p.a
            pltpu.make_async_copy(self.sent(half, mine), self.own[half], self.sems.at[half, 0]).start()

    def exchange(self):
        for half in range(2):
            own, arrived = self.own[half], self.first[half]
            await_bytes(arrived, self.sems.at[half, 2])
            await_bytes(own, self.sems.at[half, 0])

            def add(n, _, own=own, arrived=arrived):
                for m in range(own.shape[1]):
                    total = own[n, m].astype(jnp.float32)
                    for k in range(arrived.shape[0]):
                        total += arrived[k, n, m].astype(jnp.float32)
                    own[n, m] = total.astype(own.dtype)
                return 0

            lax.fori_loop(0, self.half, add, 0)
            for k in range(1, self.counts[half][1]):
                to, replica = self.peer(half, 1, k)
                remote(
                    own.at[:, to],
                    self.second[half].at[k - 1],
                    self.sems.at[half, 3],
                    self.sems.at[half, 4],
                    replica=replica,
                ).start()

    def placed(self, half, rows):
        a, b = rows
        if self.turned:
            width = self.out.shape[-1] // 2
            return self.out.at[:, a, b, :, pl.ds(half * width, width)]
        return self.out.at[half, a, b]

    def total(self):
        p = self.p
        for half in range(2):
            own, arrived = self.own[half], self.second[half]
            mine = p.a if half == 0 else p.b
            await_bytes(arrived, self.sems.at[half, 4])

            def add(n, _, own=own, arrived=arrived, mine=mine):
                total = own[n, mine].astype(jnp.float32)
                for k in range(arrived.shape[0]):
                    total += arrived[k, n].astype(jnp.float32)
                own[n, mine] = total.astype(own.dtype)
                return 0

            lax.fori_loop(0, self.half, add, 0)
        if self.turned:
            columns = pl.ds(pl.multiple_of(p.me * self.width, self.width), self.width)

            def each(to, do):
                def all_of(ref):
                    for i in range(self.count):
                        do(ref.at[:, pl.ds(i * self.width, self.width)], self.out.at[i, p.a, p.b, :, columns])

                pl.when(to < self.half)(lambda: all_of(self.own[0].at[to, p.a]))
                pl.when(to >= self.half)(lambda: all_of(self.own[1].at[to - self.half, p.b]))

            def send(k, _):
                to = lax.rem(p.me + k, p.fsdp)
                each(
                    to,
                    lambda ref, target: remote(
                        ref, target, self.sems.at[0, 5], self.sems.at[0, 6], fsdp=to
                    ).start(),
                )
                return 0

            lax.fori_loop(1, p.fsdp, send, 0)
            each(
                p.me,
                lambda ref, target: pltpu.make_async_copy(ref, target, self.sems.at[0, 6]).start(),
            )
        else:
            for half in range(2):
                mine = p.a if half == 0 else p.b
                pltpu.make_async_copy(
                    self.own[half].at[0, mine], self.out.at[half, p.a, p.b], self.sems.at[half, 6]
                ).start()

    def spread(self):
        p = self.p
        if self.turned:
            await_bytes(self.out.at[:, p.a, p.b], self.sems.at[0, 6])
        for half in range(2):
            ref = self.placed(half, (p.a, p.b))
            if not self.turned:
                await_bytes(ref, self.sems.at[half, 6])
            for k in range(1, self.counts[half][1]):
                _, replica = self.peer(half, 1, k)
                remote(ref, ref, self.sems.at[half, 7], self.sems.at[half, 8], replica=replica).start()

    def spread_bytes(self, half):
        some = pl.ds(0, self.counts[half][1] - 1)
        return self.placed(half, (some, 0) if half == 0 else (0, some))

    def held(self, half):
        every = pl.ds(0, self.counts[half][1])
        return self.placed(half, (every, self.p.b) if half == 0 else (self.p.a, every))

    def widen(self):
        for half in range(2):
            await_bytes(self.spread_bytes(half), self.sems.at[half, 8])
            ref = self.held(half)
            for k in range(1, self.counts[half][0]):
                _, replica = self.peer(half, 0, k)
                remote(ref, ref, self.sems.at[half, 9], self.sems.at[half, 10], replica=replica).start()

    def widen_bytes(self, half):
        every, some = pl.ds(0, self.counts[half][1]), pl.ds(0, self.counts[half][0] - 1)
        return self.placed(half, (every, some) if half == 0 else (some, every))

    def finish(self):
        p = self.p
        for half in range(2):
            await_bytes(self.widen_bytes(half), self.sems.at[half, 10])
            await_bytes(self.first[half], self.sems.at[half, 1])
            await_bytes(self.second[half], self.sems.at[half, 3])
            await_bytes(self.spread_bytes(half), self.sems.at[half, 7])
            await_bytes(self.widen_bytes(half), self.sems.at[half, 9])
        if self.turned:
            await_bytes(
                self.out.at[:, p.a, p.b, :, pl.ds(0, (p.fsdp - 1) * self.width)], self.sems.at[0, 5]
            )


def reduce_scratch(n, high, wide, rows, columns):
    low = functools.partial(pltpu.VMEM, dtype=jnp.bfloat16)
    half = n // 2
    return [
        low((half, high, rows, columns)),
        low((half, wide, rows, columns)),
        low((wide - 1, half, high, rows, columns)),
        low((high - 1, half, wide, rows, columns)),
        low((high - 1, half, rows, columns)),
        low((wide - 1, half, rows, columns)),
        pltpu.SemaphoreType.DMA((2, 11)),
    ]


def back_kernel(
    tokens,
    cotangent,
    after_attn,
    gains,
    terms_in,
    part_down,
    part_gate,
    part_up,
    lowered_one,
    slab_qkv,
    w_out,
    queries,
    keys,
    values,
    attended,
    logs,
    cosine,
    sine,
    grad_tokens,
    gain_out,
    out_down,
    out_gate,
    out_up,
    out_qkv,
    out_out,
    terms,
    across,
    slots,
    branch,
    grad_after,
    summed,
    grad_low,
    grad_key,
    grad_value,
    grads,
    part_qkv,
    part_out,
    gain_terms,
    gain_slots,
    gain_sums,
    gain_sems,
    load_sems,
    *rest,
):
    place = Place()
    chips, block = place.chips, tokens.shape[0]
    model, width = tokens.shape[1], queries.shape[1]
    share = gains.shape[2]
    tile = 2 * block
    scatter_at, gather_at, rest = rest[:6], rest[6:12], rest[12:]

    def reducer(i, part, out, turned):
        at = rest[7 * i : 7 * i + 7]
        return Reduce(place, part, out, at[:6], at[6], turned)

    down = reducer(0, part_down, out_down, False)
    gate = reducer(1, part_gate, out_gate, True)
    up = reducer(2, part_up, out_up, True)
    qkv = reducer(3, part_qkv, out_qkv, True)
    out = reducer(4, part_out, out_out, False)

    def load(t):
        at = pl.ds(t * tile, tile)
        return pltpu.make_async_copy(terms_in.at[at], terms.at[at], load_sems.at[t])

    for t in range(chips):
        load(t).start()
    place.enter()
    scatter = Scatter(place, terms, across, slots, block, scatter_at)
    for t in range(chips):
        load(t).wait()
        scatter.side(t).start()
    down.start()
    gate.start()
    up.start()
    for t in range(chips):
        scatter.cross(t)
    for step in range(1, chips):
        if step == chips - 1:
            down.exchange()
        scatter.step(step)
    scatter.finish(summed)

    def norm_back(values, gain_row, grad, result, carried):
        held = values[...].astype(jnp.float32)
        factor = lax.rsqrt(jnp.mean(held * held, axis=-1, keepdims=True) + eps_norm)
        dots = jnp.zeros((block, 1), jnp.float32)
        for j in range(model // share):
            at = pl.ds(j * share, share)
            normed = values[:, at].astype(jnp.float32) * factor
            product = grad[:, at] * normed
            gain_terms[j, gain_row : gain_row + 1, :] = jnp.sum(product, axis=0, keepdims=True)
            dots += jnp.sum(product * gains[j, gain_row : gain_row + 1, :], axis=-1, keepdims=True)
        dots = dots / model
        for j in range(model // share):
            at = pl.ds(j * share, share)
            normed = values[:, at].astype(jnp.float32) * factor
            scaled = grad[:, at] * gains[j, gain_row : gain_row + 1, :]
            result[:, at] = carried[:, at].astype(jnp.float32) + factor * (scaled - normed * dots)

    gain_terms[...] = jnp.zeros_like(gain_terms)
    norm_back(after_attn, 1, summed, grad_after, cotangent)
    here = pl.ds(pl.multiple_of(place.me * block, block), block)
    branch[here, :] = grad_after[...].astype(jnp.bfloat16)
    gather = Gather(place, branch, block, gather_at)
    gather.start()
    scatter.drain()
    for step in range(1, chips):
        if step == chips - 1:
            gate.exchange()
        gather.step(step)
    gather.finish()
    down.total()

    def attend_rows(t, _):
        at = pl.ds(pl.multiple_of(t * tile, tile), tile)
        grad_low[at, :] = contract_last(branch[at, :], w_out[...]).astype(jnp.bfloat16)
        return 0

    lax.fori_loop(0, chips, attend_rows, 0)
    high, wide, piece = place.high, place.wide, part_out.shape[3]
    columns = part_out.shape[-1]
    for half in range(2):
        for at in range(0, columns, 512):
            got = contract_first(
                attended[...], branch[:, half * columns + at : half * columns + at + 512]
            ).astype(jnp.bfloat16)
            part_out[half, :, :, :, at : at + 512] = got.reshape(high, wide, piece, 512)
    out.start()
    reload = pltpu.make_async_copy(lowered_one, branch, load_sems.at[0])
    reload.start()
    down.spread()

    scale = HEAD_DIM**-0.5
    grad_key[...] = jnp.zeros_like(grad_key)
    grad_value[...] = jnp.zeros_like(grad_value)
    pair = 2 * HEAD_DIM
    height = tile * 1024 // max(queries.shape[0], 1024)
    for first in range(0, queries.shape[0], height):
        rows, seen = pl.ds(first, height), pl.ds(0, first + height)

        def heads(h, _, first=first, rows=rows, seen=seen):
            lanes = pl.ds(pl.multiple_of(h * pair, pair), pair)
            q2, g2, log2 = queries[rows, lanes], grad_low[rows, lanes], logs[rows, lanes]
            k2, v2 = keys[seen, lanes], values[seen, lanes]
            for_queries, for_keys, for_values = [], [], []
            for at in (0, HEAD_DIM):
                head = slice(at, at + HEAD_DIM)
                q, g, k = q2[:, head], g2[:, head], k2[:, head]
                weights = jnp.exp(scores_of(q, k, first) - log2[:, at : at + 1])
                grad_weights = contract_last(g, v2[:, head])
                delta = jnp.sum(weights * grad_weights, axis=-1, keepdims=True)
                grad_scores = (weights * (grad_weights - delta)).astype(jnp.bfloat16)
                for_queries.append(dot(grad_scores, k))
                for_keys.append(contract_first(grad_scores, q))
                for_values.append(contract_first(weights.astype(jnp.bfloat16), g))
            got = jnp.concatenate(for_queries, axis=1) * scale
            got = got * cosine[rows, :] - partner(got) * sine[rows, :]
            grads[rows, lanes] = got.astype(jnp.bfloat16)
            grad_key[seen, lanes] += jnp.concatenate(for_keys, axis=1) * scale
            grad_value[seen, lanes] += jnp.concatenate(for_values, axis=1)
            return 0

        lax.fori_loop(0, width // pair, heads, 0)
    up.exchange()
    gate.total()

    def turn_back(t, _):
        at = pl.ds(pl.multiple_of(t * tile, tile), tile)
        for j in range(0, width, pair):
            got = grad_key[at, j : j + pair]
            got = got * cosine[at, :] - partner(got) * sine[at, :]
            grads[at, width + j : width + j + pair] = got.astype(jnp.bfloat16)
        grads[at, 2 * width :] = grad_value[at, :].astype(jnp.bfloat16)
        got = contract_last(grads[at, :width], slab_qkv[:model, :])
        got += contract_last(grads[at, width : 2 * width], slab_qkv[model : 2 * model, :])
        got += contract_last(grads[at, 2 * width :], slab_qkv[2 * model :, :])
        terms[at, :] = got.astype(jnp.bfloat16)
        return 0

    lax.fori_loop(0, chips, turn_back, 0)
    for t in range(chips):
        scatter.side(t).start()
    reload.wait()

    def weigh(j, _):
        rows = part_qkv.shape[3]
        left = branch[:, pl.ds(pl.multiple_of(j * share, share), share)]
        got = contract_first(left, grads[...]).astype(jnp.bfloat16)
        part_qkv[j] = got.reshape(high, wide, rows, 3 * width)
        return 0

    lax.fori_loop(0, place.fsdp, weigh, 0)
    qkv.start()
    for t in range(chips):
        scatter.cross(t)
    for step in range(1, chips):
        scatter.step(step)
    up.total()
    gate.spread()
    out.exchange()
    scatter.finish(summed)
    norm_back(tokens, 0, summed, grad_tokens, grad_after)

    def send_gain(k, _):
        to = lax.rem(place.me + k, place.fsdp)
        remote(
            gain_terms.at[to], gain_slots.at[place.me], gain_sems.at[0], gain_sems.at[1], fsdp=to
        ).start()
        return 0

    lax.fori_loop(1, place.fsdp, send_gain, 0)
    gain_slots[place.me] = gain_terms[place.me]
    down.widen()
    up.spread()
    gate.widen()
    qkv.exchange()
    out.total()
    await_bytes(gain_slots.at[pl.ds(0, place.fsdp - 1)], gain_sems.at[1])
    gain_sums[place.replica] = jnp.sum(gain_slots[...], axis=0)

    def send_sum(k, _):
        ref = gain_sums.at[place.replica]
        to = lax.rem(place.replica + k, place.replicas)
        remote(ref, ref, gain_sems.at[2], gain_sems.at[3], replica=to).start()
        return 0

    lax.fori_loop(1, place.replicas, send_sum, 0)
    qkv.total()
    out.spread()
    up.widen()
    qkv.spread()
    out.widen()
    qkv.widen()
    await_bytes(gain_sums.at[pl.ds(0, place.replicas - 1)], gain_sems.at[3])
    gain_out[...] = jnp.sum(gain_sums[...], axis=0)
    await_bytes(gain_slots.at[pl.ds(0, place.fsdp - 1)], gain_sems.at[0])
    await_bytes(gain_sums.at[pl.ds(0, place.replicas - 1)], gain_sems.at[2])
    scatter.drain()
    for reduce in (down, gate, up, out, qkv):
        reduce.finish()


def back(
    tokens,
    cotangent,
    after_attn,
    gains,
    terms,
    part_down,
    part_gate,
    part_up,
    lowered_one,
    slab_qkv,
    w_out,
    queries,
    keys,
    values,
    attended,
    logs,
    cosine,
    sine,
):
    fsdp, replicas = lax.axis_size("fsdp"), lax.axis_size("replica")
    chips, high, wide = fsdp // 2, 2, replicas // 2
    block, model = tokens.shape
    rows, width = queries.shape
    share = gains.shape[2]
    low, full = jnp.bfloat16, jnp.float32
    hbm, vmem = pl.BlockSpec(memory_space=pl.ANY), pl.BlockSpec(memory_space=pltpu.VMEM)
    shape = jax.ShapeDtypeStruct
    thin = share // replicas
    hidden = part_down.shape[0]
    columns = part_gate.shape[1]
    down_piece = (2, high, wide, hidden // (2 * replicas), model)
    wide_piece = (fsdp, high, wide, thin, columns)
    qkv_piece = (fsdp, high, wide, thin, 3 * width)
    out_piece = (2, high, wide, width // replicas, model // 2)
    dma = pltpu.SemaphoreType.DMA
    return pl.pallas_call(
        back_kernel,
        in_specs=[vmem] * 4 + [hbm] * 5 + [vmem] * 9,
        out_specs=[vmem] * 2 + [hbm] * 5,
        out_shape=[
            shape((block, model), full),
            shape((8, share), full),
            shape(down_piece, low),
            shape((1, high, wide, thin, fsdp * columns), low),
            shape((1, high, wide, thin, fsdp * columns), low),
            shape((3, high, wide, thin, fsdp * width), low),
            shape(out_piece, low),
        ],
        scratch_shapes=[
            pltpu.VMEM((rows, model), low),
            pltpu.VMEM((chips * block, model), low),
            pltpu.VMEM((chips + 1, block, model), low),
            pltpu.VMEM((rows, model), low),
            pltpu.VMEM((block, model), full),
            pltpu.VMEM((block, model), full),
            pltpu.VMEM((rows, width), low),
            pltpu.VMEM((rows, width), full),
            pltpu.VMEM((rows, width), full),
            pltpu.VMEM((rows, 3 * width), low),
            pltpu.VMEM(qkv_piece, low),
            pltpu.VMEM(out_piece, low),
            pltpu.VMEM((fsdp, 8, share), full),
            pltpu.VMEM((fsdp, 8, share), full),
            pltpu.VMEM((replicas, 8, share), full),
            dma((4,)),
            dma((chips,)),
        ]
        + scatter_sems(chips)
        + line_sems(chips)
        + reduce_scratch(*down_piece)
        + reduce_scratch(*wide_piece)
        + reduce_scratch(*wide_piece)
        + reduce_scratch(*qkv_piece)
        + reduce_scratch(*out_piece),
        compiler_params=pltpu.CompilerParams(
            collective_id=1, has_side_effects=True, vmem_limit_bytes=VMEM_LIMIT
        ),
        name="back",
    )(
        tokens,
        cotangent,
        after_attn,
        gains,
        terms,
        part_down.reshape(down_piece),
        part_gate.reshape(wide_piece),
        part_up.reshape(wide_piece),
        lowered_one,
        slab_qkv,
        w_out,
        queries,
        keys,
        values,
        attended,
        logs,
        cosine,
        sine,
    )


def weigh_kernel(low_ref, gate_ref, up_ref, hidden_ref, cot_ref, out_down, out_gate, out_up):
    out_down[...] = contract_first(hidden_ref[...], cot_ref[...]).astype(jnp.bfloat16)
    out_gate[...] = contract_first(low_ref[...], gate_ref[...]).astype(jnp.bfloat16)
    out_up[...] = contract_first(low_ref[...], up_ref[...]).astype(jnp.bfloat16)


def weigh(lowered_two, grad_gate, grad_up, hidden, cotangents):
    rows, model = lowered_two.shape
    wide = hidden.shape[1]
    steps = 4
    low = jnp.bfloat16

    def whole(shape):
        return pl.BlockSpec(shape, lambda i: (0, 0), pipeline_mode=pl.Buffered(1))

    return pl.pallas_call(
        weigh_kernel,
        grid=(steps,),
        in_specs=[
            pl.BlockSpec((rows, model // steps), lambda i: (0, i)),
            whole((rows, wide)),
            whole((rows, wide)),
            pl.BlockSpec((rows, wide // steps), lambda i: (0, i)),
            whole((rows, model)),
        ],
        out_specs=[
            pl.BlockSpec((wide // steps, model), lambda i: (i, 0)),
            pl.BlockSpec((model // steps, wide), lambda i: (i, 0)),
            pl.BlockSpec((model // steps, wide), lambda i: (i, 0)),
        ],
        out_shape=[
            jax.ShapeDtypeStruct((wide, model), low),
            jax.ShapeDtypeStruct((model, wide), low),
            jax.ShapeDtypeStruct((model, wide), low),
        ],
        compiler_params=pltpu.CompilerParams(vmem_limit_bytes=VMEM_LIMIT),
        cost_estimate=pl.CostEstimate(
            flops=6 * rows * model * wide, bytes_accessed=4 * rows * model + 6 * rows * wide + 6 * model * wide, transcendentals=0
        ),
        name="weigh",
    )(lowered_two, grad_gate, grad_up, hidden, cotangents)


def scatter(partial):
    return lax.psum_scatter(partial, "fsdp", scatter_dimension=0, tiled=True).astype(jnp.float32)


def local(
    tokens, attn_gain, w_query, w_key, w_value, w_out, ffn_gain, w_gate, w_up, w_down, cotangent
):
    cosine, sine = rope_tables(tokens.shape[0] * lax.axis_size("fsdp"))
    (
        lowered_one,
        lowered_two,
        cotangents,
        slab_qkv,
        hidden,
        grad_gate,
        grad_up,
        terms,
        sums,
        queries,
        keys,
        values,
        attended,
        logs,
        after_attn,
        gains,
    ) = front(
        tokens,
        cotangent,
        attn_gain,
        ffn_gain,
        w_query,
        w_key,
        w_value,
        w_out,
        w_gate,
        w_up,
        w_down,
        cosine,
        sine,
    )
    outputs = (after_attn + scatter(sums)).astype(jnp.bfloat16)
    part_down, part_gate, part_up = weigh(lowered_two, grad_gate, grad_up, hidden, cotangents)
    grad_tokens, gain_grads, low_down, low_gate, low_up, low_qkv, low_out = back(
        tokens,
        cotangent,
        after_attn,
        gains,
        terms,
        part_down,
        part_gate,
        part_up,
        lowered_one,
        slab_qkv,
        w_out,
        queries,
        keys,
        values,
        attended,
        logs,
        cosine,
        sine,
    )

    def wider(low, like):
        return low.reshape(like.shape).astype(jnp.float32)

    low_out = low_out.reshape(2, w_out.shape[0], -1).transpose(1, 0, 2)
    return (
        outputs,
        grad_tokens,
        gain_grads[0],
        wider(low_qkv[0], w_query),
        wider(low_qkv[1], w_key),
        wider(low_qkv[2], w_value),
        wider(low_out, w_out),
        gain_grads[1],
        wider(low_gate, w_gate),
        wider(low_up, w_up),
        wider(low_down, w_down),
    )


def solution(mesh):
    rows = P("fsdp", None)
    tokens = P(("replica", "fsdp"), None)
    gain = P("fsdp")
    return jax.shard_map(
        local,
        mesh=mesh,
        in_specs=(tokens, gain, rows, rows, rows, rows, gain, rows, rows, rows, tokens),
        out_specs=(tokens, tokens, gain, rows, rows, rows, rows, gain, rows, rows, rows),
        check_vma=False,
    )
```

```python
import functools

import jax
import jax.numpy as jnp
import numpy as np
from jax import lax
from jax.experimental import pallas as pl
from jax.experimental.pallas import tpu as pltpu
from jax.sharding import PartitionSpec as P

HEAD_DIM = 64

eps_norm = 1e-05
rope_base = 130000.0
masked_score = -1e30


def rope_tables(row_count):
    lane = np.arange(2 * HEAD_DIM) % HEAD_DIM
    halfway = HEAD_DIM // 2
    spacing = ((lane % halfway) * np.float32(2.0) / HEAD_DIM).astype(np.float32)
    frequency = np.power(np.float32(rope_base), -spacing)
    angles = np.arange(row_count, dtype=np.float32)[:, None] * frequency[None, :]
    sign = np.where(lane < halfway, -1.0, 1.0).astype(np.float32)
    return np.cos(angles).astype(np.float32), (np.sin(angles) * sign[None, :]).astype(np.float32)


def dot(left, right):
    return jnp.dot(left, right, preferred_element_type=jnp.float32)


def contract_last(left, right):
    return lax.dot_general(
        left, right, (((1,), (1,)), ((), ())), preferred_element_type=jnp.float32
    )


def contract_first(left, right):
    return lax.dot_general(
        left, right, (((0,), (0,)), ((), ())), preferred_element_type=jnp.float32
    )


def scores_of(queries, keys, first_row):
    rows, columns = queries.shape[0], keys.shape[0]
    scores = contract_last(queries, keys) * HEAD_DIM**-0.5
    at_row = lax.broadcasted_iota(jnp.int32, (rows, columns), 0) + first_row
    at_column = lax.broadcasted_iota(jnp.int32, (rows, columns), 1)
    return jnp.where(at_column <= at_row, scores, masked_score)


MESH = pl.DeviceIdType.MESH
VMEM_LIMIT = 60 * 2**20


def remote(src, dst, send, recv, **where):
    return pltpu.make_async_remote_copy(
        src_ref=src, dst_ref=dst, send_sem=send, recv_sem=recv, device_id=where, device_id_type=MESH
    )


def await_bytes(ref, sem):
    pltpu.make_async_copy(ref, ref, sem).wait()


def rows_at(ref, index, size):
    return ref.at[pl.ds(pl.multiple_of(index * size, size), size)]


class Place:
    def __init__(self):
        self.fsdp, self.replicas = lax.axis_size("fsdp"), lax.axis_size("replica")
        self.me, self.replica = lax.axis_index("fsdp"), lax.axis_index("replica")
        self.chips = self.fsdp // 2
        self.chip, self.core = self.me // 2, self.me % 2
        self.sibling = self.me + 1 - 2 * self.core
        self.high, self.wide = 2, self.replicas // 2
        self.a, self.b = self.replica // self.wide, self.replica % self.wide
        self.counts = ((self.wide, self.high), (self.high, self.wide))
        self.above = self.chip + 1 < self.chips
        self.below = self.chip >= 1

    def peer(self, half, stage, k):
        if half == stage:
            to = lax.rem(self.b + k, self.wide)
            return to, self.a * self.wide + to
        to = lax.rem(self.a + k, self.high)
        return to, to * self.wide + self.b

    def nearest(self, k):
        found = jnp.int32(0)
        for chip in range(self.chips):
            order = sorted(range(self.chips), key=lambda other, chip=chip: (abs(other - chip), other))
            found = found + jnp.where(self.chip == chip, order[k], 0)
        return found

    def enter(self):
        barrier = pltpu.get_barrier_semaphore()

        def greet(k, _):
            to = lax.rem(self.me + k, self.fsdp)
            pl.semaphore_signal(barrier, inc=1, device_id={"fsdp": to}, device_id_type=MESH)
            return 0

        def greet_replica(k, _):
            to = lax.rem(self.replica + k, self.replicas)
            pl.semaphore_signal(barrier, inc=1, device_id={"replica": to}, device_id_type=MESH)
            return 0

        lax.fori_loop(1, self.fsdp, greet, 0)
        lax.fori_loop(1, self.replicas, greet_replica, 0)
        pl.semaphore_wait(barrier, self.fsdp - 1 + self.replicas - 1)


def line_sems(chips):
    return [pltpu.SemaphoreType.DMA((chips,))] * 6


class Gather:
    def __init__(self, place, buf, block, sems, own=None):
        self.p, self.buf, self.block, self.own = place, buf, block, own
        self.up_out, self.up_in, self.down_out, self.down_in, self.side_out, self.side_in = sems

    def held(self, chip):
        return rows_at(self.buf, 2 * chip + self.p.core, self.block)

    def up(self, step):
        ref = self.held(self.p.chip - step + 1)
        src = self.own if step == 1 and self.own is not None else ref
        return remote(src, ref, self.up_out.at[step], self.up_in.at[step], fsdp=self.p.me + 2)

    def down(self, step):
        ref = self.held(self.p.chip + step - 1)
        src = self.own if step == 1 and self.own is not None else ref
        return remote(src, ref, self.down_out.at[step], self.down_in.at[step], fsdp=self.p.me - 2)

    def side(self, chip, src=None):
        ref = self.held(chip)
        src = ref if src is None else src
        return remote(src, ref, self.side_out.at[chip], self.side_in.at[chip], fsdp=self.p.sibling)

    def start(self):
        p = self.p
        pl.when(p.above)(lambda: self.up(1).start())
        pl.when(p.below)(lambda: self.down(1).start())
        self.side(p.chip, self.own).start()

    def step(self, step):
        p = self.p
        from_below, from_above = p.chip - step, p.chip + step

        @pl.when(from_below >= 0)
        def _():
            await_bytes(self.held(from_below), self.up_in.at[step])
            if step + 1 < p.chips:
                pl.when(p.above)(lambda: self.up(step + 1).start())
            self.side(from_below).start()

        @pl.when(from_above < p.chips)
        def _():
            await_bytes(self.held(from_above), self.down_in.at[step])
            if step + 1 < p.chips:
                pl.when(p.below)(lambda: self.down(step + 1).start())
            self.side(from_above).start()

    def across(self, chip):
        await_bytes(rows_at(self.buf, 2 * chip + 1 - self.p.core, self.block), self.side_in.at[chip])

    def drain(self):
        p = self.p
        for step in range(1, p.chips):
            pl.when(jnp.logical_and(p.above, p.chip - step + 1 >= 0))(
                lambda step=step: self.up(step).wait_send()
            )
            pl.when(jnp.logical_and(p.below, p.chip + step - 1 < p.chips))(
                lambda step=step: self.down(step).wait_send()
            )
        for chip in range(p.chips):
            self.side(chip).wait_send()

    def finish(self):
        for chip in range(self.p.chips):
            self.across(chip)
        self.drain()


class Scatter:
    def __init__(self, place, terms, across, slots, block, sems):
        self.p, self.terms, self.across, self.slots, self.block = place, terms, across, slots, block
        self.up_out, self.up_in, self.down_out, self.down_in, self.side_out, self.side_in = sems

    def side(self, chip):
        p = self.p
        return remote(
            rows_at(self.terms, 2 * chip + 1 - p.core, self.block),
            rows_at(self.across, chip, self.block),
            self.side_out.at[chip],
            self.side_in.at[chip],
            fsdp=p.sibling,
        )

    def term(self, chip):
        return rows_at(self.terms, 2 * chip + self.p.core, self.block)

    def up(self, step):
        return remote(
            self.term(self.p.chips - step + self.p.chip),
            self.slots.at[step - self.p.chip - 1],
            self.up_out.at[step],
            self.up_in.at[step],
            fsdp=self.p.me + 2,
        )

    def down(self, step):
        return remote(
            self.term(self.p.chip - self.p.chips + step),
            self.slots.at[step + 1],
            self.down_out.at[step],
            self.down_in.at[step],
            fsdp=self.p.me - 2,
        )

    def add(self, chip, arrived):
        term = self.term(chip)
        term[...] = (term[...].astype(jnp.float32) + arrived[...].astype(jnp.float32)).astype(term.dtype)

    def cross(self, chip):
        arrived = rows_at(self.across, chip, self.block)
        await_bytes(arrived, self.side_in.at[chip])
        self.add(chip, arrived)

    def step(self, step):
        p = self.p
        rising, falling = p.chips - step + p.chip, p.chip - p.chips + step

        @pl.when(jnp.logical_and(p.above, rising < p.chips))
        def _():
            if step > 1:

                @pl.when(p.below)
                def _():
                    arrived = self.slots.at[step - 1 - p.chip]
                    await_bytes(arrived, self.up_in.at[step - 1])
                    self.add(rising, arrived)

            self.up(step).start()

        @pl.when(jnp.logical_and(p.below, falling >= 0))
        def _():
            if step > 1:

                @pl.when(p.above)
                def _():
                    arrived = self.slots.at[step]
                    await_bytes(arrived, self.down_in.at[step - 1])
                    self.add(falling, arrived)

            self.down(step).start()

    def finish(self, total):
        p, last = self.p, self.p.chips - 1
        total[...] = self.term(p.chip)[...].astype(jnp.float32)

        @pl.when(p.below)
        def _():
            await_bytes(self.slots.at[last - p.chip], self.up_in.at[last])
            total[...] += self.slots[last - p.chip].astype(jnp.float32)

        @pl.when(p.above)
        def _():
            await_bytes(self.slots.at[last + 1], self.down_in.at[last])
            total[...] += self.slots[last + 1].astype(jnp.float32)

    def drain(self):
        p = self.p
        for step in range(1, p.chips):
            pl.when(jnp.logical_and(p.above, p.chips - step + p.chip < p.chips))(
                lambda step=step: self.up(step).wait_send()
            )
            pl.when(jnp.logical_and(p.below, p.chip - p.chips + step >= 0))(
                lambda step=step: self.down(step).wait_send()
            )
        for chip in range(p.chips):
            self.side(chip).wait_send()


def scatter_sems(chips):
    dma = pltpu.SemaphoreType.DMA
    return [dma((chips,))] * 6


class Turn:
    def __init__(self, place, weight, slab, first, sems):
        self.p, self.weight, self.slab, self.first = place, weight, slab, first
        self.far_out, self.far_in, self.near_out, self.near_in, self.pass_out, self.pass_in, self.own = sems
        self.height, self.width = weight.shape[0], slab.shape[1]
        self.share = self.height // place.replicas

    def far_rows(self):
        return (self.p.fsdp - 2) * self.share

    def piece(self, block, share):
        at = self.first + block * self.height + share * self.share
        return self.slab.at[pl.ds(pl.multiple_of(at, self.share), self.share)]

    def whole(self, block):
        at = self.first + block * self.height
        return self.slab.at[pl.ds(pl.multiple_of(at, self.height), self.height)]

    def columns(self, to):
        return pl.ds(pl.multiple_of(to * self.width, self.width), self.width)

    def start(self):
        p = self.p

        def send(k, _):
            to = lax.rem(2 * p.chip + 2 + k, p.fsdp)
            share = pl.ds(pl.multiple_of(p.replica * self.share, self.share), self.share)
            remote(
                self.weight.at[share, self.columns(to)],
                self.piece(p.me, p.replica),
                self.far_out,
                self.far_in,
                fsdp=to,
            ).start()
            return 0

        lax.fori_loop(0, p.fsdp - 2, send, 0)
        self.near().start()
        self.mine().start()

    def near(self):
        p = self.p
        return remote(
            self.weight.at[:, self.columns(p.sibling)], self.whole(p.me), self.near_out, self.near_in, fsdp=p.sibling
        )

    def mine(self):
        return pltpu.make_async_copy(self.weight.at[:, self.columns(self.p.me)], self.whole(self.p.me), self.own)

    def await_far(self):
        await_bytes(self.slab.at[pl.ds(0, self.far_rows())], self.far_in)

    def pass_on(self):
        p = self.p

        def one(k, _):
            ref = self.piece(lax.rem(2 * p.chip + 2 + k, p.fsdp), p.replica)

            def send(j, _):
                remote(
                    ref, ref, self.pass_out, self.pass_in, replica=lax.rem(p.replica + j, p.replicas)
                ).start()
                return 0

            return lax.fori_loop(1, p.replicas, send, 0)

        lax.fori_loop(0, p.fsdp - 2, one, 0)

    def finish(self):
        p = self.p
        passed = self.slab.at[pl.ds(0, (p.replicas - 1) * self.far_rows())]
        await_bytes(passed, self.pass_in)
        await_bytes(self.whole(p.sibling), self.near_in)
        self.mine().wait()

    def drain(self):
        p = self.p
        await_bytes(self.slab.at[pl.ds(0, self.far_rows())], self.far_out)
        self.near().wait_send()
        await_bytes(self.slab.at[pl.ds(0, (p.replicas - 1) * self.far_rows())], self.pass_out)


def turn_sems():
    return [pltpu.SemaphoreType.DMA(())] * 7


def partner(values):
    halfway = HEAD_DIM // 2
    width = values.shape[1]
    lane = lax.broadcasted_iota(jnp.int32, values.shape, 1) % HEAD_DIM
    return jnp.where(
        lane < halfway,
        pltpu.roll(values, width - halfway, axis=1),
        pltpu.roll(values, halfway, axis=1),
    )


def front_kernel(
    tokens,
    cotangent,
    gain_one,
    gain_two,
    w_query,
    w_key,
    w_value,
    w_out,
    w_gate,
    w_up,
    w_down,
    cosine,
    sine,
    lowered_one,
    lowered_two_out,
    cotangents,
    slab_qkv_out,
    hidden_out,
    grad_gate_out,
    grad_up_out,
    terms_out,
    sums_out,
    queries,
    keys,
    values,
    attended,
    logs,
    after_attn,
    gains,
    low,
    tiles,
    lowered_two,
    slab_qkv,
    slab_gate,
    slab_up,
    held_down,
    terms,
    across,
    slots,
    tile_hidden,
    tile_gate,
    tile_up,
    tile_terms,
    tile_sums,
    gain_rows,
    gain_out,
    gain_in,
    copy_sems,
    load_sems,
    store_sems,
    *sems,
):
    place = Place()
    chips, block = place.chips, tokens.shape[0]
    model, width = tokens.shape[1], queries.shape[1]
    share = gain_one.shape[1]
    tile = 2 * block
    one_at, cot_at, two_at, scatter_at = sems[:6], sems[6:12], sems[12:18], sems[18:24]
    turn_at = [sems[24 + 7 * i : 31 + 7 * i] for i in range(5)]
    turns = [
        Turn(place, weight, slab_qkv, i * model, turn_at[i])
        for i, weight in enumerate((w_query, w_key, w_value))
    ]
    turn_gate = Turn(place, w_gate, slab_gate, 0, turn_at[3])
    turn_up = Turn(place, w_up, slab_up, 0, turn_at[4])
    here = pl.ds(pl.multiple_of(place.me * block, block), block)

    gain_rows[...] = jnp.zeros_like(gain_rows)
    gain_rows[0:1, :] = gain_one[...].astype(jnp.float32)
    gain_rows[1:2, :] = gain_two[...].astype(jnp.float32)
    load_down = pltpu.make_async_copy(w_down, held_down, copy_sems.at[0])
    load_down.start()
    keep_cot = pltpu.make_async_copy(cotangent, cotangents.at[here], copy_sems.at[1])
    keep_cot.start()
    place.enter()

    def send_gains(k, _):
        to = lax.rem(place.me + k, place.fsdp)
        remote(gain_rows, gains.at[place.me], gain_out, gain_in, fsdp=to).start()
        return 0

    lax.fori_loop(1, place.fsdp, send_gains, 0)
    for turn in turns:
        turn.start()
    gains[place.me] = gain_rows[...]
    inputs = tokens[...].astype(jnp.float32)
    factor = lax.rsqrt(jnp.mean(inputs * inputs, axis=-1, keepdims=True) + eps_norm)
    await_bytes(gains.at[pl.ds(0, place.fsdp - 1)], gain_in)
    for j in range(model // share):
        at = pl.ds(j * share, share)
        normed = tokens[:, at].astype(jnp.float32) * factor
        low[:, at] = (normed * gains[j, 0:1, :]).astype(jnp.bfloat16)
    first = Gather(place, lowered_one, block, one_at, low)
    first.start()
    keep_low = pltpu.make_async_copy(low, lowered_one.at[here], copy_sems.at[2])
    keep_low.start()
    for turn in turns:
        turn.await_far()
        turn.pass_on()
    for step in range(1, chips):
        if step == chips - 1:
            turn_gate.start()
        first.step(step)
    turn_up.start()
    third = Gather(place, cotangents, block, cot_at, cotangent)
    third.start()
    keep_low.wait()
    first.finish()

    def load(source, t, slot):
        return pltpu.make_async_copy(rows_at(source, t, tile), tiles.at[slot], load_sems.at[slot])

    load(lowered_one, 0, 0).start()
    for turn in turns:
        turn.finish()
    keep_slab = pltpu.make_async_copy(slab_qkv, slab_qkv_out, copy_sems.at[3])
    keep_slab.start()
    for t in range(chips):
        if t + 1 < chips:
            load(lowered_one, t + 1, (t + 1) % 2).start()
        load(lowered_one, t, t % 2).wait()
        at = pl.ds(t * tile, tile)
        for i, ref in enumerate((queries, keys, values)):
            out = dot(tiles[t % 2], slab_qkv[i * model : (i + 1) * model, :])
            if i < 2:
                for j in range(0, width, 2 * HEAD_DIM):
                    pair = out[:, j : j + 2 * HEAD_DIM]
                    pair = pair * cosine[at, :] + partner(pair) * sine[at, :]
                    ref[at, j : j + 2 * HEAD_DIM] = pair.astype(jnp.bfloat16)
            else:
                ref[at, :] = out.astype(jnp.bfloat16)
    scatter = Scatter(place, terms, across, slots, block, scatter_at)
    pair = 2 * HEAD_DIM
    for t in range(chips):
        here_t, seen = pl.ds(t * tile, tile), pl.ds(0, (t + 1) * tile)

        def heads(h, _, t=t, here_t=here_t, seen=seen):
            lanes = pl.ds(pl.multiple_of(h * pair, pair), pair)
            q2, k2, v2 = queries[here_t, lanes], keys[seen, lanes], values[seen, lanes]
            mixed, stats = [], []
            for at in (0, HEAD_DIM):
                head = slice(at, at + HEAD_DIM)
                scores = scores_of(q2[:, head], k2[:, head], t * tile)
                most = jnp.max(scores, axis=-1, keepdims=True)
                weights = jnp.exp(scores - most)
                total = jnp.sum(weights, axis=-1, keepdims=True)
                mixed.append(dot((weights / total).astype(jnp.bfloat16), v2[:, head]))
                stats.append(jnp.broadcast_to(most + jnp.log(total), (tile, HEAD_DIM)))
            attended[here_t, lanes] = jnp.concatenate(mixed, axis=1).astype(jnp.bfloat16)
            logs[here_t, lanes] = jnp.concatenate(stats, axis=1)
            return 0

        lax.fori_loop(0, width // pair, heads, 0)
        terms[here_t, :] = dot(attended[here_t, :], w_out[...]).astype(jnp.bfloat16)
        scatter.side(t).start()
    turn_gate.await_far()
    turn_gate.pass_on()
    for t in range(chips):
        scatter.cross(t)
    for step in range(1, chips):
        scatter.step(step)
        if step == 1:
            turn_up.await_far()
            turn_up.pass_on()
        if step < chips - 1:
            third.step(step)
    scatter.finish(after_attn)
    after_attn[...] += tokens[...].astype(jnp.float32)
    after = after_attn[...]
    factor = lax.rsqrt(jnp.mean(after * after, axis=-1, keepdims=True) + eps_norm)
    for j in range(model // share):
        at = pl.ds(j * share, share)
        normed = after_attn[:, at] * factor
        lowered_two[here, at] = (normed * gains[j, 1:2, :]).astype(jnp.bfloat16)
    second = Gather(place, lowered_two, block, two_at)
    second.start()
    third.step(chips - 1)
    keep_cot.wait()
    third.finish()
    load(cotangents, place.nearest(0), 0).start()
    turn_gate.finish()
    turn_up.finish()
    load_down.wait()

    def stores(k, t):
        slot = k % 2
        pairs = (
            (tile_hidden, hidden_out),
            (tile_gate, grad_gate_out),
            (tile_up, grad_up_out),
            (tile_terms, terms_out),
            (tile_sums, sums_out),
        )
        return [
            pltpu.make_async_copy(held.at[slot], rows_at(out, t, tile), store_sems.at[i, slot])
            for i, (held, out) in enumerate(pairs)
        ]

    for k in range(chips):
        t, slot = place.nearest(k), k % 2
        if k > 0:
            second.step(k)
        second.across(t)
        if k + 1 < chips:
            load(cotangents, place.nearest(k + 1), (k + 1) % 2).start()
        load(cotangents, t, slot).wait()
        if k > 1:
            for store in stores(k - 2, place.nearest(k - 2)):
                store.wait()
        rows = lowered_two[pl.ds(pl.multiple_of(t * tile, tile), tile), :]
        gate = dot(rows, slab_gate[...])
        up = dot(rows, slab_up[...])
        grad_hidden = contract_last(tiles[slot], held_down[...])
        sigmoid = jax.nn.sigmoid(gate)
        silu = gate * sigmoid
        hidden = (silu * up).astype(jnp.bfloat16)
        grad_gate = (grad_hidden * up * sigmoid * (1.0 + gate * (1.0 - sigmoid))).astype(jnp.bfloat16)
        grad_up = (grad_hidden * silu).astype(jnp.bfloat16)
        tile_hidden[slot] = hidden
        tile_gate[slot] = grad_gate
        tile_up[slot] = grad_up
        got = contract_last(grad_gate, slab_gate[...]) + contract_last(grad_up, slab_up[...])
        tile_terms[slot] = got.astype(jnp.bfloat16)
        tile_sums[slot] = dot(hidden, held_down[...]).astype(jnp.bfloat16)
        for store in stores(k, t):
            store.start()
    keep_two = pltpu.make_async_copy(lowered_two, lowered_two_out, copy_sems.at[4])
    keep_two.start()
    second.drain()
    scatter.drain()
    for turn in turns + [turn_gate, turn_up]:
        turn.drain()
    await_bytes(gains.at[pl.ds(0, place.fsdp - 1)], gain_out)
    keep_slab.wait()
    for k in range(max(chips - 2, 0), chips):
        for store in stores(k, place.nearest(k)):
            store.wait()
    keep_two.wait()


def front(
    tokens, cotangent, gain_one, gain_two, w_query, w_key, w_value, w_out, w_gate, w_up, w_down, cosine, sine
):
    fsdp = lax.axis_size("fsdp")
    chips = fsdp // 2
    block, model = tokens.shape
    rows, width, wide = fsdp * block, w_query.shape[1] // fsdp, w_gate.shape[1] // fsdp
    tile = 2 * block
    share = gain_one.shape[0]
    low, full = jnp.bfloat16, jnp.float32
    hbm, vmem = pl.BlockSpec(memory_space=pl.ANY), pl.BlockSpec(memory_space=pltpu.VMEM)
    shape = jax.ShapeDtypeStruct
    dma = pltpu.SemaphoreType.DMA
    return pl.pallas_call(
        front_kernel,
        in_specs=[vmem] * 4 + [hbm] * 3 + [vmem] + [hbm] * 3 + [vmem] * 2,
        out_specs=[hbm] * 9 + [vmem] * 7,
        out_shape=[
            shape((rows, model), low),
            shape((rows, model), low),
            shape((rows, model), low),
            shape((3 * model, width), low),
            shape((rows, wide), low),
            shape((rows, wide), low),
            shape((rows, wide), low),
            shape((rows, model), low),
            shape((rows, model), low),
            shape((rows, width), low),
            shape((rows, width), low),
            shape((rows, width), low),
            shape((rows, width), low),
            shape((rows, width), full),
            shape((block, model), full),
            shape((fsdp, 8, share), full),
        ],
        scratch_shapes=[
            pltpu.VMEM((block, model), low),
            pltpu.VMEM((2, tile, model), low),
            pltpu.VMEM((rows, model), low),
            pltpu.VMEM((3 * model, width), low),
            pltpu.VMEM((model, wide), low),
            pltpu.VMEM((model, wide), low),
            pltpu.VMEM((wide, model), low),
            pltpu.VMEM((rows, model), low),
            pltpu.VMEM((chips * block, model), low),
            pltpu.VMEM((chips + 1, block, model), low),
            pltpu.VMEM((2, tile, wide), low),
            pltpu.VMEM((2, tile, wide), low),
            pltpu.VMEM((2, tile, wide), low),
            pltpu.VMEM((2, tile, model), low),
            pltpu.VMEM((2, tile, model), low),
            pltpu.VMEM((8, share), full),
            dma(()),
            dma(()),
            dma((5,)),
            dma((2,)),
            dma((5, 2)),
        ]
        + line_sems(chips) * 3
        + scatter_sems(chips)
        + turn_sems() * 5,
        compiler_params=pltpu.CompilerParams(
            collective_id=0, has_side_effects=True, vmem_limit_bytes=VMEM_LIMIT
        ),
        name="front",
    )(
        tokens,
        cotangent,
        gain_one.reshape(1, -1),
        gain_two.reshape(1, -1),
        w_query,
        w_key,
        w_value,
        w_out,
        w_gate,
        w_up,
        w_down,
        cosine,
        sine,
    )


class Reduce:
    def __init__(self, place, part, first, second, sems):
        self.p, self.part, self.first, self.second, self.sems = place, part, first, second, sems
        self.half = part.shape[0] // 2

    def rows(self, half):
        return pl.ds(half * self.half, self.half)

    def sent(self, half, to):
        if half == 0:
            return self.part.at[self.rows(0), :, to]
        return self.part.at[self.rows(1), to]

    def own(self, half):
        return self.sent(half, self.p.b if half == 0 else self.p.a)

    def start(self):
        for half in range(2):
            for k in range(1, self.p.counts[half][0]):
                to, replica = self.p.peer(half, 0, k)
                remote(
                    self.sent(half, to),
                    self.first[half].at[k - 1],
                    self.sems.at[half, 0],
                    self.sems.at[half, 1],
                    replica=replica,
                ).start()

    def exchange(self):
        for half in range(2):
            own, arrived = self.own(half), self.first[half]
            await_bytes(arrived, self.sems.at[half, 1])

            def add(n, _, own=own, arrived=arrived):
                for m in range(own.shape[1]):
                    total = own[n, m].astype(jnp.float32)
                    for k in range(arrived.shape[0]):
                        total += arrived[k, n, m].astype(jnp.float32)
                    own[n, m] = total.astype(own.dtype)
                return 0

            lax.fori_loop(0, self.half, add, 0)
            for k in range(1, self.p.counts[half][1]):
                to, replica = self.p.peer(half, 1, k)
                remote(
                    own.at[:, to],
                    self.second[half].at[k - 1],
                    self.sems.at[half, 2],
                    self.sems.at[half, 3],
                    replica=replica,
                ).start()

    def total(self):
        for half in range(2):
            own, arrived = self.held(half), self.second[half]
            await_bytes(arrived, self.sems.at[half, 3])

            def add(n, _, own=own, arrived=arrived):
                total = own[n].astype(jnp.float32)
                for k in range(arrived.shape[0]):
                    total += arrived[k, n].astype(jnp.float32)
                own[n] = total.astype(own.dtype)
                return 0

            lax.fori_loop(0, self.half, add, 0)

    def held(self, half):
        return self.part.at[self.rows(half), self.p.a, self.p.b]

    def piece(self, n):
        return self.part.at[n, self.p.a, self.p.b]

    def drain(self):
        for half in range(2):
            await_bytes(self.first[half], self.sems.at[half, 0])
            await_bytes(self.second[half], self.sems.at[half, 2])


def reduce_scratch(n, high, wide, rows, columns):
    low = functools.partial(pltpu.VMEM, dtype=jnp.bfloat16)
    half = n // 2
    return [
        low((n, high, wide, rows, columns)),
        low((wide - 1, half, high, rows, columns)),
        low((high - 1, half, wide, rows, columns)),
        low((high - 1, half, rows, columns)),
        low((wide - 1, half, rows, columns)),
        pltpu.SemaphoreType.DMA((2, 4)),
    ]


def reducer(place, refs):
    part, first_a, first_b, second_a, second_b, sems = refs
    return Reduce(place, part, (first_a, first_b), (second_a, second_b), sems)


class Spread:
    def __init__(self, place, piece, out, sems, turned):
        self.p, self.piece, self.out, self.sems, self.turned = place, piece, out, sems, turned

    def start(self):
        p = self.p
        if self.turned:
            count = self.out.shape[0]
            width = self.out.shape[-1] // p.fsdp
            columns = pl.ds(pl.multiple_of(p.me * width, width), width)

            def pairs(to):
                ref = self.piece(to)
                return [
                    (ref.at[:, pl.ds(i * width, width)], self.out.at[i, p.a, p.b, :, columns])
                    for i in range(count)
                ]

            def send(k, _):
                to = lax.rem(p.me + k, p.fsdp)
                for ref, target in pairs(to):
                    remote(ref, target, self.sems.at[0, 0], self.sems.at[0, 1], fsdp=to).start()
                return 0

            lax.fori_loop(1, p.fsdp, send, 0)
            for ref, target in pairs(p.me):
                pltpu.make_async_copy(ref, target, self.sems.at[0, 1]).start()
        else:
            for half in range(2):
                pltpu.make_async_copy(
                    self.piece(half), self.out.at[half, p.a, p.b], self.sems.at[half, 1]
                ).start()

    def placed(self, half, rows):
        a, b = rows
        if self.turned:
            width = self.out.shape[-1] // 2
            return self.out.at[:, a, b, :, pl.ds(half * width, width)]
        return self.out.at[half, a, b]

    def spread(self):
        p = self.p
        if self.turned:
            await_bytes(self.out.at[:, p.a, p.b], self.sems.at[0, 1])
        for half in range(2):
            ref = self.placed(half, (p.a, p.b))
            src = ref if self.turned else self.piece(half)
            for k in range(1, p.counts[half][1]):
                _, replica = p.peer(half, 1, k)
                remote(src, ref, self.sems.at[half, 2], self.sems.at[half, 3], replica=replica).start()

    def spread_bytes(self, half):
        some = pl.ds(0, self.p.counts[half][1] - 1)
        return self.placed(half, (some, 0) if half == 0 else (0, some))

    def widen(self):
        p = self.p
        for half in range(2):
            if not self.turned:
                await_bytes(self.placed(half, (p.a, p.b)), self.sems.at[half, 1])
            await_bytes(self.spread_bytes(half), self.sems.at[half, 3])
            every = pl.ds(0, p.counts[half][1])
            ref = self.placed(half, (every, p.b) if half == 0 else (p.a, every))
            for k in range(1, p.counts[half][0]):
                _, replica = p.peer(half, 0, k)
                remote(ref, ref, self.sems.at[half, 4], self.sems.at[half, 5], replica=replica).start()

    def widen_bytes(self, half):
        counts = self.p.counts[half]
        every, some = pl.ds(0, counts[1]), pl.ds(0, counts[0] - 1)
        return self.placed(half, (every, some) if half == 0 else (some, every))

    def finish(self):
        p = self.p
        for half in range(2):
            await_bytes(self.widen_bytes(half), self.sems.at[half, 5])
            await_bytes(self.spread_bytes(half), self.sems.at[half, 2])
            await_bytes(self.widen_bytes(half), self.sems.at[half, 4])
        if self.turned:
            width = self.out.shape[-1] // p.fsdp
            await_bytes(
                self.out.at[:, p.a, p.b, :, pl.ds(0, (p.fsdp - 1) * width)], self.sems.at[0, 0]
            )


def spread_sems():
    return [pltpu.SemaphoreType.DMA((2, 6))]


def norm_back(values, gain_row, gains, grad, carried, result, gain_terms):
    block, model = values.shape
    share = gains.shape[2]
    held = values[...].astype(jnp.float32)
    factor = lax.rsqrt(jnp.mean(held * held, axis=-1, keepdims=True) + eps_norm)
    dots = jnp.zeros((block, 1), jnp.float32)
    for j in range(model // share):
        at = pl.ds(j * share, share)
        normed = values[:, at].astype(jnp.float32) * factor
        product = grad[:, at] * normed
        gain_terms[j, gain_row : gain_row + 1, :] = jnp.sum(product, axis=0, keepdims=True)
        dots += jnp.sum(product * gains[j, gain_row : gain_row + 1, :], axis=-1, keepdims=True)
    dots = dots / model
    for j in range(model // share):
        at = pl.ds(j * share, share)
        normed = values[:, at].astype(jnp.float32) * factor
        scaled = grad[:, at] * gains[j, gain_row : gain_row + 1, :]
        result[:, at] = carried[:, at].astype(jnp.float32) + factor * (scaled - normed * dots)


def weigh_kernel(
    cotangent,
    after_attn,
    gains,
    terms_in,
    lowered_two,
    cotangents,
    hidden_in,
    grad_gate_in,
    grad_up_in,
    grad_after,
    gain_terms,
    branch,
    sum_down,
    sum_gate,
    sum_up,
    tokens_held,
    hidden,
    grad_gate,
    grad_up,
    terms,
    across,
    slots,
    summed,
    low,
    load_sems,
    store_sems,
    *rest,
):
    place = Place()
    chips, block = place.chips, cotangent.shape[0]
    model = cotangent.shape[1]
    tile = 2 * block
    scatter_at, gather_at = rest[:6], rest[6:12]
    down, gate, up = [reducer(place, rest[12 + 6 * i : 18 + 6 * i]) for i in range(3)]

    def load(t):
        at = pl.ds(t * tile, tile)
        return pltpu.make_async_copy(terms_in.at[at], terms.at[at], load_sems.at[t])

    loads = [
        pltpu.make_async_copy(source, target, load_sems.at[chips + i])
        for i, (source, target) in enumerate(
            (
                (cotangents, tokens_held),
                (hidden_in, hidden),
                (grad_gate_in, grad_gate),
                (grad_up_in, grad_up),
                (lowered_two, tokens_held),
            )
        )
    ]
    for t in range(chips):
        load(t).start()
    for copy in loads[:4]:
        copy.start()
    place.enter()
    scatter = Scatter(place, terms, across, slots, block, scatter_at)
    for t in range(chips):
        load(t).wait()
        scatter.side(t).start()
    gain_terms[...] = jnp.zeros_like(gain_terms)
    loads[0].wait()
    loads[1].wait()
    _, high, wide, thin, _ = down.part.shape
    columns = min(tile, hidden.shape[1])
    for i in range(0, hidden.shape[1], columns):
        got = contract_first(hidden[:, i : i + columns], tokens_held[...]).astype(jnp.bfloat16)
        for m in range(0, columns, thin):
            n = (i + m) // thin
            down.part[n // (high * wide), n // wide % high, n % wide] = got[m : m + thin, :]
    loads[4].start()
    down.start()
    for t in range(chips):
        scatter.cross(t)
    scatter.step(1)
    loads[4].wait()

    def weigh(reduce, grads):
        share = model // place.fsdp

        def rows(j, _):
            left = tokens_held[:, pl.ds(pl.multiple_of(j * share, share), share)]
            got = contract_first(left, grads[...]).astype(jnp.bfloat16)
            reduce.part[j] = got.reshape(reduce.part.shape[1:])
            return 0

        lax.fori_loop(0, place.fsdp, rows, 0)
        reduce.start()

    loads[2].wait()
    weigh(gate, grad_gate)
    if chips > 2:
        scatter.step(2)
    loads[3].wait()
    weigh(up, grad_up)
    for step in range(3, chips):
        scatter.step(step)
    scatter.finish(summed)
    norm_back(after_attn, 1, gains, summed, cotangent, grad_after, gain_terms)
    low[...] = grad_after[...].astype(jnp.bfloat16)
    here = pl.ds(pl.multiple_of(place.me * block, block), block)
    gather = Gather(place, branch, block, gather_at, low)
    gather.start()
    keep = pltpu.make_async_copy(low, branch.at[here], store_sems.at[0])
    keep.start()
    scatter.drain()
    down.exchange()
    for step in range(1, chips):
        gather.step(step)
        if step == 1:
            gate.exchange()
        if step == max(chips - 2, 1):
            up.exchange()
    keep.wait()
    gather.finish()
    stores = []
    for i, (reduce, out) in enumerate(((down, sum_down), (gate, sum_gate), (up, sum_up))):
        reduce.total()
        for half in range(2):
            store = pltpu.make_async_copy(
                reduce.held(half), out.at[reduce.rows(half)], store_sems.at[1 + 2 * i + half]
            )
            store.start()
            stores.append(store)
    for reduce in (down, gate, up):
        reduce.drain()
    for store in stores:
        store.wait()


def weigh(cotangent, after_attn, gains, terms, lowered_two, cotangents, hidden, grad_gate, grad_up):
    fsdp, replicas = lax.axis_size("fsdp"), lax.axis_size("replica")
    chips, high, wide = fsdp // 2, 2, replicas // 2
    block, model = cotangent.shape
    rows, columns = hidden.shape
    share = gains.shape[2]
    low, full = jnp.bfloat16, jnp.float32
    hbm, vmem = pl.BlockSpec(memory_space=pl.ANY), pl.BlockSpec(memory_space=pltpu.VMEM)
    shape = jax.ShapeDtypeStruct
    down_piece = (2, high, wide, columns // (2 * replicas), model)
    wide_piece = (fsdp, high, wide, share // replicas, columns)
    dma = pltpu.SemaphoreType.DMA
    return pl.pallas_call(
        weigh_kernel,
        in_specs=[vmem] * 3 + [hbm] * 6,
        out_specs=[vmem] * 2 + [hbm] * 4,
        out_shape=[
            shape((block, model), full),
            shape((fsdp, 8, share), full),
            shape((rows, model), low),
            shape((2,) + down_piece[3:], low),
            shape((fsdp,) + wide_piece[3:], low),
            shape((fsdp,) + wide_piece[3:], low),
        ],
        scratch_shapes=[
            pltpu.VMEM((rows, model), low),
            pltpu.VMEM((rows, columns), low),
            pltpu.VMEM((rows, columns), low),
            pltpu.VMEM((rows, columns), low),
            pltpu.VMEM((rows, model), low),
            pltpu.VMEM((chips * block, model), low),
            pltpu.VMEM((chips + 1, block, model), low),
            pltpu.VMEM((block, model), full),
            pltpu.VMEM((block, model), low),
            dma((chips + 5,)),
            dma((7,)),
        ]
        + scatter_sems(chips)
        + line_sems(chips)
        + reduce_scratch(*down_piece)
        + reduce_scratch(*wide_piece)
        + reduce_scratch(*wide_piece),
        compiler_params=pltpu.CompilerParams(
            collective_id=1, has_side_effects=True, vmem_limit_bytes=VMEM_LIMIT
        ),
        name="weigh",
    )(cotangent, after_attn, gains, terms, lowered_two, cotangents, hidden, grad_gate, grad_up)


def back_kernel(
    tokens,
    gains,
    grad_after,
    gain_terms_in,
    sum_down,
    sum_gate,
    sum_up,
    branch_in,
    lowered_one,
    slab_qkv,
    w_out,
    queries,
    keys,
    values,
    attended,
    logs,
    cosine,
    sine,
    grad_tokens,
    gain_out,
    out_down,
    out_gate,
    out_up,
    out_qkv,
    out_out,
    terms,
    across,
    slots,
    branch,
    summed,
    grad_low,
    grad_key,
    grad_value,
    grads,
    gain_terms,
    gain_slots,
    gain_sums,
    gain_sems,
    load_sems,
    *rest,
):
    place = Place()
    chips, block = place.chips, tokens.shape[0]
    model, width = tokens.shape[1], queries.shape[1]
    share = gains.shape[2]
    tile = 2 * block
    scatter_at, rest = rest[:6], rest[6:]
    down = Spread(place, lambda n: sum_down.at[n], out_down, rest[0], False)
    gate = Spread(place, lambda n: sum_gate.at[n], out_gate, rest[1], True)
    up = Spread(place, lambda n: sum_up.at[n], out_up, rest[2], True)
    qkv, out = reducer(place, rest[5:11]), reducer(place, rest[11:17])
    qkv_spread = Spread(place, qkv.piece, out_qkv, rest[3], True)
    out_spread = Spread(place, out.piece, out_out, rest[4], False)
    load = pltpu.make_async_copy(branch_in, branch, load_sems.at[0])
    load.start()
    place.enter()
    down.start()
    down.spread()
    gate.start()
    up.start()
    load.wait()

    def attend_rows(t, _):
        at = pl.ds(pl.multiple_of(t * tile, tile), tile)
        grad_low[at, :] = contract_last(branch[at, :], w_out[...]).astype(jnp.bfloat16)
        return 0

    lax.fori_loop(0, chips, attend_rows, 0)
    _, high, wide, thin, columns = out.part.shape
    for half in range(2):
        for at in range(0, columns, 512):
            got = contract_first(
                attended[...], branch[:, half * columns + at : half * columns + at + 512]
            ).astype(jnp.bfloat16)
            out.part[half, :, :, :, at : at + 512] = got.reshape(high, wide, thin, 512)
    out.start()
    reload = pltpu.make_async_copy(lowered_one, branch, load_sems.at[1])
    reload.start()
    down.widen()

    scale = HEAD_DIM**-0.5
    grad_key[...] = jnp.zeros_like(grad_key)
    grad_value[...] = jnp.zeros_like(grad_value)
    pair = 2 * HEAD_DIM
    height = tile * 1024 // max(queries.shape[0], 1024)
    for first in range(0, queries.shape[0], height):
        rows, seen = pl.ds(first, height), pl.ds(0, first + height)

        def heads(h, _, first=first, rows=rows, seen=seen):
            lanes = pl.ds(pl.multiple_of(h * pair, pair), pair)
            q2, g2, log2 = queries[rows, lanes], grad_low[rows, lanes], logs[rows, lanes]
            k2, v2 = keys[seen, lanes], values[seen, lanes]
            for_queries, for_keys, for_values = [], [], []
            for at in (0, HEAD_DIM):
                head = slice(at, at + HEAD_DIM)
                q, g, k = q2[:, head], g2[:, head], k2[:, head]
                weights = jnp.exp(scores_of(q, k, first) - log2[:, at : at + 1])
                grad_weights = contract_last(g, v2[:, head])
                delta = jnp.sum(weights * grad_weights, axis=-1, keepdims=True)
                grad_scores = (weights * (grad_weights - delta)).astype(jnp.bfloat16)
                for_queries.append(dot(grad_scores, k))
                for_keys.append(contract_first(grad_scores, q))
                for_values.append(contract_first(weights.astype(jnp.bfloat16), g))
            got = jnp.concatenate(for_queries, axis=1) * scale
            got = got * cosine[rows, :] - partner(got) * sine[rows, :]
            grads[rows, lanes] = got.astype(jnp.bfloat16)
            grad_key[seen, lanes] += jnp.concatenate(for_keys, axis=1) * scale
            grad_value[seen, lanes] += jnp.concatenate(for_values, axis=1)
            return 0

        lax.fori_loop(0, width // pair, heads, 0)
    gate.spread()

    def turn_back(t, _):
        at = pl.ds(pl.multiple_of(t * tile, tile), tile)
        for j in range(0, width, pair):
            got = grad_key[at, j : j + pair]
            got = got * cosine[at, :] - partner(got) * sine[at, :]
            grads[at, width + j : width + j + pair] = got.astype(jnp.bfloat16)
        grads[at, 2 * width :] = grad_value[at, :].astype(jnp.bfloat16)
        got = contract_last(grads[at, :width], slab_qkv[:model, :])
        got += contract_last(grads[at, width : 2 * width], slab_qkv[model : 2 * model, :])
        got += contract_last(grads[at, 2 * width :], slab_qkv[2 * model :, :])
        terms[at, :] = got.astype(jnp.bfloat16)
        return 0

    lax.fori_loop(0, chips, turn_back, 0)
    scatter = Scatter(place, terms, across, slots, block, scatter_at)
    for t in range(chips):
        scatter.side(t).start()
    reload.wait()

    def weigh_rows(j, _):
        left = branch[:, pl.ds(pl.multiple_of(j * share, share), share)]
        got = contract_first(left, grads[...]).astype(jnp.bfloat16)
        qkv.part[j] = got.reshape(qkv.part.shape[1:])
        return 0

    lax.fori_loop(0, place.fsdp, weigh_rows, 0)
    qkv.start()
    up.spread()
    out.exchange()
    for t in range(chips):
        scatter.cross(t)
    for step in range(1, chips):
        scatter.step(step)
        if step == 1:
            gate.widen()
        if step == max(chips - 2, 1):
            qkv.exchange()
    out.total()
    out_spread.start()
    out_spread.spread()
    scatter.finish(summed)
    gain_terms[...] = gain_terms_in[...]
    norm_back(tokens, 0, gains, summed, grad_after, grad_tokens, gain_terms)

    def send_gain(k, _):
        to = lax.rem(place.me + k, place.fsdp)
        remote(
            gain_terms.at[to], gain_slots.at[place.me], gain_sems.at[0], gain_sems.at[1], fsdp=to
        ).start()
        return 0

    lax.fori_loop(1, place.fsdp, send_gain, 0)
    gain_slots[place.me] = gain_terms[place.me]
    qkv.total()
    qkv_spread.start()
    up.widen()
    await_bytes(gain_slots.at[pl.ds(0, place.fsdp - 1)], gain_sems.at[1])
    gain_sums[place.replica] = jnp.sum(gain_slots[...], axis=0)

    def send_sum(k, _):
        ref = gain_sums.at[place.replica]
        to = lax.rem(place.replica + k, place.replicas)
        remote(ref, ref, gain_sems.at[2], gain_sems.at[3], replica=to).start()
        return 0

    lax.fori_loop(1, place.replicas, send_sum, 0)
    qkv_spread.spread()
    out_spread.widen()
    qkv_spread.widen()
    await_bytes(gain_sums.at[pl.ds(0, place.replicas - 1)], gain_sems.at[3])
    gain_out[...] = jnp.sum(gain_sums[...], axis=0)
    await_bytes(gain_slots.at[pl.ds(0, place.fsdp - 1)], gain_sems.at[0])
    await_bytes(gain_sums.at[pl.ds(0, place.replicas - 1)], gain_sems.at[2])
    scatter.drain()
    qkv.drain()
    out.drain()
    for spread in (down, gate, up, out_spread, qkv_spread):
        spread.finish()


def back(
    tokens,
    gains,
    grad_after,
    gain_terms,
    sum_down,
    sum_gate,
    sum_up,
    branch,
    lowered_one,
    slab_qkv,
    w_out,
    queries,
    keys,
    values,
    attended,
    logs,
    cosine,
    sine,
):
    fsdp, replicas = lax.axis_size("fsdp"), lax.axis_size("replica")
    chips, high, wide = fsdp // 2, 2, replicas // 2
    block, model = tokens.shape
    rows, width = queries.shape
    share = gains.shape[2]
    low, full = jnp.bfloat16, jnp.float32
    hbm, vmem = pl.BlockSpec(memory_space=pl.ANY), pl.BlockSpec(memory_space=pltpu.VMEM)
    shape = jax.ShapeDtypeStruct
    thin = share // replicas
    columns = sum_gate.shape[-1]
    qkv_piece = (fsdp, high, wide, thin, 3 * width)
    out_piece = (2, high, wide, width // replicas, model // 2)
    dma = pltpu.SemaphoreType.DMA
    return pl.pallas_call(
        back_kernel,
        in_specs=[vmem] * 4 + [hbm] * 5 + [vmem] * 9,
        out_specs=[vmem] * 2 + [hbm] * 5,
        out_shape=[
            shape((block, model), full),
            shape((8, share), full),
            shape((2, high, wide) + sum_down.shape[1:], low),
            shape((1, high, wide, thin, fsdp * columns), low),
            shape((1, high, wide, thin, fsdp * columns), low),
            shape((3, high, wide, thin, fsdp * width), low),
            shape(out_piece, low),
        ],
        scratch_shapes=[
            pltpu.VMEM((rows, model), low),
            pltpu.VMEM((chips * block, model), low),
            pltpu.VMEM((chips + 1, block, model), low),
            pltpu.VMEM((rows, model), low),
            pltpu.VMEM((block, model), full),
            pltpu.VMEM((rows, width), low),
            pltpu.VMEM((rows, width), full),
            pltpu.VMEM((rows, width), full),
            pltpu.VMEM((rows, 3 * width), low),
            pltpu.VMEM((fsdp, 8, share), full),
            pltpu.VMEM((fsdp, 8, share), full),
            pltpu.VMEM((replicas, 8, share), full),
            dma((4,)),
            dma((2,)),
        ]
        + scatter_sems(chips)
        + spread_sems() * 5
        + reduce_scratch(*qkv_piece)
        + reduce_scratch(*out_piece),
        compiler_params=pltpu.CompilerParams(
            collective_id=2, has_side_effects=True, vmem_limit_bytes=VMEM_LIMIT
        ),
        name="back",
    )(
        tokens,
        gains,
        grad_after,
        gain_terms,
        sum_down,
        sum_gate,
        sum_up,
        branch,
        lowered_one,
        slab_qkv,
        w_out,
        queries,
        keys,
        values,
        attended,
        logs,
        cosine,
        sine,
    )


def scatter(partial):
    return lax.psum_scatter(partial, "fsdp", scatter_dimension=0, tiled=True).astype(jnp.float32)


def local(
    tokens, attn_gain, w_query, w_key, w_value, w_out, ffn_gain, w_gate, w_up, w_down, cotangent
):
    cosine, sine = rope_tables(tokens.shape[0] * lax.axis_size("fsdp"))
    (
        lowered_one,
        lowered_two,
        cotangents,
        slab_qkv,
        hidden,
        grad_gate,
        grad_up,
        terms,
        sums,
        queries,
        keys,
        values,
        attended,
        logs,
        after_attn,
        gains,
    ) = front(
        tokens,
        cotangent,
        attn_gain,
        ffn_gain,
        w_query,
        w_key,
        w_value,
        w_out,
        w_gate,
        w_up,
        w_down,
        cosine,
        sine,
    )
    grad_after, gain_terms, branch, sum_down, sum_gate, sum_up = weigh(
        cotangent, after_attn, gains, terms, lowered_two, cotangents, hidden, grad_gate, grad_up
    )
    sums, grad_after = lax.optimization_barrier((sums, grad_after))
    outputs = (after_attn + scatter(sums)).astype(jnp.bfloat16)
    grad_tokens, gain_grads, low_down, low_gate, low_up, low_qkv, low_out = back(
        tokens,
        gains,
        grad_after,
        gain_terms,
        sum_down,
        sum_gate,
        sum_up,
        branch,
        lowered_one,
        slab_qkv,
        w_out,
        queries,
        keys,
        values,
        attended,
        logs,
        cosine,
        sine,
    )

    def wider(low, like):
        return low.reshape(like.shape).astype(jnp.float32)

    low_out = low_out.reshape(2, w_out.shape[0], -1).transpose(1, 0, 2)
    return (
        outputs,
        grad_tokens,
        gain_grads[0],
        wider(low_qkv[0], w_query),
        wider(low_qkv[1], w_key),
        wider(low_qkv[2], w_value),
        wider(low_out, w_out),
        gain_grads[1],
        wider(low_gate, w_gate),
        wider(low_up, w_up),
        wider(low_down, w_down),
    )


def solution(mesh):
    rows = P("fsdp", None)
    tokens = P(("replica", "fsdp"), None)
    gain = P("fsdp")
    return jax.shard_map(
        local,
        mesh=mesh,
        in_specs=(tokens, gain, rows, rows, rows, rows, gain, rows, rows, rows, tokens),
        out_specs=(tokens, tokens, gain, rows, rows, rows, rows, gain, rows, rows, rows),
        check_vma=False,
    )
```

```python
import functools

import jax
import jax.numpy as jnp
import numpy as np
from jax import lax
from jax.experimental import pallas as pl
from jax.experimental.pallas import tpu as pltpu
from jax.sharding import PartitionSpec as P

HEAD_DIM = 64

eps_norm = 1e-05
rope_base = 130000.0
masked_score = -1e30


def rope_tables(row_count):
    lane = np.arange(2 * HEAD_DIM) % HEAD_DIM
    halfway = HEAD_DIM // 2
    spacing = ((lane % halfway) * np.float32(2.0) / HEAD_DIM).astype(np.float32)
    frequency = np.power(np.float32(rope_base), -spacing)
    angles = np.arange(row_count, dtype=np.float32)[:, None] * frequency[None, :]
    sign = np.where(lane < halfway, -1.0, 1.0).astype(np.float32)
    return np.cos(angles).astype(np.float32), (np.sin(angles) * sign[None, :]).astype(np.float32)


def dot(left, right):
    return jnp.dot(left, right, preferred_element_type=jnp.float32)


def contract_last(left, right):
    return lax.dot_general(
        left, right, (((1,), (1,)), ((), ())), preferred_element_type=jnp.float32
    )


def contract_first(left, right):
    return lax.dot_general(
        left, right, (((0,), (0,)), ((), ())), preferred_element_type=jnp.float32
    )


def scores_of(queries, keys, first_row):
    rows, columns = queries.shape[0], keys.shape[0]
    scores = contract_last(queries, keys) * HEAD_DIM**-0.5
    at_row = lax.broadcasted_iota(jnp.int32, (rows, columns), 0) + first_row
    at_column = lax.broadcasted_iota(jnp.int32, (rows, columns), 1)
    return jnp.where(at_column <= at_row, scores, masked_score)


MESH = pl.DeviceIdType.MESH
VMEM_LIMIT = 60 * 2**20


def remote(src, dst, send, recv, **where):
    return pltpu.make_async_remote_copy(
        src_ref=src, dst_ref=dst, send_sem=send, recv_sem=recv, device_id=where, device_id_type=MESH
    )


def await_bytes(ref, sem):
    pltpu.make_async_copy(ref, ref, sem).wait()


def rows_at(ref, index, size):
    return ref.at[pl.ds(pl.multiple_of(index * size, size), size)]


class Place:
    def __init__(self):
        self.fsdp, self.replicas = lax.axis_size("fsdp"), lax.axis_size("replica")
        self.me, self.replica = lax.axis_index("fsdp"), lax.axis_index("replica")
        self.chips = self.fsdp // 2
        self.chip, self.core = self.me // 2, self.me % 2
        self.sibling = self.me + 1 - 2 * self.core
        self.high, self.wide = 2, self.replicas // 2
        self.a, self.b = self.replica // self.wide, self.replica % self.wide
        self.counts = ((self.wide, self.high), (self.high, self.wide))
        self.above = self.chip + 1 < self.chips
        self.below = self.chip >= 1

    def peer(self, half, stage, k):
        if half == stage:
            to = lax.rem(self.b + k, self.wide)
            return to, self.a * self.wide + to
        to = lax.rem(self.a + k, self.high)
        return to, to * self.wide + self.b

    def at_step(self, step, do):
        if step == 0:
            do(self.chip)
            return
        pl.when(self.chip >= step)(lambda: do(self.chip - step))
        pl.when(self.chip + step < self.chips)(lambda: do(self.chip + step))

    def nearest(self, k):
        found = jnp.int32(0)
        for chip in range(self.chips):
            order = sorted(range(self.chips), key=lambda other, chip=chip: (abs(other - chip), other))
            found = found + jnp.where(self.chip == chip, order[k], 0)
        return found

    def enter(self):
        barrier = pltpu.get_barrier_semaphore()

        def greet(k, _):
            to = lax.rem(self.me + k, self.fsdp)
            pl.semaphore_signal(barrier, inc=1, device_id={"fsdp": to}, device_id_type=MESH)
            return 0

        def greet_replica(k, _):
            to = lax.rem(self.replica + k, self.replicas)
            pl.semaphore_signal(barrier, inc=1, device_id={"replica": to}, device_id_type=MESH)
            return 0

        lax.fori_loop(1, self.fsdp, greet, 0)
        lax.fori_loop(1, self.replicas, greet_replica, 0)
        pl.semaphore_wait(barrier, self.fsdp - 1 + self.replicas - 1)


def line_sems(chips):
    return [pltpu.SemaphoreType.DMA((chips,))] * 6


class Gather:
    def __init__(self, place, buf, block, sems, own=None):
        self.p, self.buf, self.block, self.own = place, buf, block, own
        self.up_out, self.up_in, self.down_out, self.down_in, self.side_out, self.side_in = sems

    def held(self, chip):
        return rows_at(self.buf, 2 * chip + self.p.core, self.block)

    def up(self, step):
        ref = self.held(self.p.chip - step + 1)
        src = self.own if step == 1 and self.own is not None else ref
        return remote(src, ref, self.up_out.at[step], self.up_in.at[step], fsdp=self.p.me + 2)

    def down(self, step):
        ref = self.held(self.p.chip + step - 1)
        src = self.own if step == 1 and self.own is not None else ref
        return remote(src, ref, self.down_out.at[step], self.down_in.at[step], fsdp=self.p.me - 2)

    def side(self, chip, src=None):
        ref = self.held(chip)
        src = ref if src is None else src
        return remote(src, ref, self.side_out.at[chip], self.side_in.at[chip], fsdp=self.p.sibling)

    def start(self):
        p = self.p
        pl.when(p.above)(lambda: self.up(1).start())
        pl.when(p.below)(lambda: self.down(1).start())
        self.side(p.chip, self.own).start()

    def step(self, step):
        p = self.p
        from_below, from_above = p.chip - step, p.chip + step

        @pl.when(from_below >= 0)
        def _():
            await_bytes(self.held(from_below), self.up_in.at[step])
            if step + 1 < p.chips:
                pl.when(p.above)(lambda: self.up(step + 1).start())
            self.side(from_below).start()

        @pl.when(from_above < p.chips)
        def _():
            await_bytes(self.held(from_above), self.down_in.at[step])
            if step + 1 < p.chips:
                pl.when(p.below)(lambda: self.down(step + 1).start())
            self.side(from_above).start()

    def across(self, chip):
        await_bytes(rows_at(self.buf, 2 * chip + 1 - self.p.core, self.block), self.side_in.at[chip])

    def drain(self):
        p = self.p
        for step in range(1, p.chips):
            pl.when(jnp.logical_and(p.above, p.chip - step + 1 >= 0))(
                lambda step=step: self.up(step).wait_send()
            )
            pl.when(jnp.logical_and(p.below, p.chip + step - 1 < p.chips))(
                lambda step=step: self.down(step).wait_send()
            )
        for chip in range(p.chips):
            self.side(chip).wait_send()

    def finish(self):
        for chip in range(self.p.chips):
            self.across(chip)
        self.drain()


class Scatter:
    def __init__(self, place, terms, across, slots, block, sems):
        self.p, self.terms, self.across, self.slots, self.block = place, terms, across, slots, block
        self.up_out, self.up_in, self.down_out, self.down_in, self.side_out, self.side_in = sems

    def side(self, chip):
        p = self.p
        return remote(
            rows_at(self.terms, 2 * chip + 1 - p.core, self.block),
            rows_at(self.across, chip, self.block),
            self.side_out.at[chip],
            self.side_in.at[chip],
            fsdp=p.sibling,
        )

    def term(self, chip):
        return rows_at(self.terms, 2 * chip + self.p.core, self.block)

    def up(self, step):
        return remote(
            self.term(self.p.chips - step + self.p.chip),
            self.slots.at[step - self.p.chip - 1],
            self.up_out.at[step],
            self.up_in.at[step],
            fsdp=self.p.me + 2,
        )

    def down(self, step):
        return remote(
            self.term(self.p.chip - self.p.chips + step),
            self.slots.at[step + 1],
            self.down_out.at[step],
            self.down_in.at[step],
            fsdp=self.p.me - 2,
        )

    def add(self, chip, arrived):
        term = self.term(chip)
        term[...] = (term[...].astype(jnp.float32) + arrived[...].astype(jnp.float32)).astype(term.dtype)

    def cross(self, chip):
        arrived = rows_at(self.across, chip, self.block)
        await_bytes(arrived, self.side_in.at[chip])
        self.add(chip, arrived)

    def step(self, step):
        p = self.p
        rising, falling = p.chips - step + p.chip, p.chip - p.chips + step

        @pl.when(jnp.logical_and(p.above, rising < p.chips))
        def _():
            if step > 1:

                @pl.when(p.below)
                def _():
                    arrived = self.slots.at[step - 1 - p.chip]
                    await_bytes(arrived, self.up_in.at[step - 1])
                    self.add(rising, arrived)

            self.up(step).start()

        @pl.when(jnp.logical_and(p.below, falling >= 0))
        def _():
            if step > 1:

                @pl.when(p.above)
                def _():
                    arrived = self.slots.at[step]
                    await_bytes(arrived, self.down_in.at[step - 1])
                    self.add(falling, arrived)

            self.down(step).start()

    def finish(self, total):
        p, last = self.p, self.p.chips - 1
        total[...] = self.term(p.chip)[...].astype(jnp.float32)

        @pl.when(p.below)
        def _():
            await_bytes(self.slots.at[last - p.chip], self.up_in.at[last])
            total[...] += self.slots[last - p.chip].astype(jnp.float32)

        @pl.when(p.above)
        def _():
            await_bytes(self.slots.at[last + 1], self.down_in.at[last])
            total[...] += self.slots[last + 1].astype(jnp.float32)

    def drain(self):
        p = self.p
        for step in range(1, p.chips):
            pl.when(jnp.logical_and(p.above, p.chips - step + p.chip < p.chips))(
                lambda step=step: self.up(step).wait_send()
            )
            pl.when(jnp.logical_and(p.below, p.chip - p.chips + step >= 0))(
                lambda step=step: self.down(step).wait_send()
            )
        for chip in range(p.chips):
            self.side(chip).wait_send()


def scatter_sems(chips):
    dma = pltpu.SemaphoreType.DMA
    return [dma((chips,))] * 6


class Turn:
    def __init__(self, place, weight, slab, first, sems):
        self.p, self.weight, self.slab, self.first = place, weight, slab, first
        self.far_out, self.far_in, self.near_out, self.near_in, self.own, self.passing = sems
        self.height, self.width = weight.shape[0], slab.shape[1]
        self.share = self.height // place.replicas

    def far_rows(self):
        return (self.p.fsdp - 2) * self.share

    def piece(self, block, share):
        at = self.first + block * self.height + share * self.share
        return self.slab.at[pl.ds(pl.multiple_of(at, self.share), self.share)]

    def whole(self, block):
        at = self.first + block * self.height
        return self.slab.at[pl.ds(pl.multiple_of(at, self.height), self.height)]

    def columns(self, to):
        return pl.ds(pl.multiple_of(to * self.width, self.width), self.width)

    def start(self):
        p = self.p

        def send(k, _):
            to = lax.rem(2 * p.chip + 2 + k, p.fsdp)
            share = pl.ds(pl.multiple_of(p.replica * self.share, self.share), self.share)
            remote(
                self.weight.at[share, self.columns(to)],
                self.piece(p.me, p.replica),
                self.far_out,
                self.far_in,
                fsdp=to,
            ).start()
            return 0

        lax.fori_loop(0, p.fsdp - 2, send, 0)
        self.near().start()
        self.mine().start()

    def near(self):
        p = self.p
        return remote(
            self.weight.at[:, self.columns(p.sibling)], self.whole(p.me), self.near_out, self.near_in, fsdp=p.sibling
        )

    def mine(self):
        return pltpu.make_async_copy(self.weight.at[:, self.columns(self.p.me)], self.whole(self.p.me), self.own)

    def await_far(self):
        await_bytes(self.slab.at[pl.ds(0, self.far_rows())], self.far_in)

    def bytes_of(self, pieces):
        return self.slab.at[pl.ds(0, pieces * self.share)]

    def pass_bytes(self, half, stage):
        first, second = self.p.counts[half]
        return self.bytes_of((self.p.chips - 1) * (second - 1 if stage == 0 else second * (first - 1)))

    def send_pieces(self, half, stage, shares):
        p = self.p

        def one(i, _):
            block = lax.rem(2 * p.chip + 2 + 2 * i + half, p.fsdp)
            for share in shares:
                ref = self.piece(block, share)
                for k in range(1, p.counts[half][1 - stage]):
                    _, replica = p.peer(half, 1 - stage, k)
                    remote(
                        ref,
                        ref,
                        self.passing.at[half, 2 * stage],
                        self.passing.at[half, 2 * stage + 1],
                        replica=replica,
                    ).start()
            return 0

        lax.fori_loop(0, p.chips - 1, one, 0)

    def pass_on(self):
        for half in range(2):
            self.send_pieces(half, 0, [self.p.replica])

    def pass_far(self):
        p = self.p
        for half in range(2):
            await_bytes(self.pass_bytes(half, 0), self.passing.at[half, 1])
            if half == 0:
                shares = [a * p.wide + p.b for a in range(p.high)]
            else:
                shares = [p.a * p.wide + b for b in range(p.wide)]
            self.send_pieces(half, 1, shares)

    def finish(self):
        for half in range(2):
            await_bytes(self.pass_bytes(half, 1), self.passing.at[half, 3])
        await_bytes(self.whole(self.p.sibling), self.near_in)
        self.mine().wait()

    def drain(self):
        await_bytes(self.slab.at[pl.ds(0, self.far_rows())], self.far_out)
        self.near().wait_send()
        for half in range(2):
            await_bytes(self.pass_bytes(half, 0), self.passing.at[half, 0])
            await_bytes(self.pass_bytes(half, 1), self.passing.at[half, 2])


def turn_sems():
    return [pltpu.SemaphoreType.DMA(())] * 5 + [pltpu.SemaphoreType.DMA((2, 4))]


class Everywhere:
    def __init__(self, place, buf, block, sems, side_sems):
        self.p, self.buf, self.block, self.sems, self.side_sems = place, buf, block, sems, side_sems
        self.width = buf.shape[3] // 2

    def columns(self, half):
        return pl.ds(half * self.width, self.width)

    def rows(self, chip):
        at = (2 * chip + self.p.core) * self.block
        return pl.ds(pl.multiple_of(at, self.block), self.block)

    def ref(self, half, a, b, chip):
        return self.buf.at[a, b, self.rows(chip), self.columns(half)]

    def spread(self, chip, own=None):
        p = self.p
        for half in range(2):
            ref = self.ref(half, p.a, p.b, chip)
            src = ref if own is None else own.at[:, self.columns(half)]
            for k in range(1, p.counts[half][1]):
                _, replica = p.peer(half, 1, k)
                remote(
                    src, ref, self.sems.at[chip, half, 0], self.sems.at[chip, half, 1], replica=replica
                ).start()

    def spread_bytes(self, half, chip):
        some = pl.ds(0, self.p.counts[half][1] - 1)
        return self.ref(half, some, 0, chip) if half == 0 else self.ref(half, 0, some, chip)

    def widen(self, chip):
        p = self.p
        for half in range(2):
            await_bytes(self.spread_bytes(half, chip), self.sems.at[chip, half, 1])
            every = pl.ds(0, p.counts[half][1])
            ref = self.ref(half, every, p.b, chip) if half == 0 else self.ref(half, p.a, every, chip)
            for k in range(1, p.counts[half][0]):
                _, replica = p.peer(half, 0, k)
                remote(
                    ref, ref, self.sems.at[chip, half, 2], self.sems.at[chip, half, 3], replica=replica
                ).start()

    def widen_bytes(self, half, chip):
        counts = self.p.counts[half]
        every, some = pl.ds(0, counts[1]), pl.ds(0, counts[0] - 1)
        return self.ref(half, every, some, chip) if half == 0 else self.ref(half, some, every, chip)

    def share(self, chip):
        p = self.p
        for half in range(2):
            await_bytes(self.widen_bytes(half, chip), self.sems.at[chip, half, 3])
        for k in range(1, p.replicas):
            other = lax.rem(p.replica + k, p.replicas)
            ref = self.buf.at[other // p.wide, other % p.wide, self.rows(chip)]
            remote(
                ref, ref, self.side_sems.at[chip, 0], self.side_sems.at[chip, 1], fsdp=p.sibling
            ).start()

    def finish(self):
        shared = self.buf.at[0, 0, pl.ds(0, (self.p.replicas - 1) * self.block)]
        for chip in range(self.p.chips):
            await_bytes(shared, self.side_sems.at[chip, 1])
            await_bytes(shared, self.side_sems.at[chip, 0])
            for half in range(2):
                await_bytes(self.spread_bytes(half, chip), self.sems.at[chip, half, 0])
                await_bytes(self.widen_bytes(half, chip), self.sems.at[chip, half, 2])


def partner(values):
    halfway = HEAD_DIM // 2
    width = values.shape[1]
    lane = lax.broadcasted_iota(jnp.int32, values.shape, 1) % HEAD_DIM
    return jnp.where(
        lane < halfway,
        pltpu.roll(values, width - halfway, axis=1),
        pltpu.roll(values, halfway, axis=1),
    )


def front_kernel(
    tokens,
    cotangent,
    gain_one,
    gain_two,
    w_query,
    w_key,
    w_value,
    w_out,
    w_gate,
    w_up,
    w_down,
    cosine,
    sine,
    lowered_one,
    lowered_two_out,
    all_cotangents,
    slab_qkv_out,
    all_hidden,
    grad_gate_out,
    grad_up_out,
    terms_out,
    sums_out,
    queries,
    keys,
    values,
    attended,
    logs,
    after_attn,
    gains,
    low,
    tiles,
    lowered_two,
    slab_qkv,
    slab_gate,
    slab_up,
    held_down,
    terms,
    across,
    slots,
    tile_hidden,
    tile_gate,
    tile_up,
    tile_terms,
    tile_sums,
    gain_rows,
    gain_out,
    gain_in,
    copy_sems,
    load_sems,
    store_sems,
    hidden_sems,
    every_sems,
    every_side,
    *sems,
):
    place = Place()
    chips, block = place.chips, tokens.shape[0]
    model, width = tokens.shape[1], queries.shape[1]
    share = gain_one.shape[0]
    tile = 2 * block
    one_at, cot_at, two_at, scatter_at = sems[:6], sems[6:12], sems[12:18], sems[18:24]
    turn_at = [sems[24 + 6 * i : 30 + 6 * i] for i in range(5)]
    cotangents = all_cotangents.at[place.a, place.b]
    every = Everywhere(place, all_cotangents, block, every_sems, every_side)
    turns = [
        Turn(place, weight, slab_qkv, i * model, turn_at[i])
        for i, weight in enumerate((w_query, w_key, w_value))
    ]
    turn_gate = Turn(place, w_gate, slab_gate, 0, turn_at[3])
    turn_up = Turn(place, w_up, slab_up, 0, turn_at[4])
    here = pl.ds(pl.multiple_of(place.me * block, block), block)

    gain_rows[...] = jnp.zeros_like(gain_rows)
    gain_rows[0, :] = gain_one[...].astype(jnp.float32)
    gain_rows[1, :] = gain_two[...].astype(jnp.float32)
    load_down = pltpu.make_async_copy(w_down, held_down, copy_sems.at[0])
    load_down.start()
    keep_cot = pltpu.make_async_copy(cotangent, cotangents.at[here], copy_sems.at[1])
    keep_cot.start()
    place.enter()

    def send_gains(k, _):
        to = lax.rem(place.me + k, place.fsdp)
        remote(gain_rows, gains.at[place.me], gain_out, gain_in, fsdp=to).start()
        return 0

    lax.fori_loop(1, place.fsdp, send_gains, 0)
    for turn in turns:
        turn.start()
    every.spread(place.chip, cotangent)
    gains[place.me] = gain_rows[...]
    inputs = tokens[...].astype(jnp.float32)
    factor = lax.rsqrt(jnp.mean(inputs * inputs, axis=-1, keepdims=True) + eps_norm)
    await_bytes(gains.at[pl.ds(0, place.fsdp - 1)], gain_in)
    for j in range(model // share):
        at = pl.ds(j * share, share)
        normed = tokens[:, at].astype(jnp.float32) * factor
        low[:, at] = (normed * gains[j, 0:1, :]).astype(jnp.bfloat16)
    first = Gather(place, lowered_one, block, one_at, low)
    first.start()
    keep_low = pltpu.make_async_copy(low, lowered_one.at[here], copy_sems.at[2])
    keep_low.start()
    for turn in turns:
        turn.await_far()
        turn.pass_on()
    for step in range(1, chips):
        if step == chips - 1:
            turn_gate.start()
        first.step(step)
        if step == 1:
            for turn in turns:
                turn.pass_far()
            keep_cot.wait()
            every.widen(place.chip)
    turn_up.start()
    third = Gather(place, cotangents, block, cot_at, cotangent)
    third.start()
    keep_low.wait()
    every.share(place.chip)
    first.finish()

    def load(source, t, slot):
        return pltpu.make_async_copy(rows_at(source, t, tile), tiles.at[slot], load_sems.at[slot])

    load(lowered_one, 0, 0).start()
    for turn in turns:
        turn.finish()
    keep_slab = pltpu.make_async_copy(slab_qkv, slab_qkv_out, copy_sems.at[3])
    keep_slab.start()
    for t in range(chips):
        if t + 1 < chips:
            load(lowered_one, t + 1, (t + 1) % 2).start()
        load(lowered_one, t, t % 2).wait()
        at = pl.ds(t * tile, tile)
        for i, ref in enumerate((queries, keys, values)):
            out = dot(tiles[t % 2], slab_qkv[i * model : (i + 1) * model, :])
            if i < 2:
                for j in range(0, width, 2 * HEAD_DIM):
                    pair = out[:, j : j + 2 * HEAD_DIM]
                    pair = pair * cosine[at, :] + partner(pair) * sine[at, :]
                    ref[at, j : j + 2 * HEAD_DIM] = pair.astype(jnp.bfloat16)
            else:
                ref[at, :] = out.astype(jnp.bfloat16)
    scatter = Scatter(place, terms, across, slots, block, scatter_at)
    pair = 2 * HEAD_DIM
    for t in range(chips):
        here_t, seen = pl.ds(t * tile, tile), pl.ds(0, (t + 1) * tile)

        def heads(h, _, t=t, here_t=here_t, seen=seen):
            lanes = pl.ds(pl.multiple_of(h * pair, pair), pair)
            q2, k2, v2 = queries[here_t, lanes], keys[seen, lanes], values[seen, lanes]
            mixed, stats = [], []
            for at in (0, HEAD_DIM):
                head = slice(at, at + HEAD_DIM)
                scores = scores_of(q2[:, head], k2[:, head], t * tile)
                most = jnp.max(scores, axis=-1, keepdims=True)
                weights = jnp.exp(scores - most)
                total = jnp.sum(weights, axis=-1, keepdims=True)
                mixed.append(dot((weights / total).astype(jnp.bfloat16), v2[:, head]))
                stats.append(jnp.broadcast_to(most + jnp.log(total), (tile, HEAD_DIM)))
            attended[here_t, lanes] = jnp.concatenate(mixed, axis=1).astype(jnp.bfloat16)
            logs[here_t, lanes] = jnp.concatenate(stats, axis=1)
            return 0

        lax.fori_loop(0, width // pair, heads, 0)
        terms[here_t, :] = dot(attended[here_t, :], w_out[...]).astype(jnp.bfloat16)
        scatter.side(t).start()
    turn_gate.await_far()
    turn_gate.pass_on()
    for t in range(chips):
        scatter.cross(t)
    for step in range(1, chips):
        scatter.step(step)
        if step == 1:
            turn_up.await_far()
            turn_up.pass_on()
            turn_gate.pass_far()
        if step == max(chips - 2, 1):
            turn_up.pass_far()
        if step < chips - 1:
            third.step(step)
            place.at_step(step, every.spread)
    scatter.finish(after_attn)
    after_attn[...] += tokens[...].astype(jnp.float32)
    after = after_attn[...]
    factor = lax.rsqrt(jnp.mean(after * after, axis=-1, keepdims=True) + eps_norm)
    for j in range(model // share):
        at = pl.ds(j * share, share)
        normed = after_attn[:, at] * factor
        lowered_two[here, at] = (normed * gains[j, 1:2, :]).astype(jnp.bfloat16)
    second = Gather(place, lowered_two, block, two_at)
    second.start()
    third.step(chips - 1)
    place.at_step(chips - 1, every.spread)
    place.at_step(1, every.widen)
    third.finish()
    load(cotangents, place.nearest(0), 0).start()
    turn_gate.finish()
    turn_up.finish()
    load_down.wait()

    def stores(k, t):
        slot = k % 2
        pairs = (
            (tile_hidden.at[:, place.replica], all_hidden.at[place.replica]),
            (tile_gate, grad_gate_out),
            (tile_up, grad_up_out),
            (tile_terms, terms_out),
            (tile_sums, sums_out),
        )
        return [
            pltpu.make_async_copy(held.at[slot], rows_at(out, t, tile), store_sems.at[i, slot])
            for i, (held, out) in enumerate(pairs)
        ]

    def hidden_bytes(slot):
        return tile_hidden.at[slot, pl.ds(0, place.replicas - 1)]

    for k in range(chips):
        t, slot = place.nearest(k), k % 2
        if k > 0:
            second.step(k)
            if k + 1 < chips:
                place.at_step(k + 1, every.widen)
            place.at_step(k, every.share)
        second.across(t)
        if k + 1 < chips:
            load(cotangents, place.nearest(k + 1), (k + 1) % 2).start()
        load(cotangents, t, slot).wait()
        if k > 1:
            for store in stores(k - 2, place.nearest(k - 2)):
                store.wait()
            await_bytes(hidden_bytes(slot), hidden_sems.at[slot])
        rows = lowered_two[pl.ds(pl.multiple_of(t * tile, tile), tile), :]
        gate = dot(rows, slab_gate[...])
        up = dot(rows, slab_up[...])
        grad_hidden = contract_last(tiles[slot], held_down[...])
        sigmoid = jax.nn.sigmoid(gate)
        silu = gate * sigmoid
        hidden = (silu * up).astype(jnp.bfloat16)
        grad_gate = (grad_hidden * up * sigmoid * (1.0 + gate * (1.0 - sigmoid))).astype(jnp.bfloat16)
        grad_up = (grad_hidden * silu).astype(jnp.bfloat16)
        part = tile_hidden.shape[3]
        for other in range(place.replicas):
            tile_hidden[slot, other] = hidden[:, other * part : (other + 1) * part]
        tile_gate[slot] = grad_gate
        tile_up[slot] = grad_up
        got = contract_last(grad_gate, slab_gate[...]) + contract_last(grad_up, slab_up[...])
        tile_terms[slot] = got.astype(jnp.bfloat16)
        tile_sums[slot] = dot(hidden, held_down[...]).astype(jnp.bfloat16)
        for store in stores(k, t):
            store.start()
        for j in range(1, place.replicas):
            to = lax.rem(place.replica + j, place.replicas)
            remote(
                tile_hidden.at[slot, to],
                rows_at(all_hidden.at[place.replica], t, tile),
                hidden_sems.at[slot],
                hidden_sems.at[2],
                replica=to,
            ).start()
    keep_two = pltpu.make_async_copy(lowered_two, lowered_two_out, copy_sems.at[4])
    keep_two.start()
    second.drain()
    scatter.drain()
    for turn in turns + [turn_gate, turn_up]:
        turn.drain()
    await_bytes(gains.at[pl.ds(0, place.fsdp - 1)], gain_out)
    keep_slab.wait()
    for k in range(max(chips - 2, 0), chips):
        for store in stores(k, place.nearest(k)):
            store.wait()
        await_bytes(hidden_bytes(k % 2), hidden_sems.at[k % 2])
    await_bytes(all_hidden.at[pl.ds(0, place.replicas - 1)], hidden_sems.at[2])
    every.finish()
    keep_two.wait()


def front(
    tokens, cotangent, gain_one, gain_two, w_query, w_key, w_value, w_out, w_gate, w_up, w_down, cosine, sine
):
    fsdp, replicas = lax.axis_size("fsdp"), lax.axis_size("replica")
    chips, high, across_b = fsdp // 2, 2, replicas // 2
    block, model = tokens.shape
    rows, width, wide = fsdp * block, w_query.shape[1] // fsdp, w_gate.shape[1] // fsdp
    tile = 2 * block
    share = gain_one.shape[0]
    low, full = jnp.bfloat16, jnp.float32
    hbm, vmem = pl.BlockSpec(memory_space=pl.ANY), pl.BlockSpec(memory_space=pltpu.VMEM)
    shape = jax.ShapeDtypeStruct
    dma = pltpu.SemaphoreType.DMA
    return pl.pallas_call(
        front_kernel,
        in_specs=[vmem] * 4 + [hbm] * 3 + [vmem] + [hbm] * 3 + [vmem] * 2,
        out_specs=[hbm] * 9 + [vmem] * 7,
        out_shape=[
            shape((rows, model), low),
            shape((rows, model), low),
            shape((high, across_b, rows, model), low),
            shape((3 * model, width), low),
            shape((replicas, rows, wide // replicas), low),
            shape((rows, wide), low),
            shape((rows, wide), low),
            shape((rows, model), low),
            shape((rows, model), low),
            shape((rows, width), low),
            shape((rows, width), low),
            shape((rows, width), low),
            shape((rows, width), low),
            shape((rows, width), full),
            shape((block, model), full),
            shape((fsdp, 8, share), full),
        ],
        scratch_shapes=[
            pltpu.VMEM((block, model), low),
            pltpu.VMEM((2, tile, model), low),
            pltpu.VMEM((rows, model), low),
            pltpu.VMEM((3 * model, width), low),
            pltpu.VMEM((model, wide), low),
            pltpu.VMEM((model, wide), low),
            pltpu.VMEM((wide, model), low),
            pltpu.VMEM((rows, model), low),
            pltpu.VMEM((chips * block, model), low),
            pltpu.VMEM((chips + 1, block, model), low),
            pltpu.VMEM((2, replicas, tile, wide // replicas), low),
            pltpu.VMEM((2, tile, wide), low),
            pltpu.VMEM((2, tile, wide), low),
            pltpu.VMEM((2, tile, model), low),
            pltpu.VMEM((2, tile, model), low),
            pltpu.VMEM((8, share), full),
            dma(()),
            dma(()),
            dma((5,)),
            dma((2,)),
            dma((5, 2)),
            dma((3,)),
            dma((chips, 2, 4)),
            dma((chips, 2)),
        ]
        + line_sems(chips) * 3
        + scatter_sems(chips)
        + turn_sems() * 5,
        compiler_params=pltpu.CompilerParams(
            collective_id=0, has_side_effects=True, vmem_limit_bytes=VMEM_LIMIT
        ),
        name="front",
    )(
        tokens,
        cotangent,
        gain_one,
        gain_two,
        w_query,
        w_key,
        w_value,
        w_out,
        w_gate,
        w_up,
        w_down,
        cosine,
        sine,
    )


class Reduce:
    def __init__(self, place, part, first, second, sems):
        self.p, self.part, self.first, self.second, self.sems = place, part, first, second, sems
        self.half = part.shape[0] // 2

    def rows(self, half):
        return pl.ds(half * self.half, self.half)

    def sent(self, half, to):
        if half == 0:
            return self.part.at[self.rows(0), :, to]
        return self.part.at[self.rows(1), to]

    def own(self, half):
        return self.sent(half, self.p.b if half == 0 else self.p.a)

    def start(self):
        for half in range(2):
            for k in range(1, self.p.counts[half][0]):
                to, replica = self.p.peer(half, 0, k)
                remote(
                    self.sent(half, to),
                    self.first[half].at[k - 1],
                    self.sems.at[half, 0],
                    self.sems.at[half, 1],
                    replica=replica,
                ).start()

    def exchange(self):
        for half in range(2):
            own, arrived = self.own(half), self.first[half]
            await_bytes(arrived, self.sems.at[half, 1])

            def add(n, _, own=own, arrived=arrived):
                for m in range(own.shape[1]):
                    total = own[n, m].astype(jnp.float32)
                    for k in range(arrived.shape[0]):
                        total += arrived[k, n, m].astype(jnp.float32)
                    own[n, m] = total.astype(own.dtype)
                return 0

            lax.fori_loop(0, self.half, add, 0)
            for k in range(1, self.p.counts[half][1]):
                to, replica = self.p.peer(half, 1, k)
                remote(
                    own.at[:, to],
                    self.second[half].at[k - 1],
                    self.sems.at[half, 2],
                    self.sems.at[half, 3],
                    replica=replica,
                ).start()

    def total(self):
        for half in range(2):
            own, arrived = self.held(half), self.second[half]
            await_bytes(arrived, self.sems.at[half, 3])

            def add(n, _, own=own, arrived=arrived):
                total = own[n].astype(jnp.float32)
                for k in range(arrived.shape[0]):
                    total += arrived[k, n].astype(jnp.float32)
                own[n] = total.astype(own.dtype)
                return 0

            lax.fori_loop(0, self.half, add, 0)

    def held(self, half):
        return self.part.at[self.rows(half), self.p.a, self.p.b]

    def piece(self, n):
        return self.part.at[n, self.p.a, self.p.b]

    def drain(self):
        for half in range(2):
            await_bytes(self.first[half], self.sems.at[half, 0])
            await_bytes(self.second[half], self.sems.at[half, 2])


def reduce_scratch(n, high, wide, rows, columns):
    low = functools.partial(pltpu.VMEM, dtype=jnp.bfloat16)
    half = n // 2
    return [
        low((n, high, wide, rows, columns)),
        low((wide - 1, half, high, rows, columns)),
        low((high - 1, half, wide, rows, columns)),
        low((high - 1, half, rows, columns)),
        low((wide - 1, half, rows, columns)),
        pltpu.SemaphoreType.DMA((2, 4)),
    ]


def reducer(place, refs):
    part, first_a, first_b, second_a, second_b, sems = refs
    return Reduce(place, part, (first_a, first_b), (second_a, second_b), sems)


class Spread:
    def __init__(self, place, piece, out, sems, turned, split=False):
        self.p, self.piece, self.out, self.sems = place, piece, out, sems
        self.turned, self.split = turned, split

    def start(self):
        p = self.p
        if self.turned:
            count = self.out.shape[0]
            width = self.out.shape[-1] // p.fsdp
            columns = pl.ds(pl.multiple_of(p.me * width, width), width)

            def pairs(to):
                ref = self.piece(to)
                return [
                    (ref.at[:, pl.ds(i * width, width)], self.out.at[i, p.a, p.b, :, columns])
                    for i in range(count)
                ]

            def send(k, _):
                to = lax.rem(p.me + k, p.fsdp)
                for ref, target in pairs(to):
                    remote(ref, target, self.sems.at[0, 0], self.sems.at[0, 1], fsdp=to).start()
                return 0

            lax.fori_loop(1, p.fsdp, send, 0)
            for ref, target in pairs(p.me):
                pltpu.make_async_copy(ref, target, self.sems.at[0, 1]).start()
        else:
            for half in range(2):
                pltpu.make_async_copy(
                    self.source(half), self.placed(half, (p.a, p.b)), self.sems.at[half, 1]
                ).start()

    def columns(self, half):
        width = self.out.shape[-1] // 2
        return pl.ds(half * width, width)

    def placed(self, half, rows):
        a, b = rows
        if self.split:
            return self.out.at[half, a, b]
        return self.out.at[:, a, b, :, self.columns(half)]

    def source(self, half):
        if self.turned:
            return self.placed(half, (self.p.a, self.p.b))
        if self.split:
            return self.piece(half)
        return self.piece(0).at[:, :, self.columns(half)]

    def spread(self):
        p = self.p
        if self.turned:
            await_bytes(self.out.at[:, p.a, p.b], self.sems.at[0, 1])
        for half in range(2):
            ref = self.placed(half, (p.a, p.b))
            for k in range(1, p.counts[half][1]):
                _, replica = p.peer(half, 1, k)
                remote(
                    self.source(half), ref, self.sems.at[half, 2], self.sems.at[half, 3], replica=replica
                ).start()

    def spread_bytes(self, half):
        some = pl.ds(0, self.p.counts[half][1] - 1)
        return self.placed(half, (some, 0) if half == 0 else (0, some))

    def widen(self):
        p = self.p
        for half in range(2):
            if not self.turned:
                await_bytes(self.placed(half, (p.a, p.b)), self.sems.at[half, 1])
            await_bytes(self.spread_bytes(half), self.sems.at[half, 3])
            every = pl.ds(0, p.counts[half][1])
            ref = self.placed(half, (every, p.b) if half == 0 else (p.a, every))
            for k in range(1, p.counts[half][0]):
                _, replica = p.peer(half, 0, k)
                remote(ref, ref, self.sems.at[half, 4], self.sems.at[half, 5], replica=replica).start()

    def widen_bytes(self, half):
        counts = self.p.counts[half]
        every, some = pl.ds(0, counts[1]), pl.ds(0, counts[0] - 1)
        return self.placed(half, (every, some) if half == 0 else (some, every))

    def finish(self):
        p = self.p
        for half in range(2):
            await_bytes(self.widen_bytes(half), self.sems.at[half, 5])
            await_bytes(self.spread_bytes(half), self.sems.at[half, 2])
            await_bytes(self.widen_bytes(half), self.sems.at[half, 4])
        if self.turned:
            width = self.out.shape[-1] // p.fsdp
            await_bytes(
                self.out.at[:, p.a, p.b, :, pl.ds(0, (p.fsdp - 1) * width)], self.sems.at[0, 0]
            )


def spread_sems():
    return [pltpu.SemaphoreType.DMA((2, 6))]


def norm_back(values, gain_row, gains, grad, carried, result, gain_terms):
    block, model = values.shape
    share = gains.shape[2]
    held = values[...].astype(jnp.float32)
    factor = lax.rsqrt(jnp.mean(held * held, axis=-1, keepdims=True) + eps_norm)
    dots = jnp.zeros((block, 1), jnp.float32)
    for j in range(model // share):
        at = pl.ds(j * share, share)
        normed = values[:, at].astype(jnp.float32) * factor
        product = grad[:, at] * normed
        gain_terms[j, gain_row : gain_row + 1, :] = jnp.sum(product, axis=0, keepdims=True)
        dots += jnp.sum(product * gains[j, gain_row : gain_row + 1, :], axis=-1, keepdims=True)
    dots = dots / model
    for j in range(model // share):
        at = pl.ds(j * share, share)
        normed = values[:, at].astype(jnp.float32) * factor
        scaled = grad[:, at] * gains[j, gain_row : gain_row + 1, :]
        result[:, at] = carried[:, at].astype(jnp.float32) + factor * (scaled - normed * dots)


def weigh_kernel(
    cotangent,
    after_attn,
    gains,
    terms_in,
    lowered_two,
    cotangents,
    hidden_in,
    grad_gate_in,
    grad_up_in,
    grad_after,
    gain_terms,
    branch,
    out_down,
    sum_gate,
    sum_up,
    left_held,
    tokens_held,
    hidden,
    grad_gate,
    grad_up,
    total,
    piece,
    terms,
    across,
    slots,
    summed,
    low,
    load_sems,
    chunk_sems,
    store_sems,
    down_sems,
    *rest,
):
    place = Place()
    chips, block = place.chips, cotangent.shape[0]
    model = cotangent.shape[1]
    tile = 2 * block
    scatter_at, gather_at = rest[:6], rest[6:12]
    gate, up = [reducer(place, rest[12 + 6 * i : 18 + 6 * i]) for i in range(2)]
    down = Spread(place, lambda n: piece, out_down, down_sems, False)
    chunk = tokens_held.shape[1]
    chunks = cotangents.shape[0] // chunk

    def load(t):
        at = pl.ds(t * tile, tile)
        return pltpu.make_async_copy(terms_in.at[at], terms.at[at], load_sems.at[t])

    def load_chunk(i):
        at = pl.ds(i * chunk, chunk)
        return [
            pltpu.make_async_copy(cotangents.at[at], tokens_held.at[i % 2], chunk_sems.at[i % 2, 0]),
            pltpu.make_async_copy(hidden_in.at[at], hidden.at[i % 2], chunk_sems.at[i % 2, 1]),
        ]

    loads = [
        pltpu.make_async_copy(source, target, load_sems.at[chips + i])
        for i, (source, target) in enumerate(
            ((lowered_two, left_held), (grad_gate_in, grad_gate), (grad_up_in, grad_up))
        )
    ]
    for t in range(chips):
        load(t).start()
    for copy in loads + load_chunk(0):
        copy.start()
    place.enter()
    scatter = Scatter(place, terms, across, slots, block, scatter_at)
    for t in range(chips):
        load(t).wait()
        scatter.side(t).start()
    gain_terms[...] = jnp.zeros_like(gain_terms)

    def weigh(reduce, grads):
        share = model // place.fsdp

        def rows(j, _):
            left = left_held[:, pl.ds(pl.multiple_of(j * share, share), share)]
            got = contract_first(left, grads[...]).astype(jnp.bfloat16)
            reduce.part[j] = got.reshape(reduce.part.shape[1:])
            return 0

        lax.fori_loop(0, place.fsdp, rows, 0)
        reduce.start()

    loads[0].wait()
    loads[1].wait()
    weigh(gate, grad_gate)
    for t in range(chips):
        scatter.cross(t)
    scatter.step(1)
    loads[2].wait()
    weigh(up, grad_up)
    if chips > 2:
        scatter.step(2)
    for i in range(chunks):
        if i + 1 < chunks:
            for copy in load_chunk(i + 1):
                copy.start()
        for copy in load_chunk(i):
            copy.wait()
        got = contract_first(hidden[i % 2], tokens_held[i % 2])
        if i == 0:
            total[...] = got
        else:
            total[...] += got
    piece[0] = total[...].astype(jnp.bfloat16)
    down.start()
    down.spread()
    for step in range(3, chips):
        scatter.step(step)
    scatter.finish(summed)
    norm_back(after_attn, 1, gains, summed, cotangent, grad_after, gain_terms)
    low[...] = grad_after[...].astype(jnp.bfloat16)
    here = pl.ds(pl.multiple_of(place.me * block, block), block)
    gather = Gather(place, branch, block, gather_at, low)
    gather.start()
    keep = pltpu.make_async_copy(low, branch.at[here], store_sems.at[0])
    keep.start()
    scatter.drain()
    gate.exchange()
    for step in range(1, chips):
        gather.step(step)
        if step == 1:
            up.exchange()
            down.widen()
    keep.wait()
    gather.finish()
    stores = []
    for i, (reduce, out) in enumerate(((gate, sum_gate), (up, sum_up))):
        reduce.total()
        for half in range(2):
            store = pltpu.make_async_copy(
                reduce.held(half), out.at[reduce.rows(half)], store_sems.at[1 + 2 * i + half]
            )
            store.start()
            stores.append(store)
    for reduce in (gate, up):
        reduce.drain()
    down.finish()
    for store in stores:
        store.wait()


def weigh(cotangent, after_attn, gains, terms, lowered_two, cotangents, hidden, grad_gate, grad_up):
    fsdp, replicas = lax.axis_size("fsdp"), lax.axis_size("replica")
    chips, high, wide = fsdp // 2, 2, replicas // 2
    block, model = cotangent.shape
    rows, columns = grad_gate.shape
    share = gains.shape[2]
    part = columns // replicas
    chunk = min(rows, 1024)
    low, full = jnp.bfloat16, jnp.float32
    hbm, vmem = pl.BlockSpec(memory_space=pl.ANY), pl.BlockSpec(memory_space=pltpu.VMEM)
    shape = jax.ShapeDtypeStruct
    wide_piece = (fsdp, high, wide, share // replicas, columns)
    dma = pltpu.SemaphoreType.DMA
    return pl.pallas_call(
        weigh_kernel,
        in_specs=[vmem] * 3 + [hbm] * 6,
        out_specs=[vmem] * 2 + [hbm] * 4,
        out_shape=[
            shape((block, model), full),
            shape((fsdp, 8, share), full),
            shape((rows, model), low),
            shape((1, high, wide, part, model), low),
            shape((fsdp,) + wide_piece[3:], low),
            shape((fsdp,) + wide_piece[3:], low),
        ],
        scratch_shapes=[
            pltpu.VMEM((rows, model), low),
            pltpu.VMEM((2, chunk, model), low),
            pltpu.VMEM((2, chunk, part), low),
            pltpu.VMEM((rows, columns), low),
            pltpu.VMEM((rows, columns), low),
            pltpu.VMEM((part, model), full),
            pltpu.VMEM((1, part, model), low),
            pltpu.VMEM((rows, model), low),
            pltpu.VMEM((chips * block, model), low),
            pltpu.VMEM((chips + 1, block, model), low),
            pltpu.VMEM((block, model), full),
            pltpu.VMEM((block, model), low),
            dma((chips + 3,)),
            dma((2, 2)),
            dma((5,)),
            dma((2, 6)),
        ]
        + scatter_sems(chips)
        + line_sems(chips)
        + reduce_scratch(*wide_piece)
        + reduce_scratch(*wide_piece),
        compiler_params=pltpu.CompilerParams(
            collective_id=1, has_side_effects=True, vmem_limit_bytes=VMEM_LIMIT
        ),
        name="weigh",
    )(
        cotangent,
        after_attn,
        gains,
        terms,
        lowered_two,
        cotangents.reshape(-1, model),
        hidden.reshape(-1, part),
        grad_gate,
        grad_up,
    )


def back_kernel(
    tokens,
    gains,
    grad_after,
    gain_terms_in,
    sum_gate,
    sum_up,
    branch_in,
    lowered_one,
    slab_qkv,
    w_out,
    queries,
    keys,
    values,
    attended,
    logs,
    cosine,
    sine,
    grad_tokens,
    gain_out,
    out_gate,
    out_up,
    out_qkv,
    out_out,
    terms,
    across,
    slots,
    branch,
    summed,
    grad_low,
    grad_key,
    grad_value,
    grads,
    gain_terms,
    gain_slots,
    gain_sums,
    gain_sems,
    load_sems,
    *rest,
):
    place = Place()
    chips, block = place.chips, tokens.shape[0]
    model, width = tokens.shape[1], queries.shape[1]
    share = gains.shape[2]
    tile = 2 * block
    scatter_at, rest = rest[:6], rest[6:]
    gate = Spread(place, lambda n: sum_gate.at[n], out_gate, rest[0], True)
    up = Spread(place, lambda n: sum_up.at[n], out_up, rest[1], True)
    qkv, out = reducer(place, rest[4:10]), reducer(place, rest[10:16])
    qkv_spread = Spread(place, qkv.piece, out_qkv, rest[2], True)
    out_spread = Spread(place, out.piece, out_out, rest[3], False, split=True)
    load = pltpu.make_async_copy(branch_in, branch, load_sems.at[0])
    load.start()
    place.enter()
    gate.start()
    up.start()
    load.wait()

    def attend_rows(t, _):
        at = pl.ds(pl.multiple_of(t * tile, tile), tile)
        grad_low[at, :] = contract_last(branch[at, :], w_out[...]).astype(jnp.bfloat16)
        return 0

    lax.fori_loop(0, chips, attend_rows, 0)
    _, high, wide, thin, columns = out.part.shape
    for half in range(2):
        for at in range(0, columns, 512):
            got = contract_first(
                attended[...], branch[:, half * columns + at : half * columns + at + 512]
            ).astype(jnp.bfloat16)
            out.part[half, :, :, :, at : at + 512] = got.reshape(high, wide, thin, 512)
    out.start()
    reload = pltpu.make_async_copy(lowered_one, branch, load_sems.at[1])
    reload.start()
    gate.spread()

    scale = HEAD_DIM**-0.5
    grad_key[...] = jnp.zeros_like(grad_key)
    grad_value[...] = jnp.zeros_like(grad_value)
    pair = 2 * HEAD_DIM
    height = tile * 1024 // max(queries.shape[0], 1024)
    for first in range(0, queries.shape[0], height):
        rows, seen = pl.ds(first, height), pl.ds(0, first + height)

        def heads(h, _, first=first, rows=rows, seen=seen):
            lanes = pl.ds(pl.multiple_of(h * pair, pair), pair)
            q2, g2, log2 = queries[rows, lanes], grad_low[rows, lanes], logs[rows, lanes]
            k2, v2 = keys[seen, lanes], values[seen, lanes]
            for_queries, for_keys, for_values = [], [], []
            for at in (0, HEAD_DIM):
                head = slice(at, at + HEAD_DIM)
                q, g, k = q2[:, head], g2[:, head], k2[:, head]
                weights = jnp.exp(scores_of(q, k, first) - log2[:, at : at + 1])
                grad_weights = contract_last(g, v2[:, head])
                delta = jnp.sum(weights * grad_weights, axis=-1, keepdims=True)
                grad_scores = (weights * (grad_weights - delta)).astype(jnp.bfloat16)
                for_queries.append(dot(grad_scores, k))
                for_keys.append(contract_first(grad_scores, q))
                for_values.append(contract_first(weights.astype(jnp.bfloat16), g))
            got = jnp.concatenate(for_queries, axis=1) * scale
            got = got * cosine[rows, :] - partner(got) * sine[rows, :]
            grads[rows, lanes] = got.astype(jnp.bfloat16)
            grad_key[seen, lanes] += jnp.concatenate(for_keys, axis=1) * scale
            grad_value[seen, lanes] += jnp.concatenate(for_values, axis=1)
            return 0

        lax.fori_loop(0, width // pair, heads, 0)
        if first + height == queries.shape[0] // 2:
            up.spread()
    gate.widen()

    def turn_back(t, _):
        at = pl.ds(pl.multiple_of(t * tile, tile), tile)
        for j in range(0, width, pair):
            got = grad_key[at, j : j + pair]
            got = got * cosine[at, :] - partner(got) * sine[at, :]
            grads[at, width + j : width + j + pair] = got.astype(jnp.bfloat16)
        grads[at, 2 * width :] = grad_value[at, :].astype(jnp.bfloat16)
        got = contract_last(grads[at, :width], slab_qkv[:model, :])
        got += contract_last(grads[at, width : 2 * width], slab_qkv[model : 2 * model, :])
        got += contract_last(grads[at, 2 * width :], slab_qkv[2 * model :, :])
        terms[at, :] = got.astype(jnp.bfloat16)
        return 0

    lax.fori_loop(0, chips, turn_back, 0)
    scatter = Scatter(place, terms, across, slots, block, scatter_at)
    for t in range(chips):
        scatter.side(t).start()
    reload.wait()

    def weigh_rows(j, _):
        left = branch[:, pl.ds(pl.multiple_of(j * share, share), share)]
        got = contract_first(left, grads[...]).astype(jnp.bfloat16)
        qkv.part[j] = got.reshape(qkv.part.shape[1:])
        return 0

    lax.fori_loop(0, place.fsdp, weigh_rows, 0)
    qkv.start()
    out.exchange()
    for t in range(chips):
        scatter.cross(t)
    for step in range(1, chips):
        scatter.step(step)
        if step == max(chips - 2, 1):
            qkv.exchange()
            up.widen()
    out.total()
    out_spread.start()
    out_spread.spread()
    scatter.finish(summed)
    gain_terms[...] = gain_terms_in[...]
    norm_back(tokens, 0, gains, summed, grad_after, grad_tokens, gain_terms)

    def send_gain(k, _):
        to = lax.rem(place.me + k, place.fsdp)
        remote(
            gain_terms.at[to], gain_slots.at[place.me], gain_sems.at[0], gain_sems.at[1], fsdp=to
        ).start()
        return 0

    lax.fori_loop(1, place.fsdp, send_gain, 0)
    gain_slots[place.me] = gain_terms[place.me]
    qkv.total()
    qkv_spread.start()
    await_bytes(gain_slots.at[pl.ds(0, place.fsdp - 1)], gain_sems.at[1])
    gain_sums[place.replica] = jnp.sum(gain_slots[...], axis=0)

    def send_sum(k, _):
        ref = gain_sums.at[place.replica]
        to = lax.rem(place.replica + k, place.replicas)
        remote(ref, ref, gain_sems.at[2], gain_sems.at[3], replica=to).start()
        return 0

    lax.fori_loop(1, place.replicas, send_sum, 0)
    qkv_spread.spread()
    out_spread.widen()
    qkv_spread.widen()
    await_bytes(gain_sums.at[pl.ds(0, place.replicas - 1)], gain_sems.at[3])
    gain_out[...] = jnp.sum(gain_sums[...], axis=0)
    await_bytes(gain_slots.at[pl.ds(0, place.fsdp - 1)], gain_sems.at[0])
    await_bytes(gain_sums.at[pl.ds(0, place.replicas - 1)], gain_sems.at[2])
    scatter.drain()
    qkv.drain()
    out.drain()
    for spread in (gate, up, out_spread, qkv_spread):
        spread.finish()


def back(
    tokens,
    gains,
    grad_after,
    gain_terms,
    sum_gate,
    sum_up,
    branch,
    lowered_one,
    slab_qkv,
    w_out,
    queries,
    keys,
    values,
    attended,
    logs,
    cosine,
    sine,
):
    fsdp, replicas = lax.axis_size("fsdp"), lax.axis_size("replica")
    chips, high, wide = fsdp // 2, 2, replicas // 2
    block, model = tokens.shape
    rows, width = queries.shape
    share = gains.shape[2]
    low, full = jnp.bfloat16, jnp.float32
    hbm, vmem = pl.BlockSpec(memory_space=pl.ANY), pl.BlockSpec(memory_space=pltpu.VMEM)
    shape = jax.ShapeDtypeStruct
    thin = share // replicas
    columns = sum_gate.shape[-1]
    qkv_piece = (fsdp, high, wide, thin, 3 * width)
    out_piece = (2, high, wide, width // replicas, model // 2)
    dma = pltpu.SemaphoreType.DMA
    return pl.pallas_call(
        back_kernel,
        in_specs=[vmem] * 4 + [hbm] * 4 + [vmem] * 9,
        out_specs=[vmem] * 2 + [hbm] * 4,
        out_shape=[
            shape((block, model), full),
            shape((8, share), full),
            shape((1, high, wide, thin, fsdp * columns), low),
            shape((1, high, wide, thin, fsdp * columns), low),
            shape((3, high, wide, thin, fsdp * width), low),
            shape(out_piece, low),
        ],
        scratch_shapes=[
            pltpu.VMEM((rows, model), low),
            pltpu.VMEM((chips * block, model), low),
            pltpu.VMEM((chips + 1, block, model), low),
            pltpu.VMEM((rows, model), low),
            pltpu.VMEM((block, model), full),
            pltpu.VMEM((rows, width), low),
            pltpu.VMEM((rows, width), full),
            pltpu.VMEM((rows, width), full),
            pltpu.VMEM((rows, 3 * width), low),
            pltpu.VMEM((fsdp, 8, share), full),
            pltpu.VMEM((fsdp, 8, share), full),
            pltpu.VMEM((replicas, 8, share), full),
            dma((4,)),
            dma((2,)),
        ]
        + scatter_sems(chips)
        + spread_sems() * 4
        + reduce_scratch(*qkv_piece)
        + reduce_scratch(*out_piece),
        compiler_params=pltpu.CompilerParams(
            collective_id=2, has_side_effects=True, vmem_limit_bytes=VMEM_LIMIT
        ),
        name="back",
    )(
        tokens,
        gains,
        grad_after,
        gain_terms,
            sum_gate,
        sum_up,
        branch,
        lowered_one,
        slab_qkv,
        w_out,
        queries,
        keys,
        values,
        attended,
        logs,
        cosine,
        sine,
    )


def widen_kernel(down, gate, up, qkv, out, w_down, w_gate, w_up, w_query, w_key, w_value, w_out):
    w_down[...] = down[...].astype(jnp.float32)
    w_gate[...] = gate[...].astype(jnp.float32)
    w_up[...] = up[...].astype(jnp.float32)
    for i, ref in enumerate((w_query, w_key, w_value)):
        ref[...] = qkv[i].astype(jnp.float32)
    half = out.shape[2]
    for i in range(2):
        w_out[:, i * half : (i + 1) * half] = out[i].astype(jnp.float32)


def widen(down, gate, up, qkv, out):
    steps = 8
    full = jnp.float32

    def rows(array):
        return pl.BlockSpec((array.shape[0] // steps, array.shape[1]), lambda i: (i, 0))

    def stacked(array):
        return pl.BlockSpec((array.shape[0], array.shape[1] // steps, array.shape[2]), lambda i: (0, i, 0))

    like = [down, gate, up, qkv[0], qkv[0], qkv[0]]
    shapes = [jax.ShapeDtypeStruct(array.shape, full) for array in like]
    shapes.append(jax.ShapeDtypeStruct((out.shape[1], 2 * out.shape[2]), full))
    return pl.pallas_call(
        widen_kernel,
        grid=(steps,),
        in_specs=[rows(down), rows(gate), rows(up), stacked(qkv), stacked(out)],
        out_specs=[rows(shape) for shape in shapes],
        out_shape=shapes,
        compiler_params=pltpu.CompilerParams(vmem_limit_bytes=VMEM_LIMIT),
        name="widen",
    )(down, gate, up, qkv, out)


def scatter(partial):
    return lax.psum_scatter(partial, "fsdp", scatter_dimension=0, tiled=True).astype(jnp.float32)


def local(
    tokens, attn_gain, w_query, w_key, w_value, w_out, ffn_gain, w_gate, w_up, w_down, cotangent
):
    cosine, sine = rope_tables(tokens.shape[0] * lax.axis_size("fsdp"))
    (
        lowered_one,
        lowered_two,
        cotangents,
        slab_qkv,
        hidden,
        grad_gate,
        grad_up,
        terms,
        sums,
        queries,
        keys,
        values,
        attended,
        logs,
        after_attn,
        gains,
    ) = front(
        tokens,
        cotangent,
        attn_gain,
        ffn_gain,
        w_query,
        w_key,
        w_value,
        w_out,
        w_gate,
        w_up,
        w_down,
        cosine,
        sine,
    )
    grad_after, gain_terms, branch, low_down, sum_gate, sum_up = weigh(
        cotangent, after_attn, gains, terms, lowered_two, cotangents, hidden, grad_gate, grad_up
    )
    sums, grad_after = lax.optimization_barrier((sums, grad_after))
    outputs = (after_attn + scatter(sums)).astype(jnp.bfloat16)
    grad_tokens, gain_grads, low_gate, low_up, low_qkv, low_out = back(
        tokens,
        gains,
        grad_after,
        gain_terms,
        sum_gate,
        sum_up,
        branch,
        lowered_one,
        slab_qkv,
        w_out,
        queries,
        keys,
        values,
        attended,
        logs,
        cosine,
        sine,
    )

    grad_w_down, grad_w_gate, grad_w_up, grad_w_query, grad_w_key, grad_w_value, grad_w_out = widen(
        low_down.reshape(w_down.shape),
        low_gate.reshape(w_gate.shape),
        low_up.reshape(w_up.shape),
        low_qkv.reshape((3,) + w_query.shape),
        low_out.reshape(2, w_out.shape[0], -1),
    )
    return (
        outputs,
        grad_tokens,
        gain_grads[0],
        grad_w_query,
        grad_w_key,
        grad_w_value,
        grad_w_out,
        gain_grads[1],
        grad_w_gate,
        grad_w_up,
        grad_w_down,
    )


def solution(mesh):
    rows = P("fsdp", None)
    tokens = P(("replica", "fsdp"), None)
    gain = P("fsdp")
    return jax.shard_map(
        local,
        mesh=mesh,
        in_specs=(tokens, gain, rows, rows, rows, rows, gain, rows, rows, rows, tokens),
        out_specs=(tokens, tokens, gain, rows, rows, rows, rows, gain, rows, rows, rows),
        check_vma=False,
    )
```

```python
import functools

import jax
import jax.numpy as jnp
import numpy as np
from jax import lax
from jax.experimental import pallas as pl
from jax.experimental.pallas import tpu as pltpu
from jax.sharding import PartitionSpec as P

HEAD_DIM = 64

eps_norm = 1e-05
rope_base = 130000.0
masked_score = -1e30


def rope_tables(row_count):
    lane = np.arange(2 * HEAD_DIM) % HEAD_DIM
    halfway = HEAD_DIM // 2
    spacing = ((lane % halfway) * np.float32(2.0) / HEAD_DIM).astype(np.float32)
    frequency = np.power(np.float32(rope_base), -spacing)
    angles = np.arange(row_count, dtype=np.float32)[:, None] * frequency[None, :]
    sign = np.where(lane < halfway, -1.0, 1.0).astype(np.float32)
    return np.cos(angles).astype(np.float32), (np.sin(angles) * sign[None, :]).astype(np.float32)


def dot(left, right):
    return jnp.dot(left, right, preferred_element_type=jnp.float32)


def contract_last(left, right):
    return lax.dot_general(
        left, right, (((1,), (1,)), ((), ())), preferred_element_type=jnp.float32
    )


def contract_first(left, right):
    return lax.dot_general(
        left, right, (((0,), (0,)), ((), ())), preferred_element_type=jnp.float32
    )


def scores_of(queries, keys, first_row):
    rows, columns = queries.shape[0], keys.shape[0]
    scores = contract_last(queries, keys) * HEAD_DIM**-0.5
    at_row = lax.broadcasted_iota(jnp.int32, (rows, columns), 0) + first_row
    at_column = lax.broadcasted_iota(jnp.int32, (rows, columns), 1)
    return jnp.where(at_column <= at_row, scores, masked_score)


MESH = pl.DeviceIdType.MESH
VMEM_LIMIT = 60 * 2**20


def remote(src, dst, send, recv, **where):
    return pltpu.make_async_remote_copy(
        src_ref=src, dst_ref=dst, send_sem=send, recv_sem=recv, device_id=where, device_id_type=MESH
    )


def await_bytes(ref, sem):
    pltpu.make_async_copy(ref, ref, sem).wait()


def rows_at(ref, index, size):
    return ref.at[pl.ds(pl.multiple_of(index * size, size), size)]


class Place:
    def __init__(self):
        self.fsdp, self.replicas = lax.axis_size("fsdp"), lax.axis_size("replica")
        self.me, self.replica = lax.axis_index("fsdp"), lax.axis_index("replica")
        self.chips = self.fsdp // 2
        self.chip, self.core = self.me // 2, self.me % 2
        self.sibling = self.me + 1 - 2 * self.core
        self.high, self.wide = 2, self.replicas // 2
        self.a, self.b = self.replica // self.wide, self.replica % self.wide
        self.counts = ((self.wide, self.high), (self.high, self.wide))
        self.above = self.chip + 1 < self.chips
        self.below = self.chip >= 1

    def peer(self, half, stage, k):
        if half == stage:
            to = lax.rem(self.b + k, self.wide)
            return to, self.a * self.wide + to
        to = lax.rem(self.a + k, self.high)
        return to, to * self.wide + self.b

    def nearest(self, k):
        found = jnp.int32(0)
        for chip in range(self.chips):
            order = sorted(range(self.chips), key=lambda other, chip=chip: (abs(other - chip), other))
            found = found + jnp.where(self.chip == chip, order[k], 0)
        return found

    def enter(self):
        barrier = pltpu.get_barrier_semaphore()

        def greet(k, _):
            to = lax.rem(self.me + k, self.fsdp)
            pl.semaphore_signal(barrier, inc=1, device_id={"fsdp": to}, device_id_type=MESH)
            return 0

        def greet_replica(k, _):
            to = lax.rem(self.replica + k, self.replicas)
            pl.semaphore_signal(barrier, inc=1, device_id={"replica": to}, device_id_type=MESH)
            return 0

        lax.fori_loop(1, self.fsdp, greet, 0)
        lax.fori_loop(1, self.replicas, greet_replica, 0)
        pl.semaphore_wait(barrier, self.fsdp - 1 + self.replicas - 1)


def line_sems(chips):
    return [pltpu.SemaphoreType.DMA((chips,))] * 6


class Gather:
    def __init__(self, place, buf, block, sems, own=None):
        self.p, self.buf, self.block, self.own = place, buf, block, own
        self.up_out, self.up_in, self.down_out, self.down_in, self.side_out, self.side_in = sems

    def held(self, chip):
        return rows_at(self.buf, 2 * chip + self.p.core, self.block)

    def up(self, step):
        ref = self.held(self.p.chip - step + 1)
        src = self.own if step == 1 and self.own is not None else ref
        return remote(src, ref, self.up_out.at[step], self.up_in.at[step], fsdp=self.p.me + 2)

    def down(self, step):
        ref = self.held(self.p.chip + step - 1)
        src = self.own if step == 1 and self.own is not None else ref
        return remote(src, ref, self.down_out.at[step], self.down_in.at[step], fsdp=self.p.me - 2)

    def side(self, chip, src=None):
        ref = self.held(chip)
        src = ref if src is None else src
        return remote(src, ref, self.side_out.at[chip], self.side_in.at[chip], fsdp=self.p.sibling)

    def start(self):
        p = self.p
        pl.when(p.above)(lambda: self.up(1).start())
        pl.when(p.below)(lambda: self.down(1).start())
        self.side(p.chip, self.own).start()

    def step(self, step):
        p = self.p
        from_below, from_above = p.chip - step, p.chip + step

        @pl.when(from_below >= 0)
        def _():
            await_bytes(self.held(from_below), self.up_in.at[step])
            if step + 1 < p.chips:
                pl.when(p.above)(lambda: self.up(step + 1).start())
            self.side(from_below).start()

        @pl.when(from_above < p.chips)
        def _():
            await_bytes(self.held(from_above), self.down_in.at[step])
            if step + 1 < p.chips:
                pl.when(p.below)(lambda: self.down(step + 1).start())
            self.side(from_above).start()

    def across(self, chip):
        await_bytes(rows_at(self.buf, 2 * chip + 1 - self.p.core, self.block), self.side_in.at[chip])

    def drain(self):
        p = self.p
        for step in range(1, p.chips):
            pl.when(jnp.logical_and(p.above, p.chip - step + 1 >= 0))(
                lambda step=step: self.up(step).wait_send()
            )
            pl.when(jnp.logical_and(p.below, p.chip + step - 1 < p.chips))(
                lambda step=step: self.down(step).wait_send()
            )
        for chip in range(p.chips):
            self.side(chip).wait_send()

    def finish(self):
        for chip in range(self.p.chips):
            self.across(chip)
        self.drain()


class Scatter:
    def __init__(self, place, terms, across, slots, block, sems):
        self.p, self.terms, self.across, self.slots, self.block = place, terms, across, slots, block
        self.up_out, self.up_in, self.down_out, self.down_in, self.side_out, self.side_in = sems

    def side(self, chip):
        p = self.p
        return remote(
            rows_at(self.terms, 2 * chip + 1 - p.core, self.block),
            rows_at(self.across, chip, self.block),
            self.side_out.at[chip],
            self.side_in.at[chip],
            fsdp=p.sibling,
        )

    def term(self, chip):
        return rows_at(self.terms, 2 * chip + self.p.core, self.block)

    def up(self, step):
        return remote(
            self.term(self.p.chips - step + self.p.chip),
            self.slots.at[step - self.p.chip - 1],
            self.up_out.at[step],
            self.up_in.at[step],
            fsdp=self.p.me + 2,
        )

    def down(self, step):
        return remote(
            self.term(self.p.chip - self.p.chips + step),
            self.slots.at[step + 1],
            self.down_out.at[step],
            self.down_in.at[step],
            fsdp=self.p.me - 2,
        )

    def add(self, chip, arrived):
        term = self.term(chip)
        term[...] = (term[...].astype(jnp.float32) + arrived[...].astype(jnp.float32)).astype(term.dtype)

    def cross(self, chip):
        arrived = rows_at(self.across, chip, self.block)
        await_bytes(arrived, self.side_in.at[chip])
        self.add(chip, arrived)

    def step(self, step):
        p = self.p
        rising, falling = p.chips - step + p.chip, p.chip - p.chips + step

        @pl.when(jnp.logical_and(p.above, rising < p.chips))
        def _():
            if step > 1:

                @pl.when(p.below)
                def _():
                    arrived = self.slots.at[step - 1 - p.chip]
                    await_bytes(arrived, self.up_in.at[step - 1])
                    self.add(rising, arrived)

            self.up(step).start()

        @pl.when(jnp.logical_and(p.below, falling >= 0))
        def _():
            if step > 1:

                @pl.when(p.above)
                def _():
                    arrived = self.slots.at[step]
                    await_bytes(arrived, self.down_in.at[step - 1])
                    self.add(falling, arrived)

            self.down(step).start()

    def finish(self, total):
        p, last = self.p, self.p.chips - 1
        total[...] = self.term(p.chip)[...].astype(jnp.float32)

        @pl.when(p.below)
        def _():
            await_bytes(self.slots.at[last - p.chip], self.up_in.at[last])
            total[...] += self.slots[last - p.chip].astype(jnp.float32)

        @pl.when(p.above)
        def _():
            await_bytes(self.slots.at[last + 1], self.down_in.at[last])
            total[...] += self.slots[last + 1].astype(jnp.float32)

    def drain(self):
        p = self.p
        for step in range(1, p.chips):
            pl.when(jnp.logical_and(p.above, p.chips - step + p.chip < p.chips))(
                lambda step=step: self.up(step).wait_send()
            )
            pl.when(jnp.logical_and(p.below, p.chip - p.chips + step >= 0))(
                lambda step=step: self.down(step).wait_send()
            )
        for chip in range(p.chips):
            self.side(chip).wait_send()


def scatter_sems(chips):
    dma = pltpu.SemaphoreType.DMA
    return [dma((chips,))] * 6


class Turn:
    def __init__(self, place, weight, slab, first, sems):
        self.p, self.weight, self.slab, self.first = place, weight, slab, first
        self.far_out, self.far_in, self.near_out, self.near_in, self.pass_out, self.pass_in, self.own = sems
        self.height, self.width = weight.shape[0], slab.shape[1]
        self.share = self.height // place.replicas

    def far_rows(self):
        return (self.p.fsdp - 2) * self.share

    def piece(self, block, share):
        at = self.first + block * self.height + share * self.share
        return self.slab.at[pl.ds(pl.multiple_of(at, self.share), self.share)]

    def whole(self, block):
        at = self.first + block * self.height
        return self.slab.at[pl.ds(pl.multiple_of(at, self.height), self.height)]

    def columns(self, to):
        return pl.ds(pl.multiple_of(to * self.width, self.width), self.width)

    def start(self):
        p = self.p

        def send(k, _):
            to = lax.rem(2 * p.chip + 2 + k, p.fsdp)
            share = pl.ds(pl.multiple_of(p.replica * self.share, self.share), self.share)
            remote(
                self.weight.at[share, self.columns(to)],
                self.piece(p.me, p.replica),
                self.far_out,
                self.far_in,
                fsdp=to,
            ).start()
            return 0

        lax.fori_loop(0, p.fsdp - 2, send, 0)
        self.near().start()
        self.mine().start()

    def near(self):
        p = self.p
        return remote(
            self.weight.at[:, self.columns(p.sibling)], self.whole(p.me), self.near_out, self.near_in, fsdp=p.sibling
        )

    def mine(self):
        return pltpu.make_async_copy(self.weight.at[:, self.columns(self.p.me)], self.whole(self.p.me), self.own)

    def await_far(self):
        await_bytes(self.slab.at[pl.ds(0, self.far_rows())], self.far_in)

    def pass_on(self):
        p = self.p

        def one(k, _):
            ref = self.piece(lax.rem(2 * p.chip + 2 + k, p.fsdp), p.replica)

            def send(j, _):
                remote(
                    ref, ref, self.pass_out, self.pass_in, replica=lax.rem(p.replica + j, p.replicas)
                ).start()
                return 0

            return lax.fori_loop(1, p.replicas, send, 0)

        lax.fori_loop(0, p.fsdp - 2, one, 0)

    def finish(self):
        p = self.p
        passed = self.slab.at[pl.ds(0, (p.replicas - 1) * self.far_rows())]
        await_bytes(passed, self.pass_in)
        await_bytes(self.whole(p.sibling), self.near_in)
        self.mine().wait()

    def drain(self):
        p = self.p
        await_bytes(self.slab.at[pl.ds(0, self.far_rows())], self.far_out)
        self.near().wait_send()
        await_bytes(self.slab.at[pl.ds(0, (p.replicas - 1) * self.far_rows())], self.pass_out)


def turn_sems():
    return [pltpu.SemaphoreType.DMA(())] * 7


def partner(values):
    halfway = HEAD_DIM // 2
    width = values.shape[1]
    lane = lax.broadcasted_iota(jnp.int32, values.shape, 1) % HEAD_DIM
    return jnp.where(
        lane < halfway,
        pltpu.roll(values, width - halfway, axis=1),
        pltpu.roll(values, halfway, axis=1),
    )


def front_kernel(
    tokens,
    cotangent,
    gain_one,
    gain_two,
    w_query,
    w_key,
    w_value,
    w_out,
    w_gate,
    w_up,
    w_down,
    cosine,
    sine,
    lowered_one,
    lowered_two_out,
    cotangents,
    slab_qkv_out,
    hidden_out,
    grad_gate_out,
    grad_up_out,
    terms_out,
    sums_out,
    queries,
    keys,
    values,
    attended,
    logs,
    after_attn,
    gains,
    low,
    tiles,
    lowered_two,
    slab_qkv,
    slab_gate,
    slab_up,
    held_down,
    terms,
    across,
    slots,
    tile_hidden,
    tile_gate,
    tile_up,
    tile_terms,
    tile_sums,
    gain_rows,
    gain_out,
    gain_in,
    copy_sems,
    load_sems,
    store_sems,
    *sems,
):
    place = Place()
    chips, block = place.chips, tokens.shape[0]
    model, width = tokens.shape[1], queries.shape[1]
    share = gain_one.shape[0]
    tile = 2 * block
    one_at, cot_at, two_at, scatter_at = sems[:6], sems[6:12], sems[12:18], sems[18:24]
    turn_at = [sems[24 + 7 * i : 31 + 7 * i] for i in range(5)]
    turns = [
        Turn(place, weight, slab_qkv, i * model, turn_at[i])
        for i, weight in enumerate((w_query, w_key, w_value))
    ]
    turn_gate = Turn(place, w_gate, slab_gate, 0, turn_at[3])
    turn_up = Turn(place, w_up, slab_up, 0, turn_at[4])
    here = pl.ds(pl.multiple_of(place.me * block, block), block)

    gain_rows[...] = jnp.zeros_like(gain_rows)
    gain_rows[0, :] = gain_one[...].astype(jnp.float32)
    gain_rows[1, :] = gain_two[...].astype(jnp.float32)
    load_down = pltpu.make_async_copy(w_down, held_down, copy_sems.at[0])
    load_down.start()
    keep_cot = pltpu.make_async_copy(cotangent, cotangents.at[here], copy_sems.at[1])
    keep_cot.start()
    place.enter()

    def send_gains(k, _):
        to = lax.rem(place.me + k, place.fsdp)
        remote(gain_rows, gains.at[place.me], gain_out, gain_in, fsdp=to).start()
        return 0

    lax.fori_loop(1, place.fsdp, send_gains, 0)
    for turn in turns:
        turn.start()
    gains[place.me] = gain_rows[...]
    inputs = tokens[...].astype(jnp.float32)
    factor = lax.rsqrt(jnp.mean(inputs * inputs, axis=-1, keepdims=True) + eps_norm)
    await_bytes(gains.at[pl.ds(0, place.fsdp - 1)], gain_in)
    for j in range(model // share):
        at = pl.ds(j * share, share)
        normed = tokens[:, at].astype(jnp.float32) * factor
        low[:, at] = (normed * gains[j, 0:1, :]).astype(jnp.bfloat16)
    first = Gather(place, lowered_one, block, one_at, low)
    first.start()
    keep_low = pltpu.make_async_copy(low, lowered_one.at[here], copy_sems.at[2])
    keep_low.start()
    for turn in turns:
        turn.await_far()
        turn.pass_on()
    for step in range(1, chips):
        if step == chips - 1:
            turn_gate.start()
        first.step(step)
    turn_up.start()
    third = Gather(place, cotangents, block, cot_at, cotangent)
    third.start()
    keep_low.wait()
    first.finish()

    def load(source, t, slot):
        return pltpu.make_async_copy(rows_at(source, t, tile), tiles.at[slot], load_sems.at[slot])

    load(lowered_one, 0, 0).start()
    for turn in turns:
        turn.finish()
    keep_slab = pltpu.make_async_copy(slab_qkv, slab_qkv_out, copy_sems.at[3])
    keep_slab.start()
    for t in range(chips):
        if t + 1 < chips:
            load(lowered_one, t + 1, (t + 1) % 2).start()
        load(lowered_one, t, t % 2).wait()
        at = pl.ds(t * tile, tile)
        for i, ref in enumerate((queries, keys, values)):
            out = dot(tiles[t % 2], slab_qkv[i * model : (i + 1) * model, :])
            if i < 2:
                for j in range(0, width, 2 * HEAD_DIM):
                    pair = out[:, j : j + 2 * HEAD_DIM]
                    pair = pair * cosine[at, :] + partner(pair) * sine[at, :]
                    ref[at, j : j + 2 * HEAD_DIM] = pair.astype(jnp.bfloat16)
            else:
                ref[at, :] = out.astype(jnp.bfloat16)
    scatter = Scatter(place, terms, across, slots, block, scatter_at)
    pair = 2 * HEAD_DIM
    for t in range(chips):
        here_t, seen = pl.ds(t * tile, tile), pl.ds(0, (t + 1) * tile)

        def heads(h, _, t=t, here_t=here_t, seen=seen):
            lanes = pl.ds(pl.multiple_of(h * pair, pair), pair)
            q2, k2, v2 = queries[here_t, lanes], keys[seen, lanes], values[seen, lanes]
            mixed, stats = [], []
            for at in (0, HEAD_DIM):
                head = slice(at, at + HEAD_DIM)
                scores = scores_of(q2[:, head], k2[:, head], t * tile)
                most = jnp.max(scores, axis=-1, keepdims=True)
                weights = jnp.exp(scores - most)
                total = jnp.sum(weights, axis=-1, keepdims=True)
                mixed.append(dot((weights / total).astype(jnp.bfloat16), v2[:, head]))
                stats.append(jnp.broadcast_to(most + jnp.log(total), (tile, HEAD_DIM)))
            attended[here_t, lanes] = jnp.concatenate(mixed, axis=1).astype(jnp.bfloat16)
            logs[here_t, lanes] = jnp.concatenate(stats, axis=1)
            return 0

        lax.fori_loop(0, width // pair, heads, 0)
        terms[here_t, :] = dot(attended[here_t, :], w_out[...]).astype(jnp.bfloat16)
        scatter.side(t).start()
    turn_gate.await_far()
    turn_gate.pass_on()
    for t in range(chips):
        scatter.cross(t)
    for step in range(1, chips):
        scatter.step(step)
        if step == 1:
            turn_up.await_far()
            turn_up.pass_on()
        if step < chips - 1:
            third.step(step)
    scatter.finish(after_attn)
    after_attn[...] += tokens[...].astype(jnp.float32)
    after = after_attn[...]
    factor = lax.rsqrt(jnp.mean(after * after, axis=-1, keepdims=True) + eps_norm)
    for j in range(model // share):
        at = pl.ds(j * share, share)
        normed = after_attn[:, at] * factor
        lowered_two[here, at] = (normed * gains[j, 1:2, :]).astype(jnp.bfloat16)
    second = Gather(place, lowered_two, block, two_at)
    second.start()
    third.step(chips - 1)
    keep_cot.wait()
    third.finish()
    load(cotangents, place.nearest(0), 0).start()
    turn_gate.finish()
    turn_up.finish()
    load_down.wait()

    def stores(k, t):
        slot = k % 2
        pairs = (
            (tile_hidden, hidden_out),
            (tile_gate, grad_gate_out),
            (tile_up, grad_up_out),
            (tile_terms, terms_out),
            (tile_sums, sums_out),
        )
        return [
            pltpu.make_async_copy(held.at[slot], rows_at(out, t, tile), store_sems.at[i, slot])
            for i, (held, out) in enumerate(pairs)
        ]

    for k in range(chips):
        t, slot = place.nearest(k), k % 2
        if k > 0:
            second.step(k)
        second.across(t)
        if k + 1 < chips:
            load(cotangents, place.nearest(k + 1), (k + 1) % 2).start()
        load(cotangents, t, slot).wait()
        if k > 1:
            for store in stores(k - 2, place.nearest(k - 2)):
                store.wait()
        rows = lowered_two[pl.ds(pl.multiple_of(t * tile, tile), tile), :]
        gate = dot(rows, slab_gate[...])
        up = dot(rows, slab_up[...])
        grad_hidden = contract_last(tiles[slot], held_down[...])
        sigmoid = jax.nn.sigmoid(gate)
        silu = gate * sigmoid
        hidden = (silu * up).astype(jnp.bfloat16)
        grad_gate = (grad_hidden * up * sigmoid * (1.0 + gate * (1.0 - sigmoid))).astype(jnp.bfloat16)
        grad_up = (grad_hidden * silu).astype(jnp.bfloat16)
        tile_hidden[slot] = hidden
        tile_gate[slot] = grad_gate
        tile_up[slot] = grad_up
        got = contract_last(grad_gate, slab_gate[...]) + contract_last(grad_up, slab_up[...])
        tile_terms[slot] = got.astype(jnp.bfloat16)
        tile_sums[slot] = dot(hidden, held_down[...]).astype(jnp.bfloat16)
        for store in stores(k, t):
            store.start()
    keep_two = pltpu.make_async_copy(lowered_two, lowered_two_out, copy_sems.at[4])
    keep_two.start()
    second.drain()
    scatter.drain()
    for turn in turns + [turn_gate, turn_up]:
        turn.drain()
    await_bytes(gains.at[pl.ds(0, place.fsdp - 1)], gain_out)
    keep_slab.wait()
    for k in range(max(chips - 2, 0), chips):
        for store in stores(k, place.nearest(k)):
            store.wait()
    keep_two.wait()


def front(
    tokens, cotangent, gain_one, gain_two, w_query, w_key, w_value, w_out, w_gate, w_up, w_down, cosine, sine
):
    fsdp = lax.axis_size("fsdp")
    chips = fsdp // 2
    block, model = tokens.shape
    rows, width, wide = fsdp * block, w_query.shape[1] // fsdp, w_gate.shape[1] // fsdp
    tile = 2 * block
    share = gain_one.shape[0]
    low, full = jnp.bfloat16, jnp.float32
    hbm, vmem = pl.BlockSpec(memory_space=pl.ANY), pl.BlockSpec(memory_space=pltpu.VMEM)
    shape = jax.ShapeDtypeStruct
    dma = pltpu.SemaphoreType.DMA
    return pl.pallas_call(
        front_kernel,
        in_specs=[vmem] * 4 + [hbm] * 3 + [vmem] + [hbm] * 3 + [vmem] * 2,
        out_specs=[hbm] * 9 + [vmem] * 7,
        out_shape=[
            shape((rows, model), low),
            shape((rows, model), low),
            shape((rows, model), low),
            shape((3 * model, width), low),
            shape((rows, wide), low),
            shape((rows, wide), low),
            shape((rows, wide), low),
            shape((rows, model), low),
            shape((rows, model), low),
            shape((rows, width), low),
            shape((rows, width), low),
            shape((rows, width), low),
            shape((rows, width), low),
            shape((rows, width), full),
            shape((block, model), full),
            shape((fsdp, 8, share), full),
        ],
        scratch_shapes=[
            pltpu.VMEM((block, model), low),
            pltpu.VMEM((2, tile, model), low),
            pltpu.VMEM((rows, model), low),
            pltpu.VMEM((3 * model, width), low),
            pltpu.VMEM((model, wide), low),
            pltpu.VMEM((model, wide), low),
            pltpu.VMEM((wide, model), low),
            pltpu.VMEM((rows, model), low),
            pltpu.VMEM((chips * block, model), low),
            pltpu.VMEM((chips + 1, block, model), low),
            pltpu.VMEM((2, tile, wide), low),
            pltpu.VMEM((2, tile, wide), low),
            pltpu.VMEM((2, tile, wide), low),
            pltpu.VMEM((2, tile, model), low),
            pltpu.VMEM((2, tile, model), low),
            pltpu.VMEM((8, share), full),
            dma(()),
            dma(()),
            dma((5,)),
            dma((2,)),
            dma((5, 2)),
        ]
        + line_sems(chips) * 3
        + scatter_sems(chips)
        + turn_sems() * 5,
        compiler_params=pltpu.CompilerParams(
            collective_id=0, has_side_effects=True, vmem_limit_bytes=VMEM_LIMIT
        ),
        name="front",
    )(
        tokens,
        cotangent,
        gain_one,
        gain_two,
        w_query,
        w_key,
        w_value,
        w_out,
        w_gate,
        w_up,
        w_down,
        cosine,
        sine,
    )


class Reduce:
    def __init__(self, place, part, first, second, sems):
        self.p, self.part, self.first, self.second, self.sems = place, part, first, second, sems
        self.half = part.shape[0] // 2

    def rows(self, half):
        return pl.ds(half * self.half, self.half)

    def sent(self, half, to):
        if half == 0:
            return self.part.at[self.rows(0), :, to]
        return self.part.at[self.rows(1), to]

    def own(self, half):
        return self.sent(half, self.p.b if half == 0 else self.p.a)

    def start(self, half):
        for k in range(1, self.p.counts[half][0]):
            to, replica = self.p.peer(half, 0, k)
            remote(
                self.sent(half, to),
                self.first[half].at[k - 1],
                self.sems.at[half, 0],
                self.sems.at[half, 1],
                replica=replica,
            ).start()

    def exchange(self):
        for half in range(2):
            own, arrived = self.own(half), self.first[half]
            await_bytes(arrived, self.sems.at[half, 1])

            def add(n, _, own=own, arrived=arrived):
                for m in range(own.shape[1]):
                    total = own[n, m].astype(jnp.float32)
                    for k in range(arrived.shape[0]):
                        total += arrived[k, n, m].astype(jnp.float32)
                    own[n, m] = total.astype(own.dtype)
                return 0

            lax.fori_loop(0, self.half, add, 0)
            for k in range(1, self.p.counts[half][1]):
                to, replica = self.p.peer(half, 1, k)
                remote(
                    own.at[:, to],
                    self.second[half].at[k - 1],
                    self.sems.at[half, 2],
                    self.sems.at[half, 3],
                    replica=replica,
                ).start()

    def total(self):
        for half in range(2):
            own, arrived = self.held(half), self.second[half]
            await_bytes(arrived, self.sems.at[half, 3])

            def add(n, _, own=own, arrived=arrived):
                total = own[n].astype(jnp.float32)
                for k in range(arrived.shape[0]):
                    total += arrived[k, n].astype(jnp.float32)
                own[n] = total.astype(own.dtype)
                return 0

            lax.fori_loop(0, self.half, add, 0)

    def held(self, half):
        return self.part.at[self.rows(half), self.p.a, self.p.b]

    def piece(self, n):
        return self.part.at[n, self.p.a, self.p.b]

    def drain(self):
        for half in range(2):
            await_bytes(self.first[half], self.sems.at[half, 0])
            await_bytes(self.second[half], self.sems.at[half, 2])


def reduce_scratch(n, high, wide, rows, columns):
    low = functools.partial(pltpu.VMEM, dtype=jnp.bfloat16)
    half = n // 2
    return [
        low((n, high, wide, rows, columns)),
        low((wide - 1, half, high, rows, columns)),
        low((high - 1, half, wide, rows, columns)),
        low((high - 1, half, rows, columns)),
        low((wide - 1, half, rows, columns)),
        pltpu.SemaphoreType.DMA((2, 4)),
    ]


def reducer(place, refs):
    part, first_a, first_b, second_a, second_b, sems = refs
    return Reduce(place, part, (first_a, first_b), (second_a, second_b), sems)


class Spread:
    def __init__(self, place, piece, out, sems, turned):
        self.p, self.piece, self.out, self.sems, self.turned = place, piece, out, sems, turned

    def start(self):
        p = self.p
        if self.turned:
            count = self.out.shape[0]
            width = self.out.shape[-1] // p.fsdp
            columns = pl.ds(pl.multiple_of(p.me * width, width), width)

            def pairs(to):
                ref = self.piece(to)
                return [
                    (ref.at[:, pl.ds(i * width, width)], self.out.at[i, p.a, p.b, :, columns])
                    for i in range(count)
                ]

            def send(k, _):
                to = lax.rem(p.me + k, p.fsdp)
                for ref, target in pairs(to):
                    remote(ref, target, self.sems.at[0, 0], self.sems.at[0, 1], fsdp=to).start()
                return 0

            lax.fori_loop(1, p.fsdp, send, 0)
            for ref, target in pairs(p.me):
                pltpu.make_async_copy(ref, target, self.sems.at[0, 1]).start()
        else:
            for half in range(2):
                pltpu.make_async_copy(
                    self.piece(half), self.out.at[half, p.a, p.b], self.sems.at[half, 1]
                ).start()

    def placed(self, half, rows):
        a, b = rows
        if self.turned:
            width = self.out.shape[-1] // 2
            return self.out.at[:, a, b, :, pl.ds(half * width, width)]
        return self.out.at[half, a, b]

    def spread(self):
        p = self.p
        if self.turned:
            await_bytes(self.out.at[:, p.a, p.b], self.sems.at[0, 1])
        for half in range(2):
            ref = self.placed(half, (p.a, p.b))
            src = ref if self.turned else self.piece(half)
            for k in range(1, p.counts[half][1]):
                _, replica = p.peer(half, 1, k)
                remote(src, ref, self.sems.at[half, 2], self.sems.at[half, 3], replica=replica).start()

    def spread_bytes(self, half):
        some = pl.ds(0, self.p.counts[half][1] - 1)
        return self.placed(half, (some, 0) if half == 0 else (0, some))

    def widen(self):
        p = self.p
        for half in range(2):
            if not self.turned:
                await_bytes(self.placed(half, (p.a, p.b)), self.sems.at[half, 1])
            await_bytes(self.spread_bytes(half), self.sems.at[half, 3])
            every = pl.ds(0, p.counts[half][1])
            ref = self.placed(half, (every, p.b) if half == 0 else (p.a, every))
            for k in range(1, p.counts[half][0]):
                _, replica = p.peer(half, 0, k)
                remote(ref, ref, self.sems.at[half, 4], self.sems.at[half, 5], replica=replica).start()

    def widen_bytes(self, half):
        counts = self.p.counts[half]
        every, some = pl.ds(0, counts[1]), pl.ds(0, counts[0] - 1)
        return self.placed(half, (every, some) if half == 0 else (some, every))

    def finish(self):
        p = self.p
        for half in range(2):
            await_bytes(self.widen_bytes(half), self.sems.at[half, 5])
            await_bytes(self.spread_bytes(half), self.sems.at[half, 2])
            await_bytes(self.widen_bytes(half), self.sems.at[half, 4])
        if self.turned:
            width = self.out.shape[-1] // p.fsdp
            await_bytes(
                self.out.at[:, p.a, p.b, :, pl.ds(0, (p.fsdp - 1) * width)], self.sems.at[0, 0]
            )


def spread_sems():
    return [pltpu.SemaphoreType.DMA((2, 6))]


def norm_back(values, gain_row, gains, grad, carried, result, gain_terms):
    block, model = values.shape
    share = gains.shape[2]
    held = values[...].astype(jnp.float32)
    factor = lax.rsqrt(jnp.mean(held * held, axis=-1, keepdims=True) + eps_norm)
    dots = jnp.zeros((block, 1), jnp.float32)
    for j in range(model // share):
        at = pl.ds(j * share, share)
        normed = values[:, at].astype(jnp.float32) * factor
        product = grad[:, at] * normed
        gain_terms[j, gain_row : gain_row + 1, :] = jnp.sum(product, axis=0, keepdims=True)
        dots += jnp.sum(product * gains[j, gain_row : gain_row + 1, :], axis=-1, keepdims=True)
    dots = dots / model
    for j in range(model // share):
        at = pl.ds(j * share, share)
        normed = values[:, at].astype(jnp.float32) * factor
        scaled = grad[:, at] * gains[j, gain_row : gain_row + 1, :]
        result[:, at] = carried[:, at].astype(jnp.float32) + factor * (scaled - normed * dots)


def weigh_kernel(
    cotangent,
    after_attn,
    gains,
    terms_in,
    lowered_two,
    cotangents,
    hidden_in,
    grad_gate_in,
    grad_up_in,
    grad_after,
    gain_terms,
    branch,
    sum_down,
    sum_gate,
    sum_up,
    tokens_held,
    hidden,
    grad_gate,
    grad_up,
    terms,
    across,
    slots,
    summed,
    low,
    load_sems,
    store_sems,
    *rest,
):
    place = Place()
    chips, block = place.chips, cotangent.shape[0]
    model = cotangent.shape[1]
    tile = 2 * block
    scatter_at, gather_at = rest[:6], rest[6:12]
    down, gate, up = [reducer(place, rest[12 + 6 * i : 18 + 6 * i]) for i in range(3)]

    def load(t):
        at = pl.ds(t * tile, tile)
        return pltpu.make_async_copy(terms_in.at[at], terms.at[at], load_sems.at[t])

    loads = [
        pltpu.make_async_copy(source, target, load_sems.at[chips + i])
        for i, (source, target) in enumerate(
            (
                (cotangents, tokens_held),
                (hidden_in, hidden),
                (grad_gate_in, grad_gate),
                (grad_up_in, grad_up),
                (lowered_two, tokens_held),
            )
        )
    ]
    for t in range(chips):
        load(t).start()
    for copy in loads[:4]:
        copy.start()
    place.enter()
    scatter = Scatter(place, terms, across, slots, block, scatter_at)
    for t in range(chips):
        load(t).wait()
        scatter.side(t).start()
    gain_terms[...] = jnp.zeros_like(gain_terms)
    loads[0].wait()
    loads[1].wait()
    _, high, wide, thin, _ = down.part.shape
    columns = min(tile, hidden.shape[1])
    for i in range(0, hidden.shape[1], columns):
        got = contract_first(hidden[:, i : i + columns], tokens_held[...]).astype(jnp.bfloat16)
        for m in range(0, columns, thin):
            n = (i + m) // thin
            down.part[n // (high * wide), n // wide % high, n % wide] = got[m : m + thin, :]
        if 2 * (i + columns) == hidden.shape[1]:
            down.start(0)
    loads[4].start()
    down.start(1)
    for t in range(chips):
        scatter.cross(t)
    scatter.step(1)
    loads[4].wait()

    def weigh(reduce, grads):
        share = model // place.fsdp

        def rows(j, _):
            left = tokens_held[:, pl.ds(pl.multiple_of(j * share, share), share)]
            got = contract_first(left, grads[...]).astype(jnp.bfloat16)
            reduce.part[j] = got.reshape(reduce.part.shape[1:])
            return 0

        for half in range(2):
            lax.fori_loop(half * chips, (half + 1) * chips, rows, 0)
            reduce.start(half)

    loads[2].wait()
    weigh(gate, grad_gate)
    if chips > 2:
        scatter.step(2)
    loads[3].wait()
    weigh(up, grad_up)
    for step in range(3, chips):
        scatter.step(step)
    scatter.finish(summed)
    norm_back(after_attn, 1, gains, summed, cotangent, grad_after, gain_terms)
    low[...] = grad_after[...].astype(jnp.bfloat16)
    here = pl.ds(pl.multiple_of(place.me * block, block), block)
    gather = Gather(place, branch, block, gather_at, low)
    gather.start()
    keep = pltpu.make_async_copy(low, branch.at[here], store_sems.at[0])
    keep.start()
    scatter.drain()
    down.exchange()
    for step in range(1, chips):
        gather.step(step)
        if step == 1:
            gate.exchange()
        if step == max(chips - 2, 1):
            up.exchange()
    keep.wait()
    gather.finish()
    stores = []
    for i, (reduce, out) in enumerate(((down, sum_down), (gate, sum_gate), (up, sum_up))):
        reduce.total()
        for half in range(2):
            store = pltpu.make_async_copy(
                reduce.held(half), out.at[reduce.rows(half)], store_sems.at[1 + 2 * i + half]
            )
            store.start()
            stores.append(store)
    for reduce in (down, gate, up):
        reduce.drain()
    for store in stores:
        store.wait()


def weigh(cotangent, after_attn, gains, terms, lowered_two, cotangents, hidden, grad_gate, grad_up):
    fsdp, replicas = lax.axis_size("fsdp"), lax.axis_size("replica")
    chips, high, wide = fsdp // 2, 2, replicas // 2
    block, model = cotangent.shape
    rows, columns = hidden.shape
    share = gains.shape[2]
    low, full = jnp.bfloat16, jnp.float32
    hbm, vmem = pl.BlockSpec(memory_space=pl.ANY), pl.BlockSpec(memory_space=pltpu.VMEM)
    shape = jax.ShapeDtypeStruct
    down_piece = (2, high, wide, columns // (2 * replicas), model)
    wide_piece = (fsdp, high, wide, share // replicas, columns)
    dma = pltpu.SemaphoreType.DMA
    return pl.pallas_call(
        weigh_kernel,
        in_specs=[vmem] * 3 + [hbm] * 6,
        out_specs=[vmem] * 2 + [hbm] * 4,
        out_shape=[
            shape((block, model), full),
            shape((fsdp, 8, share), full),
            shape((rows, model), low),
            shape((2,) + down_piece[3:], low),
            shape((fsdp,) + wide_piece[3:], low),
            shape((fsdp,) + wide_piece[3:], low),
        ],
        scratch_shapes=[
            pltpu.VMEM((rows, model), low),
            pltpu.VMEM((rows, columns), low),
            pltpu.VMEM((rows, columns), low),
            pltpu.VMEM((rows, columns), low),
            pltpu.VMEM((rows, model), low),
            pltpu.VMEM((chips * block, model), low),
            pltpu.VMEM((chips + 1, block, model), low),
            pltpu.VMEM((block, model), full),
            pltpu.VMEM((block, model), low),
            dma((chips + 5,)),
            dma((7,)),
        ]
        + scatter_sems(chips)
        + line_sems(chips)
        + reduce_scratch(*down_piece)
        + reduce_scratch(*wide_piece)
        + reduce_scratch(*wide_piece),
        compiler_params=pltpu.CompilerParams(
            collective_id=1, has_side_effects=True, vmem_limit_bytes=VMEM_LIMIT
        ),
        name="weigh",
    )(cotangent, after_attn, gains, terms, lowered_two, cotangents, hidden, grad_gate, grad_up)


def back_kernel(
    tokens,
    gains,
    grad_after,
    gain_terms_in,
    after_attn,
    sums,
    sum_down,
    sum_gate,
    sum_up,
    branch_in,
    lowered_one,
    slab_qkv,
    w_out,
    queries,
    keys,
    values,
    attended,
    logs,
    cosine,
    sine,
    outputs,
    grad_tokens,
    gain_out,
    out_down,
    out_gate,
    out_up,
    out_qkv,
    out_out,
    terms,
    across,
    slots,
    branch,
    summed,
    grad_low,
    grad_key,
    grad_value,
    grads,
    gain_terms,
    gain_slots,
    gain_sums,
    gain_sems,
    load_sems,
    *rest,
):
    place = Place()
    chips, block = place.chips, tokens.shape[0]
    model, width = tokens.shape[1], queries.shape[1]
    share = gains.shape[2]
    tile = 2 * block
    scatter_at, rest = rest[:6], rest[6:]
    down = Spread(place, lambda n: sum_down.at[n], out_down, rest[0], False)
    gate = Spread(place, lambda n: sum_gate.at[n], out_gate, rest[1], True)
    up = Spread(place, lambda n: sum_up.at[n], out_up, rest[2], True)
    qkv, out = reducer(place, rest[5:11]), reducer(place, rest[11:17])
    qkv_spread = Spread(place, qkv.piece, out_qkv, rest[3], True)
    out_spread = Spread(place, out.piece, out_out, rest[4], False)
    load = pltpu.make_async_copy(branch_in, branch, load_sems.at[0])
    load.start()
    place.enter()
    down.start()
    down.spread()
    gate.start()
    up.start()
    load.wait()

    def attend_rows(t, _):
        at = pl.ds(pl.multiple_of(t * tile, tile), tile)
        grad_low[at, :] = contract_last(branch[at, :], w_out[...]).astype(jnp.bfloat16)
        return 0

    lax.fori_loop(0, chips, attend_rows, 0)
    _, high, wide, thin, columns = out.part.shape
    for half in range(2):
        for at in range(0, columns, 512):
            got = contract_first(
                attended[...], branch[:, half * columns + at : half * columns + at + 512]
            ).astype(jnp.bfloat16)
            out.part[half, :, :, :, at : at + 512] = got.reshape(high, wide, thin, 512)
    out.start(0)
    out.start(1)
    reload = pltpu.make_async_copy(lowered_one, branch, load_sems.at[1])
    reload.start()
    down.widen()

    scale = HEAD_DIM**-0.5
    grad_key[...] = jnp.zeros_like(grad_key)
    grad_value[...] = jnp.zeros_like(grad_value)
    pair = 2 * HEAD_DIM
    height = tile * 1024 // max(queries.shape[0], 1024)
    for first in range(0, queries.shape[0], height):
        rows, seen = pl.ds(first, height), pl.ds(0, first + height)

        def heads(h, _, first=first, rows=rows, seen=seen):
            lanes = pl.ds(pl.multiple_of(h * pair, pair), pair)
            q2, g2, log2 = queries[rows, lanes], grad_low[rows, lanes], logs[rows, lanes]
            k2, v2 = keys[seen, lanes], values[seen, lanes]
            for_queries, for_keys, for_values = [], [], []
            for at in (0, HEAD_DIM):
                head = slice(at, at + HEAD_DIM)
                q, g, k = q2[:, head], g2[:, head], k2[:, head]
                weights = jnp.exp(scores_of(q, k, first) - log2[:, at : at + 1])
                grad_weights = contract_last(g, v2[:, head])
                delta = jnp.sum(weights * grad_weights, axis=-1, keepdims=True)
                grad_scores = (weights * (grad_weights - delta)).astype(jnp.bfloat16)
                for_queries.append(dot(grad_scores, k))
                for_keys.append(contract_first(grad_scores, q))
                for_values.append(contract_first(weights.astype(jnp.bfloat16), g))
            got = jnp.concatenate(for_queries, axis=1) * scale
            got = got * cosine[rows, :] - partner(got) * sine[rows, :]
            grads[rows, lanes] = got.astype(jnp.bfloat16)
            grad_key[seen, lanes] += jnp.concatenate(for_keys, axis=1) * scale
            grad_value[seen, lanes] += jnp.concatenate(for_values, axis=1)
            return 0

        lax.fori_loop(0, width // pair, heads, 0)

    def turn_back(t, _):
        at = pl.ds(pl.multiple_of(t * tile, tile), tile)
        for j in range(0, width, pair):
            got = grad_key[at, j : j + pair]
            got = got * cosine[at, :] - partner(got) * sine[at, :]
            grads[at, width + j : width + j + pair] = got.astype(jnp.bfloat16)
        grads[at, 2 * width :] = grad_value[at, :].astype(jnp.bfloat16)
        got = contract_last(grads[at, :width], slab_qkv[:model, :])
        got += contract_last(grads[at, width : 2 * width], slab_qkv[model : 2 * model, :])
        got += contract_last(grads[at, 2 * width :], slab_qkv[2 * model :, :])
        terms[at, :] = got.astype(jnp.bfloat16)
        return 0

    lax.fori_loop(0, chips, turn_back, 0)
    scatter = Scatter(place, terms, across, slots, block, scatter_at)
    for t in range(chips):
        scatter.side(t).start()
    reload.wait()

    def weigh_rows(j, _):
        left = branch[:, pl.ds(pl.multiple_of(j * share, share), share)]
        got = contract_first(left, grads[...]).astype(jnp.bfloat16)
        qkv.part[j] = got.reshape(qkv.part.shape[1:])
        return 0

    for half in range(2):
        lax.fori_loop(half * chips, (half + 1) * chips, weigh_rows, 0)
        qkv.start(half)
    gate.spread()
    for t in range(chips):
        scatter.cross(t)
    for step in range(1, chips):
        scatter.step(step)
        if step == 1:
            out.exchange()
            up.spread()
        if step == max(chips - 2, 1):
            qkv.exchange()
    gate.widen()
    out.total()
    out_spread.start()
    out_spread.spread()
    scatter.finish(summed)
    gain_terms[...] = gain_terms_in[...]
    norm_back(tokens, 0, gains, summed, grad_after, grad_tokens, gain_terms)

    def send_gain(k, _):
        to = lax.rem(place.me + k, place.fsdp)
        remote(
            gain_terms.at[to], gain_slots.at[place.me], gain_sems.at[0], gain_sems.at[1], fsdp=to
        ).start()
        return 0

    lax.fori_loop(1, place.fsdp, send_gain, 0)
    gain_slots[place.me] = gain_terms[place.me]
    scatter.drain()
    load_sums = pltpu.make_async_copy(sums, terms, load_sems.at[0])
    load_sums.start()
    qkv.total()
    qkv_spread.start()
    await_bytes(gain_slots.at[pl.ds(0, place.fsdp - 1)], gain_sems.at[1])
    gain_sums[place.replica] = jnp.sum(gain_slots[...], axis=0)

    def send_sum(k, _):
        ref = gain_sums.at[place.replica]
        to = lax.rem(place.replica + k, place.replicas)
        remote(ref, ref, gain_sems.at[2], gain_sems.at[3], replica=to).start()
        return 0

    lax.fori_loop(1, place.replicas, send_sum, 0)

    load_sums.wait()
    for t in range(chips):
        scatter.side(t).start()
    up.widen()
    for t in range(chips):
        scatter.cross(t)
    scatter.step(1)
    qkv_spread.spread()
    for step in range(2, chips):
        scatter.step(step)
        if step == 2:
            out_spread.widen()
    if chips == 2:
        out_spread.widen()
    scatter.finish(summed)
    outputs[...] = (summed[...] + after_attn[...]).astype(outputs.dtype)
    qkv_spread.widen()
    await_bytes(gain_sums.at[pl.ds(0, place.replicas - 1)], gain_sems.at[3])
    gain_out[...] = jnp.sum(gain_sums[...], axis=0)
    await_bytes(gain_slots.at[pl.ds(0, place.fsdp - 1)], gain_sems.at[0])
    await_bytes(gain_sums.at[pl.ds(0, place.replicas - 1)], gain_sems.at[2])
    scatter.drain()
    qkv.drain()
    out.drain()
    for spread in (down, gate, up, out_spread, qkv_spread):
        spread.finish()


def back(
    tokens,
    gains,
    grad_after,
    gain_terms,
    after_attn,
    sums,
    sum_down,
    sum_gate,
    sum_up,
    branch,
    lowered_one,
    slab_qkv,
    w_out,
    queries,
    keys,
    values,
    attended,
    logs,
    cosine,
    sine,
):
    fsdp, replicas = lax.axis_size("fsdp"), lax.axis_size("replica")
    chips, high, wide = fsdp // 2, 2, replicas // 2
    block, model = tokens.shape
    rows, width = queries.shape
    share = gains.shape[2]
    low, full = jnp.bfloat16, jnp.float32
    hbm, vmem = pl.BlockSpec(memory_space=pl.ANY), pl.BlockSpec(memory_space=pltpu.VMEM)
    shape = jax.ShapeDtypeStruct
    thin = share // replicas
    columns = sum_gate.shape[-1]
    qkv_piece = (fsdp, high, wide, thin, 3 * width)
    out_piece = (2, high, wide, width // replicas, model // 2)
    dma = pltpu.SemaphoreType.DMA
    return pl.pallas_call(
        back_kernel,
        in_specs=[vmem] * 5 + [hbm] * 6 + [vmem] * 9,
        out_specs=[vmem] * 3 + [hbm] * 5,
        out_shape=[
            shape((block, model), low),
            shape((block, model), full),
            shape((8, share), full),
            shape((2, high, wide) + sum_down.shape[1:], low),
            shape((1, high, wide, thin, fsdp * columns), low),
            shape((1, high, wide, thin, fsdp * columns), low),
            shape((3, high, wide, thin, fsdp * width), low),
            shape(out_piece, low),
        ],
        scratch_shapes=[
            pltpu.VMEM((rows, model), low),
            pltpu.VMEM((chips * block, model), low),
            pltpu.VMEM((chips + 1, block, model), low),
            pltpu.VMEM((rows, model), low),
            pltpu.VMEM((block, model), full),
            pltpu.VMEM((rows, width), low),
            pltpu.VMEM((rows, width), full),
            pltpu.VMEM((rows, width), full),
            pltpu.VMEM((rows, 3 * width), low),
            pltpu.VMEM((fsdp, 8, share), full),
            pltpu.VMEM((fsdp, 8, share), full),
            pltpu.VMEM((replicas, 8, share), full),
            dma((4,)),
            dma((2,)),
        ]
        + scatter_sems(chips)
        + spread_sems() * 5
        + reduce_scratch(*qkv_piece)
        + reduce_scratch(*out_piece),
        compiler_params=pltpu.CompilerParams(
            collective_id=2, has_side_effects=True, vmem_limit_bytes=VMEM_LIMIT
        ),
        name="back",
    )(
        tokens,
        gains,
        grad_after,
        gain_terms,
        after_attn,
        sums,
        sum_down,
        sum_gate,
        sum_up,
        branch,
        lowered_one,
        slab_qkv,
        w_out,
        queries,
        keys,
        values,
        attended,
        logs,
        cosine,
        sine,
    )


def widen_kernel(down, gate, up, qkv, out, w_down, w_gate, w_up, w_query, w_key, w_value, w_out):
    w_down[...] = down[...].astype(jnp.float32)
    w_gate[...] = gate[...].astype(jnp.float32)
    w_up[...] = up[...].astype(jnp.float32)
    for i, ref in enumerate((w_query, w_key, w_value)):
        ref[...] = qkv[i].astype(jnp.float32)
    half = out.shape[2]
    for i in range(2):
        w_out[:, i * half : (i + 1) * half] = out[i].astype(jnp.float32)


def widen(down, gate, up, qkv, out):
    steps = 8
    full = jnp.float32

    def rows(array):
        return pl.BlockSpec((array.shape[0] // steps, array.shape[1]), lambda i: (i, 0))

    def stacked(array):
        return pl.BlockSpec((array.shape[0], array.shape[1] // steps, array.shape[2]), lambda i: (0, i, 0))

    like = [down, gate, up, qkv[0], qkv[0], qkv[0]]
    shapes = [jax.ShapeDtypeStruct(array.shape, full) for array in like]
    shapes.append(jax.ShapeDtypeStruct((out.shape[1], 2 * out.shape[2]), full))
    return pl.pallas_call(
        widen_kernel,
        grid=(steps,),
        in_specs=[rows(down), rows(gate), rows(up), stacked(qkv), stacked(out)],
        out_specs=[rows(shape) for shape in shapes],
        out_shape=shapes,
        compiler_params=pltpu.CompilerParams(vmem_limit_bytes=VMEM_LIMIT),
        name="widen",
    )(down, gate, up, qkv, out)


def local(
    tokens, attn_gain, w_query, w_key, w_value, w_out, ffn_gain, w_gate, w_up, w_down, cotangent
):
    cosine, sine = rope_tables(tokens.shape[0] * lax.axis_size("fsdp"))
    (
        lowered_one,
        lowered_two,
        cotangents,
        slab_qkv,
        hidden,
        grad_gate,
        grad_up,
        terms,
        sums,
        queries,
        keys,
        values,
        attended,
        logs,
        after_attn,
        gains,
    ) = front(
        tokens,
        cotangent,
        attn_gain,
        ffn_gain,
        w_query,
        w_key,
        w_value,
        w_out,
        w_gate,
        w_up,
        w_down,
        cosine,
        sine,
    )
    grad_after, gain_terms, branch, sum_down, sum_gate, sum_up = weigh(
        cotangent, after_attn, gains, terms, lowered_two, cotangents, hidden, grad_gate, grad_up
    )
    outputs, grad_tokens, gain_grads, low_down, low_gate, low_up, low_qkv, low_out = back(
        tokens,
        gains,
        grad_after,
        gain_terms,
        after_attn,
        sums,
        sum_down,
        sum_gate,
        sum_up,
        branch,
        lowered_one,
        slab_qkv,
        w_out,
        queries,
        keys,
        values,
        attended,
        logs,
        cosine,
        sine,
    )
    grad_w_down, grad_w_gate, grad_w_up, grad_w_query, grad_w_key, grad_w_value, grad_w_out = widen(
        low_down.reshape(w_down.shape),
        low_gate.reshape(w_gate.shape),
        low_up.reshape(w_up.shape),
        low_qkv.reshape((3,) + w_query.shape),
        low_out.reshape(2, w_out.shape[0], -1),
    )
    return (
        outputs,
        grad_tokens,
        gain_grads[0],
        grad_w_query,
        grad_w_key,
        grad_w_value,
        grad_w_out,
        gain_grads[1],
        grad_w_gate,
        grad_w_up,
        grad_w_down,
    )


def solution(mesh):
    rows = P("fsdp", None)
    tokens = P(("replica", "fsdp"), None)
    gain = P("fsdp")
    return jax.shard_map(
        local,
        mesh=mesh,
        in_specs=(tokens, gain, rows, rows, rows, rows, gain, rows, rows, rows, tokens),
        out_specs=(tokens, tokens, gain, rows, rows, rows, rows, gain, rows, rows, rows),
        check_vma=False,
    )
```

```python
import functools

import jax
import jax.numpy as jnp
import numpy as np
from jax import lax
from jax.experimental import pallas as pl
from jax.experimental.pallas import tpu as pltpu
from jax.sharding import PartitionSpec as P

HEAD_DIM = 64

eps_norm = 1e-05
rope_base = 130000.0
masked_score = -1e30


def rope_tables(row_count):
    lane = np.arange(2 * HEAD_DIM) % HEAD_DIM
    halfway = HEAD_DIM // 2
    spacing = ((lane % halfway) * np.float32(2.0) / HEAD_DIM).astype(np.float32)
    frequency = np.power(np.float32(rope_base), -spacing)
    angles = np.arange(row_count, dtype=np.float32)[:, None] * frequency[None, :]
    sign = np.where(lane < halfway, -1.0, 1.0).astype(np.float32)
    return np.cos(angles).astype(np.float32), (np.sin(angles) * sign[None, :]).astype(np.float32)


def dot(left, right):
    return jnp.dot(left, right, preferred_element_type=jnp.float32)


def contract_last(left, right):
    return lax.dot_general(
        left, right, (((1,), (1,)), ((), ())), preferred_element_type=jnp.float32
    )


def contract_first(left, right):
    return lax.dot_general(
        left, right, (((0,), (0,)), ((), ())), preferred_element_type=jnp.float32
    )


def scores_of(queries, keys, first_row):
    rows, columns = queries.shape[0], keys.shape[0]
    scores = contract_last(queries, keys) * HEAD_DIM**-0.5
    at_row = lax.broadcasted_iota(jnp.int32, (rows, columns), 0) + first_row
    at_column = lax.broadcasted_iota(jnp.int32, (rows, columns), 1)
    return jnp.where(at_column <= at_row, scores, masked_score)


MESH = pl.DeviceIdType.MESH
VMEM_LIMIT = 60 * 2**20


def remote(src, dst, send, recv, **where):
    return pltpu.make_async_remote_copy(
        src_ref=src, dst_ref=dst, send_sem=send, recv_sem=recv, device_id=where, device_id_type=MESH
    )


def await_bytes(ref, sem):
    pltpu.make_async_copy(ref, ref, sem).wait()


def rows_at(ref, index, size):
    return ref.at[pl.ds(pl.multiple_of(index * size, size), size)]


class Place:
    def __init__(self):
        self.fsdp, self.replicas = lax.axis_size("fsdp"), lax.axis_size("replica")
        self.me, self.replica = lax.axis_index("fsdp"), lax.axis_index("replica")
        self.chips = self.fsdp // 2
        self.chip, self.core = self.me // 2, self.me % 2
        self.sibling = self.me + 1 - 2 * self.core
        self.high, self.wide = 2, self.replicas // 2
        self.a, self.b = self.replica // self.wide, self.replica % self.wide
        self.counts = ((self.wide, self.high), (self.high, self.wide))
        self.above = self.chip + 1 < self.chips
        self.below = self.chip >= 1

    def peer(self, half, stage, k):
        if half == stage:
            to = lax.rem(self.b + k, self.wide)
            return to, self.a * self.wide + to
        to = lax.rem(self.a + k, self.high)
        return to, to * self.wide + self.b

    def at_step(self, step, do):
        if step == 0:
            do(self.chip)
            return
        pl.when(self.chip >= step)(lambda: do(self.chip - step))
        pl.when(self.chip + step < self.chips)(lambda: do(self.chip + step))

    def nearest(self, k):
        found = jnp.int32(0)
        for chip in range(self.chips):
            order = sorted(range(self.chips), key=lambda other, chip=chip: (abs(other - chip), other))
            found = found + jnp.where(self.chip == chip, order[k], 0)
        return found

    def enter(self):
        barrier = pltpu.get_barrier_semaphore()

        def greet(k, _):
            to = lax.rem(self.me + k, self.fsdp)
            pl.semaphore_signal(barrier, inc=1, device_id={"fsdp": to}, device_id_type=MESH)
            return 0

        def greet_replica(k, _):
            to = lax.rem(self.replica + k, self.replicas)
            pl.semaphore_signal(barrier, inc=1, device_id={"replica": to}, device_id_type=MESH)
            return 0

        lax.fori_loop(1, self.fsdp, greet, 0)
        lax.fori_loop(1, self.replicas, greet_replica, 0)
        pl.semaphore_wait(barrier, self.fsdp - 1 + self.replicas - 1)


def line_sems(chips):
    return [pltpu.SemaphoreType.DMA((chips,))] * 6


class Gather:
    def __init__(self, place, buf, block, sems, own=None):
        self.p, self.buf, self.block, self.own = place, buf, block, own
        self.up_out, self.up_in, self.down_out, self.down_in, self.side_out, self.side_in = sems

    def held(self, chip):
        return rows_at(self.buf, 2 * chip + self.p.core, self.block)

    def up(self, step):
        ref = self.held(self.p.chip - step + 1)
        src = self.own if step == 1 and self.own is not None else ref
        return remote(src, ref, self.up_out.at[step], self.up_in.at[step], fsdp=self.p.me + 2)

    def down(self, step):
        ref = self.held(self.p.chip + step - 1)
        src = self.own if step == 1 and self.own is not None else ref
        return remote(src, ref, self.down_out.at[step], self.down_in.at[step], fsdp=self.p.me - 2)

    def side(self, chip, src=None):
        ref = self.held(chip)
        src = ref if src is None else src
        return remote(src, ref, self.side_out.at[chip], self.side_in.at[chip], fsdp=self.p.sibling)

    def start(self):
        p = self.p
        pl.when(p.above)(lambda: self.up(1).start())
        pl.when(p.below)(lambda: self.down(1).start())
        self.side(p.chip, self.own).start()

    def step(self, step):
        p = self.p
        from_below, from_above = p.chip - step, p.chip + step

        @pl.when(from_below >= 0)
        def _():
            await_bytes(self.held(from_below), self.up_in.at[step])
            if step + 1 < p.chips:
                pl.when(p.above)(lambda: self.up(step + 1).start())
            self.side(from_below).start()

        @pl.when(from_above < p.chips)
        def _():
            await_bytes(self.held(from_above), self.down_in.at[step])
            if step + 1 < p.chips:
                pl.when(p.below)(lambda: self.down(step + 1).start())
            self.side(from_above).start()

    def across(self, chip):
        await_bytes(rows_at(self.buf, 2 * chip + 1 - self.p.core, self.block), self.side_in.at[chip])

    def drain(self):
        p = self.p
        for step in range(1, p.chips):
            pl.when(jnp.logical_and(p.above, p.chip - step + 1 >= 0))(
                lambda step=step: self.up(step).wait_send()
            )
            pl.when(jnp.logical_and(p.below, p.chip + step - 1 < p.chips))(
                lambda step=step: self.down(step).wait_send()
            )
        for chip in range(p.chips):
            self.side(chip).wait_send()

    def finish(self):
        for chip in range(self.p.chips):
            self.across(chip)
        self.drain()


class Scatter:
    def __init__(self, place, terms, across, slots, block, sems):
        self.p, self.terms, self.across, self.slots, self.block = place, terms, across, slots, block
        self.up_out, self.up_in, self.down_out, self.down_in, self.side_out, self.side_in = sems

    def side(self, chip):
        p = self.p
        return remote(
            rows_at(self.terms, 2 * chip + 1 - p.core, self.block),
            rows_at(self.across, chip, self.block),
            self.side_out.at[chip],
            self.side_in.at[chip],
            fsdp=p.sibling,
        )

    def term(self, chip):
        return rows_at(self.terms, 2 * chip + self.p.core, self.block)

    def up(self, step):
        return remote(
            self.term(self.p.chips - step + self.p.chip),
            self.slots.at[step - self.p.chip - 1],
            self.up_out.at[step],
            self.up_in.at[step],
            fsdp=self.p.me + 2,
        )

    def down(self, step):
        return remote(
            self.term(self.p.chip - self.p.chips + step),
            self.slots.at[step + 1],
            self.down_out.at[step],
            self.down_in.at[step],
            fsdp=self.p.me - 2,
        )

    def add(self, chip, arrived):
        term = self.term(chip)
        term[...] = (term[...].astype(jnp.float32) + arrived[...].astype(jnp.float32)).astype(term.dtype)

    def cross(self, chip):
        arrived = rows_at(self.across, chip, self.block)
        await_bytes(arrived, self.side_in.at[chip])
        self.add(chip, arrived)

    def step(self, step):
        p = self.p
        rising, falling = p.chips - step + p.chip, p.chip - p.chips + step

        @pl.when(jnp.logical_and(p.above, rising < p.chips))
        def _():
            if step > 1:

                @pl.when(p.below)
                def _():
                    arrived = self.slots.at[step - 1 - p.chip]
                    await_bytes(arrived, self.up_in.at[step - 1])
                    self.add(rising, arrived)

            self.up(step).start()

        @pl.when(jnp.logical_and(p.below, falling >= 0))
        def _():
            if step > 1:

                @pl.when(p.above)
                def _():
                    arrived = self.slots.at[step]
                    await_bytes(arrived, self.down_in.at[step - 1])
                    self.add(falling, arrived)

            self.down(step).start()

    def finish(self, total):
        p, last = self.p, self.p.chips - 1
        total[...] = self.term(p.chip)[...].astype(jnp.float32)

        @pl.when(p.below)
        def _():
            await_bytes(self.slots.at[last - p.chip], self.up_in.at[last])
            total[...] += self.slots[last - p.chip].astype(jnp.float32)

        @pl.when(p.above)
        def _():
            await_bytes(self.slots.at[last + 1], self.down_in.at[last])
            total[...] += self.slots[last + 1].astype(jnp.float32)

    def drain(self):
        p = self.p
        for step in range(1, p.chips):
            pl.when(jnp.logical_and(p.above, p.chips - step + p.chip < p.chips))(
                lambda step=step: self.up(step).wait_send()
            )
            pl.when(jnp.logical_and(p.below, p.chip - p.chips + step >= 0))(
                lambda step=step: self.down(step).wait_send()
            )
        for chip in range(p.chips):
            self.side(chip).wait_send()


def scatter_sems(chips):
    dma = pltpu.SemaphoreType.DMA
    return [dma((chips,))] * 6


class Turn:
    def __init__(self, place, weight, slab, first, sems):
        self.p, self.weight, self.slab, self.first = place, weight, slab, first
        self.far_out, self.far_in, self.near_out, self.near_in, self.own, self.passing = sems
        self.height, self.width = weight.shape[0], slab.shape[1]
        self.share = self.height // place.replicas

    def far_rows(self):
        return (self.p.fsdp - 2) * self.share

    def piece(self, block, share):
        at = self.first + block * self.height + share * self.share
        return self.slab.at[pl.ds(pl.multiple_of(at, self.share), self.share)]

    def whole(self, block):
        at = self.first + block * self.height
        return self.slab.at[pl.ds(pl.multiple_of(at, self.height), self.height)]

    def columns(self, to):
        return pl.ds(pl.multiple_of(to * self.width, self.width), self.width)

    def start(self):
        p = self.p

        def send(k, _):
            to = lax.rem(2 * p.chip + 2 + k, p.fsdp)
            share = pl.ds(pl.multiple_of(p.replica * self.share, self.share), self.share)
            remote(
                self.weight.at[share, self.columns(to)],
                self.piece(p.me, p.replica),
                self.far_out,
                self.far_in,
                fsdp=to,
            ).start()
            return 0

        lax.fori_loop(0, p.fsdp - 2, send, 0)
        self.near().start()
        self.mine().start()

    def near(self):
        p = self.p
        return remote(
            self.weight.at[:, self.columns(p.sibling)], self.whole(p.me), self.near_out, self.near_in, fsdp=p.sibling
        )

    def mine(self):
        return pltpu.make_async_copy(self.weight.at[:, self.columns(self.p.me)], self.whole(self.p.me), self.own)

    def await_far(self):
        await_bytes(self.slab.at[pl.ds(0, self.far_rows())], self.far_in)

    def bytes_of(self, pieces):
        return self.slab.at[pl.ds(0, pieces * self.share)]

    def pass_bytes(self, half, stage):
        first, second = self.p.counts[half]
        return self.bytes_of((self.p.chips - 1) * (second - 1 if stage == 0 else second * (first - 1)))

    def send_pieces(self, half, stage, shares):
        p = self.p

        def one(i, _):
            block = lax.rem(2 * p.chip + 2 + 2 * i + half, p.fsdp)
            for share in shares:
                ref = self.piece(block, share)
                for k in range(1, p.counts[half][1 - stage]):
                    _, replica = p.peer(half, 1 - stage, k)
                    remote(
                        ref,
                        ref,
                        self.passing.at[half, 2 * stage],
                        self.passing.at[half, 2 * stage + 1],
                        replica=replica,
                    ).start()
            return 0

        lax.fori_loop(0, p.chips - 1, one, 0)

    def pass_on(self):
        for half in range(2):
            self.send_pieces(half, 0, [self.p.replica])

    def pass_far(self):
        p = self.p
        for half in range(2):
            await_bytes(self.pass_bytes(half, 0), self.passing.at[half, 1])
            if half == 0:
                shares = [a * p.wide + p.b for a in range(p.high)]
            else:
                shares = [p.a * p.wide + b for b in range(p.wide)]
            self.send_pieces(half, 1, shares)

    def finish(self):
        for half in range(2):
            await_bytes(self.pass_bytes(half, 1), self.passing.at[half, 3])
        await_bytes(self.whole(self.p.sibling), self.near_in)
        self.mine().wait()

    def drain(self):
        await_bytes(self.slab.at[pl.ds(0, self.far_rows())], self.far_out)
        self.near().wait_send()
        for half in range(2):
            await_bytes(self.pass_bytes(half, 0), self.passing.at[half, 0])
            await_bytes(self.pass_bytes(half, 1), self.passing.at[half, 2])


def turn_sems():
    return [pltpu.SemaphoreType.DMA(())] * 5 + [pltpu.SemaphoreType.DMA((2, 4))]


class Everywhere:
    def __init__(self, place, buf, block, sems, side_sems):
        self.p, self.buf, self.block, self.sems, self.side_sems = place, buf, block, sems, side_sems
        self.width = buf.shape[3] // 2

    def columns(self, half):
        return pl.ds(half * self.width, self.width)

    def rows(self, chip):
        at = (2 * chip + self.p.core) * self.block
        return pl.ds(pl.multiple_of(at, self.block), self.block)

    def ref(self, half, a, b, chip):
        return self.buf.at[a, b, self.rows(chip), self.columns(half)]

    def spread(self, chip, own=None):
        p = self.p
        for half in range(2):
            ref = self.ref(half, p.a, p.b, chip)
            src = ref if own is None else own.at[:, self.columns(half)]
            for k in range(1, p.counts[half][1]):
                _, replica = p.peer(half, 1, k)
                remote(
                    src, ref, self.sems.at[chip, half, 0], self.sems.at[chip, half, 1], replica=replica
                ).start()

    def spread_bytes(self, half, chip):
        some = pl.ds(0, self.p.counts[half][1] - 1)
        return self.ref(half, some, 0, chip) if half == 0 else self.ref(half, 0, some, chip)

    def widen(self, chip):
        p = self.p
        for half in range(2):
            await_bytes(self.spread_bytes(half, chip), self.sems.at[chip, half, 1])
            every = pl.ds(0, p.counts[half][1])
            ref = self.ref(half, every, p.b, chip) if half == 0 else self.ref(half, p.a, every, chip)
            for k in range(1, p.counts[half][0]):
                _, replica = p.peer(half, 0, k)
                remote(
                    ref, ref, self.sems.at[chip, half, 2], self.sems.at[chip, half, 3], replica=replica
                ).start()

    def widen_bytes(self, half, chip):
        counts = self.p.counts[half]
        every, some = pl.ds(0, counts[1]), pl.ds(0, counts[0] - 1)
        return self.ref(half, every, some, chip) if half == 0 else self.ref(half, some, every, chip)

    def share(self, chip):
        p = self.p
        for half in range(2):
            await_bytes(self.widen_bytes(half, chip), self.sems.at[chip, half, 3])
        for k in range(1, p.replicas):
            other = lax.rem(p.replica + k, p.replicas)
            ref = self.buf.at[other // p.wide, other % p.wide, self.rows(chip)]
            remote(
                ref, ref, self.side_sems.at[chip, 0], self.side_sems.at[chip, 1], fsdp=p.sibling
            ).start()

    def finish(self):
        shared = self.buf.at[0, 0, pl.ds(0, (self.p.replicas - 1) * self.block)]
        for chip in range(self.p.chips):
            await_bytes(shared, self.side_sems.at[chip, 1])
            await_bytes(shared, self.side_sems.at[chip, 0])
            for half in range(2):
                await_bytes(self.spread_bytes(half, chip), self.sems.at[chip, half, 0])
                await_bytes(self.widen_bytes(half, chip), self.sems.at[chip, half, 2])


def partner(values):
    halfway = HEAD_DIM // 2
    width = values.shape[1]
    lane = lax.broadcasted_iota(jnp.int32, values.shape, 1) % HEAD_DIM
    return jnp.where(
        lane < halfway,
        pltpu.roll(values, width - halfway, axis=1),
        pltpu.roll(values, halfway, axis=1),
    )


def front_kernel(
    tokens,
    cotangent,
    gain_one,
    gain_two,
    w_query,
    w_key,
    w_value,
    w_out,
    w_gate,
    w_up,
    w_down,
    cosine,
    sine,
    lowered_one,
    lowered_two_out,
    all_cotangents,
    slab_qkv_out,
    all_hidden,
    grad_gate_out,
    grad_up_out,
    terms_out,
    sums_out,
    queries,
    keys,
    values,
    attended,
    logs,
    after_attn,
    gains,
    low,
    tiles,
    lowered_two,
    slab_qkv,
    slab_gate,
    slab_up,
    held_down,
    terms,
    across,
    slots,
    tile_hidden,
    tile_gate,
    tile_up,
    tile_terms,
    tile_sums,
    gain_rows,
    gain_out,
    gain_in,
    copy_sems,
    load_sems,
    store_sems,
    hidden_sems,
    every_sems,
    every_side,
    *sems,
):
    place = Place()
    chips, block = place.chips, tokens.shape[0]
    model, width = tokens.shape[1], queries.shape[1]
    share = gain_one.shape[0]
    tile = 2 * block
    one_at, cot_at, two_at, scatter_at = sems[:6], sems[6:12], sems[12:18], sems[18:24]
    turn_at = [sems[24 + 6 * i : 30 + 6 * i] for i in range(5)]
    cotangents = all_cotangents.at[place.a, place.b]
    every = Everywhere(place, all_cotangents, block, every_sems, every_side)
    turns = [
        Turn(place, weight, slab_qkv, i * model, turn_at[i])
        for i, weight in enumerate((w_query, w_key, w_value))
    ]
    turn_gate = Turn(place, w_gate, slab_gate, 0, turn_at[3])
    turn_up = Turn(place, w_up, slab_up, 0, turn_at[4])
    here = pl.ds(pl.multiple_of(place.me * block, block), block)

    gain_rows[...] = jnp.zeros_like(gain_rows)
    gain_rows[0, :] = gain_one[...].astype(jnp.float32)
    gain_rows[1, :] = gain_two[...].astype(jnp.float32)
    load_down = pltpu.make_async_copy(w_down, held_down, copy_sems.at[0])
    load_down.start()
    keep_cot = pltpu.make_async_copy(cotangent, cotangents.at[here], copy_sems.at[1])
    keep_cot.start()
    place.enter()

    def send_gains(k, _):
        to = lax.rem(place.me + k, place.fsdp)
        remote(gain_rows, gains.at[place.me], gain_out, gain_in, fsdp=to).start()
        return 0

    lax.fori_loop(1, place.fsdp, send_gains, 0)
    for turn in turns:
        turn.start()
    every.spread(place.chip, cotangent)
    gains[place.me] = gain_rows[...]
    inputs = tokens[...].astype(jnp.float32)
    factor = lax.rsqrt(jnp.mean(inputs * inputs, axis=-1, keepdims=True) + eps_norm)
    await_bytes(gains.at[pl.ds(0, place.fsdp - 1)], gain_in)
    for j in range(model // share):
        at = pl.ds(j * share, share)
        normed = tokens[:, at].astype(jnp.float32) * factor
        low[:, at] = (normed * gains[j, 0:1, :]).astype(jnp.bfloat16)
    first = Gather(place, lowered_one, block, one_at, low)
    first.start()
    keep_low = pltpu.make_async_copy(low, lowered_one.at[here], copy_sems.at[2])
    keep_low.start()
    for turn in turns:
        turn.await_far()
        turn.pass_on()
    for step in range(1, chips):
        if step == chips - 1:
            turn_gate.start()
        first.step(step)
        if step == 1:
            for turn in turns:
                turn.pass_far()
            keep_cot.wait()
            every.widen(place.chip)
    turn_up.start()
    keep_low.wait()
    first.finish()

    def load(source, t, slot):
        return pltpu.make_async_copy(rows_at(source, t, tile), tiles.at[slot], load_sems.at[slot])

    load(lowered_one, 0, 0).start()
    for turn in turns:
        turn.finish()
    keep_slab = pltpu.make_async_copy(slab_qkv, slab_qkv_out, copy_sems.at[3])
    keep_slab.start()
    for t in range(chips):
        if t + 1 < chips:
            load(lowered_one, t + 1, (t + 1) % 2).start()
        load(lowered_one, t, t % 2).wait()
        at = pl.ds(t * tile, tile)
        for i, ref in enumerate((queries, keys, values)):
            out = dot(tiles[t % 2], slab_qkv[i * model : (i + 1) * model, :])
            if i < 2:
                for j in range(0, width, 2 * HEAD_DIM):
                    pair = out[:, j : j + 2 * HEAD_DIM]
                    pair = pair * cosine[at, :] + partner(pair) * sine[at, :]
                    ref[at, j : j + 2 * HEAD_DIM] = pair.astype(jnp.bfloat16)
            else:
                ref[at, :] = out.astype(jnp.bfloat16)
    scatter = Scatter(place, terms, across, slots, block, scatter_at)
    pair = 2 * HEAD_DIM
    for t in range(chips):
        here_t, seen = pl.ds(t * tile, tile), pl.ds(0, (t + 1) * tile)

        def heads(h, _, t=t, here_t=here_t, seen=seen):
            lanes = pl.ds(pl.multiple_of(h * pair, pair), pair)
            q2, k2, v2 = queries[here_t, lanes], keys[seen, lanes], values[seen, lanes]
            mixed, stats = [], []
            for at in (0, HEAD_DIM):
                head = slice(at, at + HEAD_DIM)
                scores = scores_of(q2[:, head], k2[:, head], t * tile)
                most = jnp.max(scores, axis=-1, keepdims=True)
                weights = jnp.exp(scores - most)
                total = jnp.sum(weights, axis=-1, keepdims=True)
                mixed.append(dot((weights / total).astype(jnp.bfloat16), v2[:, head]))
                stats.append(jnp.broadcast_to(most + jnp.log(total), (tile, HEAD_DIM)))
            attended[here_t, lanes] = jnp.concatenate(mixed, axis=1).astype(jnp.bfloat16)
            logs[here_t, lanes] = jnp.concatenate(stats, axis=1)
            return 0

        lax.fori_loop(0, width // pair, heads, 0)
        terms[here_t, :] = dot(attended[here_t, :], w_out[...]).astype(jnp.bfloat16)
        scatter.side(t).start()
    turn_gate.await_far()
    turn_gate.pass_on()
    for t in range(chips):
        scatter.cross(t)
    scatter.step(1)
    third = Gather(place, cotangents, block, cot_at, cotangent)
    third.start()
    turn_gate.pass_far()
    turn_up.await_far()
    turn_up.pass_on()
    every.share(place.chip)
    for step in range(2, chips):
        scatter.step(step)
        if step == 2:
            turn_up.pass_far()
        third.step(step - 1)
        place.at_step(step - 1, every.spread)
    if chips == 2:
        turn_up.pass_far()
    scatter.finish(after_attn)
    after_attn[...] += tokens[...].astype(jnp.float32)
    after = after_attn[...]
    factor = lax.rsqrt(jnp.mean(after * after, axis=-1, keepdims=True) + eps_norm)
    for j in range(model // share):
        at = pl.ds(j * share, share)
        normed = after_attn[:, at] * factor
        lowered_two[here, at] = (normed * gains[j, 1:2, :]).astype(jnp.bfloat16)
    second = Gather(place, lowered_two, block, two_at)
    second.start()
    third.step(chips - 1)
    place.at_step(chips - 1, every.spread)
    place.at_step(1, every.widen)
    third.finish()
    load(cotangents, place.nearest(0), 0).start()
    turn_gate.finish()
    turn_up.finish()
    load_down.wait()

    def stores(k, t):
        slot = k % 2
        pairs = (
            (tile_hidden.at[:, place.replica], all_hidden.at[place.replica]),
            (tile_gate, grad_gate_out),
            (tile_up, grad_up_out),
            (tile_terms, terms_out),
            (tile_sums, sums_out),
        )
        return [
            pltpu.make_async_copy(held.at[slot], rows_at(out, t, tile), store_sems.at[i, slot])
            for i, (held, out) in enumerate(pairs)
        ]

    def hidden_bytes(slot):
        return tile_hidden.at[slot, pl.ds(0, place.replicas - 1)]

    for k in range(chips):
        t, slot = place.nearest(k), k % 2
        if k > 0:
            second.step(k)
            if k + 1 < chips:
                place.at_step(k + 1, every.widen)
        second.across(t)
        if k + 1 < chips:
            load(cotangents, place.nearest(k + 1), (k + 1) % 2).start()
        load(cotangents, t, slot).wait()
        if k > 1:
            for store in stores(k - 2, place.nearest(k - 2)):
                store.wait()
            await_bytes(hidden_bytes(slot), hidden_sems.at[slot])
        rows = lowered_two[pl.ds(pl.multiple_of(t * tile, tile), tile), :]
        gate = dot(rows, slab_gate[...])
        up = dot(rows, slab_up[...])
        grad_hidden = contract_last(tiles[slot], held_down[...])
        sigmoid = jax.nn.sigmoid(gate)
        silu = gate * sigmoid
        hidden = (silu * up).astype(jnp.bfloat16)
        grad_gate = (grad_hidden * up * sigmoid * (1.0 + gate * (1.0 - sigmoid))).astype(jnp.bfloat16)
        grad_up = (grad_hidden * silu).astype(jnp.bfloat16)
        part = tile_hidden.shape[3]
        for other in range(place.replicas):
            tile_hidden[slot, other] = hidden[:, other * part : (other + 1) * part]
        tile_gate[slot] = grad_gate
        tile_up[slot] = grad_up
        got = contract_last(grad_gate, slab_gate[...]) + contract_last(grad_up, slab_up[...])
        tile_terms[slot] = got.astype(jnp.bfloat16)
        tile_sums[slot] = dot(hidden, held_down[...]).astype(jnp.bfloat16)
        for store in stores(k, t):
            store.start()
        for j in range(1, place.replicas):
            to = lax.rem(place.replica + j, place.replicas)
            remote(
                tile_hidden.at[slot, to],
                rows_at(all_hidden.at[place.replica], t, tile),
                hidden_sems.at[slot],
                hidden_sems.at[2],
                replica=to,
            ).start()
        if k > 1:
            place.at_step(k - 1, every.share)
    place.at_step(chips - 1, every.share)
    keep_two = pltpu.make_async_copy(lowered_two, lowered_two_out, copy_sems.at[4])
    keep_two.start()
    second.drain()
    scatter.drain()
    for turn in turns + [turn_gate, turn_up]:
        turn.drain()
    await_bytes(gains.at[pl.ds(0, place.fsdp - 1)], gain_out)
    keep_slab.wait()
    for k in range(max(chips - 2, 0), chips):
        for store in stores(k, place.nearest(k)):
            store.wait()
        await_bytes(hidden_bytes(k % 2), hidden_sems.at[k % 2])
    await_bytes(all_hidden.at[pl.ds(0, place.replicas - 1)], hidden_sems.at[2])
    every.finish()
    keep_two.wait()


def front(
    tokens, cotangent, gain_one, gain_two, w_query, w_key, w_value, w_out, w_gate, w_up, w_down, cosine, sine
):
    fsdp, replicas = lax.axis_size("fsdp"), lax.axis_size("replica")
    chips, high, across_b = fsdp // 2, 2, replicas // 2
    block, model = tokens.shape
    rows, width, wide = fsdp * block, w_query.shape[1] // fsdp, w_gate.shape[1] // fsdp
    tile = 2 * block
    share = gain_one.shape[0]
    low, full = jnp.bfloat16, jnp.float32
    hbm, vmem = pl.BlockSpec(memory_space=pl.ANY), pl.BlockSpec(memory_space=pltpu.VMEM)
    shape = jax.ShapeDtypeStruct
    dma = pltpu.SemaphoreType.DMA
    return pl.pallas_call(
        front_kernel,
        in_specs=[vmem] * 4 + [hbm] * 3 + [vmem] + [hbm] * 3 + [vmem] * 2,
        out_specs=[hbm] * 9 + [vmem] * 7,
        out_shape=[
            shape((rows, model), low),
            shape((rows, model), low),
            shape((high, across_b, rows, model), low),
            shape((3 * model, width), low),
            shape((replicas, rows, wide // replicas), low),
            shape((rows, wide), low),
            shape((rows, wide), low),
            shape((rows, model), low),
            shape((rows, model), low),
            shape((rows, width), low),
            shape((rows, width), low),
            shape((rows, width), low),
            shape((rows, width), low),
            shape((rows, width), full),
            shape((block, model), full),
            shape((fsdp, 8, share), full),
        ],
        scratch_shapes=[
            pltpu.VMEM((block, model), low),
            pltpu.VMEM((2, tile, model), low),
            pltpu.VMEM((rows, model), low),
            pltpu.VMEM((3 * model, width), low),
            pltpu.VMEM((model, wide), low),
            pltpu.VMEM((model, wide), low),
            pltpu.VMEM((wide, model), low),
            pltpu.VMEM((rows, model), low),
            pltpu.VMEM((chips * block, model), low),
            pltpu.VMEM((chips + 1, block, model), low),
            pltpu.VMEM((2, replicas, tile, wide // replicas), low),
            pltpu.VMEM((2, tile, wide), low),
            pltpu.VMEM((2, tile, wide), low),
            pltpu.VMEM((2, tile, model), low),
            pltpu.VMEM((2, tile, model), low),
            pltpu.VMEM((8, share), full),
            dma(()),
            dma(()),
            dma((5,)),
            dma((2,)),
            dma((5, 2)),
            dma((3,)),
            dma((chips, 2, 4)),
            dma((chips, 2)),
        ]
        + line_sems(chips) * 3
        + scatter_sems(chips)
        + turn_sems() * 5,
        compiler_params=pltpu.CompilerParams(
            collective_id=0, has_side_effects=True, vmem_limit_bytes=VMEM_LIMIT
        ),
        name="front",
    )(
        tokens,
        cotangent,
        gain_one,
        gain_two,
        w_query,
        w_key,
        w_value,
        w_out,
        w_gate,
        w_up,
        w_down,
        cosine,
        sine,
    )


class Reduce:
    def __init__(self, place, part, first, second, sems):
        self.p, self.part, self.first, self.second, self.sems = place, part, first, second, sems
        self.half = part.shape[0] // 2

    def rows(self, half):
        return pl.ds(half * self.half, self.half)

    def sent(self, half, to):
        if half == 0:
            return self.part.at[self.rows(0), :, to]
        return self.part.at[self.rows(1), to]

    def own(self, half):
        return self.sent(half, self.p.b if half == 0 else self.p.a)

    def start(self, half):
        for k in range(1, self.p.counts[half][0]):
            to, replica = self.p.peer(half, 0, k)
            remote(
                self.sent(half, to),
                self.first[half].at[k - 1],
                self.sems.at[half, 0],
                self.sems.at[half, 1],
                replica=replica,
            ).start()

    def exchange(self):
        for half in range(2):
            own, arrived = self.own(half), self.first[half]
            await_bytes(arrived, self.sems.at[half, 1])

            def add(n, _, own=own, arrived=arrived):
                for m in range(own.shape[1]):
                    total = own[n, m].astype(jnp.float32)
                    for k in range(arrived.shape[0]):
                        total += arrived[k, n, m].astype(jnp.float32)
                    own[n, m] = total.astype(own.dtype)
                return 0

            lax.fori_loop(0, self.half, add, 0)
            for k in range(1, self.p.counts[half][1]):
                to, replica = self.p.peer(half, 1, k)
                remote(
                    own.at[:, to],
                    self.second[half].at[k - 1],
                    self.sems.at[half, 2],
                    self.sems.at[half, 3],
                    replica=replica,
                ).start()

    def total(self):
        for half in range(2):
            own, arrived = self.held(half), self.second[half]
            await_bytes(arrived, self.sems.at[half, 3])

            def add(n, _, own=own, arrived=arrived):
                total = own[n].astype(jnp.float32)
                for k in range(arrived.shape[0]):
                    total += arrived[k, n].astype(jnp.float32)
                own[n] = total.astype(own.dtype)
                return 0

            lax.fori_loop(0, self.half, add, 0)

    def held(self, half):
        return self.part.at[self.rows(half), self.p.a, self.p.b]

    def piece(self, n):
        return self.part.at[n, self.p.a, self.p.b]

    def drain(self):
        for half in range(2):
            await_bytes(self.first[half], self.sems.at[half, 0])
            await_bytes(self.second[half], self.sems.at[half, 2])


def reduce_scratch(n, high, wide, rows, columns):
    low = functools.partial(pltpu.VMEM, dtype=jnp.bfloat16)
    half = n // 2
    return [
        low((n, high, wide, rows, columns)),
        low((wide - 1, half, high, rows, columns)),
        low((high - 1, half, wide, rows, columns)),
        low((high - 1, half, rows, columns)),
        low((wide - 1, half, rows, columns)),
        pltpu.SemaphoreType.DMA((2, 4)),
    ]


def reducer(place, refs):
    part, first_a, first_b, second_a, second_b, sems = refs
    return Reduce(place, part, (first_a, first_b), (second_a, second_b), sems)


class Spread:
    def __init__(self, place, piece, out, sems, turned, split=False):
        self.p, self.piece, self.out, self.sems = place, piece, out, sems
        self.turned, self.split = turned, split

    def start(self):
        p = self.p
        if self.turned:
            count = self.out.shape[0]
            width = self.out.shape[-1] // p.fsdp
            columns = pl.ds(pl.multiple_of(p.me * width, width), width)

            def pairs(to):
                ref = self.piece(to)
                return [
                    (ref.at[:, pl.ds(i * width, width)], self.out.at[i, p.a, p.b, :, columns])
                    for i in range(count)
                ]

            def send(k, _):
                to = lax.rem(p.me + k, p.fsdp)
                for ref, target in pairs(to):
                    remote(ref, target, self.sems.at[0, 0], self.sems.at[0, 1], fsdp=to).start()
                return 0

            lax.fori_loop(1, p.fsdp, send, 0)
            for ref, target in pairs(p.me):
                pltpu.make_async_copy(ref, target, self.sems.at[0, 1]).start()
        else:
            for half in range(2):
                pltpu.make_async_copy(
                    self.source(half), self.placed(half, (p.a, p.b)), self.sems.at[half, 1]
                ).start()

    def columns(self, half):
        width = self.out.shape[-1] // 2
        return pl.ds(half * width, width)

    def placed(self, half, rows):
        a, b = rows
        if self.split:
            return self.out.at[half, a, b]
        return self.out.at[:, a, b, :, self.columns(half)]

    def source(self, half):
        if self.turned:
            return self.placed(half, (self.p.a, self.p.b))
        if self.split:
            return self.piece(half)
        return self.piece(0).at[:, :, self.columns(half)]

    def spread(self):
        p = self.p
        if self.turned:
            await_bytes(self.out.at[:, p.a, p.b], self.sems.at[0, 1])
        for half in range(2):
            ref = self.placed(half, (p.a, p.b))
            for k in range(1, p.counts[half][1]):
                _, replica = p.peer(half, 1, k)
                remote(
                    self.source(half), ref, self.sems.at[half, 2], self.sems.at[half, 3], replica=replica
                ).start()

    def region(self, half):
        every = pl.ds(0, self.p.counts[half][1])
        return self.placed(half, (every, self.p.b) if half == 0 else (self.p.a, every))

    def spread_bytes(self, half):
        some = pl.ds(0, self.p.counts[half][1] - 1)
        return self.placed(half, (some, 0) if half == 0 else (0, some))

    def widen(self):
        p = self.p
        for half in range(2):
            if not self.turned:
                await_bytes(self.placed(half, (p.a, p.b)), self.sems.at[half, 1])
            await_bytes(self.spread_bytes(half), self.sems.at[half, 3])
            ref = self.region(half)
            for k in range(1, p.counts[half][0]):
                _, replica = p.peer(half, 0, k)
                remote(ref, ref, self.sems.at[half, 4], self.sems.at[half, 5], replica=replica).start()

    def widen_bytes(self, half):
        counts = self.p.counts[half]
        every, some = pl.ds(0, counts[1]), pl.ds(0, counts[0] - 1)
        return self.placed(half, (every, some) if half == 0 else (some, every))

    def finish(self):
        p = self.p
        for half in range(2):
            await_bytes(self.widen_bytes(half), self.sems.at[half, 5])
            await_bytes(self.spread_bytes(half), self.sems.at[half, 2])
            await_bytes(self.widen_bytes(half), self.sems.at[half, 4])
        if self.turned:
            width = self.out.shape[-1] // p.fsdp
            await_bytes(
                self.out.at[:, p.a, p.b, :, pl.ds(0, (p.fsdp - 1) * width)], self.sems.at[0, 0]
            )


def spread_sems():
    return [pltpu.SemaphoreType.DMA((2, 6))]


def norm_back(values, gain_row, gains, grad, carried, result, gain_terms):
    block, model = values.shape
    share = gains.shape[2]
    held = values[...].astype(jnp.float32)
    factor = lax.rsqrt(jnp.mean(held * held, axis=-1, keepdims=True) + eps_norm)
    dots = jnp.zeros((block, 1), jnp.float32)
    for j in range(model // share):
        at = pl.ds(j * share, share)
        normed = values[:, at].astype(jnp.float32) * factor
        product = grad[:, at] * normed
        gain_terms[j, gain_row : gain_row + 1, :] = jnp.sum(product, axis=0, keepdims=True)
        dots += jnp.sum(product * gains[j, gain_row : gain_row + 1, :], axis=-1, keepdims=True)
    dots = dots / model
    for j in range(model // share):
        at = pl.ds(j * share, share)
        normed = values[:, at].astype(jnp.float32) * factor
        scaled = grad[:, at] * gains[j, gain_row : gain_row + 1, :]
        result[:, at] = carried[:, at].astype(jnp.float32) + factor * (scaled - normed * dots)


def weigh_kernel(
    cotangent,
    after_attn,
    gains,
    terms_in,
    lowered_two,
    cotangents,
    hidden_in,
    grad_gate_in,
    grad_up_in,
    grad_after,
    gain_terms,
    branch,
    out_down,
    sum_gate,
    sum_up,
    left_held,
    tokens_held,
    hidden,
    grad_gate,
    grad_up,
    total,
    piece,
    terms,
    across,
    slots,
    summed,
    low,
    load_sems,
    chunk_sems,
    store_sems,
    down_sems,
    *rest,
):
    place = Place()
    chips, block = place.chips, cotangent.shape[0]
    model = cotangent.shape[1]
    tile = 2 * block
    scatter_at, gather_at = rest[:6], rest[6:12]
    gate, up = [reducer(place, rest[12 + 6 * i : 18 + 6 * i]) for i in range(2)]
    down = Spread(place, lambda n: piece, out_down, down_sems, False)
    chunk = tokens_held.shape[1]
    chunks = cotangents.shape[0] // chunk

    def load(t):
        at = pl.ds(t * tile, tile)
        return pltpu.make_async_copy(terms_in.at[at], terms.at[at], load_sems.at[t])

    def load_chunk(i):
        at = pl.ds(i * chunk, chunk)
        return [
            pltpu.make_async_copy(cotangents.at[at], tokens_held.at[i % 2], chunk_sems.at[i % 2, 0]),
            pltpu.make_async_copy(hidden_in.at[at], hidden.at[i % 2], chunk_sems.at[i % 2, 1]),
        ]

    loads = [
        pltpu.make_async_copy(source, target, load_sems.at[chips + i])
        for i, (source, target) in enumerate(
            ((lowered_two, left_held), (grad_gate_in, grad_gate), (grad_up_in, grad_up))
        )
    ]
    for t in range(chips):
        load(t).start()
    for copy in loads + load_chunk(0):
        copy.start()
    place.enter()
    scatter = Scatter(place, terms, across, slots, block, scatter_at)
    for t in range(chips):
        load(t).wait()
        scatter.side(t).start()
    gain_terms[...] = jnp.zeros_like(gain_terms)

    def weigh(reduce, grads):
        share = model // place.fsdp

        def rows(j, _):
            left = left_held[:, pl.ds(pl.multiple_of(j * share, share), share)]
            got = contract_first(left, grads[...]).astype(jnp.bfloat16)
            reduce.part[j] = got.reshape(reduce.part.shape[1:])
            return 0

        for half in range(2):
            lax.fori_loop(half * chips, (half + 1) * chips, rows, 0)
            reduce.start(half)

    loads[0].wait()
    loads[1].wait()
    weigh(gate, grad_gate)
    for t in range(chips):
        scatter.cross(t)
    scatter.step(1)
    loads[2].wait()
    weigh(up, grad_up)
    if chips > 2:
        scatter.step(2)
    for i in range(chunks):
        if i + 1 < chunks:
            for copy in load_chunk(i + 1):
                copy.start()
        for copy in load_chunk(i):
            copy.wait()
        got = contract_first(hidden[i % 2], tokens_held[i % 2])
        if i == 0:
            total[...] = got
        else:
            total[...] += got
    piece[0] = total[...].astype(jnp.bfloat16)
    down.start()
    down.spread()
    for step in range(3, chips):
        scatter.step(step)
    scatter.finish(summed)
    norm_back(after_attn, 1, gains, summed, cotangent, grad_after, gain_terms)
    low[...] = grad_after[...].astype(jnp.bfloat16)
    here = pl.ds(pl.multiple_of(place.me * block, block), block)
    gather = Gather(place, branch, block, gather_at, low)
    gather.start()
    keep = pltpu.make_async_copy(low, branch.at[here], store_sems.at[0])
    keep.start()
    scatter.drain()
    gate.exchange()
    for step in range(1, chips):
        gather.step(step)
        if step == 1:
            up.exchange()
    keep.wait()
    gather.finish()
    stores = []
    for i, (reduce, out) in enumerate(((gate, sum_gate), (up, sum_up))):
        reduce.total()
        for half in range(2):
            store = pltpu.make_async_copy(
                reduce.held(half), out.at[reduce.rows(half)], store_sems.at[1 + 2 * i + half]
            )
            store.start()
            stores.append(store)
    for reduce in (gate, up):
        reduce.drain()
    for half in range(2):
        await_bytes(down.placed(half, (place.a, place.b)), down.sems.at[half, 1])
        await_bytes(down.spread_bytes(half), down.sems.at[half, 2])
        await_bytes(down.spread_bytes(half), down.sems.at[half, 3])
    for store in stores:
        store.wait()


def weigh(cotangent, after_attn, gains, terms, lowered_two, cotangents, hidden, grad_gate, grad_up):
    fsdp, replicas = lax.axis_size("fsdp"), lax.axis_size("replica")
    chips, high, wide = fsdp // 2, 2, replicas // 2
    block, model = cotangent.shape
    rows, columns = grad_gate.shape
    share = gains.shape[2]
    part = columns // replicas
    chunk = min(rows, 1024)
    low, full = jnp.bfloat16, jnp.float32
    hbm, vmem = pl.BlockSpec(memory_space=pl.ANY), pl.BlockSpec(memory_space=pltpu.VMEM)
    shape = jax.ShapeDtypeStruct
    wide_piece = (fsdp, high, wide, share // replicas, columns)
    dma = pltpu.SemaphoreType.DMA
    return pl.pallas_call(
        weigh_kernel,
        in_specs=[vmem] * 3 + [hbm] * 6,
        out_specs=[vmem] * 2 + [hbm] * 4,
        out_shape=[
            shape((block, model), full),
            shape((fsdp, 8, share), full),
            shape((rows, model), low),
            shape((1, high, wide, part, model), low),
            shape((fsdp,) + wide_piece[3:], low),
            shape((fsdp,) + wide_piece[3:], low),
        ],
        scratch_shapes=[
            pltpu.VMEM((rows, model), low),
            pltpu.VMEM((2, chunk, model), low),
            pltpu.VMEM((2, chunk, part), low),
            pltpu.VMEM((rows, columns), low),
            pltpu.VMEM((rows, columns), low),
            pltpu.VMEM((part, model), full),
            pltpu.VMEM((1, part, model), low),
            pltpu.VMEM((rows, model), low),
            pltpu.VMEM((chips * block, model), low),
            pltpu.VMEM((chips + 1, block, model), low),
            pltpu.VMEM((block, model), full),
            pltpu.VMEM((block, model), low),
            dma((chips + 3,)),
            dma((2, 2)),
            dma((5,)),
            dma((2, 6)),
        ]
        + scatter_sems(chips)
        + line_sems(chips)
        + reduce_scratch(*wide_piece)
        + reduce_scratch(*wide_piece),
        compiler_params=pltpu.CompilerParams(
            collective_id=1, has_side_effects=True, vmem_limit_bytes=VMEM_LIMIT
        ),
        name="weigh",
    )(
        cotangent,
        after_attn,
        gains,
        terms,
        lowered_two,
        cotangents.reshape(-1, model),
        hidden.reshape(-1, part),
        grad_gate,
        grad_up,
    )


def back_kernel(
    tokens,
    gains,
    grad_after,
    gain_terms_in,
    after_attn,
    sums,
    half_down,
    sum_gate,
    sum_up,
    branch_in,
    lowered_one,
    slab_qkv,
    w_out,
    queries,
    keys,
    values,
    attended,
    logs,
    cosine,
    sine,
    outputs,
    grad_tokens,
    gain_out,
    out_down,
    out_gate,
    out_up,
    out_qkv,
    out_out,
    terms,
    across,
    slots,
    branch,
    summed,
    grad_low,
    grad_key,
    grad_value,
    grads,
    gain_terms,
    gain_slots,
    gain_sums,
    gain_sems,
    load_sems,
    *rest,
):
    place = Place()
    chips, block = place.chips, tokens.shape[0]
    model, width = tokens.shape[1], queries.shape[1]
    share = gains.shape[2]
    tile = 2 * block
    scatter_at, rest = rest[:6], rest[6:]
    down = Spread(place, None, out_down, rest[0], False)
    held_down = Spread(place, None, half_down, None, False)
    gate = Spread(place, lambda n: sum_gate.at[n], out_gate, rest[1], True)
    up = Spread(place, lambda n: sum_up.at[n], out_up, rest[2], True)
    qkv, out = reducer(place, rest[5:11]), reducer(place, rest[11:17])
    qkv_spread = Spread(place, qkv.piece, out_qkv, rest[3], True)
    out_spread = Spread(place, out.piece, out_out, rest[4], False, split=True)
    load = pltpu.make_async_copy(branch_in, branch, load_sems.at[0])
    load.start()
    place.enter()
    keeps = []
    for half in range(2):
        src, ref = held_down.region(half), down.region(half)
        for k in range(1, place.counts[half][0]):
            _, replica = place.peer(half, 0, k)
            remote(src, ref, down.sems.at[half, 4], down.sems.at[half, 5], replica=replica).start()
        keeps.append(pltpu.make_async_copy(src, ref, down.sems.at[half, 1]))
        keeps[-1].start()
    gate.start()
    up.start()
    load.wait()

    def attend_rows(t, _):
        at = pl.ds(pl.multiple_of(t * tile, tile), tile)
        grad_low[at, :] = contract_last(branch[at, :], w_out[...]).astype(jnp.bfloat16)
        return 0

    lax.fori_loop(0, chips, attend_rows, 0)
    _, high, wide, thin, columns = out.part.shape
    for half in range(2):
        for at in range(0, columns, 512):
            got = contract_first(
                attended[...], branch[:, half * columns + at : half * columns + at + 512]
            ).astype(jnp.bfloat16)
            out.part[half, :, :, :, at : at + 512] = got.reshape(high, wide, thin, 512)
    out.start(0)
    out.start(1)
    reload = pltpu.make_async_copy(lowered_one, branch, load_sems.at[1])
    reload.start()

    scale = HEAD_DIM**-0.5
    grad_key[...] = jnp.zeros_like(grad_key)
    grad_value[...] = jnp.zeros_like(grad_value)
    pair = 2 * HEAD_DIM
    height = tile * 1024 // max(queries.shape[0], 1024)
    for first in range(0, queries.shape[0], height):
        rows, seen = pl.ds(first, height), pl.ds(0, first + height)

        def heads(h, _, first=first, rows=rows, seen=seen):
            lanes = pl.ds(pl.multiple_of(h * pair, pair), pair)
            q2, g2, log2 = queries[rows, lanes], grad_low[rows, lanes], logs[rows, lanes]
            k2, v2 = keys[seen, lanes], values[seen, lanes]
            for_queries, for_keys, for_values = [], [], []
            for at in (0, HEAD_DIM):
                head = slice(at, at + HEAD_DIM)
                q, g, k = q2[:, head], g2[:, head], k2[:, head]
                weights = jnp.exp(scores_of(q, k, first) - log2[:, at : at + 1])
                grad_weights = contract_last(g, v2[:, head])
                delta = jnp.sum(weights * grad_weights, axis=-1, keepdims=True)
                grad_scores = (weights * (grad_weights - delta)).astype(jnp.bfloat16)
                for_queries.append(dot(grad_scores, k))
                for_keys.append(contract_first(grad_scores, q))
                for_values.append(contract_first(weights.astype(jnp.bfloat16), g))
            got = jnp.concatenate(for_queries, axis=1) * scale
            got = got * cosine[rows, :] - partner(got) * sine[rows, :]
            grads[rows, lanes] = got.astype(jnp.bfloat16)
            grad_key[seen, lanes] += jnp.concatenate(for_keys, axis=1) * scale
            grad_value[seen, lanes] += jnp.concatenate(for_values, axis=1)
            return 0

        lax.fori_loop(0, width // pair, heads, 0)

    def turn_back(t, _):
        at = pl.ds(pl.multiple_of(t * tile, tile), tile)
        for j in range(0, width, pair):
            got = grad_key[at, j : j + pair]
            got = got * cosine[at, :] - partner(got) * sine[at, :]
            grads[at, width + j : width + j + pair] = got.astype(jnp.bfloat16)
        grads[at, 2 * width :] = grad_value[at, :].astype(jnp.bfloat16)
        got = contract_last(grads[at, :width], slab_qkv[:model, :])
        got += contract_last(grads[at, width : 2 * width], slab_qkv[model : 2 * model, :])
        got += contract_last(grads[at, 2 * width :], slab_qkv[2 * model :, :])
        terms[at, :] = got.astype(jnp.bfloat16)
        return 0

    lax.fori_loop(0, chips, turn_back, 0)
    scatter = Scatter(place, terms, across, slots, block, scatter_at)
    for t in range(chips):
        scatter.side(t).start()
    reload.wait()

    def weigh_rows(j, _):
        left = branch[:, pl.ds(pl.multiple_of(j * share, share), share)]
        got = contract_first(left, grads[...]).astype(jnp.bfloat16)
        qkv.part[j] = got.reshape(qkv.part.shape[1:])
        return 0

    for half in range(2):
        lax.fori_loop(half * chips, (half + 1) * chips, weigh_rows, 0)
        qkv.start(half)
    gate.spread()
    for t in range(chips):
        scatter.cross(t)
    for step in range(1, chips):
        scatter.step(step)
        if step == 1:
            out.exchange()
            up.spread()
        if step == max(chips - 2, 1):
            qkv.exchange()
    gate.widen()
    out.total()
    out_spread.start()
    out_spread.spread()
    scatter.finish(summed)
    gain_terms[...] = gain_terms_in[...]
    norm_back(tokens, 0, gains, summed, grad_after, grad_tokens, gain_terms)

    def send_gain(k, _):
        to = lax.rem(place.me + k, place.fsdp)
        remote(
            gain_terms.at[to], gain_slots.at[place.me], gain_sems.at[0], gain_sems.at[1], fsdp=to
        ).start()
        return 0

    lax.fori_loop(1, place.fsdp, send_gain, 0)
    gain_slots[place.me] = gain_terms[place.me]
    scatter.drain()
    load_sums = pltpu.make_async_copy(sums, terms, load_sems.at[0])
    load_sums.start()
    qkv.total()
    qkv_spread.start()
    await_bytes(gain_slots.at[pl.ds(0, place.fsdp - 1)], gain_sems.at[1])
    gain_sums[place.replica] = jnp.sum(gain_slots[...], axis=0)

    def send_sum(k, _):
        ref = gain_sums.at[place.replica]
        to = lax.rem(place.replica + k, place.replicas)
        remote(ref, ref, gain_sems.at[2], gain_sems.at[3], replica=to).start()
        return 0

    lax.fori_loop(1, place.replicas, send_sum, 0)

    load_sums.wait()
    for t in range(chips):
        scatter.side(t).start()
    up.widen()
    for t in range(chips):
        scatter.cross(t)
    scatter.step(1)
    qkv_spread.spread()
    for step in range(2, chips):
        scatter.step(step)
        if step == 2:
            out_spread.widen()
    if chips == 2:
        out_spread.widen()
    scatter.finish(summed)
    outputs[...] = (summed[...] + after_attn[...]).astype(outputs.dtype)
    qkv_spread.widen()
    await_bytes(gain_sums.at[pl.ds(0, place.replicas - 1)], gain_sems.at[3])
    gain_out[...] = jnp.sum(gain_sums[...], axis=0)
    await_bytes(gain_slots.at[pl.ds(0, place.fsdp - 1)], gain_sems.at[0])
    await_bytes(gain_sums.at[pl.ds(0, place.replicas - 1)], gain_sems.at[2])
    scatter.drain()
    qkv.drain()
    out.drain()
    for half in range(2):
        await_bytes(down.widen_bytes(half), down.sems.at[half, 5])
        await_bytes(down.widen_bytes(half), down.sems.at[half, 4])
        keeps[half].wait()
    for spread in (gate, up, out_spread, qkv_spread):
        spread.finish()


def back(
    tokens,
    gains,
    grad_after,
    gain_terms,
    after_attn,
    sums,
    half_down,
    sum_gate,
    sum_up,
    branch,
    lowered_one,
    slab_qkv,
    w_out,
    queries,
    keys,
    values,
    attended,
    logs,
    cosine,
    sine,
):
    fsdp, replicas = lax.axis_size("fsdp"), lax.axis_size("replica")
    chips, high, wide = fsdp // 2, 2, replicas // 2
    block, model = tokens.shape
    rows, width = queries.shape
    share = gains.shape[2]
    low, full = jnp.bfloat16, jnp.float32
    hbm, vmem = pl.BlockSpec(memory_space=pl.ANY), pl.BlockSpec(memory_space=pltpu.VMEM)
    shape = jax.ShapeDtypeStruct
    thin = share // replicas
    columns = sum_gate.shape[-1]
    qkv_piece = (fsdp, high, wide, thin, 3 * width)
    out_piece = (2, high, wide, width // replicas, model // 2)
    dma = pltpu.SemaphoreType.DMA
    return pl.pallas_call(
        back_kernel,
        in_specs=[vmem] * 5 + [hbm] * 6 + [vmem] * 9,
        out_specs=[vmem] * 3 + [hbm] * 5,
        out_shape=[
            shape((block, model), low),
            shape((block, model), full),
            shape((8, share), full),
            shape(half_down.shape, low),
            shape((1, high, wide, thin, fsdp * columns), low),
            shape((1, high, wide, thin, fsdp * columns), low),
            shape((3, high, wide, thin, fsdp * width), low),
            shape(out_piece, low),
        ],
        scratch_shapes=[
            pltpu.VMEM((rows, model), low),
            pltpu.VMEM((chips * block, model), low),
            pltpu.VMEM((chips + 1, block, model), low),
            pltpu.VMEM((rows, model), low),
            pltpu.VMEM((block, model), full),
            pltpu.VMEM((rows, width), low),
            pltpu.VMEM((rows, width), full),
            pltpu.VMEM((rows, width), full),
            pltpu.VMEM((rows, 3 * width), low),
            pltpu.VMEM((fsdp, 8, share), full),
            pltpu.VMEM((fsdp, 8, share), full),
            pltpu.VMEM((replicas, 8, share), full),
            dma((4,)),
            dma((2,)),
        ]
        + scatter_sems(chips)
        + spread_sems() * 5
        + reduce_scratch(*qkv_piece)
        + reduce_scratch(*out_piece),
        compiler_params=pltpu.CompilerParams(
            collective_id=2, has_side_effects=True, vmem_limit_bytes=VMEM_LIMIT
        ),
        name="back",
    )(
        tokens,
        gains,
        grad_after,
        gain_terms,
        after_attn,
        sums,
        half_down,
        sum_gate,
        sum_up,
        branch,
        lowered_one,
        slab_qkv,
        w_out,
        queries,
        keys,
        values,
        attended,
        logs,
        cosine,
        sine,
    )


def widen_kernel(down, gate, up, qkv, out, w_down, w_gate, w_up, w_query, w_key, w_value, w_out):
    w_down[...] = down[...].astype(jnp.float32)
    w_gate[...] = gate[...].astype(jnp.float32)
    w_up[...] = up[...].astype(jnp.float32)
    for i, ref in enumerate((w_query, w_key, w_value)):
        ref[...] = qkv[i].astype(jnp.float32)
    half = out.shape[2]
    for i in range(2):
        w_out[:, i * half : (i + 1) * half] = out[i].astype(jnp.float32)


def widen(down, gate, up, qkv, out):
    steps = 8
    full = jnp.float32

    def rows(array):
        return pl.BlockSpec((array.shape[0] // steps, array.shape[1]), lambda i: (i, 0))

    def stacked(array):
        return pl.BlockSpec((array.shape[0], array.shape[1] // steps, array.shape[2]), lambda i: (0, i, 0))

    like = [down, gate, up, qkv[0], qkv[0], qkv[0]]
    shapes = [jax.ShapeDtypeStruct(array.shape, full) for array in like]
    shapes.append(jax.ShapeDtypeStruct((out.shape[1], 2 * out.shape[2]), full))
    return pl.pallas_call(
        widen_kernel,
        grid=(steps,),
        in_specs=[rows(down), rows(gate), rows(up), stacked(qkv), stacked(out)],
        out_specs=[rows(shape) for shape in shapes],
        out_shape=shapes,
        compiler_params=pltpu.CompilerParams(vmem_limit_bytes=VMEM_LIMIT),
        name="widen",
    )(down, gate, up, qkv, out)


def local(
    tokens, attn_gain, w_query, w_key, w_value, w_out, ffn_gain, w_gate, w_up, w_down, cotangent
):
    cosine, sine = rope_tables(tokens.shape[0] * lax.axis_size("fsdp"))
    (
        lowered_one,
        lowered_two,
        cotangents,
        slab_qkv,
        hidden,
        grad_gate,
        grad_up,
        terms,
        sums,
        queries,
        keys,
        values,
        attended,
        logs,
        after_attn,
        gains,
    ) = front(
        tokens,
        cotangent,
        attn_gain,
        ffn_gain,
        w_query,
        w_key,
        w_value,
        w_out,
        w_gate,
        w_up,
        w_down,
        cosine,
        sine,
    )
    grad_after, gain_terms, branch, half_down, sum_gate, sum_up = weigh(
        cotangent, after_attn, gains, terms, lowered_two, cotangents, hidden, grad_gate, grad_up
    )
    outputs, grad_tokens, gain_grads, low_down, low_gate, low_up, low_qkv, low_out = back(
        tokens,
        gains,
        grad_after,
        gain_terms,
        after_attn,
        sums,
        half_down,
        sum_gate,
        sum_up,
        branch,
        lowered_one,
        slab_qkv,
        w_out,
        queries,
        keys,
        values,
        attended,
        logs,
        cosine,
        sine,
    )
    grad_w_down, grad_w_gate, grad_w_up, grad_w_query, grad_w_key, grad_w_value, grad_w_out = widen(
        low_down.reshape(w_down.shape),
        low_gate.reshape(w_gate.shape),
        low_up.reshape(w_up.shape),
        low_qkv.reshape((3,) + w_query.shape),
        low_out.reshape(2, w_out.shape[0], -1),
    )
    return (
        outputs,
        grad_tokens,
        gain_grads[0],
        grad_w_query,
        grad_w_key,
        grad_w_value,
        grad_w_out,
        gain_grads[1],
        grad_w_gate,
        grad_w_up,
        grad_w_down,
    )


def solution(mesh):
    rows = P("fsdp", None)
    tokens = P(("replica", "fsdp"), None)
    gain = P("fsdp")
    return jax.shard_map(
        local,
        mesh=mesh,
        in_specs=(tokens, gain, rows, rows, rows, rows, gain, rows, rows, rows, tokens),
        out_specs=(tokens, tokens, gain, rows, rows, rows, rows, gain, rows, rows, rows),
        check_vma=False,
    )
```

```python
import functools

import jax
import jax.numpy as jnp
import numpy as np
from jax import lax
from jax.experimental import pallas as pl
from jax.experimental.pallas import tpu as pltpu
from jax.sharding import PartitionSpec as P

HEAD_DIM = 64

eps_norm = 1e-05
rope_base = 130000.0
masked_score = -1e30


def rope_tables(row_count):
    lane = np.arange(2 * HEAD_DIM) % HEAD_DIM
    halfway = HEAD_DIM // 2
    spacing = ((lane % halfway) * np.float32(2.0) / HEAD_DIM).astype(np.float32)
    frequency = np.power(np.float32(rope_base), -spacing)
    angles = np.arange(row_count, dtype=np.float32)[:, None] * frequency[None, :]
    sign = np.where(lane < halfway, -1.0, 1.0).astype(np.float32)
    return np.cos(angles).astype(np.float32), (np.sin(angles) * sign[None, :]).astype(np.float32)


def dot(left, right):
    return jnp.dot(left, right, preferred_element_type=jnp.float32)


def contract_last(left, right):
    return lax.dot_general(
        left, right, (((1,), (1,)), ((), ())), preferred_element_type=jnp.float32
    )


def contract_first(left, right):
    return lax.dot_general(
        left, right, (((0,), (0,)), ((), ())), preferred_element_type=jnp.float32
    )


def scores_of(queries, keys, first_row):
    rows, columns = queries.shape[0], keys.shape[0]
    scores = contract_last(queries, keys) * HEAD_DIM**-0.5
    at_row = lax.broadcasted_iota(jnp.int32, (rows, columns), 0) + first_row
    at_column = lax.broadcasted_iota(jnp.int32, (rows, columns), 1)
    return jnp.where(at_column <= at_row, scores, masked_score)


MESH = pl.DeviceIdType.MESH
VMEM_LIMIT = 60 * 2**20


def remote(src, dst, send, recv, **where):
    return pltpu.make_async_remote_copy(
        src_ref=src, dst_ref=dst, send_sem=send, recv_sem=recv, device_id=where, device_id_type=MESH
    )


def await_bytes(ref, sem):
    pltpu.make_async_copy(ref, ref, sem).wait()


def rows_at(ref, index, size):
    return ref.at[pl.ds(pl.multiple_of(index * size, size), size)]


class Place:
    def __init__(self):
        self.fsdp, self.replicas = lax.axis_size("fsdp"), lax.axis_size("replica")
        self.me, self.replica = lax.axis_index("fsdp"), lax.axis_index("replica")
        self.chips = self.fsdp // 2
        self.chip, self.core = self.me // 2, self.me % 2
        self.sibling = self.me + 1 - 2 * self.core
        self.high, self.wide = 2, self.replicas // 2
        self.a, self.b = self.replica // self.wide, self.replica % self.wide
        self.counts = ((self.wide, self.high), (self.high, self.wide))
        self.above = self.chip + 1 < self.chips
        self.below = self.chip >= 1

    def peer(self, half, stage, k):
        if half == stage:
            to = lax.rem(self.b + k, self.wide)
            return to, self.a * self.wide + to
        to = lax.rem(self.a + k, self.high)
        return to, to * self.wide + self.b

    def at_step(self, step, do):
        if step == 0:
            do(self.chip)
            return
        pl.when(self.chip >= step)(lambda: do(self.chip - step))
        pl.when(self.chip + step < self.chips)(lambda: do(self.chip + step))

    def nearest(self, k):
        found = jnp.int32(0)
        for chip in range(self.chips):
            order = sorted(range(self.chips), key=lambda other, chip=chip: (abs(other - chip), other))
            found = found + jnp.where(self.chip == chip, order[k], 0)
        return found

    def enter(self):
        barrier = pltpu.get_barrier_semaphore()

        def greet(k, _):
            to = lax.rem(self.me + k, self.fsdp)
            pl.semaphore_signal(barrier, inc=1, device_id={"fsdp": to}, device_id_type=MESH)
            return 0

        def greet_replica(k, _):
            to = lax.rem(self.replica + k, self.replicas)
            pl.semaphore_signal(barrier, inc=1, device_id={"replica": to}, device_id_type=MESH)
            return 0

        lax.fori_loop(1, self.fsdp, greet, 0)
        lax.fori_loop(1, self.replicas, greet_replica, 0)
        pl.semaphore_wait(barrier, self.fsdp - 1 + self.replicas - 1)


def line_sems(chips):
    return [pltpu.SemaphoreType.DMA((chips,))] * 6


class Gather:
    def __init__(self, place, buf, block, sems, own=None):
        self.p, self.buf, self.block, self.own = place, buf, block, own
        self.up_out, self.up_in, self.down_out, self.down_in, self.side_out, self.side_in = sems

    def held(self, chip):
        return rows_at(self.buf, 2 * chip + self.p.core, self.block)

    def up(self, step):
        ref = self.held(self.p.chip - step + 1)
        src = self.own if step == 1 and self.own is not None else ref
        return remote(src, ref, self.up_out.at[step], self.up_in.at[step], fsdp=self.p.me + 2)

    def down(self, step):
        ref = self.held(self.p.chip + step - 1)
        src = self.own if step == 1 and self.own is not None else ref
        return remote(src, ref, self.down_out.at[step], self.down_in.at[step], fsdp=self.p.me - 2)

    def side(self, chip, src=None):
        ref = self.held(chip)
        src = ref if src is None else src
        return remote(src, ref, self.side_out.at[chip], self.side_in.at[chip], fsdp=self.p.sibling)

    def start(self):
        p = self.p
        pl.when(p.above)(lambda: self.up(1).start())
        pl.when(p.below)(lambda: self.down(1).start())
        self.side(p.chip, self.own).start()

    def step(self, step):
        p = self.p
        from_below, from_above = p.chip - step, p.chip + step

        @pl.when(from_below >= 0)
        def _():
            await_bytes(self.held(from_below), self.up_in.at[step])
            if step + 1 < p.chips:
                pl.when(p.above)(lambda: self.up(step + 1).start())
            self.side(from_below).start()

        @pl.when(from_above < p.chips)
        def _():
            await_bytes(self.held(from_above), self.down_in.at[step])
            if step + 1 < p.chips:
                pl.when(p.below)(lambda: self.down(step + 1).start())
            self.side(from_above).start()

    def across(self, chip):
        await_bytes(rows_at(self.buf, 2 * chip + 1 - self.p.core, self.block), self.side_in.at[chip])

    def drain(self):
        p = self.p
        for step in range(1, p.chips):
            pl.when(jnp.logical_and(p.above, p.chip - step + 1 >= 0))(
                lambda step=step: self.up(step).wait_send()
            )
            pl.when(jnp.logical_and(p.below, p.chip + step - 1 < p.chips))(
                lambda step=step: self.down(step).wait_send()
            )
        for chip in range(p.chips):
            self.side(chip).wait_send()

    def finish(self):
        for chip in range(self.p.chips):
            self.across(chip)
        self.drain()


class Scatter:
    def __init__(self, place, terms, across, slots, block, sems):
        self.p, self.terms, self.across, self.slots, self.block = place, terms, across, slots, block
        self.up_out, self.up_in, self.down_out, self.down_in, self.side_out, self.side_in = sems

    def side(self, chip):
        p = self.p
        return remote(
            rows_at(self.terms, 2 * chip + 1 - p.core, self.block),
            rows_at(self.across, chip, self.block),
            self.side_out.at[chip],
            self.side_in.at[chip],
            fsdp=p.sibling,
        )

    def term(self, chip):
        return rows_at(self.terms, 2 * chip + self.p.core, self.block)

    def up(self, step):
        return remote(
            self.term(self.p.chips - step + self.p.chip),
            self.slots.at[step - self.p.chip - 1],
            self.up_out.at[step],
            self.up_in.at[step],
            fsdp=self.p.me + 2,
        )

    def down(self, step):
        return remote(
            self.term(self.p.chip - self.p.chips + step),
            self.slots.at[step + 1],
            self.down_out.at[step],
            self.down_in.at[step],
            fsdp=self.p.me - 2,
        )

    def add(self, chip, arrived):
        term = self.term(chip)
        term[...] = (term[...].astype(jnp.float32) + arrived[...].astype(jnp.float32)).astype(term.dtype)

    def cross(self, chip):
        arrived = rows_at(self.across, chip, self.block)
        await_bytes(arrived, self.side_in.at[chip])
        self.add(chip, arrived)

    def step(self, step):
        p = self.p
        rising, falling = p.chips - step + p.chip, p.chip - p.chips + step

        @pl.when(jnp.logical_and(p.above, rising < p.chips))
        def _():
            if step > 1:

                @pl.when(p.below)
                def _():
                    arrived = self.slots.at[step - 1 - p.chip]
                    await_bytes(arrived, self.up_in.at[step - 1])
                    self.add(rising, arrived)

            self.up(step).start()

        @pl.when(jnp.logical_and(p.below, falling >= 0))
        def _():
            if step > 1:

                @pl.when(p.above)
                def _():
                    arrived = self.slots.at[step]
                    await_bytes(arrived, self.down_in.at[step - 1])
                    self.add(falling, arrived)

            self.down(step).start()

    def finish(self, total):
        p, last = self.p, self.p.chips - 1
        total[...] = self.term(p.chip)[...].astype(jnp.float32)

        @pl.when(p.below)
        def _():
            await_bytes(self.slots.at[last - p.chip], self.up_in.at[last])
            total[...] += self.slots[last - p.chip].astype(jnp.float32)

        @pl.when(p.above)
        def _():
            await_bytes(self.slots.at[last + 1], self.down_in.at[last])
            total[...] += self.slots[last + 1].astype(jnp.float32)

    def drain(self):
        p = self.p
        for step in range(1, p.chips):
            pl.when(jnp.logical_and(p.above, p.chips - step + p.chip < p.chips))(
                lambda step=step: self.up(step).wait_send()
            )
            pl.when(jnp.logical_and(p.below, p.chip - p.chips + step >= 0))(
                lambda step=step: self.down(step).wait_send()
            )
        for chip in range(p.chips):
            self.side(chip).wait_send()


def scatter_sems(chips):
    dma = pltpu.SemaphoreType.DMA
    return [dma((chips,))] * 6


class Turn:
    def __init__(self, place, weight, slab, first, sems):
        self.p, self.weight, self.slab, self.first = place, weight, slab, first
        self.far_out, self.far_in, self.near_out, self.near_in, self.own, self.passing = sems
        self.height, self.width = weight.shape[0], slab.shape[1]
        self.share = self.height // place.replicas

    def far_rows(self):
        return (self.p.fsdp - 2) * self.share

    def piece(self, block, share):
        at = self.first + block * self.height + share * self.share
        return self.slab.at[pl.ds(pl.multiple_of(at, self.share), self.share)]

    def whole(self, block):
        at = self.first + block * self.height
        return self.slab.at[pl.ds(pl.multiple_of(at, self.height), self.height)]

    def columns(self, to):
        return pl.ds(pl.multiple_of(to * self.width, self.width), self.width)

    def start(self):
        p = self.p

        def send(k, _):
            to = lax.rem(2 * p.chip + 2 + k, p.fsdp)
            share = pl.ds(pl.multiple_of(p.replica * self.share, self.share), self.share)
            remote(
                self.weight.at[share, self.columns(to)],
                self.piece(p.me, p.replica),
                self.far_out,
                self.far_in,
                fsdp=to,
            ).start()
            return 0

        lax.fori_loop(0, p.fsdp - 2, send, 0)
        self.near().start()
        self.mine().start()

    def near(self):
        p = self.p
        return remote(
            self.weight.at[:, self.columns(p.sibling)], self.whole(p.me), self.near_out, self.near_in, fsdp=p.sibling
        )

    def mine(self):
        return pltpu.make_async_copy(self.weight.at[:, self.columns(self.p.me)], self.whole(self.p.me), self.own)

    def await_far(self):
        await_bytes(self.slab.at[pl.ds(0, self.far_rows())], self.far_in)

    def bytes_of(self, pieces):
        return self.slab.at[pl.ds(0, pieces * self.share)]

    def pass_bytes(self, half, stage):
        first, second = self.p.counts[half]
        return self.bytes_of((self.p.chips - 1) * (second - 1 if stage == 0 else second * (first - 1)))

    def send_pieces(self, half, stage, shares):
        p = self.p

        def one(i, _):
            block = lax.rem(2 * p.chip + 2 + 2 * i + half, p.fsdp)
            for share in shares:
                ref = self.piece(block, share)
                for k in range(1, p.counts[half][1 - stage]):
                    _, replica = p.peer(half, 1 - stage, k)
                    remote(
                        ref,
                        ref,
                        self.passing.at[half, 2 * stage],
                        self.passing.at[half, 2 * stage + 1],
                        replica=replica,
                    ).start()
            return 0

        lax.fori_loop(0, p.chips - 1, one, 0)

    def pass_on(self):
        for half in range(2):
            self.send_pieces(half, 0, [self.p.replica])

    def pass_far(self):
        p = self.p
        for half in range(2):
            await_bytes(self.pass_bytes(half, 0), self.passing.at[half, 1])
            if half == 0:
                shares = [a * p.wide + p.b for a in range(p.high)]
            else:
                shares = [p.a * p.wide + b for b in range(p.wide)]
            self.send_pieces(half, 1, shares)

    def finish(self):
        for half in range(2):
            await_bytes(self.pass_bytes(half, 1), self.passing.at[half, 3])
        await_bytes(self.whole(self.p.sibling), self.near_in)
        self.mine().wait()

    def drain(self):
        await_bytes(self.slab.at[pl.ds(0, self.far_rows())], self.far_out)
        self.near().wait_send()
        for half in range(2):
            await_bytes(self.pass_bytes(half, 0), self.passing.at[half, 0])
            await_bytes(self.pass_bytes(half, 1), self.passing.at[half, 2])


def turn_sems():
    return [pltpu.SemaphoreType.DMA(())] * 5 + [pltpu.SemaphoreType.DMA((2, 4))]


class Everywhere:
    def __init__(self, place, buf, block, sems, side_sems):
        self.p, self.buf, self.block, self.sems, self.side_sems = place, buf, block, sems, side_sems
        self.width = buf.shape[3] // 2

    def columns(self, half):
        return pl.ds(half * self.width, self.width)

    def rows(self, chip):
        at = (2 * chip + self.p.core) * self.block
        return pl.ds(pl.multiple_of(at, self.block), self.block)

    def ref(self, half, a, b, chip):
        return self.buf.at[a, b, self.rows(chip), self.columns(half)]

    def spread(self, chip, own=None):
        p = self.p
        for half in range(2):
            ref = self.ref(half, p.a, p.b, chip)
            src = ref if own is None else own.at[:, self.columns(half)]
            for k in range(1, p.counts[half][1]):
                _, replica = p.peer(half, 1, k)
                remote(
                    src, ref, self.sems.at[chip, half, 0], self.sems.at[chip, half, 1], replica=replica
                ).start()

    def spread_bytes(self, half, chip):
        some = pl.ds(0, self.p.counts[half][1] - 1)
        return self.ref(half, some, 0, chip) if half == 0 else self.ref(half, 0, some, chip)

    def widen(self, chip):
        p = self.p
        for half in range(2):
            await_bytes(self.spread_bytes(half, chip), self.sems.at[chip, half, 1])
            every = pl.ds(0, p.counts[half][1])
            ref = self.ref(half, every, p.b, chip) if half == 0 else self.ref(half, p.a, every, chip)
            for k in range(1, p.counts[half][0]):
                _, replica = p.peer(half, 0, k)
                remote(
                    ref, ref, self.sems.at[chip, half, 2], self.sems.at[chip, half, 3], replica=replica
                ).start()

    def widen_bytes(self, half, chip):
        counts = self.p.counts[half]
        every, some = pl.ds(0, counts[1]), pl.ds(0, counts[0] - 1)
        return self.ref(half, every, some, chip) if half == 0 else self.ref(half, some, every, chip)

    def share(self, chip):
        p = self.p
        for half in range(2):
            await_bytes(self.widen_bytes(half, chip), self.sems.at[chip, half, 3])
        for k in range(1, p.replicas):
            other = lax.rem(p.replica + k, p.replicas)
            ref = self.buf.at[other // p.wide, other % p.wide, self.rows(chip)]
            remote(
                ref, ref, self.side_sems.at[chip, 0], self.side_sems.at[chip, 1], fsdp=p.sibling
            ).start()

    def finish(self):
        shared = self.buf.at[0, 0, pl.ds(0, (self.p.replicas - 1) * self.block)]
        for chip in range(self.p.chips):
            await_bytes(shared, self.side_sems.at[chip, 1])
            await_bytes(shared, self.side_sems.at[chip, 0])
            for half in range(2):
                await_bytes(self.spread_bytes(half, chip), self.sems.at[chip, half, 0])
                await_bytes(self.widen_bytes(half, chip), self.sems.at[chip, half, 2])


def partner(values):
    halfway = HEAD_DIM // 2
    width = values.shape[1]
    lane = lax.broadcasted_iota(jnp.int32, values.shape, 1) % HEAD_DIM
    return jnp.where(
        lane < halfway,
        pltpu.roll(values, width - halfway, axis=1),
        pltpu.roll(values, halfway, axis=1),
    )


def front_kernel(
    tokens,
    cotangent,
    gain_one,
    gain_two,
    w_query,
    w_key,
    w_value,
    w_out,
    w_gate,
    w_up,
    w_down,
    cosine,
    sine,
    lowered_one,
    lowered_two_out,
    all_cotangents,
    slab_qkv_out,
    all_hidden,
    grad_gate_out,
    grad_up_out,
    terms_out,
    sums_out,
    queries,
    keys,
    values,
    attended,
    logs,
    after_attn,
    gains,
    low,
    tiles,
    lowered_two,
    slab_qkv,
    slab_gate,
    slab_up,
    held_down,
    terms,
    across,
    slots,
    tile_hidden,
    tile_gate,
    tile_up,
    tile_terms,
    tile_sums,
    gain_rows,
    gain_out,
    gain_in,
    copy_sems,
    load_sems,
    store_sems,
    hidden_sems,
    every_sems,
    every_side,
    *sems,
):
    place = Place()
    chips, block = place.chips, tokens.shape[0]
    model, width = tokens.shape[1], queries.shape[1]
    share = gain_one.shape[0]
    tile = 2 * block
    one_at, cot_at, two_at, scatter_at = sems[:6], sems[6:12], sems[12:18], sems[18:24]
    turn_at = [sems[24 + 6 * i : 30 + 6 * i] for i in range(5)]
    cotangents = all_cotangents.at[place.a, place.b]
    every = Everywhere(place, all_cotangents, block, every_sems, every_side)
    turns = [
        Turn(place, weight, slab_qkv, i * model, turn_at[i])
        for i, weight in enumerate((w_query, w_key, w_value))
    ]
    turn_gate = Turn(place, w_gate, slab_gate, 0, turn_at[3])
    turn_up = Turn(place, w_up, slab_up, 0, turn_at[4])
    here = pl.ds(pl.multiple_of(place.me * block, block), block)

    gain_rows[...] = jnp.zeros_like(gain_rows)
    gain_rows[0, :] = gain_one[...].astype(jnp.float32)
    gain_rows[1, :] = gain_two[...].astype(jnp.float32)
    load_down = pltpu.make_async_copy(w_down, held_down, copy_sems.at[0])
    load_down.start()
    keep_cot = pltpu.make_async_copy(cotangent, cotangents.at[here], copy_sems.at[1])
    keep_cot.start()
    place.enter()

    def send_gains(k, _):
        to = lax.rem(place.me + k, place.fsdp)
        remote(gain_rows, gains.at[place.me], gain_out, gain_in, fsdp=to).start()
        return 0

    lax.fori_loop(1, place.fsdp, send_gains, 0)
    for turn in turns:
        turn.start()
    every.spread(place.chip, cotangent)
    gains[place.me] = gain_rows[...]
    inputs = tokens[...].astype(jnp.float32)
    factor = lax.rsqrt(jnp.mean(inputs * inputs, axis=-1, keepdims=True) + eps_norm)
    await_bytes(gains.at[pl.ds(0, place.fsdp - 1)], gain_in)
    for j in range(model // share):
        at = pl.ds(j * share, share)
        normed = tokens[:, at].astype(jnp.float32) * factor
        low[:, at] = (normed * gains[j, 0:1, :]).astype(jnp.bfloat16)
    first = Gather(place, lowered_one, block, one_at, low)
    first.start()
    keep_low = pltpu.make_async_copy(low, lowered_one.at[here], copy_sems.at[2])
    keep_low.start()
    at_end = jnp.logical_or(place.chip == 0, place.chip == chips - 1)
    pl.when(at_end)(turn_gate.start)
    for turn in turns:
        turn.await_far()
        turn.pass_on()
    for step in range(1, chips):
        if step == chips - 1:
            pl.when(jnp.logical_not(at_end))(turn_gate.start)
        first.step(step)
        if step == 1:
            for turn in turns:
                turn.pass_far()
            keep_cot.wait()
            every.widen(place.chip)
    turn_up.start()
    third = Gather(place, cotangents, block, cot_at, cotangent)
    third.start()
    keep_low.wait()
    first.finish()

    def load(source, t, slot):
        return pltpu.make_async_copy(rows_at(source, t, tile), tiles.at[slot], load_sems.at[slot])

    load(lowered_one, 0, 0).start()
    for turn in turns:
        turn.finish()
    keep_slab = pltpu.make_async_copy(slab_qkv, slab_qkv_out, copy_sems.at[3])
    keep_slab.start()
    for t in range(chips):
        if t + 1 < chips:
            load(lowered_one, t + 1, (t + 1) % 2).start()
        load(lowered_one, t, t % 2).wait()
        at = pl.ds(t * tile, tile)
        for i, ref in enumerate((queries, keys, values)):
            out = dot(tiles[t % 2], slab_qkv[i * model : (i + 1) * model, :])
            if i < 2:
                for j in range(0, width, 2 * HEAD_DIM):
                    pair = out[:, j : j + 2 * HEAD_DIM]
                    pair = pair * cosine[at, :] + partner(pair) * sine[at, :]
                    ref[at, j : j + 2 * HEAD_DIM] = pair.astype(jnp.bfloat16)
            else:
                ref[at, :] = out.astype(jnp.bfloat16)
    scatter = Scatter(place, terms, across, slots, block, scatter_at)
    pair = 2 * HEAD_DIM
    for t in range(chips):
        here_t, seen = pl.ds(t * tile, tile), pl.ds(0, (t + 1) * tile)

        def heads(h, _, t=t, here_t=here_t, seen=seen):
            lanes = pl.ds(pl.multiple_of(h * pair, pair), pair)
            q2, k2, v2 = queries[here_t, lanes], keys[seen, lanes], values[seen, lanes]
            mixed, stats = [], []
            for at in (0, HEAD_DIM):
                head = slice(at, at + HEAD_DIM)
                scores = scores_of(q2[:, head], k2[:, head], t * tile)
                most = jnp.max(scores, axis=-1, keepdims=True)
                weights = jnp.exp(scores - most)
                total = jnp.sum(weights, axis=-1, keepdims=True)
                mixed.append(dot((weights / total).astype(jnp.bfloat16), v2[:, head]))
                stats.append(jnp.broadcast_to(most + jnp.log(total), (tile, HEAD_DIM)))
            attended[here_t, lanes] = jnp.concatenate(mixed, axis=1).astype(jnp.bfloat16)
            logs[here_t, lanes] = jnp.concatenate(stats, axis=1)
            return 0

        lax.fori_loop(0, width // pair, heads, 0)
        terms[here_t, :] = dot(attended[here_t, :], w_out[...]).astype(jnp.bfloat16)
        scatter.side(t).start()
    turn_gate.await_far()
    turn_gate.pass_on()
    for t in range(chips):
        scatter.cross(t)
    for step in range(1, chips):
        scatter.step(step)
        if step == 1:
            turn_gate.pass_far()
            turn_up.await_far()
            turn_up.pass_on()
        if step < chips - 1:
            third.step(step)
        if step == 1:
            turn_up.pass_far()
        if step < chips - 1:
            place.at_step(step, every.spread)
        if step == 2:
            every.share(place.chip)
        if step == chips - 1 and chips > 2:
            place.at_step(1, every.widen)
    scatter.finish(after_attn)
    after_attn[...] += tokens[...].astype(jnp.float32)
    after = after_attn[...]
    factor = lax.rsqrt(jnp.mean(after * after, axis=-1, keepdims=True) + eps_norm)
    for j in range(model // share):
        at = pl.ds(j * share, share)
        normed = after_attn[:, at] * factor
        lowered_two[here, at] = (normed * gains[j, 1:2, :]).astype(jnp.bfloat16)
    second = Gather(place, lowered_two, block, two_at)
    second.start()
    third.step(chips - 1)
    place.at_step(chips - 1, every.spread)
    if chips == 2:
        every.share(place.chip)
        place.at_step(1, every.widen)
    third.finish()
    if chips > 2:
        place.at_step(2, every.widen)
    load(cotangents, place.nearest(0), 0).start()
    turn_gate.finish()
    turn_up.finish()
    load_down.wait()

    def stores(k, t):
        slot = k % 2
        pairs = (
            (tile_hidden.at[:, place.replica], all_hidden.at[place.replica]),
            (tile_gate, grad_gate_out),
            (tile_up, grad_up_out),
            (tile_terms, terms_out),
            (tile_sums, sums_out),
        )
        return [
            pltpu.make_async_copy(held.at[slot], rows_at(out, t, tile), store_sems.at[i, slot])
            for i, (held, out) in enumerate(pairs)
        ]

    def hidden_bytes(slot):
        return tile_hidden.at[slot, pl.ds(0, place.replicas - 1)]

    for k in range(chips):
        t, slot = place.nearest(k), k % 2
        if k > 0:
            second.step(k)
            if k + 2 < chips:
                place.at_step(k + 2, every.widen)
        second.across(t)
        if k + 1 < chips:
            load(cotangents, place.nearest(k + 1), (k + 1) % 2).start()
        load(cotangents, t, slot).wait()
        if k > 1:
            for store in stores(k - 2, place.nearest(k - 2)):
                store.wait()
            await_bytes(hidden_bytes(slot), hidden_sems.at[slot])
        rows = lowered_two[pl.ds(pl.multiple_of(t * tile, tile), tile), :]
        gate = dot(rows, slab_gate[...])
        up = dot(rows, slab_up[...])
        grad_hidden = contract_last(tiles[slot], held_down[...])
        sigmoid = jax.nn.sigmoid(gate)
        silu = gate * sigmoid
        hidden = (silu * up).astype(jnp.bfloat16)
        grad_gate = (grad_hidden * up * sigmoid * (1.0 + gate * (1.0 - sigmoid))).astype(jnp.bfloat16)
        grad_up = (grad_hidden * silu).astype(jnp.bfloat16)
        part = tile_hidden.shape[3]
        for other in range(place.replicas):
            tile_hidden[slot, other] = hidden[:, other * part : (other + 1) * part]
        tile_gate[slot] = grad_gate
        tile_up[slot] = grad_up
        got = contract_last(grad_gate, slab_gate[...]) + contract_last(grad_up, slab_up[...])
        tile_terms[slot] = got.astype(jnp.bfloat16)
        tile_sums[slot] = dot(hidden, held_down[...]).astype(jnp.bfloat16)
        for store in stores(k, t):
            store.start()
        for j in range(1, place.replicas):
            to = lax.rem(place.replica + j, place.replicas)
            remote(
                tile_hidden.at[slot, to],
                rows_at(all_hidden.at[place.replica], t, tile),
                hidden_sems.at[slot],
                hidden_sems.at[2],
                replica=to,
            ).start()
        if k > 1:
            place.at_step(k - 1, every.share)
    place.at_step(chips - 1, every.share)
    keep_two = pltpu.make_async_copy(lowered_two, lowered_two_out, copy_sems.at[4])
    keep_two.start()
    second.drain()
    scatter.drain()
    for turn in turns + [turn_gate, turn_up]:
        turn.drain()
    await_bytes(gains.at[pl.ds(0, place.fsdp - 1)], gain_out)
    keep_slab.wait()
    for k in range(max(chips - 2, 0), chips):
        for store in stores(k, place.nearest(k)):
            store.wait()
        await_bytes(hidden_bytes(k % 2), hidden_sems.at[k % 2])
    await_bytes(all_hidden.at[pl.ds(0, place.replicas - 1)], hidden_sems.at[2])
    every.finish()
    keep_two.wait()


def front(
    tokens, cotangent, gain_one, gain_two, w_query, w_key, w_value, w_out, w_gate, w_up, w_down, cosine, sine
):
    fsdp, replicas = lax.axis_size("fsdp"), lax.axis_size("replica")
    chips, high, across_b = fsdp // 2, 2, replicas // 2
    block, model = tokens.shape
    rows, width, wide = fsdp * block, w_query.shape[1] // fsdp, w_gate.shape[1] // fsdp
    tile = 2 * block
    share = gain_one.shape[0]
    low, full = jnp.bfloat16, jnp.float32
    hbm, vmem = pl.BlockSpec(memory_space=pl.ANY), pl.BlockSpec(memory_space=pltpu.VMEM)
    shape = jax.ShapeDtypeStruct
    dma = pltpu.SemaphoreType.DMA
    return pl.pallas_call(
        front_kernel,
        in_specs=[vmem] * 4 + [hbm] * 3 + [vmem] + [hbm] * 3 + [vmem] * 2,
        out_specs=[hbm] * 9 + [vmem] * 7,
        out_shape=[
            shape((rows, model), low),
            shape((rows, model), low),
            shape((high, across_b, rows, model), low),
            shape((3 * model, width), low),
            shape((replicas, rows, wide // replicas), low),
            shape((rows, wide), low),
            shape((rows, wide), low),
            shape((rows, model), low),
            shape((rows, model), low),
            shape((rows, width), low),
            shape((rows, width), low),
            shape((rows, width), low),
            shape((rows, width), low),
            shape((rows, width), full),
            shape((block, model), full),
            shape((fsdp, 8, share), full),
        ],
        scratch_shapes=[
            pltpu.VMEM((block, model), low),
            pltpu.VMEM((2, tile, model), low),
            pltpu.VMEM((rows, model), low),
            pltpu.VMEM((3 * model, width), low),
            pltpu.VMEM((model, wide), low),
            pltpu.VMEM((model, wide), low),
            pltpu.VMEM((wide, model), low),
            pltpu.VMEM((rows, model), low),
            pltpu.VMEM((chips * block, model), low),
            pltpu.VMEM((chips + 1, block, model), low),
            pltpu.VMEM((2, replicas, tile, wide // replicas), low),
            pltpu.VMEM((2, tile, wide), low),
            pltpu.VMEM((2, tile, wide), low),
            pltpu.VMEM((2, tile, model), low),
            pltpu.VMEM((2, tile, model), low),
            pltpu.VMEM((8, share), full),
            dma(()),
            dma(()),
            dma((5,)),
            dma((2,)),
            dma((5, 2)),
            dma((3,)),
            dma((chips, 2, 4)),
            dma((chips, 2)),
        ]
        + line_sems(chips) * 3
        + scatter_sems(chips)
        + turn_sems() * 5,
        compiler_params=pltpu.CompilerParams(
            collective_id=0, has_side_effects=True, vmem_limit_bytes=VMEM_LIMIT
        ),
        name="front",
    )(
        tokens,
        cotangent,
        gain_one,
        gain_two,
        w_query,
        w_key,
        w_value,
        w_out,
        w_gate,
        w_up,
        w_down,
        cosine,
        sine,
    )


class Reduce:
    def __init__(self, place, part, first, second, sems):
        self.p, self.part, self.first, self.second, self.sems = place, part, first, second, sems
        self.half = part.shape[0] // 2

    def rows(self, half):
        return pl.ds(half * self.half, self.half)

    def sent(self, half, to):
        if half == 0:
            return self.part.at[self.rows(0), :, to]
        return self.part.at[self.rows(1), to]

    def own(self, half):
        return self.sent(half, self.p.b if half == 0 else self.p.a)

    def start(self, half):
        for k in range(1, self.p.counts[half][0]):
            to, replica = self.p.peer(half, 0, k)
            remote(
                self.sent(half, to),
                self.first[half].at[k - 1],
                self.sems.at[half, 0],
                self.sems.at[half, 1],
                replica=replica,
            ).start()

    def exchange(self):
        for half in range(2):
            own, arrived = self.own(half), self.first[half]
            await_bytes(arrived, self.sems.at[half, 1])

            def add(n, _, own=own, arrived=arrived):
                for m in range(own.shape[1]):
                    total = own[n, m].astype(jnp.float32)
                    for k in range(arrived.shape[0]):
                        total += arrived[k, n, m].astype(jnp.float32)
                    own[n, m] = total.astype(own.dtype)
                return 0

            lax.fori_loop(0, self.half, add, 0)
            for k in range(1, self.p.counts[half][1]):
                to, replica = self.p.peer(half, 1, k)
                remote(
                    own.at[:, to],
                    self.second[half].at[k - 1],
                    self.sems.at[half, 2],
                    self.sems.at[half, 3],
                    replica=replica,
                ).start()

    def total(self):
        for half in range(2):
            own, arrived = self.held(half), self.second[half]
            await_bytes(arrived, self.sems.at[half, 3])

            def add(n, _, own=own, arrived=arrived):
                total = own[n].astype(jnp.float32)
                for k in range(arrived.shape[0]):
                    total += arrived[k, n].astype(jnp.float32)
                own[n] = total.astype(own.dtype)
                return 0

            lax.fori_loop(0, self.half, add, 0)

    def held(self, half):
        return self.part.at[self.rows(half), self.p.a, self.p.b]

    def piece(self, n):
        return self.part.at[n, self.p.a, self.p.b]

    def drain(self):
        for half in range(2):
            await_bytes(self.first[half], self.sems.at[half, 0])
            await_bytes(self.second[half], self.sems.at[half, 2])


def reduce_scratch(n, high, wide, rows, columns):
    low = functools.partial(pltpu.VMEM, dtype=jnp.bfloat16)
    half = n // 2
    return [
        low((n, high, wide, rows, columns)),
        low((wide - 1, half, high, rows, columns)),
        low((high - 1, half, wide, rows, columns)),
        low((high - 1, half, rows, columns)),
        low((wide - 1, half, rows, columns)),
        pltpu.SemaphoreType.DMA((2, 4)),
    ]


def reducer(place, refs):
    part, first_a, first_b, second_a, second_b, sems = refs
    return Reduce(place, part, (first_a, first_b), (second_a, second_b), sems)


class Spread:
    def __init__(self, place, piece, out, sems, turned, split=False):
        self.p, self.piece, self.out, self.sems = place, piece, out, sems
        self.turned, self.split = turned, split

    def start(self):
        p = self.p
        if self.turned:
            count = self.out.shape[0]
            width = self.out.shape[-1] // p.fsdp
            columns = pl.ds(pl.multiple_of(p.me * width, width), width)

            def pairs(to):
                ref = self.piece(to)
                return [
                    (ref.at[:, pl.ds(i * width, width)], self.out.at[i, p.a, p.b, :, columns])
                    for i in range(count)
                ]

            def send(k, _):
                to = lax.rem(p.me + k, p.fsdp)
                for ref, target in pairs(to):
                    remote(ref, target, self.sems.at[0, 0], self.sems.at[0, 1], fsdp=to).start()
                return 0

            lax.fori_loop(1, p.fsdp, send, 0)
            for ref, target in pairs(p.me):
                pltpu.make_async_copy(ref, target, self.sems.at[0, 1]).start()
        else:
            for half in range(2):
                pltpu.make_async_copy(
                    self.source(half), self.placed(half, (p.a, p.b)), self.sems.at[half, 1]
                ).start()

    def columns(self, half):
        width = self.out.shape[-1] // 2
        return pl.ds(half * width, width)

    def placed(self, half, rows):
        a, b = rows
        if self.split:
            return self.out.at[half, a, b]
        return self.out.at[:, a, b, :, self.columns(half)]

    def source(self, half):
        if self.turned:
            return self.placed(half, (self.p.a, self.p.b))
        if self.split:
            return self.piece(half)
        return self.piece(0).at[:, :, self.columns(half)]

    def spread(self):
        p = self.p
        if self.turned:
            await_bytes(self.out.at[:, p.a, p.b], self.sems.at[0, 1])
        for half in range(2):
            ref = self.placed(half, (p.a, p.b))
            for k in range(1, p.counts[half][1]):
                _, replica = p.peer(half, 1, k)
                remote(
                    self.source(half), ref, self.sems.at[half, 2], self.sems.at[half, 3], replica=replica
                ).start()

    def region(self, half):
        every = pl.ds(0, self.p.counts[half][1])
        return self.placed(half, (every, self.p.b) if half == 0 else (self.p.a, every))

    def spread_bytes(self, half):
        some = pl.ds(0, self.p.counts[half][1] - 1)
        return self.placed(half, (some, 0) if half == 0 else (0, some))

    def widen(self):
        p = self.p
        for half in range(2):
            if not self.turned:
                await_bytes(self.placed(half, (p.a, p.b)), self.sems.at[half, 1])
            await_bytes(self.spread_bytes(half), self.sems.at[half, 3])
            ref = self.region(half)
            for k in range(1, p.counts[half][0]):
                _, replica = p.peer(half, 0, k)
                remote(ref, ref, self.sems.at[half, 4], self.sems.at[half, 5], replica=replica).start()

    def widen_bytes(self, half):
        counts = self.p.counts[half]
        every, some = pl.ds(0, counts[1]), pl.ds(0, counts[0] - 1)
        return self.placed(half, (every, some) if half == 0 else (some, every))

    def finish(self):
        p = self.p
        for half in range(2):
            await_bytes(self.widen_bytes(half), self.sems.at[half, 5])
            await_bytes(self.spread_bytes(half), self.sems.at[half, 2])
            await_bytes(self.widen_bytes(half), self.sems.at[half, 4])
        if self.turned:
            width = self.out.shape[-1] // p.fsdp
            await_bytes(
                self.out.at[:, p.a, p.b, :, pl.ds(0, (p.fsdp - 1) * width)], self.sems.at[0, 0]
            )


def spread_sems():
    return [pltpu.SemaphoreType.DMA((2, 6))]


def norm_back(values, gain_row, gains, grad, carried, result, gain_terms):
    block, model = values.shape
    share = gains.shape[2]
    held = values[...].astype(jnp.float32)
    factor = lax.rsqrt(jnp.mean(held * held, axis=-1, keepdims=True) + eps_norm)
    dots = jnp.zeros((block, 1), jnp.float32)
    for j in range(model // share):
        at = pl.ds(j * share, share)
        normed = values[:, at].astype(jnp.float32) * factor
        product = grad[:, at] * normed
        gain_terms[j, gain_row : gain_row + 1, :] = jnp.sum(product, axis=0, keepdims=True)
        dots += jnp.sum(product * gains[j, gain_row : gain_row + 1, :], axis=-1, keepdims=True)
    dots = dots / model
    for j in range(model // share):
        at = pl.ds(j * share, share)
        normed = values[:, at].astype(jnp.float32) * factor
        scaled = grad[:, at] * gains[j, gain_row : gain_row + 1, :]
        result[:, at] = carried[:, at].astype(jnp.float32) + factor * (scaled - normed * dots)


def weigh_kernel(
    cotangent,
    after_attn,
    gains,
    terms_in,
    lowered_two,
    cotangents,
    hidden_in,
    grad_gate_in,
    grad_up_in,
    grad_after,
    gain_terms,
    branch,
    out_down,
    sum_gate,
    sum_up,
    left_held,
    tokens_held,
    hidden,
    grad_gate,
    grad_up,
    total,
    piece,
    terms,
    across,
    slots,
    summed,
    low,
    load_sems,
    chunk_sems,
    store_sems,
    down_sems,
    *rest,
):
    place = Place()
    chips, block = place.chips, cotangent.shape[0]
    model = cotangent.shape[1]
    tile = 2 * block
    scatter_at, gather_at = rest[:6], rest[6:12]
    gate, up = [reducer(place, rest[12 + 6 * i : 18 + 6 * i]) for i in range(2)]
    down = Spread(place, lambda n: piece, out_down, down_sems, False)
    chunk = tokens_held.shape[1]
    chunks = cotangents.shape[0] // chunk

    def load(t):
        at = pl.ds(t * tile, tile)
        return pltpu.make_async_copy(terms_in.at[at], terms.at[at], load_sems.at[t])

    def load_chunk(i):
        at = pl.ds(i * chunk, chunk)
        return [
            pltpu.make_async_copy(cotangents.at[at], tokens_held.at[i % 2], chunk_sems.at[i % 2, 0]),
            pltpu.make_async_copy(hidden_in.at[at], hidden.at[i % 2], chunk_sems.at[i % 2, 1]),
        ]

    loads = [
        pltpu.make_async_copy(source, target, load_sems.at[chips + i])
        for i, (source, target) in enumerate(
            ((lowered_two, left_held), (grad_gate_in, grad_gate), (grad_up_in, grad_up))
        )
    ]
    for t in range(chips):
        load(t).start()
    for copy in loads + load_chunk(0):
        copy.start()
    place.enter()
    scatter = Scatter(place, terms, across, slots, block, scatter_at)
    for t in range(chips):
        load(t).wait()
        scatter.side(t).start()
    gain_terms[...] = jnp.zeros_like(gain_terms)

    def weigh(reduce, grads):
        share = model // place.fsdp

        def rows(j, _):
            left = left_held[:, pl.ds(pl.multiple_of(j * share, share), share)]
            got = contract_first(left, grads[...]).astype(jnp.bfloat16)
            reduce.part[j] = got.reshape(reduce.part.shape[1:])
            return 0

        for half in range(2):
            lax.fori_loop(half * chips, (half + 1) * chips, rows, 0)
            reduce.start(half)

    loads[0].wait()
    loads[1].wait()
    weigh(gate, grad_gate)
    for t in range(chips):
        scatter.cross(t)
    scatter.step(1)
    loads[2].wait()
    weigh(up, grad_up)
    if chips > 2:
        scatter.step(2)
    for i in range(chunks):
        if i + 1 < chunks:
            for copy in load_chunk(i + 1):
                copy.start()
        for copy in load_chunk(i):
            copy.wait()
        got = contract_first(hidden[i % 2], tokens_held[i % 2])
        if i == 0:
            total[...] = got
        else:
            total[...] += got
    piece[0] = total[...].astype(jnp.bfloat16)
    down.start()
    down.spread()
    for step in range(3, chips):
        scatter.step(step)
    scatter.finish(summed)
    norm_back(after_attn, 1, gains, summed, cotangent, grad_after, gain_terms)
    low[...] = grad_after[...].astype(jnp.bfloat16)
    here = pl.ds(pl.multiple_of(place.me * block, block), block)
    gather = Gather(place, branch, block, gather_at, low)
    gather.start()
    keep = pltpu.make_async_copy(low, branch.at[here], store_sems.at[0])
    keep.start()
    scatter.drain()
    gate.exchange()
    for step in range(1, chips):
        gather.step(step)
        if step == 1:
            up.exchange()
    keep.wait()
    gather.finish()
    stores = []
    for i, (reduce, out) in enumerate(((gate, sum_gate), (up, sum_up))):
        reduce.total()
        for half in range(2):
            store = pltpu.make_async_copy(
                reduce.held(half), out.at[reduce.rows(half)], store_sems.at[1 + 2 * i + half]
            )
            store.start()
            stores.append(store)
    for reduce in (gate, up):
        reduce.drain()
    for half in range(2):
        await_bytes(down.placed(half, (place.a, place.b)), down.sems.at[half, 1])
        await_bytes(down.spread_bytes(half), down.sems.at[half, 2])
        await_bytes(down.spread_bytes(half), down.sems.at[half, 3])
    for store in stores:
        store.wait()


def weigh(cotangent, after_attn, gains, terms, lowered_two, cotangents, hidden, grad_gate, grad_up):
    fsdp, replicas = lax.axis_size("fsdp"), lax.axis_size("replica")
    chips, high, wide = fsdp // 2, 2, replicas // 2
    block, model = cotangent.shape
    rows, columns = grad_gate.shape
    share = gains.shape[2]
    part = columns // replicas
    chunk = min(rows, 1024)
    low, full = jnp.bfloat16, jnp.float32
    hbm, vmem = pl.BlockSpec(memory_space=pl.ANY), pl.BlockSpec(memory_space=pltpu.VMEM)
    shape = jax.ShapeDtypeStruct
    wide_piece = (fsdp, high, wide, share // replicas, columns)
    dma = pltpu.SemaphoreType.DMA
    return pl.pallas_call(
        weigh_kernel,
        in_specs=[vmem] * 3 + [hbm] * 6,
        out_specs=[vmem] * 2 + [hbm] * 4,
        out_shape=[
            shape((block, model), full),
            shape((fsdp, 8, share), full),
            shape((rows, model), low),
            shape((1, high, wide, part, model), low),
            shape((fsdp,) + wide_piece[3:], low),
            shape((fsdp,) + wide_piece[3:], low),
        ],
        scratch_shapes=[
            pltpu.VMEM((rows, model), low),
            pltpu.VMEM((2, chunk, model), low),
            pltpu.VMEM((2, chunk, part), low),
            pltpu.VMEM((rows, columns), low),
            pltpu.VMEM((rows, columns), low),
            pltpu.VMEM((part, model), full),
            pltpu.VMEM((1, part, model), low),
            pltpu.VMEM((rows, model), low),
            pltpu.VMEM((chips * block, model), low),
            pltpu.VMEM((chips + 1, block, model), low),
            pltpu.VMEM((block, model), full),
            pltpu.VMEM((block, model), low),
            dma((chips + 3,)),
            dma((2, 2)),
            dma((5,)),
            dma((2, 6)),
        ]
        + scatter_sems(chips)
        + line_sems(chips)
        + reduce_scratch(*wide_piece)
        + reduce_scratch(*wide_piece),
        compiler_params=pltpu.CompilerParams(
            collective_id=1, has_side_effects=True, vmem_limit_bytes=VMEM_LIMIT
        ),
        name="weigh",
    )(
        cotangent,
        after_attn,
        gains,
        terms,
        lowered_two,
        cotangents.reshape(-1, model),
        hidden.reshape(-1, part),
        grad_gate,
        grad_up,
    )


def back_kernel(
    tokens,
    gains,
    grad_after,
    gain_terms_in,
    after_attn,
    sums,
    half_down,
    sum_gate,
    sum_up,
    branch_in,
    lowered_one,
    slab_qkv,
    w_out,
    queries,
    keys,
    values,
    attended,
    logs,
    cosine,
    sine,
    outputs,
    grad_tokens,
    gain_out,
    out_down,
    out_gate,
    out_up,
    out_qkv,
    out_out,
    terms,
    across,
    slots,
    branch,
    summed,
    grad_low,
    grad_key,
    grad_value,
    grads,
    gain_terms,
    gain_slots,
    gain_sums,
    gain_sems,
    load_sems,
    *rest,
):
    place = Place()
    chips, block = place.chips, tokens.shape[0]
    model, width = tokens.shape[1], queries.shape[1]
    share = gains.shape[2]
    tile = 2 * block
    scatter_at, rest = rest[:6], rest[6:]
    down = Spread(place, None, out_down, rest[0], False)
    held_down = Spread(place, None, half_down, None, False)
    gate = Spread(place, lambda n: sum_gate.at[n], out_gate, rest[1], True)
    up = Spread(place, lambda n: sum_up.at[n], out_up, rest[2], True)
    qkv, out = reducer(place, rest[5:11]), reducer(place, rest[11:17])
    qkv_spread = Spread(place, qkv.piece, out_qkv, rest[3], True)
    out_spread = Spread(place, out.piece, out_out, rest[4], False, split=True)
    load = pltpu.make_async_copy(branch_in, branch, load_sems.at[0])
    load.start()
    place.enter()
    keeps = []
    for half in range(2):
        src, ref = held_down.region(half), down.region(half)
        for k in range(1, place.counts[half][0]):
            _, replica = place.peer(half, 0, k)
            remote(src, ref, down.sems.at[half, 4], down.sems.at[half, 5], replica=replica).start()
        keeps.append(pltpu.make_async_copy(src, ref, down.sems.at[half, 1]))
        keeps[-1].start()
    gate.start()
    up.start()
    load.wait()

    def attend_rows(t, _):
        at = pl.ds(pl.multiple_of(t * tile, tile), tile)
        grad_low[at, :] = contract_last(branch[at, :], w_out[...]).astype(jnp.bfloat16)
        return 0

    lax.fori_loop(0, chips, attend_rows, 0)
    _, high, wide, thin, columns = out.part.shape
    for half in range(2):
        for at in range(0, columns, 512):
            got = contract_first(
                attended[...], branch[:, half * columns + at : half * columns + at + 512]
            ).astype(jnp.bfloat16)
            out.part[half, :, :, :, at : at + 512] = got.reshape(high, wide, thin, 512)
    out.start(0)
    out.start(1)
    reload = pltpu.make_async_copy(lowered_one, branch, load_sems.at[1])
    reload.start()

    scale = HEAD_DIM**-0.5
    grad_key[...] = jnp.zeros_like(grad_key)
    grad_value[...] = jnp.zeros_like(grad_value)
    pair = 2 * HEAD_DIM
    height = tile * 1024 // max(queries.shape[0], 1024)
    for first in range(0, queries.shape[0], height):
        rows, seen = pl.ds(first, height), pl.ds(0, first + height)

        def heads(h, _, first=first, rows=rows, seen=seen):
            lanes = pl.ds(pl.multiple_of(h * pair, pair), pair)
            q2, g2, log2 = queries[rows, lanes], grad_low[rows, lanes], logs[rows, lanes]
            k2, v2 = keys[seen, lanes], values[seen, lanes]
            for_queries, for_keys, for_values = [], [], []
            for at in (0, HEAD_DIM):
                head = slice(at, at + HEAD_DIM)
                q, g, k = q2[:, head], g2[:, head], k2[:, head]
                weights = jnp.exp(scores_of(q, k, first) - log2[:, at : at + 1])
                grad_weights = contract_last(g, v2[:, head])
                delta = jnp.sum(weights * grad_weights, axis=-1, keepdims=True)
                grad_scores = (weights * (grad_weights - delta)).astype(jnp.bfloat16)
                for_queries.append(dot(grad_scores, k))
                for_keys.append(contract_first(grad_scores, q))
                for_values.append(contract_first(weights.astype(jnp.bfloat16), g))
            got = jnp.concatenate(for_queries, axis=1) * scale
            got = got * cosine[rows, :] - partner(got) * sine[rows, :]
            grads[rows, lanes] = got.astype(jnp.bfloat16)
            grad_key[seen, lanes] += jnp.concatenate(for_keys, axis=1) * scale
            grad_value[seen, lanes] += jnp.concatenate(for_values, axis=1)
            return 0

        lax.fori_loop(0, width // pair, heads, 0)

    def turn_back(t, _):
        at = pl.ds(pl.multiple_of(t * tile, tile), tile)
        for j in range(0, width, pair):
            got = grad_key[at, j : j + pair]
            got = got * cosine[at, :] - partner(got) * sine[at, :]
            grads[at, width + j : width + j + pair] = got.astype(jnp.bfloat16)
        grads[at, 2 * width :] = grad_value[at, :].astype(jnp.bfloat16)
        got = contract_last(grads[at, :width], slab_qkv[:model, :])
        got += contract_last(grads[at, width : 2 * width], slab_qkv[model : 2 * model, :])
        got += contract_last(grads[at, 2 * width :], slab_qkv[2 * model :, :])
        terms[at, :] = got.astype(jnp.bfloat16)
        return 0

    lax.fori_loop(0, chips, turn_back, 0)
    scatter = Scatter(place, terms, across, slots, block, scatter_at)
    for t in range(chips):
        scatter.side(t).start()
    reload.wait()

    def weigh_rows(j, _):
        left = branch[:, pl.ds(pl.multiple_of(j * share, share), share)]
        got = contract_first(left, grads[...]).astype(jnp.bfloat16)
        qkv.part[j] = got.reshape(qkv.part.shape[1:])
        return 0

    for half in range(2):
        lax.fori_loop(half * chips, (half + 1) * chips, weigh_rows, 0)
        qkv.start(half)
    gate.spread()
    for t in range(chips):
        scatter.cross(t)
    for step in range(1, chips):
        scatter.step(step)
        if step == 1:
            out.exchange()
            up.spread()
        if step == max(chips - 2, 1):
            qkv.exchange()
    gate.widen()
    out.total()
    out_spread.start()
    out_spread.spread()
    scatter.finish(summed)
    gain_terms[...] = gain_terms_in[...]
    norm_back(tokens, 0, gains, summed, grad_after, grad_tokens, gain_terms)

    def send_gain(k, _):
        to = lax.rem(place.me + k, place.fsdp)
        remote(
            gain_terms.at[to], gain_slots.at[place.me], gain_sems.at[0], gain_sems.at[1], fsdp=to
        ).start()
        return 0

    lax.fori_loop(1, place.fsdp, send_gain, 0)
    gain_slots[place.me] = gain_terms[place.me]
    scatter.drain()
    load_sums = pltpu.make_async_copy(sums, terms, load_sems.at[0])
    load_sums.start()
    qkv.total()
    qkv_spread.start()
    await_bytes(gain_slots.at[pl.ds(0, place.fsdp - 1)], gain_sems.at[1])
    gain_sums[place.replica] = jnp.sum(gain_slots[...], axis=0)

    def send_sum(k, _):
        ref = gain_sums.at[place.replica]
        to = lax.rem(place.replica + k, place.replicas)
        remote(ref, ref, gain_sems.at[2], gain_sems.at[3], replica=to).start()
        return 0

    lax.fori_loop(1, place.replicas, send_sum, 0)

    load_sums.wait()
    for t in range(chips):
        scatter.side(t).start()
    up.widen()
    for t in range(chips):
        scatter.cross(t)
    scatter.step(1)
    qkv_spread.spread()
    for step in range(2, chips):
        scatter.step(step)
        if step == 2:
            out_spread.widen()
    if chips == 2:
        out_spread.widen()
    scatter.finish(summed)
    outputs[...] = (summed[...] + after_attn[...]).astype(outputs.dtype)
    qkv_spread.widen()
    await_bytes(gain_sums.at[pl.ds(0, place.replicas - 1)], gain_sems.at[3])
    gain_out[...] = jnp.sum(gain_sums[...], axis=0)
    await_bytes(gain_slots.at[pl.ds(0, place.fsdp - 1)], gain_sems.at[0])
    await_bytes(gain_sums.at[pl.ds(0, place.replicas - 1)], gain_sems.at[2])
    scatter.drain()
    qkv.drain()
    out.drain()
    for half in range(2):
        await_bytes(down.widen_bytes(half), down.sems.at[half, 5])
        await_bytes(down.widen_bytes(half), down.sems.at[half, 4])
        keeps[half].wait()
    for spread in (gate, up, out_spread, qkv_spread):
        spread.finish()


def back(
    tokens,
    gains,
    grad_after,
    gain_terms,
    after_attn,
    sums,
    half_down,
    sum_gate,
    sum_up,
    branch,
    lowered_one,
    slab_qkv,
    w_out,
    queries,
    keys,
    values,
    attended,
    logs,
    cosine,
    sine,
):
    fsdp, replicas = lax.axis_size("fsdp"), lax.axis_size("replica")
    chips, high, wide = fsdp // 2, 2, replicas // 2
    block, model = tokens.shape
    rows, width = queries.shape
    share = gains.shape[2]
    low, full = jnp.bfloat16, jnp.float32
    hbm, vmem = pl.BlockSpec(memory_space=pl.ANY), pl.BlockSpec(memory_space=pltpu.VMEM)
    shape = jax.ShapeDtypeStruct
    thin = share // replicas
    columns = sum_gate.shape[-1]
    qkv_piece = (fsdp, high, wide, thin, 3 * width)
    out_piece = (2, high, wide, width // replicas, model // 2)
    dma = pltpu.SemaphoreType.DMA
    return pl.pallas_call(
        back_kernel,
        in_specs=[vmem] * 5 + [hbm] * 6 + [vmem] * 9,
        out_specs=[vmem] * 3 + [hbm] * 5,
        out_shape=[
            shape((block, model), low),
            shape((block, model), full),
            shape((8, share), full),
            shape(half_down.shape, low),
            shape((1, high, wide, thin, fsdp * columns), low),
            shape((1, high, wide, thin, fsdp * columns), low),
            shape((3, high, wide, thin, fsdp * width), low),
            shape(out_piece, low),
        ],
        scratch_shapes=[
            pltpu.VMEM((rows, model), low),
            pltpu.VMEM((chips * block, model), low),
            pltpu.VMEM((chips + 1, block, model), low),
            pltpu.VMEM((rows, model), low),
            pltpu.VMEM((block, model), full),
            pltpu.VMEM((rows, width), low),
            pltpu.VMEM((rows, width), full),
            pltpu.VMEM((rows, width), full),
            pltpu.VMEM((rows, 3 * width), low),
            pltpu.VMEM((fsdp, 8, share), full),
            pltpu.VMEM((fsdp, 8, share), full),
            pltpu.VMEM((replicas, 8, share), full),
            dma((4,)),
            dma((2,)),
        ]
        + scatter_sems(chips)
        + spread_sems() * 5
        + reduce_scratch(*qkv_piece)
        + reduce_scratch(*out_piece),
        compiler_params=pltpu.CompilerParams(
            collective_id=2, has_side_effects=True, vmem_limit_bytes=VMEM_LIMIT
        ),
        name="back",
    )(
        tokens,
        gains,
        grad_after,
        gain_terms,
        after_attn,
        sums,
        half_down,
        sum_gate,
        sum_up,
        branch,
        lowered_one,
        slab_qkv,
        w_out,
        queries,
        keys,
        values,
        attended,
        logs,
        cosine,
        sine,
    )


def widen_kernel(down, gate, up, qkv, out, w_down, w_gate, w_up, w_query, w_key, w_value, w_out):
    w_down[...] = down[...].astype(jnp.float32)
    w_gate[...] = gate[...].astype(jnp.float32)
    w_up[...] = up[...].astype(jnp.float32)
    for i, ref in enumerate((w_query, w_key, w_value)):
        ref[...] = qkv[i].astype(jnp.float32)
    half = out.shape[2]
    for i in range(2):
        w_out[:, i * half : (i + 1) * half] = out[i].astype(jnp.float32)


def widen(down, gate, up, qkv, out):
    steps = 8
    full = jnp.float32

    def rows(array):
        return pl.BlockSpec((array.shape[0] // steps, array.shape[1]), lambda i: (i, 0))

    def stacked(array):
        return pl.BlockSpec((array.shape[0], array.shape[1] // steps, array.shape[2]), lambda i: (0, i, 0))

    like = [down, gate, up, qkv[0], qkv[0], qkv[0]]
    shapes = [jax.ShapeDtypeStruct(array.shape, full) for array in like]
    shapes.append(jax.ShapeDtypeStruct((out.shape[1], 2 * out.shape[2]), full))
    return pl.pallas_call(
        widen_kernel,
        grid=(steps,),
        in_specs=[rows(down), rows(gate), rows(up), stacked(qkv), stacked(out)],
        out_specs=[rows(shape) for shape in shapes],
        out_shape=shapes,
        compiler_params=pltpu.CompilerParams(vmem_limit_bytes=VMEM_LIMIT),
        name="widen",
    )(down, gate, up, qkv, out)


def local(
    tokens, attn_gain, w_query, w_key, w_value, w_out, ffn_gain, w_gate, w_up, w_down, cotangent
):
    cosine, sine = rope_tables(tokens.shape[0] * lax.axis_size("fsdp"))
    (
        lowered_one,
        lowered_two,
        cotangents,
        slab_qkv,
        hidden,
        grad_gate,
        grad_up,
        terms,
        sums,
        queries,
        keys,
        values,
        attended,
        logs,
        after_attn,
        gains,
    ) = front(
        tokens,
        cotangent,
        attn_gain,
        ffn_gain,
        w_query,
        w_key,
        w_value,
        w_out,
        w_gate,
        w_up,
        w_down,
        cosine,
        sine,
    )
    grad_after, gain_terms, branch, half_down, sum_gate, sum_up = weigh(
        cotangent, after_attn, gains, terms, lowered_two, cotangents, hidden, grad_gate, grad_up
    )
    outputs, grad_tokens, gain_grads, low_down, low_gate, low_up, low_qkv, low_out = back(
        tokens,
        gains,
        grad_after,
        gain_terms,
        after_attn,
        sums,
        half_down,
        sum_gate,
        sum_up,
        branch,
        lowered_one,
        slab_qkv,
        w_out,
        queries,
        keys,
        values,
        attended,
        logs,
        cosine,
        sine,
    )
    grad_w_down, grad_w_gate, grad_w_up, grad_w_query, grad_w_key, grad_w_value, grad_w_out = widen(
        low_down.reshape(w_down.shape),
        low_gate.reshape(w_gate.shape),
        low_up.reshape(w_up.shape),
        low_qkv.reshape((3,) + w_query.shape),
        low_out.reshape(2, w_out.shape[0], -1),
    )
    return (
        outputs,
        grad_tokens,
        gain_grads[0],
        grad_w_query,
        grad_w_key,
        grad_w_value,
        grad_w_out,
        gain_grads[1],
        grad_w_gate,
        grad_w_up,
        grad_w_down,
    )


def solution(mesh):
    rows = P("fsdp", None)
    tokens = P(("replica", "fsdp"), None)
    gain = P("fsdp")
    return jax.shard_map(
        local,
        mesh=mesh,
        in_specs=(tokens, gain, rows, rows, rows, rows, gain, rows, rows, rows, tokens),
        out_specs=(tokens, tokens, gain, rows, rows, rows, rows, gain, rows, rows, rows),
        check_vma=False,
    )
```

```python
import functools

import jax
import jax.numpy as jnp
import numpy as np
from jax import lax
from jax.experimental import pallas as pl
from jax.experimental.pallas import tpu as pltpu
from jax.sharding import PartitionSpec as P

HEAD_DIM = 64

eps_norm = 1e-05
rope_base = 130000.0
masked_score = -1e30


def rope_tables(row_count):
    lane = np.arange(2 * HEAD_DIM) % HEAD_DIM
    halfway = HEAD_DIM // 2
    spacing = ((lane % halfway) * np.float32(2.0) / HEAD_DIM).astype(np.float32)
    frequency = np.power(np.float32(rope_base), -spacing)
    angles = np.arange(row_count, dtype=np.float32)[:, None] * frequency[None, :]
    sign = np.where(lane < halfway, -1.0, 1.0).astype(np.float32)
    return np.cos(angles).astype(np.float32), (np.sin(angles) * sign[None, :]).astype(np.float32)


def dot(left, right):
    return jnp.dot(left, right, preferred_element_type=jnp.float32)


def contract_last(left, right):
    return lax.dot_general(
        left, right, (((1,), (1,)), ((), ())), preferred_element_type=jnp.float32
    )


def contract_first(left, right):
    return lax.dot_general(
        left, right, (((0,), (0,)), ((), ())), preferred_element_type=jnp.float32
    )


def scores_of(queries, keys, first_row):
    rows, columns = queries.shape[0], keys.shape[0]
    scores = contract_last(queries, keys) * HEAD_DIM**-0.5
    at_row = lax.broadcasted_iota(jnp.int32, (rows, columns), 0) + first_row
    at_column = lax.broadcasted_iota(jnp.int32, (rows, columns), 1)
    return jnp.where(at_column <= at_row, scores, masked_score)


MESH = pl.DeviceIdType.MESH
VMEM_LIMIT = 60 * 2**20


def remote(src, dst, send, recv, **where):
    return pltpu.make_async_remote_copy(
        src_ref=src, dst_ref=dst, send_sem=send, recv_sem=recv, device_id=where, device_id_type=MESH
    )


def await_bytes(ref, sem):
    pltpu.make_async_copy(ref, ref, sem).wait()


def rows_at(ref, index, size):
    return ref.at[pl.ds(pl.multiple_of(index * size, size), size)]


class Place:
    def __init__(self):
        self.fsdp, self.replicas = lax.axis_size("fsdp"), lax.axis_size("replica")
        self.me, self.replica = lax.axis_index("fsdp"), lax.axis_index("replica")
        self.chips = self.fsdp // 2
        self.chip, self.core = self.me // 2, self.me % 2
        self.sibling = self.me + 1 - 2 * self.core
        self.high, self.wide = 2, self.replicas // 2
        self.a, self.b = self.replica // self.wide, self.replica % self.wide
        self.counts = ((self.wide, self.high), (self.high, self.wide))
        self.above = self.chip + 1 < self.chips
        self.below = self.chip >= 1

    def peer(self, half, stage, k):
        if half == stage:
            to = lax.rem(self.b + k, self.wide)
            return to, self.a * self.wide + to
        to = lax.rem(self.a + k, self.high)
        return to, to * self.wide + self.b

    def nearest(self, k):
        found = jnp.int32(0)
        for chip in range(self.chips):
            order = sorted(range(self.chips), key=lambda other, chip=chip: (abs(other - chip), other))
            found = found + jnp.where(self.chip == chip, order[k], 0)
        return found

    def enter(self):
        barrier = pltpu.get_barrier_semaphore()

        def greet(k, _):
            to = lax.rem(self.me + k, self.fsdp)
            pl.semaphore_signal(barrier, inc=1, device_id={"fsdp": to}, device_id_type=MESH)
            return 0

        def greet_replica(k, _):
            to = lax.rem(self.replica + k, self.replicas)
            pl.semaphore_signal(barrier, inc=1, device_id={"replica": to}, device_id_type=MESH)
            return 0

        lax.fori_loop(1, self.fsdp, greet, 0)
        lax.fori_loop(1, self.replicas, greet_replica, 0)
        pl.semaphore_wait(barrier, self.fsdp - 1 + self.replicas - 1)


def line_sems(chips):
    return [pltpu.SemaphoreType.DMA((chips,))] * 6


class Gather:
    def __init__(self, place, buf, block, sems, own=None):
        self.p, self.buf, self.block, self.own = place, buf, block, own
        self.up_out, self.up_in, self.down_out, self.down_in, self.side_out, self.side_in = sems

    def held(self, chip):
        return rows_at(self.buf, 2 * chip + self.p.core, self.block)

    def up(self, step):
        ref = self.held(self.p.chip - step + 1)
        src = self.own if step == 1 and self.own is not None else ref
        return remote(src, ref, self.up_out.at[step], self.up_in.at[step], fsdp=self.p.me + 2)

    def down(self, step):
        ref = self.held(self.p.chip + step - 1)
        src = self.own if step == 1 and self.own is not None else ref
        return remote(src, ref, self.down_out.at[step], self.down_in.at[step], fsdp=self.p.me - 2)

    def side(self, chip, src=None):
        ref = self.held(chip)
        src = ref if src is None else src
        return remote(src, ref, self.side_out.at[chip], self.side_in.at[chip], fsdp=self.p.sibling)

    def start(self):
        p = self.p
        pl.when(p.above)(lambda: self.up(1).start())
        pl.when(p.below)(lambda: self.down(1).start())
        self.side(p.chip, self.own).start()

    def step(self, step):
        p = self.p
        from_below, from_above = p.chip - step, p.chip + step

        @pl.when(from_below >= 0)
        def _():
            await_bytes(self.held(from_below), self.up_in.at[step])
            if step + 1 < p.chips:
                pl.when(p.above)(lambda: self.up(step + 1).start())
            self.side(from_below).start()

        @pl.when(from_above < p.chips)
        def _():
            await_bytes(self.held(from_above), self.down_in.at[step])
            if step + 1 < p.chips:
                pl.when(p.below)(lambda: self.down(step + 1).start())
            self.side(from_above).start()

    def across(self, chip):
        await_bytes(rows_at(self.buf, 2 * chip + 1 - self.p.core, self.block), self.side_in.at[chip])

    def drain(self):
        p = self.p
        for step in range(1, p.chips):
            pl.when(jnp.logical_and(p.above, p.chip - step + 1 >= 0))(
                lambda step=step: self.up(step).wait_send()
            )
            pl.when(jnp.logical_and(p.below, p.chip + step - 1 < p.chips))(
                lambda step=step: self.down(step).wait_send()
            )
        for chip in range(p.chips):
            self.side(chip).wait_send()

    def finish(self):
        for chip in range(self.p.chips):
            self.across(chip)
        self.drain()


class Scatter:
    def __init__(self, place, terms, across, slots, block, sems):
        self.p, self.terms, self.across, self.slots, self.block = place, terms, across, slots, block
        self.up_out, self.up_in, self.down_out, self.down_in, self.side_out, self.side_in = sems

    def side(self, chip):
        p = self.p
        return remote(
            rows_at(self.terms, 2 * chip + 1 - p.core, self.block),
            rows_at(self.across, chip, self.block),
            self.side_out.at[chip],
            self.side_in.at[chip],
            fsdp=p.sibling,
        )

    def term(self, chip):
        return rows_at(self.terms, 2 * chip + self.p.core, self.block)

    def up(self, step):
        return remote(
            self.term(self.p.chips - step + self.p.chip),
            self.slots.at[step - self.p.chip - 1],
            self.up_out.at[step],
            self.up_in.at[step],
            fsdp=self.p.me + 2,
        )

    def down(self, step):
        return remote(
            self.term(self.p.chip - self.p.chips + step),
            self.slots.at[step + 1],
            self.down_out.at[step],
            self.down_in.at[step],
            fsdp=self.p.me - 2,
        )

    def add(self, chip, arrived):
        term = self.term(chip)
        term[...] = (term[...].astype(jnp.float32) + arrived[...].astype(jnp.float32)).astype(term.dtype)

    def cross(self, chip):
        arrived = rows_at(self.across, chip, self.block)
        await_bytes(arrived, self.side_in.at[chip])
        self.add(chip, arrived)

    def step(self, step):
        p = self.p
        rising, falling = p.chips - step + p.chip, p.chip - p.chips + step

        @pl.when(jnp.logical_and(p.above, rising < p.chips))
        def _():
            if step > 1:

                @pl.when(p.below)
                def _():
                    arrived = self.slots.at[step - 1 - p.chip]
                    await_bytes(arrived, self.up_in.at[step - 1])
                    self.add(rising, arrived)

            self.up(step).start()

        @pl.when(jnp.logical_and(p.below, falling >= 0))
        def _():
            if step > 1:

                @pl.when(p.above)
                def _():
                    arrived = self.slots.at[step]
                    await_bytes(arrived, self.down_in.at[step - 1])
                    self.add(falling, arrived)

            self.down(step).start()

    def finish(self, total):
        p, last = self.p, self.p.chips - 1
        total[...] = self.term(p.chip)[...].astype(jnp.float32)

        @pl.when(p.below)
        def _():
            await_bytes(self.slots.at[last - p.chip], self.up_in.at[last])
            total[...] += self.slots[last - p.chip].astype(jnp.float32)

        @pl.when(p.above)
        def _():
            await_bytes(self.slots.at[last + 1], self.down_in.at[last])
            total[...] += self.slots[last + 1].astype(jnp.float32)

    def drain(self):
        p = self.p
        for step in range(1, p.chips):
            pl.when(jnp.logical_and(p.above, p.chips - step + p.chip < p.chips))(
                lambda step=step: self.up(step).wait_send()
            )
            pl.when(jnp.logical_and(p.below, p.chip - p.chips + step >= 0))(
                lambda step=step: self.down(step).wait_send()
            )
        for chip in range(p.chips):
            self.side(chip).wait_send()


def scatter_sems(chips):
    dma = pltpu.SemaphoreType.DMA
    return [dma((chips,))] * 6


class Turn:
    def __init__(self, place, weight, slab, first, sems):
        self.p, self.weight, self.slab, self.first = place, weight, slab, first
        self.far_out, self.far_in, self.near_out, self.near_in, self.own, self.passing = sems
        self.height, self.width = weight.shape[0], slab.shape[1]
        self.share = self.height // place.replicas

    def far_rows(self):
        return (self.p.fsdp - 2) * self.share

    def piece(self, block, share):
        at = self.first + block * self.height + share * self.share
        return self.slab.at[pl.ds(pl.multiple_of(at, self.share), self.share)]

    def whole(self, block):
        at = self.first + block * self.height
        return self.slab.at[pl.ds(pl.multiple_of(at, self.height), self.height)]

    def columns(self, to):
        return pl.ds(pl.multiple_of(to * self.width, self.width), self.width)

    def start(self):
        p = self.p

        def send(k, _):
            to = lax.rem(2 * p.chip + 2 + k, p.fsdp)
            share = pl.ds(pl.multiple_of(p.replica * self.share, self.share), self.share)
            remote(
                self.weight.at[share, self.columns(to)],
                self.piece(p.me, p.replica),
                self.far_out,
                self.far_in,
                fsdp=to,
            ).start()
            return 0

        lax.fori_loop(0, p.fsdp - 2, send, 0)
        self.near().start()
        self.mine().start()

    def near(self):
        p = self.p
        return remote(
            self.weight.at[:, self.columns(p.sibling)], self.whole(p.me), self.near_out, self.near_in, fsdp=p.sibling
        )

    def mine(self):
        return pltpu.make_async_copy(self.weight.at[:, self.columns(self.p.me)], self.whole(self.p.me), self.own)

    def await_far(self):
        await_bytes(self.slab.at[pl.ds(0, self.far_rows())], self.far_in)

    def bytes_of(self, pieces):
        return self.slab.at[pl.ds(0, pieces * self.share)]

    def pass_bytes(self, half, stage):
        first, second = self.p.counts[half]
        return self.bytes_of((self.p.chips - 1) * (second - 1 if stage == 0 else second * (first - 1)))

    def send_pieces(self, half, stage, shares):
        p = self.p

        def one(i, _):
            block = lax.rem(2 * p.chip + 2 + 2 * i + half, p.fsdp)
            for share in shares:
                ref = self.piece(block, share)
                for k in range(1, p.counts[half][1 - stage]):
                    _, replica = p.peer(half, 1 - stage, k)
                    remote(
                        ref,
                        ref,
                        self.passing.at[half, 2 * stage],
                        self.passing.at[half, 2 * stage + 1],
                        replica=replica,
                    ).start()
            return 0

        lax.fori_loop(0, p.chips - 1, one, 0)

    def pass_on(self):
        for half in range(2):
            self.send_pieces(half, 0, [self.p.replica])

    def pass_far(self):
        p = self.p
        for half in range(2):
            await_bytes(self.pass_bytes(half, 0), self.passing.at[half, 1])
            if half == 0:
                shares = [a * p.wide + p.b for a in range(p.high)]
            else:
                shares = [p.a * p.wide + b for b in range(p.wide)]
            self.send_pieces(half, 1, shares)

    def finish(self):
        for half in range(2):
            await_bytes(self.pass_bytes(half, 1), self.passing.at[half, 3])
        await_bytes(self.whole(self.p.sibling), self.near_in)
        self.mine().wait()

    def drain(self):
        await_bytes(self.slab.at[pl.ds(0, self.far_rows())], self.far_out)
        self.near().wait_send()
        for half in range(2):
            await_bytes(self.pass_bytes(half, 0), self.passing.at[half, 0])
            await_bytes(self.pass_bytes(half, 1), self.passing.at[half, 2])


def turn_sems():
    return [pltpu.SemaphoreType.DMA(())] * 5 + [pltpu.SemaphoreType.DMA((2, 4))]


def partner(values):
    halfway = HEAD_DIM // 2
    width = values.shape[1]
    lane = lax.broadcasted_iota(jnp.int32, values.shape, 1) % HEAD_DIM
    return jnp.where(
        lane < halfway,
        pltpu.roll(values, width - halfway, axis=1),
        pltpu.roll(values, halfway, axis=1),
    )


def front_kernel(
    tokens,
    cotangent,
    gain_one,
    gain_two,
    w_query,
    w_key,
    w_value,
    w_out,
    w_gate,
    w_up,
    w_down,
    cosine,
    sine,
    lowered_one,
    lowered_two_out,
    cotangents,
    slab_qkv_out,
    hidden_out,
    grad_gate_out,
    grad_up_out,
    terms_out,
    sums_out,
    queries,
    keys,
    values,
    attended,
    logs,
    after_attn,
    gains,
    low,
    tiles,
    lowered_two,
    slab_qkv,
    slab_gate,
    slab_up,
    held_down,
    terms,
    across,
    slots,
    tile_hidden,
    tile_gate,
    tile_up,
    tile_terms,
    tile_sums,
    gain_rows,
    gain_out,
    gain_in,
    copy_sems,
    load_sems,
    store_sems,
    *sems,
):
    place = Place()
    chips, block = place.chips, tokens.shape[0]
    model, width = tokens.shape[1], queries.shape[1]
    share = gain_one.shape[0]
    tile = 2 * block
    one_at, cot_at, two_at, scatter_at = sems[:6], sems[6:12], sems[12:18], sems[18:24]
    turn_at = [sems[24 + 6 * i : 30 + 6 * i] for i in range(5)]
    turns = [
        Turn(place, weight, slab_qkv, i * model, turn_at[i])
        for i, weight in enumerate((w_query, w_key, w_value))
    ]
    turn_gate = Turn(place, w_gate, slab_gate, 0, turn_at[3])
    turn_up = Turn(place, w_up, slab_up, 0, turn_at[4])
    here = pl.ds(pl.multiple_of(place.me * block, block), block)

    gain_rows[...] = jnp.zeros_like(gain_rows)
    gain_rows[0, :] = gain_one[...].astype(jnp.float32)
    gain_rows[1, :] = gain_two[...].astype(jnp.float32)
    load_down = pltpu.make_async_copy(w_down, held_down, copy_sems.at[0])
    load_down.start()
    keep_cot = pltpu.make_async_copy(cotangent, cotangents.at[here], copy_sems.at[1])
    keep_cot.start()
    place.enter()

    def send_gains(k, _):
        to = lax.rem(place.me + k, place.fsdp)
        remote(gain_rows, gains.at[place.me], gain_out, gain_in, fsdp=to).start()
        return 0

    lax.fori_loop(1, place.fsdp, send_gains, 0)
    for turn in turns:
        turn.start()
    gains[place.me] = gain_rows[...]
    inputs = tokens[...].astype(jnp.float32)
    factor = lax.rsqrt(jnp.mean(inputs * inputs, axis=-1, keepdims=True) + eps_norm)
    await_bytes(gains.at[pl.ds(0, place.fsdp - 1)], gain_in)
    for j in range(model // share):
        at = pl.ds(j * share, share)
        normed = tokens[:, at].astype(jnp.float32) * factor
        low[:, at] = (normed * gains[j, 0:1, :]).astype(jnp.bfloat16)
    first = Gather(place, lowered_one, block, one_at, low)
    first.start()
    keep_low = pltpu.make_async_copy(low, lowered_one.at[here], copy_sems.at[2])
    keep_low.start()
    for turn in turns:
        turn.await_far()
        turn.pass_on()
    for step in range(1, chips):
        if step == chips - 1:
            turn_gate.start()
        first.step(step)
        if step == 1:
            for turn in turns:
                turn.pass_far()
    turn_up.start()
    third = Gather(place, cotangents, block, cot_at, cotangent)
    third.start()
    keep_low.wait()
    first.finish()

    def load(source, t, slot):
        return pltpu.make_async_copy(rows_at(source, t, tile), tiles.at[slot], load_sems.at[slot])

    load(lowered_one, 0, 0).start()
    for turn in turns:
        turn.finish()
    keep_slab = pltpu.make_async_copy(slab_qkv, slab_qkv_out, copy_sems.at[3])
    keep_slab.start()
    for t in range(chips):
        if t + 1 < chips:
            load(lowered_one, t + 1, (t + 1) % 2).start()
        load(lowered_one, t, t % 2).wait()
        at = pl.ds(t * tile, tile)
        for i, ref in enumerate((queries, keys, values)):
            out = dot(tiles[t % 2], slab_qkv[i * model : (i + 1) * model, :])
            if i < 2:
                for j in range(0, width, 2 * HEAD_DIM):
                    pair = out[:, j : j + 2 * HEAD_DIM]
                    pair = pair * cosine[at, :] + partner(pair) * sine[at, :]
                    ref[at, j : j + 2 * HEAD_DIM] = pair.astype(jnp.bfloat16)
            else:
                ref[at, :] = out.astype(jnp.bfloat16)
    scatter = Scatter(place, terms, across, slots, block, scatter_at)
    pair = 2 * HEAD_DIM
    for t in range(chips):
        here_t, seen = pl.ds(t * tile, tile), pl.ds(0, (t + 1) * tile)

        def heads(h, _, t=t, here_t=here_t, seen=seen):
            lanes = pl.ds(pl.multiple_of(h * pair, pair), pair)
            q2, k2, v2 = queries[here_t, lanes], keys[seen, lanes], values[seen, lanes]
            mixed, stats = [], []
            for at in (0, HEAD_DIM):
                head = slice(at, at + HEAD_DIM)
                scores = scores_of(q2[:, head], k2[:, head], t * tile)
                most = jnp.max(scores, axis=-1, keepdims=True)
                weights = jnp.exp(scores - most)
                total = jnp.sum(weights, axis=-1, keepdims=True)
                mixed.append(dot((weights / total).astype(jnp.bfloat16), v2[:, head]))
                stats.append(jnp.broadcast_to(most + jnp.log(total), (tile, HEAD_DIM)))
            attended[here_t, lanes] = jnp.concatenate(mixed, axis=1).astype(jnp.bfloat16)
            logs[here_t, lanes] = jnp.concatenate(stats, axis=1)
            return 0

        lax.fori_loop(0, width // pair, heads, 0)
        terms[here_t, :] = dot(attended[here_t, :], w_out[...]).astype(jnp.bfloat16)
        scatter.side(t).start()
    turn_gate.await_far()
    turn_gate.pass_on()
    for t in range(chips):
        scatter.cross(t)
    for step in range(1, chips):
        scatter.step(step)
        if step == 1:
            turn_gate.pass_far()
            turn_up.await_far()
            turn_up.pass_on()
        if step < chips - 1:
            third.step(step)
        if step == max(chips - 2, 1):
            turn_up.pass_far()
    scatter.finish(after_attn)
    after_attn[...] += tokens[...].astype(jnp.float32)
    after = after_attn[...]
    factor = lax.rsqrt(jnp.mean(after * after, axis=-1, keepdims=True) + eps_norm)
    for j in range(model // share):
        at = pl.ds(j * share, share)
        normed = after_attn[:, at] * factor
        lowered_two[here, at] = (normed * gains[j, 1:2, :]).astype(jnp.bfloat16)
    second = Gather(place, lowered_two, block, two_at)
    second.start()
    third.step(chips - 1)
    keep_cot.wait()
    third.finish()
    load(cotangents, place.nearest(0), 0).start()
    turn_gate.finish()
    turn_up.finish()
    load_down.wait()

    def stores(k, t):
        slot = k % 2
        pairs = (
            (tile_hidden, hidden_out),
            (tile_gate, grad_gate_out),
            (tile_up, grad_up_out),
            (tile_terms, terms_out),
            (tile_sums, sums_out),
        )
        return [
            pltpu.make_async_copy(held.at[slot], rows_at(out, t, tile), store_sems.at[i, slot])
            for i, (held, out) in enumerate(pairs)
        ]

    for k in range(chips):
        t, slot = place.nearest(k), k % 2
        if k > 0:
            second.step(k)
        second.across(t)
        if k + 1 < chips:
            load(cotangents, place.nearest(k + 1), (k + 1) % 2).start()
        load(cotangents, t, slot).wait()
        if k > 1:
            for store in stores(k - 2, place.nearest(k - 2)):
                store.wait()
        rows = lowered_two[pl.ds(pl.multiple_of(t * tile, tile), tile), :]
        gate = dot(rows, slab_gate[...])
        up = dot(rows, slab_up[...])
        grad_hidden = contract_last(tiles[slot], held_down[...])
        sigmoid = jax.nn.sigmoid(gate)
        silu = gate * sigmoid
        hidden = (silu * up).astype(jnp.bfloat16)
        grad_gate = (grad_hidden * up * sigmoid * (1.0 + gate * (1.0 - sigmoid))).astype(jnp.bfloat16)
        grad_up = (grad_hidden * silu).astype(jnp.bfloat16)
        tile_hidden[slot] = hidden
        tile_gate[slot] = grad_gate
        tile_up[slot] = grad_up
        got = contract_last(grad_gate, slab_gate[...]) + contract_last(grad_up, slab_up[...])
        tile_terms[slot] = got.astype(jnp.bfloat16)
        tile_sums[slot] = dot(hidden, held_down[...]).astype(jnp.bfloat16)
        for store in stores(k, t):
            store.start()
    keep_two = pltpu.make_async_copy(lowered_two, lowered_two_out, copy_sems.at[4])
    keep_two.start()
    second.drain()
    scatter.drain()
    for turn in turns + [turn_gate, turn_up]:
        turn.drain()
    await_bytes(gains.at[pl.ds(0, place.fsdp - 1)], gain_out)
    keep_slab.wait()
    for k in range(max(chips - 2, 0), chips):
        for store in stores(k, place.nearest(k)):
            store.wait()
    keep_two.wait()


def front(
    tokens, cotangent, gain_one, gain_two, w_query, w_key, w_value, w_out, w_gate, w_up, w_down, cosine, sine
):
    fsdp = lax.axis_size("fsdp")
    chips = fsdp // 2
    block, model = tokens.shape
    rows, width, wide = fsdp * block, w_query.shape[1] // fsdp, w_gate.shape[1] // fsdp
    tile = 2 * block
    share = gain_one.shape[0]
    low, full = jnp.bfloat16, jnp.float32
    hbm, vmem = pl.BlockSpec(memory_space=pl.ANY), pl.BlockSpec(memory_space=pltpu.VMEM)
    shape = jax.ShapeDtypeStruct
    dma = pltpu.SemaphoreType.DMA
    return pl.pallas_call(
        front_kernel,
        in_specs=[vmem] * 4 + [hbm] * 3 + [vmem] + [hbm] * 3 + [vmem] * 2,
        out_specs=[hbm] * 9 + [vmem] * 7,
        out_shape=[
            shape((rows, model), low),
            shape((rows, model), low),
            shape((rows, model), low),
            shape((3 * model, width), low),
            shape((rows, wide), low),
            shape((rows, wide), low),
            shape((rows, wide), low),
            shape((rows, model), low),
            shape((rows, model), low),
            shape((rows, width), low),
            shape((rows, width), low),
            shape((rows, width), low),
            shape((rows, width), low),
            shape((rows, width), full),
            shape((block, model), full),
            shape((fsdp, 8, share), full),
        ],
        scratch_shapes=[
            pltpu.VMEM((block, model), low),
            pltpu.VMEM((2, tile, model), low),
            pltpu.VMEM((rows, model), low),
            pltpu.VMEM((3 * model, width), low),
            pltpu.VMEM((model, wide), low),
            pltpu.VMEM((model, wide), low),
            pltpu.VMEM((wide, model), low),
            pltpu.VMEM((rows, model), low),
            pltpu.VMEM((chips * block, model), low),
            pltpu.VMEM((chips + 1, block, model), low),
            pltpu.VMEM((2, tile, wide), low),
            pltpu.VMEM((2, tile, wide), low),
            pltpu.VMEM((2, tile, wide), low),
            pltpu.VMEM((2, tile, model), low),
            pltpu.VMEM((2, tile, model), low),
            pltpu.VMEM((8, share), full),
            dma(()),
            dma(()),
            dma((5,)),
            dma((2,)),
            dma((5, 2)),
        ]
        + line_sems(chips) * 3
        + scatter_sems(chips)
        + turn_sems() * 5,
        compiler_params=pltpu.CompilerParams(
            collective_id=0, has_side_effects=True, vmem_limit_bytes=VMEM_LIMIT
        ),
        name="front",
    )(
        tokens,
        cotangent,
        gain_one,
        gain_two,
        w_query,
        w_key,
        w_value,
        w_out,
        w_gate,
        w_up,
        w_down,
        cosine,
        sine,
    )


class Reduce:
    def __init__(self, place, part, first, second, sems):
        self.p, self.part, self.first, self.second, self.sems = place, part, first, second, sems
        self.half = part.shape[0] // 2

    def rows(self, half):
        return pl.ds(half * self.half, self.half)

    def sent(self, half, to):
        if half == 0:
            return self.part.at[self.rows(0), :, to]
        return self.part.at[self.rows(1), to]

    def own(self, half):
        return self.sent(half, self.p.b if half == 0 else self.p.a)

    def start(self, half):
        for k in range(1, self.p.counts[half][0]):
            to, replica = self.p.peer(half, 0, k)
            remote(
                self.sent(half, to),
                self.first[half].at[k - 1],
                self.sems.at[half, 0],
                self.sems.at[half, 1],
                replica=replica,
            ).start()

    def exchange(self):
        for half in range(2):
            own, arrived = self.own(half), self.first[half]
            await_bytes(arrived, self.sems.at[half, 1])

            def add(n, _, own=own, arrived=arrived):
                for m in range(own.shape[1]):
                    total = own[n, m].astype(jnp.float32)
                    for k in range(arrived.shape[0]):
                        total += arrived[k, n, m].astype(jnp.float32)
                    own[n, m] = total.astype(own.dtype)
                return 0

            lax.fori_loop(0, self.half, add, 0)
            for k in range(1, self.p.counts[half][1]):
                to, replica = self.p.peer(half, 1, k)
                remote(
                    own.at[:, to],
                    self.second[half].at[k - 1],
                    self.sems.at[half, 2],
                    self.sems.at[half, 3],
                    replica=replica,
                ).start()

    def total(self):
        for half in range(2):
            own, arrived = self.held(half), self.second[half]
            await_bytes(arrived, self.sems.at[half, 3])

            def add(n, _, own=own, arrived=arrived):
                total = own[n].astype(jnp.float32)
                for k in range(arrived.shape[0]):
                    total += arrived[k, n].astype(jnp.float32)
                own[n] = total.astype(own.dtype)
                return 0

            lax.fori_loop(0, self.half, add, 0)

    def held(self, half):
        return self.part.at[self.rows(half), self.p.a, self.p.b]

    def piece(self, n):
        return self.part.at[n, self.p.a, self.p.b]

    def drain(self):
        for half in range(2):
            await_bytes(self.first[half], self.sems.at[half, 0])
            await_bytes(self.second[half], self.sems.at[half, 2])


def reduce_scratch(n, high, wide, rows, columns):
    low = functools.partial(pltpu.VMEM, dtype=jnp.bfloat16)
    half = n // 2
    return [
        low((n, high, wide, rows, columns)),
        low((wide - 1, half, high, rows, columns)),
        low((high - 1, half, wide, rows, columns)),
        low((high - 1, half, rows, columns)),
        low((wide - 1, half, rows, columns)),
        pltpu.SemaphoreType.DMA((2, 4)),
    ]


def reducer(place, refs):
    part, first_a, first_b, second_a, second_b, sems = refs
    return Reduce(place, part, (first_a, first_b), (second_a, second_b), sems)


class Spread:
    def __init__(self, place, piece, out, sems, turned):
        self.p, self.piece, self.out, self.sems, self.turned = place, piece, out, sems, turned

    def start(self):
        p = self.p
        if self.turned:
            count = self.out.shape[0]
            width = self.out.shape[-1] // p.fsdp
            columns = pl.ds(pl.multiple_of(p.me * width, width), width)

            def pairs(to):
                ref = self.piece(to)
                return [
                    (ref.at[:, pl.ds(i * width, width)], self.out.at[i, p.a, p.b, :, columns])
                    for i in range(count)
                ]

            def send(k, _):
                to = lax.rem(p.me + k, p.fsdp)
                for ref, target in pairs(to):
                    remote(ref, target, self.sems.at[0, 0], self.sems.at[0, 1], fsdp=to).start()
                return 0

            lax.fori_loop(1, p.fsdp, send, 0)
            for ref, target in pairs(p.me):
                pltpu.make_async_copy(ref, target, self.sems.at[0, 1]).start()
        else:
            for half in range(2):
                pltpu.make_async_copy(
                    self.piece(half), self.out.at[half, p.a, p.b], self.sems.at[half, 1]
                ).start()

    def placed(self, half, rows):
        a, b = rows
        if self.turned:
            width = self.out.shape[-1] // 2
            return self.out.at[:, a, b, :, pl.ds(half * width, width)]
        return self.out.at[half, a, b]

    def spread(self):
        p = self.p
        if self.turned:
            await_bytes(self.out.at[:, p.a, p.b], self.sems.at[0, 1])
        for half in range(2):
            ref = self.placed(half, (p.a, p.b))
            src = ref if self.turned else self.piece(half)
            for k in range(1, p.counts[half][1]):
                _, replica = p.peer(half, 1, k)
                remote(src, ref, self.sems.at[half, 2], self.sems.at[half, 3], replica=replica).start()

    def spread_bytes(self, half):
        some = pl.ds(0, self.p.counts[half][1] - 1)
        return self.placed(half, (some, 0) if half == 0 else (0, some))

    def widen(self):
        p = self.p
        for half in range(2):
            if not self.turned:
                await_bytes(self.placed(half, (p.a, p.b)), self.sems.at[half, 1])
            await_bytes(self.spread_bytes(half), self.sems.at[half, 3])
            every = pl.ds(0, p.counts[half][1])
            ref = self.placed(half, (every, p.b) if half == 0 else (p.a, every))
            for k in range(1, p.counts[half][0]):
                _, replica = p.peer(half, 0, k)
                remote(ref, ref, self.sems.at[half, 4], self.sems.at[half, 5], replica=replica).start()

    def widen_bytes(self, half):
        counts = self.p.counts[half]
        every, some = pl.ds(0, counts[1]), pl.ds(0, counts[0] - 1)
        return self.placed(half, (every, some) if half == 0 else (some, every))

    def finish(self):
        p = self.p
        for half in range(2):
            await_bytes(self.widen_bytes(half), self.sems.at[half, 5])
            await_bytes(self.spread_bytes(half), self.sems.at[half, 2])
            await_bytes(self.widen_bytes(half), self.sems.at[half, 4])
        if self.turned:
            width = self.out.shape[-1] // p.fsdp
            await_bytes(
                self.out.at[:, p.a, p.b, :, pl.ds(0, (p.fsdp - 1) * width)], self.sems.at[0, 0]
            )


def spread_sems():
    return [pltpu.SemaphoreType.DMA((2, 6))]


def norm_back(values, gain_row, gains, grad, carried, result, gain_terms):
    block, model = values.shape
    share = gains.shape[2]
    held = values[...].astype(jnp.float32)
    factor = lax.rsqrt(jnp.mean(held * held, axis=-1, keepdims=True) + eps_norm)
    dots = jnp.zeros((block, 1), jnp.float32)
    for j in range(model // share):
        at = pl.ds(j * share, share)
        normed = values[:, at].astype(jnp.float32) * factor
        product = grad[:, at] * normed
        gain_terms[j, gain_row : gain_row + 1, :] = jnp.sum(product, axis=0, keepdims=True)
        dots += jnp.sum(product * gains[j, gain_row : gain_row + 1, :], axis=-1, keepdims=True)
    dots = dots / model
    for j in range(model // share):
        at = pl.ds(j * share, share)
        normed = values[:, at].astype(jnp.float32) * factor
        scaled = grad[:, at] * gains[j, gain_row : gain_row + 1, :]
        result[:, at] = carried[:, at].astype(jnp.float32) + factor * (scaled - normed * dots)


def weigh_kernel(
    cotangent,
    after_attn,
    gains,
    terms_in,
    lowered_two,
    cotangents,
    hidden_in,
    grad_gate_in,
    grad_up_in,
    grad_after,
    gain_terms,
    branch,
    sum_down,
    sum_gate,
    sum_up,
    tokens_held,
    hidden,
    grad_gate,
    grad_up,
    terms,
    across,
    slots,
    summed,
    low,
    load_sems,
    store_sems,
    *rest,
):
    place = Place()
    chips, block = place.chips, cotangent.shape[0]
    model = cotangent.shape[1]
    tile = 2 * block
    scatter_at, gather_at = rest[:6], rest[6:12]
    down, gate, up = [reducer(place, rest[12 + 6 * i : 18 + 6 * i]) for i in range(3)]

    def load(t):
        at = pl.ds(t * tile, tile)
        return pltpu.make_async_copy(terms_in.at[at], terms.at[at], load_sems.at[t])

    loads = [
        pltpu.make_async_copy(source, target, load_sems.at[chips + i])
        for i, (source, target) in enumerate(
            (
                (cotangents, tokens_held),
                (hidden_in, hidden),
                (grad_gate_in, grad_gate),
                (grad_up_in, grad_up),
                (lowered_two, tokens_held),
            )
        )
    ]
    for t in range(chips):
        load(t).start()
    for copy in loads[:4]:
        copy.start()
    place.enter()
    scatter = Scatter(place, terms, across, slots, block, scatter_at)
    for t in range(chips):
        load(t).wait()
        scatter.side(t).start()
    gain_terms[...] = jnp.zeros_like(gain_terms)
    loads[0].wait()
    loads[1].wait()
    _, high, wide, thin, _ = down.part.shape
    columns = min(tile, hidden.shape[1])
    for i in range(0, hidden.shape[1], columns):
        got = contract_first(hidden[:, i : i + columns], tokens_held[...]).astype(jnp.bfloat16)
        for m in range(0, columns, thin):
            n = (i + m) // thin
            down.part[n // (high * wide), n // wide % high, n % wide] = got[m : m + thin, :]
        if 2 * (i + columns) == hidden.shape[1]:
            down.start(0)
    loads[4].start()
    down.start(1)
    for t in range(chips):
        scatter.cross(t)
    scatter.step(1)
    loads[4].wait()

    def weigh(reduce, grads):
        share = model // place.fsdp

        def rows(j, _):
            left = tokens_held[:, pl.ds(pl.multiple_of(j * share, share), share)]
            got = contract_first(left, grads[...]).astype(jnp.bfloat16)
            reduce.part[j] = got.reshape(reduce.part.shape[1:])
            return 0

        for half in range(2):
            lax.fori_loop(half * chips, (half + 1) * chips, rows, 0)
            reduce.start(half)

    loads[2].wait()
    weigh(gate, grad_gate)
    if chips > 2:
        scatter.step(2)
    loads[3].wait()
    weigh(up, grad_up)
    for step in range(3, chips):
        scatter.step(step)
    scatter.finish(summed)
    norm_back(after_attn, 1, gains, summed, cotangent, grad_after, gain_terms)
    low[...] = grad_after[...].astype(jnp.bfloat16)
    here = pl.ds(pl.multiple_of(place.me * block, block), block)
    gather = Gather(place, branch, block, gather_at, low)
    gather.start()
    keep = pltpu.make_async_copy(low, branch.at[here], store_sems.at[0])
    keep.start()
    scatter.drain()
    down.exchange()
    for step in range(1, chips):
        gather.step(step)
        if step == 1:
            gate.exchange()
        if step == max(chips - 2, 1):
            up.exchange()
    keep.wait()
    gather.finish()
    stores = []
    for i, (reduce, out) in enumerate(((down, sum_down), (gate, sum_gate), (up, sum_up))):
        reduce.total()
        for half in range(2):
            store = pltpu.make_async_copy(
                reduce.held(half), out.at[reduce.rows(half)], store_sems.at[1 + 2 * i + half]
            )
            store.start()
            stores.append(store)
    for reduce in (down, gate, up):
        reduce.drain()
    for store in stores:
        store.wait()


def weigh(cotangent, after_attn, gains, terms, lowered_two, cotangents, hidden, grad_gate, grad_up):
    fsdp, replicas = lax.axis_size("fsdp"), lax.axis_size("replica")
    chips, high, wide = fsdp // 2, 2, replicas // 2
    block, model = cotangent.shape
    rows, columns = hidden.shape
    share = gains.shape[2]
    low, full = jnp.bfloat16, jnp.float32
    hbm, vmem = pl.BlockSpec(memory_space=pl.ANY), pl.BlockSpec(memory_space=pltpu.VMEM)
    shape = jax.ShapeDtypeStruct
    down_piece = (2, high, wide, columns // (2 * replicas), model)
    wide_piece = (fsdp, high, wide, share // replicas, columns)
    dma = pltpu.SemaphoreType.DMA
    return pl.pallas_call(
        weigh_kernel,
        in_specs=[vmem] * 3 + [hbm] * 6,
        out_specs=[vmem] * 2 + [hbm] * 4,
        out_shape=[
            shape((block, model), full),
            shape((fsdp, 8, share), full),
            shape((rows, model), low),
            shape((2,) + down_piece[3:], low),
            shape((fsdp,) + wide_piece[3:], low),
            shape((fsdp,) + wide_piece[3:], low),
        ],
        scratch_shapes=[
            pltpu.VMEM((rows, model), low),
            pltpu.VMEM((rows, columns), low),
            pltpu.VMEM((rows, columns), low),
            pltpu.VMEM((rows, columns), low),
            pltpu.VMEM((rows, model), low),
            pltpu.VMEM((chips * block, model), low),
            pltpu.VMEM((chips + 1, block, model), low),
            pltpu.VMEM((block, model), full),
            pltpu.VMEM((block, model), low),
            dma((chips + 5,)),
            dma((7,)),
        ]
        + scatter_sems(chips)
        + line_sems(chips)
        + reduce_scratch(*down_piece)
        + reduce_scratch(*wide_piece)
        + reduce_scratch(*wide_piece),
        compiler_params=pltpu.CompilerParams(
            collective_id=1, has_side_effects=True, vmem_limit_bytes=VMEM_LIMIT
        ),
        name="weigh",
    )(cotangent, after_attn, gains, terms, lowered_two, cotangents, hidden, grad_gate, grad_up)


def back_kernel(
    tokens,
    gains,
    grad_after,
    gain_terms_in,
    after_attn,
    sums,
    sum_down,
    sum_gate,
    sum_up,
    branch_in,
    lowered_one,
    slab_qkv,
    w_out,
    queries,
    keys,
    values,
    attended,
    logs,
    cosine,
    sine,
    outputs,
    grad_tokens,
    gain_out,
    out_down,
    out_gate,
    out_up,
    out_qkv,
    out_out,
    terms,
    across,
    slots,
    branch,
    summed,
    grad_low,
    grad_key,
    grad_value,
    grads,
    gain_terms,
    gain_slots,
    gain_sums,
    gain_sems,
    load_sems,
    *rest,
):
    place = Place()
    chips, block = place.chips, tokens.shape[0]
    model, width = tokens.shape[1], queries.shape[1]
    share = gains.shape[2]
    tile = 2 * block
    scatter_at, rest = rest[:6], rest[6:]
    down = Spread(place, lambda n: sum_down.at[n], out_down, rest[0], False)
    gate = Spread(place, lambda n: sum_gate.at[n], out_gate, rest[1], True)
    up = Spread(place, lambda n: sum_up.at[n], out_up, rest[2], True)
    qkv, out = reducer(place, rest[5:11]), reducer(place, rest[11:17])
    qkv_spread = Spread(place, qkv.piece, out_qkv, rest[3], True)
    out_spread = Spread(place, out.piece, out_out, rest[4], False)
    load = pltpu.make_async_copy(branch_in, branch, load_sems.at[0])
    load.start()
    place.enter()
    down.start()
    down.spread()
    gate.start()
    up.start()
    load.wait()

    def attend_rows(t, _):
        at = pl.ds(pl.multiple_of(t * tile, tile), tile)
        grad_low[at, :] = contract_last(branch[at, :], w_out[...]).astype(jnp.bfloat16)
        return 0

    lax.fori_loop(0, chips, attend_rows, 0)
    _, high, wide, thin, columns = out.part.shape
    for half in range(2):
        for at in range(0, columns, 512):
            got = contract_first(
                attended[...], branch[:, half * columns + at : half * columns + at + 512]
            ).astype(jnp.bfloat16)
            out.part[half, :, :, :, at : at + 512] = got.reshape(high, wide, thin, 512)
    out.start(0)
    out.start(1)
    reload = pltpu.make_async_copy(lowered_one, branch, load_sems.at[1])
    reload.start()
    down.widen()

    scale = HEAD_DIM**-0.5
    grad_key[...] = jnp.zeros_like(grad_key)
    grad_value[...] = jnp.zeros_like(grad_value)
    pair = 2 * HEAD_DIM
    height = tile * 1024 // max(queries.shape[0], 1024)
    for first in range(0, queries.shape[0], height):
        rows, seen = pl.ds(first, height), pl.ds(0, first + height)

        def heads(h, _, first=first, rows=rows, seen=seen):
            lanes = pl.ds(pl.multiple_of(h * pair, pair), pair)
            q2, g2, log2 = queries[rows, lanes], grad_low[rows, lanes], logs[rows, lanes]
            k2, v2 = keys[seen, lanes], values[seen, lanes]
            for_queries, for_keys, for_values = [], [], []
            for at in (0, HEAD_DIM):
                head = slice(at, at + HEAD_DIM)
                q, g, k = q2[:, head], g2[:, head], k2[:, head]
                weights = jnp.exp(scores_of(q, k, first) - log2[:, at : at + 1])
                grad_weights = contract_last(g, v2[:, head])
                delta = jnp.sum(weights * grad_weights, axis=-1, keepdims=True)
                grad_scores = (weights * (grad_weights - delta)).astype(jnp.bfloat16)
                for_queries.append(dot(grad_scores, k))
                for_keys.append(contract_first(grad_scores, q))
                for_values.append(contract_first(weights.astype(jnp.bfloat16), g))
            got = jnp.concatenate(for_queries, axis=1) * scale
            got = got * cosine[rows, :] - partner(got) * sine[rows, :]
            grads[rows, lanes] = got.astype(jnp.bfloat16)
            grad_key[seen, lanes] += jnp.concatenate(for_keys, axis=1) * scale
            grad_value[seen, lanes] += jnp.concatenate(for_values, axis=1)
            return 0

        lax.fori_loop(0, width // pair, heads, 0)

    def turn_back(t, _):
        at = pl.ds(pl.multiple_of(t * tile, tile), tile)
        for j in range(0, width, pair):
            got = grad_key[at, j : j + pair]
            got = got * cosine[at, :] - partner(got) * sine[at, :]
            grads[at, width + j : width + j + pair] = got.astype(jnp.bfloat16)
        grads[at, 2 * width :] = grad_value[at, :].astype(jnp.bfloat16)
        got = contract_last(grads[at, :width], slab_qkv[:model, :])
        got += contract_last(grads[at, width : 2 * width], slab_qkv[model : 2 * model, :])
        got += contract_last(grads[at, 2 * width :], slab_qkv[2 * model :, :])
        terms[at, :] = got.astype(jnp.bfloat16)
        return 0

    lax.fori_loop(0, chips, turn_back, 0)
    scatter = Scatter(place, terms, across, slots, block, scatter_at)
    for t in range(chips):
        scatter.side(t).start()
    reload.wait()

    def weigh_rows(j, _):
        left = branch[:, pl.ds(pl.multiple_of(j * share, share), share)]
        got = contract_first(left, grads[...]).astype(jnp.bfloat16)
        qkv.part[j] = got.reshape(qkv.part.shape[1:])
        return 0

    for half in range(2):
        lax.fori_loop(half * chips, (half + 1) * chips, weigh_rows, 0)
        qkv.start(half)
    gate.spread()
    for t in range(chips):
        scatter.cross(t)
    for step in range(1, chips):
        scatter.step(step)
        if step == 1:
            out.exchange()
            up.spread()
        if step == max(chips - 2, 1):
            qkv.exchange()
    gate.widen()
    out.total()
    out_spread.start()
    out_spread.spread()
    scatter.finish(summed)
    gain_terms[...] = gain_terms_in[...]
    norm_back(tokens, 0, gains, summed, grad_after, grad_tokens, gain_terms)

    def send_gain(k, _):
        to = lax.rem(place.me + k, place.fsdp)
        remote(
            gain_terms.at[to], gain_slots.at[place.me], gain_sems.at[0], gain_sems.at[1], fsdp=to
        ).start()
        return 0

    lax.fori_loop(1, place.fsdp, send_gain, 0)
    gain_slots[place.me] = gain_terms[place.me]
    scatter.drain()
    load_sums = pltpu.make_async_copy(sums, terms, load_sems.at[0])
    load_sums.start()
    qkv.total()
    qkv_spread.start()
    await_bytes(gain_slots.at[pl.ds(0, place.fsdp - 1)], gain_sems.at[1])
    gain_sums[place.replica] = jnp.sum(gain_slots[...], axis=0)

    def send_sum(k, _):
        ref = gain_sums.at[place.replica]
        to = lax.rem(place.replica + k, place.replicas)
        remote(ref, ref, gain_sems.at[2], gain_sems.at[3], replica=to).start()
        return 0

    lax.fori_loop(1, place.replicas, send_sum, 0)

    load_sums.wait()
    for t in range(chips):
        scatter.side(t).start()
    up.widen()
    for t in range(chips):
        scatter.cross(t)
    scatter.step(1)
    qkv_spread.spread()
    for step in range(2, chips):
        scatter.step(step)
        if step == 2:
            out_spread.widen()
    if chips == 2:
        out_spread.widen()
    scatter.finish(summed)
    outputs[...] = (summed[...] + after_attn[...]).astype(outputs.dtype)
    qkv_spread.widen()
    await_bytes(gain_sums.at[pl.ds(0, place.replicas - 1)], gain_sems.at[3])
    gain_out[...] = jnp.sum(gain_sums[...], axis=0)
    await_bytes(gain_slots.at[pl.ds(0, place.fsdp - 1)], gain_sems.at[0])
    await_bytes(gain_sums.at[pl.ds(0, place.replicas - 1)], gain_sems.at[2])
    scatter.drain()
    qkv.drain()
    out.drain()
    for spread in (down, gate, up, out_spread, qkv_spread):
        spread.finish()


def back(
    tokens,
    gains,
    grad_after,
    gain_terms,
    after_attn,
    sums,
    sum_down,
    sum_gate,
    sum_up,
    branch,
    lowered_one,
    slab_qkv,
    w_out,
    queries,
    keys,
    values,
    attended,
    logs,
    cosine,
    sine,
):
    fsdp, replicas = lax.axis_size("fsdp"), lax.axis_size("replica")
    chips, high, wide = fsdp // 2, 2, replicas // 2
    block, model = tokens.shape
    rows, width = queries.shape
    share = gains.shape[2]
    low, full = jnp.bfloat16, jnp.float32
    hbm, vmem = pl.BlockSpec(memory_space=pl.ANY), pl.BlockSpec(memory_space=pltpu.VMEM)
    shape = jax.ShapeDtypeStruct
    thin = share // replicas
    columns = sum_gate.shape[-1]
    qkv_piece = (fsdp, high, wide, thin, 3 * width)
    out_piece = (2, high, wide, width // replicas, model // 2)
    dma = pltpu.SemaphoreType.DMA
    return pl.pallas_call(
        back_kernel,
        in_specs=[vmem] * 5 + [hbm] * 6 + [vmem] * 9,
        out_specs=[vmem] * 3 + [hbm] * 5,
        out_shape=[
            shape((block, model), low),
            shape((block, model), full),
            shape((8, share), full),
            shape((2, high, wide) + sum_down.shape[1:], low),
            shape((1, high, wide, thin, fsdp * columns), low),
            shape((1, high, wide, thin, fsdp * columns), low),
            shape((3, high, wide, thin, fsdp * width), low),
            shape(out_piece, low),
        ],
        scratch_shapes=[
            pltpu.VMEM((rows, model), low),
            pltpu.VMEM((chips * block, model), low),
            pltpu.VMEM((chips + 1, block, model), low),
            pltpu.VMEM((rows, model), low),
            pltpu.VMEM((block, model), full),
            pltpu.VMEM((rows, width), low),
            pltpu.VMEM((rows, width), full),
            pltpu.VMEM((rows, width), full),
            pltpu.VMEM((rows, 3 * width), low),
            pltpu.VMEM((fsdp, 8, share), full),
            pltpu.VMEM((fsdp, 8, share), full),
            pltpu.VMEM((replicas, 8, share), full),
            dma((4,)),
            dma((2,)),
        ]
        + scatter_sems(chips)
        + spread_sems() * 5
        + reduce_scratch(*qkv_piece)
        + reduce_scratch(*out_piece),
        compiler_params=pltpu.CompilerParams(
            collective_id=2, has_side_effects=True, vmem_limit_bytes=VMEM_LIMIT
        ),
        name="back",
    )(
        tokens,
        gains,
        grad_after,
        gain_terms,
        after_attn,
        sums,
        sum_down,
        sum_gate,
        sum_up,
        branch,
        lowered_one,
        slab_qkv,
        w_out,
        queries,
        keys,
        values,
        attended,
        logs,
        cosine,
        sine,
    )


def widen_kernel(
    down,
    gate,
    up,
    qkv,
    out,
    outputs_in,
    tokens_in,
    gains,
    w_down,
    w_gate,
    w_up,
    w_query,
    w_key,
    w_value,
    w_out,
    outputs,
    grad_tokens,
    gain_one,
    gain_two,
):
    w_down[...] = down[...].astype(jnp.float32)
    w_gate[...] = gate[...].astype(jnp.float32)
    w_up[...] = up[...].astype(jnp.float32)
    for i, ref in enumerate((w_query, w_key, w_value)):
        ref[...] = qkv[i].astype(jnp.float32)
    half = out.shape[2]
    for i in range(2):
        w_out[:, i * half : (i + 1) * half] = out[i].astype(jnp.float32)
    outputs[...] = outputs_in[...]
    grad_tokens[...] = tokens_in[...]
    gain_one[...] = gains[0, :]
    gain_two[...] = gains[1, :]


def widen(down, gate, up, qkv, out, outputs, grad_tokens, gains):
    steps = min(16, gate.shape[0] // 16)
    token_steps = outputs.shape[0] // 16
    full = jnp.float32

    def rows(array):
        return pl.BlockSpec((array.shape[0] // steps, array.shape[1]), lambda i: (i, 0))

    def tokens(array):
        return pl.BlockSpec(
            (array.shape[0] // token_steps, array.shape[1]), lambda i: (jnp.minimum(i, token_steps - 1), 0)
        )

    def stacked(array):
        return pl.BlockSpec((array.shape[0], array.shape[1] // steps, array.shape[2]), lambda i: (0, i, 0))

    like = [down, gate, up, qkv[0], qkv[0], qkv[0]]
    shapes = [jax.ShapeDtypeStruct(array.shape, full) for array in like]
    shapes.append(jax.ShapeDtypeStruct((out.shape[1], 2 * out.shape[2]), full))
    row = jax.ShapeDtypeStruct(gains.shape[1:], full)
    whole = pl.BlockSpec(gains.shape, lambda i: (0, 0))
    line = pl.BlockSpec(gains.shape[1:], lambda i: (0,))
    return pl.pallas_call(
        widen_kernel,
        grid=(steps,),
        in_specs=[rows(down), rows(gate), rows(up), stacked(qkv), stacked(out)]
        + [tokens(outputs), tokens(grad_tokens), whole],
        out_specs=[rows(shape) for shape in shapes]
        + [tokens(outputs), tokens(grad_tokens), line, line],
        out_shape=shapes
        + [jax.ShapeDtypeStruct(array.shape, array.dtype) for array in (outputs, grad_tokens)]
        + [row, row],
        compiler_params=pltpu.CompilerParams(vmem_limit_bytes=VMEM_LIMIT),
        name="widen",
    )(down, gate, up, qkv, out, outputs, grad_tokens, gains)


def local(
    tokens, attn_gain, w_query, w_key, w_value, w_out, ffn_gain, w_gate, w_up, w_down, cotangent
):
    cosine, sine = rope_tables(tokens.shape[0] * lax.axis_size("fsdp"))
    (
        lowered_one,
        lowered_two,
        cotangents,
        slab_qkv,
        hidden,
        grad_gate,
        grad_up,
        terms,
        sums,
        queries,
        keys,
        values,
        attended,
        logs,
        after_attn,
        gains,
    ) = front(
        tokens,
        cotangent,
        attn_gain,
        ffn_gain,
        w_query,
        w_key,
        w_value,
        w_out,
        w_gate,
        w_up,
        w_down,
        cosine,
        sine,
    )
    grad_after, gain_terms, branch, sum_down, sum_gate, sum_up = weigh(
        cotangent, after_attn, gains, terms, lowered_two, cotangents, hidden, grad_gate, grad_up
    )
    outputs, grad_tokens, gain_grads, low_down, low_gate, low_up, low_qkv, low_out = back(
        tokens,
        gains,
        grad_after,
        gain_terms,
        after_attn,
        sums,
        sum_down,
        sum_gate,
        sum_up,
        branch,
        lowered_one,
        slab_qkv,
        w_out,
        queries,
        keys,
        values,
        attended,
        logs,
        cosine,
        sine,
    )
    (
        grad_w_down,
        grad_w_gate,
        grad_w_up,
        grad_w_query,
        grad_w_key,
        grad_w_value,
        grad_w_out,
        outputs,
        grad_tokens,
        grad_attn_gain,
        grad_ffn_gain,
    ) = widen(
        low_down.reshape(w_down.shape),
        low_gate.reshape(w_gate.shape),
        low_up.reshape(w_up.shape),
        low_qkv.reshape((3,) + w_query.shape),
        low_out.reshape(2, w_out.shape[0], -1),
        outputs,
        grad_tokens,
        gain_grads,
    )
    return (
        outputs,
        grad_tokens,
        grad_attn_gain,
        grad_w_query,
        grad_w_key,
        grad_w_value,
        grad_w_out,
        grad_ffn_gain,
        grad_w_gate,
        grad_w_up,
        grad_w_down,
    )


def solution(mesh):
    rows = P("fsdp", None)
    tokens = P(("replica", "fsdp"), None)
    gain = P("fsdp")
    return jax.shard_map(
        local,
        mesh=mesh,
        in_specs=(tokens, gain, rows, rows, rows, rows, gain, rows, rows, rows, tokens),
        out_specs=(tokens, tokens, gain, rows, rows, rows, rows, gain, rows, rows, rows),
        check_vma=False,
    )
```

```python
import functools

import jax
import jax.numpy as jnp
import numpy as np
from jax import lax
from jax.experimental import pallas as pl
from jax.experimental.pallas import tpu as pltpu
from jax.sharding import PartitionSpec as P

HEAD_DIM = 64

eps_norm = 1e-05
rope_base = 130000.0
masked_score = -1e30


def rope_tables(row_count):
    lane = np.arange(2 * HEAD_DIM) % HEAD_DIM
    halfway = HEAD_DIM // 2
    spacing = ((lane % halfway) * np.float32(2.0) / HEAD_DIM).astype(np.float32)
    frequency = np.power(np.float32(rope_base), -spacing)
    angles = np.arange(row_count, dtype=np.float32)[:, None] * frequency[None, :]
    sign = np.where(lane < halfway, -1.0, 1.0).astype(np.float32)
    return np.cos(angles).astype(np.float32), (np.sin(angles) * sign[None, :]).astype(np.float32)


def dot(left, right):
    return jnp.dot(left, right, preferred_element_type=jnp.float32)


def contract_last(left, right):
    return lax.dot_general(
        left, right, (((1,), (1,)), ((), ())), preferred_element_type=jnp.float32
    )


def contract_first(left, right):
    return lax.dot_general(
        left, right, (((0,), (0,)), ((), ())), preferred_element_type=jnp.float32
    )


def scores_of(queries, keys, first_row):
    rows, columns = queries.shape[0], keys.shape[0]
    scores = contract_last(queries, keys) * HEAD_DIM**-0.5
    at_row = lax.broadcasted_iota(jnp.int32, (rows, columns), 0) + first_row
    at_column = lax.broadcasted_iota(jnp.int32, (rows, columns), 1)
    return jnp.where(at_column <= at_row, scores, masked_score)


MESH = pl.DeviceIdType.MESH
VMEM_LIMIT = 61 * 2**20


def remote(src, dst, send, recv, **where):
    return pltpu.make_async_remote_copy(
        src_ref=src, dst_ref=dst, send_sem=send, recv_sem=recv, device_id=where, device_id_type=MESH
    )


def await_bytes(ref, sem):
    pltpu.make_async_copy(ref, ref, sem).wait()


def rows_at(ref, index, size):
    return ref.at[pl.ds(pl.multiple_of(index * size, size), size)]


class Place:
    def __init__(self):
        self.fsdp, self.replicas = lax.axis_size("fsdp"), lax.axis_size("replica")
        self.me, self.replica = lax.axis_index("fsdp"), lax.axis_index("replica")
        self.chips = self.fsdp // 2
        self.chip, self.core = self.me // 2, self.me % 2
        self.sibling = self.me + 1 - 2 * self.core
        self.high, self.wide = 2, self.replicas // 2
        self.a, self.b = self.replica // self.wide, self.replica % self.wide
        self.counts = ((self.wide, self.high), (self.high, self.wide))
        self.above = self.chip + 1 < self.chips
        self.below = self.chip >= 1

    def peer(self, half, stage, k):
        if half == stage:
            to = lax.rem(self.b + k, self.wide)
            return to, self.a * self.wide + to
        to = lax.rem(self.a + k, self.high)
        return to, to * self.wide + self.b

    def nearest(self, k):
        found = jnp.int32(0)
        for chip in range(self.chips):
            order = sorted(range(self.chips), key=lambda other, chip=chip: (abs(other - chip), other))
            found = found + jnp.where(self.chip == chip, order[k], 0)
        return found

    def enter(self):
        barrier = pltpu.get_barrier_semaphore()

        def greet(k, _):
            to = lax.rem(self.me + k, self.fsdp)
            pl.semaphore_signal(barrier, inc=1, device_id={"fsdp": to}, device_id_type=MESH)
            return 0

        def greet_replica(k, _):
            to = lax.rem(self.replica + k, self.replicas)
            pl.semaphore_signal(barrier, inc=1, device_id={"replica": to}, device_id_type=MESH)
            return 0

        lax.fori_loop(1, self.fsdp, greet, 0)
        lax.fori_loop(1, self.replicas, greet_replica, 0)
        pl.semaphore_wait(barrier, self.fsdp - 1 + self.replicas - 1)


def line_sems(chips):
    return [pltpu.SemaphoreType.DMA((chips,))] * 6


class Gather:
    def __init__(self, place, buf, block, sems, own=None):
        self.p, self.buf, self.block, self.own = place, buf, block, own
        self.up_out, self.up_in, self.down_out, self.down_in, self.side_out, self.side_in = sems

    def held(self, chip):
        return rows_at(self.buf, 2 * chip + self.p.core, self.block)

    def up(self, step):
        ref = self.held(self.p.chip - step + 1)
        src = self.own if step == 1 and self.own is not None else ref
        return remote(src, ref, self.up_out.at[step], self.up_in.at[step], fsdp=self.p.me + 2)

    def down(self, step):
        ref = self.held(self.p.chip + step - 1)
        src = self.own if step == 1 and self.own is not None else ref
        return remote(src, ref, self.down_out.at[step], self.down_in.at[step], fsdp=self.p.me - 2)

    def side(self, chip, src=None):
        ref = self.held(chip)
        src = ref if src is None else src
        return remote(src, ref, self.side_out.at[chip], self.side_in.at[chip], fsdp=self.p.sibling)

    def start(self):
        p = self.p
        pl.when(p.above)(lambda: self.up(1).start())
        pl.when(p.below)(lambda: self.down(1).start())
        self.side(p.chip, self.own).start()

    def step(self, step):
        p = self.p
        from_below, from_above = p.chip - step, p.chip + step

        @pl.when(from_below >= 0)
        def _():
            await_bytes(self.held(from_below), self.up_in.at[step])
            if step + 1 < p.chips:
                pl.when(p.above)(lambda: self.up(step + 1).start())
            self.side(from_below).start()

        @pl.when(from_above < p.chips)
        def _():
            await_bytes(self.held(from_above), self.down_in.at[step])
            if step + 1 < p.chips:
                pl.when(p.below)(lambda: self.down(step + 1).start())
            self.side(from_above).start()

    def across(self, chip):
        await_bytes(rows_at(self.buf, 2 * chip + 1 - self.p.core, self.block), self.side_in.at[chip])

    def drain(self):
        p = self.p
        for step in range(1, p.chips):
            pl.when(jnp.logical_and(p.above, p.chip - step + 1 >= 0))(
                lambda step=step: self.up(step).wait_send()
            )
            pl.when(jnp.logical_and(p.below, p.chip + step - 1 < p.chips))(
                lambda step=step: self.down(step).wait_send()
            )
        for chip in range(p.chips):
            self.side(chip).wait_send()

    def finish(self):
        for chip in range(self.p.chips):
            self.across(chip)
        self.drain()


class Scatter:
    def __init__(self, place, terms, across, slots, block, sems):
        self.p, self.terms, self.across, self.slots, self.block = place, terms, across, slots, block
        self.up_out, self.up_in, self.down_out, self.down_in, self.side_out, self.side_in = sems

    def side(self, chip):
        p = self.p
        return remote(
            rows_at(self.terms, 2 * chip + 1 - p.core, self.block),
            rows_at(self.across, chip, self.block),
            self.side_out.at[chip],
            self.side_in.at[chip],
            fsdp=p.sibling,
        )

    def term(self, chip):
        return rows_at(self.terms, 2 * chip + self.p.core, self.block)

    def up(self, step):
        return remote(
            self.term(self.p.chips - step + self.p.chip),
            self.slots.at[step - self.p.chip - 1],
            self.up_out.at[step],
            self.up_in.at[step],
            fsdp=self.p.me + 2,
        )

    def down(self, step):
        return remote(
            self.term(self.p.chip - self.p.chips + step),
            self.slots.at[step + 1],
            self.down_out.at[step],
            self.down_in.at[step],
            fsdp=self.p.me - 2,
        )

    def add(self, chip, arrived):
        term = self.term(chip)
        term[...] = (term[...].astype(jnp.float32) + arrived[...].astype(jnp.float32)).astype(term.dtype)

    def cross(self, chip):
        arrived = rows_at(self.across, chip, self.block)
        await_bytes(arrived, self.side_in.at[chip])
        self.add(chip, arrived)

    def step(self, step):
        p = self.p
        rising, falling = p.chips - step + p.chip, p.chip - p.chips + step

        @pl.when(jnp.logical_and(p.above, rising < p.chips))
        def _():
            if step > 1:

                @pl.when(p.below)
                def _():
                    arrived = self.slots.at[step - 1 - p.chip]
                    await_bytes(arrived, self.up_in.at[step - 1])
                    self.add(rising, arrived)

            self.up(step).start()

        @pl.when(jnp.logical_and(p.below, falling >= 0))
        def _():
            if step > 1:

                @pl.when(p.above)
                def _():
                    arrived = self.slots.at[step]
                    await_bytes(arrived, self.down_in.at[step - 1])
                    self.add(falling, arrived)

            self.down(step).start()

    def finish(self, total):
        p, last = self.p, self.p.chips - 1
        total[...] = self.term(p.chip)[...].astype(jnp.float32)

        @pl.when(p.below)
        def _():
            await_bytes(self.slots.at[last - p.chip], self.up_in.at[last])
            total[...] += self.slots[last - p.chip].astype(jnp.float32)

        @pl.when(p.above)
        def _():
            await_bytes(self.slots.at[last + 1], self.down_in.at[last])
            total[...] += self.slots[last + 1].astype(jnp.float32)

    def drain(self):
        p = self.p
        for step in range(1, p.chips):
            pl.when(jnp.logical_and(p.above, p.chips - step + p.chip < p.chips))(
                lambda step=step: self.up(step).wait_send()
            )
            pl.when(jnp.logical_and(p.below, p.chip - p.chips + step >= 0))(
                lambda step=step: self.down(step).wait_send()
            )
        for chip in range(p.chips):
            self.side(chip).wait_send()


def scatter_sems(chips):
    dma = pltpu.SemaphoreType.DMA
    return [dma((chips,))] * 6


class Turn:
    def __init__(self, place, weight, slab, first, sems):
        self.p, self.weight, self.slab, self.first = place, weight, slab, first
        self.far_out, self.far_in, self.near_out, self.near_in, self.own, self.passing = sems
        self.height, self.width = weight.shape[0], slab.shape[1]
        self.share = self.height // place.replicas

    def far_rows(self):
        return (self.p.fsdp - 2) * self.share

    def piece(self, block, share):
        at = self.first + block * self.height + share * self.share
        return self.slab.at[pl.ds(pl.multiple_of(at, self.share), self.share)]

    def whole(self, block):
        at = self.first + block * self.height
        return self.slab.at[pl.ds(pl.multiple_of(at, self.height), self.height)]

    def columns(self, to):
        return pl.ds(pl.multiple_of(to * self.width, self.width), self.width)

    def start(self):
        p = self.p

        def send(k, _):
            to = lax.rem(2 * p.chip + 2 + k, p.fsdp)
            share = pl.ds(pl.multiple_of(p.replica * self.share, self.share), self.share)
            remote(
                self.weight.at[share, self.columns(to)],
                self.piece(p.me, p.replica),
                self.far_out,
                self.far_in,
                fsdp=to,
            ).start()
            return 0

        lax.fori_loop(0, p.fsdp - 2, send, 0)
        self.near().start()
        self.mine().start()

    def near(self):
        p = self.p
        return remote(
            self.weight.at[:, self.columns(p.sibling)], self.whole(p.me), self.near_out, self.near_in, fsdp=p.sibling
        )

    def mine(self):
        return pltpu.make_async_copy(self.weight.at[:, self.columns(self.p.me)], self.whole(self.p.me), self.own)

    def await_far(self):
        await_bytes(self.slab.at[pl.ds(0, self.far_rows())], self.far_in)

    def bytes_of(self, pieces):
        return self.slab.at[pl.ds(0, pieces * self.share)]

    def pass_bytes(self, half, stage):
        first, second = self.p.counts[half]
        return self.bytes_of((self.p.chips - 1) * (second - 1 if stage == 0 else second * (first - 1)))

    def send_pieces(self, half, stage, shares):
        p = self.p

        def one(i, _):
            block = lax.rem(2 * p.chip + 2 + 2 * i + half, p.fsdp)
            for share in shares:
                ref = self.piece(block, share)
                for k in range(1, p.counts[half][1 - stage]):
                    _, replica = p.peer(half, 1 - stage, k)
                    remote(
                        ref,
                        ref,
                        self.passing.at[half, 2 * stage],
                        self.passing.at[half, 2 * stage + 1],
                        replica=replica,
                    ).start()
            return 0

        lax.fori_loop(0, p.chips - 1, one, 0)

    def pass_on(self):
        for half in range(2):
            self.send_pieces(half, 0, [self.p.replica])

    def pass_far(self):
        p = self.p
        for half in range(2):
            await_bytes(self.pass_bytes(half, 0), self.passing.at[half, 1])
            if half == 0:
                shares = [a * p.wide + p.b for a in range(p.high)]
            else:
                shares = [p.a * p.wide + b for b in range(p.wide)]
            self.send_pieces(half, 1, shares)

    def finish(self):
        for half in range(2):
            await_bytes(self.pass_bytes(half, 1), self.passing.at[half, 3])
        await_bytes(self.whole(self.p.sibling), self.near_in)
        self.mine().wait()

    def drain(self):
        await_bytes(self.slab.at[pl.ds(0, self.far_rows())], self.far_out)
        self.near().wait_send()
        for half in range(2):
            await_bytes(self.pass_bytes(half, 0), self.passing.at[half, 0])
            await_bytes(self.pass_bytes(half, 1), self.passing.at[half, 2])


def turn_sems():
    return [pltpu.SemaphoreType.DMA(())] * 5 + [pltpu.SemaphoreType.DMA((2, 4))]


def partner(values):
    halfway = HEAD_DIM // 2
    width = values.shape[1]
    lane = lax.broadcasted_iota(jnp.int32, values.shape, 1) % HEAD_DIM
    return jnp.where(
        lane < halfway,
        pltpu.roll(values, width - halfway, axis=1),
        pltpu.roll(values, halfway, axis=1),
    )


def front_kernel(
    tokens,
    cotangent,
    gain_one,
    gain_two,
    w_query,
    w_key,
    w_value,
    w_out,
    w_gate,
    w_up,
    w_down,
    cosine,
    sine,
    lowered_one,
    lowered_two_out,
    cotangents,
    slab_qkv_out,
    hidden_out,
    grad_gate_out,
    grad_up_out,
    terms_out,
    sums_out,
    queries,
    keys,
    values,
    attended,
    logs,
    after_attn,
    gains,
    low,
    tiles,
    lowered_two,
    slab_qkv,
    slab_gate,
    slab_up,
    held_down,
    terms,
    across,
    slots,
    tile_hidden,
    tile_gate,
    tile_up,
    tile_terms,
    tile_sums,
    gain_rows,
    gain_out,
    gain_in,
    copy_sems,
    load_sems,
    store_sems,
    *sems,
):
    place = Place()
    chips, block = place.chips, tokens.shape[0]
    model, width = tokens.shape[1], queries.shape[1]
    share = gain_one.shape[0]
    tile = 2 * block
    one_at, cot_at, two_at, scatter_at = sems[:6], sems[6:12], sems[12:18], sems[18:24]
    turn_at = [sems[24 + 6 * i : 30 + 6 * i] for i in range(5)]
    turns = [
        Turn(place, weight, slab_qkv, i * model, turn_at[i])
        for i, weight in enumerate((w_query, w_key, w_value))
    ]
    turn_gate = Turn(place, w_gate, slab_gate, 0, turn_at[3])
    turn_up = Turn(place, w_up, slab_up, 0, turn_at[4])
    here = pl.ds(pl.multiple_of(place.me * block, block), block)

    gain_rows[...] = jnp.zeros_like(gain_rows)
    gain_rows[0, :] = gain_one[...].astype(jnp.float32)
    gain_rows[1, :] = gain_two[...].astype(jnp.float32)
    load_down = pltpu.make_async_copy(w_down, held_down, copy_sems.at[0])
    load_down.start()
    keep_cot = pltpu.make_async_copy(cotangent, cotangents.at[here], copy_sems.at[1])
    keep_cot.start()
    place.enter()

    def send_gains(k, _):
        to = lax.rem(place.me + k, place.fsdp)
        remote(gain_rows, gains.at[place.me], gain_out, gain_in, fsdp=to).start()
        return 0

    lax.fori_loop(1, place.fsdp, send_gains, 0)
    for turn in turns:
        turn.start()
    gains[place.me] = gain_rows[...]
    inputs = tokens[...].astype(jnp.float32)
    factor = lax.rsqrt(jnp.mean(inputs * inputs, axis=-1, keepdims=True) + eps_norm)
    await_bytes(gains.at[pl.ds(0, place.fsdp - 1)], gain_in)
    for j in range(model // share):
        at = pl.ds(j * share, share)
        normed = tokens[:, at].astype(jnp.float32) * factor
        low[:, at] = (normed * gains[j, 0:1, :]).astype(jnp.bfloat16)
    first = Gather(place, lowered_one, block, one_at, low)
    first.start()
    keep_low = pltpu.make_async_copy(low, lowered_one.at[here], copy_sems.at[2])
    keep_low.start()
    for turn in turns:
        turn.await_far()
        turn.pass_on()
    for step in range(1, chips - 1):
        first.step(step)
        if step == 1:
            for turn in turns:
                turn.pass_far()
    turn_gate.start()
    if chips == 2:
        for turn in turns:
            turn.pass_far()
    keep_low.wait()

    def load(source, t, slot):
        return pltpu.make_async_copy(rows_at(source, t, tile), tiles.at[slot], load_sems.at[slot])

    def fetch(k):
        first.across(place.nearest(k))
        load(lowered_one, place.nearest(k), k % 2).start()

    def project(k):
        t = place.nearest(k)
        load(lowered_one, t, k % 2).wait()
        at = pl.ds(pl.multiple_of(t * tile, tile), tile)
        for i, ref in enumerate((queries, keys, values)):
            out = dot(tiles[k % 2], slab_qkv[i * model : (i + 1) * model, :])
            if i < 2:
                for j in range(0, width, 2 * HEAD_DIM):
                    pair = out[:, j : j + 2 * HEAD_DIM]
                    pair = pair * cosine[at, :] + partner(pair) * sine[at, :]
                    ref[at, j : j + 2 * HEAD_DIM] = pair.astype(jnp.bfloat16)
            else:
                ref[at, :] = out.astype(jnp.bfloat16)

    early = max(chips - 2, 1)
    fetch(0)
    for turn in turns:
        turn.finish()
    keep_slab = pltpu.make_async_copy(slab_qkv, slab_qkv_out, copy_sems.at[3])
    keep_slab.start()
    third = Gather(place, cotangents, block, cot_at, cotangent)
    for k in range(chips):
        if k + 1 == early:
            first.step(chips - 1)
            turn_up.start()
            third.start()
        if k + 1 < chips:
            fetch(k + 1)
        project(k)
    first.drain()
    scatter = Scatter(place, terms, across, slots, block, scatter_at)
    pair = 2 * HEAD_DIM
    for t in range(chips):
        here_t, seen = pl.ds(t * tile, tile), pl.ds(0, (t + 1) * tile)

        def heads(h, _, t=t, here_t=here_t, seen=seen):
            lanes = pl.ds(pl.multiple_of(h * pair, pair), pair)
            q2, k2, v2 = queries[here_t, lanes], keys[seen, lanes], values[seen, lanes]
            mixed, stats = [], []
            for at in (0, HEAD_DIM):
                head = slice(at, at + HEAD_DIM)
                scores = scores_of(q2[:, head], k2[:, head], t * tile)
                most = jnp.max(scores, axis=-1, keepdims=True)
                weights = jnp.exp(scores - most)
                total = jnp.sum(weights, axis=-1, keepdims=True)
                mixed.append(dot((weights / total).astype(jnp.bfloat16), v2[:, head]))
                stats.append(jnp.broadcast_to(most + jnp.log(total), (tile, HEAD_DIM)))
            attended[here_t, lanes] = jnp.concatenate(mixed, axis=1).astype(jnp.bfloat16)
            logs[here_t, lanes] = jnp.concatenate(stats, axis=1)
            return 0

        lax.fori_loop(0, width // pair, heads, 0)
        terms[here_t, :] = dot(attended[here_t, :], w_out[...]).astype(jnp.bfloat16)
        scatter.side(t).start()
    turn_gate.await_far()
    turn_gate.pass_on()
    for t in range(chips):
        scatter.cross(t)
    for step in range(1, chips):
        scatter.step(step)
        if step == 1:
            turn_gate.pass_far()
            turn_up.await_far()
            turn_up.pass_on()
        if step < chips - 1:
            third.step(step)
        if step == 1:
            turn_up.pass_far()
    scatter.finish(after_attn)
    after_attn[...] += tokens[...].astype(jnp.float32)
    after = after_attn[...]
    factor = lax.rsqrt(jnp.mean(after * after, axis=-1, keepdims=True) + eps_norm)
    for j in range(model // share):
        at = pl.ds(j * share, share)
        normed = after_attn[:, at] * factor
        lowered_two[here, at] = (normed * gains[j, 1:2, :]).astype(jnp.bfloat16)
    second = Gather(place, lowered_two, block, two_at)
    second.start()
    third.step(chips - 1)
    keep_cot.wait()
    third.finish()
    load(cotangents, place.nearest(0), 0).start()
    turn_gate.finish()
    turn_up.finish()
    load_down.wait()

    def stores(k, t):
        slot = k % 2
        pairs = (
            (tile_hidden, hidden_out),
            (tile_gate, grad_gate_out),
            (tile_up, grad_up_out),
            (tile_terms, terms_out),
            (tile_sums, sums_out),
        )
        return [
            pltpu.make_async_copy(held.at[slot], rows_at(out, t, tile), store_sems.at[i, slot])
            for i, (held, out) in enumerate(pairs)
        ]

    for k in range(chips):
        t, slot = place.nearest(k), k % 2
        if k > 0:
            second.step(k)
        second.across(t)
        if k + 1 < chips:
            load(cotangents, place.nearest(k + 1), (k + 1) % 2).start()
        load(cotangents, t, slot).wait()
        if k > 1:
            for store in stores(k - 2, place.nearest(k - 2)):
                store.wait()
        rows = lowered_two[pl.ds(pl.multiple_of(t * tile, tile), tile), :]
        gate = dot(rows, slab_gate[...])
        up = dot(rows, slab_up[...])
        grad_hidden = contract_last(tiles[slot], held_down[...])
        sigmoid = jax.nn.sigmoid(gate)
        silu = gate * sigmoid
        hidden = (silu * up).astype(jnp.bfloat16)
        grad_gate = (grad_hidden * up * sigmoid * (1.0 + gate * (1.0 - sigmoid))).astype(jnp.bfloat16)
        grad_up = (grad_hidden * silu).astype(jnp.bfloat16)
        tile_hidden[slot] = hidden
        tile_gate[slot] = grad_gate
        tile_up[slot] = grad_up
        got = contract_last(grad_gate, slab_gate[...]) + contract_last(grad_up, slab_up[...])
        tile_terms[slot] = got.astype(jnp.bfloat16)
        tile_sums[slot] = dot(hidden, held_down[...]).astype(jnp.bfloat16)
        for store in stores(k, t):
            store.start()
    keep_two = pltpu.make_async_copy(lowered_two, lowered_two_out, copy_sems.at[4])
    keep_two.start()
    second.drain()
    scatter.drain()
    for turn in turns + [turn_gate, turn_up]:
        turn.drain()
    await_bytes(gains.at[pl.ds(0, place.fsdp - 1)], gain_out)
    keep_slab.wait()
    for k in range(max(chips - 2, 0), chips):
        for store in stores(k, place.nearest(k)):
            store.wait()
    keep_two.wait()


def front(
    tokens, cotangent, gain_one, gain_two, w_query, w_key, w_value, w_out, w_gate, w_up, w_down, cosine, sine
):
    fsdp = lax.axis_size("fsdp")
    chips = fsdp // 2
    block, model = tokens.shape
    rows, width, wide = fsdp * block, w_query.shape[1] // fsdp, w_gate.shape[1] // fsdp
    tile = 2 * block
    share = gain_one.shape[0]
    low, full = jnp.bfloat16, jnp.float32
    hbm, vmem = pl.BlockSpec(memory_space=pl.ANY), pl.BlockSpec(memory_space=pltpu.VMEM)
    shape = jax.ShapeDtypeStruct
    dma = pltpu.SemaphoreType.DMA
    return pl.pallas_call(
        front_kernel,
        in_specs=[vmem] * 4 + [hbm] * 3 + [vmem] + [hbm] * 3 + [vmem] * 2,
        out_specs=[hbm] * 9 + [vmem] * 7,
        out_shape=[
            shape((rows, model), low),
            shape((rows, model), low),
            shape((rows, model), low),
            shape((3 * model, width), low),
            shape((rows, wide), low),
            shape((rows, wide), low),
            shape((rows, wide), low),
            shape((rows, model), low),
            shape((rows, model), low),
            shape((rows, width), low),
            shape((rows, width), low),
            shape((rows, width), low),
            shape((rows, width), low),
            shape((rows, width), full),
            shape((block, model), full),
            shape((fsdp, 8, share), full),
        ],
        scratch_shapes=[
            pltpu.VMEM((block, model), low),
            pltpu.VMEM((2, tile, model), low),
            pltpu.VMEM((rows, model), low),
            pltpu.VMEM((3 * model, width), low),
            pltpu.VMEM((model, wide), low),
            pltpu.VMEM((model, wide), low),
            pltpu.VMEM((wide, model), low),
            pltpu.VMEM((rows, model), low),
            pltpu.VMEM((chips * block, model), low),
            pltpu.VMEM((chips + 1, block, model), low),
            pltpu.VMEM((2, tile, wide), low),
            pltpu.VMEM((2, tile, wide), low),
            pltpu.VMEM((2, tile, wide), low),
            pltpu.VMEM((2, tile, model), low),
            pltpu.VMEM((2, tile, model), low),
            pltpu.VMEM((8, share), full),
            dma(()),
            dma(()),
            dma((5,)),
            dma((2,)),
            dma((5, 2)),
        ]
        + line_sems(chips) * 3
        + scatter_sems(chips)
        + turn_sems() * 5,
        compiler_params=pltpu.CompilerParams(
            collective_id=0, has_side_effects=True, vmem_limit_bytes=VMEM_LIMIT
        ),
        name="front",
    )(
        tokens,
        cotangent,
        gain_one,
        gain_two,
        w_query,
        w_key,
        w_value,
        w_out,
        w_gate,
        w_up,
        w_down,
        cosine,
        sine,
    )


class Reduce:
    def __init__(self, place, part, first, second, sems):
        self.p, self.part, self.first, self.second, self.sems = place, part, first, second, sems
        self.half = part.shape[0] // 2

    def rows(self, half):
        return pl.ds(half * self.half, self.half)

    def sent(self, half, to):
        if half == 0:
            return self.part.at[self.rows(0), :, to]
        return self.part.at[self.rows(1), to]

    def own(self, half):
        return self.sent(half, self.p.b if half == 0 else self.p.a)

    def start(self, half):
        for k in range(1, self.p.counts[half][0]):
            to, replica = self.p.peer(half, 0, k)
            remote(
                self.sent(half, to),
                self.first[half].at[k - 1],
                self.sems.at[half, 0],
                self.sems.at[half, 1],
                replica=replica,
            ).start()

    def exchange(self):
        for half in range(2):
            own, arrived = self.own(half), self.first[half]
            await_bytes(arrived, self.sems.at[half, 1])

            def add(n, _, own=own, arrived=arrived):
                for m in range(own.shape[1]):
                    total = own[n, m].astype(jnp.float32)
                    for k in range(arrived.shape[0]):
                        total += arrived[k, n, m].astype(jnp.float32)
                    own[n, m] = total.astype(own.dtype)
                return 0

            lax.fori_loop(0, self.half, add, 0)
            for k in range(1, self.p.counts[half][1]):
                to, replica = self.p.peer(half, 1, k)
                remote(
                    own.at[:, to],
                    self.second[half].at[k - 1],
                    self.sems.at[half, 2],
                    self.sems.at[half, 3],
                    replica=replica,
                ).start()

    def total(self):
        for half in range(2):
            own, arrived = self.held(half), self.second[half]
            await_bytes(arrived, self.sems.at[half, 3])

            def add(n, _, own=own, arrived=arrived):
                total = own[n].astype(jnp.float32)
                for k in range(arrived.shape[0]):
                    total += arrived[k, n].astype(jnp.float32)
                own[n] = total.astype(own.dtype)
                return 0

            lax.fori_loop(0, self.half, add, 0)

    def held(self, half):
        return self.part.at[self.rows(half), self.p.a, self.p.b]

    def piece(self, n):
        return self.part.at[n, self.p.a, self.p.b]

    def drain(self):
        for half in range(2):
            await_bytes(self.first[half], self.sems.at[half, 0])
            await_bytes(self.second[half], self.sems.at[half, 2])


def reduce_scratch(n, high, wide, rows, columns):
    low = functools.partial(pltpu.VMEM, dtype=jnp.bfloat16)
    half = n // 2
    return [
        low((n, high, wide, rows, columns)),
        low((wide - 1, half, high, rows, columns)),
        low((high - 1, half, wide, rows, columns)),
        low((high - 1, half, rows, columns)),
        low((wide - 1, half, rows, columns)),
        pltpu.SemaphoreType.DMA((2, 4)),
    ]


def reducer(place, refs):
    part, first_a, first_b, second_a, second_b, sems = refs
    return Reduce(place, part, (first_a, first_b), (second_a, second_b), sems)


class Spread:
    def __init__(self, place, piece, out, sems, turned):
        self.p, self.piece, self.out, self.sems, self.turned = place, piece, out, sems, turned

    def start(self):
        p = self.p
        if self.turned:
            count = self.out.shape[0]
            width = self.out.shape[-1] // p.fsdp
            columns = pl.ds(pl.multiple_of(p.me * width, width), width)

            def pairs(to):
                ref = self.piece(to)
                return [
                    (ref.at[:, pl.ds(i * width, width)], self.out.at[i, p.a, p.b, :, columns])
                    for i in range(count)
                ]

            def send(k, _):
                to = lax.rem(p.me + k, p.fsdp)
                for ref, target in pairs(to):
                    remote(ref, target, self.sems.at[0, 0], self.sems.at[0, 1], fsdp=to).start()
                return 0

            lax.fori_loop(1, p.fsdp, send, 0)
            for ref, target in pairs(p.me):
                pltpu.make_async_copy(ref, target, self.sems.at[0, 1]).start()
        else:
            for half in range(2):
                pltpu.make_async_copy(
                    self.piece(half), self.out.at[half, p.a, p.b], self.sems.at[half, 1]
                ).start()

    def placed(self, half, rows):
        a, b = rows
        if self.turned:
            width = self.out.shape[-1] // 2
            return self.out.at[:, a, b, :, pl.ds(half * width, width)]
        return self.out.at[half, a, b]

    def spread(self):
        p = self.p
        if self.turned:
            await_bytes(self.out.at[:, p.a, p.b], self.sems.at[0, 1])
        for half in range(2):
            ref = self.placed(half, (p.a, p.b))
            src = ref if self.turned else self.piece(half)
            for k in range(1, p.counts[half][1]):
                _, replica = p.peer(half, 1, k)
                remote(src, ref, self.sems.at[half, 2], self.sems.at[half, 3], replica=replica).start()

    def spread_bytes(self, half):
        some = pl.ds(0, self.p.counts[half][1] - 1)
        return self.placed(half, (some, 0) if half == 0 else (0, some))

    def widen(self):
        p = self.p
        for half in range(2):
            if not self.turned:
                await_bytes(self.placed(half, (p.a, p.b)), self.sems.at[half, 1])
            await_bytes(self.spread_bytes(half), self.sems.at[half, 3])
            every = pl.ds(0, p.counts[half][1])
            ref = self.placed(half, (every, p.b) if half == 0 else (p.a, every))
            for k in range(1, p.counts[half][0]):
                _, replica = p.peer(half, 0, k)
                remote(ref, ref, self.sems.at[half, 4], self.sems.at[half, 5], replica=replica).start()

    def widen_bytes(self, half):
        counts = self.p.counts[half]
        every, some = pl.ds(0, counts[1]), pl.ds(0, counts[0] - 1)
        return self.placed(half, (every, some) if half == 0 else (some, every))

    def finish(self):
        p = self.p
        for half in range(2):
            await_bytes(self.widen_bytes(half), self.sems.at[half, 5])
            await_bytes(self.spread_bytes(half), self.sems.at[half, 2])
            await_bytes(self.widen_bytes(half), self.sems.at[half, 4])
        if self.turned:
            width = self.out.shape[-1] // p.fsdp
            await_bytes(
                self.out.at[:, p.a, p.b, :, pl.ds(0, (p.fsdp - 1) * width)], self.sems.at[0, 0]
            )


def spread_sems():
    return [pltpu.SemaphoreType.DMA((2, 6))]


def norm_back(values, gain_row, gains, grad, carried, result, gain_terms):
    block, model = values.shape
    share = gains.shape[2]
    held = values[...].astype(jnp.float32)
    factor = lax.rsqrt(jnp.mean(held * held, axis=-1, keepdims=True) + eps_norm)
    dots = jnp.zeros((block, 1), jnp.float32)
    for j in range(model // share):
        at = pl.ds(j * share, share)
        normed = values[:, at].astype(jnp.float32) * factor
        product = grad[:, at] * normed
        gain_terms[j, gain_row : gain_row + 1, :] = jnp.sum(product, axis=0, keepdims=True)
        dots += jnp.sum(product * gains[j, gain_row : gain_row + 1, :], axis=-1, keepdims=True)
    dots = dots / model
    for j in range(model // share):
        at = pl.ds(j * share, share)
        normed = values[:, at].astype(jnp.float32) * factor
        scaled = grad[:, at] * gains[j, gain_row : gain_row + 1, :]
        result[:, at] = carried[:, at].astype(jnp.float32) + factor * (scaled - normed * dots)


def weigh_kernel(
    cotangent,
    after_attn,
    gains,
    terms_in,
    lowered_two,
    cotangents,
    hidden_in,
    grad_gate_in,
    grad_up_in,
    w_out,
    queries,
    keys,
    values,
    logs,
    cosine,
    sine,
    grad_after,
    gain_terms,
    grads,
    branch,
    sum_down,
    sum_gate,
    sum_up,
    tokens_held,
    hidden,
    grad_gate,
    grad_up,
    terms,
    across,
    slots,
    summed,
    low,
    grad_low,
    grad_key,
    grad_value,
    load_sems,
    store_sems,
    *rest,
):
    place = Place()
    chips, block = place.chips, cotangent.shape[0]
    model = cotangent.shape[1]
    tile = 2 * block
    scatter_at, gather_at = rest[:6], rest[6:12]
    down, gate, up = [reducer(place, rest[12 + 6 * i : 18 + 6 * i]) for i in range(3)]

    def load(t):
        at = pl.ds(t * tile, tile)
        return pltpu.make_async_copy(terms_in.at[at], terms.at[at], load_sems.at[t])

    loads = [
        pltpu.make_async_copy(source, target, load_sems.at[chips + i])
        for i, (source, target) in enumerate(
            (
                (cotangents, tokens_held),
                (hidden_in, hidden),
                (grad_gate_in, grad_gate),
                (grad_up_in, grad_up),
                (lowered_two, tokens_held),
            )
        )
    ]
    for t in range(chips):
        load(t).start()
    for copy in loads[:4]:
        copy.start()
    place.enter()
    scatter = Scatter(place, terms, across, slots, block, scatter_at)
    for t in range(chips):
        load(t).wait()
        scatter.side(t).start()
    gain_terms[...] = jnp.zeros_like(gain_terms)
    loads[0].wait()
    loads[1].wait()
    _, high, wide, thin, _ = down.part.shape
    columns = min(tile, hidden.shape[1])
    for i in range(0, hidden.shape[1], columns):
        got = contract_first(hidden[:, i : i + columns], tokens_held[...]).astype(jnp.bfloat16)
        for m in range(0, columns, thin):
            n = (i + m) // thin
            down.part[n // (high * wide), n // wide % high, n % wide] = got[m : m + thin, :]
        if 2 * (i + columns) == hidden.shape[1]:
            down.start(0)
    loads[4].start()
    down.start(1)
    for t in range(chips):
        scatter.cross(t)
    scatter.step(1)
    loads[4].wait()

    def weigh(reduce, grads):
        share = model // place.fsdp

        def rows(j, _):
            left = tokens_held[:, pl.ds(pl.multiple_of(j * share, share), share)]
            got = contract_first(left, grads[...]).astype(jnp.bfloat16)
            reduce.part[j] = got.reshape(reduce.part.shape[1:])
            return 0

        for half in range(2):
            lax.fori_loop(half * chips, (half + 1) * chips, rows, 0)
            reduce.start(half)

    loads[2].wait()
    weigh(gate, grad_gate)
    if chips > 2:
        scatter.step(2)
    loads[3].wait()
    weigh(up, grad_up)
    for step in range(3, chips):
        scatter.step(step)
    scatter.finish(summed)
    norm_back(after_attn, 1, gains, summed, cotangent, grad_after, gain_terms)
    low[...] = grad_after[...].astype(jnp.bfloat16)
    here = pl.ds(pl.multiple_of(place.me * block, block), block)
    gather = Gather(place, branch, block, gather_at, low)
    gather.start()
    keep = pltpu.make_async_copy(low, branch.at[here], store_sems.at[0])
    keep.start()
    scatter.drain()
    down.exchange()
    for step in range(1, chips):
        gather.step(step)
        if step == 1:
            gate.exchange()
        if step == max(chips - 2, 1):
            up.exchange()
    keep.wait()
    gather.finish()
    fetch = pltpu.make_async_copy(branch, tokens_held, load_sems.at[0])
    fetch.start()
    down.total()
    fetch.wait()

    def attend_rows(t, _):
        at = pl.ds(pl.multiple_of(t * tile, tile), tile)
        grad_low[at, :] = contract_last(tokens_held[at, :], w_out[...]).astype(jnp.bfloat16)
        return 0

    lax.fori_loop(0, chips, attend_rows, 0)
    width = queries.shape[1]
    scale = HEAD_DIM**-0.5
    grad_key[...] = jnp.zeros_like(grad_key)
    grad_value[...] = jnp.zeros_like(grad_value)
    pair = 2 * HEAD_DIM
    height = tile * 1024 // max(queries.shape[0], 1024)
    for first in range(0, queries.shape[0], height):
        rows, seen = pl.ds(first, height), pl.ds(0, first + height)

        def heads(h, _, first=first, rows=rows, seen=seen):
            lanes = pl.ds(pl.multiple_of(h * pair, pair), pair)
            q2, g2, log2 = queries[rows, lanes], grad_low[rows, lanes], logs[rows, lanes]
            k2, v2 = keys[seen, lanes], values[seen, lanes]
            for_queries, for_keys, for_values = [], [], []
            for at in (0, HEAD_DIM):
                head = slice(at, at + HEAD_DIM)
                q, g, k = q2[:, head], g2[:, head], k2[:, head]
                weights = jnp.exp(scores_of(q, k, first) - log2[:, at : at + 1])
                grad_weights = contract_last(g, v2[:, head])
                delta = jnp.sum(weights * grad_weights, axis=-1, keepdims=True)
                grad_scores = (weights * (grad_weights - delta)).astype(jnp.bfloat16)
                for_queries.append(dot(grad_scores, k))
                for_keys.append(contract_first(grad_scores, q))
                for_values.append(contract_first(weights.astype(jnp.bfloat16), g))
            got = jnp.concatenate(for_queries, axis=1) * scale
            got = got * cosine[rows, :] - partner(got) * sine[rows, :]
            grads[rows, lanes] = got.astype(jnp.bfloat16)
            grad_key[seen, lanes] += jnp.concatenate(for_keys, axis=1) * scale
            grad_value[seen, lanes] += jnp.concatenate(for_values, axis=1)
            return 0

        lax.fori_loop(0, width // pair, heads, 0)

    def turn_keys(t, _):
        at = pl.ds(pl.multiple_of(t * tile, tile), tile)
        for j in range(0, width, pair):
            got = grad_key[at, j : j + pair]
            got = got * cosine[at, :] - partner(got) * sine[at, :]
            grads[at, width + j : width + j + pair] = got.astype(jnp.bfloat16)
        grads[at, 2 * width :] = grad_value[at, :].astype(jnp.bfloat16)
        return 0

    lax.fori_loop(0, chips, turn_keys, 0)
    stores = []
    for i, (reduce, out) in enumerate(((down, sum_down), (gate, sum_gate), (up, sum_up))):
        if i > 0:
            reduce.total()
        for half in range(2):
            store = pltpu.make_async_copy(
                reduce.held(half), out.at[reduce.rows(half)], store_sems.at[1 + 2 * i + half]
            )
            store.start()
            stores.append(store)
    for reduce in (down, gate, up):
        reduce.drain()
    for store in stores:
        store.wait()


def weigh(
    cotangent,
    after_attn,
    gains,
    terms,
    lowered_two,
    cotangents,
    hidden,
    grad_gate,
    grad_up,
    w_out,
    queries,
    keys,
    values,
    logs,
    cosine,
    sine,
):
    fsdp, replicas = lax.axis_size("fsdp"), lax.axis_size("replica")
    chips, high, wide = fsdp // 2, 2, replicas // 2
    block, model = cotangent.shape
    rows, columns = hidden.shape
    width = queries.shape[1]
    share = gains.shape[2]
    low, full = jnp.bfloat16, jnp.float32
    hbm, vmem = pl.BlockSpec(memory_space=pl.ANY), pl.BlockSpec(memory_space=pltpu.VMEM)
    shape = jax.ShapeDtypeStruct
    down_piece = (2, high, wide, columns // (2 * replicas), model)
    wide_piece = (fsdp, high, wide, share // replicas, columns)
    dma = pltpu.SemaphoreType.DMA
    return pl.pallas_call(
        weigh_kernel,
        in_specs=[vmem] * 3 + [hbm] * 6 + [vmem] * 7,
        out_specs=[vmem] * 3 + [hbm] * 4,
        out_shape=[
            shape((block, model), full),
            shape((fsdp, 8, share), full),
            shape((rows, 3 * width), low),
            shape((rows, model), low),
            shape((2,) + down_piece[3:], low),
            shape((fsdp,) + wide_piece[3:], low),
            shape((fsdp,) + wide_piece[3:], low),
        ],
        scratch_shapes=[
            pltpu.VMEM((rows, model), low),
            pltpu.VMEM((rows, columns), low),
            pltpu.VMEM((rows, columns), low),
            pltpu.VMEM((rows, columns), low),
            pltpu.VMEM((rows, model), low),
            pltpu.VMEM((chips * block, model), low),
            pltpu.VMEM((chips + 1, block, model), low),
            pltpu.VMEM((block, model), full),
            pltpu.VMEM((block, model), low),
            pltpu.VMEM((rows, width), low),
            pltpu.VMEM((rows, width), full),
            pltpu.VMEM((rows, width), full),
            dma((chips + 5,)),
            dma((7,)),
        ]
        + scatter_sems(chips)
        + line_sems(chips)
        + reduce_scratch(*down_piece)
        + reduce_scratch(*wide_piece)
        + reduce_scratch(*wide_piece),
        compiler_params=pltpu.CompilerParams(
            collective_id=1, has_side_effects=True, vmem_limit_bytes=VMEM_LIMIT
        ),
        name="weigh",
    )(
        cotangent,
        after_attn,
        gains,
        terms,
        lowered_two,
        cotangents,
        hidden,
        grad_gate,
        grad_up,
        w_out,
        queries,
        keys,
        values,
        logs,
        cosine,
        sine,
    )


def back_kernel(
    tokens,
    gains,
    grad_after,
    gain_terms_in,
    after_attn,
    sums,
    sum_down,
    sum_gate,
    sum_up,
    branch_in,
    lowered_one,
    slab_qkv,
    attended,
    grads,
    outputs,
    grad_tokens,
    gain_out,
    out_down,
    out_gate,
    out_up,
    out_qkv,
    out_out,
    terms,
    across,
    slots,
    branch,
    summed,
    gain_terms,
    gain_slots,
    gain_sums,
    gain_sems,
    load_sems,
    *rest,
):
    place = Place()
    chips, block = place.chips, tokens.shape[0]
    model, width = tokens.shape[1], attended.shape[1]
    share = gains.shape[2]
    tile = 2 * block
    scatter_at, rest = rest[:6], rest[6:]
    down = Spread(place, lambda n: sum_down.at[n], out_down, rest[0], False)
    gate = Spread(place, lambda n: sum_gate.at[n], out_gate, rest[1], True)
    up = Spread(place, lambda n: sum_up.at[n], out_up, rest[2], True)
    qkv, out = reducer(place, rest[5:11]), reducer(place, rest[11:17])
    qkv_spread = Spread(place, qkv.piece, out_qkv, rest[3], True)
    out_spread = Spread(place, out.piece, out_out, rest[4], False)
    load = pltpu.make_async_copy(lowered_one, branch, load_sems.at[0])
    load.start()
    place.enter()
    down.start()
    down.spread()
    gate.start()
    up.start()
    load.wait()

    def weigh_rows(j, _):
        left = branch[:, pl.ds(pl.multiple_of(j * share, share), share)]
        got = contract_first(left, grads[...]).astype(jnp.bfloat16)
        qkv.part[j] = got.reshape(qkv.part.shape[1:])
        return 0

    for half in range(2):
        lax.fori_loop(half * chips, (half + 1) * chips, weigh_rows, 0)
        qkv.start(half)
    reload = pltpu.make_async_copy(branch_in, branch, load_sems.at[1])
    reload.start()
    scatter = Scatter(place, terms, across, slots, block, scatter_at)

    def back_rows(t, _):
        at = pl.ds(pl.multiple_of(t * tile, tile), tile)
        got = contract_last(grads[at, :width], slab_qkv[:model, :])
        got += contract_last(grads[at, width : 2 * width], slab_qkv[model : 2 * model, :])
        got += contract_last(grads[at, 2 * width :], slab_qkv[2 * model :, :])
        terms[at, :] = got.astype(jnp.bfloat16)
        return 0

    lax.fori_loop(0, chips, back_rows, 0)
    for t in range(chips):
        scatter.side(t).start()
    down.widen()
    reload.wait()
    _, high, wide, thin, columns = out.part.shape
    for half in range(2):
        for at in range(0, columns, 512):
            got = contract_first(
                attended[...], branch[:, half * columns + at : half * columns + at + 512]
            ).astype(jnp.bfloat16)
            out.part[half, :, :, :, at : at + 512] = got.reshape(high, wide, thin, 512)
    out.start(0)
    out.start(1)
    gate.spread()
    for t in range(chips):
        scatter.cross(t)
    for step in range(1, chips):
        scatter.step(step)
        if step == 1:
            qkv.exchange()
            up.spread()
        if step == max(chips - 2, 1):
            out.exchange()
    gate.widen()
    out.total()
    out_spread.start()
    out_spread.spread()
    scatter.finish(summed)
    gain_terms[...] = gain_terms_in[...]
    norm_back(tokens, 0, gains, summed, grad_after, grad_tokens, gain_terms)

    def send_gain(k, _):
        to = lax.rem(place.me + k, place.fsdp)
        remote(
            gain_terms.at[to], gain_slots.at[place.me], gain_sems.at[0], gain_sems.at[1], fsdp=to
        ).start()
        return 0

    lax.fori_loop(1, place.fsdp, send_gain, 0)
    gain_slots[place.me] = gain_terms[place.me]
    scatter.drain()
    load_sums = pltpu.make_async_copy(sums, terms, load_sems.at[0])
    load_sums.start()
    qkv.total()
    qkv_spread.start()
    await_bytes(gain_slots.at[pl.ds(0, place.fsdp - 1)], gain_sems.at[1])
    gain_sums[place.replica] = jnp.sum(gain_slots[...], axis=0)

    def send_sum(k, _):
        ref = gain_sums.at[place.replica]
        to = lax.rem(place.replica + k, place.replicas)
        remote(ref, ref, gain_sems.at[2], gain_sems.at[3], replica=to).start()
        return 0

    lax.fori_loop(1, place.replicas, send_sum, 0)

    load_sums.wait()
    for t in range(chips):
        scatter.side(t).start()
    up.widen()
    for t in range(chips):
        scatter.cross(t)
    scatter.step(1)
    qkv_spread.spread()
    for step in range(2, chips):
        scatter.step(step)
        if step == 2:
            out_spread.widen()
    if chips == 2:
        out_spread.widen()
    scatter.finish(summed)
    outputs[...] = (summed[...] + after_attn[...]).astype(outputs.dtype)
    qkv_spread.widen()
    await_bytes(gain_sums.at[pl.ds(0, place.replicas - 1)], gain_sems.at[3])
    gain_out[...] = jnp.sum(gain_sums[...], axis=0)
    await_bytes(gain_slots.at[pl.ds(0, place.fsdp - 1)], gain_sems.at[0])
    await_bytes(gain_sums.at[pl.ds(0, place.replicas - 1)], gain_sems.at[2])
    scatter.drain()
    qkv.drain()
    out.drain()
    for spread in (down, gate, up, out_spread, qkv_spread):
        spread.finish()


def back(
    tokens,
    gains,
    grad_after,
    gain_terms,
    after_attn,
    sums,
    sum_down,
    sum_gate,
    sum_up,
    branch,
    lowered_one,
    slab_qkv,
    attended,
    grads,
):
    fsdp, replicas = lax.axis_size("fsdp"), lax.axis_size("replica")
    chips, high, wide = fsdp // 2, 2, replicas // 2
    block, model = tokens.shape
    rows, width = attended.shape
    share = gains.shape[2]
    low, full = jnp.bfloat16, jnp.float32
    hbm, vmem = pl.BlockSpec(memory_space=pl.ANY), pl.BlockSpec(memory_space=pltpu.VMEM)
    shape = jax.ShapeDtypeStruct
    thin = share // replicas
    columns = sum_gate.shape[-1]
    qkv_piece = (fsdp, high, wide, thin, 3 * width)
    out_piece = (2, high, wide, width // replicas, model // 2)
    dma = pltpu.SemaphoreType.DMA
    return pl.pallas_call(
        back_kernel,
        in_specs=[vmem] * 5 + [hbm] * 6 + [vmem] * 3,
        out_specs=[vmem] * 3 + [hbm] * 5,
        out_shape=[
            shape((block, model), low),
            shape((block, model), full),
            shape((8, share), full),
            shape((2, high, wide) + sum_down.shape[1:], low),
            shape((1, high, wide, thin, fsdp * columns), low),
            shape((1, high, wide, thin, fsdp * columns), low),
            shape((3, high, wide, thin, fsdp * width), low),
            shape(out_piece, low),
        ],
        scratch_shapes=[
            pltpu.VMEM((rows, model), low),
            pltpu.VMEM((chips * block, model), low),
            pltpu.VMEM((chips + 1, block, model), low),
            pltpu.VMEM((rows, model), low),
            pltpu.VMEM((block, model), full),
            pltpu.VMEM((fsdp, 8, share), full),
            pltpu.VMEM((fsdp, 8, share), full),
            pltpu.VMEM((replicas, 8, share), full),
            dma((4,)),
            dma((2,)),
        ]
        + scatter_sems(chips)
        + spread_sems() * 5
        + reduce_scratch(*qkv_piece)
        + reduce_scratch(*out_piece),
        compiler_params=pltpu.CompilerParams(
            collective_id=2, has_side_effects=True, vmem_limit_bytes=VMEM_LIMIT
        ),
        name="back",
    )(
        tokens,
        gains,
        grad_after,
        gain_terms,
        after_attn,
        sums,
        sum_down,
        sum_gate,
        sum_up,
        branch,
        lowered_one,
        slab_qkv,
        attended,
        grads,
    )


def widen_kernel(
    down,
    gate,
    up,
    qkv,
    out,
    outputs_in,
    tokens_in,
    gains,
    w_down,
    w_gate,
    w_up,
    w_query,
    w_key,
    w_value,
    w_out,
    outputs,
    grad_tokens,
    gain_one,
    gain_two,
):
    w_down[...] = down[...].astype(jnp.float32)
    w_gate[...] = gate[...].astype(jnp.float32)
    w_up[...] = up[...].astype(jnp.float32)
    for i, ref in enumerate((w_query, w_key, w_value)):
        ref[...] = qkv[i].astype(jnp.float32)
    half = out.shape[2]
    for i in range(2):
        w_out[:, i * half : (i + 1) * half] = out[i].astype(jnp.float32)
    outputs[...] = outputs_in[...]
    grad_tokens[...] = tokens_in[...]
    gain_one[...] = gains[0, :]
    gain_two[...] = gains[1, :]


def widen(down, gate, up, qkv, out, outputs, grad_tokens, gains):
    steps = min(16, gate.shape[0] // 16)
    token_steps = outputs.shape[0] // 16
    full = jnp.float32

    def rows(array):
        return pl.BlockSpec((array.shape[0] // steps, array.shape[1]), lambda i: (i, 0))

    def tokens(array):
        return pl.BlockSpec(
            (array.shape[0] // token_steps, array.shape[1]), lambda i: (jnp.minimum(i, token_steps - 1), 0)
        )

    def stacked(array):
        return pl.BlockSpec((array.shape[0], array.shape[1] // steps, array.shape[2]), lambda i: (0, i, 0))

    like = [down, gate, up, qkv[0], qkv[0], qkv[0]]
    shapes = [jax.ShapeDtypeStruct(array.shape, full) for array in like]
    shapes.append(jax.ShapeDtypeStruct((out.shape[1], 2 * out.shape[2]), full))
    row = jax.ShapeDtypeStruct(gains.shape[1:], full)
    whole = pl.BlockSpec(gains.shape, lambda i: (0, 0))
    line = pl.BlockSpec(gains.shape[1:], lambda i: (0,))
    return pl.pallas_call(
        widen_kernel,
        grid=(steps,),
        in_specs=[rows(down), rows(gate), rows(up), stacked(qkv), stacked(out)]
        + [tokens(outputs), tokens(grad_tokens), whole],
        out_specs=[rows(shape) for shape in shapes]
        + [tokens(outputs), tokens(grad_tokens), line, line],
        out_shape=shapes
        + [jax.ShapeDtypeStruct(array.shape, array.dtype) for array in (outputs, grad_tokens)]
        + [row, row],
        compiler_params=pltpu.CompilerParams(vmem_limit_bytes=VMEM_LIMIT),
        name="widen",
    )(down, gate, up, qkv, out, outputs, grad_tokens, gains)


def local(
    tokens, attn_gain, w_query, w_key, w_value, w_out, ffn_gain, w_gate, w_up, w_down, cotangent
):
    cosine, sine = rope_tables(tokens.shape[0] * lax.axis_size("fsdp"))
    (
        lowered_one,
        lowered_two,
        cotangents,
        slab_qkv,
        hidden,
        grad_gate,
        grad_up,
        terms,
        sums,
        queries,
        keys,
        values,
        attended,
        logs,
        after_attn,
        gains,
    ) = front(
        tokens,
        cotangent,
        attn_gain,
        ffn_gain,
        w_query,
        w_key,
        w_value,
        w_out,
        w_gate,
        w_up,
        w_down,
        cosine,
        sine,
    )
    grad_after, gain_terms, grads, branch, sum_down, sum_gate, sum_up = weigh(
        cotangent,
        after_attn,
        gains,
        terms,
        lowered_two,
        cotangents,
        hidden,
        grad_gate,
        grad_up,
        w_out,
        queries,
        keys,
        values,
        logs,
        cosine,
        sine,
    )
    outputs, grad_tokens, gain_grads, low_down, low_gate, low_up, low_qkv, low_out = back(
        tokens,
        gains,
        grad_after,
        gain_terms,
        after_attn,
        sums,
        sum_down,
        sum_gate,
        sum_up,
        branch,
        lowered_one,
        slab_qkv,
        attended,
        grads,
    )
    (
        grad_w_down,
        grad_w_gate,
        grad_w_up,
        grad_w_query,
        grad_w_key,
        grad_w_value,
        grad_w_out,
        outputs,
        grad_tokens,
        grad_attn_gain,
        grad_ffn_gain,
    ) = widen(
        low_down.reshape(w_down.shape),
        low_gate.reshape(w_gate.shape),
        low_up.reshape(w_up.shape),
        low_qkv.reshape((3,) + w_query.shape),
        low_out.reshape(2, w_out.shape[0], -1),
        outputs,
        grad_tokens,
        gain_grads,
    )
    return (
        outputs,
        grad_tokens,
        grad_attn_gain,
        grad_w_query,
        grad_w_key,
        grad_w_value,
        grad_w_out,
        grad_ffn_gain,
        grad_w_gate,
        grad_w_up,
        grad_w_down,
    )


def solution(mesh):
    rows = P("fsdp", None)
    tokens = P(("replica", "fsdp"), None)
    gain = P("fsdp")
    return jax.shard_map(
        local,
        mesh=mesh,
        in_specs=(tokens, gain, rows, rows, rows, rows, gain, rows, rows, rows, tokens),
        out_specs=(tokens, tokens, gain, rows, rows, rows, rows, gain, rows, rows, rows),
        check_vma=False,
    )
```

```python
import functools

import jax
import jax.numpy as jnp
import numpy as np
from jax import lax
from jax.experimental import pallas as pl
from jax.experimental.pallas import tpu as pltpu
from jax.sharding import PartitionSpec as P

HEAD_DIM = 64

eps_norm = 1e-05
rope_base = 130000.0
masked_score = -1e30


def rope_tables(row_count):
    lane = np.arange(2 * HEAD_DIM) % HEAD_DIM
    halfway = HEAD_DIM // 2
    spacing = ((lane % halfway) * np.float32(2.0) / HEAD_DIM).astype(np.float32)
    frequency = np.power(np.float32(rope_base), -spacing)
    angles = np.arange(row_count, dtype=np.float32)[:, None] * frequency[None, :]
    sign = np.where(lane < halfway, -1.0, 1.0).astype(np.float32)
    return np.cos(angles).astype(np.float32), (np.sin(angles) * sign[None, :]).astype(np.float32)


def dot(left, right):
    return jnp.dot(left, right, preferred_element_type=jnp.float32)


def contract_last(left, right):
    return lax.dot_general(
        left, right, (((1,), (1,)), ((), ())), preferred_element_type=jnp.float32
    )


def contract_first(left, right):
    return lax.dot_general(
        left, right, (((0,), (0,)), ((), ())), preferred_element_type=jnp.float32
    )


def scores_of(queries, keys, first_row):
    rows, columns = queries.shape[0], keys.shape[0]
    scores = contract_last(queries, keys) * HEAD_DIM**-0.5
    at_row = lax.broadcasted_iota(jnp.int32, (rows, columns), 0) + first_row
    at_column = lax.broadcasted_iota(jnp.int32, (rows, columns), 1)
    return jnp.where(at_column <= at_row, scores, masked_score)


MESH = pl.DeviceIdType.MESH
VMEM_LIMIT = 61 * 2**20


def remote(src, dst, send, recv, **where):
    return pltpu.make_async_remote_copy(
        src_ref=src, dst_ref=dst, send_sem=send, recv_sem=recv, device_id=where, device_id_type=MESH
    )


def await_bytes(ref, sem):
    pltpu.make_async_copy(ref, ref, sem).wait()


def rows_at(ref, index, size):
    return ref.at[pl.ds(pl.multiple_of(index * size, size), size)]


class Place:
    def __init__(self):
        self.fsdp, self.replicas = lax.axis_size("fsdp"), lax.axis_size("replica")
        self.me, self.replica = lax.axis_index("fsdp"), lax.axis_index("replica")
        self.chips = self.fsdp // 2
        self.chip, self.core = self.me // 2, self.me % 2
        self.sibling = self.me + 1 - 2 * self.core
        self.high, self.wide = 2, self.replicas // 2
        self.a, self.b = self.replica // self.wide, self.replica % self.wide
        self.counts = ((self.wide, self.high), (self.high, self.wide))
        self.above = self.chip + 1 < self.chips
        self.below = self.chip >= 1

    def peer(self, half, stage, k):
        if half == stage:
            to = lax.rem(self.b + k, self.wide)
            return to, self.a * self.wide + to
        to = lax.rem(self.a + k, self.high)
        return to, to * self.wide + self.b

    def nearest(self, k):
        found = jnp.int32(0)
        for chip in range(self.chips):
            order = sorted(range(self.chips), key=lambda other, chip=chip: (abs(other - chip), other))
            found = found + jnp.where(self.chip == chip, order[k], 0)
        return found

    def enter(self):
        barrier = pltpu.get_barrier_semaphore()

        def greet(k, _):
            to = lax.rem(self.me + k, self.fsdp)
            pl.semaphore_signal(barrier, inc=1, device_id={"fsdp": to}, device_id_type=MESH)
            return 0

        def greet_replica(k, _):
            to = lax.rem(self.replica + k, self.replicas)
            pl.semaphore_signal(barrier, inc=1, device_id={"replica": to}, device_id_type=MESH)
            return 0

        lax.fori_loop(1, self.fsdp, greet, 0)
        lax.fori_loop(1, self.replicas, greet_replica, 0)
        pl.semaphore_wait(barrier, self.fsdp - 1 + self.replicas - 1)


def line_sems(chips):
    return [pltpu.SemaphoreType.DMA((chips,))] * 6


class Gather:
    def __init__(self, place, buf, block, sems, own=None):
        self.p, self.buf, self.block, self.own = place, buf, block, own
        self.up_out, self.up_in, self.down_out, self.down_in, self.side_out, self.side_in = sems

    def held(self, chip):
        return rows_at(self.buf, 2 * chip + self.p.core, self.block)

    def up(self, step):
        ref = self.held(self.p.chip - step + 1)
        src = self.own if step == 1 and self.own is not None else ref
        return remote(src, ref, self.up_out.at[step], self.up_in.at[step], fsdp=self.p.me + 2)

    def down(self, step):
        ref = self.held(self.p.chip + step - 1)
        src = self.own if step == 1 and self.own is not None else ref
        return remote(src, ref, self.down_out.at[step], self.down_in.at[step], fsdp=self.p.me - 2)

    def side(self, chip, src=None):
        ref = self.held(chip)
        src = ref if src is None else src
        return remote(src, ref, self.side_out.at[chip], self.side_in.at[chip], fsdp=self.p.sibling)

    def start(self):
        p = self.p
        pl.when(p.above)(lambda: self.up(1).start())
        pl.when(p.below)(lambda: self.down(1).start())
        self.side(p.chip, self.own).start()

    def step(self, step):
        p = self.p
        from_below, from_above = p.chip - step, p.chip + step

        @pl.when(from_below >= 0)
        def _():
            await_bytes(self.held(from_below), self.up_in.at[step])
            if step + 1 < p.chips:
                pl.when(p.above)(lambda: self.up(step + 1).start())
            self.side(from_below).start()

        @pl.when(from_above < p.chips)
        def _():
            await_bytes(self.held(from_above), self.down_in.at[step])
            if step + 1 < p.chips:
                pl.when(p.below)(lambda: self.down(step + 1).start())
            self.side(from_above).start()

    def across(self, chip):
        await_bytes(rows_at(self.buf, 2 * chip + 1 - self.p.core, self.block), self.side_in.at[chip])

    def drain(self):
        p = self.p
        for step in range(1, p.chips):
            pl.when(jnp.logical_and(p.above, p.chip - step + 1 >= 0))(
                lambda step=step: self.up(step).wait_send()
            )
            pl.when(jnp.logical_and(p.below, p.chip + step - 1 < p.chips))(
                lambda step=step: self.down(step).wait_send()
            )
        for chip in range(p.chips):
            self.side(chip).wait_send()

    def finish(self):
        for chip in range(self.p.chips):
            self.across(chip)
        self.drain()


class Scatter:
    def __init__(self, place, terms, across, slots, block, sems):
        self.p, self.terms, self.across, self.slots, self.block = place, terms, across, slots, block
        self.up_out, self.up_in, self.down_out, self.down_in, self.side_out, self.side_in = sems

    def side(self, chip):
        p = self.p
        return remote(
            rows_at(self.terms, 2 * chip + 1 - p.core, self.block),
            rows_at(self.across, chip, self.block),
            self.side_out.at[chip],
            self.side_in.at[chip],
            fsdp=p.sibling,
        )

    def term(self, chip):
        return rows_at(self.terms, 2 * chip + self.p.core, self.block)

    def up(self, step):
        return remote(
            self.term(self.p.chips - step + self.p.chip),
            self.slots.at[step - self.p.chip - 1],
            self.up_out.at[step],
            self.up_in.at[step],
            fsdp=self.p.me + 2,
        )

    def down(self, step):
        return remote(
            self.term(self.p.chip - self.p.chips + step),
            self.slots.at[step + 1],
            self.down_out.at[step],
            self.down_in.at[step],
            fsdp=self.p.me - 2,
        )

    def add(self, chip, arrived):
        term = self.term(chip)
        term[...] = (term[...].astype(jnp.float32) + arrived[...].astype(jnp.float32)).astype(term.dtype)

    def cross(self, chip):
        arrived = rows_at(self.across, chip, self.block)
        await_bytes(arrived, self.side_in.at[chip])
        self.add(chip, arrived)

    def step(self, step):
        p = self.p
        rising, falling = p.chips - step + p.chip, p.chip - p.chips + step

        @pl.when(jnp.logical_and(p.above, rising < p.chips))
        def _():
            if step > 1:

                @pl.when(p.below)
                def _():
                    arrived = self.slots.at[step - 1 - p.chip]
                    await_bytes(arrived, self.up_in.at[step - 1])
                    self.add(rising, arrived)

            self.up(step).start()

        @pl.when(jnp.logical_and(p.below, falling >= 0))
        def _():
            if step > 1:

                @pl.when(p.above)
                def _():
                    arrived = self.slots.at[step]
                    await_bytes(arrived, self.down_in.at[step - 1])
                    self.add(falling, arrived)

            self.down(step).start()

    def finish(self, total):
        p, last = self.p, self.p.chips - 1
        total[...] = self.term(p.chip)[...].astype(jnp.float32)

        @pl.when(p.below)
        def _():
            await_bytes(self.slots.at[last - p.chip], self.up_in.at[last])
            total[...] += self.slots[last - p.chip].astype(jnp.float32)

        @pl.when(p.above)
        def _():
            await_bytes(self.slots.at[last + 1], self.down_in.at[last])
            total[...] += self.slots[last + 1].astype(jnp.float32)

    def drain(self):
        p = self.p
        for step in range(1, p.chips):
            pl.when(jnp.logical_and(p.above, p.chips - step + p.chip < p.chips))(
                lambda step=step: self.up(step).wait_send()
            )
            pl.when(jnp.logical_and(p.below, p.chip - p.chips + step >= 0))(
                lambda step=step: self.down(step).wait_send()
            )
        for chip in range(p.chips):
            self.side(chip).wait_send()


def scatter_sems(chips):
    dma = pltpu.SemaphoreType.DMA
    return [dma((chips,))] * 6


class Turn:
    def __init__(self, place, weight, slab, first, sems):
        self.p, self.weight, self.slab, self.first = place, weight, slab, first
        self.far_out, self.far_in, self.near_out, self.near_in, self.own, self.passing = sems
        self.height, self.width = weight.shape[0], slab.shape[1]
        self.share = self.height // place.replicas

    def far_rows(self):
        return (self.p.fsdp - 2) * self.share

    def piece(self, block, share):
        at = self.first + block * self.height + share * self.share
        return self.slab.at[pl.ds(pl.multiple_of(at, self.share), self.share)]

    def whole(self, block):
        at = self.first + block * self.height
        return self.slab.at[pl.ds(pl.multiple_of(at, self.height), self.height)]

    def columns(self, to):
        return pl.ds(pl.multiple_of(to * self.width, self.width), self.width)

    def start(self):
        p = self.p

        def send(k, _):
            to = lax.rem(2 * p.chip + 2 + k, p.fsdp)
            share = pl.ds(pl.multiple_of(p.replica * self.share, self.share), self.share)
            remote(
                self.weight.at[share, self.columns(to)],
                self.piece(p.me, p.replica),
                self.far_out,
                self.far_in,
                fsdp=to,
            ).start()
            return 0

        lax.fori_loop(0, p.fsdp - 2, send, 0)
        self.near().start()
        self.mine().start()

    def near(self):
        p = self.p
        return remote(
            self.weight.at[:, self.columns(p.sibling)], self.whole(p.me), self.near_out, self.near_in, fsdp=p.sibling
        )

    def mine(self):
        return pltpu.make_async_copy(self.weight.at[:, self.columns(self.p.me)], self.whole(self.p.me), self.own)

    def await_far(self):
        await_bytes(self.slab.at[pl.ds(0, self.far_rows())], self.far_in)

    def bytes_of(self, pieces):
        return self.slab.at[pl.ds(0, pieces * self.share)]

    def pass_bytes(self, half, stage):
        first, second = self.p.counts[half]
        return self.bytes_of((self.p.chips - 1) * (second - 1 if stage == 0 else second * (first - 1)))

    def send_pieces(self, half, stage, shares):
        p = self.p

        def one(i, _):
            block = lax.rem(2 * p.chip + 2 + 2 * i + half, p.fsdp)
            for share in shares:
                ref = self.piece(block, share)
                for k in range(1, p.counts[half][1 - stage]):
                    _, replica = p.peer(half, 1 - stage, k)
                    remote(
                        ref,
                        ref,
                        self.passing.at[half, 2 * stage],
                        self.passing.at[half, 2 * stage + 1],
                        replica=replica,
                    ).start()
            return 0

        lax.fori_loop(0, p.chips - 1, one, 0)

    def pass_on(self):
        for half in range(2):
            self.send_pieces(half, 0, [self.p.replica])

    def pass_far(self):
        p = self.p
        for half in range(2):
            await_bytes(self.pass_bytes(half, 0), self.passing.at[half, 1])
            if half == 0:
                shares = [a * p.wide + p.b for a in range(p.high)]
            else:
                shares = [p.a * p.wide + b for b in range(p.wide)]
            self.send_pieces(half, 1, shares)

    def finish(self):
        for half in range(2):
            await_bytes(self.pass_bytes(half, 1), self.passing.at[half, 3])
        await_bytes(self.whole(self.p.sibling), self.near_in)
        self.mine().wait()

    def drain(self):
        await_bytes(self.slab.at[pl.ds(0, self.far_rows())], self.far_out)
        self.near().wait_send()
        for half in range(2):
            await_bytes(self.pass_bytes(half, 0), self.passing.at[half, 0])
            await_bytes(self.pass_bytes(half, 1), self.passing.at[half, 2])


def turn_sems():
    return [pltpu.SemaphoreType.DMA(())] * 5 + [pltpu.SemaphoreType.DMA((2, 4))]


def partner(values):
    halfway = HEAD_DIM // 2
    width = values.shape[1]
    lane = lax.broadcasted_iota(jnp.int32, values.shape, 1) % HEAD_DIM
    return jnp.where(
        lane < halfway,
        pltpu.roll(values, width - halfway, axis=1),
        pltpu.roll(values, halfway, axis=1),
    )


def front_kernel(
    tokens,
    cotangent,
    gain_one,
    gain_two,
    w_query,
    w_key,
    w_value,
    w_out,
    w_gate,
    w_up,
    w_down,
    cosine,
    sine,
    lowered_one,
    lowered_two_out,
    cotangents,
    slab_qkv_out,
    hidden_out,
    grad_gate_out,
    grad_up_out,
    terms_out,
    sums_out,
    queries,
    keys,
    values,
    attended,
    logs,
    after_attn,
    gains,
    low,
    tiles,
    lowered_two,
    slab_qkv,
    slab_gate,
    slab_up,
    held_down,
    terms,
    across,
    slots,
    tile_hidden,
    tile_gate,
    tile_up,
    tile_terms,
    tile_sums,
    gain_rows,
    gain_out,
    gain_in,
    copy_sems,
    load_sems,
    store_sems,
    *sems,
):
    place = Place()
    chips, block = place.chips, tokens.shape[0]
    model, width = tokens.shape[1], queries.shape[1]
    share = gain_one.shape[0]
    tile = 2 * block
    one_at, cot_at, two_at, scatter_at = sems[:6], sems[6:12], sems[12:18], sems[18:24]
    turn_at = [sems[24 + 6 * i : 30 + 6 * i] for i in range(5)]
    turns = [
        Turn(place, weight, slab_qkv, i * model, turn_at[i])
        for i, weight in enumerate((w_query, w_key, w_value))
    ]
    turn_gate = Turn(place, w_gate, slab_gate, 0, turn_at[3])
    turn_up = Turn(place, w_up, slab_up, 0, turn_at[4])
    here = pl.ds(pl.multiple_of(place.me * block, block), block)

    gain_rows[...] = jnp.zeros_like(gain_rows)
    gain_rows[0, :] = gain_one[...].astype(jnp.float32)
    gain_rows[1, :] = gain_two[...].astype(jnp.float32)
    load_down = pltpu.make_async_copy(w_down, held_down, copy_sems.at[0])
    load_down.start()
    keep_cot = pltpu.make_async_copy(cotangent, cotangents.at[here], copy_sems.at[1])
    keep_cot.start()
    place.enter()

    def send_gains(k, _):
        to = lax.rem(place.me + k, place.fsdp)
        remote(gain_rows, gains.at[place.me], gain_out, gain_in, fsdp=to).start()
        return 0

    lax.fori_loop(1, place.fsdp, send_gains, 0)
    for turn in turns:
        turn.start()
    gains[place.me] = gain_rows[...]
    inputs = tokens[...].astype(jnp.float32)
    factor = lax.rsqrt(jnp.mean(inputs * inputs, axis=-1, keepdims=True) + eps_norm)
    await_bytes(gains.at[pl.ds(0, place.fsdp - 1)], gain_in)
    for j in range(model // share):
        at = pl.ds(j * share, share)
        normed = tokens[:, at].astype(jnp.float32) * factor
        low[:, at] = (normed * gains[j, 0:1, :]).astype(jnp.bfloat16)
    first = Gather(place, lowered_one, block, one_at, low)
    first.start()
    keep_low = pltpu.make_async_copy(low, lowered_one.at[here], copy_sems.at[2])
    keep_low.start()
    for turn in turns:
        turn.await_far()
        turn.pass_on()
    for step in range(1, chips):
        if step == chips - 1:
            turn_gate.start()
        first.step(step)
        if step == 1:
            for turn in turns:
                turn.pass_far()
    turn_up.start()
    third = Gather(place, cotangents, block, cot_at, cotangent)
    third.start()
    keep_low.wait()
    first.finish()

    def load(source, t, slot):
        return pltpu.make_async_copy(rows_at(source, t, tile), tiles.at[slot], load_sems.at[slot])

    load(lowered_one, 0, 0).start()
    for turn in turns:
        turn.finish()
    keep_slab = pltpu.make_async_copy(slab_qkv, slab_qkv_out, copy_sems.at[3])
    keep_slab.start()
    for t in range(chips):
        if t + 1 < chips:
            load(lowered_one, t + 1, (t + 1) % 2).start()
        load(lowered_one, t, t % 2).wait()
        at = pl.ds(t * tile, tile)
        for i, ref in enumerate((queries, keys, values)):
            out = dot(tiles[t % 2], slab_qkv[i * model : (i + 1) * model, :])
            if i < 2:
                for j in range(0, width, 2 * HEAD_DIM):
                    pair = out[:, j : j + 2 * HEAD_DIM]
                    pair = pair * cosine[at, :] + partner(pair) * sine[at, :]
                    ref[at, j : j + 2 * HEAD_DIM] = pair.astype(jnp.bfloat16)
            else:
                ref[at, :] = out.astype(jnp.bfloat16)
    scatter = Scatter(place, terms, across, slots, block, scatter_at)
    pair = 2 * HEAD_DIM
    for t in range(chips):
        here_t, seen = pl.ds(t * tile, tile), pl.ds(0, (t + 1) * tile)

        def heads(h, _, t=t, here_t=here_t, seen=seen):
            lanes = pl.ds(pl.multiple_of(h * pair, pair), pair)
            q2, k2, v2 = queries[here_t, lanes], keys[seen, lanes], values[seen, lanes]
            mixed, stats = [], []
            for at in (0, HEAD_DIM):
                head = slice(at, at + HEAD_DIM)
                scores = scores_of(q2[:, head], k2[:, head], t * tile)
                most = jnp.max(scores, axis=-1, keepdims=True)
                weights = jnp.exp(scores - most)
                total = jnp.sum(weights, axis=-1, keepdims=True)
                mixed.append(dot((weights / total).astype(jnp.bfloat16), v2[:, head]))
                stats.append(jnp.broadcast_to(most + jnp.log(total), (tile, HEAD_DIM)))
            attended[here_t, lanes] = jnp.concatenate(mixed, axis=1).astype(jnp.bfloat16)
            logs[here_t, lanes] = jnp.concatenate(stats, axis=1)
            return 0

        lax.fori_loop(0, width // pair, heads, 0)
        terms[here_t, :] = dot(attended[here_t, :], w_out[...]).astype(jnp.bfloat16)
        scatter.side(t).start()
    turn_gate.await_far()
    turn_gate.pass_on()
    for t in range(chips):
        scatter.cross(t)
    for step in range(1, chips):
        scatter.step(step)
        if step == 1:
            turn_gate.pass_far()
            turn_up.await_far()
            turn_up.pass_on()
        if step < chips - 1:
            third.step(step)
        if step == max(chips - 2, 1):
            turn_up.pass_far()
    scatter.finish(after_attn)
    after_attn[...] += tokens[...].astype(jnp.float32)
    after = after_attn[...]
    factor = lax.rsqrt(jnp.mean(after * after, axis=-1, keepdims=True) + eps_norm)
    for j in range(model // share):
        at = pl.ds(j * share, share)
        normed = after_attn[:, at] * factor
        lowered_two[here, at] = (normed * gains[j, 1:2, :]).astype(jnp.bfloat16)
    second = Gather(place, lowered_two, block, two_at)
    second.start()
    third.step(chips - 1)
    keep_cot.wait()
    third.finish()
    load(cotangents, place.nearest(0), 0).start()
    turn_gate.finish()
    turn_up.finish()
    load_down.wait()

    def stores(k, t):
        slot = k % 2
        pairs = (
            (tile_hidden, hidden_out),
            (tile_gate, grad_gate_out),
            (tile_up, grad_up_out),
            (tile_terms, terms_out),
            (tile_sums, sums_out),
        )
        return [
            pltpu.make_async_copy(held.at[slot], rows_at(out, t, tile), store_sems.at[i, slot])
            for i, (held, out) in enumerate(pairs)
        ]

    for k in range(chips):
        t, slot = place.nearest(k), k % 2
        if k > 0:
            second.step(k)
        second.across(t)
        if k + 1 < chips:
            load(cotangents, place.nearest(k + 1), (k + 1) % 2).start()
        load(cotangents, t, slot).wait()
        if k > 1:
            for store in stores(k - 2, place.nearest(k - 2)):
                store.wait()
        rows = lowered_two[pl.ds(pl.multiple_of(t * tile, tile), tile), :]
        gate = dot(rows, slab_gate[...])
        up = dot(rows, slab_up[...])
        grad_hidden = contract_last(tiles[slot], held_down[...])
        sigmoid = jax.nn.sigmoid(gate)
        silu = gate * sigmoid
        hidden = (silu * up).astype(jnp.bfloat16)
        grad_gate = (grad_hidden * up * sigmoid * (1.0 + gate * (1.0 - sigmoid))).astype(jnp.bfloat16)
        grad_up = (grad_hidden * silu).astype(jnp.bfloat16)
        tile_hidden[slot] = hidden
        tile_gate[slot] = grad_gate
        tile_up[slot] = grad_up
        got = contract_last(grad_gate, slab_gate[...]) + contract_last(grad_up, slab_up[...])
        tile_terms[slot] = got.astype(jnp.bfloat16)
        tile_sums[slot] = dot(hidden, held_down[...]).astype(jnp.bfloat16)
        for store in stores(k, t):
            store.start()
    keep_two = pltpu.make_async_copy(lowered_two, lowered_two_out, copy_sems.at[4])
    keep_two.start()
    second.drain()
    scatter.drain()
    for turn in turns + [turn_gate, turn_up]:
        turn.drain()
    await_bytes(gains.at[pl.ds(0, place.fsdp - 1)], gain_out)
    keep_slab.wait()
    for k in range(max(chips - 2, 0), chips):
        for store in stores(k, place.nearest(k)):
            store.wait()
    keep_two.wait()


def front(
    tokens, cotangent, gain_one, gain_two, w_query, w_key, w_value, w_out, w_gate, w_up, w_down, cosine, sine
):
    fsdp = lax.axis_size("fsdp")
    chips = fsdp // 2
    block, model = tokens.shape
    rows, width, wide = fsdp * block, w_query.shape[1] // fsdp, w_gate.shape[1] // fsdp
    tile = 2 * block
    share = gain_one.shape[0]
    low, full = jnp.bfloat16, jnp.float32
    hbm, vmem = pl.BlockSpec(memory_space=pl.ANY), pl.BlockSpec(memory_space=pltpu.VMEM)
    shape = jax.ShapeDtypeStruct
    dma = pltpu.SemaphoreType.DMA
    return pl.pallas_call(
        front_kernel,
        in_specs=[vmem] * 4 + [hbm] * 3 + [vmem] + [hbm] * 3 + [vmem] * 2,
        out_specs=[hbm] * 9 + [vmem] * 7,
        out_shape=[
            shape((rows, model), low),
            shape((rows, model), low),
            shape((rows, model), low),
            shape((3 * model, width), low),
            shape((rows, wide), low),
            shape((rows, wide), low),
            shape((rows, wide), low),
            shape((rows, model), low),
            shape((rows, model), low),
            shape((rows, width), low),
            shape((rows, width), low),
            shape((rows, width), low),
            shape((rows, width), low),
            shape((rows, width), full),
            shape((block, model), full),
            shape((fsdp, 8, share), full),
        ],
        scratch_shapes=[
            pltpu.VMEM((block, model), low),
            pltpu.VMEM((2, tile, model), low),
            pltpu.VMEM((rows, model), low),
            pltpu.VMEM((3 * model, width), low),
            pltpu.VMEM((model, wide), low),
            pltpu.VMEM((model, wide), low),
            pltpu.VMEM((wide, model), low),
            pltpu.VMEM((rows, model), low),
            pltpu.VMEM((chips * block, model), low),
            pltpu.VMEM((chips + 1, block, model), low),
            pltpu.VMEM((2, tile, wide), low),
            pltpu.VMEM((2, tile, wide), low),
            pltpu.VMEM((2, tile, wide), low),
            pltpu.VMEM((2, tile, model), low),
            pltpu.VMEM((2, tile, model), low),
            pltpu.VMEM((8, share), full),
            dma(()),
            dma(()),
            dma((5,)),
            dma((2,)),
            dma((5, 2)),
        ]
        + line_sems(chips) * 3
        + scatter_sems(chips)
        + turn_sems() * 5,
        compiler_params=pltpu.CompilerParams(
            collective_id=0, has_side_effects=True, vmem_limit_bytes=VMEM_LIMIT
        ),
        name="front",
    )(
        tokens,
        cotangent,
        gain_one,
        gain_two,
        w_query,
        w_key,
        w_value,
        w_out,
        w_gate,
        w_up,
        w_down,
        cosine,
        sine,
    )


class Reduce:
    def __init__(self, place, part, first, second, sems):
        self.p, self.part, self.first, self.second, self.sems = place, part, first, second, sems
        self.half = part.shape[0] // 2

    def rows(self, half):
        return pl.ds(half * self.half, self.half)

    def sent(self, half, to):
        if half == 0:
            return self.part.at[self.rows(0), :, to]
        return self.part.at[self.rows(1), to]

    def own(self, half):
        return self.sent(half, self.p.b if half == 0 else self.p.a)

    def start(self, half):
        for k in range(1, self.p.counts[half][0]):
            to, replica = self.p.peer(half, 0, k)
            remote(
                self.sent(half, to),
                self.first[half].at[k - 1],
                self.sems.at[half, 0],
                self.sems.at[half, 1],
                replica=replica,
            ).start()

    def exchange(self):
        for half in range(2):
            own, arrived = self.own(half), self.first[half]
            await_bytes(arrived, self.sems.at[half, 1])

            def add(n, _, own=own, arrived=arrived):
                for m in range(own.shape[1]):
                    total = own[n, m].astype(jnp.float32)
                    for k in range(arrived.shape[0]):
                        total += arrived[k, n, m].astype(jnp.float32)
                    own[n, m] = total.astype(own.dtype)
                return 0

            lax.fori_loop(0, self.half, add, 0)
            for k in range(1, self.p.counts[half][1]):
                to, replica = self.p.peer(half, 1, k)
                remote(
                    own.at[:, to],
                    self.second[half].at[k - 1],
                    self.sems.at[half, 2],
                    self.sems.at[half, 3],
                    replica=replica,
                ).start()

    def total(self):
        for half in range(2):
            own, arrived = self.held(half), self.second[half]
            await_bytes(arrived, self.sems.at[half, 3])

            def add(n, _, own=own, arrived=arrived):
                total = own[n].astype(jnp.float32)
                for k in range(arrived.shape[0]):
                    total += arrived[k, n].astype(jnp.float32)
                own[n] = total.astype(own.dtype)
                return 0

            lax.fori_loop(0, self.half, add, 0)

    def held(self, half):
        return self.part.at[self.rows(half), self.p.a, self.p.b]

    def piece(self, n):
        return self.part.at[n, self.p.a, self.p.b]

    def drain(self):
        for half in range(2):
            await_bytes(self.first[half], self.sems.at[half, 0])
            await_bytes(self.second[half], self.sems.at[half, 2])


def reduce_scratch(n, high, wide, rows, columns):
    low = functools.partial(pltpu.VMEM, dtype=jnp.bfloat16)
    half = n // 2
    return [
        low((n, high, wide, rows, columns)),
        low((wide - 1, half, high, rows, columns)),
        low((high - 1, half, wide, rows, columns)),
        low((high - 1, half, rows, columns)),
        low((wide - 1, half, rows, columns)),
        pltpu.SemaphoreType.DMA((2, 4)),
    ]


def reducer(place, refs):
    part, first_a, first_b, second_a, second_b, sems = refs
    return Reduce(place, part, (first_a, first_b), (second_a, second_b), sems)


class Spread:
    def __init__(self, place, piece, out, sems, turned):
        self.p, self.piece, self.out, self.sems, self.turned = place, piece, out, sems, turned

    def start(self):
        p = self.p
        if self.turned:
            count = self.out.shape[0]
            width = self.out.shape[-1] // p.fsdp
            columns = pl.ds(pl.multiple_of(p.me * width, width), width)

            def pairs(to):
                ref = self.piece(to)
                return [
                    (ref.at[:, pl.ds(i * width, width)], self.out.at[i, p.a, p.b, :, columns])
                    for i in range(count)
                ]

            def send(k, _):
                to = lax.rem(p.me + k, p.fsdp)
                for ref, target in pairs(to):
                    remote(ref, target, self.sems.at[0, 0], self.sems.at[0, 1], fsdp=to).start()
                return 0

            lax.fori_loop(1, p.fsdp, send, 0)
            for ref, target in pairs(p.me):
                pltpu.make_async_copy(ref, target, self.sems.at[0, 1]).start()
        else:
            for half in range(2):
                pltpu.make_async_copy(
                    self.piece(half), self.out.at[half, p.a, p.b], self.sems.at[half, 1]
                ).start()

    def placed(self, half, rows):
        a, b = rows
        if self.turned:
            width = self.out.shape[-1] // 2
            return self.out.at[:, a, b, :, pl.ds(half * width, width)]
        return self.out.at[half, a, b]

    def spread(self):
        p = self.p
        if self.turned:
            await_bytes(self.out.at[:, p.a, p.b], self.sems.at[0, 1])
        for half in range(2):
            ref = self.placed(half, (p.a, p.b))
            src = ref if self.turned else self.piece(half)
            for k in range(1, p.counts[half][1]):
                _, replica = p.peer(half, 1, k)
                remote(src, ref, self.sems.at[half, 2], self.sems.at[half, 3], replica=replica).start()

    def spread_bytes(self, half):
        some = pl.ds(0, self.p.counts[half][1] - 1)
        return self.placed(half, (some, 0) if half == 0 else (0, some))

    def widen(self):
        p = self.p
        for half in range(2):
            if not self.turned:
                await_bytes(self.placed(half, (p.a, p.b)), self.sems.at[half, 1])
            await_bytes(self.spread_bytes(half), self.sems.at[half, 3])
            every = pl.ds(0, p.counts[half][1])
            ref = self.placed(half, (every, p.b) if half == 0 else (p.a, every))
            for k in range(1, p.counts[half][0]):
                _, replica = p.peer(half, 0, k)
                remote(ref, ref, self.sems.at[half, 4], self.sems.at[half, 5], replica=replica).start()

    def widen_bytes(self, half):
        counts = self.p.counts[half]
        every, some = pl.ds(0, counts[1]), pl.ds(0, counts[0] - 1)
        return self.placed(half, (every, some) if half == 0 else (some, every))

    def finish(self):
        p = self.p
        for half in range(2):
            await_bytes(self.widen_bytes(half), self.sems.at[half, 5])
            await_bytes(self.spread_bytes(half), self.sems.at[half, 2])
            await_bytes(self.widen_bytes(half), self.sems.at[half, 4])
        if self.turned:
            width = self.out.shape[-1] // p.fsdp
            await_bytes(
                self.out.at[:, p.a, p.b, :, pl.ds(0, (p.fsdp - 1) * width)], self.sems.at[0, 0]
            )


def spread_sems():
    return [pltpu.SemaphoreType.DMA((2, 6))]


def norm_back(values, gain_row, gains, grad, carried, result, gain_terms):
    block, model = values.shape
    share = gains.shape[2]
    held = values[...].astype(jnp.float32)
    factor = lax.rsqrt(jnp.mean(held * held, axis=-1, keepdims=True) + eps_norm)
    dots = jnp.zeros((block, 1), jnp.float32)
    for j in range(model // share):
        at = pl.ds(j * share, share)
        normed = values[:, at].astype(jnp.float32) * factor
        product = grad[:, at] * normed
        gain_terms[j, gain_row : gain_row + 1, :] = jnp.sum(product, axis=0, keepdims=True)
        dots += jnp.sum(product * gains[j, gain_row : gain_row + 1, :], axis=-1, keepdims=True)
    dots = dots / model
    for j in range(model // share):
        at = pl.ds(j * share, share)
        normed = values[:, at].astype(jnp.float32) * factor
        scaled = grad[:, at] * gains[j, gain_row : gain_row + 1, :]
        result[:, at] = carried[:, at].astype(jnp.float32) + factor * (scaled - normed * dots)


def weigh_kernel(
    cotangent,
    after_attn,
    gains,
    terms_in,
    lowered_two,
    cotangents,
    hidden_in,
    grad_gate_in,
    grad_up_in,
    w_out,
    queries,
    keys,
    values,
    logs,
    cosine,
    sine,
    grad_after,
    gain_terms,
    grads,
    branch,
    sum_down,
    sum_gate,
    sum_up,
    tokens_held,
    hidden,
    grad_gate,
    grad_up,
    terms,
    across,
    slots,
    summed,
    low,
    grad_low,
    grad_key,
    grad_value,
    load_sems,
    store_sems,
    *rest,
):
    place = Place()
    chips, block = place.chips, cotangent.shape[0]
    model = cotangent.shape[1]
    tile = 2 * block
    scatter_at, gather_at = rest[:6], rest[6:12]
    down, gate, up = [reducer(place, rest[12 + 6 * i : 18 + 6 * i]) for i in range(3)]

    def load(t):
        at = pl.ds(t * tile, tile)
        return pltpu.make_async_copy(terms_in.at[at], terms.at[at], load_sems.at[t])

    loads = [
        pltpu.make_async_copy(source, target, load_sems.at[chips + i])
        for i, (source, target) in enumerate(
            (
                (cotangents, tokens_held),
                (hidden_in, hidden),
                (grad_gate_in, grad_gate),
                (grad_up_in, grad_up),
                (lowered_two, tokens_held),
            )
        )
    ]
    for t in range(chips):
        load(t).start()
    for copy in loads[:4]:
        copy.start()
    place.enter()
    scatter = Scatter(place, terms, across, slots, block, scatter_at)
    for t in range(chips):
        load(t).wait()
        scatter.side(t).start()
    gain_terms[...] = jnp.zeros_like(gain_terms)
    loads[0].wait()
    loads[1].wait()
    _, high, wide, thin, _ = down.part.shape
    columns = min(tile, hidden.shape[1])
    for i in range(0, hidden.shape[1], columns):
        got = contract_first(hidden[:, i : i + columns], tokens_held[...]).astype(jnp.bfloat16)
        for m in range(0, columns, thin):
            n = (i + m) // thin
            down.part[n // (high * wide), n // wide % high, n % wide] = got[m : m + thin, :]
        if 2 * (i + columns) == hidden.shape[1]:
            down.start(0)
    loads[4].start()
    down.start(1)
    for t in range(chips):
        scatter.cross(t)
    scatter.step(1)
    loads[4].wait()

    def weigh(reduce, grads):
        share = model // place.fsdp

        def rows(j, _):
            left = tokens_held[:, pl.ds(pl.multiple_of(j * share, share), share)]
            got = contract_first(left, grads[...]).astype(jnp.bfloat16)
            reduce.part[j] = got.reshape(reduce.part.shape[1:])
            return 0

        for half in range(2):
            lax.fori_loop(half * chips, (half + 1) * chips, rows, 0)
            reduce.start(half)

    loads[2].wait()
    weigh(gate, grad_gate)
    if chips > 2:
        scatter.step(2)
    loads[3].wait()
    weigh(up, grad_up)
    for step in range(3, chips):
        scatter.step(step)
    scatter.finish(summed)
    norm_back(after_attn, 1, gains, summed, cotangent, grad_after, gain_terms)
    low[...] = grad_after[...].astype(jnp.bfloat16)
    here = pl.ds(pl.multiple_of(place.me * block, block), block)
    gather = Gather(place, branch, block, gather_at, low)
    gather.start()
    keep = pltpu.make_async_copy(low, branch.at[here], store_sems.at[0])
    keep.start()
    scatter.drain()
    down.exchange()
    for step in range(1, chips):
        gather.step(step)
        if step == 1:
            gate.exchange()
        if step == max(chips - 2, 1):
            up.exchange()
    keep.wait()
    gather.finish()
    fetch = pltpu.make_async_copy(branch, tokens_held, load_sems.at[0])
    fetch.start()
    down.total()
    fetch.wait()

    def attend_rows(t, _):
        at = pl.ds(pl.multiple_of(t * tile, tile), tile)
        grad_low[at, :] = contract_last(tokens_held[at, :], w_out[...]).astype(jnp.bfloat16)
        return 0

    lax.fori_loop(0, chips, attend_rows, 0)
    width = queries.shape[1]
    scale = HEAD_DIM**-0.5
    grad_key[...] = jnp.zeros_like(grad_key)
    grad_value[...] = jnp.zeros_like(grad_value)
    pair = 2 * HEAD_DIM
    height = tile * 1024 // max(queries.shape[0], 1024)
    for first in range(0, queries.shape[0], height):
        rows, seen = pl.ds(first, height), pl.ds(0, first + height)

        def heads(h, _, first=first, rows=rows, seen=seen):
            lanes = pl.ds(pl.multiple_of(h * pair, pair), pair)
            q2, g2, log2 = queries[rows, lanes], grad_low[rows, lanes], logs[rows, lanes]
            k2, v2 = keys[seen, lanes], values[seen, lanes]
            for_queries, for_keys, for_values = [], [], []
            for at in (0, HEAD_DIM):
                head = slice(at, at + HEAD_DIM)
                q, g, k = q2[:, head], g2[:, head], k2[:, head]
                weights = jnp.exp(scores_of(q, k, first) - log2[:, at : at + 1])
                grad_weights = contract_last(g, v2[:, head])
                delta = jnp.sum(weights * grad_weights, axis=-1, keepdims=True)
                grad_scores = (weights * (grad_weights - delta)).astype(jnp.bfloat16)
                for_queries.append(dot(grad_scores, k))
                for_keys.append(contract_first(grad_scores, q))
                for_values.append(contract_first(weights.astype(jnp.bfloat16), g))
            got = jnp.concatenate(for_queries, axis=1) * scale
            got = got * cosine[rows, :] - partner(got) * sine[rows, :]
            grads[rows, lanes] = got.astype(jnp.bfloat16)
            grad_key[seen, lanes] += jnp.concatenate(for_keys, axis=1) * scale
            grad_value[seen, lanes] += jnp.concatenate(for_values, axis=1)
            return 0

        lax.fori_loop(0, width // pair, heads, 0)

    def turn_keys(t, _):
        at = pl.ds(pl.multiple_of(t * tile, tile), tile)
        for j in range(0, width, pair):
            got = grad_key[at, j : j + pair]
            got = got * cosine[at, :] - partner(got) * sine[at, :]
            grads[at, width + j : width + j + pair] = got.astype(jnp.bfloat16)
        grads[at, 2 * width :] = grad_value[at, :].astype(jnp.bfloat16)
        return 0

    lax.fori_loop(0, chips, turn_keys, 0)
    stores = []
    for i, (reduce, out) in enumerate(((down, sum_down), (gate, sum_gate), (up, sum_up))):
        if i > 0:
            reduce.total()
        for half in range(2):
            store = pltpu.make_async_copy(
                reduce.held(half), out.at[reduce.rows(half)], store_sems.at[1 + 2 * i + half]
            )
            store.start()
            stores.append(store)
    for reduce in (down, gate, up):
        reduce.drain()
    for store in stores:
        store.wait()


def weigh(
    cotangent,
    after_attn,
    gains,
    terms,
    lowered_two,
    cotangents,
    hidden,
    grad_gate,
    grad_up,
    w_out,
    queries,
    keys,
    values,
    logs,
    cosine,
    sine,
):
    fsdp, replicas = lax.axis_size("fsdp"), lax.axis_size("replica")
    chips, high, wide = fsdp // 2, 2, replicas // 2
    block, model = cotangent.shape
    rows, columns = hidden.shape
    width = queries.shape[1]
    share = gains.shape[2]
    low, full = jnp.bfloat16, jnp.float32
    hbm, vmem = pl.BlockSpec(memory_space=pl.ANY), pl.BlockSpec(memory_space=pltpu.VMEM)
    shape = jax.ShapeDtypeStruct
    down_piece = (2, high, wide, columns // (2 * replicas), model)
    wide_piece = (fsdp, high, wide, share // replicas, columns)
    dma = pltpu.SemaphoreType.DMA
    return pl.pallas_call(
        weigh_kernel,
        in_specs=[vmem] * 3 + [hbm] * 6 + [vmem] * 7,
        out_specs=[vmem] * 3 + [hbm] * 4,
        out_shape=[
            shape((block, model), full),
            shape((fsdp, 8, share), full),
            shape((rows, 3 * width), low),
            shape((rows, model), low),
            shape((2,) + down_piece[3:], low),
            shape((fsdp,) + wide_piece[3:], low),
            shape((fsdp,) + wide_piece[3:], low),
        ],
        scratch_shapes=[
            pltpu.VMEM((rows, model), low),
            pltpu.VMEM((rows, columns), low),
            pltpu.VMEM((rows, columns), low),
            pltpu.VMEM((rows, columns), low),
            pltpu.VMEM((rows, model), low),
            pltpu.VMEM((chips * block, model), low),
            pltpu.VMEM((chips + 1, block, model), low),
            pltpu.VMEM((block, model), full),
            pltpu.VMEM((block, model), low),
            pltpu.VMEM((rows, width), low),
            pltpu.VMEM((rows, width), full),
            pltpu.VMEM((rows, width), full),
            dma((chips + 5,)),
            dma((7,)),
        ]
        + scatter_sems(chips)
        + line_sems(chips)
        + reduce_scratch(*down_piece)
        + reduce_scratch(*wide_piece)
        + reduce_scratch(*wide_piece),
        compiler_params=pltpu.CompilerParams(
            collective_id=1, has_side_effects=True, vmem_limit_bytes=VMEM_LIMIT
        ),
        name="weigh",
    )(
        cotangent,
        after_attn,
        gains,
        terms,
        lowered_two,
        cotangents,
        hidden,
        grad_gate,
        grad_up,
        w_out,
        queries,
        keys,
        values,
        logs,
        cosine,
        sine,
    )


def back_kernel(
    tokens,
    gains,
    grad_after,
    gain_terms_in,
    after_attn,
    sums,
    sum_down,
    sum_gate,
    sum_up,
    branch_in,
    lowered_one,
    slab_qkv,
    attended,
    grads,
    outputs,
    grad_tokens,
    gain_out,
    out_down,
    out_gate,
    out_up,
    out_qkv,
    out_out,
    terms,
    across,
    slots,
    branch,
    summed,
    gain_terms,
    gain_slots,
    gain_sums,
    gain_sems,
    load_sems,
    *rest,
):
    place = Place()
    chips, block = place.chips, tokens.shape[0]
    model, width = tokens.shape[1], attended.shape[1]
    share = gains.shape[2]
    tile = 2 * block
    scatter_at, rest = rest[:6], rest[6:]
    down = Spread(place, lambda n: sum_down.at[n], out_down, rest[0], False)
    gate = Spread(place, lambda n: sum_gate.at[n], out_gate, rest[1], True)
    up = Spread(place, lambda n: sum_up.at[n], out_up, rest[2], True)
    qkv, out = reducer(place, rest[5:11]), reducer(place, rest[11:17])
    qkv_spread = Spread(place, qkv.piece, out_qkv, rest[3], True)
    out_spread = Spread(place, out.piece, out_out, rest[4], False)
    load = pltpu.make_async_copy(lowered_one, branch, load_sems.at[0])
    load.start()
    place.enter()
    down.start()
    down.spread()
    gate.start()
    load.wait()

    def weigh_rows(j, _):
        left = branch[:, pl.ds(pl.multiple_of(j * share, share), share)]
        got = contract_first(left, grads[...]).astype(jnp.bfloat16)
        qkv.part[j] = got.reshape(qkv.part.shape[1:])
        return 0

    for half in range(2):
        lax.fori_loop(half * chips, (half + 1) * chips, weigh_rows, 0)
        qkv.start(half)
    reload = pltpu.make_async_copy(branch_in, branch, load_sems.at[1])
    reload.start()
    scatter = Scatter(place, terms, across, slots, block, scatter_at)

    def back_rows(t, _):
        at = pl.ds(pl.multiple_of(t * tile, tile), tile)
        got = contract_last(grads[at, :width], slab_qkv[:model, :])
        got += contract_last(grads[at, width : 2 * width], slab_qkv[model : 2 * model, :])
        got += contract_last(grads[at, 2 * width :], slab_qkv[2 * model :, :])
        terms[at, :] = got.astype(jnp.bfloat16)
        return 0

    lax.fori_loop(0, chips, back_rows, 0)
    for t in range(chips):
        scatter.side(t).start()
    down.widen()
    reload.wait()
    _, high, wide, thin, columns = out.part.shape
    for half in range(2):
        for at in range(0, columns, 512):
            got = contract_first(
                attended[...], branch[:, half * columns + at : half * columns + at + 512]
            ).astype(jnp.bfloat16)
            out.part[half, :, :, :, at : at + 512] = got.reshape(high, wide, thin, 512)
    out.start(0)
    out.start(1)
    for t in range(chips):
        scatter.cross(t)
    scatter.step(1)
    gate.spread()
    qkv.exchange()
    for step in range(2, chips):
        scatter.step(step)
    up.start()
    scatter.finish(summed)
    gain_terms[...] = gain_terms_in[...]
    norm_back(tokens, 0, gains, summed, grad_after, grad_tokens, gain_terms)

    def send_gain(k, _):
        to = lax.rem(place.me + k, place.fsdp)
        remote(
            gain_terms.at[to], gain_slots.at[place.me], gain_sems.at[0], gain_sems.at[1], fsdp=to
        ).start()
        return 0

    lax.fori_loop(1, place.fsdp, send_gain, 0)
    gain_slots[place.me] = gain_terms[place.me]
    scatter.drain()
    load_sums = pltpu.make_async_copy(sums, terms, load_sems.at[0])
    load_sums.start()
    out.exchange()
    gate.widen()
    qkv.total()
    qkv_spread.start()
    await_bytes(gain_slots.at[pl.ds(0, place.fsdp - 1)], gain_sems.at[1])
    gain_sums[place.replica] = jnp.sum(gain_slots[...], axis=0)

    def send_sum(k, _):
        ref = gain_sums.at[place.replica]
        to = lax.rem(place.replica + k, place.replicas)
        remote(ref, ref, gain_sems.at[2], gain_sems.at[3], replica=to).start()
        return 0

    lax.fori_loop(1, place.replicas, send_sum, 0)

    load_sums.wait()
    for t in range(chips):
        scatter.side(t).start()
    up.spread()
    for t in range(chips):
        scatter.cross(t)
    scatter.step(1)
    out.total()
    out_spread.start()
    out_spread.spread()
    qkv_spread.spread()
    up.widen()
    for step in range(2, chips):
        scatter.step(step)
    out_spread.widen()
    scatter.finish(summed)
    outputs[...] = (summed[...] + after_attn[...]).astype(outputs.dtype)
    qkv_spread.widen()
    await_bytes(gain_sums.at[pl.ds(0, place.replicas - 1)], gain_sems.at[3])
    gain_out[...] = jnp.sum(gain_sums[...], axis=0)
    await_bytes(gain_slots.at[pl.ds(0, place.fsdp - 1)], gain_sems.at[0])
    await_bytes(gain_sums.at[pl.ds(0, place.replicas - 1)], gain_sems.at[2])
    scatter.drain()
    qkv.drain()
    out.drain()
    for spread in (down, gate, up, out_spread, qkv_spread):
        spread.finish()


def back(
    tokens,
    gains,
    grad_after,
    gain_terms,
    after_attn,
    sums,
    sum_down,
    sum_gate,
    sum_up,
    branch,
    lowered_one,
    slab_qkv,
    attended,
    grads,
):
    fsdp, replicas = lax.axis_size("fsdp"), lax.axis_size("replica")
    chips, high, wide = fsdp // 2, 2, replicas // 2
    block, model = tokens.shape
    rows, width = attended.shape
    share = gains.shape[2]
    low, full = jnp.bfloat16, jnp.float32
    hbm, vmem = pl.BlockSpec(memory_space=pl.ANY), pl.BlockSpec(memory_space=pltpu.VMEM)
    shape = jax.ShapeDtypeStruct
    thin = share // replicas
    columns = sum_gate.shape[-1]
    qkv_piece = (fsdp, high, wide, thin, 3 * width)
    out_piece = (2, high, wide, width // replicas, model // 2)
    dma = pltpu.SemaphoreType.DMA
    return pl.pallas_call(
        back_kernel,
        in_specs=[vmem] * 5 + [hbm] * 6 + [vmem] * 3,
        out_specs=[vmem] * 3 + [hbm] * 5,
        out_shape=[
            shape((block, model), low),
            shape((block, model), full),
            shape((8, share), full),
            shape((2, high, wide) + sum_down.shape[1:], low),
            shape((1, high, wide, thin, fsdp * columns), low),
            shape((1, high, wide, thin, fsdp * columns), low),
            shape((3, high, wide, thin, fsdp * width), low),
            shape(out_piece, low),
        ],
        scratch_shapes=[
            pltpu.VMEM((rows, model), low),
            pltpu.VMEM((chips * block, model), low),
            pltpu.VMEM((chips + 1, block, model), low),
            pltpu.VMEM((rows, model), low),
            pltpu.VMEM((block, model), full),
            pltpu.VMEM((fsdp, 8, share), full),
            pltpu.VMEM((fsdp, 8, share), full),
            pltpu.VMEM((replicas, 8, share), full),
            dma((4,)),
            dma((2,)),
        ]
        + scatter_sems(chips)
        + spread_sems() * 5
        + reduce_scratch(*qkv_piece)
        + reduce_scratch(*out_piece),
        compiler_params=pltpu.CompilerParams(
            collective_id=2, has_side_effects=True, vmem_limit_bytes=VMEM_LIMIT
        ),
        name="back",
    )(
        tokens,
        gains,
        grad_after,
        gain_terms,
        after_attn,
        sums,
        sum_down,
        sum_gate,
        sum_up,
        branch,
        lowered_one,
        slab_qkv,
        attended,
        grads,
    )


def widen_kernel(
    down,
    gate,
    up,
    qkv,
    out,
    outputs_in,
    tokens_in,
    gains,
    w_down,
    w_gate,
    w_up,
    w_query,
    w_key,
    w_value,
    w_out,
    outputs,
    grad_tokens,
    gain_one,
    gain_two,
):
    w_down[...] = down[...].astype(jnp.float32)
    w_gate[...] = gate[...].astype(jnp.float32)
    w_up[...] = up[...].astype(jnp.float32)
    for i, ref in enumerate((w_query, w_key, w_value)):
        ref[...] = qkv[i].astype(jnp.float32)
    half = out.shape[2]
    for i in range(2):
        w_out[:, i * half : (i + 1) * half] = out[i].astype(jnp.float32)
    outputs[...] = outputs_in[...]
    grad_tokens[...] = tokens_in[...]
    gain_one[...] = gains[0, :]
    gain_two[...] = gains[1, :]


def widen(down, gate, up, qkv, out, outputs, grad_tokens, gains):
    steps = min(16, gate.shape[0] // 16)
    token_steps = outputs.shape[0] // 16
    full = jnp.float32

    def rows(array):
        return pl.BlockSpec((array.shape[0] // steps, array.shape[1]), lambda i: (i, 0))

    def tokens(array):
        return pl.BlockSpec(
            (array.shape[0] // token_steps, array.shape[1]), lambda i: (jnp.minimum(i, token_steps - 1), 0)
        )

    def stacked(array):
        return pl.BlockSpec((array.shape[0], array.shape[1] // steps, array.shape[2]), lambda i: (0, i, 0))

    like = [down, gate, up, qkv[0], qkv[0], qkv[0]]
    shapes = [jax.ShapeDtypeStruct(array.shape, full) for array in like]
    shapes.append(jax.ShapeDtypeStruct((out.shape[1], 2 * out.shape[2]), full))
    row = jax.ShapeDtypeStruct(gains.shape[1:], full)
    whole = pl.BlockSpec(gains.shape, lambda i: (0, 0))
    line = pl.BlockSpec(gains.shape[1:], lambda i: (0,))
    return pl.pallas_call(
        widen_kernel,
        grid=(steps,),
        in_specs=[rows(down), rows(gate), rows(up), stacked(qkv), stacked(out)]
        + [tokens(outputs), tokens(grad_tokens), whole],
        out_specs=[rows(shape) for shape in shapes]
        + [tokens(outputs), tokens(grad_tokens), line, line],
        out_shape=shapes
        + [jax.ShapeDtypeStruct(array.shape, array.dtype) for array in (outputs, grad_tokens)]
        + [row, row],
        compiler_params=pltpu.CompilerParams(vmem_limit_bytes=VMEM_LIMIT),
        name="widen",
    )(down, gate, up, qkv, out, outputs, grad_tokens, gains)


def local(
    tokens, attn_gain, w_query, w_key, w_value, w_out, ffn_gain, w_gate, w_up, w_down, cotangent
):
    cosine, sine = rope_tables(tokens.shape[0] * lax.axis_size("fsdp"))
    (
        lowered_one,
        lowered_two,
        cotangents,
        slab_qkv,
        hidden,
        grad_gate,
        grad_up,
        terms,
        sums,
        queries,
        keys,
        values,
        attended,
        logs,
        after_attn,
        gains,
    ) = front(
        tokens,
        cotangent,
        attn_gain,
        ffn_gain,
        w_query,
        w_key,
        w_value,
        w_out,
        w_gate,
        w_up,
        w_down,
        cosine,
        sine,
    )
    grad_after, gain_terms, grads, branch, sum_down, sum_gate, sum_up = weigh(
        cotangent,
        after_attn,
        gains,
        terms,
        lowered_two,
        cotangents,
        hidden,
        grad_gate,
        grad_up,
        w_out,
        queries,
        keys,
        values,
        logs,
        cosine,
        sine,
    )
    outputs, grad_tokens, gain_grads, low_down, low_gate, low_up, low_qkv, low_out = back(
        tokens,
        gains,
        grad_after,
        gain_terms,
        after_attn,
        sums,
        sum_down,
        sum_gate,
        sum_up,
        branch,
        lowered_one,
        slab_qkv,
        attended,
        grads,
    )
    (
        grad_w_down,
        grad_w_gate,
        grad_w_up,
        grad_w_query,
        grad_w_key,
        grad_w_value,
        grad_w_out,
        outputs,
        grad_tokens,
        grad_attn_gain,
        grad_ffn_gain,
    ) = widen(
        low_down.reshape(w_down.shape),
        low_gate.reshape(w_gate.shape),
        low_up.reshape(w_up.shape),
        low_qkv.reshape((3,) + w_query.shape),
        low_out.reshape(2, w_out.shape[0], -1),
        outputs,
        grad_tokens,
        gain_grads,
    )
    return (
        outputs,
        grad_tokens,
        grad_attn_gain,
        grad_w_query,
        grad_w_key,
        grad_w_value,
        grad_w_out,
        grad_ffn_gain,
        grad_w_gate,
        grad_w_up,
        grad_w_down,
    )


def solution(mesh):
    rows = P("fsdp", None)
    tokens = P(("replica", "fsdp"), None)
    gain = P("fsdp")
    return jax.shard_map(
        local,
        mesh=mesh,
        in_specs=(tokens, gain, rows, rows, rows, rows, gain, rows, rows, rows, tokens),
        out_specs=(tokens, tokens, gain, rows, rows, rows, rows, gain, rows, rows, rows),
        check_vma=False,
    )
```

```python
import functools

import jax
import jax.numpy as jnp
import numpy as np
from jax import lax
from jax.experimental import pallas as pl
from jax.experimental.pallas import tpu as pltpu
from jax.sharding import PartitionSpec as P

HEAD_DIM = 64

eps_norm = 1e-05
rope_base = 130000.0
masked_score = -1e30


def rope_tables(row_count):
    lane = np.arange(2 * HEAD_DIM) % HEAD_DIM
    halfway = HEAD_DIM // 2
    spacing = ((lane % halfway) * np.float32(2.0) / HEAD_DIM).astype(np.float32)
    frequency = np.power(np.float32(rope_base), -spacing)
    angles = np.arange(row_count, dtype=np.float32)[:, None] * frequency[None, :]
    sign = np.where(lane < halfway, -1.0, 1.0).astype(np.float32)
    return np.cos(angles).astype(np.float32), (np.sin(angles) * sign[None, :]).astype(np.float32)


def dot(left, right):
    return jnp.dot(left, right, preferred_element_type=jnp.float32)


def contract_last(left, right):
    return lax.dot_general(
        left, right, (((1,), (1,)), ((), ())), preferred_element_type=jnp.float32
    )


def contract_first(left, right):
    return lax.dot_general(
        left, right, (((0,), (0,)), ((), ())), preferred_element_type=jnp.float32
    )


def scores_of(queries, keys, first_row):
    rows, columns = queries.shape[0], keys.shape[0]
    scores = contract_last(queries, keys) * HEAD_DIM**-0.5
    at_row = lax.broadcasted_iota(jnp.int32, (rows, columns), 0) + first_row
    at_column = lax.broadcasted_iota(jnp.int32, (rows, columns), 1)
    return jnp.where(at_column <= at_row, scores, masked_score)


MESH = pl.DeviceIdType.MESH
VMEM_LIMIT = 61 * 2**20


def remote(src, dst, send, recv, **where):
    return pltpu.make_async_remote_copy(
        src_ref=src, dst_ref=dst, send_sem=send, recv_sem=recv, device_id=where, device_id_type=MESH
    )


def await_bytes(ref, sem):
    pltpu.make_async_copy(ref, ref, sem).wait()


def rows_at(ref, index, size):
    return ref.at[pl.ds(pl.multiple_of(index * size, size), size)]


class Place:
    def __init__(self):
        self.fsdp, self.replicas = lax.axis_size("fsdp"), lax.axis_size("replica")
        self.me, self.replica = lax.axis_index("fsdp"), lax.axis_index("replica")
        self.chips = self.fsdp // 2
        self.chip, self.core = self.me // 2, self.me % 2
        self.sibling = self.me + 1 - 2 * self.core
        self.high, self.wide = 2, self.replicas // 2
        self.a, self.b = self.replica // self.wide, self.replica % self.wide
        self.counts = ((self.wide, self.high), (self.high, self.wide))
        self.above = self.chip + 1 < self.chips
        self.below = self.chip >= 1

    def peer(self, half, stage, k):
        if half == stage:
            to = lax.rem(self.b + k, self.wide)
            return to, self.a * self.wide + to
        to = lax.rem(self.a + k, self.high)
        return to, to * self.wide + self.b

    def nearest(self, k):
        found = jnp.int32(0)
        for chip in range(self.chips):
            order = sorted(range(self.chips), key=lambda other, chip=chip: (abs(other - chip), other))
            found = found + jnp.where(self.chip == chip, order[k], 0)
        return found

    def enter(self):
        barrier = pltpu.get_barrier_semaphore()

        def greet(k, _):
            to = lax.rem(self.me + k, self.fsdp)
            pl.semaphore_signal(barrier, inc=1, device_id={"fsdp": to}, device_id_type=MESH)
            return 0

        def greet_replica(k, _):
            to = lax.rem(self.replica + k, self.replicas)
            pl.semaphore_signal(barrier, inc=1, device_id={"replica": to}, device_id_type=MESH)
            return 0

        lax.fori_loop(1, self.fsdp, greet, 0)
        lax.fori_loop(1, self.replicas, greet_replica, 0)
        pl.semaphore_wait(barrier, self.fsdp - 1 + self.replicas - 1)


def line_sems(chips):
    return [pltpu.SemaphoreType.DMA((chips,))] * 6


class Gather:
    def __init__(self, place, buf, block, sems, own=None):
        self.p, self.buf, self.block, self.own = place, buf, block, own
        self.up_out, self.up_in, self.down_out, self.down_in, self.side_out, self.side_in = sems

    def held(self, chip):
        return rows_at(self.buf, 2 * chip + self.p.core, self.block)

    def up(self, step):
        ref = self.held(self.p.chip - step + 1)
        src = self.own if step == 1 and self.own is not None else ref
        return remote(src, ref, self.up_out.at[step], self.up_in.at[step], fsdp=self.p.me + 2)

    def down(self, step):
        ref = self.held(self.p.chip + step - 1)
        src = self.own if step == 1 and self.own is not None else ref
        return remote(src, ref, self.down_out.at[step], self.down_in.at[step], fsdp=self.p.me - 2)

    def side(self, chip, src=None):
        ref = self.held(chip)
        src = ref if src is None else src
        return remote(src, ref, self.side_out.at[chip], self.side_in.at[chip], fsdp=self.p.sibling)

    def start(self):
        p = self.p
        pl.when(p.above)(lambda: self.up(1).start())
        pl.when(p.below)(lambda: self.down(1).start())
        self.side(p.chip, self.own).start()

    def step(self, step):
        p = self.p
        from_below, from_above = p.chip - step, p.chip + step

        @pl.when(from_below >= 0)
        def _():
            await_bytes(self.held(from_below), self.up_in.at[step])
            if step + 1 < p.chips:
                pl.when(p.above)(lambda: self.up(step + 1).start())
            self.side(from_below).start()

        @pl.when(from_above < p.chips)
        def _():
            await_bytes(self.held(from_above), self.down_in.at[step])
            if step + 1 < p.chips:
                pl.when(p.below)(lambda: self.down(step + 1).start())
            self.side(from_above).start()

    def across(self, chip):
        await_bytes(rows_at(self.buf, 2 * chip + 1 - self.p.core, self.block), self.side_in.at[chip])

    def drain(self):
        p = self.p
        for step in range(1, p.chips):
            pl.when(jnp.logical_and(p.above, p.chip - step + 1 >= 0))(
                lambda step=step: self.up(step).wait_send()
            )
            pl.when(jnp.logical_and(p.below, p.chip + step - 1 < p.chips))(
                lambda step=step: self.down(step).wait_send()
            )
        for chip in range(p.chips):
            self.side(chip).wait_send()

    def finish(self):
        for chip in range(self.p.chips):
            self.across(chip)
        self.drain()


class Scatter:
    def __init__(self, place, terms, across, slots, block, sems):
        self.p, self.terms, self.across, self.slots, self.block = place, terms, across, slots, block
        self.up_out, self.up_in, self.down_out, self.down_in, self.side_out, self.side_in = sems

    def side(self, chip):
        p = self.p
        return remote(
            rows_at(self.terms, 2 * chip + 1 - p.core, self.block),
            rows_at(self.across, chip, self.block),
            self.side_out.at[chip],
            self.side_in.at[chip],
            fsdp=p.sibling,
        )

    def term(self, chip):
        return rows_at(self.terms, 2 * chip + self.p.core, self.block)

    def up(self, step):
        return remote(
            self.term(self.p.chips - step + self.p.chip),
            self.slots.at[step - self.p.chip - 1],
            self.up_out.at[step],
            self.up_in.at[step],
            fsdp=self.p.me + 2,
        )

    def down(self, step):
        return remote(
            self.term(self.p.chip - self.p.chips + step),
            self.slots.at[step + 1],
            self.down_out.at[step],
            self.down_in.at[step],
            fsdp=self.p.me - 2,
        )

    def add(self, chip, arrived):
        term = self.term(chip)
        term[...] = (term[...].astype(jnp.float32) + arrived[...].astype(jnp.float32)).astype(term.dtype)

    def cross(self, chip):
        arrived = rows_at(self.across, chip, self.block)
        await_bytes(arrived, self.side_in.at[chip])
        self.add(chip, arrived)

    def step(self, step):
        p = self.p
        rising, falling = p.chips - step + p.chip, p.chip - p.chips + step

        @pl.when(jnp.logical_and(p.above, rising < p.chips))
        def _():
            if step > 1:

                @pl.when(p.below)
                def _():
                    arrived = self.slots.at[step - 1 - p.chip]
                    await_bytes(arrived, self.up_in.at[step - 1])
                    self.add(rising, arrived)

            self.up(step).start()

        @pl.when(jnp.logical_and(p.below, falling >= 0))
        def _():
            if step > 1:

                @pl.when(p.above)
                def _():
                    arrived = self.slots.at[step]
                    await_bytes(arrived, self.down_in.at[step - 1])
                    self.add(falling, arrived)

            self.down(step).start()

    def finish(self, total):
        p, last = self.p, self.p.chips - 1
        total[...] = self.term(p.chip)[...].astype(jnp.float32)

        @pl.when(p.below)
        def _():
            await_bytes(self.slots.at[last - p.chip], self.up_in.at[last])
            total[...] += self.slots[last - p.chip].astype(jnp.float32)

        @pl.when(p.above)
        def _():
            await_bytes(self.slots.at[last + 1], self.down_in.at[last])
            total[...] += self.slots[last + 1].astype(jnp.float32)

    def drain(self):
        p = self.p
        for step in range(1, p.chips):
            pl.when(jnp.logical_and(p.above, p.chips - step + p.chip < p.chips))(
                lambda step=step: self.up(step).wait_send()
            )
            pl.when(jnp.logical_and(p.below, p.chip - p.chips + step >= 0))(
                lambda step=step: self.down(step).wait_send()
            )
        for chip in range(p.chips):
            self.side(chip).wait_send()


def scatter_sems(chips):
    dma = pltpu.SemaphoreType.DMA
    return [dma((chips,))] * 6


class Turn:
    def __init__(self, place, weight, slab, first, sems):
        self.p, self.weight, self.slab, self.first = place, weight, slab, first
        self.far_out, self.far_in, self.near_out, self.near_in, self.own, self.passing = sems
        self.height, self.width = weight.shape[0], slab.shape[1]
        self.share = self.height // place.replicas

    def far_rows(self):
        return (self.p.fsdp - 2) * self.share

    def piece(self, block, share):
        at = self.first + block * self.height + share * self.share
        return self.slab.at[pl.ds(pl.multiple_of(at, self.share), self.share)]

    def whole(self, block):
        at = self.first + block * self.height
        return self.slab.at[pl.ds(pl.multiple_of(at, self.height), self.height)]

    def columns(self, to):
        return pl.ds(pl.multiple_of(to * self.width, self.width), self.width)

    def start(self):
        p = self.p

        def send(k, _):
            to = lax.rem(2 * p.chip + 2 + k, p.fsdp)
            share = pl.ds(pl.multiple_of(p.replica * self.share, self.share), self.share)
            remote(
                self.weight.at[share, self.columns(to)],
                self.piece(p.me, p.replica),
                self.far_out,
                self.far_in,
                fsdp=to,
            ).start()
            return 0

        lax.fori_loop(0, p.fsdp - 2, send, 0)
        self.near().start()
        self.mine().start()

    def near(self):
        p = self.p
        return remote(
            self.weight.at[:, self.columns(p.sibling)], self.whole(p.me), self.near_out, self.near_in, fsdp=p.sibling
        )

    def mine(self):
        return pltpu.make_async_copy(self.weight.at[:, self.columns(self.p.me)], self.whole(self.p.me), self.own)

    def await_far(self):
        await_bytes(self.slab.at[pl.ds(0, self.far_rows())], self.far_in)

    def bytes_of(self, pieces):
        return self.slab.at[pl.ds(0, pieces * self.share)]

    def pass_bytes(self, half, stage):
        first, second = self.p.counts[half]
        return self.bytes_of((self.p.chips - 1) * (second - 1 if stage == 0 else second * (first - 1)))

    def send_pieces(self, half, stage, shares):
        p = self.p

        def one(i, _):
            block = lax.rem(2 * p.chip + 2 + 2 * i + half, p.fsdp)
            for share in shares:
                ref = self.piece(block, share)
                for k in range(1, p.counts[half][1 - stage]):
                    _, replica = p.peer(half, 1 - stage, k)
                    remote(
                        ref,
                        ref,
                        self.passing.at[half, 2 * stage],
                        self.passing.at[half, 2 * stage + 1],
                        replica=replica,
                    ).start()
            return 0

        lax.fori_loop(0, p.chips - 1, one, 0)

    def pass_on(self):
        for half in range(2):
            self.send_pieces(half, 0, [self.p.replica])

    def pass_far(self):
        p = self.p
        for half in range(2):
            await_bytes(self.pass_bytes(half, 0), self.passing.at[half, 1])
            if half == 0:
                shares = [a * p.wide + p.b for a in range(p.high)]
            else:
                shares = [p.a * p.wide + b for b in range(p.wide)]
            self.send_pieces(half, 1, shares)

    def finish(self):
        for half in range(2):
            await_bytes(self.pass_bytes(half, 1), self.passing.at[half, 3])
        await_bytes(self.whole(self.p.sibling), self.near_in)
        self.mine().wait()

    def drain(self):
        await_bytes(self.slab.at[pl.ds(0, self.far_rows())], self.far_out)
        self.near().wait_send()
        for half in range(2):
            await_bytes(self.pass_bytes(half, 0), self.passing.at[half, 0])
            await_bytes(self.pass_bytes(half, 1), self.passing.at[half, 2])


def turn_sems():
    return [pltpu.SemaphoreType.DMA(())] * 5 + [pltpu.SemaphoreType.DMA((2, 4))]


def partner(values):
    halfway = HEAD_DIM // 2
    width = values.shape[1]
    lane = lax.broadcasted_iota(jnp.int32, values.shape, 1) % HEAD_DIM
    return jnp.where(
        lane < halfway,
        pltpu.roll(values, width - halfway, axis=1),
        pltpu.roll(values, halfway, axis=1),
    )


def front_kernel(
    tokens,
    cotangent,
    gain_one,
    gain_two,
    w_query,
    w_key,
    w_value,
    w_out_in,
    w_gate,
    w_up,
    w_down,
    cosine_in,
    sine_in,
    lowered_one,
    lowered_two_out,
    cotangents,
    slab_qkv_out,
    hidden_out,
    grad_gate_out,
    grad_up_out,
    terms_out,
    sums_out,
    queries_out,
    keys_out,
    values_out,
    attended_out,
    logs_out,
    after_out,
    gains,
    w_out,
    cosine,
    sine,
    queries,
    keys,
    values,
    attended,
    logs,
    after_attn,
    low,
    tiles,
    lowered_two,
    slab_qkv,
    slab_gate,
    slab_up,
    held_down,
    terms,
    across,
    slots,
    tile_hidden,
    tile_gate,
    tile_up,
    tile_terms,
    tile_sums,
    gain_rows,
    gain_out,
    gain_in,
    copy_sems,
    load_sems,
    store_sems,
    *sems,
):
    place = Place()
    chips, block = place.chips, tokens.shape[0]
    model, width = tokens.shape[1], queries.shape[1]
    share = gain_one.shape[0]
    tile = 2 * block
    one_at, cot_at, two_at, scatter_at = sems[:6], sems[6:12], sems[12:18], sems[18:24]
    turn_at = [sems[24 + 6 * i : 30 + 6 * i] for i in range(5)]
    turns = [
        Turn(place, weight, slab_qkv, i * model, turn_at[i])
        for i, weight in enumerate((w_query, w_key, w_value))
    ]
    turn_gate = Turn(place, w_gate, slab_gate, 0, turn_at[3])
    turn_up = Turn(place, w_up, slab_up, 0, turn_at[4])
    here = pl.ds(pl.multiple_of(place.me * block, block), block)

    gain_rows[...] = jnp.zeros_like(gain_rows)
    gain_rows[0, :] = gain_one[...].astype(jnp.float32)
    gain_rows[1, :] = gain_two[...].astype(jnp.float32)
    load_down = pltpu.make_async_copy(w_down, held_down, copy_sems.at[0])
    load_down.start()
    loads = [
        pltpu.make_async_copy(source, target, copy_sems.at[5 + i])
        for i, (source, target) in enumerate(((w_out_in, w_out), (cosine_in, cosine), (sine_in, sine)))
    ]
    keeps = [
        pltpu.make_async_copy(source, target, copy_sems.at[8 + i])
        for i, (source, target) in enumerate(
            (
                (queries, queries_out),
                (keys, keys_out),
                (values, values_out),
                (attended, attended_out),
                (logs, logs_out),
                (after_attn, after_out),
            )
        )
    ]
    for copy in loads:
        copy.start()
    keep_cot = pltpu.make_async_copy(cotangent, cotangents.at[here], copy_sems.at[1])
    keep_cot.start()
    place.enter()

    def send_gains(k, _):
        to = lax.rem(place.me + k, place.fsdp)
        remote(gain_rows, gains.at[place.me], gain_out, gain_in, fsdp=to).start()
        return 0

    lax.fori_loop(1, place.fsdp, send_gains, 0)
    for turn in turns:
        turn.start()
    gains[place.me] = gain_rows[...]
    inputs = tokens[...].astype(jnp.float32)
    factor = lax.rsqrt(jnp.mean(inputs * inputs, axis=-1, keepdims=True) + eps_norm)
    await_bytes(gains.at[pl.ds(0, place.fsdp - 1)], gain_in)
    for j in range(model // share):
        at = pl.ds(j * share, share)
        normed = tokens[:, at].astype(jnp.float32) * factor
        low[:, at] = (normed * gains[j, 0:1, :]).astype(jnp.bfloat16)
    first = Gather(place, lowered_one, block, one_at, low)
    first.start()
    keep_low = pltpu.make_async_copy(low, lowered_one.at[here], copy_sems.at[2])
    keep_low.start()
    for turn in turns:
        turn.await_far()
        turn.pass_on()
    for step in range(1, chips):
        first.step(step)
        if step == 1:
            for turn in turns:
                turn.pass_far()
    turn_gate.start()
    turn_up.start()
    third = Gather(place, cotangents, block, cot_at, cotangent)
    third.start()
    keep_low.wait()
    first.finish()

    def load(source, t, slot):
        return pltpu.make_async_copy(rows_at(source, t, tile), tiles.at[slot], load_sems.at[slot])

    load(lowered_one, 0, 0).start()
    for turn in turns:
        turn.finish()
    keep_slab = pltpu.make_async_copy(slab_qkv, slab_qkv_out, copy_sems.at[3])
    keep_slab.start()
    for copy in loads:
        copy.wait()
    for t in range(chips):
        if t + 1 < chips:
            load(lowered_one, t + 1, (t + 1) % 2).start()
        load(lowered_one, t, t % 2).wait()
        at = pl.ds(t * tile, tile)
        for i, ref in enumerate((queries, keys, values)):
            out = dot(tiles[t % 2], slab_qkv[i * model : (i + 1) * model, :])
            if i < 2:
                for j in range(0, width, 2 * HEAD_DIM):
                    pair = out[:, j : j + 2 * HEAD_DIM]
                    pair = pair * cosine[at, :] + partner(pair) * sine[at, :]
                    ref[at, j : j + 2 * HEAD_DIM] = pair.astype(jnp.bfloat16)
            else:
                ref[at, :] = out.astype(jnp.bfloat16)
    scatter = Scatter(place, terms, across, slots, block, scatter_at)
    pair = 2 * HEAD_DIM
    for t in range(chips):
        here_t, seen = pl.ds(t * tile, tile), pl.ds(0, (t + 1) * tile)

        def heads(h, _, t=t, here_t=here_t, seen=seen):
            lanes = pl.ds(pl.multiple_of(h * pair, pair), pair)
            q2, k2, v2 = queries[here_t, lanes], keys[seen, lanes], values[seen, lanes]
            mixed, stats = [], []
            for at in (0, HEAD_DIM):
                head = slice(at, at + HEAD_DIM)
                scores = scores_of(q2[:, head], k2[:, head], t * tile)
                most = jnp.max(scores, axis=-1, keepdims=True)
                weights = jnp.exp(scores - most)
                total = jnp.sum(weights, axis=-1, keepdims=True)
                mixed.append(dot((weights / total).astype(jnp.bfloat16), v2[:, head]))
                stats.append(jnp.broadcast_to(most + jnp.log(total), (tile, HEAD_DIM)))
            attended[here_t, lanes] = jnp.concatenate(mixed, axis=1).astype(jnp.bfloat16)
            logs[here_t, lanes] = jnp.concatenate(stats, axis=1)
            return 0

        lax.fori_loop(0, width // pair, heads, 0)
        terms[here_t, :] = dot(attended[here_t, :], w_out[...]).astype(jnp.bfloat16)
        scatter.side(t).start()
    for keep in keeps[:5]:
        keep.start()
    turn_gate.await_far()
    turn_gate.pass_on()
    for t in range(chips):
        scatter.cross(t)
    for step in range(1, chips):
        scatter.step(step)
        if step == 1:
            turn_gate.pass_far()
            turn_up.await_far()
            turn_up.pass_on()
        if step < chips - 1:
            third.step(step)
        if step == max(chips - 2, 1):
            turn_up.pass_far()
    scatter.finish(after_attn)
    after_attn[...] += tokens[...].astype(jnp.float32)
    after = after_attn[...]
    factor = lax.rsqrt(jnp.mean(after * after, axis=-1, keepdims=True) + eps_norm)
    for j in range(model // share):
        at = pl.ds(j * share, share)
        normed = after_attn[:, at] * factor
        lowered_two[here, at] = (normed * gains[j, 1:2, :]).astype(jnp.bfloat16)
    second = Gather(place, lowered_two, block, two_at)
    second.start()
    keeps[5].start()
    third.step(chips - 1)
    keep_cot.wait()
    third.finish()
    load(cotangents, place.nearest(0), 0).start()
    turn_gate.finish()
    turn_up.finish()
    load_down.wait()

    def stores(k, t):
        slot = k % 2
        pairs = (
            (tile_hidden, hidden_out),
            (tile_gate, grad_gate_out),
            (tile_up, grad_up_out),
            (tile_terms, terms_out),
            (tile_sums, sums_out),
        )
        return [
            pltpu.make_async_copy(held.at[slot], rows_at(out, t, tile), store_sems.at[i, slot])
            for i, (held, out) in enumerate(pairs)
        ]

    for k in range(chips):
        t, slot = place.nearest(k), k % 2
        if k > 0:
            second.step(k)
        second.across(t)
        if k + 1 < chips:
            load(cotangents, place.nearest(k + 1), (k + 1) % 2).start()
        load(cotangents, t, slot).wait()
        if k > 1:
            for store in stores(k - 2, place.nearest(k - 2)):
                store.wait()
        rows = lowered_two[pl.ds(pl.multiple_of(t * tile, tile), tile), :]
        gate = dot(rows, slab_gate[...])
        up = dot(rows, slab_up[...])
        grad_hidden = contract_last(tiles[slot], held_down[...])
        sigmoid = jax.nn.sigmoid(gate)
        silu = gate * sigmoid
        hidden = (silu * up).astype(jnp.bfloat16)
        grad_gate = (grad_hidden * up * sigmoid * (1.0 + gate * (1.0 - sigmoid))).astype(jnp.bfloat16)
        grad_up = (grad_hidden * silu).astype(jnp.bfloat16)
        tile_hidden[slot] = hidden
        tile_gate[slot] = grad_gate
        tile_up[slot] = grad_up
        got = contract_last(grad_gate, slab_gate[...]) + contract_last(grad_up, slab_up[...])
        tile_terms[slot] = got.astype(jnp.bfloat16)
        tile_sums[slot] = dot(hidden, held_down[...]).astype(jnp.bfloat16)
        for store in stores(k, t):
            store.start()
    keep_two = pltpu.make_async_copy(lowered_two, lowered_two_out, copy_sems.at[4])
    keep_two.start()
    second.drain()
    scatter.drain()
    for turn in turns + [turn_gate, turn_up]:
        turn.drain()
    await_bytes(gains.at[pl.ds(0, place.fsdp - 1)], gain_out)
    keep_slab.wait()
    for keep in keeps:
        keep.wait()
    for k in range(max(chips - 2, 0), chips):
        for store in stores(k, place.nearest(k)):
            store.wait()
    keep_two.wait()


def front(
    tokens, cotangent, gain_one, gain_two, w_query, w_key, w_value, w_out, w_gate, w_up, w_down, cosine, sine
):
    fsdp = lax.axis_size("fsdp")
    chips = fsdp // 2
    block, model = tokens.shape
    rows, width, wide = fsdp * block, w_query.shape[1] // fsdp, w_gate.shape[1] // fsdp
    tile = 2 * block
    share = gain_one.shape[0]
    low, full = jnp.bfloat16, jnp.float32
    hbm, vmem = pl.BlockSpec(memory_space=pl.ANY), pl.BlockSpec(memory_space=pltpu.VMEM)
    shape = jax.ShapeDtypeStruct
    dma = pltpu.SemaphoreType.DMA
    return pl.pallas_call(
        front_kernel,
        in_specs=[vmem] * 4 + [hbm] * 9,
        out_specs=[hbm] * 15 + [vmem],
        out_shape=[
            shape((rows, model), low),
            shape((rows, model), low),
            shape((rows, model), low),
            shape((3 * model, width), low),
            shape((rows, wide), low),
            shape((rows, wide), low),
            shape((rows, wide), low),
            shape((rows, model), low),
            shape((rows, model), low),
            shape((rows, width), low),
            shape((rows, width), low),
            shape((rows, width), low),
            shape((rows, width), low),
            shape((rows, width), full),
            shape((block, model), full),
            shape((fsdp, 8, share), full),
        ],
        scratch_shapes=[
            pltpu.VMEM(w_out.shape, low),
            pltpu.VMEM(cosine.shape, full),
            pltpu.VMEM(sine.shape, full),
            pltpu.VMEM((rows, width), low),
            pltpu.VMEM((rows, width), low),
            pltpu.VMEM((rows, width), low),
            pltpu.VMEM((rows, width), low),
            pltpu.VMEM((rows, width), full),
            pltpu.VMEM((block, model), full),
            pltpu.VMEM((block, model), low),
            pltpu.VMEM((2, tile, model), low),
            pltpu.VMEM((rows, model), low),
            pltpu.VMEM((3 * model, width), low),
            pltpu.VMEM((model, wide), low),
            pltpu.VMEM((model, wide), low),
            pltpu.VMEM((wide, model), low),
            pltpu.VMEM((rows, model), low),
            pltpu.VMEM((chips * block, model), low),
            pltpu.VMEM((chips + 1, block, model), low),
            pltpu.VMEM((2, tile, wide), low),
            pltpu.VMEM((2, tile, wide), low),
            pltpu.VMEM((2, tile, wide), low),
            pltpu.VMEM((2, tile, model), low),
            pltpu.VMEM((2, tile, model), low),
            pltpu.VMEM((8, share), full),
            dma(()),
            dma(()),
            dma((14,)),
            dma((2,)),
            dma((5, 2)),
        ]
        + line_sems(chips) * 3
        + scatter_sems(chips)
        + turn_sems() * 5,
        compiler_params=pltpu.CompilerParams(
            collective_id=0, has_side_effects=True, vmem_limit_bytes=VMEM_LIMIT
        ),
        name="front",
    )(
        tokens,
        cotangent,
        gain_one,
        gain_two,
        w_query,
        w_key,
        w_value,
        w_out,
        w_gate,
        w_up,
        w_down,
        cosine,
        sine,
    )


class Reduce:
    def __init__(self, place, part, first, second, sems):
        self.p, self.part, self.first, self.second, self.sems = place, part, first, second, sems
        self.half = part.shape[0] // 2

    def rows(self, half):
        return pl.ds(half * self.half, self.half)

    def sent(self, half, to):
        if half == 0:
            return self.part.at[self.rows(0), :, to]
        return self.part.at[self.rows(1), to]

    def own(self, half):
        return self.sent(half, self.p.b if half == 0 else self.p.a)

    def start(self, half):
        for k in range(1, self.p.counts[half][0]):
            to, replica = self.p.peer(half, 0, k)
            remote(
                self.sent(half, to),
                self.first[half].at[k - 1],
                self.sems.at[half, 0],
                self.sems.at[half, 1],
                replica=replica,
            ).start()

    def exchange(self):
        for half in range(2):
            own, arrived = self.own(half), self.first[half]
            await_bytes(arrived, self.sems.at[half, 1])

            def add(n, _, own=own, arrived=arrived):
                for m in range(own.shape[1]):
                    total = own[n, m].astype(jnp.float32)
                    for k in range(arrived.shape[0]):
                        total += arrived[k, n, m].astype(jnp.float32)
                    own[n, m] = total.astype(own.dtype)
                return 0

            lax.fori_loop(0, self.half, add, 0)
            for k in range(1, self.p.counts[half][1]):
                to, replica = self.p.peer(half, 1, k)
                remote(
                    own.at[:, to],
                    self.second[half].at[k - 1],
                    self.sems.at[half, 2],
                    self.sems.at[half, 3],
                    replica=replica,
                ).start()

    def total(self):
        for half in range(2):
            own, arrived = self.held(half), self.second[half]
            await_bytes(arrived, self.sems.at[half, 3])

            def add(n, _, own=own, arrived=arrived):
                total = own[n].astype(jnp.float32)
                for k in range(arrived.shape[0]):
                    total += arrived[k, n].astype(jnp.float32)
                own[n] = total.astype(own.dtype)
                return 0

            lax.fori_loop(0, self.half, add, 0)

    def held(self, half):
        return self.part.at[self.rows(half), self.p.a, self.p.b]

    def piece(self, n):
        return self.part.at[n, self.p.a, self.p.b]

    def drain(self):
        for half in range(2):
            await_bytes(self.first[half], self.sems.at[half, 0])
            await_bytes(self.second[half], self.sems.at[half, 2])


def reduce_scratch(n, high, wide, rows, columns):
    low = functools.partial(pltpu.VMEM, dtype=jnp.bfloat16)
    half = n // 2
    return [
        low((n, high, wide, rows, columns)),
        low((wide - 1, half, high, rows, columns)),
        low((high - 1, half, wide, rows, columns)),
        low((high - 1, half, rows, columns)),
        low((wide - 1, half, rows, columns)),
        pltpu.SemaphoreType.DMA((2, 4)),
    ]


def reducer(place, refs):
    part, first_a, first_b, second_a, second_b, sems = refs
    return Reduce(place, part, (first_a, first_b), (second_a, second_b), sems)


class Spread:
    def __init__(self, place, piece, out, sems, turned):
        self.p, self.piece, self.out, self.sems, self.turned = place, piece, out, sems, turned

    def start(self):
        p = self.p
        if self.turned:
            count = self.out.shape[0]
            width = self.out.shape[-1] // p.fsdp
            columns = pl.ds(pl.multiple_of(p.me * width, width), width)

            def pairs(to):
                ref = self.piece(to)
                return [
                    (ref.at[:, pl.ds(i * width, width)], self.out.at[i, p.a, p.b, :, columns])
                    for i in range(count)
                ]

            def send(k, _):
                to = lax.rem(p.me + k, p.fsdp)
                for ref, target in pairs(to):
                    remote(ref, target, self.sems.at[0, 0], self.sems.at[0, 1], fsdp=to).start()
                return 0

            lax.fori_loop(1, p.fsdp, send, 0)
            for ref, target in pairs(p.me):
                pltpu.make_async_copy(ref, target, self.sems.at[0, 1]).start()
        else:
            for half in range(2):
                pltpu.make_async_copy(
                    self.piece(half), self.out.at[half, p.a, p.b], self.sems.at[half, 1]
                ).start()

    def placed(self, half, rows):
        a, b = rows
        if self.turned:
            width = self.out.shape[-1] // 2
            return self.out.at[:, a, b, :, pl.ds(half * width, width)]
        return self.out.at[half, a, b]

    def spread(self):
        p = self.p
        if self.turned:
            await_bytes(self.out.at[:, p.a, p.b], self.sems.at[0, 1])
        for half in range(2):
            ref = self.placed(half, (p.a, p.b))
            src = ref if self.turned else self.piece(half)
            for k in range(1, p.counts[half][1]):
                _, replica = p.peer(half, 1, k)
                remote(src, ref, self.sems.at[half, 2], self.sems.at[half, 3], replica=replica).start()

    def spread_bytes(self, half):
        some = pl.ds(0, self.p.counts[half][1] - 1)
        return self.placed(half, (some, 0) if half == 0 else (0, some))

    def widen(self):
        p = self.p
        for half in range(2):
            if not self.turned:
                await_bytes(self.placed(half, (p.a, p.b)), self.sems.at[half, 1])
            await_bytes(self.spread_bytes(half), self.sems.at[half, 3])
            every = pl.ds(0, p.counts[half][1])
            ref = self.placed(half, (every, p.b) if half == 0 else (p.a, every))
            for k in range(1, p.counts[half][0]):
                _, replica = p.peer(half, 0, k)
                remote(ref, ref, self.sems.at[half, 4], self.sems.at[half, 5], replica=replica).start()

    def widen_bytes(self, half):
        counts = self.p.counts[half]
        every, some = pl.ds(0, counts[1]), pl.ds(0, counts[0] - 1)
        return self.placed(half, (every, some) if half == 0 else (some, every))

    def finish(self):
        p = self.p
        for half in range(2):
            await_bytes(self.widen_bytes(half), self.sems.at[half, 5])
            await_bytes(self.spread_bytes(half), self.sems.at[half, 2])
            await_bytes(self.widen_bytes(half), self.sems.at[half, 4])
        if self.turned:
            width = self.out.shape[-1] // p.fsdp
            await_bytes(
                self.out.at[:, p.a, p.b, :, pl.ds(0, (p.fsdp - 1) * width)], self.sems.at[0, 0]
            )


def spread_sems():
    return [pltpu.SemaphoreType.DMA((2, 6))]


def norm_back(values, gain_row, gains, grad, carried, result, gain_terms):
    block, model = values.shape
    share = gains.shape[2]
    held = values[...].astype(jnp.float32)
    factor = lax.rsqrt(jnp.mean(held * held, axis=-1, keepdims=True) + eps_norm)
    dots = jnp.zeros((block, 1), jnp.float32)
    for j in range(model // share):
        at = pl.ds(j * share, share)
        normed = values[:, at].astype(jnp.float32) * factor
        product = grad[:, at] * normed
        gain_terms[j, gain_row : gain_row + 1, :] = jnp.sum(product, axis=0, keepdims=True)
        dots += jnp.sum(product * gains[j, gain_row : gain_row + 1, :], axis=-1, keepdims=True)
    dots = dots / model
    for j in range(model // share):
        at = pl.ds(j * share, share)
        normed = values[:, at].astype(jnp.float32) * factor
        scaled = grad[:, at] * gains[j, gain_row : gain_row + 1, :]
        result[:, at] = carried[:, at].astype(jnp.float32) + factor * (scaled - normed * dots)


def weigh_kernel(
    cotangent,
    after_in,
    gains,
    terms_in,
    lowered_two,
    cotangents,
    hidden_in,
    grad_gate_in,
    grad_up_in,
    w_out_in,
    queries_in,
    keys_in,
    values_in,
    logs_in,
    cosine_in,
    sine_in,
    gain_terms,
    grad_after_out,
    grads_out,
    branch,
    sum_down,
    sum_gate,
    sum_up,
    after_attn,
    w_out,
    queries,
    keys,
    values,
    logs,
    cosine,
    sine,
    grad_after,
    grads,
    tokens_held,
    hidden,
    grad_gate,
    grad_up,
    terms,
    across,
    slots,
    summed,
    low,
    grad_low,
    grad_key,
    grad_value,
    load_sems,
    store_sems,
    late_sems,
    *rest,
):
    place = Place()
    chips, block = place.chips, cotangent.shape[0]
    model = cotangent.shape[1]
    tile = 2 * block
    scatter_at, gather_at = rest[:6], rest[6:12]
    down, gate, up = [reducer(place, rest[12 + 6 * i : 18 + 6 * i]) for i in range(3)]

    def load(t):
        at = pl.ds(t * tile, tile)
        return pltpu.make_async_copy(terms_in.at[at], terms.at[at], load_sems.at[t])

    loads = [
        pltpu.make_async_copy(source, target, load_sems.at[chips + i])
        for i, (source, target) in enumerate(
            (
                (cotangents, tokens_held),
                (hidden_in, hidden),
                (grad_gate_in, grad_gate),
                (grad_up_in, grad_up),
                (lowered_two, tokens_held),
            )
        )
    ]
    for t in range(chips):
        load(t).start()
    for copy in loads[:4]:
        copy.start()
    late = [
        pltpu.make_async_copy(source, target, late_sems.at[i])
        for i, (source, target) in enumerate(
            (
                (after_in, after_attn),
                (w_out_in, w_out),
                (queries_in, queries),
                (keys_in, keys),
                (values_in, values),
                (logs_in, logs),
                (cosine_in, cosine),
                (sine_in, sine),
            )
        )
    ]
    for copy in late:
        copy.start()
    keep_after = pltpu.make_async_copy(grad_after, grad_after_out, late_sems.at[8])
    keep_grads = pltpu.make_async_copy(grads, grads_out, late_sems.at[9])
    place.enter()
    scatter = Scatter(place, terms, across, slots, block, scatter_at)
    for t in range(chips):
        load(t).wait()
        scatter.side(t).start()
    gain_terms[...] = jnp.zeros_like(gain_terms)
    loads[0].wait()
    loads[1].wait()
    _, high, wide, thin, _ = down.part.shape
    columns = min(tile, hidden.shape[1])
    for i in range(0, hidden.shape[1], columns):
        got = contract_first(hidden[:, i : i + columns], tokens_held[...]).astype(jnp.bfloat16)
        for m in range(0, columns, thin):
            n = (i + m) // thin
            down.part[n // (high * wide), n // wide % high, n % wide] = got[m : m + thin, :]
        if 2 * (i + columns) == hidden.shape[1]:
            down.start(0)
    loads[4].start()
    down.start(1)
    for t in range(chips):
        scatter.cross(t)
    scatter.step(1)
    loads[4].wait()

    def weigh(reduce, grads):
        share = model // place.fsdp

        def rows(j, _):
            left = tokens_held[:, pl.ds(pl.multiple_of(j * share, share), share)]
            got = contract_first(left, grads[...]).astype(jnp.bfloat16)
            reduce.part[j] = got.reshape(reduce.part.shape[1:])
            return 0

        for half in range(2):
            lax.fori_loop(half * chips, (half + 1) * chips, rows, 0)
            reduce.start(half)

    loads[2].wait()
    weigh(gate, grad_gate)
    if chips > 2:
        scatter.step(2)
    loads[3].wait()
    weigh(up, grad_up)
    for step in range(3, chips):
        scatter.step(step)
    scatter.finish(summed)
    late[0].wait()
    norm_back(after_attn, 1, gains, summed, cotangent, grad_after, gain_terms)
    keep_after.start()
    low[...] = grad_after[...].astype(jnp.bfloat16)
    here = pl.ds(pl.multiple_of(place.me * block, block), block)
    gather = Gather(place, branch, block, gather_at, low)
    gather.start()
    keep = pltpu.make_async_copy(low, branch.at[here], store_sems.at[0])
    keep.start()
    scatter.drain()
    down.exchange()
    for step in range(1, chips):
        gather.step(step)
        if step == 1:
            gate.exchange()
        if step == max(chips - 2, 1):
            up.exchange()
    keep.wait()
    gather.finish()
    fetch = pltpu.make_async_copy(branch, tokens_held, load_sems.at[0])
    fetch.start()
    down.total()
    fetch.wait()
    for copy in late[1:]:
        copy.wait()

    def attend_rows(t, _):
        at = pl.ds(pl.multiple_of(t * tile, tile), tile)
        grad_low[at, :] = contract_last(tokens_held[at, :], w_out[...]).astype(jnp.bfloat16)
        return 0

    lax.fori_loop(0, chips, attend_rows, 0)
    width = queries.shape[1]
    scale = HEAD_DIM**-0.5
    grad_key[...] = jnp.zeros_like(grad_key)
    grad_value[...] = jnp.zeros_like(grad_value)
    pair = 2 * HEAD_DIM
    height = tile * 1024 // max(queries.shape[0], 1024)
    for first in range(0, queries.shape[0], height):
        rows, seen = pl.ds(first, height), pl.ds(0, first + height)

        def heads(h, _, first=first, rows=rows, seen=seen):
            lanes = pl.ds(pl.multiple_of(h * pair, pair), pair)
            q2, g2, log2 = queries[rows, lanes], grad_low[rows, lanes], logs[rows, lanes]
            k2, v2 = keys[seen, lanes], values[seen, lanes]
            for_queries, for_keys, for_values = [], [], []
            for at in (0, HEAD_DIM):
                head = slice(at, at + HEAD_DIM)
                q, g, k = q2[:, head], g2[:, head], k2[:, head]
                weights = jnp.exp(scores_of(q, k, first) - log2[:, at : at + 1])
                grad_weights = contract_last(g, v2[:, head])
                delta = jnp.sum(weights * grad_weights, axis=-1, keepdims=True)
                grad_scores = (weights * (grad_weights - delta)).astype(jnp.bfloat16)
                for_queries.append(dot(grad_scores, k))
                for_keys.append(contract_first(grad_scores, q))
                for_values.append(contract_first(weights.astype(jnp.bfloat16), g))
            got = jnp.concatenate(for_queries, axis=1) * scale
            got = got * cosine[rows, :] - partner(got) * sine[rows, :]
            grads[rows, lanes] = got.astype(jnp.bfloat16)
            grad_key[seen, lanes] += jnp.concatenate(for_keys, axis=1) * scale
            grad_value[seen, lanes] += jnp.concatenate(for_values, axis=1)
            return 0

        lax.fori_loop(0, width // pair, heads, 0)

    def turn_keys(t, _):
        at = pl.ds(pl.multiple_of(t * tile, tile), tile)
        for j in range(0, width, pair):
            got = grad_key[at, j : j + pair]
            got = got * cosine[at, :] - partner(got) * sine[at, :]
            grads[at, width + j : width + j + pair] = got.astype(jnp.bfloat16)
        grads[at, 2 * width :] = grad_value[at, :].astype(jnp.bfloat16)
        return 0

    lax.fori_loop(0, chips, turn_keys, 0)
    keep_grads.start()
    stores = [keep_after, keep_grads]
    for i, (reduce, out) in enumerate(((down, sum_down), (gate, sum_gate), (up, sum_up))):
        if i > 0:
            reduce.total()
        for half in range(2):
            store = pltpu.make_async_copy(
                reduce.held(half), out.at[reduce.rows(half)], store_sems.at[1 + 2 * i + half]
            )
            store.start()
            stores.append(store)
    for reduce in (down, gate, up):
        reduce.drain()
    for store in stores:
        store.wait()


def weigh(
    cotangent,
    after_attn,
    gains,
    terms,
    lowered_two,
    cotangents,
    hidden,
    grad_gate,
    grad_up,
    w_out,
    queries,
    keys,
    values,
    logs,
    cosine,
    sine,
):
    fsdp, replicas = lax.axis_size("fsdp"), lax.axis_size("replica")
    chips, high, wide = fsdp // 2, 2, replicas // 2
    block, model = cotangent.shape
    rows, columns = hidden.shape
    width = queries.shape[1]
    share = gains.shape[2]
    low, full = jnp.bfloat16, jnp.float32
    hbm, vmem = pl.BlockSpec(memory_space=pl.ANY), pl.BlockSpec(memory_space=pltpu.VMEM)
    shape = jax.ShapeDtypeStruct
    down_piece = (2, high, wide, columns // (2 * replicas), model)
    wide_piece = (fsdp, high, wide, share // replicas, columns)
    dma = pltpu.SemaphoreType.DMA
    return pl.pallas_call(
        weigh_kernel,
        in_specs=[vmem, hbm, vmem] + [hbm] * 13,
        out_specs=[vmem] + [hbm] * 6,
        out_shape=[
            shape((fsdp, 8, share), full),
            shape((block, model), full),
            shape((rows, 3 * width), low),
            shape((rows, model), low),
            shape((2,) + down_piece[3:], low),
            shape((fsdp,) + wide_piece[3:], low),
            shape((fsdp,) + wide_piece[3:], low),
        ],
        scratch_shapes=[
            pltpu.VMEM((block, model), full),
            pltpu.VMEM(w_out.shape, low),
            pltpu.VMEM((rows, width), low),
            pltpu.VMEM((rows, width), low),
            pltpu.VMEM((rows, width), low),
            pltpu.VMEM((rows, width), full),
            pltpu.VMEM(cosine.shape, full),
            pltpu.VMEM(sine.shape, full),
            pltpu.VMEM((block, model), full),
            pltpu.VMEM((rows, 3 * width), low),
            pltpu.VMEM((rows, model), low),
            pltpu.VMEM((rows, columns), low),
            pltpu.VMEM((rows, columns), low),
            pltpu.VMEM((rows, columns), low),
            pltpu.VMEM((rows, model), low),
            pltpu.VMEM((chips * block, model), low),
            pltpu.VMEM((chips + 1, block, model), low),
            pltpu.VMEM((block, model), full),
            pltpu.VMEM((block, model), low),
            pltpu.VMEM((rows, width), low),
            pltpu.VMEM((rows, width), full),
            pltpu.VMEM((rows, width), full),
            dma((chips + 5,)),
            dma((7,)),
            dma((10,)),
        ]
        + scatter_sems(chips)
        + line_sems(chips)
        + reduce_scratch(*down_piece)
        + reduce_scratch(*wide_piece)
        + reduce_scratch(*wide_piece),
        compiler_params=pltpu.CompilerParams(
            collective_id=1, has_side_effects=True, vmem_limit_bytes=VMEM_LIMIT
        ),
        name="weigh",
    )(
        cotangent,
        after_attn,
        gains,
        terms,
        lowered_two,
        cotangents,
        hidden,
        grad_gate,
        grad_up,
        w_out,
        queries,
        keys,
        values,
        logs,
        cosine,
        sine,
    )


def back_kernel(
    tokens,
    gains,
    grad_after_in,
    gain_terms_in,
    after_in,
    sums,
    sum_down,
    sum_gate,
    sum_up,
    branch_in,
    lowered_one,
    slab_in,
    attended_in,
    grads_in,
    outputs,
    grad_tokens,
    gain_out,
    out_down,
    out_gate,
    out_up,
    out_qkv,
    out_out,
    grad_after,
    after_attn,
    slab_qkv,
    attended,
    grads,
    terms,
    across,
    slots,
    branch,
    summed,
    gain_terms,
    gain_slots,
    gain_sums,
    gain_sems,
    load_sems,
    *rest,
):
    place = Place()
    chips, block = place.chips, tokens.shape[0]
    model, width = tokens.shape[1], attended.shape[1]
    share = gains.shape[2]
    tile = 2 * block
    scatter_at, rest = rest[:6], rest[6:]
    down = Spread(place, lambda n: sum_down.at[n], out_down, rest[0], False)
    gate = Spread(place, lambda n: sum_gate.at[n], out_gate, rest[1], True)
    up = Spread(place, lambda n: sum_up.at[n], out_up, rest[2], True)
    qkv, out = reducer(place, rest[5:11]), reducer(place, rest[11:17])
    qkv_spread = Spread(place, qkv.piece, out_qkv, rest[3], True)
    out_spread = Spread(place, out.piece, out_out, rest[4], False)
    load = pltpu.make_async_copy(lowered_one, branch, load_sems.at[0])
    load.start()
    loads = [
        pltpu.make_async_copy(source, target, load_sems.at[2 + i])
        for i, (source, target) in enumerate(
            (
                (grads_in, grads),
                (slab_in, slab_qkv),
                (attended_in, attended),
                (grad_after_in, grad_after),
                (after_in, after_attn),
            )
        )
    ]
    for copy in loads:
        copy.start()
    place.enter()
    down.start()
    down.spread()
    gate.start()
    load.wait()
    loads[0].wait()

    def weigh_rows(j, _):
        left = branch[:, pl.ds(pl.multiple_of(j * share, share), share)]
        got = contract_first(left, grads[...]).astype(jnp.bfloat16)
        qkv.part[j] = got.reshape(qkv.part.shape[1:])
        return 0

    for half in range(2):
        lax.fori_loop(half * chips, (half + 1) * chips, weigh_rows, 0)
        qkv.start(half)
    reload = pltpu.make_async_copy(branch_in, branch, load_sems.at[1])
    reload.start()
    scatter = Scatter(place, terms, across, slots, block, scatter_at)

    def back_rows(t, _):
        at = pl.ds(pl.multiple_of(t * tile, tile), tile)
        got = contract_last(grads[at, :width], slab_qkv[:model, :])
        got += contract_last(grads[at, width : 2 * width], slab_qkv[model : 2 * model, :])
        got += contract_last(grads[at, 2 * width :], slab_qkv[2 * model :, :])
        terms[at, :] = got.astype(jnp.bfloat16)
        return 0

    loads[1].wait()
    lax.fori_loop(0, chips, back_rows, 0)
    for t in range(chips):
        scatter.side(t).start()
    down.widen()
    reload.wait()
    loads[2].wait()
    _, high, wide, thin, columns = out.part.shape
    for half in range(2):
        for at in range(0, columns, 512):
            got = contract_first(
                attended[...], branch[:, half * columns + at : half * columns + at + 512]
            ).astype(jnp.bfloat16)
            out.part[half, :, :, :, at : at + 512] = got.reshape(high, wide, thin, 512)
    out.start(0)
    out.start(1)
    for t in range(chips):
        scatter.cross(t)
    scatter.step(1)
    gate.spread()
    qkv.exchange()
    for step in range(2, chips):
        scatter.step(step)
    up.start()
    scatter.finish(summed)
    gain_terms[...] = gain_terms_in[...]
    loads[3].wait()
    loads[4].wait()
    norm_back(tokens, 0, gains, summed, grad_after, grad_tokens, gain_terms)

    def send_gain(k, _):
        to = lax.rem(place.me + k, place.fsdp)
        remote(
            gain_terms.at[to], gain_slots.at[place.me], gain_sems.at[0], gain_sems.at[1], fsdp=to
        ).start()
        return 0

    lax.fori_loop(1, place.fsdp, send_gain, 0)
    gain_slots[place.me] = gain_terms[place.me]
    scatter.drain()
    load_sums = pltpu.make_async_copy(sums, terms, load_sems.at[0])
    load_sums.start()
    out.exchange()
    gate.widen()
    qkv.total()
    qkv_spread.start()
    await_bytes(gain_slots.at[pl.ds(0, place.fsdp - 1)], gain_sems.at[1])
    gain_sums[place.replica] = jnp.sum(gain_slots[...], axis=0)

    def send_sum(k, _):
        ref = gain_sums.at[place.replica]
        to = lax.rem(place.replica + k, place.replicas)
        remote(ref, ref, gain_sems.at[2], gain_sems.at[3], replica=to).start()
        return 0

    lax.fori_loop(1, place.replicas, send_sum, 0)

    load_sums.wait()
    for t in range(chips):
        scatter.side(t).start()
    up.spread()
    for t in range(chips):
        scatter.cross(t)
    scatter.step(1)
    out.total()
    out_spread.start()
    out_spread.spread()
    qkv_spread.spread()
    up.widen()
    for step in range(2, chips):
        scatter.step(step)
    out_spread.widen()
    scatter.finish(summed)
    outputs[...] = (summed[...] + after_attn[...]).astype(outputs.dtype)
    qkv_spread.widen()
    await_bytes(gain_sums.at[pl.ds(0, place.replicas - 1)], gain_sems.at[3])
    gain_out[...] = jnp.sum(gain_sums[...], axis=0)
    await_bytes(gain_slots.at[pl.ds(0, place.fsdp - 1)], gain_sems.at[0])
    await_bytes(gain_sums.at[pl.ds(0, place.replicas - 1)], gain_sems.at[2])
    scatter.drain()
    qkv.drain()
    out.drain()
    for spread in (down, gate, up, out_spread, qkv_spread):
        spread.finish()


def back(
    tokens,
    gains,
    grad_after,
    gain_terms,
    after_attn,
    sums,
    sum_down,
    sum_gate,
    sum_up,
    branch,
    lowered_one,
    slab_qkv,
    attended,
    grads,
):
    fsdp, replicas = lax.axis_size("fsdp"), lax.axis_size("replica")
    chips, high, wide = fsdp // 2, 2, replicas // 2
    block, model = tokens.shape
    rows, width = attended.shape
    share = gains.shape[2]
    low, full = jnp.bfloat16, jnp.float32
    hbm, vmem = pl.BlockSpec(memory_space=pl.ANY), pl.BlockSpec(memory_space=pltpu.VMEM)
    shape = jax.ShapeDtypeStruct
    thin = share // replicas
    columns = sum_gate.shape[-1]
    qkv_piece = (fsdp, high, wide, thin, 3 * width)
    out_piece = (2, high, wide, width // replicas, model // 2)
    dma = pltpu.SemaphoreType.DMA
    return pl.pallas_call(
        back_kernel,
        in_specs=[vmem, vmem, hbm, vmem] + [hbm] * 10,
        out_specs=[vmem] * 3 + [hbm] * 5,
        out_shape=[
            shape((block, model), low),
            shape((block, model), full),
            shape((8, share), full),
            shape((2, high, wide) + sum_down.shape[1:], low),
            shape((1, high, wide, thin, fsdp * columns), low),
            shape((1, high, wide, thin, fsdp * columns), low),
            shape((3, high, wide, thin, fsdp * width), low),
            shape(out_piece, low),
        ],
        scratch_shapes=[
            pltpu.VMEM((block, model), full),
            pltpu.VMEM((block, model), full),
            pltpu.VMEM(slab_qkv.shape, low),
            pltpu.VMEM((rows, width), low),
            pltpu.VMEM((rows, 3 * width), low),
            pltpu.VMEM((rows, model), low),
            pltpu.VMEM((chips * block, model), low),
            pltpu.VMEM((chips + 1, block, model), low),
            pltpu.VMEM((rows, model), low),
            pltpu.VMEM((block, model), full),
            pltpu.VMEM((fsdp, 8, share), full),
            pltpu.VMEM((fsdp, 8, share), full),
            pltpu.VMEM((replicas, 8, share), full),
            dma((4,)),
            dma((7,)),
        ]
        + scatter_sems(chips)
        + spread_sems() * 5
        + reduce_scratch(*qkv_piece)
        + reduce_scratch(*out_piece),
        compiler_params=pltpu.CompilerParams(
            collective_id=2, has_side_effects=True, vmem_limit_bytes=VMEM_LIMIT
        ),
        name="back",
    )(
        tokens,
        gains,
        grad_after,
        gain_terms,
        after_attn,
        sums,
        sum_down,
        sum_gate,
        sum_up,
        branch,
        lowered_one,
        slab_qkv,
        attended,
        grads,
    )


def widen_kernel(
    down,
    gate,
    up,
    qkv,
    out,
    outputs_in,
    tokens_in,
    gains,
    w_down,
    w_gate,
    w_up,
    w_query,
    w_key,
    w_value,
    w_out,
    outputs,
    grad_tokens,
    gain_one,
    gain_two,
):
    w_down[...] = down[...].astype(jnp.float32)
    w_gate[...] = gate[...].astype(jnp.float32)
    w_up[...] = up[...].astype(jnp.float32)
    for i, ref in enumerate((w_query, w_key, w_value)):
        ref[...] = qkv[i].astype(jnp.float32)
    half = out.shape[2]
    for i in range(2):
        w_out[:, i * half : (i + 1) * half] = out[i].astype(jnp.float32)
    outputs[...] = outputs_in[...]
    grad_tokens[...] = tokens_in[...]
    gain_one[...] = gains[0, :]
    gain_two[...] = gains[1, :]


def widen(down, gate, up, qkv, out, outputs, grad_tokens, gains):
    steps = min(16, gate.shape[0] // 16)
    token_steps = outputs.shape[0] // 16
    full = jnp.float32

    def rows(array):
        return pl.BlockSpec((array.shape[0] // steps, array.shape[1]), lambda i: (i, 0))

    def tokens(array):
        return pl.BlockSpec(
            (array.shape[0] // token_steps, array.shape[1]), lambda i: (jnp.minimum(i, token_steps - 1), 0)
        )

    def stacked(array):
        return pl.BlockSpec((array.shape[0], array.shape[1] // steps, array.shape[2]), lambda i: (0, i, 0))

    like = [down, gate, up, qkv[0], qkv[0], qkv[0]]
    shapes = [jax.ShapeDtypeStruct(array.shape, full) for array in like]
    shapes.append(jax.ShapeDtypeStruct((out.shape[1], 2 * out.shape[2]), full))
    row = jax.ShapeDtypeStruct(gains.shape[1:], full)
    whole = pl.BlockSpec(gains.shape, lambda i: (0, 0))
    line = pl.BlockSpec(gains.shape[1:], lambda i: (0,))
    return pl.pallas_call(
        widen_kernel,
        grid=(steps,),
        in_specs=[rows(down), rows(gate), rows(up), stacked(qkv), stacked(out)]
        + [tokens(outputs), tokens(grad_tokens), whole],
        out_specs=[rows(shape) for shape in shapes]
        + [tokens(outputs), tokens(grad_tokens), line, line],
        out_shape=shapes
        + [jax.ShapeDtypeStruct(array.shape, array.dtype) for array in (outputs, grad_tokens)]
        + [row, row],
        compiler_params=pltpu.CompilerParams(vmem_limit_bytes=VMEM_LIMIT),
        name="widen",
    )(down, gate, up, qkv, out, outputs, grad_tokens, gains)


def local(
    tokens, attn_gain, w_query, w_key, w_value, w_out, ffn_gain, w_gate, w_up, w_down, cotangent
):
    cosine, sine = rope_tables(tokens.shape[0] * lax.axis_size("fsdp"))
    (
        lowered_one,
        lowered_two,
        cotangents,
        slab_qkv,
        hidden,
        grad_gate,
        grad_up,
        terms,
        sums,
        queries,
        keys,
        values,
        attended,
        logs,
        after_attn,
        gains,
    ) = front(
        tokens,
        cotangent,
        attn_gain,
        ffn_gain,
        w_query,
        w_key,
        w_value,
        w_out,
        w_gate,
        w_up,
        w_down,
        cosine,
        sine,
    )
    gain_terms, grad_after, grads, branch, sum_down, sum_gate, sum_up = weigh(
        cotangent,
        after_attn,
        gains,
        terms,
        lowered_two,
        cotangents,
        hidden,
        grad_gate,
        grad_up,
        w_out,
        queries,
        keys,
        values,
        logs,
        cosine,
        sine,
    )
    outputs, grad_tokens, gain_grads, low_down, low_gate, low_up, low_qkv, low_out = back(
        tokens,
        gains,
        grad_after,
        gain_terms,
        after_attn,
        sums,
        sum_down,
        sum_gate,
        sum_up,
        branch,
        lowered_one,
        slab_qkv,
        attended,
        grads,
    )
    (
        grad_w_down,
        grad_w_gate,
        grad_w_up,
        grad_w_query,
        grad_w_key,
        grad_w_value,
        grad_w_out,
        outputs,
        grad_tokens,
        grad_attn_gain,
        grad_ffn_gain,
    ) = widen(
        low_down.reshape(w_down.shape),
        low_gate.reshape(w_gate.shape),
        low_up.reshape(w_up.shape),
        low_qkv.reshape((3,) + w_query.shape),
        low_out.reshape(2, w_out.shape[0], -1),
        outputs,
        grad_tokens,
        gain_grads,
    )
    return (
        outputs,
        grad_tokens,
        grad_attn_gain,
        grad_w_query,
        grad_w_key,
        grad_w_value,
        grad_w_out,
        grad_ffn_gain,
        grad_w_gate,
        grad_w_up,
        grad_w_down,
    )


def solution(mesh):
    rows = P("fsdp", None)
    tokens = P(("replica", "fsdp"), None)
    gain = P("fsdp")
    return jax.shard_map(
        local,
        mesh=mesh,
        in_specs=(tokens, gain, rows, rows, rows, rows, gain, rows, rows, rows, tokens),
        out_specs=(tokens, tokens, gain, rows, rows, rows, rows, gain, rows, rows, rows),
        check_vma=False,
    )
```

```python
import functools

import jax
import jax.numpy as jnp
import numpy as np
from jax import lax
from jax.experimental import pallas as pl
from jax.experimental.pallas import tpu as pltpu
from jax.sharding import PartitionSpec as P

HEAD_DIM = 64

eps_norm = 1e-05
rope_base = 130000.0
masked_score = -1e30


def rope_tables(row_count):
    lane = np.arange(2 * HEAD_DIM) % HEAD_DIM
    halfway = HEAD_DIM // 2
    spacing = ((lane % halfway) * np.float32(2.0) / HEAD_DIM).astype(np.float32)
    frequency = np.power(np.float32(rope_base), -spacing)
    angles = np.arange(row_count, dtype=np.float32)[:, None] * frequency[None, :]
    sign = np.where(lane < halfway, -1.0, 1.0).astype(np.float32)
    return np.cos(angles).astype(np.float32), (np.sin(angles) * sign[None, :]).astype(np.float32)


def dot(left, right):
    return jnp.dot(left, right, preferred_element_type=jnp.float32)


def contract_last(left, right):
    return lax.dot_general(
        left, right, (((1,), (1,)), ((), ())), preferred_element_type=jnp.float32
    )


def contract_first(left, right):
    return lax.dot_general(
        left, right, (((0,), (0,)), ((), ())), preferred_element_type=jnp.float32
    )


def scores_of(queries, keys, first_row):
    rows, columns = queries.shape[0], keys.shape[0]
    scores = contract_last(queries, keys) * HEAD_DIM**-0.5
    at_row = lax.broadcasted_iota(jnp.int32, (rows, columns), 0) + first_row
    at_column = lax.broadcasted_iota(jnp.int32, (rows, columns), 1)
    return jnp.where(at_column <= at_row, scores, masked_score)


MESH = pl.DeviceIdType.MESH
VMEM_LIMIT = 61 * 2**20


def remote(src, dst, send, recv, **where):
    return pltpu.make_async_remote_copy(
        src_ref=src, dst_ref=dst, send_sem=send, recv_sem=recv, device_id=where, device_id_type=MESH
    )


def await_bytes(ref, sem):
    pltpu.make_async_copy(ref, ref, sem).wait()


def rows_at(ref, index, size):
    return ref.at[pl.ds(pl.multiple_of(index * size, size), size)]


class Place:
    def __init__(self):
        self.fsdp, self.replicas = lax.axis_size("fsdp"), lax.axis_size("replica")
        self.me, self.replica = lax.axis_index("fsdp"), lax.axis_index("replica")
        self.chips = self.fsdp // 2
        self.chip, self.core = self.me // 2, self.me % 2
        self.sibling = self.me + 1 - 2 * self.core
        self.high, self.wide = 2, self.replicas // 2
        self.a, self.b = self.replica // self.wide, self.replica % self.wide
        self.counts = ((self.wide, self.high), (self.high, self.wide))
        self.above = self.chip + 1 < self.chips
        self.below = self.chip >= 1

    def peer(self, half, stage, k):
        if half == stage:
            to = lax.rem(self.b + k, self.wide)
            return to, self.a * self.wide + to
        to = lax.rem(self.a + k, self.high)
        return to, to * self.wide + self.b

    def nearest(self, k):
        found = jnp.int32(0)
        for chip in range(self.chips):
            order = sorted(range(self.chips), key=lambda other, chip=chip: (abs(other - chip), other))
            found = found + jnp.where(self.chip == chip, order[k], 0)
        return found

    def enter(self):
        barrier = pltpu.get_barrier_semaphore()

        def greet(k, _):
            to = lax.rem(self.me + k, self.fsdp)
            pl.semaphore_signal(barrier, inc=1, device_id={"fsdp": to}, device_id_type=MESH)
            return 0

        def greet_replica(k, _):
            to = lax.rem(self.replica + k, self.replicas)
            pl.semaphore_signal(barrier, inc=1, device_id={"replica": to}, device_id_type=MESH)
            return 0

        lax.fori_loop(1, self.fsdp, greet, 0)
        lax.fori_loop(1, self.replicas, greet_replica, 0)
        pl.semaphore_wait(barrier, self.fsdp - 1 + self.replicas - 1)


def line_sems(chips):
    return [pltpu.SemaphoreType.DMA((chips,))] * 6


class Gather:
    def __init__(self, place, buf, block, sems, own=None):
        self.p, self.buf, self.block, self.own = place, buf, block, own
        self.up_out, self.up_in, self.down_out, self.down_in, self.side_out, self.side_in = sems

    def held(self, chip):
        return rows_at(self.buf, 2 * chip + self.p.core, self.block)

    def up(self, step):
        ref = self.held(self.p.chip - step + 1)
        src = self.own if step == 1 and self.own is not None else ref
        return remote(src, ref, self.up_out.at[step], self.up_in.at[step], fsdp=self.p.me + 2)

    def down(self, step):
        ref = self.held(self.p.chip + step - 1)
        src = self.own if step == 1 and self.own is not None else ref
        return remote(src, ref, self.down_out.at[step], self.down_in.at[step], fsdp=self.p.me - 2)

    def side(self, chip, src=None):
        ref = self.held(chip)
        src = ref if src is None else src
        return remote(src, ref, self.side_out.at[chip], self.side_in.at[chip], fsdp=self.p.sibling)

    def start(self):
        p = self.p
        pl.when(p.above)(lambda: self.up(1).start())
        pl.when(p.below)(lambda: self.down(1).start())
        self.side(p.chip, self.own).start()

    def step(self, step):
        p = self.p
        from_below, from_above = p.chip - step, p.chip + step

        @pl.when(from_below >= 0)
        def _():
            await_bytes(self.held(from_below), self.up_in.at[step])
            if step + 1 < p.chips:
                pl.when(p.above)(lambda: self.up(step + 1).start())
            self.side(from_below).start()

        @pl.when(from_above < p.chips)
        def _():
            await_bytes(self.held(from_above), self.down_in.at[step])
            if step + 1 < p.chips:
                pl.when(p.below)(lambda: self.down(step + 1).start())
            self.side(from_above).start()

    def across(self, chip):
        await_bytes(rows_at(self.buf, 2 * chip + 1 - self.p.core, self.block), self.side_in.at[chip])

    def drain(self):
        p = self.p
        for step in range(1, p.chips):
            pl.when(jnp.logical_and(p.above, p.chip - step + 1 >= 0))(
                lambda step=step: self.up(step).wait_send()
            )
            pl.when(jnp.logical_and(p.below, p.chip + step - 1 < p.chips))(
                lambda step=step: self.down(step).wait_send()
            )
        for chip in range(p.chips):
            self.side(chip).wait_send()

    def finish(self):
        for chip in range(self.p.chips):
            self.across(chip)
        self.drain()


class Scatter:
    def __init__(self, place, terms, across, slots, block, sems):
        self.p, self.terms, self.across, self.slots, self.block = place, terms, across, slots, block
        self.up_out, self.up_in, self.down_out, self.down_in, self.side_out, self.side_in = sems

    def side(self, chip):
        p = self.p
        return remote(
            rows_at(self.terms, 2 * chip + 1 - p.core, self.block),
            rows_at(self.across, chip, self.block),
            self.side_out.at[chip],
            self.side_in.at[chip],
            fsdp=p.sibling,
        )

    def term(self, chip):
        return rows_at(self.terms, 2 * chip + self.p.core, self.block)

    def up(self, step):
        return remote(
            self.term(self.p.chips - step + self.p.chip),
            self.slots.at[step - self.p.chip - 1],
            self.up_out.at[step],
            self.up_in.at[step],
            fsdp=self.p.me + 2,
        )

    def down(self, step):
        return remote(
            self.term(self.p.chip - self.p.chips + step),
            self.slots.at[step + 1],
            self.down_out.at[step],
            self.down_in.at[step],
            fsdp=self.p.me - 2,
        )

    def add(self, chip, arrived):
        term = self.term(chip)
        term[...] = (term[...].astype(jnp.float32) + arrived[...].astype(jnp.float32)).astype(term.dtype)

    def cross(self, chip):
        arrived = rows_at(self.across, chip, self.block)
        await_bytes(arrived, self.side_in.at[chip])
        self.add(chip, arrived)

    def step(self, step):
        p = self.p
        rising, falling = p.chips - step + p.chip, p.chip - p.chips + step

        @pl.when(jnp.logical_and(p.above, rising < p.chips))
        def _():
            if step > 1:

                @pl.when(p.below)
                def _():
                    arrived = self.slots.at[step - 1 - p.chip]
                    await_bytes(arrived, self.up_in.at[step - 1])
                    self.add(rising, arrived)

            self.up(step).start()

        @pl.when(jnp.logical_and(p.below, falling >= 0))
        def _():
            if step > 1:

                @pl.when(p.above)
                def _():
                    arrived = self.slots.at[step]
                    await_bytes(arrived, self.down_in.at[step - 1])
                    self.add(falling, arrived)

            self.down(step).start()

    def finish(self, total):
        p, last = self.p, self.p.chips - 1
        total[...] = self.term(p.chip)[...].astype(jnp.float32)

        @pl.when(p.below)
        def _():
            await_bytes(self.slots.at[last - p.chip], self.up_in.at[last])
            total[...] += self.slots[last - p.chip].astype(jnp.float32)

        @pl.when(p.above)
        def _():
            await_bytes(self.slots.at[last + 1], self.down_in.at[last])
            total[...] += self.slots[last + 1].astype(jnp.float32)

    def drain(self):
        p = self.p
        for step in range(1, p.chips):
            pl.when(jnp.logical_and(p.above, p.chips - step + p.chip < p.chips))(
                lambda step=step: self.up(step).wait_send()
            )
            pl.when(jnp.logical_and(p.below, p.chip - p.chips + step >= 0))(
                lambda step=step: self.down(step).wait_send()
            )
        for chip in range(p.chips):
            self.side(chip).wait_send()


def scatter_sems(chips):
    dma = pltpu.SemaphoreType.DMA
    return [dma((chips,))] * 6


class Turn:
    def __init__(self, place, weight, slab, first, sems):
        self.p, self.weight, self.slab, self.first = place, weight, slab, first
        self.far_out, self.far_in, self.near_out, self.near_in, self.own, self.passing = sems
        self.height, self.width = weight.shape[0], slab.shape[1]
        self.share = self.height // place.replicas

    def far_rows(self):
        return (self.p.fsdp - 2) * self.share

    def piece(self, block, share):
        at = self.first + block * self.height + share * self.share
        return self.slab.at[pl.ds(pl.multiple_of(at, self.share), self.share)]

    def whole(self, block):
        at = self.first + block * self.height
        return self.slab.at[pl.ds(pl.multiple_of(at, self.height), self.height)]

    def columns(self, to):
        return pl.ds(pl.multiple_of(to * self.width, self.width), self.width)

    def start(self):
        p = self.p

        def send(k, _):
            to = lax.rem(2 * p.chip + 2 + k, p.fsdp)
            share = pl.ds(pl.multiple_of(p.replica * self.share, self.share), self.share)
            remote(
                self.weight.at[share, self.columns(to)],
                self.piece(p.me, p.replica),
                self.far_out,
                self.far_in,
                fsdp=to,
            ).start()
            return 0

        lax.fori_loop(0, p.fsdp - 2, send, 0)
        self.near().start()
        self.mine().start()

    def near(self):
        p = self.p
        return remote(
            self.weight.at[:, self.columns(p.sibling)], self.whole(p.me), self.near_out, self.near_in, fsdp=p.sibling
        )

    def mine(self):
        return pltpu.make_async_copy(self.weight.at[:, self.columns(self.p.me)], self.whole(self.p.me), self.own)

    def await_far(self):
        await_bytes(self.slab.at[pl.ds(0, self.far_rows())], self.far_in)

    def bytes_of(self, pieces):
        return self.slab.at[pl.ds(0, pieces * self.share)]

    def pass_bytes(self, half, stage):
        first, second = self.p.counts[half]
        return self.bytes_of((self.p.chips - 1) * (second - 1 if stage == 0 else second * (first - 1)))

    def send_pieces(self, half, stage, shares):
        p = self.p

        def one(i, _):
            block = lax.rem(2 * p.chip + 2 + 2 * i + half, p.fsdp)
            for share in shares:
                ref = self.piece(block, share)
                for k in range(1, p.counts[half][1 - stage]):
                    _, replica = p.peer(half, 1 - stage, k)
                    remote(
                        ref,
                        ref,
                        self.passing.at[half, 2 * stage],
                        self.passing.at[half, 2 * stage + 1],
                        replica=replica,
                    ).start()
            return 0

        lax.fori_loop(0, p.chips - 1, one, 0)

    def pass_on(self):
        for half in range(2):
            self.send_pieces(half, 0, [self.p.replica])

    def pass_far(self):
        p = self.p
        for half in range(2):
            await_bytes(self.pass_bytes(half, 0), self.passing.at[half, 1])
            if half == 0:
                shares = [a * p.wide + p.b for a in range(p.high)]
            else:
                shares = [p.a * p.wide + b for b in range(p.wide)]
            self.send_pieces(half, 1, shares)

    def finish(self):
        for half in range(2):
            await_bytes(self.pass_bytes(half, 1), self.passing.at[half, 3])
        await_bytes(self.whole(self.p.sibling), self.near_in)
        self.mine().wait()

    def drain(self):
        await_bytes(self.slab.at[pl.ds(0, self.far_rows())], self.far_out)
        self.near().wait_send()
        for half in range(2):
            await_bytes(self.pass_bytes(half, 0), self.passing.at[half, 0])
            await_bytes(self.pass_bytes(half, 1), self.passing.at[half, 2])


def turn_sems():
    return [pltpu.SemaphoreType.DMA(())] * 5 + [pltpu.SemaphoreType.DMA((2, 4))]


def partner(values):
    halfway = HEAD_DIM // 2
    width = values.shape[1]
    lane = lax.broadcasted_iota(jnp.int32, values.shape, 1) % HEAD_DIM
    return jnp.where(
        lane < halfway,
        pltpu.roll(values, width - halfway, axis=1),
        pltpu.roll(values, halfway, axis=1),
    )


def front_kernel(
    tokens,
    cotangent,
    gain_one,
    gain_two,
    w_query,
    w_key,
    w_value,
    w_out_in,
    w_gate,
    w_up,
    w_down,
    cosine_in,
    sine_in,
    lowered_one,
    lowered_two_out,
    cotangents,
    slab_qkv_out,
    hidden_out,
    grad_gate_out,
    grad_up_out,
    terms_out,
    sums_out,
    queries_out,
    keys_out,
    values_out,
    attended_out,
    logs_out,
    after_out,
    gains,
    w_out,
    cosine,
    sine,
    queries,
    keys,
    values,
    attended,
    logs,
    after_attn,
    low,
    tiles,
    lowered_two,
    slab_qkv,
    slab_gate,
    slab_up,
    held_down,
    terms,
    across,
    slots,
    tile_hidden,
    tile_gate,
    tile_up,
    tile_terms,
    tile_sums,
    gain_rows,
    gain_out,
    gain_in,
    copy_sems,
    load_sems,
    store_sems,
    *sems,
):
    place = Place()
    chips, block = place.chips, tokens.shape[0]
    model, width = tokens.shape[1], queries.shape[1]
    share = gain_one.shape[0]
    tile = 2 * block
    one_at, cot_at, two_at, scatter_at = sems[:6], sems[6:12], sems[12:18], sems[18:24]
    turn_at = [sems[24 + 6 * i : 30 + 6 * i] for i in range(5)]
    turns = [
        Turn(place, weight, slab_qkv, i * model, turn_at[i])
        for i, weight in enumerate((w_query, w_key, w_value))
    ]
    turn_gate = Turn(place, w_gate, slab_gate, 0, turn_at[3])
    turn_up = Turn(place, w_up, slab_up, 0, turn_at[4])
    here = pl.ds(pl.multiple_of(place.me * block, block), block)

    gain_rows[...] = jnp.zeros_like(gain_rows)
    gain_rows[0, :] = gain_one[...].astype(jnp.float32)
    gain_rows[1, :] = gain_two[...].astype(jnp.float32)
    load_down = pltpu.make_async_copy(w_down, held_down, copy_sems.at[0])
    load_down.start()
    loads = [
        pltpu.make_async_copy(source, target, copy_sems.at[5 + i])
        for i, (source, target) in enumerate(((w_out_in, w_out), (cosine_in, cosine), (sine_in, sine)))
    ]
    keeps = [
        pltpu.make_async_copy(source, target, copy_sems.at[8 + i])
        for i, (source, target) in enumerate(
            (
                (queries, queries_out),
                (keys, keys_out),
                (values, values_out),
                (attended, attended_out),
                (logs, logs_out),
                (after_attn, after_out),
            )
        )
    ]
    for copy in loads:
        copy.start()
    keep_cot = pltpu.make_async_copy(cotangent, cotangents.at[here], copy_sems.at[1])
    keep_cot.start()
    place.enter()

    def send_gains(k, _):
        to = lax.rem(place.me + k, place.fsdp)
        remote(gain_rows, gains.at[place.me], gain_out, gain_in, fsdp=to).start()
        return 0

    lax.fori_loop(1, place.fsdp, send_gains, 0)
    for turn in turns:
        turn.start()
    gains[place.me] = gain_rows[...]
    inputs = tokens[...].astype(jnp.float32)
    factor = lax.rsqrt(jnp.mean(inputs * inputs, axis=-1, keepdims=True) + eps_norm)
    await_bytes(gains.at[pl.ds(0, place.fsdp - 1)], gain_in)
    for j in range(model // share):
        at = pl.ds(j * share, share)
        normed = tokens[:, at].astype(jnp.float32) * factor
        low[:, at] = (normed * gains[j, 0:1, :]).astype(jnp.bfloat16)
    first = Gather(place, lowered_one, block, one_at, low)
    first.start()
    keep_low = pltpu.make_async_copy(low, lowered_one.at[here], copy_sems.at[2])
    keep_low.start()
    for turn in turns:
        turn.await_far()
        turn.pass_on()
    for step in range(1, chips):
        if step == chips - 1:
            turn_gate.start()
        first.step(step)
        if step == 1:
            for turn in turns:
                turn.pass_far()
    turn_up.start()
    third = Gather(place, cotangents, block, cot_at, cotangent)
    third.start()
    keep_low.wait()
    first.finish()

    def load(source, t, slot):
        return pltpu.make_async_copy(rows_at(source, t, tile), tiles.at[slot], load_sems.at[slot])

    load(lowered_one, 0, 0).start()
    for turn in turns:
        turn.finish()
    keep_slab = pltpu.make_async_copy(slab_qkv, slab_qkv_out, copy_sems.at[3])
    keep_slab.start()
    for copy in loads:
        copy.wait()
    for t in range(chips):
        if t + 1 < chips:
            load(lowered_one, t + 1, (t + 1) % 2).start()
        load(lowered_one, t, t % 2).wait()
        at = pl.ds(t * tile, tile)
        for i, ref in enumerate((queries, keys, values)):
            out = dot(tiles[t % 2], slab_qkv[i * model : (i + 1) * model, :])
            if i < 2:
                for j in range(0, width, 2 * HEAD_DIM):
                    pair = out[:, j : j + 2 * HEAD_DIM]
                    pair = pair * cosine[at, :] + partner(pair) * sine[at, :]
                    ref[at, j : j + 2 * HEAD_DIM] = pair.astype(jnp.bfloat16)
            else:
                ref[at, :] = out.astype(jnp.bfloat16)
    scatter = Scatter(place, terms, across, slots, block, scatter_at)
    pair = 2 * HEAD_DIM
    for t in range(chips):
        here_t, seen = pl.ds(t * tile, tile), pl.ds(0, (t + 1) * tile)

        def heads(h, _, t=t, here_t=here_t, seen=seen):
            lanes = pl.ds(pl.multiple_of(h * pair, pair), pair)
            q2, k2, v2 = queries[here_t, lanes], keys[seen, lanes], values[seen, lanes]
            mixed, stats = [], []
            for at in (0, HEAD_DIM):
                head = slice(at, at + HEAD_DIM)
                scores = scores_of(q2[:, head], k2[:, head], t * tile)
                most = jnp.max(scores, axis=-1, keepdims=True)
                weights = jnp.exp(scores - most)
                total = jnp.sum(weights, axis=-1, keepdims=True)
                mixed.append(dot((weights / total).astype(jnp.bfloat16), v2[:, head]))
                stats.append(jnp.broadcast_to(most + jnp.log(total), (tile, HEAD_DIM)))
            attended[here_t, lanes] = jnp.concatenate(mixed, axis=1).astype(jnp.bfloat16)
            logs[here_t, lanes] = jnp.concatenate(stats, axis=1)
            return 0

        lax.fori_loop(0, width // pair, heads, 0)
        terms[here_t, :] = dot(attended[here_t, :], w_out[...]).astype(jnp.bfloat16)
        scatter.side(t).start()
    for keep in keeps[:5]:
        keep.start()
    turn_gate.await_far()
    turn_gate.pass_on()
    for t in range(chips):
        scatter.cross(t)
    for step in range(1, chips):
        scatter.step(step)
        if step == 1:
            turn_gate.pass_far()
            turn_up.await_far()
            turn_up.pass_on()
        if step < chips - 1:
            third.step(step)
        if step == 1:
            turn_up.pass_far()
    scatter.finish(after_attn)
    after_attn[...] += tokens[...].astype(jnp.float32)
    after = after_attn[...]
    factor = lax.rsqrt(jnp.mean(after * after, axis=-1, keepdims=True) + eps_norm)
    for j in range(model // share):
        at = pl.ds(j * share, share)
        normed = after_attn[:, at] * factor
        lowered_two[here, at] = (normed * gains[j, 1:2, :]).astype(jnp.bfloat16)
    second = Gather(place, lowered_two, block, two_at)
    second.start()
    keeps[5].start()
    third.step(chips - 1)
    keep_cot.wait()
    third.finish()
    load(cotangents, place.nearest(0), 0).start()
    turn_gate.finish()
    turn_up.finish()
    load_down.wait()

    def stores(k, t):
        slot = k % 2
        pairs = (
            (tile_hidden, hidden_out),
            (tile_gate, grad_gate_out),
            (tile_up, grad_up_out),
            (tile_terms, terms_out),
            (tile_sums, sums_out),
        )
        return [
            pltpu.make_async_copy(held.at[slot], rows_at(out, t, tile), store_sems.at[i, slot])
            for i, (held, out) in enumerate(pairs)
        ]

    for k in range(chips):
        t, slot = place.nearest(k), k % 2
        if k > 0:
            second.step(k)
        second.across(t)
        if k + 1 < chips:
            load(cotangents, place.nearest(k + 1), (k + 1) % 2).start()
        load(cotangents, t, slot).wait()
        if k > 1:
            for store in stores(k - 2, place.nearest(k - 2)):
                store.wait()
        rows = lowered_two[pl.ds(pl.multiple_of(t * tile, tile), tile), :]
        gate = dot(rows, slab_gate[...])
        up = dot(rows, slab_up[...])
        grad_hidden = contract_last(tiles[slot], held_down[...])
        sigmoid = jax.nn.sigmoid(gate)
        silu = gate * sigmoid
        hidden = (silu * up).astype(jnp.bfloat16)
        grad_gate = (grad_hidden * up * sigmoid * (1.0 + gate * (1.0 - sigmoid))).astype(jnp.bfloat16)
        grad_up = (grad_hidden * silu).astype(jnp.bfloat16)
        tile_hidden[slot] = hidden
        tile_gate[slot] = grad_gate
        tile_up[slot] = grad_up
        got = contract_last(grad_gate, slab_gate[...]) + contract_last(grad_up, slab_up[...])
        tile_terms[slot] = got.astype(jnp.bfloat16)
        tile_sums[slot] = dot(hidden, held_down[...]).astype(jnp.bfloat16)
        for store in stores(k, t):
            store.start()
    keep_two = pltpu.make_async_copy(lowered_two, lowered_two_out, copy_sems.at[4])
    keep_two.start()
    second.drain()
    scatter.drain()
    for turn in turns + [turn_gate, turn_up]:
        turn.drain()
    await_bytes(gains.at[pl.ds(0, place.fsdp - 1)], gain_out)
    keep_slab.wait()
    for keep in keeps:
        keep.wait()
    for k in range(max(chips - 2, 0), chips):
        for store in stores(k, place.nearest(k)):
            store.wait()
    keep_two.wait()


def front(
    tokens, cotangent, gain_one, gain_two, w_query, w_key, w_value, w_out, w_gate, w_up, w_down, cosine, sine
):
    fsdp = lax.axis_size("fsdp")
    chips = fsdp // 2
    block, model = tokens.shape
    rows, width, wide = fsdp * block, w_query.shape[1] // fsdp, w_gate.shape[1] // fsdp
    tile = 2 * block
    share = gain_one.shape[0]
    low, full = jnp.bfloat16, jnp.float32
    hbm, vmem = pl.BlockSpec(memory_space=pl.ANY), pl.BlockSpec(memory_space=pltpu.VMEM)
    shape = jax.ShapeDtypeStruct
    dma = pltpu.SemaphoreType.DMA
    return pl.pallas_call(
        front_kernel,
        in_specs=[vmem] * 4 + [hbm] * 9,
        out_specs=[hbm] * 15 + [vmem],
        out_shape=[
            shape((rows, model), low),
            shape((rows, model), low),
            shape((rows, model), low),
            shape((3 * model, width), low),
            shape((rows, wide), low),
            shape((rows, wide), low),
            shape((rows, wide), low),
            shape((rows, model), low),
            shape((rows, model), low),
            shape((rows, width), low),
            shape((rows, width), low),
            shape((rows, width), low),
            shape((rows, width), low),
            shape((rows, width), full),
            shape((block, model), full),
            shape((fsdp, 8, share), full),
        ],
        scratch_shapes=[
            pltpu.VMEM(w_out.shape, low),
            pltpu.VMEM(cosine.shape, full),
            pltpu.VMEM(sine.shape, full),
            pltpu.VMEM((rows, width), low),
            pltpu.VMEM((rows, width), low),
            pltpu.VMEM((rows, width), low),
            pltpu.VMEM((rows, width), low),
            pltpu.VMEM((rows, width), full),
            pltpu.VMEM((block, model), full),
            pltpu.VMEM((block, model), low),
            pltpu.VMEM((2, tile, model), low),
            pltpu.VMEM((rows, model), low),
            pltpu.VMEM((3 * model, width), low),
            pltpu.VMEM((model, wide), low),
            pltpu.VMEM((model, wide), low),
            pltpu.VMEM((wide, model), low),
            pltpu.VMEM((rows, model), low),
            pltpu.VMEM((chips * block, model), low),
            pltpu.VMEM((chips + 1, block, model), low),
            pltpu.VMEM((2, tile, wide), low),
            pltpu.VMEM((2, tile, wide), low),
            pltpu.VMEM((2, tile, wide), low),
            pltpu.VMEM((2, tile, model), low),
            pltpu.VMEM((2, tile, model), low),
            pltpu.VMEM((8, share), full),
            dma(()),
            dma(()),
            dma((14,)),
            dma((2,)),
            dma((5, 2)),
        ]
        + line_sems(chips) * 3
        + scatter_sems(chips)
        + turn_sems() * 5,
        compiler_params=pltpu.CompilerParams(
            collective_id=0, has_side_effects=True, vmem_limit_bytes=VMEM_LIMIT
        ),
        name="front",
    )(
        tokens,
        cotangent,
        gain_one,
        gain_two,
        w_query,
        w_key,
        w_value,
        w_out,
        w_gate,
        w_up,
        w_down,
        cosine,
        sine,
    )


class Reduce:
    def __init__(self, place, part, first, second, sems):
        self.p, self.part, self.first, self.second, self.sems = place, part, first, second, sems
        self.half = part.shape[0] // 2

    def rows(self, half):
        return pl.ds(half * self.half, self.half)

    def sent(self, half, to):
        if half == 0:
            return self.part.at[self.rows(0), :, to]
        return self.part.at[self.rows(1), to]

    def own(self, half):
        return self.sent(half, self.p.b if half == 0 else self.p.a)

    def start(self, half):
        for k in range(1, self.p.counts[half][0]):
            to, replica = self.p.peer(half, 0, k)
            remote(
                self.sent(half, to),
                self.first[half].at[k - 1],
                self.sems.at[half, 0],
                self.sems.at[half, 1],
                replica=replica,
            ).start()

    def exchange(self):
        for half in range(2):
            own, arrived = self.own(half), self.first[half]
            await_bytes(arrived, self.sems.at[half, 1])

            def add(n, _, own=own, arrived=arrived):
                for m in range(own.shape[1]):
                    total = own[n, m].astype(jnp.float32)
                    for k in range(arrived.shape[0]):
                        total += arrived[k, n, m].astype(jnp.float32)
                    own[n, m] = total.astype(own.dtype)
                return 0

            lax.fori_loop(0, self.half, add, 0)
            for k in range(1, self.p.counts[half][1]):
                to, replica = self.p.peer(half, 1, k)
                remote(
                    own.at[:, to],
                    self.second[half].at[k - 1],
                    self.sems.at[half, 2],
                    self.sems.at[half, 3],
                    replica=replica,
                ).start()

    def total(self):
        for half in range(2):
            own, arrived = self.held(half), self.second[half]
            await_bytes(arrived, self.sems.at[half, 3])

            def add(n, _, own=own, arrived=arrived):
                total = own[n].astype(jnp.float32)
                for k in range(arrived.shape[0]):
                    total += arrived[k, n].astype(jnp.float32)
                own[n] = total.astype(own.dtype)
                return 0

            lax.fori_loop(0, self.half, add, 0)

    def held(self, half):
        return self.part.at[self.rows(half), self.p.a, self.p.b]

    def piece(self, n):
        return self.part.at[n, self.p.a, self.p.b]

    def drain(self):
        for half in range(2):
            await_bytes(self.first[half], self.sems.at[half, 0])
            await_bytes(self.second[half], self.sems.at[half, 2])


def reduce_scratch(n, high, wide, rows, columns):
    low = functools.partial(pltpu.VMEM, dtype=jnp.bfloat16)
    half = n // 2
    return [
        low((n, high, wide, rows, columns)),
        low((wide - 1, half, high, rows, columns)),
        low((high - 1, half, wide, rows, columns)),
        low((high - 1, half, rows, columns)),
        low((wide - 1, half, rows, columns)),
        pltpu.SemaphoreType.DMA((2, 4)),
    ]


def reducer(place, refs):
    part, first_a, first_b, second_a, second_b, sems = refs
    return Reduce(place, part, (first_a, first_b), (second_a, second_b), sems)


class Spread:
    def __init__(self, place, piece, out, sems, turned):
        self.p, self.piece, self.out, self.sems, self.turned = place, piece, out, sems, turned

    def start(self):
        p = self.p
        if self.turned:
            count = self.out.shape[0]
            width = self.out.shape[-1] // p.fsdp
            columns = pl.ds(pl.multiple_of(p.me * width, width), width)

            def pairs(to):
                ref = self.piece(to)
                return [
                    (ref.at[:, pl.ds(i * width, width)], self.out.at[i, p.a, p.b, :, columns])
                    for i in range(count)
                ]

            def send(k, _):
                to = lax.rem(p.me + k, p.fsdp)
                for ref, target in pairs(to):
                    remote(ref, target, self.sems.at[0, 0], self.sems.at[0, 1], fsdp=to).start()
                return 0

            lax.fori_loop(1, p.fsdp, send, 0)
            for ref, target in pairs(p.me):
                pltpu.make_async_copy(ref, target, self.sems.at[0, 1]).start()
        else:
            for half in range(2):
                pltpu.make_async_copy(
                    self.piece(half), self.out.at[half, p.a, p.b], self.sems.at[half, 1]
                ).start()

    def placed(self, half, rows):
        a, b = rows
        if self.turned:
            width = self.out.shape[-1] // 2
            return self.out.at[:, a, b, :, pl.ds(half * width, width)]
        return self.out.at[half, a, b]

    def spread(self):
        p = self.p
        if self.turned:
            await_bytes(self.out.at[:, p.a, p.b], self.sems.at[0, 1])
        for half in range(2):
            ref = self.placed(half, (p.a, p.b))
            src = ref if self.turned else self.piece(half)
            for k in range(1, p.counts[half][1]):
                _, replica = p.peer(half, 1, k)
                remote(src, ref, self.sems.at[half, 2], self.sems.at[half, 3], replica=replica).start()

    def spread_bytes(self, half):
        some = pl.ds(0, self.p.counts[half][1] - 1)
        return self.placed(half, (some, 0) if half == 0 else (0, some))

    def widen(self):
        p = self.p
        for half in range(2):
            if not self.turned:
                await_bytes(self.placed(half, (p.a, p.b)), self.sems.at[half, 1])
            await_bytes(self.spread_bytes(half), self.sems.at[half, 3])
            every = pl.ds(0, p.counts[half][1])
            ref = self.placed(half, (every, p.b) if half == 0 else (p.a, every))
            for k in range(1, p.counts[half][0]):
                _, replica = p.peer(half, 0, k)
                remote(ref, ref, self.sems.at[half, 4], self.sems.at[half, 5], replica=replica).start()

    def widen_bytes(self, half):
        counts = self.p.counts[half]
        every, some = pl.ds(0, counts[1]), pl.ds(0, counts[0] - 1)
        return self.placed(half, (every, some) if half == 0 else (some, every))

    def finish(self):
        p = self.p
        for half in range(2):
            await_bytes(self.widen_bytes(half), self.sems.at[half, 5])
            await_bytes(self.spread_bytes(half), self.sems.at[half, 2])
            await_bytes(self.widen_bytes(half), self.sems.at[half, 4])
        if self.turned:
            width = self.out.shape[-1] // p.fsdp
            await_bytes(
                self.out.at[:, p.a, p.b, :, pl.ds(0, (p.fsdp - 1) * width)], self.sems.at[0, 0]
            )


def spread_sems():
    return [pltpu.SemaphoreType.DMA((2, 6))]


def norm_back(values, gain_row, gains, grad, carried, result, gain_terms):
    block, model = values.shape
    share = gains.shape[2]
    held = values[...].astype(jnp.float32)
    factor = lax.rsqrt(jnp.mean(held * held, axis=-1, keepdims=True) + eps_norm)
    dots = jnp.zeros((block, 1), jnp.float32)
    for j in range(model // share):
        at = pl.ds(j * share, share)
        normed = values[:, at].astype(jnp.float32) * factor
        product = grad[:, at] * normed
        gain_terms[j, gain_row : gain_row + 1, :] = jnp.sum(product, axis=0, keepdims=True)
        dots += jnp.sum(product * gains[j, gain_row : gain_row + 1, :], axis=-1, keepdims=True)
    dots = dots / model
    for j in range(model // share):
        at = pl.ds(j * share, share)
        normed = values[:, at].astype(jnp.float32) * factor
        scaled = grad[:, at] * gains[j, gain_row : gain_row + 1, :]
        result[:, at] = carried[:, at].astype(jnp.float32) + factor * (scaled - normed * dots)


def weigh_kernel(
    cotangent,
    after_in,
    gains,
    terms_in,
    lowered_two,
    cotangents,
    hidden_in,
    grad_gate_in,
    grad_up_in,
    w_out_in,
    queries_in,
    keys_in,
    values_in,
    logs_in,
    cosine_in,
    sine_in,
    gain_terms,
    grad_after_out,
    grads_out,
    branch,
    sum_down,
    sum_gate,
    sum_up,
    after_attn,
    w_out,
    queries,
    keys,
    values,
    logs,
    cosine,
    sine,
    grad_after,
    grads,
    tokens_held,
    hidden,
    grad_gate,
    grad_up,
    terms,
    across,
    slots,
    summed,
    low,
    grad_low,
    grad_key,
    grad_value,
    load_sems,
    store_sems,
    late_sems,
    *rest,
):
    place = Place()
    chips, block = place.chips, cotangent.shape[0]
    model = cotangent.shape[1]
    tile = 2 * block
    scatter_at, gather_at = rest[:6], rest[6:12]
    down, gate, up = [reducer(place, rest[12 + 6 * i : 18 + 6 * i]) for i in range(3)]

    def load(t):
        at = pl.ds(t * tile, tile)
        return pltpu.make_async_copy(terms_in.at[at], terms.at[at], load_sems.at[t])

    loads = [
        pltpu.make_async_copy(source, target, load_sems.at[chips + i])
        for i, (source, target) in enumerate(
            (
                (cotangents, tokens_held),
                (hidden_in, hidden),
                (grad_gate_in, grad_gate),
                (grad_up_in, grad_up),
                (lowered_two, tokens_held),
            )
        )
    ]
    for t in range(chips):
        load(t).start()
    for copy in loads[:4]:
        copy.start()
    late = [
        pltpu.make_async_copy(source, target, late_sems.at[i])
        for i, (source, target) in enumerate(
            (
                (after_in, after_attn),
                (w_out_in, w_out),
                (queries_in, queries),
                (keys_in, keys),
                (values_in, values),
                (logs_in, logs),
                (cosine_in, cosine),
                (sine_in, sine),
            )
        )
    ]
    for copy in late:
        copy.start()
    keep_after = pltpu.make_async_copy(grad_after, grad_after_out, late_sems.at[8])
    keep_grads = pltpu.make_async_copy(grads, grads_out, late_sems.at[9])
    place.enter()
    scatter = Scatter(place, terms, across, slots, block, scatter_at)
    for t in range(chips):
        load(t).wait()
        scatter.side(t).start()
    gain_terms[...] = jnp.zeros_like(gain_terms)
    loads[0].wait()
    loads[1].wait()
    _, high, wide, thin, _ = down.part.shape
    columns = min(tile, hidden.shape[1])
    for i in range(0, hidden.shape[1], columns):
        got = contract_first(hidden[:, i : i + columns], tokens_held[...]).astype(jnp.bfloat16)
        for m in range(0, columns, thin):
            n = (i + m) // thin
            down.part[n // (high * wide), n // wide % high, n % wide] = got[m : m + thin, :]
        if 2 * (i + columns) == hidden.shape[1]:
            down.start(0)
    loads[4].start()
    down.start(1)
    for t in range(chips):
        scatter.cross(t)
    scatter.step(1)
    loads[4].wait()

    def weigh(reduce, grads):
        share = model // place.fsdp

        def rows(j, _):
            left = tokens_held[:, pl.ds(pl.multiple_of(j * share, share), share)]
            got = contract_first(left, grads[...]).astype(jnp.bfloat16)
            reduce.part[j] = got.reshape(reduce.part.shape[1:])
            return 0

        for half in range(2):
            lax.fori_loop(half * chips, (half + 1) * chips, rows, 0)
            reduce.start(half)

    loads[2].wait()
    weigh(gate, grad_gate)
    if chips > 2:
        scatter.step(2)
    loads[3].wait()
    weigh(up, grad_up)
    for step in range(3, chips):
        scatter.step(step)
    scatter.finish(summed)
    late[0].wait()
    norm_back(after_attn, 1, gains, summed, cotangent, grad_after, gain_terms)
    keep_after.start()
    low[...] = grad_after[...].astype(jnp.bfloat16)
    here = pl.ds(pl.multiple_of(place.me * block, block), block)
    gather = Gather(place, branch, block, gather_at, low)
    gather.start()
    keep = pltpu.make_async_copy(low, branch.at[here], store_sems.at[0])
    keep.start()
    scatter.drain()
    down.exchange()
    for step in range(1, chips):
        gather.step(step)
        if step == 1:
            gate.exchange()
        if step == max(chips - 2, 1):
            up.exchange()
    keep.wait()
    gather.finish()
    fetch = pltpu.make_async_copy(branch, tokens_held, load_sems.at[0])
    fetch.start()
    down.total()
    fetch.wait()
    for copy in late[1:]:
        copy.wait()

    def attend_rows(t, _):
        at = pl.ds(pl.multiple_of(t * tile, tile), tile)
        grad_low[at, :] = contract_last(tokens_held[at, :], w_out[...]).astype(jnp.bfloat16)
        return 0

    lax.fori_loop(0, chips, attend_rows, 0)
    width = queries.shape[1]
    scale = HEAD_DIM**-0.5
    grad_key[...] = jnp.zeros_like(grad_key)
    grad_value[...] = jnp.zeros_like(grad_value)
    pair = 2 * HEAD_DIM
    height = tile * 1024 // max(queries.shape[0], 1024)
    for first in range(0, queries.shape[0], height):
        rows, seen = pl.ds(first, height), pl.ds(0, first + height)

        def heads(h, _, first=first, rows=rows, seen=seen):
            lanes = pl.ds(pl.multiple_of(h * pair, pair), pair)
            q2, g2, log2 = queries[rows, lanes], grad_low[rows, lanes], logs[rows, lanes]
            k2, v2 = keys[seen, lanes], values[seen, lanes]
            for_queries, for_keys, for_values = [], [], []
            for at in (0, HEAD_DIM):
                head = slice(at, at + HEAD_DIM)
                q, g, k = q2[:, head], g2[:, head], k2[:, head]
                weights = jnp.exp(scores_of(q, k, first) - log2[:, at : at + 1])
                grad_weights = contract_last(g, v2[:, head])
                delta = jnp.sum(weights * grad_weights, axis=-1, keepdims=True)
                grad_scores = (weights * (grad_weights - delta)).astype(jnp.bfloat16)
                for_queries.append(dot(grad_scores, k))
                for_keys.append(contract_first(grad_scores, q))
                for_values.append(contract_first(weights.astype(jnp.bfloat16), g))
            got = jnp.concatenate(for_queries, axis=1) * scale
            got = got * cosine[rows, :] - partner(got) * sine[rows, :]
            grads[rows, lanes] = got.astype(jnp.bfloat16)
            grad_key[seen, lanes] += jnp.concatenate(for_keys, axis=1) * scale
            grad_value[seen, lanes] += jnp.concatenate(for_values, axis=1)
            return 0

        lax.fori_loop(0, width // pair, heads, 0)

    def turn_keys(t, _):
        at = pl.ds(pl.multiple_of(t * tile, tile), tile)
        for j in range(0, width, pair):
            got = grad_key[at, j : j + pair]
            got = got * cosine[at, :] - partner(got) * sine[at, :]
            grads[at, width + j : width + j + pair] = got.astype(jnp.bfloat16)
        grads[at, 2 * width :] = grad_value[at, :].astype(jnp.bfloat16)
        return 0

    lax.fori_loop(0, chips, turn_keys, 0)
    keep_grads.start()
    stores = [keep_after, keep_grads]
    for i, (reduce, out) in enumerate(((down, sum_down), (gate, sum_gate), (up, sum_up))):
        if i > 0:
            reduce.total()
        for half in range(2):
            store = pltpu.make_async_copy(
                reduce.held(half), out.at[reduce.rows(half)], store_sems.at[1 + 2 * i + half]
            )
            store.start()
            stores.append(store)
    for reduce in (down, gate, up):
        reduce.drain()
    for store in stores:
        store.wait()


def weigh(
    cotangent,
    after_attn,
    gains,
    terms,
    lowered_two,
    cotangents,
    hidden,
    grad_gate,
    grad_up,
    w_out,
    queries,
    keys,
    values,
    logs,
    cosine,
    sine,
):
    fsdp, replicas = lax.axis_size("fsdp"), lax.axis_size("replica")
    chips, high, wide = fsdp // 2, 2, replicas // 2
    block, model = cotangent.shape
    rows, columns = hidden.shape
    width = queries.shape[1]
    share = gains.shape[2]
    low, full = jnp.bfloat16, jnp.float32
    hbm, vmem = pl.BlockSpec(memory_space=pl.ANY), pl.BlockSpec(memory_space=pltpu.VMEM)
    shape = jax.ShapeDtypeStruct
    down_piece = (2, high, wide, columns // (2 * replicas), model)
    wide_piece = (fsdp, high, wide, share // replicas, columns)
    dma = pltpu.SemaphoreType.DMA
    return pl.pallas_call(
        weigh_kernel,
        in_specs=[vmem, hbm, vmem] + [hbm] * 13,
        out_specs=[vmem] + [hbm] * 6,
        out_shape=[
            shape((fsdp, 8, share), full),
            shape((block, model), full),
            shape((rows, 3 * width), low),
            shape((rows, model), low),
            shape((2,) + down_piece[3:], low),
            shape((fsdp,) + wide_piece[3:], low),
            shape((fsdp,) + wide_piece[3:], low),
        ],
        scratch_shapes=[
            pltpu.VMEM((block, model), full),
            pltpu.VMEM(w_out.shape, low),
            pltpu.VMEM((rows, width), low),
            pltpu.VMEM((rows, width), low),
            pltpu.VMEM((rows, width), low),
            pltpu.VMEM((rows, width), full),
            pltpu.VMEM(cosine.shape, full),
            pltpu.VMEM(sine.shape, full),
            pltpu.VMEM((block, model), full),
            pltpu.VMEM((rows, 3 * width), low),
            pltpu.VMEM((rows, model), low),
            pltpu.VMEM((rows, columns), low),
            pltpu.VMEM((rows, columns), low),
            pltpu.VMEM((rows, columns), low),
            pltpu.VMEM((rows, model), low),
            pltpu.VMEM((chips * block, model), low),
            pltpu.VMEM((chips + 1, block, model), low),
            pltpu.VMEM((block, model), full),
            pltpu.VMEM((block, model), low),
            pltpu.VMEM((rows, width), low),
            pltpu.VMEM((rows, width), full),
            pltpu.VMEM((rows, width), full),
            dma((chips + 5,)),
            dma((7,)),
            dma((10,)),
        ]
        + scatter_sems(chips)
        + line_sems(chips)
        + reduce_scratch(*down_piece)
        + reduce_scratch(*wide_piece)
        + reduce_scratch(*wide_piece),
        compiler_params=pltpu.CompilerParams(
            collective_id=1, has_side_effects=True, vmem_limit_bytes=VMEM_LIMIT
        ),
        name="weigh",
    )(
        cotangent,
        after_attn,
        gains,
        terms,
        lowered_two,
        cotangents,
        hidden,
        grad_gate,
        grad_up,
        w_out,
        queries,
        keys,
        values,
        logs,
        cosine,
        sine,
    )


def back_kernel(
    tokens,
    gains,
    grad_after_in,
    gain_terms_in,
    after_in,
    sums,
    sum_down,
    sum_gate,
    sum_up,
    branch_in,
    lowered_one,
    slab_in,
    attended_in,
    grads_in,
    outputs,
    grad_tokens,
    gain_out,
    out_down,
    out_gate,
    out_up,
    out_qkv,
    out_out,
    grad_after,
    after_attn,
    slab_qkv,
    attended,
    grads,
    terms,
    across,
    slots,
    branch,
    summed,
    gain_terms,
    gain_slots,
    gain_sums,
    gain_sems,
    load_sems,
    *rest,
):
    place = Place()
    chips, block = place.chips, tokens.shape[0]
    model, width = tokens.shape[1], attended.shape[1]
    share = gains.shape[2]
    tile = 2 * block
    scatter_at, rest = rest[:6], rest[6:]
    down = Spread(place, lambda n: sum_down.at[n], out_down, rest[0], False)
    gate = Spread(place, lambda n: sum_gate.at[n], out_gate, rest[1], True)
    up = Spread(place, lambda n: sum_up.at[n], out_up, rest[2], True)
    qkv, out = reducer(place, rest[5:11]), reducer(place, rest[11:17])
    qkv_spread = Spread(place, qkv.piece, out_qkv, rest[3], True)
    out_spread = Spread(place, out.piece, out_out, rest[4], False)
    load = pltpu.make_async_copy(lowered_one, branch, load_sems.at[0])
    load.start()
    loads = [
        pltpu.make_async_copy(source, target, load_sems.at[2 + i])
        for i, (source, target) in enumerate(
            (
                (grads_in, grads),
                (slab_in, slab_qkv),
                (attended_in, attended),
                (grad_after_in, grad_after),
                (after_in, after_attn),
            )
        )
    ]
    for copy in loads:
        copy.start()
    place.enter()
    down.start()
    down.spread()
    gate.start()
    load.wait()
    loads[0].wait()

    def weigh_rows(j, _):
        left = branch[:, pl.ds(pl.multiple_of(j * share, share), share)]
        got = contract_first(left, grads[...]).astype(jnp.bfloat16)
        qkv.part[j] = got.reshape(qkv.part.shape[1:])
        return 0

    for half in range(2):
        lax.fori_loop(half * chips, (half + 1) * chips, weigh_rows, 0)
        qkv.start(half)
    reload = pltpu.make_async_copy(branch_in, branch, load_sems.at[1])
    reload.start()
    scatter = Scatter(place, terms, across, slots, block, scatter_at)

    def back_rows(t, _):
        at = pl.ds(pl.multiple_of(t * tile, tile), tile)
        got = contract_last(grads[at, :width], slab_qkv[:model, :])
        got += contract_last(grads[at, width : 2 * width], slab_qkv[model : 2 * model, :])
        got += contract_last(grads[at, 2 * width :], slab_qkv[2 * model :, :])
        terms[at, :] = got.astype(jnp.bfloat16)
        return 0

    loads[1].wait()
    lax.fori_loop(0, chips, back_rows, 0)
    for t in range(chips):
        scatter.side(t).start()
    down.widen()
    reload.wait()
    loads[2].wait()
    _, high, wide, thin, columns = out.part.shape
    for half in range(2):
        for at in range(0, columns, 512):
            got = contract_first(
                attended[...], branch[:, half * columns + at : half * columns + at + 512]
            ).astype(jnp.bfloat16)
            out.part[half, :, :, :, at : at + 512] = got.reshape(high, wide, thin, 512)
    out.start(0)
    out.start(1)
    for t in range(chips):
        scatter.cross(t)
    scatter.step(1)
    gate.spread()
    qkv.exchange()
    for step in range(2, chips):
        scatter.step(step)
    up.start()
    scatter.finish(summed)
    gain_terms[...] = gain_terms_in[...]
    loads[3].wait()
    loads[4].wait()
    norm_back(tokens, 0, gains, summed, grad_after, grad_tokens, gain_terms)

    def send_gain(k, _):
        to = lax.rem(place.me + k, place.fsdp)
        remote(
            gain_terms.at[to], gain_slots.at[place.me], gain_sems.at[0], gain_sems.at[1], fsdp=to
        ).start()
        return 0

    lax.fori_loop(1, place.fsdp, send_gain, 0)
    gain_slots[place.me] = gain_terms[place.me]
    scatter.drain()
    load_sums = pltpu.make_async_copy(sums, terms, load_sems.at[0])
    load_sums.start()
    out.exchange()
    gate.widen()
    qkv.total()
    qkv_spread.start()
    await_bytes(gain_slots.at[pl.ds(0, place.fsdp - 1)], gain_sems.at[1])
    gain_sums[place.replica] = jnp.sum(gain_slots[...], axis=0)

    def send_sum(k, _):
        ref = gain_sums.at[place.replica]
        to = lax.rem(place.replica + k, place.replicas)
        remote(ref, ref, gain_sems.at[2], gain_sems.at[3], replica=to).start()
        return 0

    lax.fori_loop(1, place.replicas, send_sum, 0)

    load_sums.wait()
    for t in range(chips):
        scatter.side(t).start()
    up.spread()
    for t in range(chips):
        scatter.cross(t)
    scatter.step(1)
    out.total()
    out_spread.start()
    out_spread.spread()
    qkv_spread.spread()
    up.widen()
    for step in range(2, chips):
        scatter.step(step)
    out_spread.widen()
    scatter.finish(summed)
    outputs[...] = (summed[...] + after_attn[...]).astype(outputs.dtype)
    qkv_spread.widen()
    await_bytes(gain_sums.at[pl.ds(0, place.replicas - 1)], gain_sems.at[3])
    gain_out[...] = jnp.sum(gain_sums[...], axis=0)
    await_bytes(gain_slots.at[pl.ds(0, place.fsdp - 1)], gain_sems.at[0])
    await_bytes(gain_sums.at[pl.ds(0, place.replicas - 1)], gain_sems.at[2])
    scatter.drain()
    qkv.drain()
    out.drain()
    for spread in (down, gate, up, out_spread, qkv_spread):
        spread.finish()


def back(
    tokens,
    gains,
    grad_after,
    gain_terms,
    after_attn,
    sums,
    sum_down,
    sum_gate,
    sum_up,
    branch,
    lowered_one,
    slab_qkv,
    attended,
    grads,
):
    fsdp, replicas = lax.axis_size("fsdp"), lax.axis_size("replica")
    chips, high, wide = fsdp // 2, 2, replicas // 2
    block, model = tokens.shape
    rows, width = attended.shape
    share = gains.shape[2]
    low, full = jnp.bfloat16, jnp.float32
    hbm, vmem = pl.BlockSpec(memory_space=pl.ANY), pl.BlockSpec(memory_space=pltpu.VMEM)
    shape = jax.ShapeDtypeStruct
    thin = share // replicas
    columns = sum_gate.shape[-1]
    qkv_piece = (fsdp, high, wide, thin, 3 * width)
    out_piece = (2, high, wide, width // replicas, model // 2)
    dma = pltpu.SemaphoreType.DMA
    return pl.pallas_call(
        back_kernel,
        in_specs=[vmem, vmem, hbm, vmem] + [hbm] * 10,
        out_specs=[vmem] * 3 + [hbm] * 5,
        out_shape=[
            shape((block, model), low),
            shape((block, model), full),
            shape((8, share), full),
            shape((2, high, wide) + sum_down.shape[1:], low),
            shape((1, high, wide, thin, fsdp * columns), low),
            shape((1, high, wide, thin, fsdp * columns), low),
            shape((3, high, wide, thin, fsdp * width), low),
            shape(out_piece, low),
        ],
        scratch_shapes=[
            pltpu.VMEM((block, model), full),
            pltpu.VMEM((block, model), full),
            pltpu.VMEM(slab_qkv.shape, low),
            pltpu.VMEM((rows, width), low),
            pltpu.VMEM((rows, 3 * width), low),
            pltpu.VMEM((rows, model), low),
            pltpu.VMEM((chips * block, model), low),
            pltpu.VMEM((chips + 1, block, model), low),
            pltpu.VMEM((rows, model), low),
            pltpu.VMEM((block, model), full),
            pltpu.VMEM((fsdp, 8, share), full),
            pltpu.VMEM((fsdp, 8, share), full),
            pltpu.VMEM((replicas, 8, share), full),
            dma((4,)),
            dma((7,)),
        ]
        + scatter_sems(chips)
        + spread_sems() * 5
        + reduce_scratch(*qkv_piece)
        + reduce_scratch(*out_piece),
        compiler_params=pltpu.CompilerParams(
            collective_id=2, has_side_effects=True, vmem_limit_bytes=VMEM_LIMIT
        ),
        name="back",
    )(
        tokens,
        gains,
        grad_after,
        gain_terms,
        after_attn,
        sums,
        sum_down,
        sum_gate,
        sum_up,
        branch,
        lowered_one,
        slab_qkv,
        attended,
        grads,
    )


def widen_kernel(
    down,
    gate,
    up,
    qkv,
    out,
    outputs_in,
    tokens_in,
    gains,
    w_down,
    w_gate,
    w_up,
    w_query,
    w_key,
    w_value,
    w_out,
    outputs,
    grad_tokens,
    gain_one,
    gain_two,
):
    w_down[...] = down[...].astype(jnp.float32)
    w_gate[...] = gate[...].astype(jnp.float32)
    w_up[...] = up[...].astype(jnp.float32)
    for i, ref in enumerate((w_query, w_key, w_value)):
        ref[...] = qkv[i].astype(jnp.float32)
    half = out.shape[2]
    for i in range(2):
        w_out[:, i * half : (i + 1) * half] = out[i].astype(jnp.float32)
    outputs[...] = outputs_in[...]
    grad_tokens[...] = tokens_in[...]
    gain_one[...] = gains[0, :]
    gain_two[...] = gains[1, :]


def widen(down, gate, up, qkv, out, outputs, grad_tokens, gains):
    steps = min(16, gate.shape[0] // 16)
    token_steps = outputs.shape[0] // 16
    full = jnp.float32

    def rows(array):
        return pl.BlockSpec((array.shape[0] // steps, array.shape[1]), lambda i: (i, 0))

    def tokens(array):
        return pl.BlockSpec(
            (array.shape[0] // token_steps, array.shape[1]), lambda i: (jnp.minimum(i, token_steps - 1), 0)
        )

    def stacked(array):
        return pl.BlockSpec((array.shape[0], array.shape[1] // steps, array.shape[2]), lambda i: (0, i, 0))

    like = [down, gate, up, qkv[0], qkv[0], qkv[0]]
    shapes = [jax.ShapeDtypeStruct(array.shape, full) for array in like]
    shapes.append(jax.ShapeDtypeStruct((out.shape[1], 2 * out.shape[2]), full))
    row = jax.ShapeDtypeStruct(gains.shape[1:], full)
    whole = pl.BlockSpec(gains.shape, lambda i: (0, 0))
    line = pl.BlockSpec(gains.shape[1:], lambda i: (0,))
    return pl.pallas_call(
        widen_kernel,
        grid=(steps,),
        in_specs=[rows(down), rows(gate), rows(up), stacked(qkv), stacked(out)]
        + [tokens(outputs), tokens(grad_tokens), whole],
        out_specs=[rows(shape) for shape in shapes]
        + [tokens(outputs), tokens(grad_tokens), line, line],
        out_shape=shapes
        + [jax.ShapeDtypeStruct(array.shape, array.dtype) for array in (outputs, grad_tokens)]
        + [row, row],
        compiler_params=pltpu.CompilerParams(vmem_limit_bytes=VMEM_LIMIT),
        name="widen",
    )(down, gate, up, qkv, out, outputs, grad_tokens, gains)


def local(
    tokens, attn_gain, w_query, w_key, w_value, w_out, ffn_gain, w_gate, w_up, w_down, cotangent
):
    cosine, sine = rope_tables(tokens.shape[0] * lax.axis_size("fsdp"))
    (
        lowered_one,
        lowered_two,
        cotangents,
        slab_qkv,
        hidden,
        grad_gate,
        grad_up,
        terms,
        sums,
        queries,
        keys,
        values,
        attended,
        logs,
        after_attn,
        gains,
    ) = front(
        tokens,
        cotangent,
        attn_gain,
        ffn_gain,
        w_query,
        w_key,
        w_value,
        w_out,
        w_gate,
        w_up,
        w_down,
        cosine,
        sine,
    )
    gain_terms, grad_after, grads, branch, sum_down, sum_gate, sum_up = weigh(
        cotangent,
        after_attn,
        gains,
        terms,
        lowered_two,
        cotangents,
        hidden,
        grad_gate,
        grad_up,
        w_out,
        queries,
        keys,
        values,
        logs,
        cosine,
        sine,
    )
    outputs, grad_tokens, gain_grads, low_down, low_gate, low_up, low_qkv, low_out = back(
        tokens,
        gains,
        grad_after,
        gain_terms,
        after_attn,
        sums,
        sum_down,
        sum_gate,
        sum_up,
        branch,
        lowered_one,
        slab_qkv,
        attended,
        grads,
    )
    (
        grad_w_down,
        grad_w_gate,
        grad_w_up,
        grad_w_query,
        grad_w_key,
        grad_w_value,
        grad_w_out,
        outputs,
        grad_tokens,
        grad_attn_gain,
        grad_ffn_gain,
    ) = widen(
        low_down.reshape(w_down.shape),
        low_gate.reshape(w_gate.shape),
        low_up.reshape(w_up.shape),
        low_qkv.reshape((3,) + w_query.shape),
        low_out.reshape(2, w_out.shape[0], -1),
        outputs,
        grad_tokens,
        gain_grads,
    )
    return (
        outputs,
        grad_tokens,
        grad_attn_gain,
        grad_w_query,
        grad_w_key,
        grad_w_value,
        grad_w_out,
        grad_ffn_gain,
        grad_w_gate,
        grad_w_up,
        grad_w_down,
    )


def solution(mesh):
    rows = P("fsdp", None)
    tokens = P(("replica", "fsdp"), None)
    gain = P("fsdp")
    return jax.shard_map(
        local,
        mesh=mesh,
        in_specs=(tokens, gain, rows, rows, rows, rows, gain, rows, rows, rows, tokens),
        out_specs=(tokens, tokens, gain, rows, rows, rows, rows, gain, rows, rows, rows),
        check_vma=False,
    )
```

```python
import functools

import jax
import jax.numpy as jnp
import numpy as np
from jax import lax
from jax.experimental import pallas as pl
from jax.experimental.pallas import tpu as pltpu
from jax.sharding import PartitionSpec as P

HEAD_DIM = 64

eps_norm = 1e-05
rope_base = 130000.0
masked_score = -1e30


def rope_tables(row_count):
    lane = np.arange(2 * HEAD_DIM) % HEAD_DIM
    halfway = HEAD_DIM // 2
    spacing = ((lane % halfway) * np.float32(2.0) / HEAD_DIM).astype(np.float32)
    frequency = np.power(np.float32(rope_base), -spacing)
    angles = np.arange(row_count, dtype=np.float32)[:, None] * frequency[None, :]
    sign = np.where(lane < halfway, -1.0, 1.0).astype(np.float32)
    return np.cos(angles).astype(np.float32), (np.sin(angles) * sign[None, :]).astype(np.float32)


def dot(left, right):
    return jnp.dot(left, right, preferred_element_type=jnp.float32)


def contract_last(left, right):
    return lax.dot_general(
        left, right, (((1,), (1,)), ((), ())), preferred_element_type=jnp.float32
    )


def contract_first(left, right):
    return lax.dot_general(
        left, right, (((0,), (0,)), ((), ())), preferred_element_type=jnp.float32
    )


def scores_of(queries, keys, first_row):
    rows, columns = queries.shape[0], keys.shape[0]
    scores = contract_last(queries, keys) * HEAD_DIM**-0.5
    at_row = lax.broadcasted_iota(jnp.int32, (rows, columns), 0) + first_row
    at_column = lax.broadcasted_iota(jnp.int32, (rows, columns), 1)
    return jnp.where(at_column <= at_row, scores, masked_score)


MESH = pl.DeviceIdType.MESH
VMEM_LIMIT = 61 * 2**20


def remote(src, dst, send, recv, **where):
    return pltpu.make_async_remote_copy(
        src_ref=src, dst_ref=dst, send_sem=send, recv_sem=recv, device_id=where, device_id_type=MESH
    )


def await_bytes(ref, sem):
    pltpu.make_async_copy(ref, ref, sem).wait()


def rows_at(ref, index, size):
    return ref.at[pl.ds(pl.multiple_of(index * size, size), size)]


class Place:
    def __init__(self):
        self.fsdp, self.replicas = lax.axis_size("fsdp"), lax.axis_size("replica")
        self.me, self.replica = lax.axis_index("fsdp"), lax.axis_index("replica")
        self.chips = self.fsdp // 2
        self.chip, self.core = self.me // 2, self.me % 2
        self.sibling = self.me + 1 - 2 * self.core
        self.high, self.wide = 2, self.replicas // 2
        self.a, self.b = self.replica // self.wide, self.replica % self.wide
        self.counts = ((self.wide, self.high), (self.high, self.wide))
        self.above = self.chip + 1 < self.chips
        self.below = self.chip >= 1

    def peer(self, half, stage, k):
        if half == stage:
            to = lax.rem(self.b + k, self.wide)
            return to, self.a * self.wide + to
        to = lax.rem(self.a + k, self.high)
        return to, to * self.wide + self.b

    def nearest(self, k):
        found = jnp.int32(0)
        for chip in range(self.chips):
            order = sorted(range(self.chips), key=lambda other, chip=chip: (abs(other - chip), other))
            found = found + jnp.where(self.chip == chip, order[k], 0)
        return found

    def enter(self):
        barrier = pltpu.get_barrier_semaphore()

        def greet(k, _):
            to = lax.rem(self.me + k, self.fsdp)
            pl.semaphore_signal(barrier, inc=1, device_id={"fsdp": to}, device_id_type=MESH)
            return 0

        def greet_replica(k, _):
            to = lax.rem(self.replica + k, self.replicas)
            pl.semaphore_signal(barrier, inc=1, device_id={"replica": to}, device_id_type=MESH)
            return 0

        lax.fori_loop(1, self.fsdp, greet, 0)
        lax.fori_loop(1, self.replicas, greet_replica, 0)
        pl.semaphore_wait(barrier, self.fsdp - 1 + self.replicas - 1)


def line_sems(chips):
    return [pltpu.SemaphoreType.DMA((chips,))] * 6


class Gather:
    def __init__(self, place, buf, block, sems, own=None):
        self.p, self.buf, self.block, self.own = place, buf, block, own
        self.up_out, self.up_in, self.down_out, self.down_in, self.side_out, self.side_in = sems

    def held(self, chip):
        return rows_at(self.buf, 2 * chip + self.p.core, self.block)

    def up(self, step):
        ref = self.held(self.p.chip - step + 1)
        src = self.own if step == 1 and self.own is not None else ref
        return remote(src, ref, self.up_out.at[step], self.up_in.at[step], fsdp=self.p.me + 2)

    def down(self, step):
        ref = self.held(self.p.chip + step - 1)
        src = self.own if step == 1 and self.own is not None else ref
        return remote(src, ref, self.down_out.at[step], self.down_in.at[step], fsdp=self.p.me - 2)

    def side(self, chip, src=None):
        ref = self.held(chip)
        src = ref if src is None else src
        return remote(src, ref, self.side_out.at[chip], self.side_in.at[chip], fsdp=self.p.sibling)

    def start(self):
        p = self.p
        pl.when(p.above)(lambda: self.up(1).start())
        pl.when(p.below)(lambda: self.down(1).start())
        self.side(p.chip, self.own).start()

    def step(self, step):
        p = self.p
        from_below, from_above = p.chip - step, p.chip + step

        @pl.when(from_below >= 0)
        def _():
            await_bytes(self.held(from_below), self.up_in.at[step])
            if step + 1 < p.chips:
                pl.when(p.above)(lambda: self.up(step + 1).start())
            self.side(from_below).start()

        @pl.when(from_above < p.chips)
        def _():
            await_bytes(self.held(from_above), self.down_in.at[step])
            if step + 1 < p.chips:
                pl.when(p.below)(lambda: self.down(step + 1).start())
            self.side(from_above).start()

    def across(self, chip):
        await_bytes(rows_at(self.buf, 2 * chip + 1 - self.p.core, self.block), self.side_in.at[chip])

    def drain(self):
        p = self.p
        for step in range(1, p.chips):
            pl.when(jnp.logical_and(p.above, p.chip - step + 1 >= 0))(
                lambda step=step: self.up(step).wait_send()
            )
            pl.when(jnp.logical_and(p.below, p.chip + step - 1 < p.chips))(
                lambda step=step: self.down(step).wait_send()
            )
        for chip in range(p.chips):
            self.side(chip).wait_send()

    def finish(self):
        for chip in range(self.p.chips):
            self.across(chip)
        self.drain()


class Scatter:
    def __init__(self, place, terms, across, slots, block, sems):
        self.p, self.terms, self.across, self.slots, self.block = place, terms, across, slots, block
        self.up_out, self.up_in, self.down_out, self.down_in, self.side_out, self.side_in = sems

    def side(self, chip):
        p = self.p
        return remote(
            rows_at(self.terms, 2 * chip + 1 - p.core, self.block),
            rows_at(self.across, chip, self.block),
            self.side_out.at[chip],
            self.side_in.at[chip],
            fsdp=p.sibling,
        )

    def term(self, chip):
        return rows_at(self.terms, 2 * chip + self.p.core, self.block)

    def up(self, step):
        return remote(
            self.term(self.p.chips - step + self.p.chip),
            self.slots.at[step - self.p.chip - 1],
            self.up_out.at[step],
            self.up_in.at[step],
            fsdp=self.p.me + 2,
        )

    def down(self, step):
        return remote(
            self.term(self.p.chip - self.p.chips + step),
            self.slots.at[step + 1],
            self.down_out.at[step],
            self.down_in.at[step],
            fsdp=self.p.me - 2,
        )

    def add(self, chip, arrived):
        term = self.term(chip)
        term[...] = (term[...].astype(jnp.float32) + arrived[...].astype(jnp.float32)).astype(term.dtype)

    def cross(self, chip):
        arrived = rows_at(self.across, chip, self.block)
        await_bytes(arrived, self.side_in.at[chip])
        self.add(chip, arrived)

    def step(self, step):
        p = self.p
        rising, falling = p.chips - step + p.chip, p.chip - p.chips + step

        @pl.when(jnp.logical_and(p.above, rising < p.chips))
        def _():
            if step > 1:

                @pl.when(p.below)
                def _():
                    arrived = self.slots.at[step - 1 - p.chip]
                    await_bytes(arrived, self.up_in.at[step - 1])
                    self.add(rising, arrived)

            self.up(step).start()

        @pl.when(jnp.logical_and(p.below, falling >= 0))
        def _():
            if step > 1:

                @pl.when(p.above)
                def _():
                    arrived = self.slots.at[step]
                    await_bytes(arrived, self.down_in.at[step - 1])
                    self.add(falling, arrived)

            self.down(step).start()

    def finish(self, total):
        p, last = self.p, self.p.chips - 1
        total[...] = self.term(p.chip)[...].astype(jnp.float32)

        @pl.when(p.below)
        def _():
            await_bytes(self.slots.at[last - p.chip], self.up_in.at[last])
            total[...] += self.slots[last - p.chip].astype(jnp.float32)

        @pl.when(p.above)
        def _():
            await_bytes(self.slots.at[last + 1], self.down_in.at[last])
            total[...] += self.slots[last + 1].astype(jnp.float32)

    def drain(self):
        p = self.p
        for step in range(1, p.chips):
            pl.when(jnp.logical_and(p.above, p.chips - step + p.chip < p.chips))(
                lambda step=step: self.up(step).wait_send()
            )
            pl.when(jnp.logical_and(p.below, p.chip - p.chips + step >= 0))(
                lambda step=step: self.down(step).wait_send()
            )
        for chip in range(p.chips):
            self.side(chip).wait_send()


def scatter_sems(chips):
    dma = pltpu.SemaphoreType.DMA
    return [dma((chips,))] * 6


class Turn:
    def __init__(self, place, weight, slab, first, sems):
        self.p, self.weight, self.slab, self.first = place, weight, slab, first
        self.far_out, self.far_in, self.near_out, self.near_in, self.own, self.passing = sems
        self.height, self.width = weight.shape[0], slab.shape[1]
        self.share = self.height // place.replicas

    def far_rows(self):
        return (self.p.fsdp - 2) * self.share

    def piece(self, block, share):
        at = self.first + block * self.height + share * self.share
        return self.slab.at[pl.ds(pl.multiple_of(at, self.share), self.share)]

    def whole(self, block):
        at = self.first + block * self.height
        return self.slab.at[pl.ds(pl.multiple_of(at, self.height), self.height)]

    def columns(self, to):
        return pl.ds(pl.multiple_of(to * self.width, self.width), self.width)

    def start(self):
        p = self.p

        def send(k, _):
            to = lax.rem(2 * p.chip + 2 + k, p.fsdp)
            share = pl.ds(pl.multiple_of(p.replica * self.share, self.share), self.share)
            remote(
                self.weight.at[share, self.columns(to)],
                self.piece(p.me, p.replica),
                self.far_out,
                self.far_in,
                fsdp=to,
            ).start()
            return 0

        lax.fori_loop(0, p.fsdp - 2, send, 0)
        self.near().start()
        self.mine().start()

    def near(self):
        p = self.p
        return remote(
            self.weight.at[:, self.columns(p.sibling)], self.whole(p.me), self.near_out, self.near_in, fsdp=p.sibling
        )

    def mine(self):
        return pltpu.make_async_copy(self.weight.at[:, self.columns(self.p.me)], self.whole(self.p.me), self.own)

    def await_far(self):
        await_bytes(self.slab.at[pl.ds(0, self.far_rows())], self.far_in)

    def bytes_of(self, pieces):
        return self.slab.at[pl.ds(0, pieces * self.share)]

    def pass_bytes(self, half, stage):
        first, second = self.p.counts[half]
        return self.bytes_of((self.p.chips - 1) * (second - 1 if stage == 0 else second * (first - 1)))

    def send_pieces(self, half, stage, shares):
        p = self.p

        def one(i, _):
            block = lax.rem(2 * p.chip + 2 + 2 * i + half, p.fsdp)
            for share in shares:
                ref = self.piece(block, share)
                for k in range(1, p.counts[half][1 - stage]):
                    _, replica = p.peer(half, 1 - stage, k)
                    remote(
                        ref,
                        ref,
                        self.passing.at[half, 2 * stage],
                        self.passing.at[half, 2 * stage + 1],
                        replica=replica,
                    ).start()
            return 0

        lax.fori_loop(0, p.chips - 1, one, 0)

    def pass_on(self):
        for half in range(2):
            self.send_pieces(half, 0, [self.p.replica])

    def pass_far(self):
        p = self.p
        for half in range(2):
            await_bytes(self.pass_bytes(half, 0), self.passing.at[half, 1])
            if half == 0:
                shares = [a * p.wide + p.b for a in range(p.high)]
            else:
                shares = [p.a * p.wide + b for b in range(p.wide)]
            self.send_pieces(half, 1, shares)

    def finish(self):
        for half in range(2):
            await_bytes(self.pass_bytes(half, 1), self.passing.at[half, 3])
        await_bytes(self.whole(self.p.sibling), self.near_in)
        self.mine().wait()

    def drain(self):
        await_bytes(self.slab.at[pl.ds(0, self.far_rows())], self.far_out)
        self.near().wait_send()
        for half in range(2):
            await_bytes(self.pass_bytes(half, 0), self.passing.at[half, 0])
            await_bytes(self.pass_bytes(half, 1), self.passing.at[half, 2])


def turn_sems():
    return [pltpu.SemaphoreType.DMA(())] * 5 + [pltpu.SemaphoreType.DMA((2, 4))]


def partner(values):
    halfway = HEAD_DIM // 2
    width = values.shape[1]
    lane = lax.broadcasted_iota(jnp.int32, values.shape, 1) % HEAD_DIM
    return jnp.where(
        lane < halfway,
        pltpu.roll(values, width - halfway, axis=1),
        pltpu.roll(values, halfway, axis=1),
    )


def front_kernel(
    tokens,
    cotangent,
    gain_one,
    gain_two,
    w_query,
    w_key,
    w_value,
    w_out,
    w_gate,
    w_up,
    w_down,
    cosine,
    sine,
    lowered_one,
    lowered_two_out,
    cotangents,
    slab_qkv_out,
    hidden_out,
    grad_gate_out,
    grad_up_out,
    terms_out,
    sums_out,
    queries,
    keys,
    values,
    attended,
    logs,
    after_attn,
    gains,
    low,
    tiles,
    lowered_two,
    slab_qkv,
    slab_gate,
    slab_up,
    held_down,
    terms,
    across,
    slots,
    tile_hidden,
    tile_gate,
    tile_up,
    tile_terms,
    tile_sums,
    gain_rows,
    gain_out,
    gain_in,
    copy_sems,
    load_sems,
    store_sems,
    *sems,
):
    place = Place()
    chips, block = place.chips, tokens.shape[0]
    model, width = tokens.shape[1], queries.shape[1]
    share = gain_one.shape[0]
    tile = 2 * block
    one_at, cot_at, two_at, scatter_at = sems[:6], sems[6:12], sems[12:18], sems[18:24]
    turn_at = [sems[24 + 6 * i : 30 + 6 * i] for i in range(5)]
    turns = [
        Turn(place, weight, slab_qkv, i * model, turn_at[i])
        for i, weight in enumerate((w_query, w_key, w_value))
    ]
    turn_gate = Turn(place, w_gate, slab_gate, 0, turn_at[3])
    turn_up = Turn(place, w_up, slab_up, 0, turn_at[4])
    here = pl.ds(pl.multiple_of(place.me * block, block), block)

    gain_rows[...] = jnp.zeros_like(gain_rows)
    gain_rows[0, :] = gain_one[...].astype(jnp.float32)
    gain_rows[1, :] = gain_two[...].astype(jnp.float32)
    load_down = pltpu.make_async_copy(w_down, held_down, copy_sems.at[0])
    load_down.start()
    keep_cot = pltpu.make_async_copy(cotangent, cotangents.at[here], copy_sems.at[1])
    keep_cot.start()
    place.enter()

    def send_gains(k, _):
        to = lax.rem(place.me + k, place.fsdp)
        remote(gain_rows, gains.at[place.me], gain_out, gain_in, fsdp=to).start()
        return 0

    lax.fori_loop(1, place.fsdp, send_gains, 0)
    for turn in turns:
        turn.start()
    gains[place.me] = gain_rows[...]
    inputs = tokens[...].astype(jnp.float32)
    factor = lax.rsqrt(jnp.mean(inputs * inputs, axis=-1, keepdims=True) + eps_norm)
    await_bytes(gains.at[pl.ds(0, place.fsdp - 1)], gain_in)
    for j in range(model // share):
        at = pl.ds(j * share, share)
        normed = tokens[:, at].astype(jnp.float32) * factor
        low[:, at] = (normed * gains[j, 0:1, :]).astype(jnp.bfloat16)
    first = Gather(place, lowered_one, block, one_at, low)
    first.start()
    keep_low = pltpu.make_async_copy(low, lowered_one.at[here], copy_sems.at[2])
    keep_low.start()
    for turn in turns:
        turn.await_far()
        turn.pass_on()
    for step in range(1, chips):
        if step == chips - 1:
            turn_gate.start()
        first.step(step)
        if step == 1:
            for turn in turns:
                turn.pass_far()
    turn_up.start()
    third = Gather(place, cotangents, block, cot_at, cotangent)
    third.start()
    keep_low.wait()
    first.finish()

    def load(source, t, slot):
        return pltpu.make_async_copy(rows_at(source, t, tile), tiles.at[slot], load_sems.at[slot])

    load(lowered_one, 0, 0).start()
    for turn in turns:
        turn.finish()
    keep_slab = pltpu.make_async_copy(slab_qkv, slab_qkv_out, copy_sems.at[3])
    keep_slab.start()
    for t in range(chips):
        if t + 1 < chips:
            load(lowered_one, t + 1, (t + 1) % 2).start()
        load(lowered_one, t, t % 2).wait()
        at = pl.ds(t * tile, tile)
        for i, ref in enumerate((queries, keys, values)):
            out = dot(tiles[t % 2], slab_qkv[i * model : (i + 1) * model, :])
            if i < 2:
                for j in range(0, width, 2 * HEAD_DIM):
                    pair = out[:, j : j + 2 * HEAD_DIM]
                    pair = pair * cosine[at, :] + partner(pair) * sine[at, :]
                    ref[at, j : j + 2 * HEAD_DIM] = pair.astype(jnp.bfloat16)
            else:
                ref[at, :] = out.astype(jnp.bfloat16)
    scatter = Scatter(place, terms, across, slots, block, scatter_at)
    pair = 2 * HEAD_DIM
    for t in range(chips):
        here_t, seen = pl.ds(t * tile, tile), pl.ds(0, (t + 1) * tile)

        def heads(h, _, t=t, here_t=here_t, seen=seen):
            lanes = pl.ds(pl.multiple_of(h * pair, pair), pair)
            q2, k2, v2 = queries[here_t, lanes], keys[seen, lanes], values[seen, lanes]
            mixed, stats = [], []
            for at in (0, HEAD_DIM):
                head = slice(at, at + HEAD_DIM)
                scores = scores_of(q2[:, head], k2[:, head], t * tile)
                most = jnp.max(scores, axis=-1, keepdims=True)
                weights = jnp.exp(scores - most)
                total = jnp.sum(weights, axis=-1, keepdims=True)
                mixed.append(dot((weights / total).astype(jnp.bfloat16), v2[:, head]))
                stats.append(jnp.broadcast_to(most + jnp.log(total), (tile, HEAD_DIM)))
            attended[here_t, lanes] = jnp.concatenate(mixed, axis=1).astype(jnp.bfloat16)
            logs[here_t, lanes] = jnp.concatenate(stats, axis=1)
            return 0

        lax.fori_loop(0, width // pair, heads, 0)
        terms[here_t, :] = dot(attended[here_t, :], w_out[...]).astype(jnp.bfloat16)
        scatter.side(t).start()
    for t in range(chips):
        scatter.cross(t)
    for step in range(1, chips):
        scatter.step(step)
        if step == 1:
            turn_gate.await_far()
            turn_gate.pass_on()
        if step < chips - 1:
            third.step(step)
        if step == 1:
            turn_gate.pass_far()
            turn_up.await_far()
            turn_up.pass_on()
        if step == max(chips - 2, 1):
            turn_up.pass_far()
    scatter.finish(after_attn)
    after_attn[...] += tokens[...].astype(jnp.float32)
    after = after_attn[...]
    factor = lax.rsqrt(jnp.mean(after * after, axis=-1, keepdims=True) + eps_norm)
    for j in range(model // share):
        at = pl.ds(j * share, share)
        normed = after_attn[:, at] * factor
        lowered_two[here, at] = (normed * gains[j, 1:2, :]).astype(jnp.bfloat16)
    second = Gather(place, lowered_two, block, two_at)
    second.start()
    third.step(chips - 1)
    keep_cot.wait()
    third.finish()
    load(cotangents, place.nearest(0), 0).start()
    turn_gate.finish()
    turn_up.finish()
    load_down.wait()

    def stores(k, t):
        slot = k % 2
        pairs = (
            (tile_hidden, hidden_out),
            (tile_gate, grad_gate_out),
            (tile_up, grad_up_out),
            (tile_terms, terms_out),
            (tile_sums, sums_out),
        )
        return [
            pltpu.make_async_copy(held.at[slot], rows_at(out, t, tile), store_sems.at[i, slot])
            for i, (held, out) in enumerate(pairs)
        ]

    for k in range(chips):
        t, slot = place.nearest(k), k % 2
        if k > 0:
            second.step(k)
        second.across(t)
        if k + 1 < chips:
            load(cotangents, place.nearest(k + 1), (k + 1) % 2).start()
        load(cotangents, t, slot).wait()
        if k > 1:
            for store in stores(k - 2, place.nearest(k - 2)):
                store.wait()
        rows = lowered_two[pl.ds(pl.multiple_of(t * tile, tile), tile), :]
        gate = dot(rows, slab_gate[...])
        up = dot(rows, slab_up[...])
        grad_hidden = contract_last(tiles[slot], held_down[...])
        sigmoid = jax.nn.sigmoid(gate)
        silu = gate * sigmoid
        hidden = (silu * up).astype(jnp.bfloat16)
        grad_gate = (grad_hidden * up * sigmoid * (1.0 + gate * (1.0 - sigmoid))).astype(jnp.bfloat16)
        grad_up = (grad_hidden * silu).astype(jnp.bfloat16)
        tile_hidden[slot] = hidden
        tile_gate[slot] = grad_gate
        tile_up[slot] = grad_up
        got = contract_last(grad_gate, slab_gate[...]) + contract_last(grad_up, slab_up[...])
        tile_terms[slot] = got.astype(jnp.bfloat16)
        tile_sums[slot] = dot(hidden, held_down[...]).astype(jnp.bfloat16)
        for store in stores(k, t):
            store.start()
    keep_two = pltpu.make_async_copy(lowered_two, lowered_two_out, copy_sems.at[4])
    keep_two.start()
    second.drain()
    scatter.drain()
    for turn in turns + [turn_gate, turn_up]:
        turn.drain()
    await_bytes(gains.at[pl.ds(0, place.fsdp - 1)], gain_out)
    keep_slab.wait()
    for k in range(max(chips - 2, 0), chips):
        for store in stores(k, place.nearest(k)):
            store.wait()
    keep_two.wait()


def front(
    tokens, cotangent, gain_one, gain_two, w_query, w_key, w_value, w_out, w_gate, w_up, w_down, cosine, sine
):
    fsdp = lax.axis_size("fsdp")
    chips = fsdp // 2
    block, model = tokens.shape
    rows, width, wide = fsdp * block, w_query.shape[1] // fsdp, w_gate.shape[1] // fsdp
    tile = 2 * block
    share = gain_one.shape[0]
    low, full = jnp.bfloat16, jnp.float32
    hbm, vmem = pl.BlockSpec(memory_space=pl.ANY), pl.BlockSpec(memory_space=pltpu.VMEM)
    shape = jax.ShapeDtypeStruct
    dma = pltpu.SemaphoreType.DMA
    return pl.pallas_call(
        front_kernel,
        in_specs=[vmem] * 4 + [hbm] * 3 + [vmem] + [hbm] * 3 + [vmem] * 2,
        out_specs=[hbm] * 9 + [vmem] * 7,
        out_shape=[
            shape((rows, model), low),
            shape((rows, model), low),
            shape((rows, model), low),
            shape((3 * model, width), low),
            shape((rows, wide), low),
            shape((rows, wide), low),
            shape((rows, wide), low),
            shape((rows, model), low),
            shape((rows, model), low),
            shape((rows, width), low),
            shape((rows, width), low),
            shape((rows, width), low),
            shape((rows, width), low),
            shape((rows, width), full),
            shape((block, model), full),
            shape((fsdp, 8, share), full),
        ],
        scratch_shapes=[
            pltpu.VMEM((block, model), low),
            pltpu.VMEM((2, tile, model), low),
            pltpu.VMEM((rows, model), low),
            pltpu.VMEM((3 * model, width), low),
            pltpu.VMEM((model, wide), low),
            pltpu.VMEM((model, wide), low),
            pltpu.VMEM((wide, model), low),
            pltpu.VMEM((rows, model), low),
            pltpu.VMEM((chips * block, model), low),
            pltpu.VMEM((chips + 1, block, model), low),
            pltpu.VMEM((2, tile, wide), low),
            pltpu.VMEM((2, tile, wide), low),
            pltpu.VMEM((2, tile, wide), low),
            pltpu.VMEM((2, tile, model), low),
            pltpu.VMEM((2, tile, model), low),
            pltpu.VMEM((8, share), full),
            dma(()),
            dma(()),
            dma((5,)),
            dma((2,)),
            dma((5, 2)),
        ]
        + line_sems(chips) * 3
        + scatter_sems(chips)
        + turn_sems() * 5,
        compiler_params=pltpu.CompilerParams(
            collective_id=0, has_side_effects=True, vmem_limit_bytes=VMEM_LIMIT
        ),
        name="front",
    )(
        tokens,
        cotangent,
        gain_one,
        gain_two,
        w_query,
        w_key,
        w_value,
        w_out,
        w_gate,
        w_up,
        w_down,
        cosine,
        sine,
    )


class Reduce:
    def __init__(self, place, part, first, second, sems):
        self.p, self.part, self.first, self.second, self.sems = place, part, first, second, sems
        self.half = part.shape[0] // 2

    def rows(self, half):
        return pl.ds(half * self.half, self.half)

    def sent(self, half, to):
        if half == 0:
            return self.part.at[self.rows(0), :, to]
        return self.part.at[self.rows(1), to]

    def own(self, half):
        return self.sent(half, self.p.b if half == 0 else self.p.a)

    def start(self, half):
        for k in range(1, self.p.counts[half][0]):
            to, replica = self.p.peer(half, 0, k)
            remote(
                self.sent(half, to),
                self.first[half].at[k - 1],
                self.sems.at[half, 0],
                self.sems.at[half, 1],
                replica=replica,
            ).start()

    def exchange(self):
        for half in range(2):
            own, arrived = self.own(half), self.first[half]
            await_bytes(arrived, self.sems.at[half, 1])

            def add(n, _, own=own, arrived=arrived):
                for m in range(own.shape[1]):
                    total = own[n, m].astype(jnp.float32)
                    for k in range(arrived.shape[0]):
                        total += arrived[k, n, m].astype(jnp.float32)
                    own[n, m] = total.astype(own.dtype)
                return 0

            lax.fori_loop(0, self.half, add, 0)
            for k in range(1, self.p.counts[half][1]):
                to, replica = self.p.peer(half, 1, k)
                remote(
                    own.at[:, to],
                    self.second[half].at[k - 1],
                    self.sems.at[half, 2],
                    self.sems.at[half, 3],
                    replica=replica,
                ).start()

    def total(self):
        for half in range(2):
            own, arrived = self.held(half), self.second[half]
            await_bytes(arrived, self.sems.at[half, 3])

            def add(n, _, own=own, arrived=arrived):
                total = own[n].astype(jnp.float32)
                for k in range(arrived.shape[0]):
                    total += arrived[k, n].astype(jnp.float32)
                own[n] = total.astype(own.dtype)
                return 0

            lax.fori_loop(0, self.half, add, 0)

    def held(self, half):
        return self.part.at[self.rows(half), self.p.a, self.p.b]

    def piece(self, n):
        return self.part.at[n, self.p.a, self.p.b]

    def drain(self):
        for half in range(2):
            await_bytes(self.first[half], self.sems.at[half, 0])
            await_bytes(self.second[half], self.sems.at[half, 2])


def reduce_scratch(n, high, wide, rows, columns):
    low = functools.partial(pltpu.VMEM, dtype=jnp.bfloat16)
    half = n // 2
    return [
        low((n, high, wide, rows, columns)),
        low((wide - 1, half, high, rows, columns)),
        low((high - 1, half, wide, rows, columns)),
        low((high - 1, half, rows, columns)),
        low((wide - 1, half, rows, columns)),
        pltpu.SemaphoreType.DMA((2, 4)),
    ]


def reducer(place, refs):
    part, first_a, first_b, second_a, second_b, sems = refs
    return Reduce(place, part, (first_a, first_b), (second_a, second_b), sems)


class Spread:
    def __init__(self, place, piece, out, sems, turned):
        self.p, self.piece, self.out, self.sems, self.turned = place, piece, out, sems, turned

    def start(self):
        p = self.p
        if self.turned:
            count = self.out.shape[0]
            width = self.out.shape[-1] // p.fsdp
            columns = pl.ds(pl.multiple_of(p.me * width, width), width)

            def pairs(to):
                ref = self.piece(to)
                return [
                    (ref.at[:, pl.ds(i * width, width)], self.out.at[i, p.a, p.b, :, columns])
                    for i in range(count)
                ]

            def send(k, _):
                to = lax.rem(p.me + k, p.fsdp)
                for ref, target in pairs(to):
                    remote(ref, target, self.sems.at[0, 0], self.sems.at[0, 1], fsdp=to).start()
                return 0

            lax.fori_loop(1, p.fsdp, send, 0)
            for ref, target in pairs(p.me):
                pltpu.make_async_copy(ref, target, self.sems.at[0, 1]).start()
        else:
            for half in range(2):
                pltpu.make_async_copy(
                    self.piece(half), self.out.at[half, p.a, p.b], self.sems.at[half, 1]
                ).start()

    def placed(self, half, rows):
        a, b = rows
        if self.turned:
            width = self.out.shape[-1] // 2
            return self.out.at[:, a, b, :, pl.ds(half * width, width)]
        return self.out.at[half, a, b]

    def spread(self):
        p = self.p
        if self.turned:
            await_bytes(self.out.at[:, p.a, p.b], self.sems.at[0, 1])
        for half in range(2):
            ref = self.placed(half, (p.a, p.b))
            src = ref if self.turned else self.piece(half)
            for k in range(1, p.counts[half][1]):
                _, replica = p.peer(half, 1, k)
                remote(src, ref, self.sems.at[half, 2], self.sems.at[half, 3], replica=replica).start()

    def spread_bytes(self, half):
        some = pl.ds(0, self.p.counts[half][1] - 1)
        return self.placed(half, (some, 0) if half == 0 else (0, some))

    def widen(self):
        p = self.p
        for half in range(2):
            if not self.turned:
                await_bytes(self.placed(half, (p.a, p.b)), self.sems.at[half, 1])
            await_bytes(self.spread_bytes(half), self.sems.at[half, 3])
            every = pl.ds(0, p.counts[half][1])
            ref = self.placed(half, (every, p.b) if half == 0 else (p.a, every))
            for k in range(1, p.counts[half][0]):
                _, replica = p.peer(half, 0, k)
                remote(ref, ref, self.sems.at[half, 4], self.sems.at[half, 5], replica=replica).start()

    def widen_bytes(self, half):
        counts = self.p.counts[half]
        every, some = pl.ds(0, counts[1]), pl.ds(0, counts[0] - 1)
        return self.placed(half, (every, some) if half == 0 else (some, every))

    def finish(self):
        p = self.p
        for half in range(2):
            await_bytes(self.widen_bytes(half), self.sems.at[half, 5])
            await_bytes(self.spread_bytes(half), self.sems.at[half, 2])
            await_bytes(self.widen_bytes(half), self.sems.at[half, 4])
        if self.turned:
            width = self.out.shape[-1] // p.fsdp
            await_bytes(
                self.out.at[:, p.a, p.b, :, pl.ds(0, (p.fsdp - 1) * width)], self.sems.at[0, 0]
            )


def spread_sems():
    return [pltpu.SemaphoreType.DMA((2, 6))]


def norm_back(values, gain_row, gains, grad, carried, result, gain_terms):
    block, model = values.shape
    share = gains.shape[2]
    held = values[...].astype(jnp.float32)
    factor = lax.rsqrt(jnp.mean(held * held, axis=-1, keepdims=True) + eps_norm)
    dots = jnp.zeros((block, 1), jnp.float32)
    for j in range(model // share):
        at = pl.ds(j * share, share)
        normed = values[:, at].astype(jnp.float32) * factor
        product = grad[:, at] * normed
        gain_terms[j, gain_row : gain_row + 1, :] = jnp.sum(product, axis=0, keepdims=True)
        dots += jnp.sum(product * gains[j, gain_row : gain_row + 1, :], axis=-1, keepdims=True)
    dots = dots / model
    for j in range(model // share):
        at = pl.ds(j * share, share)
        normed = values[:, at].astype(jnp.float32) * factor
        scaled = grad[:, at] * gains[j, gain_row : gain_row + 1, :]
        result[:, at] = carried[:, at].astype(jnp.float32) + factor * (scaled - normed * dots)


def weigh_kernel(
    cotangent,
    after_in,
    gains,
    terms_in,
    lowered_two,
    cotangents,
    hidden_in,
    grad_gate_in,
    grad_up_in,
    w_out_in,
    queries_in,
    keys_in,
    values_in,
    logs_in,
    cosine_in,
    sine_in,
    gain_terms,
    grad_after_out,
    grads_out,
    branch,
    sum_down,
    sum_gate,
    sum_up,
    after_attn,
    w_out,
    queries,
    keys,
    values,
    logs,
    cosine,
    sine,
    grad_after,
    grads,
    tokens_held,
    hidden,
    grad_gate,
    grad_up,
    terms,
    across,
    slots,
    summed,
    low,
    grad_low,
    grad_key,
    grad_value,
    load_sems,
    store_sems,
    late_sems,
    *rest,
):
    place = Place()
    chips, block = place.chips, cotangent.shape[0]
    model = cotangent.shape[1]
    tile = 2 * block
    scatter_at, gather_at = rest[:6], rest[6:12]
    down, gate, up = [reducer(place, rest[12 + 6 * i : 18 + 6 * i]) for i in range(3)]

    def load(t):
        at = pl.ds(t * tile, tile)
        return pltpu.make_async_copy(terms_in.at[at], terms.at[at], load_sems.at[t])

    loads = [
        pltpu.make_async_copy(source, target, load_sems.at[chips + i])
        for i, (source, target) in enumerate(
            (
                (cotangents, tokens_held),
                (hidden_in, hidden),
                (grad_gate_in, grad_gate),
                (grad_up_in, grad_up),
                (lowered_two, tokens_held),
            )
        )
    ]
    for t in range(chips):
        load(t).start()
    for copy in loads[:4]:
        copy.start()
    late = [
        pltpu.make_async_copy(source, target, late_sems.at[i])
        for i, (source, target) in enumerate(
            (
                (after_in, after_attn),
                (w_out_in, w_out),
                (queries_in, queries),
                (keys_in, keys),
                (values_in, values),
                (logs_in, logs),
                (cosine_in, cosine),
                (sine_in, sine),
            )
        )
    ]
    for copy in late:
        copy.start()
    keep_after = pltpu.make_async_copy(grad_after, grad_after_out, late_sems.at[8])
    keep_grads = pltpu.make_async_copy(grads, grads_out, late_sems.at[9])
    place.enter()
    scatter = Scatter(place, terms, across, slots, block, scatter_at)
    for t in range(chips):
        load(t).wait()
        scatter.side(t).start()
    gain_terms[...] = jnp.zeros_like(gain_terms)
    loads[0].wait()
    loads[1].wait()
    _, high, wide, thin, _ = down.part.shape
    columns = min(tile, hidden.shape[1])
    for i in range(0, hidden.shape[1], columns):
        got = contract_first(hidden[:, i : i + columns], tokens_held[...]).astype(jnp.bfloat16)
        for m in range(0, columns, thin):
            n = (i + m) // thin
            down.part[n // (high * wide), n // wide % high, n % wide] = got[m : m + thin, :]
        if 2 * (i + columns) == hidden.shape[1]:
            down.start(0)
    loads[4].start()
    down.start(1)
    for t in range(chips):
        scatter.cross(t)
    scatter.step(1)
    loads[4].wait()

    def weigh(reduce, grads):
        share = model // place.fsdp

        def rows(j, _):
            left = tokens_held[:, pl.ds(pl.multiple_of(j * share, share), share)]
            got = contract_first(left, grads[...]).astype(jnp.bfloat16)
            reduce.part[j] = got.reshape(reduce.part.shape[1:])
            return 0

        for half in range(2):
            lax.fori_loop(half * chips, (half + 1) * chips, rows, 0)
            reduce.start(half)

    loads[2].wait()
    weigh(gate, grad_gate)
    if chips > 2:
        scatter.step(2)
    loads[3].wait()
    weigh(up, grad_up)
    for step in range(3, chips):
        scatter.step(step)
    scatter.finish(summed)
    late[0].wait()
    norm_back(after_attn, 1, gains, summed, cotangent, grad_after, gain_terms)
    keep_after.start()
    low[...] = grad_after[...].astype(jnp.bfloat16)
    here = pl.ds(pl.multiple_of(place.me * block, block), block)
    gather = Gather(place, branch, block, gather_at, low)
    gather.start()
    keep = pltpu.make_async_copy(low, branch.at[here], store_sems.at[0])
    keep.start()
    scatter.drain()
    down.exchange()
    for step in range(1, chips):
        gather.step(step)
        if step == 1:
            gate.exchange()
        if step == max(chips - 2, 1):
            up.exchange()
    keep.wait()
    gather.finish()
    fetch = pltpu.make_async_copy(branch, tokens_held, load_sems.at[0])
    fetch.start()
    down.total()
    fetch.wait()
    for copy in late[1:]:
        copy.wait()

    def attend_rows(t, _):
        at = pl.ds(pl.multiple_of(t * tile, tile), tile)
        grad_low[at, :] = contract_last(tokens_held[at, :], w_out[...]).astype(jnp.bfloat16)
        return 0

    lax.fori_loop(0, chips, attend_rows, 0)
    width = queries.shape[1]
    scale = HEAD_DIM**-0.5
    grad_key[...] = jnp.zeros_like(grad_key)
    grad_value[...] = jnp.zeros_like(grad_value)
    pair = 2 * HEAD_DIM
    height = tile * 1024 // max(queries.shape[0], 1024)
    for first in range(0, queries.shape[0], height):
        rows, seen = pl.ds(first, height), pl.ds(0, first + height)

        def heads(h, _, first=first, rows=rows, seen=seen):
            lanes = pl.ds(pl.multiple_of(h * pair, pair), pair)
            q2, g2, log2 = queries[rows, lanes], grad_low[rows, lanes], logs[rows, lanes]
            k2, v2 = keys[seen, lanes], values[seen, lanes]
            for_queries, for_keys, for_values = [], [], []
            for at in (0, HEAD_DIM):
                head = slice(at, at + HEAD_DIM)
                q, g, k = q2[:, head], g2[:, head], k2[:, head]
                weights = jnp.exp(scores_of(q, k, first) - log2[:, at : at + 1])
                grad_weights = contract_last(g, v2[:, head])
                delta = jnp.sum(weights * grad_weights, axis=-1, keepdims=True)
                grad_scores = (weights * (grad_weights - delta)).astype(jnp.bfloat16)
                for_queries.append(dot(grad_scores, k))
                for_keys.append(contract_first(grad_scores, q))
                for_values.append(contract_first(weights.astype(jnp.bfloat16), g))
            got = jnp.concatenate(for_queries, axis=1) * scale
            got = got * cosine[rows, :] - partner(got) * sine[rows, :]
            grads[rows, lanes] = got.astype(jnp.bfloat16)
            grad_key[seen, lanes] += jnp.concatenate(for_keys, axis=1) * scale
            grad_value[seen, lanes] += jnp.concatenate(for_values, axis=1)
            return 0

        lax.fori_loop(0, width // pair, heads, 0)

    def turn_keys(t, _):
        at = pl.ds(pl.multiple_of(t * tile, tile), tile)
        for j in range(0, width, pair):
            got = grad_key[at, j : j + pair]
            got = got * cosine[at, :] - partner(got) * sine[at, :]
            grads[at, width + j : width + j + pair] = got.astype(jnp.bfloat16)
        grads[at, 2 * width :] = grad_value[at, :].astype(jnp.bfloat16)
        return 0

    lax.fori_loop(0, chips, turn_keys, 0)
    keep_grads.start()
    stores = [keep_after, keep_grads]
    for i, (reduce, out) in enumerate(((down, sum_down), (gate, sum_gate), (up, sum_up))):
        if i > 0:
            reduce.total()
        for half in range(2):
            store = pltpu.make_async_copy(
                reduce.held(half), out.at[reduce.rows(half)], store_sems.at[1 + 2 * i + half]
            )
            store.start()
            stores.append(store)
    for reduce in (down, gate, up):
        reduce.drain()
    for store in stores:
        store.wait()


def weigh(
    cotangent,
    after_attn,
    gains,
    terms,
    lowered_two,
    cotangents,
    hidden,
    grad_gate,
    grad_up,
    w_out,
    queries,
    keys,
    values,
    logs,
    cosine,
    sine,
):
    fsdp, replicas = lax.axis_size("fsdp"), lax.axis_size("replica")
    chips, high, wide = fsdp // 2, 2, replicas // 2
    block, model = cotangent.shape
    rows, columns = hidden.shape
    width = queries.shape[1]
    share = gains.shape[2]
    low, full = jnp.bfloat16, jnp.float32
    hbm, vmem = pl.BlockSpec(memory_space=pl.ANY), pl.BlockSpec(memory_space=pltpu.VMEM)
    shape = jax.ShapeDtypeStruct
    down_piece = (2, high, wide, columns // (2 * replicas), model)
    wide_piece = (fsdp, high, wide, share // replicas, columns)
    dma = pltpu.SemaphoreType.DMA
    return pl.pallas_call(
        weigh_kernel,
        in_specs=[vmem, hbm, vmem] + [hbm] * 13,
        out_specs=[vmem] + [hbm] * 6,
        out_shape=[
            shape((fsdp, 8, share), full),
            shape((block, model), full),
            shape((rows, 3 * width), low),
            shape((rows, model), low),
            shape((2,) + down_piece[3:], low),
            shape((fsdp,) + wide_piece[3:], low),
            shape((fsdp,) + wide_piece[3:], low),
        ],
        scratch_shapes=[
            pltpu.VMEM((block, model), full),
            pltpu.VMEM(w_out.shape, low),
            pltpu.VMEM((rows, width), low),
            pltpu.VMEM((rows, width), low),
            pltpu.VMEM((rows, width), low),
            pltpu.VMEM((rows, width), full),
            pltpu.VMEM(cosine.shape, full),
            pltpu.VMEM(sine.shape, full),
            pltpu.VMEM((block, model), full),
            pltpu.VMEM((rows, 3 * width), low),
            pltpu.VMEM((rows, model), low),
            pltpu.VMEM((rows, columns), low),
            pltpu.VMEM((rows, columns), low),
            pltpu.VMEM((rows, columns), low),
            pltpu.VMEM((rows, model), low),
            pltpu.VMEM((chips * block, model), low),
            pltpu.VMEM((chips + 1, block, model), low),
            pltpu.VMEM((block, model), full),
            pltpu.VMEM((block, model), low),
            pltpu.VMEM((rows, width), low),
            pltpu.VMEM((rows, width), full),
            pltpu.VMEM((rows, width), full),
            dma((chips + 5,)),
            dma((7,)),
            dma((10,)),
        ]
        + scatter_sems(chips)
        + line_sems(chips)
        + reduce_scratch(*down_piece)
        + reduce_scratch(*wide_piece)
        + reduce_scratch(*wide_piece),
        compiler_params=pltpu.CompilerParams(
            collective_id=1, has_side_effects=True, vmem_limit_bytes=VMEM_LIMIT
        ),
        name="weigh",
    )(
        cotangent,
        after_attn,
        gains,
        terms,
        lowered_two,
        cotangents,
        hidden,
        grad_gate,
        grad_up,
        w_out,
        queries,
        keys,
        values,
        logs,
        cosine,
        sine,
    )


def back_kernel(
    tokens,
    gains,
    grad_after_in,
    gain_terms_in,
    after_in,
    sums,
    sum_down,
    sum_gate,
    sum_up,
    branch_in,
    lowered_one,
    slab_in,
    attended_in,
    grads_in,
    outputs,
    grad_tokens,
    gain_out,
    out_down,
    out_gate,
    out_up,
    out_qkv,
    out_out,
    grad_after,
    after_attn,
    slab_qkv,
    attended,
    grads,
    terms,
    across,
    slots,
    branch,
    summed,
    gain_terms,
    gain_slots,
    gain_sums,
    gain_sems,
    load_sems,
    *rest,
):
    place = Place()
    chips, block = place.chips, tokens.shape[0]
    model, width = tokens.shape[1], attended.shape[1]
    share = gains.shape[2]
    tile = 2 * block
    scatter_at, rest = rest[:6], rest[6:]
    down = Spread(place, lambda n: sum_down.at[n], out_down, rest[0], False)
    gate = Spread(place, lambda n: sum_gate.at[n], out_gate, rest[1], True)
    up = Spread(place, lambda n: sum_up.at[n], out_up, rest[2], True)
    qkv, out = reducer(place, rest[5:11]), reducer(place, rest[11:17])
    qkv_spread = Spread(place, qkv.piece, out_qkv, rest[3], True)
    out_spread = Spread(place, out.piece, out_out, rest[4], False)
    load = pltpu.make_async_copy(lowered_one, branch, load_sems.at[0])
    load.start()
    loads = [
        pltpu.make_async_copy(source, target, load_sems.at[2 + i])
        for i, (source, target) in enumerate(
            (
                (grads_in, grads),
                (slab_in, slab_qkv),
                (attended_in, attended),
                (grad_after_in, grad_after),
                (after_in, after_attn),
            )
        )
    ]
    for copy in loads:
        copy.start()
    place.enter()
    down.start()
    down.spread()
    gate.start()
    load.wait()
    loads[0].wait()

    def weigh_rows(j, _):
        left = branch[:, pl.ds(pl.multiple_of(j * share, share), share)]
        got = contract_first(left, grads[...]).astype(jnp.bfloat16)
        qkv.part[j] = got.reshape(qkv.part.shape[1:])
        return 0

    for half in range(2):
        lax.fori_loop(half * chips, (half + 1) * chips, weigh_rows, 0)
        qkv.start(half)
    reload = pltpu.make_async_copy(branch_in, branch, load_sems.at[1])
    reload.start()
    scatter = Scatter(place, terms, across, slots, block, scatter_at)

    def back_rows(t, _):
        at = pl.ds(pl.multiple_of(t * tile, tile), tile)
        got = contract_last(grads[at, :width], slab_qkv[:model, :])
        got += contract_last(grads[at, width : 2 * width], slab_qkv[model : 2 * model, :])
        got += contract_last(grads[at, 2 * width :], slab_qkv[2 * model :, :])
        terms[at, :] = got.astype(jnp.bfloat16)
        return 0

    loads[1].wait()
    lax.fori_loop(0, chips, back_rows, 0)
    for t in range(chips):
        scatter.side(t).start()
    down.widen()
    reload.wait()
    loads[2].wait()
    _, high, wide, thin, columns = out.part.shape
    for half in range(2):
        for at in range(0, columns, 512):
            got = contract_first(
                attended[...], branch[:, half * columns + at : half * columns + at + 512]
            ).astype(jnp.bfloat16)
            out.part[half, :, :, :, at : at + 512] = got.reshape(high, wide, thin, 512)
    out.start(0)
    out.start(1)
    for t in range(chips):
        scatter.cross(t)
    scatter.step(1)
    gate.spread()
    qkv.exchange()
    for step in range(2, chips):
        scatter.step(step)
    up.start()
    scatter.finish(summed)
    gain_terms[...] = gain_terms_in[...]
    loads[3].wait()
    loads[4].wait()
    norm_back(tokens, 0, gains, summed, grad_after, grad_tokens, gain_terms)

    def send_gain(k, _):
        to = lax.rem(place.me + k, place.fsdp)
        remote(
            gain_terms.at[to], gain_slots.at[place.me], gain_sems.at[0], gain_sems.at[1], fsdp=to
        ).start()
        return 0

    lax.fori_loop(1, place.fsdp, send_gain, 0)
    gain_slots[place.me] = gain_terms[place.me]
    scatter.drain()
    load_sums = pltpu.make_async_copy(sums, terms, load_sems.at[0])
    load_sums.start()
    out.exchange()
    gate.widen()
    qkv.total()
    qkv_spread.start()
    await_bytes(gain_slots.at[pl.ds(0, place.fsdp - 1)], gain_sems.at[1])
    gain_sums[place.replica] = jnp.sum(gain_slots[...], axis=0)

    def send_sum(k, _):
        ref = gain_sums.at[place.replica]
        to = lax.rem(place.replica + k, place.replicas)
        remote(ref, ref, gain_sems.at[2], gain_sems.at[3], replica=to).start()
        return 0

    lax.fori_loop(1, place.replicas, send_sum, 0)

    load_sums.wait()
    for t in range(chips):
        scatter.side(t).start()
    up.spread()
    for t in range(chips):
        scatter.cross(t)
    scatter.step(1)
    out.total()
    out_spread.start()
    out_spread.spread()
    qkv_spread.spread()
    up.widen()
    for step in range(2, chips):
        scatter.step(step)
    out_spread.widen()
    scatter.finish(summed)
    outputs[...] = (summed[...] + after_attn[...]).astype(outputs.dtype)
    qkv_spread.widen()
    await_bytes(gain_sums.at[pl.ds(0, place.replicas - 1)], gain_sems.at[3])
    gain_out[...] = jnp.sum(gain_sums[...], axis=0)
    await_bytes(gain_slots.at[pl.ds(0, place.fsdp - 1)], gain_sems.at[0])
    await_bytes(gain_sums.at[pl.ds(0, place.replicas - 1)], gain_sems.at[2])
    scatter.drain()
    qkv.drain()
    out.drain()
    for spread in (down, gate, up, out_spread, qkv_spread):
        spread.finish()


def back(
    tokens,
    gains,
    grad_after,
    gain_terms,
    after_attn,
    sums,
    sum_down,
    sum_gate,
    sum_up,
    branch,
    lowered_one,
    slab_qkv,
    attended,
    grads,
):
    fsdp, replicas = lax.axis_size("fsdp"), lax.axis_size("replica")
    chips, high, wide = fsdp // 2, 2, replicas // 2
    block, model = tokens.shape
    rows, width = attended.shape
    share = gains.shape[2]
    low, full = jnp.bfloat16, jnp.float32
    hbm, vmem = pl.BlockSpec(memory_space=pl.ANY), pl.BlockSpec(memory_space=pltpu.VMEM)
    shape = jax.ShapeDtypeStruct
    thin = share // replicas
    columns = sum_gate.shape[-1]
    qkv_piece = (fsdp, high, wide, thin, 3 * width)
    out_piece = (2, high, wide, width // replicas, model // 2)
    dma = pltpu.SemaphoreType.DMA
    return pl.pallas_call(
        back_kernel,
        in_specs=[vmem, vmem, hbm, vmem] + [hbm] * 10,
        out_specs=[vmem] * 3 + [hbm] * 5,
        out_shape=[
            shape((block, model), low),
            shape((block, model), full),
            shape((8, share), full),
            shape((2, high, wide) + sum_down.shape[1:], low),
            shape((1, high, wide, thin, fsdp * columns), low),
            shape((1, high, wide, thin, fsdp * columns), low),
            shape((3, high, wide, thin, fsdp * width), low),
            shape(out_piece, low),
        ],
        scratch_shapes=[
            pltpu.VMEM((block, model), full),
            pltpu.VMEM((block, model), full),
            pltpu.VMEM(slab_qkv.shape, low),
            pltpu.VMEM((rows, width), low),
            pltpu.VMEM((rows, 3 * width), low),
            pltpu.VMEM((rows, model), low),
            pltpu.VMEM((chips * block, model), low),
            pltpu.VMEM((chips + 1, block, model), low),
            pltpu.VMEM((rows, model), low),
            pltpu.VMEM((block, model), full),
            pltpu.VMEM((fsdp, 8, share), full),
            pltpu.VMEM((fsdp, 8, share), full),
            pltpu.VMEM((replicas, 8, share), full),
            dma((4,)),
            dma((7,)),
        ]
        + scatter_sems(chips)
        + spread_sems() * 5
        + reduce_scratch(*qkv_piece)
        + reduce_scratch(*out_piece),
        compiler_params=pltpu.CompilerParams(
            collective_id=2, has_side_effects=True, vmem_limit_bytes=VMEM_LIMIT
        ),
        name="back",
    )(
        tokens,
        gains,
        grad_after,
        gain_terms,
        after_attn,
        sums,
        sum_down,
        sum_gate,
        sum_up,
        branch,
        lowered_one,
        slab_qkv,
        attended,
        grads,
    )


def widen_kernel(
    down,
    gate,
    up,
    qkv,
    out,
    outputs_in,
    tokens_in,
    gains,
    w_down,
    w_gate,
    w_up,
    w_query,
    w_key,
    w_value,
    w_out,
    outputs,
    grad_tokens,
    gain_one,
    gain_two,
):
    w_down[...] = down[...].astype(jnp.float32)
    w_gate[...] = gate[...].astype(jnp.float32)
    w_up[...] = up[...].astype(jnp.float32)
    for i, ref in enumerate((w_query, w_key, w_value)):
        ref[...] = qkv[i].astype(jnp.float32)
    half = out.shape[2]
    for i in range(2):
        w_out[:, i * half : (i + 1) * half] = out[i].astype(jnp.float32)
    outputs[...] = outputs_in[...]
    grad_tokens[...] = tokens_in[...]
    gain_one[...] = gains[0, :]
    gain_two[...] = gains[1, :]


def widen(down, gate, up, qkv, out, outputs, grad_tokens, gains):
    steps = min(16, gate.shape[0] // 16)
    token_steps = outputs.shape[0] // 16
    full = jnp.float32

    def rows(array):
        return pl.BlockSpec((array.shape[0] // steps, array.shape[1]), lambda i: (i, 0))

    def tokens(array):
        return pl.BlockSpec(
            (array.shape[0] // token_steps, array.shape[1]), lambda i: (jnp.minimum(i, token_steps - 1), 0)
        )

    def stacked(array):
        return pl.BlockSpec((array.shape[0], array.shape[1] // steps, array.shape[2]), lambda i: (0, i, 0))

    like = [down, gate, up, qkv[0], qkv[0], qkv[0]]
    shapes = [jax.ShapeDtypeStruct(array.shape, full) for array in like]
    shapes.append(jax.ShapeDtypeStruct((out.shape[1], 2 * out.shape[2]), full))
    row = jax.ShapeDtypeStruct(gains.shape[1:], full)
    whole = pl.BlockSpec(gains.shape, lambda i: (0, 0))
    line = pl.BlockSpec(gains.shape[1:], lambda i: (0,))
    return pl.pallas_call(
        widen_kernel,
        grid=(steps,),
        in_specs=[rows(down), rows(gate), rows(up), stacked(qkv), stacked(out)]
        + [tokens(outputs), tokens(grad_tokens), whole],
        out_specs=[rows(shape) for shape in shapes]
        + [tokens(outputs), tokens(grad_tokens), line, line],
        out_shape=shapes
        + [jax.ShapeDtypeStruct(array.shape, array.dtype) for array in (outputs, grad_tokens)]
        + [row, row],
        compiler_params=pltpu.CompilerParams(vmem_limit_bytes=VMEM_LIMIT),
        name="widen",
    )(down, gate, up, qkv, out, outputs, grad_tokens, gains)


def local(
    tokens, attn_gain, w_query, w_key, w_value, w_out, ffn_gain, w_gate, w_up, w_down, cotangent
):
    cosine, sine = rope_tables(tokens.shape[0] * lax.axis_size("fsdp"))
    (
        lowered_one,
        lowered_two,
        cotangents,
        slab_qkv,
        hidden,
        grad_gate,
        grad_up,
        terms,
        sums,
        queries,
        keys,
        values,
        attended,
        logs,
        after_attn,
        gains,
    ) = front(
        tokens,
        cotangent,
        attn_gain,
        ffn_gain,
        w_query,
        w_key,
        w_value,
        w_out,
        w_gate,
        w_up,
        w_down,
        cosine,
        sine,
    )
    gain_terms, grad_after, grads, branch, sum_down, sum_gate, sum_up = weigh(
        cotangent,
        after_attn,
        gains,
        terms,
        lowered_two,
        cotangents,
        hidden,
        grad_gate,
        grad_up,
        w_out,
        queries,
        keys,
        values,
        logs,
        cosine,
        sine,
    )
    outputs, grad_tokens, gain_grads, low_down, low_gate, low_up, low_qkv, low_out = back(
        tokens,
        gains,
        grad_after,
        gain_terms,
        after_attn,
        sums,
        sum_down,
        sum_gate,
        sum_up,
        branch,
        lowered_one,
        slab_qkv,
        attended,
        grads,
    )
    (
        grad_w_down,
        grad_w_gate,
        grad_w_up,
        grad_w_query,
        grad_w_key,
        grad_w_value,
        grad_w_out,
        outputs,
        grad_tokens,
        grad_attn_gain,
        grad_ffn_gain,
    ) = widen(
        low_down.reshape(w_down.shape),
        low_gate.reshape(w_gate.shape),
        low_up.reshape(w_up.shape),
        low_qkv.reshape((3,) + w_query.shape),
        low_out.reshape(2, w_out.shape[0], -1),
        outputs,
        grad_tokens,
        gain_grads,
    )
    return (
        outputs,
        grad_tokens,
        grad_attn_gain,
        grad_w_query,
        grad_w_key,
        grad_w_value,
        grad_w_out,
        grad_ffn_gain,
        grad_w_gate,
        grad_w_up,
        grad_w_down,
    )


def solution(mesh):
    rows = P("fsdp", None)
    tokens = P(("replica", "fsdp"), None)
    gain = P("fsdp")
    return jax.shard_map(
        local,
        mesh=mesh,
        in_specs=(tokens, gain, rows, rows, rows, rows, gain, rows, rows, rows, tokens),
        out_specs=(tokens, tokens, gain, rows, rows, rows, rows, gain, rows, rows, rows),
        check_vma=False,
    )
```

```python
import functools

import jax
import jax.numpy as jnp
import numpy as np
from jax import lax
from jax.experimental import pallas as pl
from jax.experimental.pallas import tpu as pltpu
from jax.sharding import PartitionSpec as P

HEAD_DIM = 64

eps_norm = 1e-05
rope_base = 130000.0
masked_score = -1e30


def rope_tables(row_count):
    lane = np.arange(2 * HEAD_DIM) % HEAD_DIM
    halfway = HEAD_DIM // 2
    spacing = ((lane % halfway) * np.float32(2.0) / HEAD_DIM).astype(np.float32)
    frequency = np.power(np.float32(rope_base), -spacing)
    angles = np.arange(row_count, dtype=np.float32)[:, None] * frequency[None, :]
    sign = np.where(lane < halfway, -1.0, 1.0).astype(np.float32)
    return np.cos(angles).astype(np.float32), (np.sin(angles) * sign[None, :]).astype(np.float32)


def dot(left, right):
    return jnp.dot(left, right, preferred_element_type=jnp.float32)


def contract_last(left, right):
    return lax.dot_general(
        left, right, (((1,), (1,)), ((), ())), preferred_element_type=jnp.float32
    )


def contract_first(left, right):
    return lax.dot_general(
        left, right, (((0,), (0,)), ((), ())), preferred_element_type=jnp.float32
    )


def scores_of(queries, keys, first_row):
    rows, columns = queries.shape[0], keys.shape[0]
    scores = contract_last(queries, keys) * HEAD_DIM**-0.5
    at_row = lax.broadcasted_iota(jnp.int32, (rows, columns), 0) + first_row
    at_column = lax.broadcasted_iota(jnp.int32, (rows, columns), 1)
    return jnp.where(at_column <= at_row, scores, masked_score)


MESH = pl.DeviceIdType.MESH
VMEM_LIMIT = 61 * 2**20


def remote(src, dst, send, recv, **where):
    return pltpu.make_async_remote_copy(
        src_ref=src, dst_ref=dst, send_sem=send, recv_sem=recv, device_id=where, device_id_type=MESH
    )


def await_bytes(ref, sem):
    pltpu.make_async_copy(ref, ref, sem).wait()


def rows_at(ref, index, size):
    return ref.at[pl.ds(pl.multiple_of(index * size, size), size)]


class Place:
    def __init__(self):
        self.fsdp, self.replicas = lax.axis_size("fsdp"), lax.axis_size("replica")
        self.me, self.replica = lax.axis_index("fsdp"), lax.axis_index("replica")
        self.chips = self.fsdp // 2
        self.chip, self.core = self.me // 2, self.me % 2
        self.sibling = self.me + 1 - 2 * self.core
        self.high, self.wide = 2, self.replicas // 2
        self.a, self.b = self.replica // self.wide, self.replica % self.wide
        self.counts = ((self.wide, self.high), (self.high, self.wide))
        self.above = self.chip + 1 < self.chips
        self.below = self.chip >= 1

    def peer(self, half, stage, k):
        if half == stage:
            to = lax.rem(self.b + k, self.wide)
            return to, self.a * self.wide + to
        to = lax.rem(self.a + k, self.high)
        return to, to * self.wide + self.b

    def nearest(self, k):
        found = jnp.int32(0)
        for chip in range(self.chips):
            order = sorted(range(self.chips), key=lambda other, chip=chip: (abs(other - chip), other))
            found = found + jnp.where(self.chip == chip, order[k], 0)
        return found

    def enter(self):
        barrier = pltpu.get_barrier_semaphore()

        def greet(k, _):
            to = lax.rem(self.me + k, self.fsdp)
            pl.semaphore_signal(barrier, inc=1, device_id={"fsdp": to}, device_id_type=MESH)
            return 0

        def greet_replica(k, _):
            to = lax.rem(self.replica + k, self.replicas)
            pl.semaphore_signal(barrier, inc=1, device_id={"replica": to}, device_id_type=MESH)
            return 0

        lax.fori_loop(1, self.fsdp, greet, 0)
        lax.fori_loop(1, self.replicas, greet_replica, 0)
        pl.semaphore_wait(barrier, self.fsdp - 1 + self.replicas - 1)


def line_sems(chips):
    return [pltpu.SemaphoreType.DMA((chips,))] * 6


class Gather:
    def __init__(self, place, buf, block, sems, own=None):
        self.p, self.buf, self.block, self.own = place, buf, block, own
        self.up_out, self.up_in, self.down_out, self.down_in, self.side_out, self.side_in = sems

    def held(self, chip):
        return rows_at(self.buf, 2 * chip + self.p.core, self.block)

    def up(self, step):
        ref = self.held(self.p.chip - step + 1)
        src = self.own if step == 1 and self.own is not None else ref
        return remote(src, ref, self.up_out.at[step], self.up_in.at[step], fsdp=self.p.me + 2)

    def down(self, step):
        ref = self.held(self.p.chip + step - 1)
        src = self.own if step == 1 and self.own is not None else ref
        return remote(src, ref, self.down_out.at[step], self.down_in.at[step], fsdp=self.p.me - 2)

    def side(self, chip, src=None):
        ref = self.held(chip)
        src = ref if src is None else src
        return remote(src, ref, self.side_out.at[chip], self.side_in.at[chip], fsdp=self.p.sibling)

    def start(self):
        p = self.p
        pl.when(p.above)(lambda: self.up(1).start())
        pl.when(p.below)(lambda: self.down(1).start())
        self.side(p.chip, self.own).start()

    def step(self, step):
        p = self.p
        from_below, from_above = p.chip - step, p.chip + step

        @pl.when(from_below >= 0)
        def _():
            await_bytes(self.held(from_below), self.up_in.at[step])
            if step + 1 < p.chips:
                pl.when(p.above)(lambda: self.up(step + 1).start())
            self.side(from_below).start()

        @pl.when(from_above < p.chips)
        def _():
            await_bytes(self.held(from_above), self.down_in.at[step])
            if step + 1 < p.chips:
                pl.when(p.below)(lambda: self.down(step + 1).start())
            self.side(from_above).start()

    def across(self, chip):
        await_bytes(rows_at(self.buf, 2 * chip + 1 - self.p.core, self.block), self.side_in.at[chip])

    def drain(self):
        p = self.p
        for step in range(1, p.chips):
            pl.when(jnp.logical_and(p.above, p.chip - step + 1 >= 0))(
                lambda step=step: self.up(step).wait_send()
            )
            pl.when(jnp.logical_and(p.below, p.chip + step - 1 < p.chips))(
                lambda step=step: self.down(step).wait_send()
            )
        for chip in range(p.chips):
            self.side(chip).wait_send()

    def finish(self):
        for chip in range(self.p.chips):
            self.across(chip)
        self.drain()


class Scatter:
    def __init__(self, place, terms, across, slots, block, sems):
        self.p, self.terms, self.across, self.slots, self.block = place, terms, across, slots, block
        self.up_out, self.up_in, self.down_out, self.down_in, self.side_out, self.side_in = sems

    def side(self, chip):
        p = self.p
        return remote(
            rows_at(self.terms, 2 * chip + 1 - p.core, self.block),
            rows_at(self.across, chip, self.block),
            self.side_out.at[chip],
            self.side_in.at[chip],
            fsdp=p.sibling,
        )

    def term(self, chip):
        return rows_at(self.terms, 2 * chip + self.p.core, self.block)

    def up(self, step):
        return remote(
            self.term(self.p.chips - step + self.p.chip),
            self.slots.at[step - self.p.chip - 1],
            self.up_out.at[step],
            self.up_in.at[step],
            fsdp=self.p.me + 2,
        )

    def down(self, step):
        return remote(
            self.term(self.p.chip - self.p.chips + step),
            self.slots.at[step + 1],
            self.down_out.at[step],
            self.down_in.at[step],
            fsdp=self.p.me - 2,
        )

    def add(self, chip, arrived):
        term = self.term(chip)
        term[...] = (term[...].astype(jnp.float32) + arrived[...].astype(jnp.float32)).astype(term.dtype)

    def cross(self, chip):
        arrived = rows_at(self.across, chip, self.block)
        await_bytes(arrived, self.side_in.at[chip])
        self.add(chip, arrived)

    def step(self, step):
        p = self.p
        rising, falling = p.chips - step + p.chip, p.chip - p.chips + step

        @pl.when(jnp.logical_and(p.above, rising < p.chips))
        def _():
            if step > 1:

                @pl.when(p.below)
                def _():
                    arrived = self.slots.at[step - 1 - p.chip]
                    await_bytes(arrived, self.up_in.at[step - 1])
                    self.add(rising, arrived)

            self.up(step).start()

        @pl.when(jnp.logical_and(p.below, falling >= 0))
        def _():
            if step > 1:

                @pl.when(p.above)
                def _():
                    arrived = self.slots.at[step]
                    await_bytes(arrived, self.down_in.at[step - 1])
                    self.add(falling, arrived)

            self.down(step).start()

    def finish(self, total):
        p, last = self.p, self.p.chips - 1
        total[...] = self.term(p.chip)[...].astype(jnp.float32)

        @pl.when(p.below)
        def _():
            await_bytes(self.slots.at[last - p.chip], self.up_in.at[last])
            total[...] += self.slots[last - p.chip].astype(jnp.float32)

        @pl.when(p.above)
        def _():
            await_bytes(self.slots.at[last + 1], self.down_in.at[last])
            total[...] += self.slots[last + 1].astype(jnp.float32)

    def drain(self):
        p = self.p
        for step in range(1, p.chips):
            pl.when(jnp.logical_and(p.above, p.chips - step + p.chip < p.chips))(
                lambda step=step: self.up(step).wait_send()
            )
            pl.when(jnp.logical_and(p.below, p.chip - p.chips + step >= 0))(
                lambda step=step: self.down(step).wait_send()
            )
        for chip in range(p.chips):
            self.side(chip).wait_send()


def scatter_sems(chips):
    dma = pltpu.SemaphoreType.DMA
    return [dma((chips,))] * 6


class Turn:
    def __init__(self, place, weight, slab, first, sems):
        self.p, self.weight, self.slab, self.first = place, weight, slab, first
        self.far_out, self.far_in, self.near_out, self.near_in, self.own, self.passing = sems
        self.height, self.width = weight.shape[0], slab.shape[1]
        self.share = self.height // place.replicas

    def far_rows(self):
        return (self.p.fsdp - 2) * self.share

    def piece(self, block, share):
        at = self.first + block * self.height + share * self.share
        return self.slab.at[pl.ds(pl.multiple_of(at, self.share), self.share)]

    def whole(self, block):
        at = self.first + block * self.height
        return self.slab.at[pl.ds(pl.multiple_of(at, self.height), self.height)]

    def columns(self, to):
        return pl.ds(pl.multiple_of(to * self.width, self.width), self.width)

    def start(self):
        p = self.p

        def send(k, _):
            to = lax.rem(2 * p.chip + 2 + k, p.fsdp)
            share = pl.ds(pl.multiple_of(p.replica * self.share, self.share), self.share)
            remote(
                self.weight.at[share, self.columns(to)],
                self.piece(p.me, p.replica),
                self.far_out,
                self.far_in,
                fsdp=to,
            ).start()
            return 0

        lax.fori_loop(0, p.fsdp - 2, send, 0)
        self.near().start()
        self.mine().start()

    def near(self):
        p = self.p
        return remote(
            self.weight.at[:, self.columns(p.sibling)], self.whole(p.me), self.near_out, self.near_in, fsdp=p.sibling
        )

    def mine(self):
        return pltpu.make_async_copy(self.weight.at[:, self.columns(self.p.me)], self.whole(self.p.me), self.own)

    def await_far(self):
        await_bytes(self.slab.at[pl.ds(0, self.far_rows())], self.far_in)

    def bytes_of(self, pieces):
        return self.slab.at[pl.ds(0, pieces * self.share)]

    def pass_bytes(self, half, stage):
        first, second = self.p.counts[half]
        return self.bytes_of((self.p.chips - 1) * (second - 1 if stage == 0 else second * (first - 1)))

    def send_pieces(self, half, stage, shares):
        p = self.p

        def one(i, _):
            block = lax.rem(2 * p.chip + 2 + 2 * i + half, p.fsdp)
            for share in shares:
                ref = self.piece(block, share)
                for k in range(1, p.counts[half][1 - stage]):
                    _, replica = p.peer(half, 1 - stage, k)
                    remote(
                        ref,
                        ref,
                        self.passing.at[half, 2 * stage],
                        self.passing.at[half, 2 * stage + 1],
                        replica=replica,
                    ).start()
            return 0

        lax.fori_loop(0, p.chips - 1, one, 0)

    def pass_on(self):
        for half in range(2):
            self.send_pieces(half, 0, [self.p.replica])

    def pass_far(self):
        p = self.p
        for half in range(2):
            await_bytes(self.pass_bytes(half, 0), self.passing.at[half, 1])
            if half == 0:
                shares = [a * p.wide + p.b for a in range(p.high)]
            else:
                shares = [p.a * p.wide + b for b in range(p.wide)]
            self.send_pieces(half, 1, shares)

    def finish(self):
        for half in range(2):
            await_bytes(self.pass_bytes(half, 1), self.passing.at[half, 3])
        await_bytes(self.whole(self.p.sibling), self.near_in)
        self.mine().wait()

    def drain(self):
        await_bytes(self.slab.at[pl.ds(0, self.far_rows())], self.far_out)
        self.near().wait_send()
        for half in range(2):
            await_bytes(self.pass_bytes(half, 0), self.passing.at[half, 0])
            await_bytes(self.pass_bytes(half, 1), self.passing.at[half, 2])


def turn_sems():
    return [pltpu.SemaphoreType.DMA(())] * 5 + [pltpu.SemaphoreType.DMA((2, 4))]


def partner(values):
    halfway = HEAD_DIM // 2
    width = values.shape[1]
    lane = lax.broadcasted_iota(jnp.int32, values.shape, 1) % HEAD_DIM
    return jnp.where(
        lane < halfway,
        pltpu.roll(values, width - halfway, axis=1),
        pltpu.roll(values, halfway, axis=1),
    )


def front_kernel(
    tokens,
    cotangent,
    gain_one,
    gain_two,
    w_query,
    w_key,
    w_value,
    w_out,
    w_gate,
    w_up,
    w_down,
    cosine,
    sine,
    lowered_one,
    lowered_two_out,
    cotangents,
    slab_qkv_out,
    hidden_out,
    grad_gate_out,
    grad_up_out,
    terms_out,
    sums_out,
    queries,
    keys,
    values,
    attended,
    logs,
    after_attn,
    gains,
    low,
    tiles,
    lowered_two,
    slab_qkv,
    slab_gate,
    slab_up,
    held_down,
    terms,
    across,
    slots,
    tile_hidden,
    tile_gate,
    tile_up,
    tile_terms,
    tile_sums,
    grad_hiddens,
    gain_rows,
    gain_out,
    gain_in,
    copy_sems,
    load_sems,
    store_sems,
    *sems,
):
    place = Place()
    chips, block = place.chips, tokens.shape[0]
    model, width = tokens.shape[1], queries.shape[1]
    share = gain_one.shape[0]
    tile = 2 * block
    one_at, cot_at, two_at, scatter_at = sems[:6], sems[6:12], sems[12:18], sems[18:24]
    turn_at = [sems[24 + 6 * i : 30 + 6 * i] for i in range(5)]
    turns = [
        Turn(place, weight, slab_qkv, i * model, turn_at[i])
        for i, weight in enumerate((w_query, w_key, w_value))
    ]
    turn_gate = Turn(place, w_gate, slab_gate, 0, turn_at[3])
    turn_up = Turn(place, w_up, slab_up, 0, turn_at[4])
    here = pl.ds(pl.multiple_of(place.me * block, block), block)

    gain_rows[...] = jnp.zeros_like(gain_rows)
    gain_rows[0, :] = gain_one[...].astype(jnp.float32)
    gain_rows[1, :] = gain_two[...].astype(jnp.float32)
    load_down = pltpu.make_async_copy(w_down, held_down, copy_sems.at[0])
    load_down.start()
    keep_cot = pltpu.make_async_copy(cotangent, cotangents.at[here], copy_sems.at[1])
    keep_cot.start()
    place.enter()

    def send_gains(k, _):
        to = lax.rem(place.me + k, place.fsdp)
        remote(gain_rows, gains.at[place.me], gain_out, gain_in, fsdp=to).start()
        return 0

    lax.fori_loop(1, place.fsdp, send_gains, 0)
    for turn in turns:
        turn.start()
    gains[place.me] = gain_rows[...]
    inputs = tokens[...].astype(jnp.float32)
    factor = lax.rsqrt(jnp.mean(inputs * inputs, axis=-1, keepdims=True) + eps_norm)
    await_bytes(gains.at[pl.ds(0, place.fsdp - 1)], gain_in)
    for j in range(model // share):
        at = pl.ds(j * share, share)
        normed = tokens[:, at].astype(jnp.float32) * factor
        low[:, at] = (normed * gains[j, 0:1, :]).astype(jnp.bfloat16)
    first = Gather(place, lowered_one, block, one_at, low)
    first.start()
    keep_low = pltpu.make_async_copy(low, lowered_one.at[here], copy_sems.at[2])
    keep_low.start()
    for turn in turns:
        turn.await_far()
        turn.pass_on()
    for step in range(1, chips):
        if step == chips - 1:
            turn_gate.start()
        first.step(step)
        if step == 1:
            for turn in turns:
                turn.pass_far()
    turn_up.start()
    third = Gather(place, cotangents, block, cot_at, cotangent)
    third.start()
    keep_low.wait()
    first.finish()

    def load(source, t, slot):
        return pltpu.make_async_copy(rows_at(source, t, tile), tiles.at[slot], load_sems.at[slot])

    load(lowered_one, 0, 0).start()
    for turn in turns:
        turn.finish()
    keep_slab = pltpu.make_async_copy(slab_qkv, slab_qkv_out, copy_sems.at[3])
    keep_slab.start()
    for t in range(chips):
        if t + 1 < chips:
            load(lowered_one, t + 1, (t + 1) % 2).start()
        load(lowered_one, t, t % 2).wait()
        at = pl.ds(t * tile, tile)
        for i, ref in enumerate((queries, keys, values)):
            out = dot(tiles[t % 2], slab_qkv[i * model : (i + 1) * model, :])
            if i < 2:
                for j in range(0, width, 2 * HEAD_DIM):
                    pair = out[:, j : j + 2 * HEAD_DIM]
                    pair = pair * cosine[at, :] + partner(pair) * sine[at, :]
                    ref[at, j : j + 2 * HEAD_DIM] = pair.astype(jnp.bfloat16)
            else:
                ref[at, :] = out.astype(jnp.bfloat16)
    scatter = Scatter(place, terms, across, slots, block, scatter_at)
    pair = 2 * HEAD_DIM
    for t in range(chips):
        here_t, seen = pl.ds(t * tile, tile), pl.ds(0, (t + 1) * tile)

        def heads(h, _, t=t, here_t=here_t, seen=seen):
            lanes = pl.ds(pl.multiple_of(h * pair, pair), pair)
            q2, k2, v2 = queries[here_t, lanes], keys[seen, lanes], values[seen, lanes]
            mixed, stats = [], []
            for at in (0, HEAD_DIM):
                head = slice(at, at + HEAD_DIM)
                scores = scores_of(q2[:, head], k2[:, head], t * tile)
                most = jnp.max(scores, axis=-1, keepdims=True)
                weights = jnp.exp(scores - most)
                total = jnp.sum(weights, axis=-1, keepdims=True)
                mixed.append(dot((weights / total).astype(jnp.bfloat16), v2[:, head]))
                stats.append(jnp.broadcast_to(most + jnp.log(total), (tile, HEAD_DIM)))
            attended[here_t, lanes] = jnp.concatenate(mixed, axis=1).astype(jnp.bfloat16)
            logs[here_t, lanes] = jnp.concatenate(stats, axis=1)
            return 0

        lax.fori_loop(0, width // pair, heads, 0)
        terms[here_t, :] = dot(attended[here_t, :], w_out[...]).astype(jnp.bfloat16)
        scatter.side(t).start()
    for t in range(chips):
        scatter.cross(t)
    for step in range(1, chips):
        scatter.step(step)
        if step == 1:
            turn_gate.await_far()
            turn_gate.pass_on()
        if step < chips - 1:
            third.step(step)
        if step == 1:
            turn_gate.pass_far()
        if step == min(2, chips - 1):
            turn_up.await_far()
            turn_up.pass_on()
        if step == chips - 1:
            turn_up.pass_far()
    scatter.finish(after_attn)
    after_attn[...] += tokens[...].astype(jnp.float32)
    after = after_attn[...]
    factor = lax.rsqrt(jnp.mean(after * after, axis=-1, keepdims=True) + eps_norm)
    for j in range(model // share):
        at = pl.ds(j * share, share)
        normed = after_attn[:, at] * factor
        lowered_two[here, at] = (normed * gains[j, 1:2, :]).astype(jnp.bfloat16)
    second = Gather(place, lowered_two, block, two_at)
    second.start()
    third.step(chips - 1)
    keep_cot.wait()
    third.finish()
    load(cotangents, place.nearest(0), 0).start()
    load_down.wait()
    for k in range(chips):
        if k + 1 < chips:
            load(cotangents, place.nearest(k + 1), (k + 1) % 2).start()
        load(cotangents, place.nearest(k), k % 2).wait()
        grad_hiddens[k] = contract_last(tiles[k % 2], held_down[...])
    turn_gate.finish()
    turn_up.finish()

    def stores(k, t):
        slot = k % 2
        pairs = (
            (tile_hidden, hidden_out),
            (tile_gate, grad_gate_out),
            (tile_up, grad_up_out),
            (tile_terms, terms_out),
            (tile_sums, sums_out),
        )
        return [
            pltpu.make_async_copy(held.at[slot], rows_at(out, t, tile), store_sems.at[i, slot])
            for i, (held, out) in enumerate(pairs)
        ]

    for k in range(chips):
        t, slot = place.nearest(k), k % 2
        if k > 0:
            second.step(k)
        second.across(t)
        if k > 1:
            for store in stores(k - 2, place.nearest(k - 2)):
                store.wait()
        rows = lowered_two[pl.ds(pl.multiple_of(t * tile, tile), tile), :]
        gate = dot(rows, slab_gate[...])
        up = dot(rows, slab_up[...])
        grad_hidden = grad_hiddens[k]
        sigmoid = jax.nn.sigmoid(gate)
        silu = gate * sigmoid
        hidden = (silu * up).astype(jnp.bfloat16)
        grad_gate = (grad_hidden * up * sigmoid * (1.0 + gate * (1.0 - sigmoid))).astype(jnp.bfloat16)
        grad_up = (grad_hidden * silu).astype(jnp.bfloat16)
        tile_hidden[slot] = hidden
        tile_gate[slot] = grad_gate
        tile_up[slot] = grad_up
        got = contract_last(grad_gate, slab_gate[...]) + contract_last(grad_up, slab_up[...])
        tile_terms[slot] = got.astype(jnp.bfloat16)
        tile_sums[slot] = dot(hidden, held_down[...]).astype(jnp.bfloat16)
        for store in stores(k, t):
            store.start()
    keep_two = pltpu.make_async_copy(lowered_two, lowered_two_out, copy_sems.at[4])
    keep_two.start()
    second.drain()
    scatter.drain()
    for turn in turns + [turn_gate, turn_up]:
        turn.drain()
    await_bytes(gains.at[pl.ds(0, place.fsdp - 1)], gain_out)
    keep_slab.wait()
    for k in range(max(chips - 2, 0), chips):
        for store in stores(k, place.nearest(k)):
            store.wait()
    keep_two.wait()


def front(
    tokens, cotangent, gain_one, gain_two, w_query, w_key, w_value, w_out, w_gate, w_up, w_down, cosine, sine
):
    fsdp = lax.axis_size("fsdp")
    chips = fsdp // 2
    block, model = tokens.shape
    rows, width, wide = fsdp * block, w_query.shape[1] // fsdp, w_gate.shape[1] // fsdp
    tile = 2 * block
    share = gain_one.shape[0]
    low, full = jnp.bfloat16, jnp.float32
    hbm, vmem = pl.BlockSpec(memory_space=pl.ANY), pl.BlockSpec(memory_space=pltpu.VMEM)
    shape = jax.ShapeDtypeStruct
    dma = pltpu.SemaphoreType.DMA
    return pl.pallas_call(
        front_kernel,
        in_specs=[vmem] * 4 + [hbm] * 3 + [vmem] + [hbm] * 3 + [vmem] * 2,
        out_specs=[hbm] * 9 + [vmem] * 7,
        out_shape=[
            shape((rows, model), low),
            shape((rows, model), low),
            shape((rows, model), low),
            shape((3 * model, width), low),
            shape((rows, wide), low),
            shape((rows, wide), low),
            shape((rows, wide), low),
            shape((rows, model), low),
            shape((rows, model), low),
            shape((rows, width), low),
            shape((rows, width), low),
            shape((rows, width), low),
            shape((rows, width), low),
            shape((rows, width), full),
            shape((block, model), full),
            shape((fsdp, 8, share), full),
        ],
        scratch_shapes=[
            pltpu.VMEM((block, model), low),
            pltpu.VMEM((2, tile, model), low),
            pltpu.VMEM((rows, model), low),
            pltpu.VMEM((3 * model, width), low),
            pltpu.VMEM((model, wide), low),
            pltpu.VMEM((model, wide), low),
            pltpu.VMEM((wide, model), low),
            pltpu.VMEM((rows, model), low),
            pltpu.VMEM((chips * block, model), low),
            pltpu.VMEM((chips + 1, block, model), low),
            pltpu.VMEM((2, tile, wide), low),
            pltpu.VMEM((2, tile, wide), low),
            pltpu.VMEM((2, tile, wide), low),
            pltpu.VMEM((2, tile, model), low),
            pltpu.VMEM((2, tile, model), low),
            pltpu.VMEM((chips, tile, wide), full),
            pltpu.VMEM((8, share), full),
            dma(()),
            dma(()),
            dma((5,)),
            dma((2,)),
            dma((5, 2)),
        ]
        + line_sems(chips) * 3
        + scatter_sems(chips)
        + turn_sems() * 5,
        compiler_params=pltpu.CompilerParams(
            collective_id=0, has_side_effects=True, vmem_limit_bytes=VMEM_LIMIT
        ),
        name="front",
    )(
        tokens,
        cotangent,
        gain_one,
        gain_two,
        w_query,
        w_key,
        w_value,
        w_out,
        w_gate,
        w_up,
        w_down,
        cosine,
        sine,
    )


class Reduce:
    def __init__(self, place, part, first, second, sems):
        self.p, self.part, self.first, self.second, self.sems = place, part, first, second, sems
        self.half = part.shape[0] // 2

    def rows(self, half):
        return pl.ds(half * self.half, self.half)

    def sent(self, half, to):
        if half == 0:
            return self.part.at[self.rows(0), :, to]
        return self.part.at[self.rows(1), to]

    def own(self, half):
        return self.sent(half, self.p.b if half == 0 else self.p.a)

    def start(self, half):
        for k in range(1, self.p.counts[half][0]):
            to, replica = self.p.peer(half, 0, k)
            remote(
                self.sent(half, to),
                self.first[half].at[k - 1],
                self.sems.at[half, 0],
                self.sems.at[half, 1],
                replica=replica,
            ).start()

    def exchange(self):
        for half in range(2):
            own, arrived = self.own(half), self.first[half]
            await_bytes(arrived, self.sems.at[half, 1])

            def add(n, _, own=own, arrived=arrived):
                for m in range(own.shape[1]):
                    total = own[n, m].astype(jnp.float32)
                    for k in range(arrived.shape[0]):
                        total += arrived[k, n, m].astype(jnp.float32)
                    own[n, m] = total.astype(own.dtype)
                return 0

            lax.fori_loop(0, self.half, add, 0)
            for k in range(1, self.p.counts[half][1]):
                to, replica = self.p.peer(half, 1, k)
                remote(
                    own.at[:, to],
                    self.second[half].at[k - 1],
                    self.sems.at[half, 2],
                    self.sems.at[half, 3],
                    replica=replica,
                ).start()

    def total(self):
        for half in range(2):
            own, arrived = self.held(half), self.second[half]
            await_bytes(arrived, self.sems.at[half, 3])

            def add(n, _, own=own, arrived=arrived):
                total = own[n].astype(jnp.float32)
                for k in range(arrived.shape[0]):
                    total += arrived[k, n].astype(jnp.float32)
                own[n] = total.astype(own.dtype)
                return 0

            lax.fori_loop(0, self.half, add, 0)

    def held(self, half):
        return self.part.at[self.rows(half), self.p.a, self.p.b]

    def piece(self, n):
        return self.part.at[n, self.p.a, self.p.b]

    def drain(self):
        for half in range(2):
            await_bytes(self.first[half], self.sems.at[half, 0])
            await_bytes(self.second[half], self.sems.at[half, 2])


def reduce_scratch(n, high, wide, rows, columns):
    low = functools.partial(pltpu.VMEM, dtype=jnp.bfloat16)
    half = n // 2
    return [
        low((n, high, wide, rows, columns)),
        low((wide - 1, half, high, rows, columns)),
        low((high - 1, half, wide, rows, columns)),
        low((high - 1, half, rows, columns)),
        low((wide - 1, half, rows, columns)),
        pltpu.SemaphoreType.DMA((2, 4)),
    ]


def reducer(place, refs):
    part, first_a, first_b, second_a, second_b, sems = refs
    return Reduce(place, part, (first_a, first_b), (second_a, second_b), sems)


class Spread:
    def __init__(self, place, piece, out, sems, turned):
        self.p, self.piece, self.out, self.sems, self.turned = place, piece, out, sems, turned

    def start(self):
        p = self.p
        if self.turned:
            count = self.out.shape[0]
            width = self.out.shape[-1] // p.fsdp
            columns = pl.ds(pl.multiple_of(p.me * width, width), width)

            def pairs(to):
                ref = self.piece(to)
                return [
                    (ref.at[:, pl.ds(i * width, width)], self.out.at[i, p.a, p.b, :, columns])
                    for i in range(count)
                ]

            def send(k, _):
                to = lax.rem(p.me + k, p.fsdp)
                for ref, target in pairs(to):
                    remote(ref, target, self.sems.at[0, 0], self.sems.at[0, 1], fsdp=to).start()
                return 0

            lax.fori_loop(1, p.fsdp, send, 0)
            for ref, target in pairs(p.me):
                pltpu.make_async_copy(ref, target, self.sems.at[0, 1]).start()
        else:
            for half in range(2):
                pltpu.make_async_copy(
                    self.piece(half), self.out.at[half, p.a, p.b], self.sems.at[half, 1]
                ).start()

    def placed(self, half, rows):
        a, b = rows
        if self.turned:
            width = self.out.shape[-1] // 2
            return self.out.at[:, a, b, :, pl.ds(half * width, width)]
        return self.out.at[half, a, b]

    def spread(self):
        p = self.p
        if self.turned:
            await_bytes(self.out.at[:, p.a, p.b], self.sems.at[0, 1])
        for half in range(2):
            ref = self.placed(half, (p.a, p.b))
            src = ref if self.turned else self.piece(half)
            for k in range(1, p.counts[half][1]):
                _, replica = p.peer(half, 1, k)
                remote(src, ref, self.sems.at[half, 2], self.sems.at[half, 3], replica=replica).start()

    def spread_bytes(self, half):
        some = pl.ds(0, self.p.counts[half][1] - 1)
        return self.placed(half, (some, 0) if half == 0 else (0, some))

    def widen(self):
        p = self.p
        for half in range(2):
            if not self.turned:
                await_bytes(self.placed(half, (p.a, p.b)), self.sems.at[half, 1])
            await_bytes(self.spread_bytes(half), self.sems.at[half, 3])
            every = pl.ds(0, p.counts[half][1])
            ref = self.placed(half, (every, p.b) if half == 0 else (p.a, every))
            for k in range(1, p.counts[half][0]):
                _, replica = p.peer(half, 0, k)
                remote(ref, ref, self.sems.at[half, 4], self.sems.at[half, 5], replica=replica).start()

    def widen_bytes(self, half):
        counts = self.p.counts[half]
        every, some = pl.ds(0, counts[1]), pl.ds(0, counts[0] - 1)
        return self.placed(half, (every, some) if half == 0 else (some, every))

    def finish(self):
        p = self.p
        for half in range(2):
            await_bytes(self.widen_bytes(half), self.sems.at[half, 5])
            await_bytes(self.spread_bytes(half), self.sems.at[half, 2])
            await_bytes(self.widen_bytes(half), self.sems.at[half, 4])
        if self.turned:
            width = self.out.shape[-1] // p.fsdp
            await_bytes(
                self.out.at[:, p.a, p.b, :, pl.ds(0, (p.fsdp - 1) * width)], self.sems.at[0, 0]
            )


def spread_sems():
    return [pltpu.SemaphoreType.DMA((2, 6))]


def norm_back(values, gain_row, gains, grad, carried, result, gain_terms):
    block, model = values.shape
    share = gains.shape[2]
    held = values[...].astype(jnp.float32)
    factor = lax.rsqrt(jnp.mean(held * held, axis=-1, keepdims=True) + eps_norm)
    dots = jnp.zeros((block, 1), jnp.float32)
    for j in range(model // share):
        at = pl.ds(j * share, share)
        normed = values[:, at].astype(jnp.float32) * factor
        product = grad[:, at] * normed
        gain_terms[j, gain_row : gain_row + 1, :] = jnp.sum(product, axis=0, keepdims=True)
        dots += jnp.sum(product * gains[j, gain_row : gain_row + 1, :], axis=-1, keepdims=True)
    dots = dots / model
    for j in range(model // share):
        at = pl.ds(j * share, share)
        normed = values[:, at].astype(jnp.float32) * factor
        scaled = grad[:, at] * gains[j, gain_row : gain_row + 1, :]
        result[:, at] = carried[:, at].astype(jnp.float32) + factor * (scaled - normed * dots)


def weigh_kernel(
    cotangent,
    after_in,
    gains,
    terms_in,
    lowered_two,
    cotangents,
    hidden_in,
    grad_gate_in,
    grad_up_in,
    w_out_in,
    queries_in,
    keys_in,
    values_in,
    logs_in,
    cosine_in,
    sine_in,
    gain_terms,
    grad_after_out,
    grads_out,
    branch,
    sum_down,
    sum_gate,
    sum_up,
    after_attn,
    w_out,
    queries,
    keys,
    values,
    logs,
    cosine,
    sine,
    grad_after,
    grads,
    tokens_held,
    hidden,
    grad_gate,
    grad_up,
    terms,
    across,
    slots,
    summed,
    low,
    grad_low,
    grad_key,
    grad_value,
    load_sems,
    store_sems,
    late_sems,
    *rest,
):
    place = Place()
    chips, block = place.chips, cotangent.shape[0]
    model = cotangent.shape[1]
    tile = 2 * block
    scatter_at, gather_at = rest[:6], rest[6:12]
    down, gate, up = [reducer(place, rest[12 + 6 * i : 18 + 6 * i]) for i in range(3)]

    def load(t):
        at = pl.ds(t * tile, tile)
        return pltpu.make_async_copy(terms_in.at[at], terms.at[at], load_sems.at[t])

    loads = [
        pltpu.make_async_copy(source, target, load_sems.at[chips + i])
        for i, (source, target) in enumerate(
            (
                (cotangents, tokens_held),
                (hidden_in, hidden),
                (grad_gate_in, grad_gate),
                (grad_up_in, grad_up),
                (lowered_two, tokens_held),
            )
        )
    ]
    for t in range(chips):
        load(t).start()
    for copy in loads[:4]:
        copy.start()
    late = [
        pltpu.make_async_copy(source, target, late_sems.at[i])
        for i, (source, target) in enumerate(
            (
                (after_in, after_attn),
                (w_out_in, w_out),
                (queries_in, queries),
                (keys_in, keys),
                (values_in, values),
                (logs_in, logs),
                (cosine_in, cosine),
                (sine_in, sine),
            )
        )
    ]
    for copy in late:
        copy.start()
    keep_after = pltpu.make_async_copy(grad_after, grad_after_out, late_sems.at[8])
    keep_grads = pltpu.make_async_copy(grads, grads_out, late_sems.at[9])
    place.enter()
    scatter = Scatter(place, terms, across, slots, block, scatter_at)
    for t in range(chips):
        load(t).wait()
        scatter.side(t).start()
    gain_terms[...] = jnp.zeros_like(gain_terms)
    loads[0].wait()
    loads[1].wait()
    _, high, wide, thin, _ = down.part.shape
    columns = min(tile, hidden.shape[1])
    for i in range(0, hidden.shape[1], columns):
        got = contract_first(hidden[:, i : i + columns], tokens_held[...]).astype(jnp.bfloat16)
        for m in range(0, columns, thin):
            n = (i + m) // thin
            down.part[n // (high * wide), n // wide % high, n % wide] = got[m : m + thin, :]
        if 2 * (i + columns) == hidden.shape[1]:
            down.start(0)
    loads[4].start()
    down.start(1)
    for t in range(chips):
        scatter.cross(t)
    scatter.step(1)
    loads[4].wait()

    def weigh(reduce, grads):
        share = model // place.fsdp

        def rows(j, _):
            left = tokens_held[:, pl.ds(pl.multiple_of(j * share, share), share)]
            got = contract_first(left, grads[...]).astype(jnp.bfloat16)
            reduce.part[j] = got.reshape(reduce.part.shape[1:])
            return 0

        for half in range(2):
            lax.fori_loop(half * chips, (half + 1) * chips, rows, 0)
            reduce.start(half)

    loads[2].wait()
    weigh(gate, grad_gate)
    if chips > 2:
        scatter.step(2)
    loads[3].wait()
    weigh(up, grad_up)
    for step in range(3, chips):
        scatter.step(step)
    scatter.finish(summed)
    late[0].wait()
    norm_back(after_attn, 1, gains, summed, cotangent, grad_after, gain_terms)
    keep_after.start()
    low[...] = grad_after[...].astype(jnp.bfloat16)
    here = pl.ds(pl.multiple_of(place.me * block, block), block)
    gather = Gather(place, branch, block, gather_at, low)
    gather.start()
    keep = pltpu.make_async_copy(low, branch.at[here], store_sems.at[0])
    keep.start()
    scatter.drain()
    down.exchange()
    for step in range(1, chips):
        gather.step(step)
        if step == 1:
            gate.exchange()
        if step == max(chips - 2, 1):
            up.exchange()
    keep.wait()
    gather.finish()
    fetch = pltpu.make_async_copy(branch, tokens_held, load_sems.at[0])
    fetch.start()
    down.total()
    fetch.wait()
    for copy in late[1:]:
        copy.wait()

    def attend_rows(t, _):
        at = pl.ds(pl.multiple_of(t * tile, tile), tile)
        grad_low[at, :] = contract_last(tokens_held[at, :], w_out[...]).astype(jnp.bfloat16)
        return 0

    lax.fori_loop(0, chips, attend_rows, 0)
    width = queries.shape[1]
    scale = HEAD_DIM**-0.5
    grad_key[...] = jnp.zeros_like(grad_key)
    grad_value[...] = jnp.zeros_like(grad_value)
    pair = 2 * HEAD_DIM
    height = tile * 1024 // max(queries.shape[0], 1024)
    for first in range(0, queries.shape[0], height):
        rows, seen = pl.ds(first, height), pl.ds(0, first + height)

        def heads(h, _, first=first, rows=rows, seen=seen):
            lanes = pl.ds(pl.multiple_of(h * pair, pair), pair)
            q2, g2, log2 = queries[rows, lanes], grad_low[rows, lanes], logs[rows, lanes]
            k2, v2 = keys[seen, lanes], values[seen, lanes]
            for_queries, for_keys, for_values = [], [], []
            for at in (0, HEAD_DIM):
                head = slice(at, at + HEAD_DIM)
                q, g, k = q2[:, head], g2[:, head], k2[:, head]
                weights = jnp.exp(scores_of(q, k, first) - log2[:, at : at + 1])
                grad_weights = contract_last(g, v2[:, head])
                delta = jnp.sum(weights * grad_weights, axis=-1, keepdims=True)
                grad_scores = (weights * (grad_weights - delta)).astype(jnp.bfloat16)
                for_queries.append(dot(grad_scores, k))
                for_keys.append(contract_first(grad_scores, q))
                for_values.append(contract_first(weights.astype(jnp.bfloat16), g))
            got = jnp.concatenate(for_queries, axis=1) * scale
            got = got * cosine[rows, :] - partner(got) * sine[rows, :]
            grads[rows, lanes] = got.astype(jnp.bfloat16)
            grad_key[seen, lanes] += jnp.concatenate(for_keys, axis=1) * scale
            grad_value[seen, lanes] += jnp.concatenate(for_values, axis=1)
            return 0

        lax.fori_loop(0, width // pair, heads, 0)

    def turn_keys(t, _):
        at = pl.ds(pl.multiple_of(t * tile, tile), tile)
        for j in range(0, width, pair):
            got = grad_key[at, j : j + pair]
            got = got * cosine[at, :] - partner(got) * sine[at, :]
            grads[at, width + j : width + j + pair] = got.astype(jnp.bfloat16)
        grads[at, 2 * width :] = grad_value[at, :].astype(jnp.bfloat16)
        return 0

    lax.fori_loop(0, chips, turn_keys, 0)
    keep_grads.start()
    stores = [keep_after, keep_grads]
    for i, (reduce, out) in enumerate(((down, sum_down), (gate, sum_gate), (up, sum_up))):
        if i > 0:
            reduce.total()
        for half in range(2):
            store = pltpu.make_async_copy(
                reduce.held(half), out.at[reduce.rows(half)], store_sems.at[1 + 2 * i + half]
            )
            store.start()
            stores.append(store)
    for reduce in (down, gate, up):
        reduce.drain()
    for store in stores:
        store.wait()


def weigh(
    cotangent,
    after_attn,
    gains,
    terms,
    lowered_two,
    cotangents,
    hidden,
    grad_gate,
    grad_up,
    w_out,
    queries,
    keys,
    values,
    logs,
    cosine,
    sine,
):
    fsdp, replicas = lax.axis_size("fsdp"), lax.axis_size("replica")
    chips, high, wide = fsdp // 2, 2, replicas // 2
    block, model = cotangent.shape
    rows, columns = hidden.shape
    width = queries.shape[1]
    share = gains.shape[2]
    low, full = jnp.bfloat16, jnp.float32
    hbm, vmem = pl.BlockSpec(memory_space=pl.ANY), pl.BlockSpec(memory_space=pltpu.VMEM)
    shape = jax.ShapeDtypeStruct
    down_piece = (2, high, wide, columns // (2 * replicas), model)
    wide_piece = (fsdp, high, wide, share // replicas, columns)
    dma = pltpu.SemaphoreType.DMA
    return pl.pallas_call(
        weigh_kernel,
        in_specs=[vmem, hbm, vmem] + [hbm] * 13,
        out_specs=[vmem] + [hbm] * 6,
        out_shape=[
            shape((fsdp, 8, share), full),
            shape((block, model), full),
            shape((rows, 3 * width), low),
            shape((rows, model), low),
            shape((2,) + down_piece[3:], low),
            shape((fsdp,) + wide_piece[3:], low),
            shape((fsdp,) + wide_piece[3:], low),
        ],
        scratch_shapes=[
            pltpu.VMEM((block, model), full),
            pltpu.VMEM(w_out.shape, low),
            pltpu.VMEM((rows, width), low),
            pltpu.VMEM((rows, width), low),
            pltpu.VMEM((rows, width), low),
            pltpu.VMEM((rows, width), full),
            pltpu.VMEM(cosine.shape, full),
            pltpu.VMEM(sine.shape, full),
            pltpu.VMEM((block, model), full),
            pltpu.VMEM((rows, 3 * width), low),
            pltpu.VMEM((rows, model), low),
            pltpu.VMEM((rows, columns), low),
            pltpu.VMEM((rows, columns), low),
            pltpu.VMEM((rows, columns), low),
            pltpu.VMEM((rows, model), low),
            pltpu.VMEM((chips * block, model), low),
            pltpu.VMEM((chips + 1, block, model), low),
            pltpu.VMEM((block, model), full),
            pltpu.VMEM((block, model), low),
            pltpu.VMEM((rows, width), low),
            pltpu.VMEM((rows, width), full),
            pltpu.VMEM((rows, width), full),
            dma((chips + 5,)),
            dma((7,)),
            dma((10,)),
        ]
        + scatter_sems(chips)
        + line_sems(chips)
        + reduce_scratch(*down_piece)
        + reduce_scratch(*wide_piece)
        + reduce_scratch(*wide_piece),
        compiler_params=pltpu.CompilerParams(
            collective_id=1, has_side_effects=True, vmem_limit_bytes=VMEM_LIMIT
        ),
        name="weigh",
    )(
        cotangent,
        after_attn,
        gains,
        terms,
        lowered_two,
        cotangents,
        hidden,
        grad_gate,
        grad_up,
        w_out,
        queries,
        keys,
        values,
        logs,
        cosine,
        sine,
    )


def back_kernel(
    tokens,
    gains,
    grad_after_in,
    gain_terms_in,
    after_in,
    sums,
    sum_down,
    sum_gate,
    sum_up,
    branch_in,
    lowered_one,
    slab_in,
    attended_in,
    grads_in,
    outputs,
    grad_tokens,
    gain_out,
    out_down,
    out_gate,
    out_up,
    out_qkv,
    out_out,
    grad_after,
    after_attn,
    slab_qkv,
    attended,
    grads,
    terms,
    across,
    slots,
    branch,
    summed,
    gain_terms,
    gain_slots,
    gain_sums,
    gain_sems,
    load_sems,
    *rest,
):
    place = Place()
    chips, block = place.chips, tokens.shape[0]
    model, width = tokens.shape[1], attended.shape[1]
    share = gains.shape[2]
    tile = 2 * block
    scatter_at, rest = rest[:6], rest[6:]
    down = Spread(place, lambda n: sum_down.at[n], out_down, rest[0], False)
    gate = Spread(place, lambda n: sum_gate.at[n], out_gate, rest[1], True)
    up = Spread(place, lambda n: sum_up.at[n], out_up, rest[2], True)
    qkv, out = reducer(place, rest[5:11]), reducer(place, rest[11:17])
    qkv_spread = Spread(place, qkv.piece, out_qkv, rest[3], True)
    out_spread = Spread(place, out.piece, out_out, rest[4], False)
    load = pltpu.make_async_copy(lowered_one, branch, load_sems.at[0])
    load.start()
    loads = [
        pltpu.make_async_copy(source, target, load_sems.at[2 + i])
        for i, (source, target) in enumerate(
            (
                (grads_in, grads),
                (slab_in, slab_qkv),
                (attended_in, attended),
                (grad_after_in, grad_after),
                (after_in, after_attn),
            )
        )
    ]
    for copy in loads:
        copy.start()
    place.enter()
    down.start()
    down.spread()
    gate.start()
    load.wait()
    loads[0].wait()

    def weigh_rows(j, _):
        left = branch[:, pl.ds(pl.multiple_of(j * share, share), share)]
        got = contract_first(left, grads[...]).astype(jnp.bfloat16)
        qkv.part[j] = got.reshape(qkv.part.shape[1:])
        return 0

    for half in range(2):
        lax.fori_loop(half * chips, (half + 1) * chips, weigh_rows, 0)
        qkv.start(half)
    reload = pltpu.make_async_copy(branch_in, branch, load_sems.at[1])
    reload.start()
    scatter = Scatter(place, terms, across, slots, block, scatter_at)

    def back_rows(t, _):
        at = pl.ds(pl.multiple_of(t * tile, tile), tile)
        got = contract_last(grads[at, :width], slab_qkv[:model, :])
        got += contract_last(grads[at, width : 2 * width], slab_qkv[model : 2 * model, :])
        got += contract_last(grads[at, 2 * width :], slab_qkv[2 * model :, :])
        terms[at, :] = got.astype(jnp.bfloat16)
        return 0

    loads[1].wait()
    lax.fori_loop(0, chips, back_rows, 0)
    for t in range(chips):
        scatter.side(t).start()
    down.widen()
    reload.wait()
    loads[2].wait()
    _, high, wide, thin, columns = out.part.shape
    for half in range(2):
        for at in range(0, columns, 512):
            got = contract_first(
                attended[...], branch[:, half * columns + at : half * columns + at + 512]
            ).astype(jnp.bfloat16)
            out.part[half, :, :, :, at : at + 512] = got.reshape(high, wide, thin, 512)
    out.start(0)
    out.start(1)
    for t in range(chips):
        scatter.cross(t)
    scatter.step(1)
    gate.spread()
    qkv.exchange()
    for step in range(2, chips):
        scatter.step(step)
    up.start()
    scatter.finish(summed)
    gain_terms[...] = gain_terms_in[...]
    loads[3].wait()
    loads[4].wait()
    norm_back(tokens, 0, gains, summed, grad_after, grad_tokens, gain_terms)

    def send_gain(k, _):
        to = lax.rem(place.me + k, place.fsdp)
        remote(
            gain_terms.at[to], gain_slots.at[place.me], gain_sems.at[0], gain_sems.at[1], fsdp=to
        ).start()
        return 0

    lax.fori_loop(1, place.fsdp, send_gain, 0)
    gain_slots[place.me] = gain_terms[place.me]
    scatter.drain()
    load_sums = pltpu.make_async_copy(sums, terms, load_sems.at[0])
    load_sums.start()
    out.exchange()
    gate.widen()
    qkv.total()
    qkv_spread.start()
    await_bytes(gain_slots.at[pl.ds(0, place.fsdp - 1)], gain_sems.at[1])
    gain_sums[place.replica] = jnp.sum(gain_slots[...], axis=0)

    def send_sum(k, _):
        ref = gain_sums.at[place.replica]
        to = lax.rem(place.replica + k, place.replicas)
        remote(ref, ref, gain_sems.at[2], gain_sems.at[3], replica=to).start()
        return 0

    lax.fori_loop(1, place.replicas, send_sum, 0)

    load_sums.wait()
    for t in range(chips):
        scatter.side(t).start()
    up.spread()
    for t in range(chips):
        scatter.cross(t)
    scatter.step(1)
    out.total()
    out_spread.start()
    out_spread.spread()
    qkv_spread.spread()
    up.widen()
    for step in range(2, chips):
        scatter.step(step)
    out_spread.widen()
    scatter.finish(summed)
    outputs[...] = (summed[...] + after_attn[...]).astype(outputs.dtype)
    qkv_spread.widen()
    await_bytes(gain_sums.at[pl.ds(0, place.replicas - 1)], gain_sems.at[3])
    gain_out[...] = jnp.sum(gain_sums[...], axis=0)
    await_bytes(gain_slots.at[pl.ds(0, place.fsdp - 1)], gain_sems.at[0])
    await_bytes(gain_sums.at[pl.ds(0, place.replicas - 1)], gain_sems.at[2])
    scatter.drain()
    qkv.drain()
    out.drain()
    for spread in (down, gate, up, out_spread, qkv_spread):
        spread.finish()


def back(
    tokens,
    gains,
    grad_after,
    gain_terms,
    after_attn,
    sums,
    sum_down,
    sum_gate,
    sum_up,
    branch,
    lowered_one,
    slab_qkv,
    attended,
    grads,
):
    fsdp, replicas = lax.axis_size("fsdp"), lax.axis_size("replica")
    chips, high, wide = fsdp // 2, 2, replicas // 2
    block, model = tokens.shape
    rows, width = attended.shape
    share = gains.shape[2]
    low, full = jnp.bfloat16, jnp.float32
    hbm, vmem = pl.BlockSpec(memory_space=pl.ANY), pl.BlockSpec(memory_space=pltpu.VMEM)
    shape = jax.ShapeDtypeStruct
    thin = share // replicas
    columns = sum_gate.shape[-1]
    qkv_piece = (fsdp, high, wide, thin, 3 * width)
    out_piece = (2, high, wide, width // replicas, model // 2)
    dma = pltpu.SemaphoreType.DMA
    return pl.pallas_call(
        back_kernel,
        in_specs=[vmem, vmem, hbm, vmem] + [hbm] * 10,
        out_specs=[vmem] * 3 + [hbm] * 5,
        out_shape=[
            shape((block, model), low),
            shape((block, model), full),
            shape((8, share), full),
            shape((2, high, wide) + sum_down.shape[1:], low),
            shape((1, high, wide, thin, fsdp * columns), low),
            shape((1, high, wide, thin, fsdp * columns), low),
            shape((3, high, wide, thin, fsdp * width), low),
            shape(out_piece, low),
        ],
        scratch_shapes=[
            pltpu.VMEM((block, model), full),
            pltpu.VMEM((block, model), full),
            pltpu.VMEM(slab_qkv.shape, low),
            pltpu.VMEM((rows, width), low),
            pltpu.VMEM((rows, 3 * width), low),
            pltpu.VMEM((rows, model), low),
            pltpu.VMEM((chips * block, model), low),
            pltpu.VMEM((chips + 1, block, model), low),
            pltpu.VMEM((rows, model), low),
            pltpu.VMEM((block, model), full),
            pltpu.VMEM((fsdp, 8, share), full),
            pltpu.VMEM((fsdp, 8, share), full),
            pltpu.VMEM((replicas, 8, share), full),
            dma((4,)),
            dma((7,)),
        ]
        + scatter_sems(chips)
        + spread_sems() * 5
        + reduce_scratch(*qkv_piece)
        + reduce_scratch(*out_piece),
        compiler_params=pltpu.CompilerParams(
            collective_id=2, has_side_effects=True, vmem_limit_bytes=VMEM_LIMIT
        ),
        name="back",
    )(
        tokens,
        gains,
        grad_after,
        gain_terms,
        after_attn,
        sums,
        sum_down,
        sum_gate,
        sum_up,
        branch,
        lowered_one,
        slab_qkv,
        attended,
        grads,
    )


def widen_kernel(
    down,
    gate,
    up,
    qkv,
    out,
    outputs_in,
    tokens_in,
    gains,
    w_down,
    w_gate,
    w_up,
    w_query,
    w_key,
    w_value,
    w_out,
    outputs,
    grad_tokens,
    gain_one,
    gain_two,
):
    w_down[...] = down[...].astype(jnp.float32)
    w_gate[...] = gate[...].astype(jnp.float32)
    w_up[...] = up[...].astype(jnp.float32)
    for i, ref in enumerate((w_query, w_key, w_value)):
        ref[...] = qkv[i].astype(jnp.float32)
    half = out.shape[2]
    for i in range(2):
        w_out[:, i * half : (i + 1) * half] = out[i].astype(jnp.float32)
    outputs[...] = outputs_in[...]
    grad_tokens[...] = tokens_in[...]
    gain_one[...] = gains[0, :]
    gain_two[...] = gains[1, :]


def widen(down, gate, up, qkv, out, outputs, grad_tokens, gains):
    steps = min(16, gate.shape[0] // 16)
    token_steps = outputs.shape[0] // 16
    full = jnp.float32

    def rows(array):
        return pl.BlockSpec((array.shape[0] // steps, array.shape[1]), lambda i: (i, 0))

    def tokens(array):
        return pl.BlockSpec(
            (array.shape[0] // token_steps, array.shape[1]), lambda i: (jnp.minimum(i, token_steps - 1), 0)
        )

    def stacked(array):
        return pl.BlockSpec((array.shape[0], array.shape[1] // steps, array.shape[2]), lambda i: (0, i, 0))

    like = [down, gate, up, qkv[0], qkv[0], qkv[0]]
    shapes = [jax.ShapeDtypeStruct(array.shape, full) for array in like]
    shapes.append(jax.ShapeDtypeStruct((out.shape[1], 2 * out.shape[2]), full))
    row = jax.ShapeDtypeStruct(gains.shape[1:], full)
    whole = pl.BlockSpec(gains.shape, lambda i: (0, 0))
    line = pl.BlockSpec(gains.shape[1:], lambda i: (0,))
    return pl.pallas_call(
        widen_kernel,
        grid=(steps,),
        in_specs=[rows(down), rows(gate), rows(up), stacked(qkv), stacked(out)]
        + [tokens(outputs), tokens(grad_tokens), whole],
        out_specs=[rows(shape) for shape in shapes]
        + [tokens(outputs), tokens(grad_tokens), line, line],
        out_shape=shapes
        + [jax.ShapeDtypeStruct(array.shape, array.dtype) for array in (outputs, grad_tokens)]
        + [row, row],
        compiler_params=pltpu.CompilerParams(vmem_limit_bytes=VMEM_LIMIT),
        name="widen",
    )(down, gate, up, qkv, out, outputs, grad_tokens, gains)


def local(
    tokens, attn_gain, w_query, w_key, w_value, w_out, ffn_gain, w_gate, w_up, w_down, cotangent
):
    cosine, sine = rope_tables(tokens.shape[0] * lax.axis_size("fsdp"))
    (
        lowered_one,
        lowered_two,
        cotangents,
        slab_qkv,
        hidden,
        grad_gate,
        grad_up,
        terms,
        sums,
        queries,
        keys,
        values,
        attended,
        logs,
        after_attn,
        gains,
    ) = front(
        tokens,
        cotangent,
        attn_gain,
        ffn_gain,
        w_query,
        w_key,
        w_value,
        w_out,
        w_gate,
        w_up,
        w_down,
        cosine,
        sine,
    )
    gain_terms, grad_after, grads, branch, sum_down, sum_gate, sum_up = weigh(
        cotangent,
        after_attn,
        gains,
        terms,
        lowered_two,
        cotangents,
        hidden,
        grad_gate,
        grad_up,
        w_out,
        queries,
        keys,
        values,
        logs,
        cosine,
        sine,
    )
    outputs, grad_tokens, gain_grads, low_down, low_gate, low_up, low_qkv, low_out = back(
        tokens,
        gains,
        grad_after,
        gain_terms,
        after_attn,
        sums,
        sum_down,
        sum_gate,
        sum_up,
        branch,
        lowered_one,
        slab_qkv,
        attended,
        grads,
    )
    (
        grad_w_down,
        grad_w_gate,
        grad_w_up,
        grad_w_query,
        grad_w_key,
        grad_w_value,
        grad_w_out,
        outputs,
        grad_tokens,
        grad_attn_gain,
        grad_ffn_gain,
    ) = widen(
        low_down.reshape(w_down.shape),
        low_gate.reshape(w_gate.shape),
        low_up.reshape(w_up.shape),
        low_qkv.reshape((3,) + w_query.shape),
        low_out.reshape(2, w_out.shape[0], -1),
        outputs,
        grad_tokens,
        gain_grads,
    )
    return (
        outputs,
        grad_tokens,
        grad_attn_gain,
        grad_w_query,
        grad_w_key,
        grad_w_value,
        grad_w_out,
        grad_ffn_gain,
        grad_w_gate,
        grad_w_up,
        grad_w_down,
    )


def solution(mesh):
    rows = P("fsdp", None)
    tokens = P(("replica", "fsdp"), None)
    gain = P("fsdp")
    return jax.shard_map(
        local,
        mesh=mesh,
        in_specs=(tokens, gain, rows, rows, rows, rows, gain, rows, rows, rows, tokens),
        out_specs=(tokens, tokens, gain, rows, rows, rows, rows, gain, rows, rows, rows),
        check_vma=False,
    )
```

```python
import functools

import jax
import jax.numpy as jnp
import numpy as np
from jax import lax
from jax.experimental import pallas as pl
from jax.experimental.pallas import tpu as pltpu
from jax.sharding import PartitionSpec as P

HEAD_DIM = 64

eps_norm = 1e-05
rope_base = 130000.0
masked_score = -1e30


def rope_tables(row_count):
    lane = np.arange(2 * HEAD_DIM) % HEAD_DIM
    halfway = HEAD_DIM // 2
    spacing = ((lane % halfway) * np.float32(2.0) / HEAD_DIM).astype(np.float32)
    frequency = np.power(np.float32(rope_base), -spacing)
    angles = np.arange(row_count, dtype=np.float32)[:, None] * frequency[None, :]
    sign = np.where(lane < halfway, -1.0, 1.0).astype(np.float32)
    return np.cos(angles).astype(np.float32), (np.sin(angles) * sign[None, :]).astype(np.float32)


def dot(left, right):
    return jnp.dot(left, right, preferred_element_type=jnp.float32)


def contract_last(left, right):
    return lax.dot_general(
        left, right, (((1,), (1,)), ((), ())), preferred_element_type=jnp.float32
    )


def contract_first(left, right):
    return lax.dot_general(
        left, right, (((0,), (0,)), ((), ())), preferred_element_type=jnp.float32
    )


def scores_of(queries, keys, first_row):
    rows, columns = queries.shape[0], keys.shape[0]
    scores = contract_last(queries, keys) * HEAD_DIM**-0.5
    at_row = lax.broadcasted_iota(jnp.int32, (rows, columns), 0) + first_row
    at_column = lax.broadcasted_iota(jnp.int32, (rows, columns), 1)
    return jnp.where(at_column <= at_row, scores, masked_score)


MESH = pl.DeviceIdType.MESH
VMEM_LIMIT = 61 * 2**20


def remote(src, dst, send, recv, **where):
    return pltpu.make_async_remote_copy(
        src_ref=src, dst_ref=dst, send_sem=send, recv_sem=recv, device_id=where, device_id_type=MESH
    )


def await_bytes(ref, sem):
    pltpu.make_async_copy(ref, ref, sem).wait()


def rows_at(ref, index, size):
    return ref.at[pl.ds(pl.multiple_of(index * size, size), size)]


class Place:
    def __init__(self):
        self.fsdp, self.replicas = lax.axis_size("fsdp"), lax.axis_size("replica")
        self.me, self.replica = lax.axis_index("fsdp"), lax.axis_index("replica")
        self.chips = self.fsdp // 2
        self.chip, self.core = self.me // 2, self.me % 2
        self.sibling = self.me + 1 - 2 * self.core
        self.high, self.wide = 2, self.replicas // 2
        self.a, self.b = self.replica // self.wide, self.replica % self.wide
        self.counts = ((self.wide, self.high), (self.high, self.wide))
        self.above = self.chip + 1 < self.chips
        self.below = self.chip >= 1

    def peer(self, half, stage, k):
        if half == stage:
            to = lax.rem(self.b + k, self.wide)
            return to, self.a * self.wide + to
        to = lax.rem(self.a + k, self.high)
        return to, to * self.wide + self.b

    def nearest(self, k):
        found = jnp.int32(0)
        for chip in range(self.chips):
            order = sorted(range(self.chips), key=lambda other, chip=chip: (abs(other - chip), other))
            found = found + jnp.where(self.chip == chip, order[k], 0)
        return found

    def enter(self):
        barrier = pltpu.get_barrier_semaphore()

        def greet(k, _):
            to = lax.rem(self.me + k, self.fsdp)
            pl.semaphore_signal(barrier, inc=1, device_id={"fsdp": to}, device_id_type=MESH)
            return 0

        def greet_replica(k, _):
            to = lax.rem(self.replica + k, self.replicas)
            pl.semaphore_signal(barrier, inc=1, device_id={"replica": to}, device_id_type=MESH)
            return 0

        lax.fori_loop(1, self.fsdp, greet, 0)
        lax.fori_loop(1, self.replicas, greet_replica, 0)
        pl.semaphore_wait(barrier, self.fsdp - 1 + self.replicas - 1)


def line_sems(chips):
    return [pltpu.SemaphoreType.DMA((chips,))] * 6


class Gather:
    def __init__(self, place, buf, block, sems, own=None):
        self.p, self.buf, self.block, self.own = place, buf, block, own
        self.up_out, self.up_in, self.down_out, self.down_in, self.side_out, self.side_in = sems

    def held(self, chip):
        return rows_at(self.buf, 2 * chip + self.p.core, self.block)

    def up(self, step):
        ref = self.held(self.p.chip - step + 1)
        src = self.own if step == 1 and self.own is not None else ref
        return remote(src, ref, self.up_out.at[step], self.up_in.at[step], fsdp=self.p.me + 2)

    def down(self, step):
        ref = self.held(self.p.chip + step - 1)
        src = self.own if step == 1 and self.own is not None else ref
        return remote(src, ref, self.down_out.at[step], self.down_in.at[step], fsdp=self.p.me - 2)

    def side(self, chip, src=None):
        ref = self.held(chip)
        src = ref if src is None else src
        return remote(src, ref, self.side_out.at[chip], self.side_in.at[chip], fsdp=self.p.sibling)

    def start(self):
        p = self.p
        pl.when(p.above)(lambda: self.up(1).start())
        pl.when(p.below)(lambda: self.down(1).start())
        self.side(p.chip, self.own).start()

    def step(self, step):
        p = self.p
        from_below, from_above = p.chip - step, p.chip + step

        @pl.when(from_below >= 0)
        def _():
            await_bytes(self.held(from_below), self.up_in.at[step])
            if step + 1 < p.chips:
                pl.when(p.above)(lambda: self.up(step + 1).start())
            self.side(from_below).start()

        @pl.when(from_above < p.chips)
        def _():
            await_bytes(self.held(from_above), self.down_in.at[step])
            if step + 1 < p.chips:
                pl.when(p.below)(lambda: self.down(step + 1).start())
            self.side(from_above).start()

    def across(self, chip):
        await_bytes(rows_at(self.buf, 2 * chip + 1 - self.p.core, self.block), self.side_in.at[chip])

    def drain(self):
        p = self.p
        for step in range(1, p.chips):
            pl.when(jnp.logical_and(p.above, p.chip - step + 1 >= 0))(
                lambda step=step: self.up(step).wait_send()
            )
            pl.when(jnp.logical_and(p.below, p.chip + step - 1 < p.chips))(
                lambda step=step: self.down(step).wait_send()
            )
        for chip in range(p.chips):
            self.side(chip).wait_send()

    def finish(self):
        for chip in range(self.p.chips):
            self.across(chip)
        self.drain()


class Scatter:
    def __init__(self, place, terms, across, slots, block, sems):
        self.p, self.terms, self.across, self.slots, self.block = place, terms, across, slots, block
        self.up_out, self.up_in, self.down_out, self.down_in, self.side_out, self.side_in = sems

    def side(self, chip):
        p = self.p
        return remote(
            rows_at(self.terms, 2 * chip + 1 - p.core, self.block),
            rows_at(self.across, chip, self.block),
            self.side_out.at[chip],
            self.side_in.at[chip],
            fsdp=p.sibling,
        )

    def term(self, chip):
        return rows_at(self.terms, 2 * chip + self.p.core, self.block)

    def up(self, step):
        return remote(
            self.term(self.p.chips - step + self.p.chip),
            self.slots.at[step - self.p.chip - 1],
            self.up_out.at[step],
            self.up_in.at[step],
            fsdp=self.p.me + 2,
        )

    def down(self, step):
        return remote(
            self.term(self.p.chip - self.p.chips + step),
            self.slots.at[step + 1],
            self.down_out.at[step],
            self.down_in.at[step],
            fsdp=self.p.me - 2,
        )

    def add(self, chip, arrived):
        term = self.term(chip)
        term[...] = (term[...].astype(jnp.float32) + arrived[...].astype(jnp.float32)).astype(term.dtype)

    def cross(self, chip):
        arrived = rows_at(self.across, chip, self.block)
        await_bytes(arrived, self.side_in.at[chip])
        self.add(chip, arrived)

    def step(self, step):
        p = self.p
        rising, falling = p.chips - step + p.chip, p.chip - p.chips + step

        @pl.when(jnp.logical_and(p.above, rising < p.chips))
        def _():
            if step > 1:

                @pl.when(p.below)
                def _():
                    arrived = self.slots.at[step - 1 - p.chip]
                    await_bytes(arrived, self.up_in.at[step - 1])
                    self.add(rising, arrived)

            self.up(step).start()

        @pl.when(jnp.logical_and(p.below, falling >= 0))
        def _():
            if step > 1:

                @pl.when(p.above)
                def _():
                    arrived = self.slots.at[step]
                    await_bytes(arrived, self.down_in.at[step - 1])
                    self.add(falling, arrived)

            self.down(step).start()

    def finish(self, total):
        p, last = self.p, self.p.chips - 1
        total[...] = self.term(p.chip)[...].astype(jnp.float32)

        @pl.when(p.below)
        def _():
            await_bytes(self.slots.at[last - p.chip], self.up_in.at[last])
            total[...] += self.slots[last - p.chip].astype(jnp.float32)

        @pl.when(p.above)
        def _():
            await_bytes(self.slots.at[last + 1], self.down_in.at[last])
            total[...] += self.slots[last + 1].astype(jnp.float32)

    def drain(self):
        p = self.p
        for step in range(1, p.chips):
            pl.when(jnp.logical_and(p.above, p.chips - step + p.chip < p.chips))(
                lambda step=step: self.up(step).wait_send()
            )
            pl.when(jnp.logical_and(p.below, p.chip - p.chips + step >= 0))(
                lambda step=step: self.down(step).wait_send()
            )
        for chip in range(p.chips):
            self.side(chip).wait_send()


def scatter_sems(chips):
    dma = pltpu.SemaphoreType.DMA
    return [dma((chips,))] * 6


class Turn:
    def __init__(self, place, weight, slab, first, sems):
        self.p, self.weight, self.slab, self.first = place, weight, slab, first
        self.far_out, self.far_in, self.near_out, self.near_in, self.own, self.passing = sems
        self.height, self.width = weight.shape[0], slab.shape[1]
        self.share = self.height // place.replicas

    def far_rows(self):
        return (self.p.fsdp - 2) * self.share

    def piece(self, block, share):
        at = self.first + block * self.height + share * self.share
        return self.slab.at[pl.ds(pl.multiple_of(at, self.share), self.share)]

    def whole(self, block):
        at = self.first + block * self.height
        return self.slab.at[pl.ds(pl.multiple_of(at, self.height), self.height)]

    def columns(self, to):
        return pl.ds(pl.multiple_of(to * self.width, self.width), self.width)

    def start(self):
        p = self.p

        def send(k, _):
            to = lax.rem(2 * p.chip + 2 + k, p.fsdp)
            share = pl.ds(pl.multiple_of(p.replica * self.share, self.share), self.share)
            remote(
                self.weight.at[share, self.columns(to)],
                self.piece(p.me, p.replica),
                self.far_out,
                self.far_in,
                fsdp=to,
            ).start()
            return 0

        lax.fori_loop(0, p.fsdp - 2, send, 0)
        self.near().start()
        self.mine().start()

    def near(self):
        p = self.p
        return remote(
            self.weight.at[:, self.columns(p.sibling)], self.whole(p.me), self.near_out, self.near_in, fsdp=p.sibling
        )

    def mine(self):
        return pltpu.make_async_copy(self.weight.at[:, self.columns(self.p.me)], self.whole(self.p.me), self.own)

    def await_far(self):
        await_bytes(self.slab.at[pl.ds(0, self.far_rows())], self.far_in)

    def bytes_of(self, pieces):
        return self.slab.at[pl.ds(0, pieces * self.share)]

    def pass_bytes(self, half, stage):
        first, second = self.p.counts[half]
        return self.bytes_of((self.p.chips - 1) * (second - 1 if stage == 0 else second * (first - 1)))

    def send_pieces(self, half, stage, shares):
        p = self.p

        def one(i, _):
            block = lax.rem(2 * p.chip + 2 + 2 * i + half, p.fsdp)
            for share in shares:
                ref = self.piece(block, share)
                for k in range(1, p.counts[half][1 - stage]):
                    _, replica = p.peer(half, 1 - stage, k)
                    remote(
                        ref,
                        ref,
                        self.passing.at[half, 2 * stage],
                        self.passing.at[half, 2 * stage + 1],
                        replica=replica,
                    ).start()
            return 0

        lax.fori_loop(0, p.chips - 1, one, 0)

    def pass_on(self):
        for half in range(2):
            self.send_pieces(half, 0, [self.p.replica])

    def pass_far(self):
        p = self.p
        for half in range(2):
            await_bytes(self.pass_bytes(half, 0), self.passing.at[half, 1])
            if half == 0:
                shares = [a * p.wide + p.b for a in range(p.high)]
            else:
                shares = [p.a * p.wide + b for b in range(p.wide)]
            self.send_pieces(half, 1, shares)

    def finish(self):
        for half in range(2):
            await_bytes(self.pass_bytes(half, 1), self.passing.at[half, 3])
        await_bytes(self.whole(self.p.sibling), self.near_in)
        self.mine().wait()

    def drain(self):
        await_bytes(self.slab.at[pl.ds(0, self.far_rows())], self.far_out)
        self.near().wait_send()
        for half in range(2):
            await_bytes(self.pass_bytes(half, 0), self.passing.at[half, 0])
            await_bytes(self.pass_bytes(half, 1), self.passing.at[half, 2])


def turn_sems():
    return [pltpu.SemaphoreType.DMA(())] * 5 + [pltpu.SemaphoreType.DMA((2, 4))]


def partner(values):
    halfway = HEAD_DIM // 2
    width = values.shape[1]
    lane = lax.broadcasted_iota(jnp.int32, values.shape, 1) % HEAD_DIM
    return jnp.where(
        lane < halfway,
        pltpu.roll(values, width - halfway, axis=1),
        pltpu.roll(values, halfway, axis=1),
    )


def front_kernel(
    tokens,
    cotangent,
    gain_one,
    gain_two,
    w_query,
    w_key,
    w_value,
    w_out,
    w_gate,
    w_up,
    w_down,
    cosine,
    sine,
    lowered_one,
    lowered_two_out,
    cotangents,
    slab_qkv_out,
    hidden_out,
    grad_gate_out,
    grad_up_out,
    terms_out,
    queries,
    keys,
    values,
    attended,
    logs,
    after_attn,
    gains,
    low,
    tiles,
    lowered_two,
    slab_qkv,
    slab_gate,
    slab_up,
    held_down,
    terms,
    across,
    slots,
    tile_hidden,
    tile_gate,
    tile_up,
    tile_terms,
    grad_hiddens,
    gain_rows,
    gain_out,
    gain_in,
    copy_sems,
    load_sems,
    store_sems,
    *sems,
):
    place = Place()
    chips, block = place.chips, tokens.shape[0]
    model, width = tokens.shape[1], queries.shape[1]
    share = gain_one.shape[0]
    tile = 2 * block
    one_at, cot_at, two_at, scatter_at = sems[:6], sems[6:12], sems[12:18], sems[18:24]
    turn_at = [sems[24 + 6 * i : 30 + 6 * i] for i in range(5)]
    turns = [
        Turn(place, weight, slab_qkv, i * model, turn_at[i])
        for i, weight in enumerate((w_query, w_key, w_value))
    ]
    turn_gate = Turn(place, w_gate, slab_gate, 0, turn_at[3])
    turn_up = Turn(place, w_up, slab_up, 0, turn_at[4])
    here = pl.ds(pl.multiple_of(place.me * block, block), block)

    gain_rows[...] = jnp.zeros_like(gain_rows)
    gain_rows[0, :] = gain_one[...].astype(jnp.float32)
    gain_rows[1, :] = gain_two[...].astype(jnp.float32)
    load_down = pltpu.make_async_copy(w_down, held_down, copy_sems.at[0])
    load_down.start()
    keep_cot = pltpu.make_async_copy(cotangent, cotangents.at[here], copy_sems.at[1])
    keep_cot.start()
    place.enter()

    def send_gains(k, _):
        to = lax.rem(place.me + k, place.fsdp)
        remote(gain_rows, gains.at[place.me], gain_out, gain_in, fsdp=to).start()
        return 0

    lax.fori_loop(1, place.fsdp, send_gains, 0)
    for turn in turns:
        turn.start()
    gains[place.me] = gain_rows[...]
    inputs = tokens[...].astype(jnp.float32)
    factor = lax.rsqrt(jnp.mean(inputs * inputs, axis=-1, keepdims=True) + eps_norm)
    await_bytes(gains.at[pl.ds(0, place.fsdp - 1)], gain_in)
    for j in range(model // share):
        at = pl.ds(j * share, share)
        normed = tokens[:, at].astype(jnp.float32) * factor
        low[:, at] = (normed * gains[j, 0:1, :]).astype(jnp.bfloat16)
    first = Gather(place, lowered_one, block, one_at, low)
    first.start()
    keep_low = pltpu.make_async_copy(low, lowered_one.at[here], copy_sems.at[2])
    keep_low.start()
    for turn in turns:
        turn.await_far()
        turn.pass_on()
    for step in range(1, chips):
        if step == chips - 1:
            turn_gate.start()
        first.step(step)
        if step == 1:
            for turn in turns:
                turn.pass_far()
    turn_up.start()
    third = Gather(place, cotangents, block, cot_at, cotangent)
    third.start()
    keep_low.wait()
    first.finish()

    def load(source, t, slot):
        return pltpu.make_async_copy(rows_at(source, t, tile), tiles.at[slot], load_sems.at[slot])

    load(lowered_one, 0, 0).start()
    for turn in turns:
        turn.finish()
    keep_slab = pltpu.make_async_copy(slab_qkv, slab_qkv_out, copy_sems.at[3])
    keep_slab.start()
    for t in range(chips):
        if t + 1 < chips:
            load(lowered_one, t + 1, (t + 1) % 2).start()
        load(lowered_one, t, t % 2).wait()
        at = pl.ds(t * tile, tile)
        for i, ref in enumerate((queries, keys, values)):
            out = dot(tiles[t % 2], slab_qkv[i * model : (i + 1) * model, :])
            if i < 2:
                for j in range(0, width, 2 * HEAD_DIM):
                    pair = out[:, j : j + 2 * HEAD_DIM]
                    pair = pair * cosine[at, :] + partner(pair) * sine[at, :]
                    ref[at, j : j + 2 * HEAD_DIM] = pair.astype(jnp.bfloat16)
            else:
                ref[at, :] = out.astype(jnp.bfloat16)
    scatter = Scatter(place, terms, across, slots, block, scatter_at)
    pair = 2 * HEAD_DIM
    for t in range(chips):
        here_t, seen = pl.ds(t * tile, tile), pl.ds(0, (t + 1) * tile)

        def heads(h, _, t=t, here_t=here_t, seen=seen):
            lanes = pl.ds(pl.multiple_of(h * pair, pair), pair)
            q2, k2, v2 = queries[here_t, lanes], keys[seen, lanes], values[seen, lanes]
            mixed, stats = [], []
            for at in (0, HEAD_DIM):
                head = slice(at, at + HEAD_DIM)
                scores = scores_of(q2[:, head], k2[:, head], t * tile)
                most = jnp.max(scores, axis=-1, keepdims=True)
                weights = jnp.exp(scores - most)
                total = jnp.sum(weights, axis=-1, keepdims=True)
                mixed.append(dot((weights / total).astype(jnp.bfloat16), v2[:, head]))
                stats.append(jnp.broadcast_to(most + jnp.log(total), (tile, HEAD_DIM)))
            attended[here_t, lanes] = jnp.concatenate(mixed, axis=1).astype(jnp.bfloat16)
            logs[here_t, lanes] = jnp.concatenate(stats, axis=1)
            return 0

        lax.fori_loop(0, width // pair, heads, 0)
        terms[here_t, :] = dot(attended[here_t, :], w_out[...]).astype(jnp.bfloat16)
        scatter.side(t).start()
    for t in range(chips):
        scatter.cross(t)
    for step in range(1, chips):
        scatter.step(step)
        if step == 1:
            turn_gate.await_far()
            turn_gate.pass_on()
        if step < chips - 1:
            third.step(step)
        if step == 1:
            turn_gate.pass_far()
        if step == min(2, chips - 1):
            turn_up.await_far()
            turn_up.pass_on()
        if step == chips - 1:
            turn_up.pass_far()
    scatter.finish(after_attn)
    after_attn[...] += tokens[...].astype(jnp.float32)
    after = after_attn[...]
    factor = lax.rsqrt(jnp.mean(after * after, axis=-1, keepdims=True) + eps_norm)
    for j in range(model // share):
        at = pl.ds(j * share, share)
        normed = after_attn[:, at] * factor
        lowered_two[here, at] = (normed * gains[j, 1:2, :]).astype(jnp.bfloat16)
    second = Gather(place, lowered_two, block, two_at)
    second.start()
    third.step(chips - 1)
    keep_cot.wait()
    third.finish()
    load(cotangents, place.nearest(0), 0).start()
    load_down.wait()
    for k in range(chips):
        if k + 1 < chips:
            load(cotangents, place.nearest(k + 1), (k + 1) % 2).start()
        load(cotangents, place.nearest(k), k % 2).wait()
        grad_hiddens[k] = contract_last(tiles[k % 2], held_down[...])
    turn_gate.finish()
    turn_up.finish()

    def stores(k, t):
        slot = k % 2
        pairs = (
            (tile_hidden, hidden_out),
            (tile_gate, grad_gate_out),
            (tile_up, grad_up_out),
            (tile_terms, terms_out),
        )
        return [
            pltpu.make_async_copy(held.at[slot], rows_at(out, t, tile), store_sems.at[i, slot])
            for i, (held, out) in enumerate(pairs)
        ]

    for k in range(chips):
        t, slot = place.nearest(k), k % 2
        if k > 0:
            second.step(k)
        second.across(t)
        if k > 1:
            for store in stores(k - 2, place.nearest(k - 2)):
                store.wait()
        rows = lowered_two[pl.ds(pl.multiple_of(t * tile, tile), tile), :]
        gate = dot(rows, slab_gate[...])
        up = dot(rows, slab_up[...])
        grad_hidden = grad_hiddens[k]
        sigmoid = jax.nn.sigmoid(gate)
        silu = gate * sigmoid
        hidden = (silu * up).astype(jnp.bfloat16)
        grad_gate = (grad_hidden * up * sigmoid * (1.0 + gate * (1.0 - sigmoid))).astype(jnp.bfloat16)
        grad_up = (grad_hidden * silu).astype(jnp.bfloat16)
        tile_hidden[slot] = hidden
        tile_gate[slot] = grad_gate
        tile_up[slot] = grad_up
        got = contract_last(grad_gate, slab_gate[...]) + contract_last(grad_up, slab_up[...])
        tile_terms[slot] = got.astype(jnp.bfloat16)
        for store in stores(k, t):
            store.start()
    keep_two = pltpu.make_async_copy(lowered_two, lowered_two_out, copy_sems.at[4])
    keep_two.start()
    second.drain()
    scatter.drain()
    for turn in turns + [turn_gate, turn_up]:
        turn.drain()
    await_bytes(gains.at[pl.ds(0, place.fsdp - 1)], gain_out)
    keep_slab.wait()
    for k in range(max(chips - 2, 0), chips):
        for store in stores(k, place.nearest(k)):
            store.wait()
    keep_two.wait()


def front(
    tokens, cotangent, gain_one, gain_two, w_query, w_key, w_value, w_out, w_gate, w_up, w_down, cosine, sine
):
    fsdp = lax.axis_size("fsdp")
    chips = fsdp // 2
    block, model = tokens.shape
    rows, width, wide = fsdp * block, w_query.shape[1] // fsdp, w_gate.shape[1] // fsdp
    tile = 2 * block
    share = gain_one.shape[0]
    low, full = jnp.bfloat16, jnp.float32
    hbm, vmem = pl.BlockSpec(memory_space=pl.ANY), pl.BlockSpec(memory_space=pltpu.VMEM)
    shape = jax.ShapeDtypeStruct
    dma = pltpu.SemaphoreType.DMA
    return pl.pallas_call(
        front_kernel,
        in_specs=[vmem] * 4 + [hbm] * 3 + [vmem] + [hbm] * 3 + [vmem] * 2,
        out_specs=[hbm] * 8 + [vmem] * 7,
        out_shape=[
            shape((rows, model), low),
            shape((rows, model), low),
            shape((rows, model), low),
            shape((3 * model, width), low),
            shape((rows, wide), low),
            shape((rows, wide), low),
            shape((rows, wide), low),
            shape((rows, model), low),
            shape((rows, width), low),
            shape((rows, width), low),
            shape((rows, width), low),
            shape((rows, width), low),
            shape((rows, width), full),
            shape((block, model), full),
            shape((fsdp, 8, share), full),
        ],
        scratch_shapes=[
            pltpu.VMEM((block, model), low),
            pltpu.VMEM((2, tile, model), low),
            pltpu.VMEM((rows, model), low),
            pltpu.VMEM((3 * model, width), low),
            pltpu.VMEM((model, wide), low),
            pltpu.VMEM((model, wide), low),
            pltpu.VMEM((wide, model), low),
            pltpu.VMEM((rows, model), low),
            pltpu.VMEM((chips * block, model), low),
            pltpu.VMEM((chips + 1, block, model), low),
            pltpu.VMEM((2, tile, wide), low),
            pltpu.VMEM((2, tile, wide), low),
            pltpu.VMEM((2, tile, wide), low),
            pltpu.VMEM((2, tile, model), low),
            pltpu.VMEM((chips, tile, wide), full),
            pltpu.VMEM((8, share), full),
            dma(()),
            dma(()),
            dma((5,)),
            dma((2,)),
            dma((5, 2)),
        ]
        + line_sems(chips) * 3
        + scatter_sems(chips)
        + turn_sems() * 5,
        compiler_params=pltpu.CompilerParams(
            collective_id=0, has_side_effects=True, vmem_limit_bytes=VMEM_LIMIT
        ),
        name="front",
    )(
        tokens,
        cotangent,
        gain_one,
        gain_two,
        w_query,
        w_key,
        w_value,
        w_out,
        w_gate,
        w_up,
        w_down,
        cosine,
        sine,
    )


class Reduce:
    def __init__(self, place, part, first, second, sems):
        self.p, self.part, self.first, self.second, self.sems = place, part, first, second, sems
        self.half = part.shape[0] // 2

    def rows(self, half):
        return pl.ds(half * self.half, self.half)

    def sent(self, half, to):
        if half == 0:
            return self.part.at[self.rows(0), :, to]
        return self.part.at[self.rows(1), to]

    def own(self, half):
        return self.sent(half, self.p.b if half == 0 else self.p.a)

    def start(self, half):
        for k in range(1, self.p.counts[half][0]):
            to, replica = self.p.peer(half, 0, k)
            remote(
                self.sent(half, to),
                self.first[half].at[k - 1],
                self.sems.at[half, 0],
                self.sems.at[half, 1],
                replica=replica,
            ).start()

    def exchange(self):
        for half in range(2):
            own, arrived = self.own(half), self.first[half]
            await_bytes(arrived, self.sems.at[half, 1])

            def add(n, _, own=own, arrived=arrived):
                for m in range(own.shape[1]):
                    total = own[n, m].astype(jnp.float32)
                    for k in range(arrived.shape[0]):
                        total += arrived[k, n, m].astype(jnp.float32)
                    own[n, m] = total.astype(own.dtype)
                return 0

            lax.fori_loop(0, self.half, add, 0)
            for k in range(1, self.p.counts[half][1]):
                to, replica = self.p.peer(half, 1, k)
                remote(
                    own.at[:, to],
                    self.second[half].at[k - 1],
                    self.sems.at[half, 2],
                    self.sems.at[half, 3],
                    replica=replica,
                ).start()

    def total(self):
        for half in range(2):
            own, arrived = self.held(half), self.second[half]
            await_bytes(arrived, self.sems.at[half, 3])

            def add(n, _, own=own, arrived=arrived):
                total = own[n].astype(jnp.float32)
                for k in range(arrived.shape[0]):
                    total += arrived[k, n].astype(jnp.float32)
                own[n] = total.astype(own.dtype)
                return 0

            lax.fori_loop(0, self.half, add, 0)

    def held(self, half):
        return self.part.at[self.rows(half), self.p.a, self.p.b]

    def piece(self, n):
        return self.part.at[n, self.p.a, self.p.b]

    def drain(self):
        for half in range(2):
            await_bytes(self.first[half], self.sems.at[half, 0])
            await_bytes(self.second[half], self.sems.at[half, 2])


def reduce_scratch(n, high, wide, rows, columns):
    low = functools.partial(pltpu.VMEM, dtype=jnp.bfloat16)
    half = n // 2
    return [
        low((n, high, wide, rows, columns)),
        low((wide - 1, half, high, rows, columns)),
        low((high - 1, half, wide, rows, columns)),
        low((high - 1, half, rows, columns)),
        low((wide - 1, half, rows, columns)),
        pltpu.SemaphoreType.DMA((2, 4)),
    ]


def reducer(place, refs):
    part, first_a, first_b, second_a, second_b, sems = refs
    return Reduce(place, part, (first_a, first_b), (second_a, second_b), sems)


class Spread:
    def __init__(self, place, piece, out, sems, turned):
        self.p, self.piece, self.out, self.sems, self.turned = place, piece, out, sems, turned

    def start(self):
        p = self.p
        if self.turned:
            count = self.out.shape[0]
            width = self.out.shape[-1] // p.fsdp
            columns = pl.ds(pl.multiple_of(p.me * width, width), width)

            def pairs(to):
                ref = self.piece(to)
                return [
                    (ref.at[:, pl.ds(i * width, width)], self.out.at[i, p.a, p.b, :, columns])
                    for i in range(count)
                ]

            def send(k, _):
                to = lax.rem(p.me + k, p.fsdp)
                for ref, target in pairs(to):
                    remote(ref, target, self.sems.at[0, 0], self.sems.at[0, 1], fsdp=to).start()
                return 0

            lax.fori_loop(1, p.fsdp, send, 0)
            for ref, target in pairs(p.me):
                pltpu.make_async_copy(ref, target, self.sems.at[0, 1]).start()
        else:
            for half in range(2):
                pltpu.make_async_copy(
                    self.piece(half), self.out.at[half, p.a, p.b], self.sems.at[half, 1]
                ).start()

    def placed(self, half, rows):
        a, b = rows
        if self.turned:
            width = self.out.shape[-1] // 2
            return self.out.at[:, a, b, :, pl.ds(half * width, width)]
        return self.out.at[half, a, b]

    def spread(self):
        p = self.p
        if self.turned:
            await_bytes(self.out.at[:, p.a, p.b], self.sems.at[0, 1])
        for half in range(2):
            ref = self.placed(half, (p.a, p.b))
            src = ref if self.turned else self.piece(half)
            for k in range(1, p.counts[half][1]):
                _, replica = p.peer(half, 1, k)
                remote(src, ref, self.sems.at[half, 2], self.sems.at[half, 3], replica=replica).start()

    def spread_bytes(self, half):
        some = pl.ds(0, self.p.counts[half][1] - 1)
        return self.placed(half, (some, 0) if half == 0 else (0, some))

    def widen(self):
        p = self.p
        for half in range(2):
            if not self.turned:
                await_bytes(self.placed(half, (p.a, p.b)), self.sems.at[half, 1])
            await_bytes(self.spread_bytes(half), self.sems.at[half, 3])
            every = pl.ds(0, p.counts[half][1])
            ref = self.placed(half, (every, p.b) if half == 0 else (p.a, every))
            for k in range(1, p.counts[half][0]):
                _, replica = p.peer(half, 0, k)
                remote(ref, ref, self.sems.at[half, 4], self.sems.at[half, 5], replica=replica).start()

    def widen_bytes(self, half):
        counts = self.p.counts[half]
        every, some = pl.ds(0, counts[1]), pl.ds(0, counts[0] - 1)
        return self.placed(half, (every, some) if half == 0 else (some, every))

    def finish(self):
        p = self.p
        for half in range(2):
            await_bytes(self.widen_bytes(half), self.sems.at[half, 5])
            await_bytes(self.spread_bytes(half), self.sems.at[half, 2])
            await_bytes(self.widen_bytes(half), self.sems.at[half, 4])
        if self.turned:
            width = self.out.shape[-1] // p.fsdp
            await_bytes(
                self.out.at[:, p.a, p.b, :, pl.ds(0, (p.fsdp - 1) * width)], self.sems.at[0, 0]
            )


def spread_sems():
    return [pltpu.SemaphoreType.DMA((2, 6))]


def norm_back(values, gain_row, gains, grad, carried, result, gain_terms):
    block, model = values.shape
    share = gains.shape[2]
    held = values[...].astype(jnp.float32)
    factor = lax.rsqrt(jnp.mean(held * held, axis=-1, keepdims=True) + eps_norm)
    dots = jnp.zeros((block, 1), jnp.float32)
    for j in range(model // share):
        at = pl.ds(j * share, share)
        normed = values[:, at].astype(jnp.float32) * factor
        product = grad[:, at] * normed
        gain_terms[j, gain_row : gain_row + 1, :] = jnp.sum(product, axis=0, keepdims=True)
        dots += jnp.sum(product * gains[j, gain_row : gain_row + 1, :], axis=-1, keepdims=True)
    dots = dots / model
    for j in range(model // share):
        at = pl.ds(j * share, share)
        normed = values[:, at].astype(jnp.float32) * factor
        scaled = grad[:, at] * gains[j, gain_row : gain_row + 1, :]
        result[:, at] = carried[:, at].astype(jnp.float32) + factor * (scaled - normed * dots)


def weigh_kernel(
    cotangent,
    after_in,
    gains,
    terms_in,
    lowered_two,
    cotangents,
    hidden_in,
    grad_gate_in,
    grad_up_in,
    w_out_in,
    queries_in,
    keys_in,
    values_in,
    logs_in,
    cosine_in,
    sine_in,
    gain_terms,
    grad_after_out,
    grads_out,
    branch,
    sum_down,
    sum_gate,
    sum_up,
    after_attn,
    w_out,
    queries,
    keys,
    values,
    logs,
    cosine,
    sine,
    grad_after,
    grads,
    tokens_held,
    hidden,
    grad_gate,
    grad_up,
    terms,
    across,
    slots,
    summed,
    low,
    grad_low,
    grad_key,
    grad_value,
    load_sems,
    store_sems,
    late_sems,
    *rest,
):
    place = Place()
    chips, block = place.chips, cotangent.shape[0]
    model = cotangent.shape[1]
    tile = 2 * block
    scatter_at, gather_at = rest[:6], rest[6:12]
    down, gate, up = [reducer(place, rest[12 + 6 * i : 18 + 6 * i]) for i in range(3)]

    def load(t):
        at = pl.ds(t * tile, tile)
        return pltpu.make_async_copy(terms_in.at[at], terms.at[at], load_sems.at[t])

    loads = [
        pltpu.make_async_copy(source, target, load_sems.at[chips + i])
        for i, (source, target) in enumerate(
            (
                (cotangents, tokens_held),
                (hidden_in, hidden),
                (grad_gate_in, grad_gate),
                (grad_up_in, grad_up),
                (lowered_two, tokens_held),
            )
        )
    ]
    for t in range(chips):
        load(t).start()
    for copy in loads[:4]:
        copy.start()
    late = [
        pltpu.make_async_copy(source, target, late_sems.at[i])
        for i, (source, target) in enumerate(
            (
                (after_in, after_attn),
                (w_out_in, w_out),
                (queries_in, queries),
                (keys_in, keys),
                (values_in, values),
                (logs_in, logs),
                (cosine_in, cosine),
                (sine_in, sine),
            )
        )
    ]
    for copy in late:
        copy.start()
    keep_after = pltpu.make_async_copy(grad_after, grad_after_out, late_sems.at[8])
    keep_grads = pltpu.make_async_copy(grads, grads_out, late_sems.at[9])
    place.enter()
    scatter = Scatter(place, terms, across, slots, block, scatter_at)
    for t in range(chips):
        load(t).wait()
        scatter.side(t).start()
    gain_terms[...] = jnp.zeros_like(gain_terms)
    loads[0].wait()
    loads[1].wait()
    _, high, wide, thin, _ = down.part.shape
    columns = min(tile, hidden.shape[1])
    for i in range(0, hidden.shape[1], columns):
        got = contract_first(hidden[:, i : i + columns], tokens_held[...]).astype(jnp.bfloat16)
        for m in range(0, columns, thin):
            n = (i + m) // thin
            down.part[n // (high * wide), n // wide % high, n % wide] = got[m : m + thin, :]
        if 2 * (i + columns) == hidden.shape[1]:
            down.start(0)
    loads[4].start()
    down.start(1)
    for t in range(chips):
        scatter.cross(t)
    scatter.step(1)
    loads[4].wait()

    def weigh(reduce, grads):
        share = model // place.fsdp

        def rows(j, _):
            left = tokens_held[:, pl.ds(pl.multiple_of(j * share, share), share)]
            got = contract_first(left, grads[...]).astype(jnp.bfloat16)
            reduce.part[j] = got.reshape(reduce.part.shape[1:])
            return 0

        for half in range(2):
            lax.fori_loop(half * chips, (half + 1) * chips, rows, 0)
            reduce.start(half)

    loads[2].wait()
    weigh(gate, grad_gate)
    if chips > 2:
        scatter.step(2)
    loads[3].wait()
    weigh(up, grad_up)
    for step in range(3, chips):
        scatter.step(step)
    scatter.finish(summed)
    late[0].wait()
    norm_back(after_attn, 1, gains, summed, cotangent, grad_after, gain_terms)
    keep_after.start()
    low[...] = grad_after[...].astype(jnp.bfloat16)
    here = pl.ds(pl.multiple_of(place.me * block, block), block)
    gather = Gather(place, branch, block, gather_at, low)
    gather.start()
    keep = pltpu.make_async_copy(low, branch.at[here], store_sems.at[0])
    keep.start()
    scatter.drain()
    down.exchange()
    for step in range(1, chips):
        gather.step(step)
        if step == 1:
            gate.exchange()
        if step == max(chips - 2, 1):
            up.exchange()
    keep.wait()
    gather.finish()
    fetch = pltpu.make_async_copy(branch, tokens_held, load_sems.at[0])
    fetch.start()
    down.total()
    fetch.wait()
    for copy in late[1:]:
        copy.wait()

    def attend_rows(t, _):
        at = pl.ds(pl.multiple_of(t * tile, tile), tile)
        grad_low[at, :] = contract_last(tokens_held[at, :], w_out[...]).astype(jnp.bfloat16)
        return 0

    lax.fori_loop(0, chips, attend_rows, 0)
    width = queries.shape[1]
    scale = HEAD_DIM**-0.5
    grad_key[...] = jnp.zeros_like(grad_key)
    grad_value[...] = jnp.zeros_like(grad_value)
    pair = 2 * HEAD_DIM
    height = tile * 1024 // max(queries.shape[0], 1024)
    for first in range(0, queries.shape[0], height):
        rows, seen = pl.ds(first, height), pl.ds(0, first + height)

        def heads(h, _, first=first, rows=rows, seen=seen):
            lanes = pl.ds(pl.multiple_of(h * pair, pair), pair)
            q2, g2, log2 = queries[rows, lanes], grad_low[rows, lanes], logs[rows, lanes]
            k2, v2 = keys[seen, lanes], values[seen, lanes]
            for_queries, for_keys, for_values = [], [], []
            for at in (0, HEAD_DIM):
                head = slice(at, at + HEAD_DIM)
                q, g, k = q2[:, head], g2[:, head], k2[:, head]
                weights = jnp.exp(scores_of(q, k, first) - log2[:, at : at + 1])
                grad_weights = contract_last(g, v2[:, head])
                delta = jnp.sum(weights * grad_weights, axis=-1, keepdims=True)
                grad_scores = (weights * (grad_weights - delta)).astype(jnp.bfloat16)
                for_queries.append(dot(grad_scores, k))
                for_keys.append(contract_first(grad_scores, q))
                for_values.append(contract_first(weights.astype(jnp.bfloat16), g))
            got = jnp.concatenate(for_queries, axis=1) * scale
            got = got * cosine[rows, :] - partner(got) * sine[rows, :]
            grads[rows, lanes] = got.astype(jnp.bfloat16)
            grad_key[seen, lanes] += jnp.concatenate(for_keys, axis=1) * scale
            grad_value[seen, lanes] += jnp.concatenate(for_values, axis=1)
            return 0

        lax.fori_loop(0, width // pair, heads, 0)

    def turn_keys(t, _):
        at = pl.ds(pl.multiple_of(t * tile, tile), tile)
        for j in range(0, width, pair):
            got = grad_key[at, j : j + pair]
            got = got * cosine[at, :] - partner(got) * sine[at, :]
            grads[at, width + j : width + j + pair] = got.astype(jnp.bfloat16)
        grads[at, 2 * width :] = grad_value[at, :].astype(jnp.bfloat16)
        return 0

    lax.fori_loop(0, chips, turn_keys, 0)
    keep_grads.start()
    stores = [keep_after, keep_grads]
    for i, (reduce, out) in enumerate(((down, sum_down), (gate, sum_gate), (up, sum_up))):
        if i > 0:
            reduce.total()
        for half in range(2):
            store = pltpu.make_async_copy(
                reduce.held(half), out.at[reduce.rows(half)], store_sems.at[1 + 2 * i + half]
            )
            store.start()
            stores.append(store)
    for reduce in (down, gate, up):
        reduce.drain()
    for store in stores:
        store.wait()


def weigh(
    cotangent,
    after_attn,
    gains,
    terms,
    lowered_two,
    cotangents,
    hidden,
    grad_gate,
    grad_up,
    w_out,
    queries,
    keys,
    values,
    logs,
    cosine,
    sine,
):
    fsdp, replicas = lax.axis_size("fsdp"), lax.axis_size("replica")
    chips, high, wide = fsdp // 2, 2, replicas // 2
    block, model = cotangent.shape
    rows, columns = hidden.shape
    width = queries.shape[1]
    share = gains.shape[2]
    low, full = jnp.bfloat16, jnp.float32
    hbm, vmem = pl.BlockSpec(memory_space=pl.ANY), pl.BlockSpec(memory_space=pltpu.VMEM)
    shape = jax.ShapeDtypeStruct
    down_piece = (2, high, wide, columns // (2 * replicas), model)
    wide_piece = (fsdp, high, wide, share // replicas, columns)
    dma = pltpu.SemaphoreType.DMA
    return pl.pallas_call(
        weigh_kernel,
        in_specs=[vmem, hbm, vmem] + [hbm] * 13,
        out_specs=[vmem] + [hbm] * 6,
        out_shape=[
            shape((fsdp, 8, share), full),
            shape((block, model), full),
            shape((rows, 3 * width), low),
            shape((rows, model), low),
            shape((2,) + down_piece[3:], low),
            shape((fsdp,) + wide_piece[3:], low),
            shape((fsdp,) + wide_piece[3:], low),
        ],
        scratch_shapes=[
            pltpu.VMEM((block, model), full),
            pltpu.VMEM(w_out.shape, low),
            pltpu.VMEM((rows, width), low),
            pltpu.VMEM((rows, width), low),
            pltpu.VMEM((rows, width), low),
            pltpu.VMEM((rows, width), full),
            pltpu.VMEM(cosine.shape, full),
            pltpu.VMEM(sine.shape, full),
            pltpu.VMEM((block, model), full),
            pltpu.VMEM((rows, 3 * width), low),
            pltpu.VMEM((rows, model), low),
            pltpu.VMEM((rows, columns), low),
            pltpu.VMEM((rows, columns), low),
            pltpu.VMEM((rows, columns), low),
            pltpu.VMEM((rows, model), low),
            pltpu.VMEM((chips * block, model), low),
            pltpu.VMEM((chips + 1, block, model), low),
            pltpu.VMEM((block, model), full),
            pltpu.VMEM((block, model), low),
            pltpu.VMEM((rows, width), low),
            pltpu.VMEM((rows, width), full),
            pltpu.VMEM((rows, width), full),
            dma((chips + 5,)),
            dma((7,)),
            dma((10,)),
        ]
        + scatter_sems(chips)
        + line_sems(chips)
        + reduce_scratch(*down_piece)
        + reduce_scratch(*wide_piece)
        + reduce_scratch(*wide_piece),
        compiler_params=pltpu.CompilerParams(
            collective_id=1, has_side_effects=True, vmem_limit_bytes=VMEM_LIMIT
        ),
        name="weigh",
    )(
        cotangent,
        after_attn,
        gains,
        terms,
        lowered_two,
        cotangents,
        hidden,
        grad_gate,
        grad_up,
        w_out,
        queries,
        keys,
        values,
        logs,
        cosine,
        sine,
    )


def back_kernel(
    tokens,
    gains,
    grad_after_in,
    gain_terms_in,
    after_in,
    hidden_in,
    w_down,
    sum_down,
    sum_gate,
    sum_up,
    branch_in,
    lowered_one,
    slab_in,
    attended_in,
    grads_in,
    outputs,
    grad_tokens,
    gain_out,
    out_down,
    out_gate,
    out_up,
    out_qkv,
    out_out,
    grad_after,
    after_attn,
    slab_qkv,
    attended,
    grads,
    hidden,
    terms,
    across,
    slots,
    branch,
    summed,
    gain_terms,
    gain_slots,
    gain_sums,
    gain_sems,
    load_sems,
    *rest,
):
    place = Place()
    chips, block = place.chips, tokens.shape[0]
    model, width = tokens.shape[1], attended.shape[1]
    share = gains.shape[2]
    tile = 2 * block
    scatter_at, rest = rest[:6], rest[6:]
    down = Spread(place, lambda n: sum_down.at[n], out_down, rest[0], False)
    gate = Spread(place, lambda n: sum_gate.at[n], out_gate, rest[1], True)
    up = Spread(place, lambda n: sum_up.at[n], out_up, rest[2], True)
    qkv, out = reducer(place, rest[5:11]), reducer(place, rest[11:17])
    qkv_spread = Spread(place, qkv.piece, out_qkv, rest[3], True)
    out_spread = Spread(place, out.piece, out_out, rest[4], False)
    load = pltpu.make_async_copy(lowered_one, branch, load_sems.at[0])
    load.start()
    loads = [
        pltpu.make_async_copy(source, target, load_sems.at[2 + i])
        for i, (source, target) in enumerate(
            (
                (grads_in, grads),
                (slab_in, slab_qkv),
                (attended_in, attended),
                (grad_after_in, grad_after),
                (after_in, after_attn),
                (hidden_in, hidden),
            )
        )
    ]
    for copy in loads:
        copy.start()
    place.enter()
    down.start()
    down.spread()
    gate.start()
    load.wait()
    loads[0].wait()

    def weigh_rows(j, _):
        left = branch[:, pl.ds(pl.multiple_of(j * share, share), share)]
        got = contract_first(left, grads[...]).astype(jnp.bfloat16)
        qkv.part[j] = got.reshape(qkv.part.shape[1:])
        return 0

    for half in range(2):
        lax.fori_loop(half * chips, (half + 1) * chips, weigh_rows, 0)
        qkv.start(half)
    reload = pltpu.make_async_copy(branch_in, branch, load_sems.at[1])
    reload.start()
    scatter = Scatter(place, terms, across, slots, block, scatter_at)

    def back_rows(t, _):
        at = pl.ds(pl.multiple_of(t * tile, tile), tile)
        got = contract_last(grads[at, :width], slab_qkv[:model, :])
        got += contract_last(grads[at, width : 2 * width], slab_qkv[model : 2 * model, :])
        got += contract_last(grads[at, 2 * width :], slab_qkv[2 * model :, :])
        terms[at, :] = got.astype(jnp.bfloat16)
        return 0

    loads[1].wait()
    lax.fori_loop(0, chips, back_rows, 0)
    for t in range(chips):
        scatter.side(t).start()
    down.widen()
    reload.wait()
    loads[2].wait()
    _, high, wide, thin, columns = out.part.shape
    for half in range(2):
        for at in range(0, columns, 512):
            got = contract_first(
                attended[...], branch[:, half * columns + at : half * columns + at + 512]
            ).astype(jnp.bfloat16)
            out.part[half, :, :, :, at : at + 512] = got.reshape(high, wide, thin, 512)
    out.start(0)
    out.start(1)
    held_down = branch.at[pl.ds(0, w_down.shape[0])]
    load_down = pltpu.make_async_copy(w_down, held_down, load_sems.at[0])
    load_down.start()
    for t in range(chips):
        scatter.cross(t)
    scatter.step(1)
    gate.spread()
    qkv.exchange()
    for step in range(2, chips):
        scatter.step(step)
    up.start()
    scatter.finish(summed)
    gain_terms[...] = gain_terms_in[...]
    loads[3].wait()
    loads[4].wait()
    norm_back(tokens, 0, gains, summed, grad_after, grad_tokens, gain_terms)

    def send_gain(k, _):
        to = lax.rem(place.me + k, place.fsdp)
        remote(
            gain_terms.at[to], gain_slots.at[place.me], gain_sems.at[0], gain_sems.at[1], fsdp=to
        ).start()
        return 0

    lax.fori_loop(1, place.fsdp, send_gain, 0)
    gain_slots[place.me] = gain_terms[place.me]
    scatter.drain()
    out.exchange()
    gate.widen()
    qkv.total()
    qkv_spread.start()
    await_bytes(gain_slots.at[pl.ds(0, place.fsdp - 1)], gain_sems.at[1])
    gain_sums[place.replica] = jnp.sum(gain_slots[...], axis=0)

    def send_sum(k, _):
        ref = gain_sums.at[place.replica]
        to = lax.rem(place.replica + k, place.replicas)
        remote(ref, ref, gain_sems.at[2], gain_sems.at[3], replica=to).start()
        return 0

    lax.fori_loop(1, place.replicas, send_sum, 0)

    up.spread()
    load_down.wait()
    loads[5].wait()

    def sum_rows(t, _):
        at = pl.ds(pl.multiple_of(t * tile, tile), tile)
        terms[at, :] = dot(hidden[at, :], held_down[...]).astype(jnp.bfloat16)
        return 0

    lax.fori_loop(0, chips, sum_rows, 0)
    for t in range(chips):
        scatter.side(t).start()
    for t in range(chips):
        scatter.cross(t)
    scatter.step(1)
    out.total()
    out_spread.start()
    out_spread.spread()
    qkv_spread.spread()
    up.widen()
    for step in range(2, chips):
        scatter.step(step)
    out_spread.widen()
    scatter.finish(summed)
    outputs[...] = (summed[...] + after_attn[...]).astype(outputs.dtype)
    qkv_spread.widen()
    await_bytes(gain_sums.at[pl.ds(0, place.replicas - 1)], gain_sems.at[3])
    gain_out[...] = jnp.sum(gain_sums[...], axis=0)
    await_bytes(gain_slots.at[pl.ds(0, place.fsdp - 1)], gain_sems.at[0])
    await_bytes(gain_sums.at[pl.ds(0, place.replicas - 1)], gain_sems.at[2])
    scatter.drain()
    qkv.drain()
    out.drain()
    for spread in (down, gate, up, out_spread, qkv_spread):
        spread.finish()


def back(
    tokens,
    gains,
    grad_after,
    gain_terms,
    after_attn,
    hidden,
    w_down,
    sum_down,
    sum_gate,
    sum_up,
    branch,
    lowered_one,
    slab_qkv,
    attended,
    grads,
):
    fsdp, replicas = lax.axis_size("fsdp"), lax.axis_size("replica")
    chips, high, wide = fsdp // 2, 2, replicas // 2
    block, model = tokens.shape
    rows, width = attended.shape
    share = gains.shape[2]
    low, full = jnp.bfloat16, jnp.float32
    hbm, vmem = pl.BlockSpec(memory_space=pl.ANY), pl.BlockSpec(memory_space=pltpu.VMEM)
    shape = jax.ShapeDtypeStruct
    thin = share // replicas
    columns = sum_gate.shape[-1]
    qkv_piece = (fsdp, high, wide, thin, 3 * width)
    out_piece = (2, high, wide, width // replicas, model // 2)
    dma = pltpu.SemaphoreType.DMA
    return pl.pallas_call(
        back_kernel,
        in_specs=[vmem, vmem, hbm, vmem] + [hbm] * 11,
        out_specs=[vmem] * 3 + [hbm] * 5,
        out_shape=[
            shape((block, model), low),
            shape((block, model), full),
            shape((8, share), full),
            shape((2, high, wide) + sum_down.shape[1:], low),
            shape((1, high, wide, thin, fsdp * columns), low),
            shape((1, high, wide, thin, fsdp * columns), low),
            shape((3, high, wide, thin, fsdp * width), low),
            shape(out_piece, low),
        ],
        scratch_shapes=[
            pltpu.VMEM((block, model), full),
            pltpu.VMEM((block, model), full),
            pltpu.VMEM(slab_qkv.shape, low),
            pltpu.VMEM((rows, width), low),
            pltpu.VMEM((rows, 3 * width), low),
            pltpu.VMEM(hidden.shape, low),
            pltpu.VMEM((rows, model), low),
            pltpu.VMEM((chips * block, model), low),
            pltpu.VMEM((chips + 1, block, model), low),
            pltpu.VMEM((rows, model), low),
            pltpu.VMEM((block, model), full),
            pltpu.VMEM((fsdp, 8, share), full),
            pltpu.VMEM((fsdp, 8, share), full),
            pltpu.VMEM((replicas, 8, share), full),
            dma((4,)),
            dma((8,)),
        ]
        + scatter_sems(chips)
        + spread_sems() * 5
        + reduce_scratch(*qkv_piece)
        + reduce_scratch(*out_piece),
        compiler_params=pltpu.CompilerParams(
            collective_id=2, has_side_effects=True, vmem_limit_bytes=VMEM_LIMIT
        ),
        name="back",
    )(
        tokens,
        gains,
        grad_after,
        gain_terms,
        after_attn,
        hidden,
        w_down,
        sum_down,
        sum_gate,
        sum_up,
        branch,
        lowered_one,
        slab_qkv,
        attended,
        grads,
    )


def widen_kernel(
    down,
    gate,
    up,
    qkv,
    out,
    outputs_in,
    tokens_in,
    gains,
    w_down,
    w_gate,
    w_up,
    w_query,
    w_key,
    w_value,
    w_out,
    outputs,
    grad_tokens,
    gain_one,
    gain_two,
):
    w_down[...] = down[...].astype(jnp.float32)
    w_gate[...] = gate[...].astype(jnp.float32)
    w_up[...] = up[...].astype(jnp.float32)
    for i, ref in enumerate((w_query, w_key, w_value)):
        ref[...] = qkv[i].astype(jnp.float32)
    half = out.shape[2]
    for i in range(2):
        w_out[:, i * half : (i + 1) * half] = out[i].astype(jnp.float32)
    outputs[...] = outputs_in[...]
    grad_tokens[...] = tokens_in[...]
    gain_one[...] = gains[0, :]
    gain_two[...] = gains[1, :]


def widen(down, gate, up, qkv, out, outputs, grad_tokens, gains):
    steps = min(16, gate.shape[0] // 16)
    token_steps = outputs.shape[0] // 16
    full = jnp.float32

    def rows(array):
        return pl.BlockSpec((array.shape[0] // steps, array.shape[1]), lambda i: (i, 0))

    def tokens(array):
        return pl.BlockSpec(
            (array.shape[0] // token_steps, array.shape[1]), lambda i: (jnp.minimum(i, token_steps - 1), 0)
        )

    def stacked(array):
        return pl.BlockSpec((array.shape[0], array.shape[1] // steps, array.shape[2]), lambda i: (0, i, 0))

    like = [down, gate, up, qkv[0], qkv[0], qkv[0]]
    shapes = [jax.ShapeDtypeStruct(array.shape, full) for array in like]
    shapes.append(jax.ShapeDtypeStruct((out.shape[1], 2 * out.shape[2]), full))
    row = jax.ShapeDtypeStruct(gains.shape[1:], full)
    whole = pl.BlockSpec(gains.shape, lambda i: (0, 0))
    line = pl.BlockSpec(gains.shape[1:], lambda i: (0,))
    return pl.pallas_call(
        widen_kernel,
        grid=(steps,),
        in_specs=[rows(down), rows(gate), rows(up), stacked(qkv), stacked(out)]
        + [tokens(outputs), tokens(grad_tokens), whole],
        out_specs=[rows(shape) for shape in shapes]
        + [tokens(outputs), tokens(grad_tokens), line, line],
        out_shape=shapes
        + [jax.ShapeDtypeStruct(array.shape, array.dtype) for array in (outputs, grad_tokens)]
        + [row, row],
        compiler_params=pltpu.CompilerParams(vmem_limit_bytes=VMEM_LIMIT),
        name="widen",
    )(down, gate, up, qkv, out, outputs, grad_tokens, gains)


def local(
    tokens, attn_gain, w_query, w_key, w_value, w_out, ffn_gain, w_gate, w_up, w_down, cotangent
):
    cosine, sine = rope_tables(tokens.shape[0] * lax.axis_size("fsdp"))
    (
        lowered_one,
        lowered_two,
        cotangents,
        slab_qkv,
        hidden,
        grad_gate,
        grad_up,
        terms,
        queries,
        keys,
        values,
        attended,
        logs,
        after_attn,
        gains,
    ) = front(
        tokens,
        cotangent,
        attn_gain,
        ffn_gain,
        w_query,
        w_key,
        w_value,
        w_out,
        w_gate,
        w_up,
        w_down,
        cosine,
        sine,
    )
    gain_terms, grad_after, grads, branch, sum_down, sum_gate, sum_up = weigh(
        cotangent,
        after_attn,
        gains,
        terms,
        lowered_two,
        cotangents,
        hidden,
        grad_gate,
        grad_up,
        w_out,
        queries,
        keys,
        values,
        logs,
        cosine,
        sine,
    )
    outputs, grad_tokens, gain_grads, low_down, low_gate, low_up, low_qkv, low_out = back(
        tokens,
        gains,
        grad_after,
        gain_terms,
        after_attn,
        hidden,
        w_down,
        sum_down,
        sum_gate,
        sum_up,
        branch,
        lowered_one,
        slab_qkv,
        attended,
        grads,
    )
    (
        grad_w_down,
        grad_w_gate,
        grad_w_up,
        grad_w_query,
        grad_w_key,
        grad_w_value,
        grad_w_out,
        outputs,
        grad_tokens,
        grad_attn_gain,
        grad_ffn_gain,
    ) = widen(
        low_down.reshape(w_down.shape),
        low_gate.reshape(w_gate.shape),
        low_up.reshape(w_up.shape),
        low_qkv.reshape((3,) + w_query.shape),
        low_out.reshape(2, w_out.shape[0], -1),
        outputs,
        grad_tokens,
        gain_grads,
    )
    return (
        outputs,
        grad_tokens,
        grad_attn_gain,
        grad_w_query,
        grad_w_key,
        grad_w_value,
        grad_w_out,
        grad_ffn_gain,
        grad_w_gate,
        grad_w_up,
        grad_w_down,
    )


def solution(mesh):
    rows = P("fsdp", None)
    tokens = P(("replica", "fsdp"), None)
    gain = P("fsdp")
    return jax.shard_map(
        local,
        mesh=mesh,
        in_specs=(tokens, gain, rows, rows, rows, rows, gain, rows, rows, rows, tokens),
        out_specs=(tokens, tokens, gain, rows, rows, rows, rows, gain, rows, rows, rows),
        check_vma=False,
    )
```
